32 devices in a mesh: seq: 8 (over z, x), fsdp: 4 (over y, core).
Axes of the slice: x: 2, y: 2, z: 4, core: 2. Of those that a mesh axis runs over, the one named last changes fastest.
Arguments:
- tokens: bfloat16 [4, 1024, 2048], P('fsdp', 'seq'), may hold values from -6 to 6
- query_key_value_weight: bfloat16 [2048, 5120], P(('seq', 'fsdp')), may hold values from -0.125 to 0.125
- w_out_t: bfloat16 [2048, 4096], P(('seq', 'fsdp')), may hold values from -0.5 to 0.5
- w_router: bfloat16 [2048, 32], P(('seq', 'fsdp')), may hold values from -0.0625 to 0.0625
- w_in: bfloat16 [32, 2048, 1536], P(('seq', 'fsdp')), may hold values from -0.125 to 0.125
- w_down: bfloat16 [32, 768, 2048], P(('seq', 'fsdp')), may hold values from -0.625 to 0.625
- attn_gain: float32 [2048], replicated, may hold values from 0.1 to 1.9
- ffn_gain: float32 [2048], replicated, may hold values from 0.1 to 1.9
- q_gain: float32 [128], replicated, may hold values from 0.5 to 2
- k_gain: float32 [128], replicated, may hold values from 0.5 to 2
- routes: int32 [4, 1024, 8], P('fsdp', 'seq'), may hold values from 0 to 31, as said below
- cotangent: bfloat16 [4, 1024, 2048], P('fsdp', 'seq'), may hold values from -6 to 6
Outputs:
- output: bfloat16 [4, 1024, 2048], P('fsdp', 'seq')
- d_tokens: bfloat16 [4, 1024, 2048], P('fsdp', 'seq')
- d_w_qkv: float32 [2048, 5120], P(('seq', 'fsdp'))
- d_w_out_t: float32 [2048, 4096], P(('seq', 'fsdp'))
- d_w_router: float32 [2048, 32], P(('seq', 'fsdp'))
- d_w_in: float32 [32, 2048, 1536], P(('seq', 'fsdp'))
- d_w_down: float32 [32, 768, 2048], P(('seq', 'fsdp'))
- d_attn_gain: float32 [2048], replicated
- d_ffn_gain: float32 [2048], replicated
- d_q_gain: float32 [128], replicated
- d_k_gain: float32 [128], replicated
The draws below stay inside these ranges and needn't reach their ends.
Inputs may be any that keep to these rules, and one draw needn't show every extreme that they name: `routes`: each token names 8 different experts. In each aligned block of 128 tokens of one sequence, 16 experts are named exactly 64 times each and the others not at all.
All inputs are finite; a program needn't handle non-finite values.
Results may differ from the reference program's by a relative error of at most 0.02.
Values may be sent and summed in bfloat16 or wider, within the bound.
A program may use at most 256 MiB of HBM per device.

```python
import math
from functools import partial
import jax
import jax.numpy as jnp
from jax import lax

MODEL_DIMENSION = 2048
QUERY_HEADS = 32
KEY_VALUE_HEADS = 4
HEAD_DIMENSION = 128
FF = 768
TOPK = 8
TOK_DEV = 128
LENGTH = 1024
SEQS = 4
EXPERTS = 32
CAP = 64


def draw_routes(key, part):
    half_count = EXPERTS // 2
    stride = half_count // TOPK
    block_count = SEQS * (LENGTH // TOK_DEV)
    favour_key, noise_key, order_key = jax.random.split(jax.random.fold_in(key, 7), 3)
    favour = jax.random.randint(favour_key, (EXPERTS,), 0, 4) * EXPERTS
    noise = jax.random.randint(noise_key, (block_count, EXPERTS), 0, 2 * EXPERTS)
    expert_ids = jnp.arange(EXPERTS, dtype=jnp.int32)
    ranking = (favour[None, :] + noise) * EXPERTS + expert_ids[None, :]
    full_set = lax.top_k(ranking, half_count)[1].astype(jnp.int32)
    orders = jax.vmap(lambda sub: jax.random.permutation(sub, TOK_DEV))(jax.random.split(order_key, block_count)).astype(jnp.int32)
    choice_steps = stride * jnp.arange(TOPK, dtype=jnp.int32)
    position = (orders[:, :, None] + choice_steps[None, None, :]) % half_count
    picked = jnp.take_along_axis(full_set, position.reshape(block_count, TOK_DEV * TOPK), axis=1)
    return picked.reshape(SEQS, LENGTH, TOPK).astype(jnp.int32)


def raised(result, own_key, source, target, blocks, factor):
    owner, partner = [(jnp.arange(result.shape[dim]) // (result.shape[dim] // blocks)).reshape([-1 if axis == dim else 1 for axis in range(result.ndim)]) for dim in (source, target)]
    chosen = jax.random.permutation(own_key, blocks)[partner]
    strong = (owner == chosen) | (owner == (partner + blocks // 2) % blocks)
    return jnp.where(strong, factor * result, result)


def block_levels(rng, extent, cuts, smallest, largest):
    def one(axis_at, blocks):
        heights = jax.random.uniform(jax.random.fold_in(jax.random.fold_in(rng, 6), axis_at), (blocks,), jnp.float32, smallest / len(cuts), largest / len(cuts))
        return jnp.repeat(jnp.exp(heights), extent[axis_at] // blocks).reshape((-1,) + (1,) * (len(extent) - axis_at - 1))

    level = one(*cuts[0])
    for cut in cuts[1:]:
        level = level * one(*cut)
    return level


def bell_draw(stream_key, shape, scale, limit, cuts=(), kind=jnp.bfloat16):
    values = jax.random.normal(stream_key, shape, jnp.float32) * scale
    if len(cuts) > 0:
        values = block_levels(stream_key, shape, cuts, -0.22, 0.18) * values
    return jnp.clip(values, min=-limit, max=limit).astype(kind)


def noise_with(own_key, extent, scale, most, shards, heavy, kind=jnp.bfloat16):
    array = scale * jax.random.normal(own_key, extent, jnp.float32)
    if shards:
        array = array * block_levels(own_key, extent, shards, -0.22, 0.18)
    return jnp.clip(raised(array, jax.random.fold_in(own_key, 3), *heavy), -most, most).astype(kind)


def setup_inputs(seed: int = 0) -> dict:
    seeds = jax.random.split(jax.random.key(seed), 13)
    tokens = noise_with(seeds[0], (SEQS, LENGTH, MODEL_DIMENSION), 1.0, 6.0, ((0, 4), (1, 8)), (1, 2, 8, 2.0))
    query_key_value_weight = bell_draw(seeds[1], (MODEL_DIMENSION, (QUERY_HEADS + 2 * KEY_VALUE_HEADS) * HEAD_DIMENSION), MODEL_DIMENSION ** -0.5, 0.125, ((0, 32),))
    w_out_t = bell_draw(seeds[2], (MODEL_DIMENSION, QUERY_HEADS * HEAD_DIMENSION), HEAD_DIMENSION ** -0.5, 0.5, ((0, 32),))
    w_router = bell_draw(seeds[3], (MODEL_DIMENSION, EXPERTS), (4 * MODEL_DIMENSION) ** -0.5, 0.0625, ((0, 32),))
    w_in = bell_draw(seeds[4], (EXPERTS, MODEL_DIMENSION, 2 * FF), MODEL_DIMENSION ** -0.5, 0.125, ((0, 32),))
    w_down = bell_draw(seeds[5], (EXPERTS, FF, MODEL_DIMENSION), (FF // 8) ** -0.5, 0.625, ((0, 32),))
    attn_gain = jnp.clip(1.0 + 0.18 * jax.random.normal(seeds[6], (MODEL_DIMENSION,), jnp.float32), 0.1, 1.9)
    ffn_gain = jnp.clip(1.0 + 0.18 * jax.random.normal(seeds[7], (MODEL_DIMENSION,), jnp.float32), 0.1, 1.9)
    q_gain = jnp.clip(jnp.exp(jax.random.uniform(seeds[8], (HEAD_DIMENSION,), jnp.float32, math.log(0.5), math.log(2.0))), 0.5, 2.0)
    k_gain = jnp.clip(jnp.exp(jax.random.uniform(seeds[9], (HEAD_DIMENSION,), jnp.float32, math.log(0.5), math.log(2.0))), 0.5, 2.0)
    routes = draw_routes(jax.random.fold_in(seeds[12], 71), 0)
    cotangent = bell_draw(seeds[11], (SEQS, LENGTH, MODEL_DIMENSION), 1.0, 6.0, ((0, 4), (1, 8)))
    return dict(tokens=tokens, query_key_value_weight=query_key_value_weight, w_out_t=w_out_t, w_router=w_router, w_in=w_in, w_down=w_down, attn_gain=attn_gain, ffn_gain=ffn_gain, q_gain=q_gain, k_gain=k_gain, routes=routes, cotangent=cotangent)


EPS = 1e-06
ROPE_BASE = 1000000.0
precise = lax.Precision.HIGHEST

@jax.custom_vjp
def lower_precision(v):
    return lax.optimization_barrier(v.astype(jnp.bfloat16)).astype(jnp.float32)

@jax.custom_vjp
def low_back(v):
    return v

def low_keep(v):
    return (lower_precision(v), None)

def low_pass(kept, grad):
    return (grad,)

def back_keep(v):
    return (v, None)

def back_low(kept, grad):
    return (lower_precision(grad),)
lower_precision.defvjp(low_keep, low_pass)
low_back.defvjp(back_keep, back_low)

def rms_scale(values, gain):
    return values * lax.rsqrt(lax.optimization_barrier(jnp.mean(values * values, axis=-1, keepdims=True)) + EPS) * gain

def rotate(values, positions):
    half_dim = values.shape[-1] // 2
    frequency = ROPE_BASE ** (-2.0 * jnp.arange(half_dim, dtype=jnp.float32) / values.shape[-1])
    angles = positions.astype(jnp.float32)[:, None] * frequency[None, :]
    cosine = jnp.cos(angles)[:, None, :]
    sine_part = jnp.sin(angles)[:, None, :]
    first_half = values[..., :half_dim]
    second = values[..., half_dim:]
    return jnp.concatenate([first_half * cosine - second * sine_part, second * cosine + first_half * sine_part], axis=-1)

def attend_whole_sequence(operands):
    query_rows_all, key_per_head, value_per_head = operands
    sequence_length = query_rows_all.shape[0]
    query_group_width = QUERY_HEADS // KEY_VALUE_HEADS
    key_full = jnp.repeat(key_per_head, query_group_width, axis=1)
    value_full = jnp.repeat(value_per_head, query_group_width, axis=1)
    block_rows = min(512, sequence_length)
    query_blocks = query_rows_all.reshape(sequence_length // block_rows, block_rows, QUERY_HEADS, HEAD_DIMENSION)
    block_starts = (jnp.arange(sequence_length // block_rows) * block_rows).astype(jnp.int32)
    key_pos = jnp.arange(sequence_length).astype(jnp.int32)
    score_scale = 1.0 / math.sqrt(HEAD_DIMENSION)

    def one_block(pieces):
        query_part, row_start = pieces
        scores = low_back(jnp.einsum('qhd,khd->hqk', query_part, key_full, precision=precise) * score_scale)
        row_pos = row_start + jnp.arange(block_rows).astype(jnp.int32)
        allowed = key_pos[None, :] <= row_pos[:, None]
        scores = jnp.where(allowed[None], scores, -1e+30)
        row_max = lax.optimization_barrier(jnp.max(scores, axis=-1, keepdims=True))
        weights = jnp.exp(scores - row_max)
        prob_low = lower_precision(weights / lax.optimization_barrier(jnp.sum(weights, axis=-1, keepdims=True)))
        mixed_out = jnp.einsum('hqk,khd->qhd', prob_low, value_full, precision=precise)
        return low_back(lower_precision(mixed_out)).reshape(block_rows, QUERY_HEADS * HEAD_DIMENSION)
    return lax.map(jax.checkpoint(one_block), (query_blocks, block_starts)).reshape(sequence_length, QUERY_HEADS * HEAD_DIMENSION)

def slot_tables(routes):
    block_routes = routes.reshape(-1, TOK_DEV * TOPK).astype(jnp.int32)
    block_count = block_routes.shape[0]
    expert_ids = jnp.arange(EXPERTS).astype(jnp.int32)
    onehot = (block_routes[:, :, None] == expert_ids[None, None, :]).astype(jnp.int32)
    earlier = (jnp.cumsum(onehot, axis=1) - onehot).astype(jnp.int32)
    slot_index = lax.optimization_barrier(jnp.sum(earlier * onehot, axis=2)).astype(jnp.int32)
    column = (jnp.arange(block_count).astype(jnp.int32)[:, None] * CAP + slot_index).astype(jnp.int32)
    route_index = jnp.arange(block_count * TOK_DEV * TOPK).astype(jnp.int32).reshape(block_count, TOK_DEV * TOPK)
    slot_table = jnp.zeros((EXPERTS, block_count * CAP), jnp.int32).at[block_routes, column].set(route_index)
    slot_used = jnp.zeros((EXPERTS, block_count * CAP), jnp.float32).at[block_routes, column].set(1.0)
    return (slot_table, slot_used)

def forward(tokens, query_key_value_weight, w_out_t, w_router, w_in, w_down, attn_gain, ffn_gain, q_gain, k_gain, routes):
    sequence_count, sequence_length, model_width = tokens.shape
    flat_tokens = tokens.reshape(sequence_count * sequence_length, model_width)
    normed_one = lower_precision(rms_scale(flat_tokens, attn_gain))
    projection_output = low_back(jnp.dot(normed_one, query_key_value_weight, precision=precise))
    positions = jnp.tile(jnp.arange(sequence_length).astype(jnp.int32), sequence_count)
    q_raw = projection_output[:, :QUERY_HEADS * HEAD_DIMENSION].reshape(-1, QUERY_HEADS, HEAD_DIMENSION)
    key_unnormed = projection_output[:, QUERY_HEADS * HEAD_DIMENSION:(QUERY_HEADS + KEY_VALUE_HEADS) * HEAD_DIMENSION].reshape(-1, KEY_VALUE_HEADS, HEAD_DIMENSION)
    query_rows_all = lower_precision(rotate(rms_scale(q_raw, q_gain), positions))
    key_per_head = lower_precision(rotate(rms_scale(key_unnormed, k_gain), positions))
    value_per_head = lower_precision(projection_output[:, (QUERY_HEADS + KEY_VALUE_HEADS) * HEAD_DIMENSION:].reshape(-1, KEY_VALUE_HEADS, HEAD_DIMENSION))
    attention_result = lax.map(attend_whole_sequence, (query_rows_all.reshape(sequence_count, sequence_length, QUERY_HEADS, HEAD_DIMENSION), key_per_head.reshape(sequence_count, sequence_length, KEY_VALUE_HEADS, HEAD_DIMENSION), value_per_head.reshape(sequence_count, sequence_length, KEY_VALUE_HEADS, HEAD_DIMENSION)))
    attention_result = attention_result.reshape(sequence_count * sequence_length, QUERY_HEADS * HEAD_DIMENSION)
    attn_out = low_back(jnp.dot(attention_result, w_out_t.T, precision=precise))
    hidden = flat_tokens + attn_out
    normed_two = lower_precision(rms_scale(hidden, ffn_gain))
    logits = low_back(jnp.dot(normed_two, w_router, precision=precise))
    route_rows = routes.reshape(-1, TOPK).astype(jnp.int32)
    chosen = jnp.take_along_axis(logits, route_rows, axis=1)
    row_max = lax.optimization_barrier(jnp.max(chosen, axis=-1, keepdims=True))
    exp_part = jnp.exp(chosen - row_max)
    gate_probs = (exp_part / lax.optimization_barrier(jnp.sum(exp_part, axis=-1, keepdims=True))).reshape(-1)
    slot_table, slot_used = slot_tables(routes)

    def expert_rows(operands):
        route_index, used_mask, gate_weight, down_weight = operands
        token_index = route_index // TOPK
        row_values = low_back(normed_two[token_index])
        gate_up = low_back(jnp.dot(row_values, gate_weight, precision=precise))
        gate_half = gate_up[:, :FF]
        up_half = gate_up[:, FF:]
        inner_act = lower_precision(gate_half * jax.nn.sigmoid(gate_half) * up_half)
        expert_out = low_back(lower_precision(jnp.dot(inner_act, down_weight, precision=precise)))
        return (gate_probs[route_index] * used_mask)[:, None] * expert_out
    weighted = lax.map(jax.checkpoint(expert_rows), (slot_table, slot_used, w_in, w_down))
    token_index = (slot_table // TOPK).reshape(-1).astype(jnp.int32)
    mixture = jnp.zeros_like(hidden).at[token_index].add(weighted.reshape(-1, model_width))
    return (hidden + mixture).reshape(sequence_count, sequence_length, model_width)

def reference(tokens, query_key_value_weight, w_out_t, w_router, w_in, w_down, attn_gain, ffn_gain, q_gain, k_gain, routes, cotangent):
    floats = (tokens, query_key_value_weight, w_out_t, w_router, w_in, w_down, attn_gain, ffn_gain, q_gain, k_gain)
    floats = tuple((operand.astype(jnp.float32) for operand in floats))
    output, pullback = jax.vjp(partial(forward, routes=routes), *floats)
    grads = pullback(cotangent.astype(jnp.float32))
    return (output.astype(jnp.bfloat16), grads[0].astype(jnp.bfloat16), grads[1], grads[2], grads[3], grads[4], grads[5], grads[6], grads[7], grads[8], grads[9])
```

```python
from functools import partial
import math

import jax
import jax.numpy as jnp
from jax import lax
from jax.sharding import PartitionSpec as P

QUERY_HEADS = 32
KEY_VALUE_HEADS = 4
HEAD_DIMENSION = 128
FF = 768
TOPK = 8


EPS = 1e-06
ROPE_BASE = 1000000.0


def rms_scale(values, gain):
    return values * lax.rsqrt(jnp.mean(values * values, axis=-1, keepdims=True) + EPS) * gain


def rotate(values, positions):
    half_dim = values.shape[-1] // 2
    frequency = ROPE_BASE ** (-2.0 * jnp.arange(half_dim, dtype=jnp.float32) / values.shape[-1])
    angles = positions.astype(jnp.float32)[:, None] * frequency[None, :]
    cosine = jnp.cos(angles)[:, None, :]
    sine_part = jnp.sin(angles)[:, None, :]
    first_half = values[..., :half_dim]
    second = values[..., half_dim:]
    return jnp.concatenate(
        [first_half * cosine - second * sine_part, second * cosine + first_half * sine_part],
        axis=-1,
    )


def head_prepare(raw_heads, gain, positions):
    return rotate(rms_scale(raw_heads, gain), positions)


def route_slots(route_flat, experts):
    onehot = (route_flat[:, None] == jnp.arange(experts, dtype=jnp.int32)[None, :]).astype(
        jnp.int32
    )
    earlier = jnp.cumsum(onehot, axis=0) - onehot
    return (onehot, jnp.sum(earlier * onehot, axis=1))


def pack_slots(row_values, expert_ids, slot_index, slot_shape):
    buffer = jnp.zeros(slot_shape, row_values.dtype)
    return buffer.at[expert_ids // slot_shape[1], expert_ids % slot_shape[1], slot_index].set(
        row_values
    )


def unpack_slots(buffer, expert_ids, slot_index):
    return buffer[expert_ids // buffer.shape[1], expert_ids % buffer.shape[1], slot_index]


def causal_scores(query_part, key_full, row_start):
    block_rows = query_part.shape[0]
    score_scale = 1.0 / math.sqrt(query_part.shape[2])
    scores = (
        jnp.einsum("qhd,khd->hqk", query_part, key_full, preferred_element_type=jnp.float32)
        * score_scale
    )
    key_pos = jnp.arange(key_full.shape[0], dtype=jnp.int32)
    row_pos = row_start + jnp.arange(block_rows, dtype=jnp.int32)
    allowed = key_pos[None, :] <= row_pos[:, None]
    return jnp.where(allowed[None], scores, -1e30)


def attend_forward(query_rows_all, key_full, value_full):
    sequence_length = query_rows_all.shape[0]
    block_rows = min(512, sequence_length)

    def one_block(block_index):
        row_start = block_index * block_rows
        query_part = lax.dynamic_slice_in_dim(query_rows_all, row_start, block_rows, 0)
        scores = causal_scores(query_part, key_full, row_start)
        row_max = jnp.max(scores, axis=-1, keepdims=True)
        weights = jnp.exp(scores - row_max)
        row_total = jnp.sum(weights, axis=-1, keepdims=True)
        prob_low = (weights / row_total).astype(jnp.bfloat16)
        mixed_out = jnp.einsum(
            "hqk,khd->qhd", prob_low, value_full, preferred_element_type=jnp.float32
        )
        return (mixed_out.astype(jnp.bfloat16), (row_max + jnp.log(row_total))[..., 0])

    mixed_out, log_total = lax.map(
        one_block, jnp.arange(sequence_length // block_rows, dtype=jnp.int32)
    )
    return (mixed_out.reshape(query_rows_all.shape), log_total)


def attend_backward(query_rows_all, key_full, value_full, log_total, d_mixed):
    sequence_length = query_rows_all.shape[0]
    block_rows = min(512, sequence_length)
    score_scale = 1.0 / math.sqrt(query_rows_all.shape[2])

    def one_block(running, block_index):
        d_key_sum, d_value_sum = running
        row_start = block_index * block_rows
        query_part = lax.dynamic_slice_in_dim(query_rows_all, row_start, block_rows, 0)
        d_part = lax.dynamic_slice_in_dim(d_mixed, row_start, block_rows, 0)
        scores = causal_scores(query_part, key_full, row_start)
        prob_full = jnp.exp(scores - log_total[block_index][..., None])
        prob_low = prob_full.astype(jnp.bfloat16)
        d_probs = jnp.einsum("qhd,khd->hqk", d_part, value_full, preferred_element_type=jnp.float32)
        row_delta = jnp.sum(prob_full * d_probs, axis=-1, keepdims=True)
        d_scores = (prob_full * (d_probs - row_delta)).astype(jnp.bfloat16)
        d_query_part = (
            jnp.einsum("hqk,khd->qhd", d_scores, key_full, preferred_element_type=jnp.float32)
            * score_scale
        )
        d_key_sum = (
            d_key_sum
            + jnp.einsum("hqk,qhd->khd", d_scores, query_part, preferred_element_type=jnp.float32)
            * score_scale
        )
        d_value_sum = d_value_sum + jnp.einsum(
            "hqk,qhd->khd", prob_low, d_part, preferred_element_type=jnp.float32
        )
        return ((d_key_sum, d_value_sum), d_query_part)

    zero_grad = jnp.zeros(key_full.shape, jnp.float32)
    (d_key_sum, d_value_sum), d_query = lax.scan(
        one_block,
        (zero_grad, zero_grad),
        jnp.arange(sequence_length // block_rows, dtype=jnp.int32),
    )
    return (d_query.reshape(query_rows_all.shape), d_key_sum, d_value_sum)


def routed_body(
    tokens,
    query_key_value_weight,
    w_out_t,
    w_router,
    w_in,
    w_down,
    attn_gain,
    ffn_gain,
    q_gain,
    k_gain,
    routes,
    cotangent,
):
    sequence_count = lax.axis_size("seq")
    shard_count = lax.axis_size("fsdp")
    experts = sequence_count * shard_count
    token_row_count = tokens.shape[1]
    model_width = tokens.shape[2]
    query_group_width = QUERY_HEADS // KEY_VALUE_HEADS
    capacity = 2 * token_row_count * TOPK // experts
    slot_shape = (sequence_count, shard_count, capacity, model_width)
    positions = lax.axis_index("seq") * token_row_count + jnp.arange(
        token_row_count, dtype=jnp.int32
    )
    full_qkv, full_out, full_router = (
        lax.all_gather(query_key_value_weight, ("seq", "fsdp"), axis=0, tiled=True),
        lax.all_gather(w_out_t, ("seq", "fsdp"), axis=0, tiled=True),
        lax.all_gather(w_router, ("seq", "fsdp"), axis=0, tiled=True),
    )
    resid_in = tokens[0].astype(jnp.float32)
    normed_one = rms_scale(resid_in, attn_gain).astype(jnp.bfloat16)
    projection_output = jnp.dot(normed_one, full_qkv, preferred_element_type=jnp.float32)
    q_raw = projection_output[:, : QUERY_HEADS * HEAD_DIMENSION].reshape(
        token_row_count, QUERY_HEADS, HEAD_DIMENSION
    )
    key_unnormed = projection_output[
        :, QUERY_HEADS * HEAD_DIMENSION : (QUERY_HEADS + KEY_VALUE_HEADS) * HEAD_DIMENSION
    ].reshape(token_row_count, KEY_VALUE_HEADS, HEAD_DIMENSION)
    value_per_head = (
        projection_output[:, (QUERY_HEADS + KEY_VALUE_HEADS) * HEAD_DIMENSION :]
        .reshape(token_row_count, KEY_VALUE_HEADS, HEAD_DIMENSION)
        .astype(jnp.bfloat16)
    )
    prepare = partial(head_prepare, positions=positions)
    query_rows_all = prepare(q_raw, q_gain).astype(jnp.bfloat16)
    key_per_head = prepare(key_unnormed, k_gain).astype(jnp.bfloat16)
    send_keys = jnp.repeat(key_per_head, query_group_width, axis=1)
    send_values = jnp.repeat(value_per_head, query_group_width, axis=1)
    head_queries, head_keys, head_values = (
        lax.all_to_all(query_rows_all, "seq", split_axis=1, concat_axis=0, tiled=True),
        lax.all_to_all(send_keys, "seq", split_axis=1, concat_axis=0, tiled=True),
        lax.all_to_all(send_values, "seq", split_axis=1, concat_axis=0, tiled=True),
    )
    mixed_heads, log_total = attend_forward(head_queries, head_keys, head_values)
    mixed_tok = lax.all_to_all(mixed_heads, "seq", split_axis=0, concat_axis=1, tiled=True)
    attention_result = mixed_tok.reshape(token_row_count, QUERY_HEADS * HEAD_DIMENSION)
    attn_out = jnp.einsum(
        "tj,dj->td", attention_result, full_out, preferred_element_type=jnp.float32
    )
    hidden = resid_in + attn_out
    normed_two = rms_scale(hidden, ffn_gain).astype(jnp.bfloat16)
    logits = jnp.dot(normed_two, full_router, preferred_element_type=jnp.float32)
    route_flat = routes[0].reshape(-1)
    onehot, slot_index = route_slots(route_flat, experts)
    onehot_float = onehot.reshape(token_row_count, TOPK, experts).astype(jnp.float32)
    chosen = jnp.sum(onehot_float * logits[:, None, :], axis=-1)
    row_max = jnp.max(chosen, axis=-1, keepdims=True)
    exp_part = jnp.exp(chosen - row_max)
    gate_probs = exp_part / jnp.sum(exp_part, axis=-1, keepdims=True)
    send_rows = pack_slots(jnp.repeat(normed_two, TOPK, axis=0), route_flat, slot_index, slot_shape)
    arrived = lax.all_to_all(
        lax.all_to_all(send_rows, "seq", split_axis=0, concat_axis=0, tiled=True),
        "fsdp",
        split_axis=1,
        concat_axis=1,
        tiled=True,
    )
    rows_in = arrived.reshape(-1, model_width)
    gate_weight = w_in[0]
    down_weight = w_down[0]
    gate_up = jnp.dot(rows_in, gate_weight, preferred_element_type=jnp.float32)
    gate_half = gate_up[:, :FF]
    up_half = gate_up[:, FF:]
    gate_sig = jax.nn.sigmoid(gate_half)
    silu_gate = gate_half * gate_sig
    inner_act = (silu_gate * up_half).astype(jnp.bfloat16)
    expert_out = jnp.dot(inner_act, down_weight, preferred_element_type=jnp.float32).astype(
        jnp.bfloat16
    )
    returned = lax.all_to_all(
        lax.all_to_all(
            expert_out.reshape(slot_shape), "seq", split_axis=0, concat_axis=0, tiled=True
        ),
        "fsdp",
        split_axis=1,
        concat_axis=1,
        tiled=True,
    )
    picked = (
        unpack_slots(returned, route_flat, slot_index)
        .astype(jnp.float32)
        .reshape(token_row_count, TOPK, model_width)
    )
    mixture = jnp.sum(gate_probs[..., None] * picked, axis=1)
    output = (hidden + mixture).astype(jnp.bfloat16)
    full_qkv, full_out, full_router = (
        lax.all_gather(query_key_value_weight, ("seq", "fsdp"), axis=0, tiled=True),
        lax.all_gather(w_out_t, ("seq", "fsdp"), axis=0, tiled=True),
        lax.all_gather(w_router, ("seq", "fsdp"), axis=0, tiled=True),
    )
    out_grad = cotangent[0].astype(jnp.float32)
    d_picked = (
        (gate_probs[..., None] * out_grad[:, None, :]).astype(jnp.bfloat16).reshape(-1, model_width)
    )
    d_gates = jnp.sum(picked * out_grad[:, None, :], axis=-1)
    d_send = pack_slots(d_picked, route_flat, slot_index, slot_shape)
    d_arrived = lax.all_to_all(
        lax.all_to_all(d_send, "seq", split_axis=0, concat_axis=0, tiled=True),
        "fsdp",
        split_axis=1,
        concat_axis=1,
        tiled=True,
    ).reshape(-1, model_width)
    d_inner = jnp.einsum("rd,fd->rf", d_arrived, down_weight, preferred_element_type=jnp.float32)
    d_gate_half = d_inner * up_half * gate_sig * (1.0 + gate_half * (1.0 - gate_sig))
    d_up_half = d_inner * silu_gate
    d_gate_up = jnp.concatenate([d_gate_half, d_up_half], axis=1).astype(jnp.bfloat16)
    d_w_down = jnp.einsum("rf,rd->fd", inner_act, d_arrived, preferred_element_type=jnp.float32)[
        None
    ]
    d_w_in = jnp.einsum("rd,rf->df", rows_in, d_gate_up, preferred_element_type=jnp.float32)[None]
    d_rows = jnp.einsum(
        "rf,df->rd", d_gate_up, gate_weight, preferred_element_type=jnp.float32
    ).astype(jnp.bfloat16)
    d_back = lax.all_to_all(
        lax.all_to_all(d_rows.reshape(slot_shape), "seq", split_axis=0, concat_axis=0, tiled=True),
        "fsdp",
        split_axis=1,
        concat_axis=1,
        tiled=True,
    )
    d_routed = jnp.sum(
        unpack_slots(d_back, route_flat, slot_index)
        .astype(jnp.float32)
        .reshape(token_row_count, TOPK, model_width),
        axis=1,
    )
    d_chosen = gate_probs * (d_gates - jnp.sum(gate_probs * d_gates, axis=-1, keepdims=True))
    d_logits = jnp.einsum("tk,tke->te", d_chosen, onehot_float).astype(jnp.bfloat16)
    d_normed_two = d_routed + jnp.einsum(
        "te,de->td", d_logits, full_router, preferred_element_type=jnp.float32
    )
    unused_two, pull_two = jax.vjp(rms_scale, hidden, ffn_gain)
    d_hidden_norm, d_ffn_gain = pull_two(d_normed_two)
    d_hidden = out_grad + d_hidden_norm
    d_attn = d_hidden.astype(jnp.bfloat16)
    d_attended = jnp.einsum(
        "td,dj->tj", d_attn, full_out, preferred_element_type=jnp.float32
    ).astype(jnp.bfloat16)
    d_heads = lax.all_to_all(
        d_attended.reshape(token_row_count, QUERY_HEADS, HEAD_DIMENSION),
        "seq",
        split_axis=1,
        concat_axis=0,
        tiled=True,
    )
    d_query, d_key_sum, d_value_sum = attend_backward(
        head_queries, head_keys, head_values, log_total, d_heads
    )
    seq_rows = head_queries.shape[0]
    local_cols = head_queries.shape[1] * HEAD_DIMENSION
    normed_all, d_attn_all = (
        lax.all_gather(normed_one, "seq", axis=0, tiled=True),
        lax.all_gather(d_attn, "seq", axis=0, tiled=True),
    )
    query_cols = lax.dynamic_slice_in_dim(
        full_qkv, lax.axis_index("seq") * local_cols, local_cols, 1
    )
    q_head_raw = jnp.dot(normed_all, query_cols, preferred_element_type=jnp.float32).reshape(
        head_queries.shape
    )
    seq_positions = jnp.arange(seq_rows, dtype=jnp.int32)
    unused_head, pull_head = jax.vjp(
        partial(head_prepare, positions=seq_positions), q_head_raw, q_gain
    )
    send_d_query, d_q_gain = pull_head(d_query)
    d_query_tok, grad_key_token_rows, grad_value_token_rows = (
        lax.all_to_all(
            send_d_query.astype(jnp.bfloat16), "seq", split_axis=0, concat_axis=1, tiled=True
        ).astype(send_d_query.dtype),
        lax.all_to_all(
            d_key_sum.astype(jnp.bfloat16), "seq", split_axis=0, concat_axis=1, tiled=True
        ).astype(d_key_sum.dtype),
        lax.all_to_all(
            d_value_sum.astype(jnp.bfloat16), "seq", split_axis=0, concat_axis=1, tiled=True
        ).astype(d_value_sum.dtype),
    )
    grad_key_per_head = jnp.sum(
        grad_key_token_rows.reshape(token_row_count, KEY_VALUE_HEADS, -1, HEAD_DIMENSION), axis=2
    )
    grad_value_per_head = jnp.sum(
        grad_value_token_rows.reshape(token_row_count, KEY_VALUE_HEADS, -1, HEAD_DIMENSION), axis=2
    )
    unused_k, pull_k = jax.vjp(prepare, key_unnormed, k_gain)
    grad_key_unnormed, d_k_gain = pull_k(grad_key_per_head)
    d_projected = jnp.concatenate(
        [
            d_query_tok.reshape(token_row_count, QUERY_HEADS * HEAD_DIMENSION),
            grad_key_unnormed.reshape(token_row_count, KEY_VALUE_HEADS * HEAD_DIMENSION),
            grad_value_per_head.reshape(token_row_count, KEY_VALUE_HEADS * HEAD_DIMENSION),
        ],
        axis=1,
    ).astype(jnp.bfloat16)
    d_normed_one = jnp.einsum(
        "tj,dj->td", d_projected, full_qkv, preferred_element_type=jnp.float32
    )
    unused_one, pull_one = jax.vjp(rms_scale, resid_in, attn_gain)
    d_resid_norm, d_attn_gain = pull_one(d_normed_one)
    d_tokens = (d_hidden + d_resid_norm).astype(jnp.bfloat16)[None]
    rows_dev = model_width // experts
    kv_count = 2 * KEY_VALUE_HEADS * HEAD_DIMENSION
    kv_grads = d_projected[:, QUERY_HEADS * HEAD_DIMENSION :]
    first_rows = normed_one
    summed = lax.psum_scatter(
        jnp.concatenate(
            [
                jnp.einsum("tc,tj->cj", first_rows, kv_grads, preferred_element_type=jnp.float32),
                jnp.einsum("tc,te->ce", normed_two, d_logits, preferred_element_type=jnp.float32),
            ],
            axis=1,
        ),
        ("seq", "fsdp"),
        scatter_dimension=0,
        tiled=True,
    )
    d_query_low = send_d_query.reshape(seq_rows, local_cols).astype(jnp.bfloat16)
    attended_heads = mixed_heads.reshape(seq_rows, local_cols)
    normed_order = (
        normed_all.reshape(seq_rows, sequence_count, shard_count, rows_dev)
        .transpose(0, 2, 1, 3)
        .reshape(seq_rows, model_width)
    )
    d_attn_order = (
        d_attn_all.reshape(seq_rows, sequence_count, shard_count, rows_dev)
        .transpose(0, 2, 1, 3)
        .reshape(seq_rows, model_width)
    )
    first_rows = normed_order
    head_sums = lax.psum_scatter(
        jnp.concatenate(
            [
                jnp.einsum(
                    "tc,tj->cj", first_rows, d_query_low, preferred_element_type=jnp.float32
                ),
                jnp.einsum(
                    "tc,tj->cj", d_attn_order, attended_heads, preferred_element_type=jnp.float32
                ),
            ],
            axis=1,
        ).astype(jnp.bfloat16),
        "fsdp",
        scatter_dimension=0,
        tiled=True,
    ).astype(jnp.float32)
    row_sums = (
        lax.all_to_all(
            head_sums.astype(jnp.bfloat16), "seq", split_axis=0, concat_axis=1, tiled=True
        )
        .astype(head_sums.dtype)
        .reshape(rows_dev, sequence_count, 2, local_cols)
    )
    d_w_query = row_sums[:, :, 0].reshape(rows_dev, QUERY_HEADS * HEAD_DIMENSION)
    d_w_out_t = row_sums[:, :, 1].reshape(rows_dev, QUERY_HEADS * HEAD_DIMENSION)
    d_w_qkv = jnp.concatenate([d_w_query, summed[:, :kv_count]], axis=1)
    d_w_router = summed[:, kv_count:]
    d_attn_gain, d_ffn_gain, d_q_gain, d_k_gain = lax.psum(
        (d_attn_gain, d_ffn_gain, d_q_gain, d_k_gain), ("seq", "fsdp")
    )
    return (
        output[None],
        d_tokens,
        d_w_qkv,
        d_w_out_t,
        d_w_router,
        d_w_in,
        d_w_down,
        d_attn_gain,
        d_ffn_gain,
        d_q_gain,
        d_k_gain,
    )


def all_gather_rows(rows, axes):
    return lax.all_gather(rows, axes, axis=0, tiled=True)


def sum_scatter_rows(partial_rows, axes):
    return lax.psum_scatter(partial_rows, axes, scatter_dimension=0, tiled=True)


def head_columns(weight, group_index):
    rows = weight.shape[0]
    query_width = QUERY_HEADS * HEAD_DIMENSION
    key_width = KEY_VALUE_HEADS * HEAD_DIMENSION
    query = weight[:, :query_width].reshape(rows, len(group_index), -1).transpose(1, 0, 2)
    keys = weight[:, query_width : query_width + key_width].reshape(rows, KEY_VALUE_HEADS, -1)
    values = weight[:, query_width + key_width :].reshape(rows, KEY_VALUE_HEADS, -1)
    keys = jnp.stack([keys[:, group] for group in group_index])
    values = jnp.stack([values[:, group] for group in group_index])
    return jnp.concatenate([query, keys, values], axis=2)


def gathered_body(
    tokens,
    query_key_value_weight,
    w_out_t,
    w_router,
    w_in,
    w_down,
    attn_gain,
    ffn_gain,
    q_gain,
    k_gain,
    routes,
    cotangent,
):
    bf16, f32 = jnp.bfloat16, jnp.float32
    both = ("seq", "fsdp")
    seq_size = lax.axis_size("seq")
    shard_size = lax.axis_size("fsdp")
    experts = seq_size * shard_size
    rows = tokens.shape[1]
    width = tokens.shape[2]
    length = rows * seq_size
    weight_rows = query_key_value_weight.shape[0]
    heads = QUERY_HEADS // seq_size
    head_cols = heads * HEAD_DIMENSION
    kv_cols = HEAD_DIMENSION
    proj_cols = head_cols + 2 * kv_cols
    all_cols = proj_cols + head_cols
    group_index = [s * heads * KEY_VALUE_HEADS // QUERY_HEADS for s in range(seq_size)]
    capacity = 2 * rows * TOPK // experts

    pieces = jnp.concatenate(
        [
            head_columns(query_key_value_weight, group_index),
            w_out_t.reshape(weight_rows, seq_size, head_cols).transpose(1, 0, 2),
        ],
        axis=2,
    )
    pieces = lax.all_to_all(pieces, "seq", split_axis=0, concat_axis=0, tiled=True)
    columns = lax.all_gather(pieces, "fsdp", axis=1).reshape(width, all_cols)
    proj_weight = columns[:, :proj_cols]
    out_weight = columns[:, proj_cols:]
    full_router = all_gather_rows(w_router, both)
    cot_all = all_gather_rows(cotangent[0], both)

    resid_in = tokens[0].astype(f32)
    normed_one = rms_scale(resid_in, attn_gain).astype(bf16)
    normed_all = all_gather_rows(normed_one, "seq")
    projected = jnp.dot(normed_all, proj_weight, preferred_element_type=f32)
    seq_positions = jnp.arange(length, dtype=jnp.int32)
    prepare = partial(head_prepare, positions=seq_positions)
    q_raw = projected[:, :head_cols].reshape(length, heads, HEAD_DIMENSION)
    k_raw = projected[:, head_cols : head_cols + kv_cols].reshape(length, 1, HEAD_DIMENSION)
    values = projected[:, head_cols + kv_cols :].astype(bf16).reshape(length, 1, HEAD_DIMENSION)
    queries = prepare(q_raw, q_gain).astype(bf16)
    keys = prepare(k_raw, k_gain).astype(bf16)
    repeat_keys = jnp.repeat(keys, heads, axis=1)
    repeat_values = jnp.repeat(values, heads, axis=1)
    mixed_heads, log_total = attend_forward(queries, repeat_keys, repeat_values)
    attended = mixed_heads.reshape(length, head_cols)
    attn_part = jnp.einsum("tj,dj->td", attended, out_weight, preferred_element_type=f32)
    attn_out = sum_scatter_rows(attn_part.astype(bf16), "seq")
    hidden = resid_in + attn_out.astype(f32)
    normed_two = rms_scale(hidden, ffn_gain).astype(bf16)

    logits = jnp.dot(normed_two, full_router, preferred_element_type=f32)
    onehot = routes[0][:, :, None] == jnp.arange(experts, dtype=jnp.int32)
    onehot_float = onehot.astype(f32)
    named = jnp.sum(onehot_float, axis=1)
    chosen = jnp.sum(onehot_float * logits[:, None, :], axis=-1)
    row_max = jnp.max(chosen, axis=-1, keepdims=True)
    exp_part = jnp.exp(chosen - row_max)
    gate_probs = exp_part / jnp.sum(exp_part, axis=-1, keepdims=True)
    gate_dense = jnp.sum(onehot_float * gate_probs[..., None], axis=1)

    gate_high = gate_dense.astype(bf16)
    gate_low = (gate_dense - gate_high.astype(f32)).astype(bf16)
    route_info = jnp.concatenate([gate_high, gate_low, named.astype(bf16)], axis=1)
    route_info = jnp.pad(route_info, ((0, 0), (0, 128 - route_info.shape[1] % 128)))
    gathered = all_gather_rows(jnp.concatenate([normed_two, route_info], axis=1), both)
    blocks = experts
    rows_all = gathered[:, :width].reshape(blocks, rows, width)
    info = gathered[:, width : width + 3 * experts].reshape(blocks, rows, 3, experts)
    me = lax.axis_index("seq") * shard_size + lax.axis_index("fsdp")
    own = lax.dynamic_index_in_dim(info, me, 3, keepdims=False).astype(f32)
    gate_own = own[:, :, 0] + own[:, :, 1]
    named_own = own[:, :, 2]
    slot = jnp.cumsum(named_own, axis=1) - named_own
    pick = (
        (slot[:, None, :] == jnp.arange(capacity, dtype=f32)[None, :, None])
        & (named_own[:, None, :] > 0)
    ).astype(bf16)
    gate_slots = jnp.einsum(
        "bct,bt->bc", pick.astype(f32), gate_own, precision=lax.Precision.HIGHEST
    ).reshape(-1, 1)
    rows_in = jnp.einsum("bct,btd->bcd", pick, rows_all, preferred_element_type=f32)
    rows_in = rows_in.astype(bf16).reshape(-1, width)
    cot_rows = jnp.einsum(
        "bct,btd->bcd",
        pick,
        cot_all.reshape(blocks, rows, width),
        preferred_element_type=f32,
    ).reshape(-1, width)

    gate_weight = w_in[0]
    down_weight = w_down[0]
    gate_up = jnp.dot(rows_in, gate_weight, preferred_element_type=f32)
    gate_half = gate_up[:, :FF]
    up_half = gate_up[:, FF:]
    gate_sig = jax.nn.sigmoid(gate_half)
    silu_gate = gate_half * gate_sig
    inner_act = (silu_gate * up_half).astype(bf16)
    expert_out = (
        jnp.dot(inner_act, down_weight, preferred_element_type=f32).astype(bf16).astype(f32)
    )
    d_gate_slots = jnp.sum(expert_out * cot_rows, axis=1)
    weighted = (gate_slots * expert_out).astype(bf16).reshape(blocks, capacity, width)
    out_part = jnp.einsum("bct,bcd->btd", pick, weighted, preferred_element_type=f32)
    mixture = sum_scatter_rows(out_part.astype(bf16).reshape(-1, width), both)
    output = (hidden + mixture.astype(f32)).astype(bf16)

    d_expert = (gate_slots * cot_rows).astype(bf16)
    d_inner = jnp.einsum("rd,fd->rf", d_expert, down_weight, preferred_element_type=f32)
    d_gate_half = d_inner * up_half * gate_sig * (1.0 + gate_half * (1.0 - gate_sig))
    d_up_half = d_inner * silu_gate
    d_gate_up = jnp.concatenate([d_gate_half, d_up_half], axis=1).astype(bf16)
    d_w_down = jnp.einsum("rf,rd->fd", inner_act, d_expert, preferred_element_type=f32)[None]
    d_w_in = jnp.einsum("rd,rf->df", rows_in, d_gate_up, preferred_element_type=f32)[None]
    d_rows = jnp.einsum("rf,df->rd", d_gate_up, gate_weight, preferred_element_type=f32)
    d_rows = d_rows.astype(bf16).reshape(blocks, capacity, width)
    d_gate_own = jnp.einsum(
        "bct,bc->bt",
        pick.astype(f32),
        d_gate_slots.reshape(blocks, capacity),
        precision=lax.Precision.HIGHEST,
    )
    d_gate_high = d_gate_own.astype(bf16)
    d_gate_low = (d_gate_own - d_gate_high.astype(f32)).astype(bf16)
    mine = (jnp.arange(experts, dtype=jnp.int32) == me).astype(bf16)
    d_info = jnp.concatenate([d_gate_high[..., None] * mine, d_gate_low[..., None] * mine], axis=2)
    d_info = jnp.pad(d_info, ((0, 0), (0, 0), (0, 128 - d_info.shape[2] % 128)))
    d_part = jnp.einsum("bct,bcd->btd", pick, d_rows, preferred_element_type=f32)
    d_part = jnp.concatenate([d_part.astype(bf16), d_info], axis=2)
    d_back = sum_scatter_rows(d_part.reshape(-1, d_part.shape[2]), both).astype(f32)

    d_gate_dense = d_back[:, width : width + experts] + d_back[:, width + experts : width + 2 * experts]
    d_gates = jnp.sum(onehot_float * d_gate_dense[:, None, :], axis=-1)
    d_chosen = gate_probs * (d_gates - jnp.sum(gate_probs * d_gates, axis=-1, keepdims=True))
    d_logits = jnp.sum(d_chosen[..., None] * onehot_float, axis=1).astype(bf16)
    d_normed_two = d_back[:, :width] + jnp.einsum(
        "te,de->td", d_logits, full_router, preferred_element_type=f32
    )
    out_grad = cotangent[0].astype(f32)
    unused_two, pull_two = jax.vjp(rms_scale, hidden, ffn_gain)
    d_hidden_norm, d_ffn_gain = pull_two(d_normed_two)
    d_hidden = out_grad + d_hidden_norm
    d_attn = d_hidden.astype(bf16)

    d_attn_all = all_gather_rows(d_attn, "seq")
    d_attended = jnp.dot(d_attn_all, out_weight, preferred_element_type=f32).astype(bf16)
    d_query, d_key_sum, d_value_sum = attend_backward(
        queries,
        repeat_keys,
        repeat_values,
        log_total,
        d_attended.reshape(length, heads, HEAD_DIMENSION),
    )
    unused_q, pull_q = jax.vjp(prepare, q_raw, q_gain)
    d_q_raw, d_q_gain = pull_q(d_query)
    unused_k, pull_k = jax.vjp(prepare, k_raw, k_gain)
    d_k_raw, d_k_gain = pull_k(jnp.sum(d_key_sum, axis=1, keepdims=True))
    d_projected = jnp.concatenate(
        [
            d_q_raw.reshape(length, head_cols),
            d_k_raw.reshape(length, kv_cols),
            jnp.sum(d_value_sum, axis=1),
        ],
        axis=1,
    ).astype(bf16)
    d_normed_part = jnp.einsum("tj,dj->td", d_projected, proj_weight, preferred_element_type=f32)
    d_normed_one = sum_scatter_rows(d_normed_part.astype(bf16), "seq").astype(f32)
    unused_one, pull_one = jax.vjp(rms_scale, resid_in, attn_gain)
    d_resid_norm, d_attn_gain = pull_one(d_normed_one)
    d_tokens = (d_hidden + d_resid_norm).astype(bf16)[None]

    d_columns = jnp.concatenate(
        [
            jnp.einsum("tc,tj->cj", normed_all, d_projected, preferred_element_type=f32),
            jnp.einsum("tc,tj->cj", d_attn_all, attended, preferred_element_type=f32),
        ],
        axis=1,
    ).astype(bf16)
    d_columns = (
        d_columns.reshape(seq_size, shard_size, weight_rows, all_cols)
        .transpose(1, 0, 2, 3)
        .reshape(width, all_cols)
    )
    d_columns = sum_scatter_rows(d_columns, "fsdp").reshape(seq_size, weight_rows, all_cols)
    d_pieces = lax.all_to_all(d_columns, "seq", split_axis=0, concat_axis=0, tiled=True).astype(f32)
    d_pieces = d_pieces.transpose(1, 0, 2)
    per_group = seq_size // KEY_VALUE_HEADS
    d_kv = d_pieces[:, :, head_cols:proj_cols].reshape(
        weight_rows, KEY_VALUE_HEADS, per_group, 2, kv_cols
    )
    d_kv = jnp.sum(d_kv, axis=2).transpose(0, 2, 1, 3).reshape(weight_rows, -1)
    d_w_qkv = jnp.concatenate([d_pieces[:, :, :head_cols].reshape(weight_rows, -1), d_kv], axis=1)
    d_w_out_t = d_pieces[:, :, proj_cols:].reshape(weight_rows, -1)
    d_w_router = sum_scatter_rows(
        jnp.einsum("tc,te->ce", normed_two, d_logits, preferred_element_type=f32), both
    )
    d_attn_gain, d_ffn_gain, d_q_gain, d_k_gain = lax.psum(
        (d_attn_gain, d_ffn_gain, d_q_gain, d_k_gain), both
    )
    return (
        output[None],
        d_tokens,
        d_w_qkv,
        d_w_out_t,
        d_w_router,
        d_w_in,
        d_w_down,
        d_attn_gain,
        d_ffn_gain,
        d_q_gain,
        d_k_gain,
    )


def gathered_fits(mesh):
    return mesh.shape["seq"] * mesh.shape["fsdp"] <= 4 * TOPK


def solution(mesh):
    return jax.shard_map(
        gathered_body if gathered_fits(mesh) else routed_body,
        mesh=mesh,
        in_specs=(
            P("fsdp", "seq", None),
            P(("seq", "fsdp"), None),
            P(("seq", "fsdp"), None),
            P(("seq", "fsdp"), None),
            P(("seq", "fsdp"), None, None),
            P(("seq", "fsdp"), None, None),
            P(),
            P(),
            P(),
            P(),
            P("fsdp", "seq", None),
            P("fsdp", "seq", None),
        ),
        out_specs=(
            P("fsdp", "seq", None),
            P("fsdp", "seq", None),
            P(("seq", "fsdp"), None),
            P(("seq", "fsdp"), None),
            P(("seq", "fsdp"), None),
            P(("seq", "fsdp"), None, None),
            P(("seq", "fsdp"), None, None),
            P(),
            P(),
            P(),
            P(),
        ),
        check_vma=False,
    )
```

```python
from functools import partial
import math

import jax
import jax.numpy as jnp
from jax import lax
from jax.experimental import pallas as pl
from jax.experimental.pallas import tpu as pltpu
from jax.sharding import PartitionSpec as P

QUERY_HEADS = 32
KEY_VALUE_HEADS = 4
HEAD_DIMENSION = 128
FF = 768
TOPK = 8


EPS = 1e-06
ROPE_BASE = 1000000.0


def rms_scale(values, gain):
    return values * lax.rsqrt(jnp.mean(values * values, axis=-1, keepdims=True) + EPS) * gain


def rotate(values, positions):
    half_dim = values.shape[-1] // 2
    frequency = ROPE_BASE ** (-2.0 * jnp.arange(half_dim, dtype=jnp.float32) / values.shape[-1])
    angles = positions.astype(jnp.float32)[:, None] * frequency[None, :]
    cosine = jnp.cos(angles)[:, None, :]
    sine_part = jnp.sin(angles)[:, None, :]
    first_half = values[..., :half_dim]
    second = values[..., half_dim:]
    return jnp.concatenate(
        [first_half * cosine - second * sine_part, second * cosine + first_half * sine_part],
        axis=-1,
    )


def head_prepare(raw_heads, gain, positions):
    return rotate(rms_scale(raw_heads, gain), positions)


def route_slots(route_flat, experts):
    onehot = (route_flat[:, None] == jnp.arange(experts, dtype=jnp.int32)[None, :]).astype(
        jnp.int32
    )
    earlier = jnp.cumsum(onehot, axis=0) - onehot
    return (onehot, jnp.sum(earlier * onehot, axis=1))


def pack_slots(row_values, expert_ids, slot_index, slot_shape):
    buffer = jnp.zeros(slot_shape, row_values.dtype)
    return buffer.at[expert_ids // slot_shape[1], expert_ids % slot_shape[1], slot_index].set(
        row_values
    )


def unpack_slots(buffer, expert_ids, slot_index):
    return buffer[expert_ids // buffer.shape[1], expert_ids % buffer.shape[1], slot_index]


def causal_scores(query_part, key_full, row_start):
    block_rows = query_part.shape[0]
    score_scale = 1.0 / math.sqrt(query_part.shape[2])
    scores = (
        jnp.einsum("qhd,khd->hqk", query_part, key_full, preferred_element_type=jnp.float32)
        * score_scale
    )
    key_pos = jnp.arange(key_full.shape[0], dtype=jnp.int32)
    row_pos = row_start + jnp.arange(block_rows, dtype=jnp.int32)
    allowed = key_pos[None, :] <= row_pos[:, None]
    return jnp.where(allowed[None], scores, -1e30)


def attend_forward(query_rows_all, key_full, value_full):
    sequence_length = query_rows_all.shape[0]
    block_rows = min(512, sequence_length)

    def one_block(block_index):
        row_start = block_index * block_rows
        query_part = lax.dynamic_slice_in_dim(query_rows_all, row_start, block_rows, 0)
        scores = causal_scores(query_part, key_full, row_start)
        row_max = jnp.max(scores, axis=-1, keepdims=True)
        weights = jnp.exp(scores - row_max)
        row_total = jnp.sum(weights, axis=-1, keepdims=True)
        prob_low = (weights / row_total).astype(jnp.bfloat16)
        mixed_out = jnp.einsum(
            "hqk,khd->qhd", prob_low, value_full, preferred_element_type=jnp.float32
        )
        return (mixed_out.astype(jnp.bfloat16), (row_max + jnp.log(row_total))[..., 0])

    mixed_out, log_total = lax.map(
        one_block, jnp.arange(sequence_length // block_rows, dtype=jnp.int32)
    )
    return (mixed_out.reshape(query_rows_all.shape), log_total)


def attend_backward(query_rows_all, key_full, value_full, log_total, d_mixed):
    sequence_length = query_rows_all.shape[0]
    block_rows = min(512, sequence_length)
    score_scale = 1.0 / math.sqrt(query_rows_all.shape[2])

    def one_block(running, block_index):
        d_key_sum, d_value_sum = running
        row_start = block_index * block_rows
        query_part = lax.dynamic_slice_in_dim(query_rows_all, row_start, block_rows, 0)
        d_part = lax.dynamic_slice_in_dim(d_mixed, row_start, block_rows, 0)
        scores = causal_scores(query_part, key_full, row_start)
        prob_full = jnp.exp(scores - log_total[block_index][..., None])
        prob_low = prob_full.astype(jnp.bfloat16)
        d_probs = jnp.einsum("qhd,khd->hqk", d_part, value_full, preferred_element_type=jnp.float32)
        row_delta = jnp.sum(prob_full * d_probs, axis=-1, keepdims=True)
        d_scores = (prob_full * (d_probs - row_delta)).astype(jnp.bfloat16)
        d_query_part = (
            jnp.einsum("hqk,khd->qhd", d_scores, key_full, preferred_element_type=jnp.float32)
            * score_scale
        )
        d_key_sum = (
            d_key_sum
            + jnp.einsum("hqk,qhd->khd", d_scores, query_part, preferred_element_type=jnp.float32)
            * score_scale
        )
        d_value_sum = d_value_sum + jnp.einsum(
            "hqk,qhd->khd", prob_low, d_part, preferred_element_type=jnp.float32
        )
        return ((d_key_sum, d_value_sum), d_query_part)

    zero_grad = jnp.zeros(key_full.shape, jnp.float32)
    (d_key_sum, d_value_sum), d_query = lax.scan(
        one_block,
        (zero_grad, zero_grad),
        jnp.arange(sequence_length // block_rows, dtype=jnp.int32),
    )
    return (d_query.reshape(query_rows_all.shape), d_key_sum, d_value_sum)


def routed_body(
    tokens,
    query_key_value_weight,
    w_out_t,
    w_router,
    w_in,
    w_down,
    attn_gain,
    ffn_gain,
    q_gain,
    k_gain,
    routes,
    cotangent,
):
    sequence_count = lax.axis_size("seq")
    shard_count = lax.axis_size("fsdp")
    experts = sequence_count * shard_count
    token_row_count = tokens.shape[1]
    model_width = tokens.shape[2]
    query_group_width = QUERY_HEADS // KEY_VALUE_HEADS
    capacity = 2 * token_row_count * TOPK // experts
    slot_shape = (sequence_count, shard_count, capacity, model_width)
    positions = lax.axis_index("seq") * token_row_count + jnp.arange(
        token_row_count, dtype=jnp.int32
    )
    full_qkv, full_out, full_router = (
        lax.all_gather(query_key_value_weight, ("seq", "fsdp"), axis=0, tiled=True),
        lax.all_gather(w_out_t, ("seq", "fsdp"), axis=0, tiled=True),
        lax.all_gather(w_router, ("seq", "fsdp"), axis=0, tiled=True),
    )
    resid_in = tokens[0].astype(jnp.float32)
    normed_one = rms_scale(resid_in, attn_gain).astype(jnp.bfloat16)
    projection_output = jnp.dot(normed_one, full_qkv, preferred_element_type=jnp.float32)
    q_raw = projection_output[:, : QUERY_HEADS * HEAD_DIMENSION].reshape(
        token_row_count, QUERY_HEADS, HEAD_DIMENSION
    )
    key_unnormed = projection_output[
        :, QUERY_HEADS * HEAD_DIMENSION : (QUERY_HEADS + KEY_VALUE_HEADS) * HEAD_DIMENSION
    ].reshape(token_row_count, KEY_VALUE_HEADS, HEAD_DIMENSION)
    value_per_head = (
        projection_output[:, (QUERY_HEADS + KEY_VALUE_HEADS) * HEAD_DIMENSION :]
        .reshape(token_row_count, KEY_VALUE_HEADS, HEAD_DIMENSION)
        .astype(jnp.bfloat16)
    )
    prepare = partial(head_prepare, positions=positions)
    query_rows_all = prepare(q_raw, q_gain).astype(jnp.bfloat16)
    key_per_head = prepare(key_unnormed, k_gain).astype(jnp.bfloat16)
    send_keys = jnp.repeat(key_per_head, query_group_width, axis=1)
    send_values = jnp.repeat(value_per_head, query_group_width, axis=1)
    head_queries, head_keys, head_values = (
        lax.all_to_all(query_rows_all, "seq", split_axis=1, concat_axis=0, tiled=True),
        lax.all_to_all(send_keys, "seq", split_axis=1, concat_axis=0, tiled=True),
        lax.all_to_all(send_values, "seq", split_axis=1, concat_axis=0, tiled=True),
    )
    mixed_heads, log_total = attend_forward(head_queries, head_keys, head_values)
    mixed_tok = lax.all_to_all(mixed_heads, "seq", split_axis=0, concat_axis=1, tiled=True)
    attention_result = mixed_tok.reshape(token_row_count, QUERY_HEADS * HEAD_DIMENSION)
    attn_out = jnp.einsum(
        "tj,dj->td", attention_result, full_out, preferred_element_type=jnp.float32
    )
    hidden = resid_in + attn_out
    normed_two = rms_scale(hidden, ffn_gain).astype(jnp.bfloat16)
    logits = jnp.dot(normed_two, full_router, preferred_element_type=jnp.float32)
    route_flat = routes[0].reshape(-1)
    onehot, slot_index = route_slots(route_flat, experts)
    onehot_float = onehot.reshape(token_row_count, TOPK, experts).astype(jnp.float32)
    chosen = jnp.sum(onehot_float * logits[:, None, :], axis=-1)
    row_max = jnp.max(chosen, axis=-1, keepdims=True)
    exp_part = jnp.exp(chosen - row_max)
    gate_probs = exp_part / jnp.sum(exp_part, axis=-1, keepdims=True)
    send_rows = pack_slots(jnp.repeat(normed_two, TOPK, axis=0), route_flat, slot_index, slot_shape)
    arrived = lax.all_to_all(
        lax.all_to_all(send_rows, "seq", split_axis=0, concat_axis=0, tiled=True),
        "fsdp",
        split_axis=1,
        concat_axis=1,
        tiled=True,
    )
    rows_in = arrived.reshape(-1, model_width)
    gate_weight = w_in[0]
    down_weight = w_down[0]
    gate_up = jnp.dot(rows_in, gate_weight, preferred_element_type=jnp.float32)
    gate_half = gate_up[:, :FF]
    up_half = gate_up[:, FF:]
    gate_sig = jax.nn.sigmoid(gate_half)
    silu_gate = gate_half * gate_sig
    inner_act = (silu_gate * up_half).astype(jnp.bfloat16)
    expert_out = jnp.dot(inner_act, down_weight, preferred_element_type=jnp.float32).astype(
        jnp.bfloat16
    )
    returned = lax.all_to_all(
        lax.all_to_all(
            expert_out.reshape(slot_shape), "seq", split_axis=0, concat_axis=0, tiled=True
        ),
        "fsdp",
        split_axis=1,
        concat_axis=1,
        tiled=True,
    )
    picked = (
        unpack_slots(returned, route_flat, slot_index)
        .astype(jnp.float32)
        .reshape(token_row_count, TOPK, model_width)
    )
    mixture = jnp.sum(gate_probs[..., None] * picked, axis=1)
    output = (hidden + mixture).astype(jnp.bfloat16)
    full_qkv, full_out, full_router = (
        lax.all_gather(query_key_value_weight, ("seq", "fsdp"), axis=0, tiled=True),
        lax.all_gather(w_out_t, ("seq", "fsdp"), axis=0, tiled=True),
        lax.all_gather(w_router, ("seq", "fsdp"), axis=0, tiled=True),
    )
    out_grad = cotangent[0].astype(jnp.float32)
    d_picked = (
        (gate_probs[..., None] * out_grad[:, None, :]).astype(jnp.bfloat16).reshape(-1, model_width)
    )
    d_gates = jnp.sum(picked * out_grad[:, None, :], axis=-1)
    d_send = pack_slots(d_picked, route_flat, slot_index, slot_shape)
    d_arrived = lax.all_to_all(
        lax.all_to_all(d_send, "seq", split_axis=0, concat_axis=0, tiled=True),
        "fsdp",
        split_axis=1,
        concat_axis=1,
        tiled=True,
    ).reshape(-1, model_width)
    d_inner = jnp.einsum("rd,fd->rf", d_arrived, down_weight, preferred_element_type=jnp.float32)
    d_gate_half = d_inner * up_half * gate_sig * (1.0 + gate_half * (1.0 - gate_sig))
    d_up_half = d_inner * silu_gate
    d_gate_up = jnp.concatenate([d_gate_half, d_up_half], axis=1).astype(jnp.bfloat16)
    d_w_down = jnp.einsum("rf,rd->fd", inner_act, d_arrived, preferred_element_type=jnp.float32)[
        None
    ]
    d_w_in = jnp.einsum("rd,rf->df", rows_in, d_gate_up, preferred_element_type=jnp.float32)[None]
    d_rows = jnp.einsum(
        "rf,df->rd", d_gate_up, gate_weight, preferred_element_type=jnp.float32
    ).astype(jnp.bfloat16)
    d_back = lax.all_to_all(
        lax.all_to_all(d_rows.reshape(slot_shape), "seq", split_axis=0, concat_axis=0, tiled=True),
        "fsdp",
        split_axis=1,
        concat_axis=1,
        tiled=True,
    )
    d_routed = jnp.sum(
        unpack_slots(d_back, route_flat, slot_index)
        .astype(jnp.float32)
        .reshape(token_row_count, TOPK, model_width),
        axis=1,
    )
    d_chosen = gate_probs * (d_gates - jnp.sum(gate_probs * d_gates, axis=-1, keepdims=True))
    d_logits = jnp.einsum("tk,tke->te", d_chosen, onehot_float).astype(jnp.bfloat16)
    d_normed_two = d_routed + jnp.einsum(
        "te,de->td", d_logits, full_router, preferred_element_type=jnp.float32
    )
    unused_two, pull_two = jax.vjp(rms_scale, hidden, ffn_gain)
    d_hidden_norm, d_ffn_gain = pull_two(d_normed_two)
    d_hidden = out_grad + d_hidden_norm
    d_attn = d_hidden.astype(jnp.bfloat16)
    d_attended = jnp.einsum(
        "td,dj->tj", d_attn, full_out, preferred_element_type=jnp.float32
    ).astype(jnp.bfloat16)
    d_heads = lax.all_to_all(
        d_attended.reshape(token_row_count, QUERY_HEADS, HEAD_DIMENSION),
        "seq",
        split_axis=1,
        concat_axis=0,
        tiled=True,
    )
    d_query, d_key_sum, d_value_sum = attend_backward(
        head_queries, head_keys, head_values, log_total, d_heads
    )
    seq_rows = head_queries.shape[0]
    local_cols = head_queries.shape[1] * HEAD_DIMENSION
    normed_all, d_attn_all = (
        lax.all_gather(normed_one, "seq", axis=0, tiled=True),
        lax.all_gather(d_attn, "seq", axis=0, tiled=True),
    )
    query_cols = lax.dynamic_slice_in_dim(
        full_qkv, lax.axis_index("seq") * local_cols, local_cols, 1
    )
    q_head_raw = jnp.dot(normed_all, query_cols, preferred_element_type=jnp.float32).reshape(
        head_queries.shape
    )
    seq_positions = jnp.arange(seq_rows, dtype=jnp.int32)
    unused_head, pull_head = jax.vjp(
        partial(head_prepare, positions=seq_positions), q_head_raw, q_gain
    )
    send_d_query, d_q_gain = pull_head(d_query)
    d_query_tok, grad_key_token_rows, grad_value_token_rows = (
        lax.all_to_all(
            send_d_query.astype(jnp.bfloat16), "seq", split_axis=0, concat_axis=1, tiled=True
        ).astype(send_d_query.dtype),
        lax.all_to_all(
            d_key_sum.astype(jnp.bfloat16), "seq", split_axis=0, concat_axis=1, tiled=True
        ).astype(d_key_sum.dtype),
        lax.all_to_all(
            d_value_sum.astype(jnp.bfloat16), "seq", split_axis=0, concat_axis=1, tiled=True
        ).astype(d_value_sum.dtype),
    )
    grad_key_per_head = jnp.sum(
        grad_key_token_rows.reshape(token_row_count, KEY_VALUE_HEADS, -1, HEAD_DIMENSION), axis=2
    )
    grad_value_per_head = jnp.sum(
        grad_value_token_rows.reshape(token_row_count, KEY_VALUE_HEADS, -1, HEAD_DIMENSION), axis=2
    )
    unused_k, pull_k = jax.vjp(prepare, key_unnormed, k_gain)
    grad_key_unnormed, d_k_gain = pull_k(grad_key_per_head)
    d_projected = jnp.concatenate(
        [
            d_query_tok.reshape(token_row_count, QUERY_HEADS * HEAD_DIMENSION),
            grad_key_unnormed.reshape(token_row_count, KEY_VALUE_HEADS * HEAD_DIMENSION),
            grad_value_per_head.reshape(token_row_count, KEY_VALUE_HEADS * HEAD_DIMENSION),
        ],
        axis=1,
    ).astype(jnp.bfloat16)
    d_normed_one = jnp.einsum(
        "tj,dj->td", d_projected, full_qkv, preferred_element_type=jnp.float32
    )
    unused_one, pull_one = jax.vjp(rms_scale, resid_in, attn_gain)
    d_resid_norm, d_attn_gain = pull_one(d_normed_one)
    d_tokens = (d_hidden + d_resid_norm).astype(jnp.bfloat16)[None]
    rows_dev = model_width // experts
    kv_count = 2 * KEY_VALUE_HEADS * HEAD_DIMENSION
    kv_grads = d_projected[:, QUERY_HEADS * HEAD_DIMENSION :]
    first_rows = normed_one
    summed = lax.psum_scatter(
        jnp.concatenate(
            [
                jnp.einsum("tc,tj->cj", first_rows, kv_grads, preferred_element_type=jnp.float32),
                jnp.einsum("tc,te->ce", normed_two, d_logits, preferred_element_type=jnp.float32),
            ],
            axis=1,
        ),
        ("seq", "fsdp"),
        scatter_dimension=0,
        tiled=True,
    )
    d_query_low = send_d_query.reshape(seq_rows, local_cols).astype(jnp.bfloat16)
    attended_heads = mixed_heads.reshape(seq_rows, local_cols)
    normed_order = (
        normed_all.reshape(seq_rows, sequence_count, shard_count, rows_dev)
        .transpose(0, 2, 1, 3)
        .reshape(seq_rows, model_width)
    )
    d_attn_order = (
        d_attn_all.reshape(seq_rows, sequence_count, shard_count, rows_dev)
        .transpose(0, 2, 1, 3)
        .reshape(seq_rows, model_width)
    )
    first_rows = normed_order
    head_sums = lax.psum_scatter(
        jnp.concatenate(
            [
                jnp.einsum(
                    "tc,tj->cj", first_rows, d_query_low, preferred_element_type=jnp.float32
                ),
                jnp.einsum(
                    "tc,tj->cj", d_attn_order, attended_heads, preferred_element_type=jnp.float32
                ),
            ],
            axis=1,
        ).astype(jnp.bfloat16),
        "fsdp",
        scatter_dimension=0,
        tiled=True,
    ).astype(jnp.float32)
    row_sums = (
        lax.all_to_all(
            head_sums.astype(jnp.bfloat16), "seq", split_axis=0, concat_axis=1, tiled=True
        )
        .astype(head_sums.dtype)
        .reshape(rows_dev, sequence_count, 2, local_cols)
    )
    d_w_query = row_sums[:, :, 0].reshape(rows_dev, QUERY_HEADS * HEAD_DIMENSION)
    d_w_out_t = row_sums[:, :, 1].reshape(rows_dev, QUERY_HEADS * HEAD_DIMENSION)
    d_w_qkv = jnp.concatenate([d_w_query, summed[:, :kv_count]], axis=1)
    d_w_router = summed[:, kv_count:]
    d_attn_gain, d_ffn_gain, d_q_gain, d_k_gain = lax.psum(
        (d_attn_gain, d_ffn_gain, d_q_gain, d_k_gain), ("seq", "fsdp")
    )
    return (
        output[None],
        d_tokens,
        d_w_qkv,
        d_w_out_t,
        d_w_router,
        d_w_in,
        d_w_down,
        d_attn_gain,
        d_ffn_gain,
        d_q_gain,
        d_k_gain,
    )


MESH = pl.DeviceIdType.MESH
VMEM_LIMIT = 60 * 2**20


class Place:
    def __init__(self):
        seq, shard = lax.axis_index("seq"), lax.axis_index("fsdp")
        self.z, self.x = seq // 2, seq % 2
        self.y, self.c = shard // 2, shard % 2
        self.z0, self.z1 = self.z % 2, self.z // 2
        self.low, self.high = self.z == 0, self.z == 3
        self.inner = (self.z0 + self.z1) == 1
        self.me = self.block(self.z, self.x, self.y, self.c)

    def device(self, z, x, y, c):
        return (z * 2 + x, y * 2 + c)

    def block(self, z, x, y, c):
        return (z * 2 + x) * 4 + y * 2 + c

    @property
    def by_x(self):
        return self.device(self.z, 1 - self.x, self.y, self.c)

    @property
    def by_y(self):
        return self.device(self.z, self.x, 1 - self.y, self.c)

    @property
    def by_core(self):
        return self.device(self.z, self.x, self.y, 1 - self.c)

    def by_z(self, step):
        return self.device(self.z + step, self.x, self.y, self.c)

    def near(self, k):
        return [self.z, 1 + self.z0, 2 - 2 * self.z0 + self.z1, 3 - 3 * self.z1][k]

    def onward(self, k):
        return [None, 2 * self.z1 - 1, 1 - 2 * self.z1, 2 * self.z1 - 1][k]

    def far(self, k):
        return self.near(3 - k)

    def toward(self, k):
        return [1 - 2 * self.z1, 1 - 2 * self.z0, 1 - 2 * self.z1][k]

    def greet(self, sides):
        barrier = pltpu.get_barrier_semaphore()
        for side in sides:
            if side != "z":
                target = {"x": self.by_x, "y": self.by_y, "core": self.by_core}[side]
                pl.semaphore_signal(barrier, inc=1, device_id=target, device_id_type=MESH)
        count = len([side for side in sides if side != "z"])
        if "z" in sides:

            @pl.when(jnp.logical_not(self.low))
            def _():
                pl.semaphore_signal(barrier, inc=1, device_id=self.by_z(-1), device_id_type=MESH)

            @pl.when(jnp.logical_not(self.high))
            def _():
                pl.semaphore_signal(barrier, inc=1, device_id=self.by_z(1), device_id_type=MESH)

            count = count + 1 + (self.z0 + self.z1) % 2
        pl.semaphore_wait(barrier, count)


def send(source, target, send_sem, recv_sem, device):
    pltpu.make_async_remote_copy(
        src_ref=source,
        dst_ref=target,
        send_sem=send_sem,
        recv_sem=recv_sem,
        device_id=device,
        device_id_type=MESH,
    ).start()


def await_bytes(ref, sem):
    pltpu.make_async_copy(ref, ref, sem).wait()


G_Z, G_X, G_Y, G_DX, G_DY, G_C0 = 0, 1, 2, 3, 4, 5
G_KINDS = 9


def gather_steps(place, own, out, ss, rs, zs, local_sem):
    p = place
    rows = out.shape[1]
    half = rows // 2
    x, y, c = p.x, p.y, p.c

    def cols(q):
        return [
            p.block(q, x, y, c),
            p.block(q, 1 - x, y, c),
            p.block(q, x, 1 - y, c),
            p.block(q, 1 - x, 1 - y, c),
        ]

    def to_core(q, j, src=None):
        b = cols(q)[j]
        send(out.at[b] if src is None else src, out.at[b], ss.at[q, G_C0 + j], rs.at[q, G_C0 + j], p.by_core)

    def plane_out(k):
        q = p.near(k)
        b = cols(q)[0]
        if k == 0:
            src = own
            for step, there in ((1, p.high), (-1, p.low)):

                @pl.when(jnp.logical_not(there))
                def _():
                    send(src, out.at[b], zs.at[q, 0 if step > 0 else 1], rs.at[q, G_Z], p.by_z(step))

            pltpu.make_async_copy(own, out.at[b], local_sem).start()
        else:
            src = out.at[b]
            await_bytes(src, rs.at[q, G_Z])

            @pl.when(p.inner)
            def _():
                send(src, src, zs.at[q, 0], rs.at[q, G_Z], p.by_z(p.onward(k)))

        send(src, out.at[b], ss.at[q, G_X], rs.at[q, G_X], p.by_x)
        send(src, out.at[b], ss.at[q, G_Y], rs.at[q, G_Y], p.by_y)
        to_core(q, 0, src)

    def plane_turn(k):
        q = p.near(k)
        bx, by = out.at[cols(q)[1]], out.at[cols(q)[2]]
        await_bytes(bx, rs.at[q, G_X])
        first = bx.at[pl.ds(0, half)]
        send(first, first, ss.at[q, G_DY], rs.at[q, G_DY], p.by_y)
        to_core(q, 1)
        await_bytes(by, rs.at[q, G_Y])
        second = by.at[pl.ds(half, half)]
        send(second, second, ss.at[q, G_DX], rs.at[q, G_DX], p.by_x)
        to_core(q, 2)

    def plane_end(k):
        q = p.near(k)
        bd = out.at[cols(q)[3]]
        await_bytes(bd.at[pl.ds(0, half)], rs.at[q, G_DY])
        await_bytes(bd.at[pl.ds(half, half)], rs.at[q, G_DX])
        to_core(q, 3)

    def plane_core(k):
        q = p.near(k)
        for j in range(4):
            await_bytes(own, rs.at[q, G_C0 + j])

    def finish():
        pltpu.make_async_copy(own, out.at[cols(p.z)[0]], local_sem).wait()
        piece = own.at[pl.ds(0, half)]
        for q in range(4):
            for kind in (G_X, G_Y, G_C0, G_C0 + 1, G_C0 + 2, G_C0 + 3):
                await_bytes(own, ss.at[q, kind])
            for kind in (G_DX, G_DY):
                await_bytes(piece, ss.at[q, kind])
        for there, slot in ((p.high, 0), (p.low, 1)):

            @pl.when(jnp.logical_not(there))
            def _():
                await_bytes(own, zs.at[p.z, slot])

        for k in range(1, 4):

            @pl.when(p.inner)
            def _():
                await_bytes(own, zs.at[p.near(k), 0])

    return plane_out, plane_turn, plane_end, plane_core, finish


def gather_all_kernel(own, out, ss, rs, zs, local_sem):
    p = Place()
    p.greet(("x", "y", "core", "z"))
    plane_out, plane_turn, plane_end, plane_core, finish = gather_steps(p, own, out, ss, rs, zs, local_sem)
    plane_out(0)
    plane_out(1)
    plane_turn(0)
    plane_out(2)
    plane_end(0)
    plane_turn(1)
    plane_out(3)
    plane_end(1)
    plane_turn(2)
    plane_end(2)
    plane_turn(3)
    plane_end(3)
    for k in range(4):
        plane_core(k)
    finish()


def gather_all(own, blocks, collective_id):
    dma = pltpu.SemaphoreType.DMA
    return pl.pallas_call(
        gather_all_kernel,
        out_shape=jax.ShapeDtypeStruct((blocks, *own.shape), own.dtype),
        in_specs=[pl.BlockSpec(memory_space=pl.ANY)],
        out_specs=pl.BlockSpec(memory_space=pl.ANY),
        scratch_shapes=[dma((4, G_KINDS)), dma((4, G_KINDS)), dma((4, 2)), dma],
        compiler_params=pltpu.CompilerParams(
            collective_id=collective_id, has_side_effects=True, vmem_limit_bytes=VMEM_LIMIT
        ),
        name="gather_all",
    )(own)


def sum_all_parts(p, part, held, core_in, x_half, y_half, x_in, y_in, z_in, out, ls, cs, cr, ss, rs, zs, zr):
    rows, width = part.shape[1], part.shape[2]
    half = rows // 2
    x, y, c = p.x, p.y, p.c

    def columns(q):
        return [(q, x, y), (q, 1 - x, y), (q, x, 1 - y), (q, 1 - x, 1 - y)]

    def start():
        for k in range(4):
            q = p.far(k)
            for j, (zz, xx, yy) in reversed(list(enumerate(columns(q)))):
                send(
                    part.at[p.block(zz, xx, yy, 1 - c)],
                    core_in.at[q * 4 + j],
                    cs.at[q, j],
                    cr.at[q, j],
                    p.by_core,
                )
                pltpu.make_async_copy(
                    part.at[p.block(zz, xx, yy, c)], held.at[q * 4 + j], ls.at[q, j]
                ).start()

    chunk = 16

    def add(target, source, count):
        @pl.loop(0, count // chunk)
        def _(i):
            at = pl.ds(pl.multiple_of(i * chunk, chunk), chunk)
            target[at, :] = (
                target[at, :].astype(jnp.float32) + source[at, :].astype(jnp.float32)
            ).astype(target.dtype)

    def plane_core(k, js=(3, 1, 2, 0)):
        q = p.far(k)
        for j in js:
            slot = q * 4 + j
            await_bytes(held.at[slot], ls.at[q, j])
            await_bytes(core_in.at[slot], cr.at[q, j])
            add(held.at[slot], core_in.at[slot], rows)
            if j == 3:
                send(held.at[slot, pl.ds(0, half)], y_half.at[q], ss.at[q, 0], rs.at[q, 0], p.by_y)
                send(held.at[slot, pl.ds(half, half)], x_half.at[q], ss.at[q, 1], rs.at[q, 1], p.by_x)

    def plane_turn(k):
        q = p.far(k)
        await_bytes(y_half.at[q], rs.at[q, 0])
        add(held.at[q * 4 + 1, pl.ds(0, half)], y_half.at[q], half)
        send(held.at[q * 4 + 1], x_in.at[q], ss.at[q, 2], rs.at[q, 2], p.by_x)
        await_bytes(x_half.at[q], rs.at[q, 1])
        add(held.at[q * 4 + 2, pl.ds(half, half)], x_half.at[q], half)
        send(held.at[q * 4 + 2], y_in.at[q], ss.at[q, 3], rs.at[q, 3], p.by_y)

    def plane_end(k):
        q = p.far(k)
        mine = held.at[q * 4]
        await_bytes(x_in.at[q], rs.at[q, 2])
        add(mine, x_in.at[q], rows)
        await_bytes(y_in.at[q], rs.at[q, 3])
        add(mine, y_in.at[q], rows)
        if k < 3:
            step = p.toward(k)
            slot = (1 - step) // 2

            @pl.when(p.inner)
            def _():
                await_bytes(z_in.at[slot, q], zr.at[slot, q])
                add(mine, z_in.at[slot, q], rows)

            send(mine, z_in.at[slot, q], zs.at[k], zr.at[slot, q], p.by_z(step))
        else:
            for slot, there in ((0, p.low), (1, p.high)):

                @pl.when(jnp.logical_not(there))
                def _():
                    await_bytes(z_in.at[slot, q], zr.at[slot, q])
                    add(mine, z_in.at[slot, q], rows)

            out[...] = mine[...]

    def finish():
        whole, piece = x_in.at[0], x_half.at[0]
        for q in range(4):
            for j in range(4):
                await_bytes(whole, cs.at[q, j])
            for kind in (0, 1):
                await_bytes(piece, ss.at[q, kind])
            for kind in (2, 3):
                await_bytes(whole, ss.at[q, kind])
        for k in range(3):
            await_bytes(whole, zs.at[k])

    return start, plane_core, plane_turn, plane_end, finish


def sum_all_kernel(part, out, *scratch):
    p = Place()
    p.greet(("x", "y", "core", "z"))
    start, plane_core, plane_turn, plane_end, finish = sum_all_parts(p, part, *scratch[:7], out, *scratch[7:])
    start()
    plane_core(0)
    plane_core(1)
    plane_turn(0)
    plane_core(2)
    plane_turn(1)
    plane_end(0)
    plane_core(3)
    plane_turn(2)
    plane_end(1)
    plane_turn(3)
    plane_end(2)
    plane_end(3)
    finish()


def sum_all_scratch(rows, width):
    dma = pltpu.SemaphoreType.DMA
    bf16 = jnp.bfloat16
    return [
        pltpu.VMEM((16, rows, width), bf16),
        pltpu.VMEM((16, rows, width), bf16),
        pltpu.VMEM((4, rows // 2, width), bf16),
        pltpu.VMEM((4, rows // 2, width), bf16),
        pltpu.VMEM((4, rows, width), bf16),
        pltpu.VMEM((4, rows, width), bf16),
        pltpu.VMEM((2, 4, rows, width), bf16),
        dma((4, 4)),
        dma((4, 4)),
        dma((4, 4)),
        dma((4, 4)),
        dma((4, 4)),
        dma((3,)),
        dma((2, 4)),
    ]


def sum_all(part, collective_id):
    blocks, rows, width = part.shape
    return pl.pallas_call(
        sum_all_kernel,
        out_shape=jax.ShapeDtypeStruct((rows, width), part.dtype),
        in_specs=[pl.BlockSpec(memory_space=pl.ANY)],
        out_specs=pl.BlockSpec(memory_space=pltpu.VMEM),
        scratch_shapes=sum_all_scratch(rows, width),
        compiler_params=pltpu.CompilerParams(
            collective_id=collective_id, has_side_effects=True, vmem_limit_bytes=VMEM_LIMIT
        ),
        name="sum_all",
    )(part)


def gather_seq_kernel(own, out, ss, rs, zs, local_sem):
    p = Place()
    p.greet(("x", "z"))

    def at(q, x):
        return out.at[q * 2 + x]

    def plane_out(k):
        q = p.near(k)
        there = at(q, p.x)
        if k == 0:
            src = own
            for step, end in ((1, p.high), (-1, p.low)):

                @pl.when(jnp.logical_not(end))
                def _():
                    send(src, there, zs.at[q, 0 if step > 0 else 1], rs.at[q, 0], p.by_z(step))

            pltpu.make_async_copy(own, there, local_sem).start()
        else:
            src = there
            await_bytes(src, rs.at[q, 0])

            @pl.when(p.inner)
            def _():
                send(src, src, zs.at[q, 0], rs.at[q, 0], p.by_z(p.onward(k)))

        send(src, there, ss.at[q], rs.at[q, 1], p.by_x)

    for k in range(4):
        plane_out(k)
    for k in range(4):
        await_bytes(own, rs.at[p.near(k), 1])
    pltpu.make_async_copy(own, at(p.z, p.x), local_sem).wait()
    for q in range(4):
        await_bytes(own, ss.at[q])
    for there, slot in ((p.high, 0), (p.low, 1)):

        @pl.when(jnp.logical_not(there))
        def _():
            await_bytes(own, zs.at[p.z, slot])

    for k in range(1, 4):

        @pl.when(p.inner)
        def _():
            await_bytes(own, zs.at[p.near(k), 0])


def gather_seq(own, collective_id):
    dma = pltpu.SemaphoreType.DMA
    return pl.pallas_call(
        gather_seq_kernel,
        out_shape=jax.ShapeDtypeStruct((8, *own.shape), own.dtype),
        in_specs=[pl.BlockSpec(memory_space=pl.ANY)],
        out_specs=pl.BlockSpec(memory_space=pl.ANY),
        scratch_shapes=[dma((4,)), dma((4, 2)), dma((4, 2)), dma],
        compiler_params=pltpu.CompilerParams(
            collective_id=collective_id, has_side_effects=True, vmem_limit_bytes=VMEM_LIMIT
        ),
        name="gather_seq",
    )(own)


def add_rows(target, source, count, chunk=16):
    @pl.loop(0, count // chunk)
    def _(i):
        at = pl.ds(pl.multiple_of(i * chunk, chunk), chunk)
        target[at, :] = (
            target[at, :].astype(jnp.float32) + source[at, :].astype(jnp.float32)
        ).astype(target.dtype)


def sum_seq_kernel(part, out, held, x_in, z_in, ls, ss, rs, zs, zr):
    p = Place()
    p.greet(("x", "z"))
    rows = part.shape[1]
    for k in range(4):
        q = p.far(k)
        send(part.at[q * 2 + 1 - p.x], x_in.at[q], ss.at[q], rs.at[q], p.by_x)
        pltpu.make_async_copy(part.at[q * 2 + p.x], held.at[q], ls.at[q]).start()
    for k in range(4):
        q = p.far(k)
        mine = held.at[q]
        await_bytes(mine, ls.at[q])
        await_bytes(x_in.at[q], rs.at[q])
        add_rows(mine, x_in.at[q], rows)
        if k < 3:
            step = p.toward(k)
            slot = (1 - step) // 2

            @pl.when(p.inner)
            def _():
                await_bytes(z_in.at[slot, q], zr.at[slot, q])
                add_rows(mine, z_in.at[slot, q], rows)

            send(mine, z_in.at[slot, q], zs.at[k], zr.at[slot, q], p.by_z(step))
        else:
            for slot, there in ((0, p.low), (1, p.high)):

                @pl.when(jnp.logical_not(there))
                def _():
                    await_bytes(z_in.at[slot, q], zr.at[slot, q])
                    add_rows(mine, z_in.at[slot, q], rows)

            out[...] = mine[...]
    for q in range(4):
        await_bytes(x_in.at[0], ss.at[q])
    for k in range(3):
        await_bytes(x_in.at[0], zs.at[k])


def sum_seq(part, collective_id):
    _, rows, width = part.shape
    dma = pltpu.SemaphoreType.DMA
    bf16 = jnp.bfloat16
    return pl.pallas_call(
        sum_seq_kernel,
        out_shape=jax.ShapeDtypeStruct((rows, width), part.dtype),
        in_specs=[pl.BlockSpec(memory_space=pl.ANY)],
        out_specs=pl.BlockSpec(memory_space=pltpu.VMEM),
        scratch_shapes=[
            pltpu.VMEM((4, rows, width), bf16),
            pltpu.VMEM((4, rows, width), bf16),
            pltpu.VMEM((2, 4, rows, width), bf16),
            dma((4,)),
            dma((4,)),
            dma((4,)),
            dma((3,)),
            dma((2, 4)),
        ],
        compiler_params=pltpu.CompilerParams(
            collective_id=collective_id, has_side_effects=True, vmem_limit_bytes=VMEM_LIMIT
        ),
        name="sum_seq",
    )(part)


def head_columns(weight, group_index):
    rows = weight.shape[0]
    query_width = QUERY_HEADS * HEAD_DIMENSION
    key_width = KEY_VALUE_HEADS * HEAD_DIMENSION
    query = weight[:, :query_width].reshape(rows, len(group_index), -1).transpose(1, 0, 2)
    keys = weight[:, query_width : query_width + key_width].reshape(rows, KEY_VALUE_HEADS, -1)
    values = weight[:, query_width + key_width :].reshape(rows, KEY_VALUE_HEADS, -1)
    keys = jnp.stack([keys[:, group] for group in group_index])
    values = jnp.stack([values[:, group] for group in group_index])
    return jnp.concatenate([query, keys, values], axis=2)


def gathered_body(
    tokens,
    query_key_value_weight,
    w_out_t,
    w_router,
    w_in,
    w_down,
    attn_gain,
    ffn_gain,
    q_gain,
    k_gain,
    routes,
    cotangent,
):
    bf16, f32 = jnp.bfloat16, jnp.float32
    both = ("seq", "fsdp")
    seq_size = lax.axis_size("seq")
    shard_size = lax.axis_size("fsdp")
    experts = seq_size * shard_size
    rows = tokens.shape[1]
    width = tokens.shape[2]
    length = rows * seq_size
    weight_rows = query_key_value_weight.shape[0]
    heads = QUERY_HEADS // seq_size
    head_cols = heads * HEAD_DIMENSION
    kv_cols = HEAD_DIMENSION
    proj_cols = head_cols + 2 * kv_cols
    all_cols = proj_cols + head_cols
    group_index = [s * heads * KEY_VALUE_HEADS // QUERY_HEADS for s in range(seq_size)]
    capacity = 2 * rows * TOPK // experts

    pieces = jnp.concatenate(
        [
            head_columns(query_key_value_weight, group_index),
            w_out_t.reshape(weight_rows, seq_size, head_cols).transpose(1, 0, 2),
        ],
        axis=2,
    )
    pieces = lax.all_to_all(pieces, "seq", split_axis=0, concat_axis=0, tiled=True)
    columns = lax.all_gather(pieces, "fsdp", axis=1).reshape(width, all_cols)
    proj_weight = columns[:, :proj_cols]
    out_weight = columns[:, proj_cols:]
    full_router = lax.all_gather(w_router, both, axis=0, tiled=True)
    cot_all = lax.all_gather(cotangent[0], both)

    resid_in = tokens[0].astype(f32)
    normed_one = rms_scale(resid_in, attn_gain).astype(bf16)
    normed_all = gather_seq(normed_one, 1).reshape(length, width)
    projected = jnp.dot(normed_all, proj_weight, preferred_element_type=f32)
    seq_positions = jnp.arange(length, dtype=jnp.int32)
    prepare = partial(head_prepare, positions=seq_positions)
    q_raw = projected[:, :head_cols].reshape(length, heads, HEAD_DIMENSION)
    k_raw = projected[:, head_cols : head_cols + kv_cols].reshape(length, 1, HEAD_DIMENSION)
    values = projected[:, head_cols + kv_cols :].astype(bf16).reshape(length, 1, HEAD_DIMENSION)
    queries = prepare(q_raw, q_gain).astype(bf16)
    keys = prepare(k_raw, k_gain).astype(bf16)
    repeat_keys = jnp.repeat(keys, heads, axis=1)
    repeat_values = jnp.repeat(values, heads, axis=1)
    mixed_heads, log_total = attend_forward(queries, repeat_keys, repeat_values)
    attended = mixed_heads.reshape(length, head_cols)
    attn_part = jnp.einsum("tj,dj->td", attended, out_weight, preferred_element_type=f32)
    attn_out = sum_seq(attn_part.astype(bf16).reshape(seq_size, rows, width), 2)
    hidden = resid_in + attn_out.astype(f32)
    normed_two = rms_scale(hidden, ffn_gain).astype(bf16)

    logits = jnp.dot(normed_two, full_router, preferred_element_type=f32)
    onehot = routes[0][:, :, None] == jnp.arange(experts, dtype=jnp.int32)
    onehot_float = onehot.astype(f32)
    named = jnp.sum(onehot_float, axis=1)
    chosen = jnp.sum(onehot_float * logits[:, None, :], axis=-1)
    row_max = jnp.max(chosen, axis=-1, keepdims=True)
    exp_part = jnp.exp(chosen - row_max)
    gate_probs = exp_part / jnp.sum(exp_part, axis=-1, keepdims=True)
    gate_dense = jnp.sum(onehot_float * gate_probs[..., None], axis=1)

    gate_high = gate_dense.astype(bf16)
    gate_low = (gate_dense - gate_high.astype(f32)).astype(bf16)
    route_info = jnp.concatenate([gate_high, gate_low, named.astype(bf16)], axis=1)
    route_info = jnp.pad(route_info, ((0, 0), (0, 128 - route_info.shape[1] % 128)))
    gathered = gather_all(jnp.concatenate([normed_two, route_info], axis=1), experts, 3)
    blocks = experts
    rows_all = gathered[:, :, :width]
    info = gathered[:, :, width : width + 3 * experts].reshape(blocks, rows, 3, experts)
    me = lax.axis_index("seq") * shard_size + lax.axis_index("fsdp")
    own = lax.dynamic_index_in_dim(info, me, 3, keepdims=False).astype(f32)
    gate_own = own[:, :, 0] + own[:, :, 1]
    named_own = own[:, :, 2]
    slot = jnp.cumsum(named_own, axis=1) - named_own
    pick = (
        (slot[:, None, :] == jnp.arange(capacity, dtype=f32)[None, :, None])
        & (named_own[:, None, :] > 0)
    ).astype(bf16)
    gate_slots = jnp.einsum(
        "bct,bt->bc", pick.astype(f32), gate_own, precision=lax.Precision.HIGHEST
    ).reshape(-1, 1)
    rows_in = jnp.einsum("bct,btd->bcd", pick, rows_all, preferred_element_type=f32)
    rows_in = rows_in.astype(bf16).reshape(-1, width)
    cot_rows = jnp.einsum(
        "bct,btd->bcd",
        pick,
        cot_all.reshape(blocks, rows, width),
        preferred_element_type=f32,
    ).reshape(-1, width)

    gate_weight = w_in[0]
    down_weight = w_down[0]
    gate_up = jnp.dot(rows_in, gate_weight, preferred_element_type=f32)
    gate_half = gate_up[:, :FF]
    up_half = gate_up[:, FF:]
    gate_sig = jax.nn.sigmoid(gate_half)
    silu_gate = gate_half * gate_sig
    inner_act = (silu_gate * up_half).astype(bf16)
    expert_out = (
        jnp.dot(inner_act, down_weight, preferred_element_type=f32).astype(bf16).astype(f32)
    )
    d_gate_slots = jnp.sum(expert_out * cot_rows, axis=1)
    weighted = (gate_slots * expert_out).astype(bf16).reshape(blocks, capacity, width)
    out_part = jnp.einsum("bct,bcd->btd", pick, weighted, preferred_element_type=f32)
    mixture = sum_all(out_part.astype(bf16), 4)
    output = (hidden + mixture.astype(f32)).astype(bf16)

    d_expert = (gate_slots * cot_rows).astype(bf16)
    d_inner = jnp.einsum("rd,fd->rf", d_expert, down_weight, preferred_element_type=f32)
    d_gate_half = d_inner * up_half * gate_sig * (1.0 + gate_half * (1.0 - gate_sig))
    d_up_half = d_inner * silu_gate
    d_gate_up = jnp.concatenate([d_gate_half, d_up_half], axis=1).astype(bf16)
    d_w_down = jnp.einsum("rf,rd->fd", inner_act, d_expert, preferred_element_type=f32)[None]
    d_w_in = jnp.einsum("rd,rf->df", rows_in, d_gate_up, preferred_element_type=f32)[None]
    d_rows = jnp.einsum("rf,df->rd", d_gate_up, gate_weight, preferred_element_type=f32)
    d_rows = d_rows.astype(bf16).reshape(blocks, capacity, width)
    d_gate_own = jnp.einsum(
        "bct,bc->bt",
        pick.astype(f32),
        d_gate_slots.reshape(blocks, capacity),
        precision=lax.Precision.HIGHEST,
    )
    d_gate_high = d_gate_own.astype(bf16)
    d_gate_low = (d_gate_own - d_gate_high.astype(f32)).astype(bf16)
    mine = (jnp.arange(experts, dtype=jnp.int32) == me).astype(bf16)
    d_info = jnp.concatenate([d_gate_high[..., None] * mine, d_gate_low[..., None] * mine], axis=2)
    d_info = jnp.pad(d_info, ((0, 0), (0, 0), (0, 128 - d_info.shape[2] % 128)))
    d_part = jnp.einsum("bct,bcd->btd", pick, d_rows, preferred_element_type=f32)
    d_part = jnp.concatenate([d_part.astype(bf16), d_info], axis=2)
    d_back = sum_all(d_part, 5).astype(f32)

    d_gate_dense = d_back[:, width : width + experts] + d_back[:, width + experts : width + 2 * experts]
    d_gates = jnp.sum(onehot_float * d_gate_dense[:, None, :], axis=-1)
    d_chosen = gate_probs * (d_gates - jnp.sum(gate_probs * d_gates, axis=-1, keepdims=True))
    d_logits = jnp.sum(d_chosen[..., None] * onehot_float, axis=1).astype(bf16)
    d_normed_two = d_back[:, :width] + jnp.einsum(
        "te,de->td", d_logits, full_router, preferred_element_type=f32
    )
    out_grad = cotangent[0].astype(f32)
    unused_two, pull_two = jax.vjp(rms_scale, hidden, ffn_gain)
    d_hidden_norm, d_ffn_gain = pull_two(d_normed_two)
    d_hidden = out_grad + d_hidden_norm
    d_attn = d_hidden.astype(bf16)

    d_attn_all = gather_seq(d_attn, 6).reshape(length, width)
    d_attended = jnp.dot(d_attn_all, out_weight, preferred_element_type=f32).astype(bf16)
    d_query, d_key_sum, d_value_sum = attend_backward(
        queries,
        repeat_keys,
        repeat_values,
        log_total,
        d_attended.reshape(length, heads, HEAD_DIMENSION),
    )
    unused_q, pull_q = jax.vjp(prepare, q_raw, q_gain)
    d_q_raw, d_q_gain = pull_q(d_query)
    unused_k, pull_k = jax.vjp(prepare, k_raw, k_gain)
    d_k_raw, d_k_gain = pull_k(jnp.sum(d_key_sum, axis=1, keepdims=True))
    d_projected = jnp.concatenate(
        [
            d_q_raw.reshape(length, head_cols),
            d_k_raw.reshape(length, kv_cols),
            jnp.sum(d_value_sum, axis=1),
        ],
        axis=1,
    ).astype(bf16)
    d_normed_part = jnp.einsum("tj,dj->td", d_projected, proj_weight, preferred_element_type=f32)
    d_normed_one = sum_seq(d_normed_part.astype(bf16).reshape(seq_size, rows, width), 7).astype(f32)
    unused_one, pull_one = jax.vjp(rms_scale, resid_in, attn_gain)
    d_resid_norm, d_attn_gain = pull_one(d_normed_one)
    d_tokens = (d_hidden + d_resid_norm).astype(bf16)[None]

    d_columns = jnp.concatenate(
        [
            jnp.einsum("tc,tj->cj", normed_all, d_projected, preferred_element_type=f32),
            jnp.einsum("tc,tj->cj", d_attn_all, attended, preferred_element_type=f32),
        ],
        axis=1,
    ).astype(bf16)
    d_columns = (
        d_columns.reshape(seq_size, shard_size, weight_rows, all_cols)
        .transpose(1, 0, 2, 3)
        .reshape(width, all_cols)
    )
    d_columns = lax.psum_scatter(d_columns, "fsdp", scatter_dimension=0, tiled=True).reshape(seq_size, weight_rows, all_cols)
    d_pieces = lax.all_to_all(d_columns, "seq", split_axis=0, concat_axis=0, tiled=True).astype(f32)
    d_pieces = d_pieces.transpose(1, 0, 2)
    per_group = seq_size // KEY_VALUE_HEADS
    d_kv = d_pieces[:, :, head_cols:proj_cols].reshape(
        weight_rows, KEY_VALUE_HEADS, per_group, 2, kv_cols
    )
    d_kv = jnp.sum(d_kv, axis=2).transpose(0, 2, 1, 3).reshape(weight_rows, -1)
    d_w_qkv = jnp.concatenate([d_pieces[:, :, :head_cols].reshape(weight_rows, -1), d_kv], axis=1)
    d_w_out_t = d_pieces[:, :, proj_cols:].reshape(weight_rows, -1)
    d_w_router = lax.psum_scatter(
        jnp.einsum("tc,te->ce", normed_two, d_logits, preferred_element_type=f32),
        both,
        scatter_dimension=0,
        tiled=True,
    )
    gains = jnp.concatenate([d_attn_gain, d_ffn_gain, d_q_gain, d_k_gain])
    gains = jnp.pad(gains, (0, -gains.shape[0] % 2048)).reshape(16, -1)
    gains = jnp.sum(gather_all(gains, experts, 8), axis=0).reshape(-1)
    d_attn_gain = gains[:width]
    d_ffn_gain = gains[width : 2 * width]
    d_q_gain = gains[2 * width : 2 * width + HEAD_DIMENSION]
    d_k_gain = gains[2 * width + HEAD_DIMENSION : 2 * width + 2 * HEAD_DIMENSION]
    return (
        output[None],
        d_tokens,
        d_w_qkv,
        d_w_out_t,
        d_w_router,
        d_w_in,
        d_w_down,
        d_attn_gain,
        d_ffn_gain,
        d_q_gain,
        d_k_gain,
    )


def gathered_fits(mesh):
    return mesh.shape["seq"] == 8 and mesh.shape["fsdp"] == 4


def solution(mesh):
    return jax.shard_map(
        gathered_body if gathered_fits(mesh) else routed_body,
        mesh=mesh,
        in_specs=(
            P("fsdp", "seq", None),
            P(("seq", "fsdp"), None),
            P(("seq", "fsdp"), None),
            P(("seq", "fsdp"), None),
            P(("seq", "fsdp"), None, None),
            P(("seq", "fsdp"), None, None),
            P(),
            P(),
            P(),
            P(),
            P("fsdp", "seq", None),
            P("fsdp", "seq", None),
        ),
        out_specs=(
            P("fsdp", "seq", None),
            P("fsdp", "seq", None),
            P(("seq", "fsdp"), None),
            P(("seq", "fsdp"), None),
            P(("seq", "fsdp"), None),
            P(("seq", "fsdp"), None, None),
            P(("seq", "fsdp"), None, None),
            P(),
            P(),
            P(),
            P(),
        ),
        check_vma=False,
    )
```

```python
from functools import partial
import math

import jax
import jax.numpy as jnp
from jax import lax
from jax.experimental import pallas as pl
from jax.experimental.pallas import tpu as pltpu
from jax.sharding import PartitionSpec as P

QUERY_HEADS = 32
KEY_VALUE_HEADS = 4
HEAD_DIMENSION = 128
FF = 768
TOPK = 8


EPS = 1e-06
ROPE_BASE = 1000000.0


def rms_scale(values, gain):
    return values * lax.rsqrt(jnp.mean(values * values, axis=-1, keepdims=True) + EPS) * gain


def rotate(values, positions):
    half_dim = values.shape[-1] // 2
    frequency = ROPE_BASE ** (-2.0 * jnp.arange(half_dim, dtype=jnp.float32) / values.shape[-1])
    angles = positions.astype(jnp.float32)[:, None] * frequency[None, :]
    cosine = jnp.cos(angles)[:, None, :]
    sine_part = jnp.sin(angles)[:, None, :]
    first_half = values[..., :half_dim]
    second = values[..., half_dim:]
    return jnp.concatenate(
        [first_half * cosine - second * sine_part, second * cosine + first_half * sine_part],
        axis=-1,
    )


def head_prepare(raw_heads, gain, positions):
    return rotate(rms_scale(raw_heads, gain), positions)


def route_slots(route_flat, experts):
    onehot = (route_flat[:, None] == jnp.arange(experts, dtype=jnp.int32)[None, :]).astype(
        jnp.int32
    )
    earlier = jnp.cumsum(onehot, axis=0) - onehot
    return (onehot, jnp.sum(earlier * onehot, axis=1))


def pack_slots(row_values, expert_ids, slot_index, slot_shape):
    buffer = jnp.zeros(slot_shape, row_values.dtype)
    return buffer.at[expert_ids // slot_shape[1], expert_ids % slot_shape[1], slot_index].set(
        row_values
    )


def unpack_slots(buffer, expert_ids, slot_index):
    return buffer[expert_ids // buffer.shape[1], expert_ids % buffer.shape[1], slot_index]


def causal_scores(query_part, key_full, row_start):
    block_rows = query_part.shape[0]
    score_scale = 1.0 / math.sqrt(query_part.shape[2])
    scores = (
        jnp.einsum("qhd,khd->hqk", query_part, key_full, preferred_element_type=jnp.float32)
        * score_scale
    )
    key_pos = jnp.arange(key_full.shape[0], dtype=jnp.int32)
    row_pos = row_start + jnp.arange(block_rows, dtype=jnp.int32)
    allowed = key_pos[None, :] <= row_pos[:, None]
    return jnp.where(allowed[None], scores, -1e30)


def attend_forward(query_rows_all, key_full, value_full):
    sequence_length = query_rows_all.shape[0]
    block_rows = min(512, sequence_length)

    def one_block(block_index):
        row_start = block_index * block_rows
        query_part = lax.dynamic_slice_in_dim(query_rows_all, row_start, block_rows, 0)
        scores = causal_scores(query_part, key_full, row_start)
        row_max = jnp.max(scores, axis=-1, keepdims=True)
        weights = jnp.exp(scores - row_max)
        row_total = jnp.sum(weights, axis=-1, keepdims=True)
        prob_low = (weights / row_total).astype(jnp.bfloat16)
        mixed_out = jnp.einsum(
            "hqk,khd->qhd", prob_low, value_full, preferred_element_type=jnp.float32
        )
        return (mixed_out.astype(jnp.bfloat16), (row_max + jnp.log(row_total))[..., 0])

    mixed_out, log_total = lax.map(
        one_block, jnp.arange(sequence_length // block_rows, dtype=jnp.int32)
    )
    return (mixed_out.reshape(query_rows_all.shape), log_total)


def attend_backward(query_rows_all, key_full, value_full, log_total, d_mixed):
    sequence_length = query_rows_all.shape[0]
    block_rows = min(512, sequence_length)
    score_scale = 1.0 / math.sqrt(query_rows_all.shape[2])

    def one_block(running, block_index):
        d_key_sum, d_value_sum = running
        row_start = block_index * block_rows
        query_part = lax.dynamic_slice_in_dim(query_rows_all, row_start, block_rows, 0)
        d_part = lax.dynamic_slice_in_dim(d_mixed, row_start, block_rows, 0)
        scores = causal_scores(query_part, key_full, row_start)
        prob_full = jnp.exp(scores - log_total[block_index][..., None])
        prob_low = prob_full.astype(jnp.bfloat16)
        d_probs = jnp.einsum("qhd,khd->hqk", d_part, value_full, preferred_element_type=jnp.float32)
        row_delta = jnp.sum(prob_full * d_probs, axis=-1, keepdims=True)
        d_scores = (prob_full * (d_probs - row_delta)).astype(jnp.bfloat16)
        d_query_part = (
            jnp.einsum("hqk,khd->qhd", d_scores, key_full, preferred_element_type=jnp.float32)
            * score_scale
        )
        d_key_sum = (
            d_key_sum
            + jnp.einsum("hqk,qhd->khd", d_scores, query_part, preferred_element_type=jnp.float32)
            * score_scale
        )
        d_value_sum = d_value_sum + jnp.einsum(
            "hqk,qhd->khd", prob_low, d_part, preferred_element_type=jnp.float32
        )
        return ((d_key_sum, d_value_sum), d_query_part)

    zero_grad = jnp.zeros(key_full.shape, jnp.float32)
    (d_key_sum, d_value_sum), d_query = lax.scan(
        one_block,
        (zero_grad, zero_grad),
        jnp.arange(sequence_length // block_rows, dtype=jnp.int32),
    )
    return (d_query.reshape(query_rows_all.shape), d_key_sum, d_value_sum)


def routed_body(
    tokens,
    query_key_value_weight,
    w_out_t,
    w_router,
    w_in,
    w_down,
    attn_gain,
    ffn_gain,
    q_gain,
    k_gain,
    routes,
    cotangent,
):
    sequence_count = lax.axis_size("seq")
    shard_count = lax.axis_size("fsdp")
    experts = sequence_count * shard_count
    token_row_count = tokens.shape[1]
    model_width = tokens.shape[2]
    query_group_width = QUERY_HEADS // KEY_VALUE_HEADS
    capacity = 2 * token_row_count * TOPK // experts
    slot_shape = (sequence_count, shard_count, capacity, model_width)
    positions = lax.axis_index("seq") * token_row_count + jnp.arange(
        token_row_count, dtype=jnp.int32
    )
    full_qkv, full_out, full_router = (
        lax.all_gather(query_key_value_weight, ("seq", "fsdp"), axis=0, tiled=True),
        lax.all_gather(w_out_t, ("seq", "fsdp"), axis=0, tiled=True),
        lax.all_gather(w_router, ("seq", "fsdp"), axis=0, tiled=True),
    )
    resid_in = tokens[0].astype(jnp.float32)
    normed_one = rms_scale(resid_in, attn_gain).astype(jnp.bfloat16)
    projection_output = jnp.dot(normed_one, full_qkv, preferred_element_type=jnp.float32)
    q_raw = projection_output[:, : QUERY_HEADS * HEAD_DIMENSION].reshape(
        token_row_count, QUERY_HEADS, HEAD_DIMENSION
    )
    key_unnormed = projection_output[
        :, QUERY_HEADS * HEAD_DIMENSION : (QUERY_HEADS + KEY_VALUE_HEADS) * HEAD_DIMENSION
    ].reshape(token_row_count, KEY_VALUE_HEADS, HEAD_DIMENSION)
    value_per_head = (
        projection_output[:, (QUERY_HEADS + KEY_VALUE_HEADS) * HEAD_DIMENSION :]
        .reshape(token_row_count, KEY_VALUE_HEADS, HEAD_DIMENSION)
        .astype(jnp.bfloat16)
    )
    prepare = partial(head_prepare, positions=positions)
    query_rows_all = prepare(q_raw, q_gain).astype(jnp.bfloat16)
    key_per_head = prepare(key_unnormed, k_gain).astype(jnp.bfloat16)
    send_keys = jnp.repeat(key_per_head, query_group_width, axis=1)
    send_values = jnp.repeat(value_per_head, query_group_width, axis=1)
    head_queries, head_keys, head_values = (
        lax.all_to_all(query_rows_all, "seq", split_axis=1, concat_axis=0, tiled=True),
        lax.all_to_all(send_keys, "seq", split_axis=1, concat_axis=0, tiled=True),
        lax.all_to_all(send_values, "seq", split_axis=1, concat_axis=0, tiled=True),
    )
    mixed_heads, log_total = attend_forward(head_queries, head_keys, head_values)
    mixed_tok = lax.all_to_all(mixed_heads, "seq", split_axis=0, concat_axis=1, tiled=True)
    attention_result = mixed_tok.reshape(token_row_count, QUERY_HEADS * HEAD_DIMENSION)
    attn_out = jnp.einsum(
        "tj,dj->td", attention_result, full_out, preferred_element_type=jnp.float32
    )
    hidden = resid_in + attn_out
    normed_two = rms_scale(hidden, ffn_gain).astype(jnp.bfloat16)
    logits = jnp.dot(normed_two, full_router, preferred_element_type=jnp.float32)
    route_flat = routes[0].reshape(-1)
    onehot, slot_index = route_slots(route_flat, experts)
    onehot_float = onehot.reshape(token_row_count, TOPK, experts).astype(jnp.float32)
    chosen = jnp.sum(onehot_float * logits[:, None, :], axis=-1)
    row_max = jnp.max(chosen, axis=-1, keepdims=True)
    exp_part = jnp.exp(chosen - row_max)
    gate_probs = exp_part / jnp.sum(exp_part, axis=-1, keepdims=True)
    send_rows = pack_slots(jnp.repeat(normed_two, TOPK, axis=0), route_flat, slot_index, slot_shape)
    arrived = lax.all_to_all(
        lax.all_to_all(send_rows, "seq", split_axis=0, concat_axis=0, tiled=True),
        "fsdp",
        split_axis=1,
        concat_axis=1,
        tiled=True,
    )
    rows_in = arrived.reshape(-1, model_width)
    gate_weight = w_in[0]
    down_weight = w_down[0]
    gate_up = jnp.dot(rows_in, gate_weight, preferred_element_type=jnp.float32)
    gate_half = gate_up[:, :FF]
    up_half = gate_up[:, FF:]
    gate_sig = jax.nn.sigmoid(gate_half)
    silu_gate = gate_half * gate_sig
    inner_act = (silu_gate * up_half).astype(jnp.bfloat16)
    expert_out = jnp.dot(inner_act, down_weight, preferred_element_type=jnp.float32).astype(
        jnp.bfloat16
    )
    returned = lax.all_to_all(
        lax.all_to_all(
            expert_out.reshape(slot_shape), "seq", split_axis=0, concat_axis=0, tiled=True
        ),
        "fsdp",
        split_axis=1,
        concat_axis=1,
        tiled=True,
    )
    picked = (
        unpack_slots(returned, route_flat, slot_index)
        .astype(jnp.float32)
        .reshape(token_row_count, TOPK, model_width)
    )
    mixture = jnp.sum(gate_probs[..., None] * picked, axis=1)
    output = (hidden + mixture).astype(jnp.bfloat16)
    full_qkv, full_out, full_router = (
        lax.all_gather(query_key_value_weight, ("seq", "fsdp"), axis=0, tiled=True),
        lax.all_gather(w_out_t, ("seq", "fsdp"), axis=0, tiled=True),
        lax.all_gather(w_router, ("seq", "fsdp"), axis=0, tiled=True),
    )
    out_grad = cotangent[0].astype(jnp.float32)
    d_picked = (
        (gate_probs[..., None] * out_grad[:, None, :]).astype(jnp.bfloat16).reshape(-1, model_width)
    )
    d_gates = jnp.sum(picked * out_grad[:, None, :], axis=-1)
    d_send = pack_slots(d_picked, route_flat, slot_index, slot_shape)
    d_arrived = lax.all_to_all(
        lax.all_to_all(d_send, "seq", split_axis=0, concat_axis=0, tiled=True),
        "fsdp",
        split_axis=1,
        concat_axis=1,
        tiled=True,
    ).reshape(-1, model_width)
    d_inner = jnp.einsum("rd,fd->rf", d_arrived, down_weight, preferred_element_type=jnp.float32)
    d_gate_half = d_inner * up_half * gate_sig * (1.0 + gate_half * (1.0 - gate_sig))
    d_up_half = d_inner * silu_gate
    d_gate_up = jnp.concatenate([d_gate_half, d_up_half], axis=1).astype(jnp.bfloat16)
    d_w_down = jnp.einsum("rf,rd->fd", inner_act, d_arrived, preferred_element_type=jnp.float32)[
        None
    ]
    d_w_in = jnp.einsum("rd,rf->df", rows_in, d_gate_up, preferred_element_type=jnp.float32)[None]
    d_rows = jnp.einsum(
        "rf,df->rd", d_gate_up, gate_weight, preferred_element_type=jnp.float32
    ).astype(jnp.bfloat16)
    d_back = lax.all_to_all(
        lax.all_to_all(d_rows.reshape(slot_shape), "seq", split_axis=0, concat_axis=0, tiled=True),
        "fsdp",
        split_axis=1,
        concat_axis=1,
        tiled=True,
    )
    d_routed = jnp.sum(
        unpack_slots(d_back, route_flat, slot_index)
        .astype(jnp.float32)
        .reshape(token_row_count, TOPK, model_width),
        axis=1,
    )
    d_chosen = gate_probs * (d_gates - jnp.sum(gate_probs * d_gates, axis=-1, keepdims=True))
    d_logits = jnp.einsum("tk,tke->te", d_chosen, onehot_float).astype(jnp.bfloat16)
    d_normed_two = d_routed + jnp.einsum(
        "te,de->td", d_logits, full_router, preferred_element_type=jnp.float32
    )
    unused_two, pull_two = jax.vjp(rms_scale, hidden, ffn_gain)
    d_hidden_norm, d_ffn_gain = pull_two(d_normed_two)
    d_hidden = out_grad + d_hidden_norm
    d_attn = d_hidden.astype(jnp.bfloat16)
    d_attended = jnp.einsum(
        "td,dj->tj", d_attn, full_out, preferred_element_type=jnp.float32
    ).astype(jnp.bfloat16)
    d_heads = lax.all_to_all(
        d_attended.reshape(token_row_count, QUERY_HEADS, HEAD_DIMENSION),
        "seq",
        split_axis=1,
        concat_axis=0,
        tiled=True,
    )
    d_query, d_key_sum, d_value_sum = attend_backward(
        head_queries, head_keys, head_values, log_total, d_heads
    )
    seq_rows = head_queries.shape[0]
    local_cols = head_queries.shape[1] * HEAD_DIMENSION
    normed_all, d_attn_all = (
        lax.all_gather(normed_one, "seq", axis=0, tiled=True),
        lax.all_gather(d_attn, "seq", axis=0, tiled=True),
    )
    query_cols = lax.dynamic_slice_in_dim(
        full_qkv, lax.axis_index("seq") * local_cols, local_cols, 1
    )
    q_head_raw = jnp.dot(normed_all, query_cols, preferred_element_type=jnp.float32).reshape(
        head_queries.shape
    )
    seq_positions = jnp.arange(seq_rows, dtype=jnp.int32)
    unused_head, pull_head = jax.vjp(
        partial(head_prepare, positions=seq_positions), q_head_raw, q_gain
    )
    send_d_query, d_q_gain = pull_head(d_query)
    d_query_tok, grad_key_token_rows, grad_value_token_rows = (
        lax.all_to_all(
            send_d_query.astype(jnp.bfloat16), "seq", split_axis=0, concat_axis=1, tiled=True
        ).astype(send_d_query.dtype),
        lax.all_to_all(
            d_key_sum.astype(jnp.bfloat16), "seq", split_axis=0, concat_axis=1, tiled=True
        ).astype(d_key_sum.dtype),
        lax.all_to_all(
            d_value_sum.astype(jnp.bfloat16), "seq", split_axis=0, concat_axis=1, tiled=True
        ).astype(d_value_sum.dtype),
    )
    grad_key_per_head = jnp.sum(
        grad_key_token_rows.reshape(token_row_count, KEY_VALUE_HEADS, -1, HEAD_DIMENSION), axis=2
    )
    grad_value_per_head = jnp.sum(
        grad_value_token_rows.reshape(token_row_count, KEY_VALUE_HEADS, -1, HEAD_DIMENSION), axis=2
    )
    unused_k, pull_k = jax.vjp(prepare, key_unnormed, k_gain)
    grad_key_unnormed, d_k_gain = pull_k(grad_key_per_head)
    d_projected = jnp.concatenate(
        [
            d_query_tok.reshape(token_row_count, QUERY_HEADS * HEAD_DIMENSION),
            grad_key_unnormed.reshape(token_row_count, KEY_VALUE_HEADS * HEAD_DIMENSION),
            grad_value_per_head.reshape(token_row_count, KEY_VALUE_HEADS * HEAD_DIMENSION),
        ],
        axis=1,
    ).astype(jnp.bfloat16)
    d_normed_one = jnp.einsum(
        "tj,dj->td", d_projected, full_qkv, preferred_element_type=jnp.float32
    )
    unused_one, pull_one = jax.vjp(rms_scale, resid_in, attn_gain)
    d_resid_norm, d_attn_gain = pull_one(d_normed_one)
    d_tokens = (d_hidden + d_resid_norm).astype(jnp.bfloat16)[None]
    rows_dev = model_width // experts
    kv_count = 2 * KEY_VALUE_HEADS * HEAD_DIMENSION
    kv_grads = d_projected[:, QUERY_HEADS * HEAD_DIMENSION :]
    first_rows = normed_one
    summed = lax.psum_scatter(
        jnp.concatenate(
            [
                jnp.einsum("tc,tj->cj", first_rows, kv_grads, preferred_element_type=jnp.float32),
                jnp.einsum("tc,te->ce", normed_two, d_logits, preferred_element_type=jnp.float32),
            ],
            axis=1,
        ),
        ("seq", "fsdp"),
        scatter_dimension=0,
        tiled=True,
    )
    d_query_low = send_d_query.reshape(seq_rows, local_cols).astype(jnp.bfloat16)
    attended_heads = mixed_heads.reshape(seq_rows, local_cols)
    normed_order = (
        normed_all.reshape(seq_rows, sequence_count, shard_count, rows_dev)
        .transpose(0, 2, 1, 3)
        .reshape(seq_rows, model_width)
    )
    d_attn_order = (
        d_attn_all.reshape(seq_rows, sequence_count, shard_count, rows_dev)
        .transpose(0, 2, 1, 3)
        .reshape(seq_rows, model_width)
    )
    first_rows = normed_order
    head_sums = lax.psum_scatter(
        jnp.concatenate(
            [
                jnp.einsum(
                    "tc,tj->cj", first_rows, d_query_low, preferred_element_type=jnp.float32
                ),
                jnp.einsum(
                    "tc,tj->cj", d_attn_order, attended_heads, preferred_element_type=jnp.float32
                ),
            ],
            axis=1,
        ).astype(jnp.bfloat16),
        "fsdp",
        scatter_dimension=0,
        tiled=True,
    ).astype(jnp.float32)
    row_sums = (
        lax.all_to_all(
            head_sums.astype(jnp.bfloat16), "seq", split_axis=0, concat_axis=1, tiled=True
        )
        .astype(head_sums.dtype)
        .reshape(rows_dev, sequence_count, 2, local_cols)
    )
    d_w_query = row_sums[:, :, 0].reshape(rows_dev, QUERY_HEADS * HEAD_DIMENSION)
    d_w_out_t = row_sums[:, :, 1].reshape(rows_dev, QUERY_HEADS * HEAD_DIMENSION)
    d_w_qkv = jnp.concatenate([d_w_query, summed[:, :kv_count]], axis=1)
    d_w_router = summed[:, kv_count:]
    d_attn_gain, d_ffn_gain, d_q_gain, d_k_gain = lax.psum(
        (d_attn_gain, d_ffn_gain, d_q_gain, d_k_gain), ("seq", "fsdp")
    )
    return (
        output[None],
        d_tokens,
        d_w_qkv,
        d_w_out_t,
        d_w_router,
        d_w_in,
        d_w_down,
        d_attn_gain,
        d_ffn_gain,
        d_q_gain,
        d_k_gain,
    )


MESH = pl.DeviceIdType.MESH
VMEM_LIMIT = 60 * 2**20


class Place:
    def __init__(self):
        seq, shard = lax.axis_index("seq"), lax.axis_index("fsdp")
        self.z, self.x = seq // 2, seq % 2
        self.y, self.c = shard // 2, shard % 2
        self.z0, self.z1 = self.z % 2, self.z // 2
        self.low, self.high = self.z == 0, self.z == 3
        self.inner = (self.z0 + self.z1) == 1
        self.me = self.block(self.z, self.x, self.y, self.c)

    def device(self, z, x, y, c):
        return (z * 2 + x, y * 2 + c)

    def block(self, z, x, y, c):
        return (z * 2 + x) * 4 + y * 2 + c

    @property
    def by_x(self):
        return self.device(self.z, 1 - self.x, self.y, self.c)

    @property
    def by_y(self):
        return self.device(self.z, self.x, 1 - self.y, self.c)

    @property
    def by_core(self):
        return self.device(self.z, self.x, self.y, 1 - self.c)

    def by_z(self, step):
        return self.device(self.z + step, self.x, self.y, self.c)

    def near(self, k):
        return [self.z, 1 + self.z0, 2 - 2 * self.z0 + self.z1, 3 - 3 * self.z1][k]

    def onward(self, k):
        return [None, 2 * self.z1 - 1, 1 - 2 * self.z1, 2 * self.z1 - 1][k]

    def far(self, k):
        return self.near(3 - k)

    def toward(self, k):
        return [1 - 2 * self.z1, 1 - 2 * self.z0, 1 - 2 * self.z1][k]

    def greet(self, sides):
        barrier = pltpu.get_barrier_semaphore()
        for side in sides:
            if side != "z":
                target = {"x": self.by_x, "y": self.by_y, "core": self.by_core}[side]
                pl.semaphore_signal(barrier, inc=1, device_id=target, device_id_type=MESH)
        count = len([side for side in sides if side != "z"])
        if "z" in sides:

            @pl.when(jnp.logical_not(self.low))
            def _():
                pl.semaphore_signal(barrier, inc=1, device_id=self.by_z(-1), device_id_type=MESH)

            @pl.when(jnp.logical_not(self.high))
            def _():
                pl.semaphore_signal(barrier, inc=1, device_id=self.by_z(1), device_id_type=MESH)

            count = count + 1 + (self.z0 + self.z1) % 2
        pl.semaphore_wait(barrier, count)


def send(source, target, send_sem, recv_sem, device):
    pltpu.make_async_remote_copy(
        src_ref=source,
        dst_ref=target,
        send_sem=send_sem,
        recv_sem=recv_sem,
        device_id=device,
        device_id_type=MESH,
    ).start()


def await_bytes(ref, sem):
    pltpu.make_async_copy(ref, ref, sem).wait()


G_Z, G_X, G_Y, G_DX, G_DY, G_C0 = 0, 1, 2, 3, 4, 5
G_KINDS = 9


def gather_steps(place, own, out, ss, rs, zs, local_sem):
    p = place
    rows = out.shape[1]
    half = rows // 2
    x, y, c = p.x, p.y, p.c

    def cols(q):
        return [
            p.block(q, x, y, c),
            p.block(q, 1 - x, y, c),
            p.block(q, x, 1 - y, c),
            p.block(q, 1 - x, 1 - y, c),
        ]

    def to_core(q, j, src=None):
        b = cols(q)[j]
        send(out.at[b] if src is None else src, out.at[b], ss.at[q, G_C0 + j], rs.at[q, G_C0 + j], p.by_core)

    def plane_out(k):
        q = p.near(k)
        b = cols(q)[0]
        if k == 0:
            src = own
            for step, there in ((1, p.high), (-1, p.low)):

                @pl.when(jnp.logical_not(there))
                def _():
                    send(src, out.at[b], zs.at[q, 0 if step > 0 else 1], rs.at[q, G_Z], p.by_z(step))

            pltpu.make_async_copy(own, out.at[b], local_sem).start()
        else:
            src = out.at[b]
            await_bytes(src, rs.at[q, G_Z])

            @pl.when(p.inner)
            def _():
                send(src, src, zs.at[q, 0], rs.at[q, G_Z], p.by_z(p.onward(k)))

        send(src, out.at[b], ss.at[q, G_X], rs.at[q, G_X], p.by_x)
        send(src, out.at[b], ss.at[q, G_Y], rs.at[q, G_Y], p.by_y)
        to_core(q, 0, src)

    def plane_turn(k):
        q = p.near(k)
        bx, by = out.at[cols(q)[1]], out.at[cols(q)[2]]
        await_bytes(bx, rs.at[q, G_X])
        first = bx.at[pl.ds(0, half)]
        send(first, first, ss.at[q, G_DY], rs.at[q, G_DY], p.by_y)
        to_core(q, 1)
        await_bytes(by, rs.at[q, G_Y])
        second = by.at[pl.ds(half, half)]
        send(second, second, ss.at[q, G_DX], rs.at[q, G_DX], p.by_x)
        to_core(q, 2)

    def plane_end(k):
        q = p.near(k)
        bd = out.at[cols(q)[3]]
        await_bytes(bd.at[pl.ds(0, half)], rs.at[q, G_DY])
        await_bytes(bd.at[pl.ds(half, half)], rs.at[q, G_DX])
        to_core(q, 3)

    def plane_core(k):
        q = p.near(k)
        for j in range(4):
            await_bytes(own, rs.at[q, G_C0 + j])

    def finish():
        piece = own.at[pl.ds(0, half)]
        for q in range(4):
            for kind in (G_X, G_Y, G_C0, G_C0 + 1, G_C0 + 2, G_C0 + 3):
                await_bytes(own, ss.at[q, kind])
            for kind in (G_DX, G_DY):
                await_bytes(piece, ss.at[q, kind])
        for there, slot in ((p.high, 0), (p.low, 1)):

            @pl.when(jnp.logical_not(there))
            def _():
                await_bytes(own, zs.at[p.z, slot])

        for k in range(1, 4):

            @pl.when(p.inner)
            def _():
                await_bytes(own, zs.at[p.near(k), 0])

    return plane_out, plane_turn, plane_end, plane_core, finish


def gather_all_kernel(own, out, ss, rs, zs, local_sem):
    p = Place()
    p.greet(("x", "y", "core", "z"))
    plane_out, plane_turn, plane_end, plane_core, finish = gather_steps(p, own, out, ss, rs, zs, local_sem)
    plane_out(0)
    plane_out(1)
    plane_turn(0)
    plane_out(2)
    plane_end(0)
    plane_turn(1)
    plane_out(3)
    plane_end(1)
    plane_turn(2)
    plane_end(2)
    plane_turn(3)
    plane_end(3)
    for k in range(4):
        plane_core(k)
    pltpu.make_async_copy(own, out.at[p.me], local_sem).wait()
    finish()


def gather_all(own, blocks, collective_id):
    dma = pltpu.SemaphoreType.DMA
    return pl.pallas_call(
        gather_all_kernel,
        out_shape=jax.ShapeDtypeStruct((blocks, *own.shape), own.dtype),
        in_specs=[pl.BlockSpec(memory_space=pl.ANY)],
        out_specs=pl.BlockSpec(memory_space=pl.ANY),
        scratch_shapes=[dma((4, G_KINDS)), dma((4, G_KINDS)), dma((4, 2)), dma],
        compiler_params=pltpu.CompilerParams(
            collective_id=collective_id, has_side_effects=True, vmem_limit_bytes=VMEM_LIMIT
        ),
        name="gather_all",
    )(own)


def sum_all_parts(p, part, held, core_in, x_half, y_half, x_in, y_in, z_in, out, ls, cs, cr, ss, rs, zs, zr):
    rows, width = part.shape[1], part.shape[2]
    half = rows // 2
    x, y, c = p.x, p.y, p.c

    def columns(q):
        return [(q, x, y), (q, 1 - x, y), (q, x, 1 - y), (q, 1 - x, 1 - y)]

    def start():
        for k in range(4):
            q = p.far(k)
            for j, (zz, xx, yy) in reversed(list(enumerate(columns(q)))):
                send(
                    part.at[p.block(zz, xx, yy, 1 - c)],
                    core_in.at[q * 4 + j],
                    cs.at[q, j],
                    cr.at[q, j],
                    p.by_core,
                )
                pltpu.make_async_copy(
                    part.at[p.block(zz, xx, yy, c)], held.at[q * 4 + j], ls.at[q, j]
                ).start()

    chunk = 16

    def add(target, source, count):
        @pl.loop(0, count // chunk)
        def _(i):
            at = pl.ds(pl.multiple_of(i * chunk, chunk), chunk)
            target[at, :] = (
                target[at, :].astype(jnp.float32) + source[at, :].astype(jnp.float32)
            ).astype(target.dtype)

    def plane_core(k, js=(3, 1, 2, 0)):
        q = p.far(k)
        for j in js:
            slot = q * 4 + j
            await_bytes(held.at[slot], ls.at[q, j])
            await_bytes(core_in.at[slot], cr.at[q, j])
            add(held.at[slot], core_in.at[slot], rows)
            if j == 3:
                send(held.at[slot, pl.ds(0, half)], y_half.at[q], ss.at[q, 0], rs.at[q, 0], p.by_y)
                send(held.at[slot, pl.ds(half, half)], x_half.at[q], ss.at[q, 1], rs.at[q, 1], p.by_x)

    def plane_turn(k):
        q = p.far(k)
        await_bytes(y_half.at[q], rs.at[q, 0])
        add(held.at[q * 4 + 1, pl.ds(0, half)], y_half.at[q], half)
        send(held.at[q * 4 + 1], x_in.at[q], ss.at[q, 2], rs.at[q, 2], p.by_x)
        await_bytes(x_half.at[q], rs.at[q, 1])
        add(held.at[q * 4 + 2, pl.ds(half, half)], x_half.at[q], half)
        send(held.at[q * 4 + 2], y_in.at[q], ss.at[q, 3], rs.at[q, 3], p.by_y)

    def plane_end(k):
        q = p.far(k)
        mine = held.at[q * 4]
        await_bytes(x_in.at[q], rs.at[q, 2])
        add(mine, x_in.at[q], rows)
        await_bytes(y_in.at[q], rs.at[q, 3])
        add(mine, y_in.at[q], rows)
        if k < 3:
            step = p.toward(k)
            slot = (1 - step) // 2

            @pl.when(p.inner)
            def _():
                await_bytes(z_in.at[slot, q], zr.at[slot, q])
                add(mine, z_in.at[slot, q], rows)

            send(mine, z_in.at[slot, q], zs.at[k], zr.at[slot, q], p.by_z(step))
        else:
            for slot, there in ((0, p.low), (1, p.high)):

                @pl.when(jnp.logical_not(there))
                def _():
                    await_bytes(z_in.at[slot, q], zr.at[slot, q])
                    add(mine, z_in.at[slot, q], rows)

            out[...] = mine[...]

    def finish():
        whole, piece = x_in.at[0], x_half.at[0]
        for q in range(4):
            for j in range(4):
                await_bytes(whole, cs.at[q, j])
            for kind in (0, 1):
                await_bytes(piece, ss.at[q, kind])
            for kind in (2, 3):
                await_bytes(whole, ss.at[q, kind])
        for k in range(3):
            await_bytes(whole, zs.at[k])

    return start, plane_core, plane_turn, plane_end, finish


def sum_all_kernel(part, out, *scratch):
    p = Place()
    p.greet(("x", "y", "core", "z"))
    start, plane_core, plane_turn, plane_end, finish = sum_all_parts(p, part, *scratch[:7], out, *scratch[7:])
    start()
    plane_core(0)
    plane_core(1)
    plane_turn(0)
    plane_core(2)
    plane_turn(1)
    plane_end(0)
    plane_core(3)
    plane_turn(2)
    plane_end(1)
    plane_turn(3)
    plane_end(2)
    plane_end(3)
    finish()


def sum_all_scratch(rows, width):
    dma = pltpu.SemaphoreType.DMA
    bf16 = jnp.bfloat16
    return [
        pltpu.VMEM((16, rows, width), bf16),
        pltpu.VMEM((16, rows, width), bf16),
        pltpu.VMEM((4, rows // 2, width), bf16),
        pltpu.VMEM((4, rows // 2, width), bf16),
        pltpu.VMEM((4, rows, width), bf16),
        pltpu.VMEM((4, rows, width), bf16),
        pltpu.VMEM((2, 4, rows, width), bf16),
        dma((4, 4)),
        dma((4, 4)),
        dma((4, 4)),
        dma((4, 4)),
        dma((4, 4)),
        dma((3,)),
        dma((2, 4)),
    ]


def sum_all(part, collective_id):
    blocks, rows, width = part.shape
    return pl.pallas_call(
        sum_all_kernel,
        out_shape=jax.ShapeDtypeStruct((rows, width), part.dtype),
        in_specs=[pl.BlockSpec(memory_space=pl.ANY)],
        out_specs=pl.BlockSpec(memory_space=pltpu.VMEM),
        scratch_shapes=sum_all_scratch(rows, width),
        compiler_params=pltpu.CompilerParams(
            collective_id=collective_id, has_side_effects=True, vmem_limit_bytes=VMEM_LIMIT
        ),
        name="sum_all",
    )(part)


def gather_seq_kernel(own, out, ss, rs, zs, local_sem):
    p = Place()
    p.greet(("x", "z"))

    def at(q, x):
        return out.at[q * 2 + x]

    def plane_out(k):
        q = p.near(k)
        there = at(q, p.x)
        if k == 0:
            src = own
            for step, end in ((1, p.high), (-1, p.low)):

                @pl.when(jnp.logical_not(end))
                def _():
                    send(src, there, zs.at[q, 0 if step > 0 else 1], rs.at[q, 0], p.by_z(step))

            pltpu.make_async_copy(own, there, local_sem).start()
        else:
            src = there
            await_bytes(src, rs.at[q, 0])

            @pl.when(p.inner)
            def _():
                send(src, src, zs.at[q, 0], rs.at[q, 0], p.by_z(p.onward(k)))

        send(src, there, ss.at[q], rs.at[q, 1], p.by_x)

    for k in range(4):
        plane_out(k)
    for k in range(4):
        await_bytes(own, rs.at[p.near(k), 1])
    pltpu.make_async_copy(own, at(p.z, p.x), local_sem).wait()
    for q in range(4):
        await_bytes(own, ss.at[q])
    for there, slot in ((p.high, 0), (p.low, 1)):

        @pl.when(jnp.logical_not(there))
        def _():
            await_bytes(own, zs.at[p.z, slot])

    for k in range(1, 4):

        @pl.when(p.inner)
        def _():
            await_bytes(own, zs.at[p.near(k), 0])


def gather_seq(own, collective_id):
    dma = pltpu.SemaphoreType.DMA
    return pl.pallas_call(
        gather_seq_kernel,
        out_shape=jax.ShapeDtypeStruct((8, *own.shape), own.dtype),
        in_specs=[pl.BlockSpec(memory_space=pl.ANY)],
        out_specs=pl.BlockSpec(memory_space=pl.ANY),
        scratch_shapes=[dma((4,)), dma((4, 2)), dma((4, 2)), dma],
        compiler_params=pltpu.CompilerParams(
            collective_id=collective_id, has_side_effects=True, vmem_limit_bytes=VMEM_LIMIT
        ),
        name="gather_seq",
    )(own)


def add_rows(target, source, count, chunk=16):
    @pl.loop(0, count // chunk)
    def _(i):
        at = pl.ds(pl.multiple_of(i * chunk, chunk), chunk)
        target[at, :] = (
            target[at, :].astype(jnp.float32) + source[at, :].astype(jnp.float32)
        ).astype(target.dtype)


def sum_seq_kernel(part, out, held, x_in, z_in, ls, ss, rs, zs, zr):
    p = Place()
    p.greet(("x", "z"))
    rows = part.shape[1]
    for k in range(4):
        q = p.far(k)
        send(part.at[q * 2 + 1 - p.x], x_in.at[q], ss.at[q], rs.at[q], p.by_x)
        pltpu.make_async_copy(part.at[q * 2 + p.x], held.at[q], ls.at[q]).start()
    for k in range(4):
        q = p.far(k)
        mine = held.at[q]
        await_bytes(mine, ls.at[q])
        await_bytes(x_in.at[q], rs.at[q])
        add_rows(mine, x_in.at[q], rows)
        if k < 3:
            step = p.toward(k)
            slot = (1 - step) // 2

            @pl.when(p.inner)
            def _():
                await_bytes(z_in.at[slot, q], zr.at[slot, q])
                add_rows(mine, z_in.at[slot, q], rows)

            send(mine, z_in.at[slot, q], zs.at[k], zr.at[slot, q], p.by_z(step))
        else:
            for slot, there in ((0, p.low), (1, p.high)):

                @pl.when(jnp.logical_not(there))
                def _():
                    await_bytes(z_in.at[slot, q], zr.at[slot, q])
                    add_rows(mine, z_in.at[slot, q], rows)

            out[...] = mine[...]
    for q in range(4):
        await_bytes(x_in.at[0], ss.at[q])
    for k in range(3):
        await_bytes(x_in.at[0], zs.at[k])


def sum_seq(part, collective_id):
    _, rows, width = part.shape
    dma = pltpu.SemaphoreType.DMA
    bf16 = jnp.bfloat16
    return pl.pallas_call(
        sum_seq_kernel,
        out_shape=jax.ShapeDtypeStruct((rows, width), part.dtype),
        in_specs=[pl.BlockSpec(memory_space=pl.ANY)],
        out_specs=pl.BlockSpec(memory_space=pltpu.VMEM),
        scratch_shapes=[
            pltpu.VMEM((4, rows, width), bf16),
            pltpu.VMEM((4, rows, width), bf16),
            pltpu.VMEM((2, 4, rows, width), bf16),
            dma((4,)),
            dma((4,)),
            dma((4,)),
            dma((3,)),
            dma((2, 4)),
        ],
        compiler_params=pltpu.CompilerParams(
            collective_id=collective_id, has_side_effects=True, vmem_limit_bytes=VMEM_LIMIT
        ),
        name="sum_seq",
    )(part)


def seq_peer(p, d):
    return ((p.z * 2 + p.x + d) % 8, p.y * 2 + p.c)


def greet_seq(p, sides=("y", "core")):
    barrier = pltpu.get_barrier_semaphore()
    for d in range(1, 8):
        pl.semaphore_signal(barrier, inc=1, device_id=seq_peer(p, d), device_id_type=MESH)
    for side in sides:
        target = {"y": p.by_y, "core": p.by_core}[side]
        pl.semaphore_signal(barrier, inc=1, device_id=target, device_id_type=MESH)
    pl.semaphore_wait(barrier, 7 + len(sides))


def enter_kernel(own, pieces, rows_out, columns, ss, rs, zs, cs, cr, ys, yr, ks, kr, local_sems):
    p = Place()
    greet_seq(p)
    place, shard = p.z * 2 + p.x, p.y * 2 + p.c
    mine = place * 4 + shard

    def rows_at(q, x):
        return rows_out.at[q * 2 + x]

    def plane_out(k):
        q = p.near(k)
        there = rows_at(q, p.x)
        if k == 0:
            src = own
            for step, end in ((1, p.high), (-1, p.low)):

                @pl.when(jnp.logical_not(end))
                def _():
                    send(src, there, zs.at[q, 0 if step > 0 else 1], rs.at[q, 0], p.by_z(step))

            pltpu.make_async_copy(own, there, local_sems.at[0]).start()
        else:
            src = there
            await_bytes(src, rs.at[q, 0])

            @pl.when(p.inner)
            def _():
                send(src, src, zs.at[q, 0], rs.at[q, 0], p.by_z(p.onward(k)))

        send(src, there, ss.at[q], rs.at[q, 1], p.by_x)

    def pass_on(d):
        block = ((place + 8 - d) % 8) * 4 + shard
        src = pieces.at[place] if d == 0 else columns.at[block]
        if d > 0:
            await_bytes(src, cr.at[d])
        send(src, columns.at[block], ys.at[d], yr.at[d], p.by_y)
        send(src, columns.at[block], ks.at[0, d], kr.at[0, d], p.by_core)

    plane_out(0)
    for d in range(1, 8):
        send(pieces.at[(place + d) % 8], columns.at[mine], cs.at[d], cr.at[d], seq_peer(p, d))
    pltpu.make_async_copy(pieces.at[place], columns.at[mine], local_sems.at[1]).start()
    pass_on(0)
    plane_out(1)
    for d in (1, 2, 7):
        pass_on(d)
    plane_out(2)
    for d in (6, 3, 5):
        pass_on(d)
    plane_out(3)
    pass_on(4)
    other = p.y * 2 + 1 - p.c
    across = (1 - p.y) * 2 + p.c
    piece = pieces.at[0]
    for d in (0, 1, 2, 7, 6, 3, 5, 4):
        block = columns.at[((place + 8 - d) % 8) * 4 + across]
        await_bytes(block, yr.at[d])
        send(block, block, ks.at[1, d], kr.at[1, d], p.by_core)
    for k in range(4):
        await_bytes(own, rs.at[p.near(k), 1])
    for d in range(8):
        await_bytes(piece, kr.at[0, d])
        await_bytes(piece, kr.at[1, d])
    pltpu.make_async_copy(own, rows_at(p.z, p.x), local_sems.at[0]).wait()
    pltpu.make_async_copy(pieces.at[place], columns.at[mine], local_sems.at[1]).wait()
    for q in range(4):
        await_bytes(own, ss.at[q])
    for there, slot in ((p.high, 0), (p.low, 1)):

        @pl.when(jnp.logical_not(there))
        def _():
            await_bytes(own, zs.at[p.z, slot])

    for k in range(1, 4):

        @pl.when(p.inner)
        def _():
            await_bytes(own, zs.at[p.near(k), 0])

    for d in range(8):
        if d > 0:
            await_bytes(piece, cs.at[d])
        await_bytes(piece, ys.at[d])
        await_bytes(piece, ks.at[0, d])
        await_bytes(piece, ks.at[1, d])


def enter(own, pieces, collective_id):
    dma = pltpu.SemaphoreType.DMA
    count, piece_rows, piece_width = pieces.shape
    return pl.pallas_call(
        enter_kernel,
        out_shape=[
            jax.ShapeDtypeStruct((count, *own.shape), own.dtype),
            jax.ShapeDtypeStruct((count * 4, piece_rows, piece_width), pieces.dtype),
        ],
        in_specs=[pl.BlockSpec(memory_space=pl.ANY)] * 2,
        out_specs=[pl.BlockSpec(memory_space=pl.ANY)] * 2,
        scratch_shapes=[
            dma((4,)),
            dma((4, 2)),
            dma((4, 2)),
            dma((8,)),
            dma((8,)),
            dma((8,)),
            dma((8,)),
            dma((2, 8)),
            dma((2, 8)),
            dma((2,)),
        ],
        compiler_params=pltpu.CompilerParams(
            collective_id=collective_id, has_side_effects=True, vmem_limit_bytes=VMEM_LIMIT
        ),
        name="enter",
    )(own, pieces)


def leave_kernel(
    part, cols, tokens, d_hidden, gain, gains,
    d_tokens, cols_out, gains_out,
    held, x_in, z_in, c_held, c_core, c_y, g_send, g_in,
    ls, ss, rs, zs, zr, cl, cs, cr, ys, yr, ts, tr, gs, gr,
):
    p = Place()
    greet_seq(p)
    rows = part.shape[1]
    place = p.z * 2 + p.x
    for turn, side in ((0, 1 - p.y), (1, p.y)):
        send(cols.at[:, side, 1 - p.c], c_core.at[turn], cs.at[turn], cr.at[turn], p.by_core)
        pltpu.make_async_copy(cols.at[:, side, p.c], c_held.at[turn], cl.at[turn]).start()
    for k in range(4):
        q = p.far(k)
        send(part.at[q * 2 + 1 - p.x], x_in.at[q], ss.at[q], rs.at[q], p.by_x)
        pltpu.make_async_copy(part.at[q * 2 + p.x], held.at[q], ls.at[q]).start()
    piece_rows = c_held.shape[2]
    order = [(place + d) % 8 for d in range(1, 9)]
    for turn in range(2):
        await_bytes(c_held.at[turn], cl.at[turn])
        await_bytes(c_core.at[turn], cr.at[turn])
        for i, s in enumerate(order):
            add_rows(c_held.at[turn, s], c_core.at[turn, s], piece_rows)
            if turn == 0:
                send(c_held.at[0, s], c_y.at[s], ys.at[s], yr.at[s], p.by_y)

    def turn_in(i):
        s = order[i]
        await_bytes(c_y.at[s], yr.at[s])
        add_rows(c_held.at[1, s], c_y.at[s], piece_rows)
        if i < 7:
            send(c_held.at[1, s], cols_out.at[place], ts.at[i], tr.at[i], seq_peer(p, i + 1))
        else:
            pltpu.make_async_copy(c_held.at[1, s], cols_out.at[place], ts.at[7]).start()

    for k in range(4):
        q = p.far(k)
        mine = held.at[q]
        await_bytes(mine, ls.at[q])
        await_bytes(x_in.at[q], rs.at[q])
        add_rows(mine, x_in.at[q], rows)
        if k < 3:
            step = p.toward(k)
            slot = (1 - step) // 2

            @pl.when(p.inner)
            def _():
                await_bytes(z_in.at[slot, q], zr.at[slot, q])
                add_rows(mine, z_in.at[slot, q], rows)

            send(mine, z_in.at[slot, q], zs.at[k], zr.at[slot, q], p.by_z(step))
            for i in ((0, 1), (2, 3), (4, 5, 6, 7))[k]:
                turn_in(i)
        else:
            for slot, there in ((0, p.low), (1, p.high)):

                @pl.when(jnp.logical_not(there))
                def _():
                    await_bytes(z_in.at[slot, q], zr.at[slot, q])
                    add_rows(mine, z_in.at[slot, q], rows)

    mine = held.at[p.z]
    g_send[0] = jnp.zeros_like(g_send[0])
    chunk = 16

    @pl.loop(0, rows // chunk)
    def _(i):
        at = pl.ds(pl.multiple_of(i * chunk, chunk), chunk)
        d_out = mine[at, :].astype(jnp.float32)
        x = tokens[at, :].astype(jnp.float32)
        scale = lax.rsqrt(jnp.mean(x * x, axis=-1, keepdims=True) + EPS)
        u = d_out * gain[...]
        dot = jnp.mean(u * x, axis=-1, keepdims=True)
        d_x = scale * u - x * (scale * scale * scale * dot)
        d_tokens[at, :] = (d_hidden[at, :] + d_x).astype(d_tokens.dtype)
        terms = d_out * x * scale
        g_send[0] += terms[:8] + terms[8:]

    first = jnp.sum(g_send[0], axis=0, keepdims=True)
    row = lax.broadcasted_iota(jnp.int32, g_send[0].shape, 0)
    g_send[0] = jnp.where(row == 0, first, gains[...])
    for t, target in enumerate((p.by_core, p.by_y, p.by_x)):
        send(g_send.at[t], g_in.at[t], gs.at[t], gr.at[t], target)
        await_bytes(g_in.at[t], gr.at[t])
        g_send[t + 1] = g_send[t] + g_in[t]
    for d in (1, 2, 3):
        target = p.device((p.z + d) % 4, p.x, p.y, p.c)
        send(g_send.at[3], g_in.at[3 + p.z], gs.at[2 + d], gr.at[2 + d], target)
    g_in[3 + p.z] = g_send[3]
    for d in (1, 2, 3):
        await_bytes(g_in.at[0], gr.at[2 + d])
    gains_out[...] = g_in[3] + g_in[4] + g_in[5] + g_in[6]

    piece = c_y.at[0]
    for i in range(8):
        if i < 7:
            await_bytes(piece, tr.at[i])
        await_bytes(piece, ts.at[i])
        await_bytes(piece, ys.at[i])
    for turn in range(2):
        await_bytes(c_core.at[turn], cs.at[turn])
    for q in range(4):
        await_bytes(x_in.at[0], ss.at[q])
    for k in range(3):
        await_bytes(x_in.at[0], zs.at[k])
    for t in range(6):
        await_bytes(g_in.at[0], gs.at[t])


def leave(part, cols, tokens, d_hidden, gain, gains, collective_id):
    _, rows, width = part.shape
    piece_rows, piece_width = cols.shape[3:]
    dma = pltpu.SemaphoreType.DMA
    bf16, f32 = jnp.bfloat16, jnp.float32
    anywhere, vmem = pl.BlockSpec(memory_space=pl.ANY), pl.BlockSpec(memory_space=pltpu.VMEM)
    return pl.pallas_call(
        leave_kernel,
        out_shape=[
            jax.ShapeDtypeStruct((rows, width), bf16),
            jax.ShapeDtypeStruct((8, piece_rows, piece_width), bf16),
            jax.ShapeDtypeStruct(gains.shape, f32),
        ],
        in_specs=[anywhere] * 2 + [vmem] * 4,
        out_specs=[vmem, anywhere, vmem],
        scratch_shapes=[
            pltpu.VMEM((4, rows, width), bf16),
            pltpu.VMEM((4, rows, width), bf16),
            pltpu.VMEM((2, 4, rows, width), bf16),
            pltpu.VMEM((2, 8, piece_rows, piece_width), bf16),
            pltpu.VMEM((2, 8, piece_rows, piece_width), bf16),
            pltpu.VMEM((8, piece_rows, piece_width), bf16),
            pltpu.VMEM((4, *gains.shape), f32),
            pltpu.VMEM((7, *gains.shape), f32),
            dma((4,)),
            dma((4,)),
            dma((4,)),
            dma((3,)),
            dma((2, 4)),
            dma((2,)),
            dma((2,)),
            dma((2,)),
            dma((8,)),
            dma((8,)),
            dma((8,)),
            dma((7,)),
            dma((6,)),
            dma((6,)),
        ],
        compiler_params=pltpu.CompilerParams(
            collective_id=collective_id, has_side_effects=True, vmem_limit_bytes=VMEM_LIMIT
        ),
        name="leave",
    )(part, cols, tokens, d_hidden, gain, gains)


NT = (((1,), (1,)), ((), ()))
TILE = 256


def mxu(a, b, dims=(((1,), (0,)), ((), ()))):
    return lax.dot_general(a, b, dims, preferred_element_type=jnp.float32)


def experts_kernel(
    own, cot_all, w_in_hbm, w_down_hbm,
    rows_all, out_part, d_part, x_all, d_expert_all, inner_all, d_gate_up_all,
    w_in, w_down, row_buf, cot_buf, pick, pick_t, gates, d_gates, x, cot, d_expert,
    by_d_gate, by_d_up, inner, d_gate_up, out_stage, d_stage,
    ss, rs, zs, local_sem, load_sems, store_sems,
):
    p = Place()
    bf16, f32 = jnp.bfloat16, jnp.float32
    width = cot_all.shape[2]
    blocks = 8
    slots = gates.shape[0]
    capacity = slots // blocks
    tokens = row_buf.shape[2]
    group = 4
    experts = rows_all.shape[0]
    p.greet(("x", "y", "core", "z"))
    plane_out, plane_turn, plane_end, plane_core, finish = gather_steps(
        p, own, rows_all, ss, rs, zs, local_sem
    )

    def weights(start):
        for i, (src, dst) in enumerate(((w_in_hbm, w_in), (w_down_hbm, w_down))):
            copy = pltpu.make_async_copy(src, dst, load_sems.at[i])
            copy.start() if start else copy.wait()

    def cot_load(k):
        return pltpu.make_async_copy(
            cot_all.at[pl.ds(p.near(k) * blocks, blocks)], cot_buf.at[k % 2], load_sems.at[2 + k]
        )

    def row_load(k):
        return pltpu.make_async_copy(
            rows_all.at[pl.ds(p.near(k) * blocks, blocks)], row_buf.at[k % 2], load_sems.at[6 + k]
        )

    def arrived(k):
        plane_core(k)
        if k == 0:
            pltpu.make_async_copy(own, rows_all.at[p.me], local_sem).wait()
        row_load(k).start()

    at_slot = {}

    def store(k, i, src, dst):
        if (k, i) not in at_slot:
            at_slot[k, i] = pltpu.make_async_copy(src, dst, store_sems.at[i, k % 2])
        return at_slot[k, i]

    def stores(k):
        q = p.near(k)
        at = pl.ds(q * slots, slots)
        plane = pl.ds(q * blocks, blocks)
        return [
            (x, x_all.at[at]),
            (d_expert, d_expert_all.at[at]),
            (inner, inner_all.at[at]),
            (d_gate_up, d_gate_up_all.at[at]),
            (out_stage, out_part.at[plane]),
            (d_stage, d_part.at[plane]),
        ]

    def put(k, i):
        store(k, i, *stores(k)[i]).start()

    def free(k, i):
        if k > 0:
            store(k - 1, i, *stores(k - 1)[i]).wait()

    def pick_rows(k):
        lane = lax.broadcasted_iota(jnp.int32, (8, 128), 1)
        line = lax.broadcasted_iota(jnp.int32, (8, 128), 0)
        select = jnp.where((lane == line * experts + p.me) & (line < 3), 1.0, 0.0).astype(bf16)
        before = jnp.where(
            lax.broadcasted_iota(jnp.int32, (tokens, tokens), 0)
            < lax.broadcasted_iota(jnp.int32, (tokens, tokens), 1),
            1.0,
            0.0,
        ).astype(bf16)
        slot_id = lax.broadcasted_iota(jnp.int32, (capacity, tokens), 0).astype(f32)
        rows, cots = row_buf.at[k % 2], cot_buf.at[k % 2]

        @pl.loop(0, blocks // group)
        def _(g):
            for i in range(group):
                info = rows[g * group + i, :, width:]
                lines = mxu(select, info, NT)
                named = lines[2:3]
                slot = mxu(lines.astype(bf16), before)[2:3]
                chosen = jnp.where((slot == slot_id) & (named > 0.5), 1.0, 0.0)
                gate = jnp.sum(chosen * (lines[0:1] + lines[1:2]), axis=1, keepdims=True)
                at = pl.ds(pl.multiple_of(g * group * capacity + i * capacity, capacity), capacity)
                gates[at, :] = jnp.broadcast_to(gate, (capacity, 128))
                lead = [jnp.zeros((capacity, tokens), bf16)] * i
                tail = [jnp.zeros((capacity, tokens), bf16)] * (group - 1 - i)
                pick[g, i * capacity : (i + 1) * capacity, :] = jnp.concatenate(
                    lead + [chosen.astype(bf16)] + tail, axis=1
                )
                turned = chosen.T
                lead = [jnp.zeros((tokens, capacity), f32)] * i
                tail = [jnp.zeros((tokens, capacity), f32)] * (group - 1 - i)
                pick_t[g, i * tokens : (i + 1) * tokens, :] = jnp.concatenate(
                    lead + [turned] + tail, axis=1
                ).astype(bf16)
            at = pl.ds(pl.multiple_of(g * group * capacity, group * capacity), group * capacity)
            scale = gates[at, :]
            scale = jnp.concatenate([scale] * (TILE // 128), axis=1)
            which = pl.ds(g * group, group)

            @pl.loop(0, width // TILE)
            def _(n):
                cols = pl.ds(pl.multiple_of(n * TILE, TILE), TILE)
                row_tile = rows[which, :, cols].reshape(group * tokens, TILE)
                x[at, cols] = mxu(pick[g], row_tile).astype(bf16)
                cot_tile = cots[which, :, cols].reshape(group * tokens, TILE)
                picked = mxu(pick[g], cot_tile)
                cot[at, cols] = picked.astype(bf16)
                d_expert[at, cols] = (scale * picked).astype(bf16)

    def up(k):
        ff = inner.shape[1]

        @pl.loop(0, ff // TILE)
        def _(n):
            cols = pl.ds(pl.multiple_of(n * TILE, TILE), TILE)
            gate = mxu(x[...], w_in[:, cols])
            raised = mxu(x[...], w_in[:, pl.ds(pl.multiple_of(ff + n * TILE, TILE), TILE)])
            sig = jax.nn.sigmoid(gate)
            silu = gate * sig
            inner[:, cols] = (silu * raised).astype(bf16)
            by_d_up[:, cols] = silu
            by_d_gate[:, cols] = raised * sig * (1.0 + gate * (1.0 - sig))

    def d_up(k):
        ff = inner.shape[1]

        @pl.loop(0, ff // TILE)
        def _(n):
            cols = pl.ds(pl.multiple_of(n * TILE, TILE), TILE)
            d_inner = mxu(d_expert[...], w_down[cols, :], NT)
            d_gate_up[:, cols] = (d_inner * by_d_gate[:, cols]).astype(bf16)
            d_gate_up[:, pl.ds(pl.multiple_of(ff + n * TILE, TILE), TILE)] = (
                d_inner * by_d_up[:, cols]
            ).astype(bf16)

    def scatter(value, stage, cols, wide):
        for g in range(blocks // group):
            part = value[g * group * capacity : (g + 1) * group * capacity]
            spread = mxu(pick_t[g], part).astype(bf16)
            stage[g * group : (g + 1) * group, :, cols] = spread.reshape(group, tokens, wide)

    def down(k):
        d_gates[...] = jnp.zeros_like(d_gates)
        scale = jnp.concatenate([gates[...]] * (TILE // 128), axis=1)

        @pl.loop(0, width // TILE)
        def _(n):
            cols = pl.ds(pl.multiple_of(n * TILE, TILE), TILE)
            result = mxu(inner[...], w_down[:, cols]).astype(bf16).astype(f32)
            product = result * cot[:, cols].astype(f32)
            total = product[:, :128]
            for j in range(1, TILE // 128):
                total = total + product[:, j * 128 : (j + 1) * 128]
            d_gates[...] += total
            scatter((scale * result).astype(bf16), out_stage, cols, TILE)

    def d_down(k):
        total = jnp.sum(d_gates[...], axis=1, keepdims=True)
        high = total.astype(bf16).astype(f32)
        lane = lax.broadcasted_iota(jnp.int32, (slots, 128), 1)
        info = jnp.where(lane == p.me, high, jnp.where(lane == experts + p.me, total - high, 0.0))
        scatter(info.astype(bf16), d_stage, pl.ds(width, 128), 128)

        @pl.loop(0, width // TILE)
        def _(n):
            cols = pl.ds(pl.multiple_of(n * TILE, TILE), TILE)
            d_rows = mxu(d_gate_up[...], w_in[cols, :], NT)
            scatter(d_rows.astype(bf16), d_stage, cols, TILE)

    plane_out(0)
    weights(True)
    cot_load(0).start()
    plane_out(1)
    plane_turn(0)
    plane_end(0)
    arrived(0)
    weights(False)
    after = {
        0: ([lambda: plane_out(2)], [lambda: plane_turn(1)], [lambda: plane_out(3)], [lambda: plane_end(1)], [lambda: arrived(1)]),
        1: ([], [lambda: plane_turn(2)], [], [lambda: plane_end(2)], [lambda: arrived(2)]),
        2: ([], [lambda: plane_turn(3)], [], [lambda: plane_end(3)], [lambda: arrived(3)]),
        3: ([], [], [], [], []),
    }
    for k in range(4):

        def service(i):
            for step in after[k][i]:
                step()

        row_load(k).wait()
        cot_load(k).wait()
        if k < 3:
            cot_load(k + 1).start()
        free(k, 0)
        free(k, 1)
        pick_rows(k)
        put(k, 0)
        put(k, 1)
        service(0)
        free(k, 2)
        up(k)
        put(k, 2)
        service(1)
        free(k, 3)
        d_up(k)
        put(k, 3)
        service(2)
        free(k, 4)
        down(k)
        put(k, 4)
        service(3)
        free(k, 5)
        d_down(k)
        put(k, 5)
        service(4)
    for i in range(6):
        free(4, i)
    finish()


def experts_gathered(own, cot_all, w_in, w_down, capacity, collective_id):
    tokens, wide = own.shape
    experts, _, width = cot_all.shape
    ff = w_down.shape[0]
    slots = 8 * capacity
    dma = pltpu.SemaphoreType.DMA
    bf16, f32 = jnp.bfloat16, jnp.float32
    anywhere = pl.BlockSpec(memory_space=pl.ANY)

    def array(*shape):
        return jax.ShapeDtypeStruct(shape, bf16)

    return pl.pallas_call(
        experts_kernel,
        out_shape=[
            array(experts, tokens, wide),
            array(experts, tokens, width),
            array(experts, tokens, wide),
            array(experts * capacity, width),
            array(experts * capacity, width),
            array(experts * capacity, ff),
            array(experts * capacity, 2 * ff),
        ],
        in_specs=[anywhere] * 4,
        out_specs=[anywhere] * 7,
        scratch_shapes=[
            pltpu.VMEM(w_in.shape, bf16),
            pltpu.VMEM(w_down.shape, bf16),
            pltpu.VMEM((2, 8, tokens, wide), bf16),
            pltpu.VMEM((2, 8, tokens, width), bf16),
            pltpu.VMEM((2, 4 * capacity, 4 * tokens), bf16),
            pltpu.VMEM((2, 4 * tokens, 4 * capacity), bf16),
            pltpu.VMEM((slots, 128), f32),
            pltpu.VMEM((slots, 128), f32),
            pltpu.VMEM((slots, width), bf16),
            pltpu.VMEM((slots, width), bf16),
            pltpu.VMEM((slots, width), bf16),
            pltpu.VMEM((slots, ff), f32),
            pltpu.VMEM((slots, ff), f32),
            pltpu.VMEM((slots, ff), bf16),
            pltpu.VMEM((slots, 2 * ff), bf16),
            pltpu.VMEM((8, tokens, width), bf16),
            pltpu.VMEM((8, tokens, wide), bf16),
            dma((4, G_KINDS)),
            dma((4, G_KINDS)),
            dma((4, 2)),
            dma,
            dma((10,)),
            dma((6, 2)),
        ],
        compiler_params=pltpu.CompilerParams(
            collective_id=collective_id, has_side_effects=True, vmem_limit_bytes=VMEM_LIMIT
        ),
        name="experts",
    )(own, cot_all, w_in, w_down)


def head_columns(weight, group_index):
    rows = weight.shape[0]
    query_width = QUERY_HEADS * HEAD_DIMENSION
    key_width = KEY_VALUE_HEADS * HEAD_DIMENSION
    query = weight[:, :query_width].reshape(rows, len(group_index), -1).transpose(1, 0, 2)
    keys = weight[:, query_width : query_width + key_width].reshape(rows, KEY_VALUE_HEADS, -1)
    values = weight[:, query_width + key_width :].reshape(rows, KEY_VALUE_HEADS, -1)
    keys = jnp.stack([keys[:, group] for group in group_index])
    values = jnp.stack([values[:, group] for group in group_index])
    return jnp.concatenate([query, keys, values], axis=2)


def gathered_body(
    tokens,
    query_key_value_weight,
    w_out_t,
    w_router,
    w_in,
    w_down,
    attn_gain,
    ffn_gain,
    q_gain,
    k_gain,
    routes,
    cotangent,
):
    bf16, f32 = jnp.bfloat16, jnp.float32
    both = ("seq", "fsdp")
    seq_size = lax.axis_size("seq")
    shard_size = lax.axis_size("fsdp")
    experts = seq_size * shard_size
    rows = tokens.shape[1]
    width = tokens.shape[2]
    length = rows * seq_size
    weight_rows = query_key_value_weight.shape[0]
    heads = QUERY_HEADS // seq_size
    head_cols = heads * HEAD_DIMENSION
    kv_cols = HEAD_DIMENSION
    proj_cols = head_cols + 2 * kv_cols
    all_cols = proj_cols + head_cols
    spare_cols = 128
    group_index = [s * heads * KEY_VALUE_HEADS // QUERY_HEADS for s in range(seq_size)]
    capacity = 2 * rows * TOPK // experts

    pieces = jnp.concatenate(
        [
            head_columns(query_key_value_weight, group_index),
            w_out_t.reshape(weight_rows, seq_size, head_cols).transpose(1, 0, 2),
            jnp.broadcast_to(
                jnp.pad(w_router, ((0, 0), (0, spare_cols - experts))),
                (seq_size, weight_rows, spare_cols),
            ),
        ],
        axis=2,
    )
    resid_in = tokens[0].astype(f32)
    normed_one = rms_scale(resid_in, attn_gain).astype(bf16)
    normed_all, columns = enter(normed_one, pieces, 1)
    normed_all = normed_all.reshape(length, width)
    columns = columns.reshape(width, -1)
    proj_weight = columns[:, :proj_cols]
    out_weight = columns[:, proj_cols:all_cols]
    full_router = columns[:, all_cols : all_cols + experts]
    columns, cot_own = lax.optimization_barrier((columns, cotangent[0]))
    cot_all = lax.all_gather(cot_own, both)

    projected = jnp.dot(normed_all, proj_weight, preferred_element_type=f32)
    seq_positions = jnp.arange(length, dtype=jnp.int32)
    prepare = partial(head_prepare, positions=seq_positions)
    q_raw = projected[:, :head_cols].reshape(length, heads, HEAD_DIMENSION)
    k_raw = projected[:, head_cols : head_cols + kv_cols].reshape(length, 1, HEAD_DIMENSION)
    values = projected[:, head_cols + kv_cols :].astype(bf16).reshape(length, 1, HEAD_DIMENSION)
    queries = prepare(q_raw, q_gain).astype(bf16)
    keys = prepare(k_raw, k_gain).astype(bf16)
    repeat_keys = jnp.repeat(keys, heads, axis=1)
    repeat_values = jnp.repeat(values, heads, axis=1)
    mixed_heads, log_total = attend_forward(queries, repeat_keys, repeat_values)
    attended = mixed_heads.reshape(length, head_cols)
    attn_part = jnp.einsum("tj,dj->td", attended, out_weight, preferred_element_type=f32)
    attn_out = sum_seq(attn_part.astype(bf16).reshape(seq_size, rows, width), 2)
    hidden = resid_in + attn_out.astype(f32)
    normed_two = rms_scale(hidden, ffn_gain).astype(bf16)

    logits = jnp.dot(normed_two, full_router, preferred_element_type=f32)
    onehot = routes[0][:, :, None] == jnp.arange(experts, dtype=jnp.int32)
    onehot_float = onehot.astype(f32)
    named = jnp.sum(onehot_float, axis=1)
    chosen = jnp.sum(onehot_float * logits[:, None, :], axis=-1)
    row_max = jnp.max(chosen, axis=-1, keepdims=True)
    exp_part = jnp.exp(chosen - row_max)
    gate_probs = exp_part / jnp.sum(exp_part, axis=-1, keepdims=True)
    gate_dense = jnp.sum(onehot_float * gate_probs[..., None], axis=1)

    gate_high = gate_dense.astype(bf16)
    gate_low = (gate_dense - gate_high.astype(f32)).astype(bf16)
    route_info = jnp.concatenate([gate_high, gate_low, named.astype(bf16)], axis=1)
    route_info = jnp.pad(route_info, ((0, 0), (0, 128 - route_info.shape[1] % 128)))
    gate_weight = w_in[0]
    down_weight = w_down[0]
    rows_all, out_part, d_part, rows_in, d_expert, inner_act, d_gate_up = experts_gathered(
        jnp.concatenate([normed_two, route_info], axis=1),
        cot_all,
        gate_weight,
        down_weight,
        capacity,
        3,
    )
    d_back = sum_all(d_part, 5).astype(f32)
    mixture = sum_all(out_part, 4)
    output = (hidden + mixture.astype(f32)).astype(bf16)
    d_w_down = jnp.einsum("rf,rd->fd", inner_act, d_expert, preferred_element_type=f32)[None]
    d_w_in = jnp.einsum("rd,rf->df", rows_in, d_gate_up, preferred_element_type=f32)[None]

    d_gate_dense = d_back[:, width : width + experts] + d_back[:, width + experts : width + 2 * experts]
    d_gates = jnp.sum(onehot_float * d_gate_dense[:, None, :], axis=-1)
    d_chosen = gate_probs * (d_gates - jnp.sum(gate_probs * d_gates, axis=-1, keepdims=True))
    d_logits = jnp.sum(d_chosen[..., None] * onehot_float, axis=1).astype(bf16)
    d_normed_two = d_back[:, :width] + jnp.einsum(
        "te,de->td", d_logits, full_router, preferred_element_type=f32
    )
    out_grad = cotangent[0].astype(f32)
    unused_two, pull_two = jax.vjp(rms_scale, hidden, ffn_gain)
    d_hidden_norm, d_ffn_gain = pull_two(d_normed_two)
    d_hidden = out_grad + d_hidden_norm
    d_attn = d_hidden.astype(bf16)

    d_send = jnp.concatenate([d_attn, jnp.pad(d_logits, ((0, 0), (0, 128 - experts)))], axis=1)
    d_attn_all = gather_seq(d_send, 6).reshape(length, -1)
    d_logits_all = d_attn_all[:, width:]
    d_attn_all = d_attn_all[:, :width]
    d_attended = jnp.dot(d_attn_all, out_weight, preferred_element_type=f32).astype(bf16)
    d_query, d_key_sum, d_value_sum = attend_backward(
        queries,
        repeat_keys,
        repeat_values,
        log_total,
        d_attended.reshape(length, heads, HEAD_DIMENSION),
    )
    unused_q, pull_q = jax.vjp(prepare, q_raw, q_gain)
    d_q_raw, d_q_gain = pull_q(d_query)
    unused_k, pull_k = jax.vjp(prepare, k_raw, k_gain)
    d_k_raw, d_k_gain = pull_k(jnp.sum(d_key_sum, axis=1, keepdims=True))
    d_projected = jnp.concatenate(
        [
            d_q_raw.reshape(length, head_cols),
            d_k_raw.reshape(length, kv_cols),
            jnp.sum(d_value_sum, axis=1),
        ],
        axis=1,
    ).astype(bf16)
    d_normed_part = jnp.einsum("tj,dj->td", d_projected, proj_weight, preferred_element_type=f32)
    router_cols = experts // seq_size
    shard = lax.axis_index("fsdp")
    two_all = lax.dynamic_index_in_dim(
        rows_all.reshape(seq_size, shard_size, rows, -1), shard, 1, keepdims=False
    )[:, :, :width].reshape(length, width)
    own_logits = lax.dynamic_slice_in_dim(
        d_logits_all, lax.axis_index("seq") * router_cols, router_cols, 1
    )
    own_logits = jnp.pad(own_logits, ((0, 0), (0, spare_cols - router_cols)))
    d_columns = jnp.concatenate(
        [
            jnp.einsum("tc,tj->cj", normed_all, d_projected, preferred_element_type=f32),
            jnp.einsum("tc,tj->cj", d_attn_all, attended, preferred_element_type=f32),
            jnp.einsum("tc,tj->cj", two_all, own_logits, preferred_element_type=f32),
        ],
        axis=1,
    ).astype(bf16)
    gains = jnp.pad(
        jnp.stack([d_ffn_gain, jnp.pad(jnp.concatenate([d_q_gain, d_k_gain]), (0, width - 2 * HEAD_DIMENSION))]),
        ((1, 5), (0, 0)),
    )
    d_tokens, d_pieces, gains = leave(
        d_normed_part.astype(bf16).reshape(seq_size, rows, width),
        d_columns.reshape(seq_size, 2, shard_size // 2, weight_rows, all_cols + spare_cols),
        tokens[0],
        d_hidden,
        attn_gain[None],
        gains,
        7,
    )
    d_tokens = d_tokens[None]
    d_pieces = d_pieces.astype(f32).transpose(1, 0, 2)
    per_group = seq_size // KEY_VALUE_HEADS
    d_kv = d_pieces[:, :, head_cols:proj_cols].reshape(
        weight_rows, KEY_VALUE_HEADS, per_group, 2, kv_cols
    )
    d_kv = jnp.sum(d_kv, axis=2).transpose(0, 2, 1, 3).reshape(weight_rows, -1)
    d_w_qkv = jnp.concatenate([d_pieces[:, :, :head_cols].reshape(weight_rows, -1), d_kv], axis=1)
    d_w_out_t = d_pieces[:, :, proj_cols:all_cols].reshape(weight_rows, -1)
    d_w_router = d_pieces[:, :, all_cols : all_cols + router_cols].reshape(weight_rows, experts)
    d_attn_gain, d_ffn_gain = gains[0], gains[1]
    d_q_gain = gains[2, :HEAD_DIMENSION]
    d_k_gain = gains[2, HEAD_DIMENSION : 2 * HEAD_DIMENSION]
    return (
        output[None],
        d_tokens,
        d_w_qkv,
        d_w_out_t,
        d_w_router,
        d_w_in,
        d_w_down,
        d_attn_gain,
        d_ffn_gain,
        d_q_gain,
        d_k_gain,
    )


def gathered_fits(mesh):
    return mesh.shape["seq"] == 8 and mesh.shape["fsdp"] == 4


def solution(mesh):
    return jax.shard_map(
        gathered_body if gathered_fits(mesh) else routed_body,
        mesh=mesh,
        in_specs=(
            P("fsdp", "seq", None),
            P(("seq", "fsdp"), None),
            P(("seq", "fsdp"), None),
            P(("seq", "fsdp"), None),
            P(("seq", "fsdp"), None, None),
            P(("seq", "fsdp"), None, None),
            P(),
            P(),
            P(),
            P(),
            P("fsdp", "seq", None),
            P("fsdp", "seq", None),
        ),
        out_specs=(
            P("fsdp", "seq", None),
            P("fsdp", "seq", None),
            P(("seq", "fsdp"), None),
            P(("seq", "fsdp"), None),
            P(("seq", "fsdp"), None),
            P(("seq", "fsdp"), None, None),
            P(("seq", "fsdp"), None, None),
            P(),
            P(),
            P(),
            P(),
        ),
        check_vma=False,
    )
```

```python
from functools import partial
import math

import jax
import jax.numpy as jnp
from jax import lax
from jax.experimental import pallas as pl
from jax.experimental.pallas import tpu as pltpu
from jax.sharding import PartitionSpec as P

QUERY_HEADS = 32
KEY_VALUE_HEADS = 4
HEAD_DIMENSION = 128
FF = 768
TOPK = 8


EPS = 1e-06
ROPE_BASE = 1000000.0


def rms_scale(values, gain):
    return values * lax.rsqrt(jnp.mean(values * values, axis=-1, keepdims=True) + EPS) * gain


def rotate(values, positions):
    half_dim = values.shape[-1] // 2
    frequency = ROPE_BASE ** (-2.0 * jnp.arange(half_dim, dtype=jnp.float32) / values.shape[-1])
    angles = positions.astype(jnp.float32)[:, None] * frequency[None, :]
    cosine = jnp.cos(angles)[:, None, :]
    sine_part = jnp.sin(angles)[:, None, :]
    first_half = values[..., :half_dim]
    second = values[..., half_dim:]
    return jnp.concatenate(
        [first_half * cosine - second * sine_part, second * cosine + first_half * sine_part],
        axis=-1,
    )


def head_prepare(raw_heads, gain, positions):
    return rotate(rms_scale(raw_heads, gain), positions)


def route_slots(route_flat, experts):
    onehot = (route_flat[:, None] == jnp.arange(experts, dtype=jnp.int32)[None, :]).astype(
        jnp.int32
    )
    earlier = jnp.cumsum(onehot, axis=0) - onehot
    return (onehot, jnp.sum(earlier * onehot, axis=1))


def pack_slots(row_values, expert_ids, slot_index, slot_shape):
    buffer = jnp.zeros(slot_shape, row_values.dtype)
    return buffer.at[expert_ids // slot_shape[1], expert_ids % slot_shape[1], slot_index].set(
        row_values
    )


def unpack_slots(buffer, expert_ids, slot_index):
    return buffer[expert_ids // buffer.shape[1], expert_ids % buffer.shape[1], slot_index]


def causal_scores(query_part, key_full, row_start):
    block_rows = query_part.shape[0]
    score_scale = 1.0 / math.sqrt(query_part.shape[2])
    scores = (
        jnp.einsum("qhd,khd->hqk", query_part, key_full, preferred_element_type=jnp.float32)
        * score_scale
    )
    key_pos = jnp.arange(key_full.shape[0], dtype=jnp.int32)
    row_pos = row_start + jnp.arange(block_rows, dtype=jnp.int32)
    allowed = key_pos[None, :] <= row_pos[:, None]
    return jnp.where(allowed[None], scores, -1e30)


def attend_forward(query_rows_all, key_full, value_full):
    sequence_length = query_rows_all.shape[0]
    block_rows = min(512, sequence_length)

    def one_block(block_index):
        row_start = block_index * block_rows
        query_part = lax.dynamic_slice_in_dim(query_rows_all, row_start, block_rows, 0)
        scores = causal_scores(query_part, key_full, row_start)
        row_max = jnp.max(scores, axis=-1, keepdims=True)
        weights = jnp.exp(scores - row_max)
        row_total = jnp.sum(weights, axis=-1, keepdims=True)
        prob_low = (weights / row_total).astype(jnp.bfloat16)
        mixed_out = jnp.einsum(
            "hqk,khd->qhd", prob_low, value_full, preferred_element_type=jnp.float32
        )
        return (mixed_out.astype(jnp.bfloat16), (row_max + jnp.log(row_total))[..., 0])

    mixed_out, log_total = lax.map(
        one_block, jnp.arange(sequence_length // block_rows, dtype=jnp.int32)
    )
    return (mixed_out.reshape(query_rows_all.shape), log_total)


def attend_backward(query_rows_all, key_full, value_full, log_total, d_mixed):
    sequence_length = query_rows_all.shape[0]
    block_rows = min(512, sequence_length)
    score_scale = 1.0 / math.sqrt(query_rows_all.shape[2])

    def one_block(running, block_index):
        d_key_sum, d_value_sum = running
        row_start = block_index * block_rows
        query_part = lax.dynamic_slice_in_dim(query_rows_all, row_start, block_rows, 0)
        d_part = lax.dynamic_slice_in_dim(d_mixed, row_start, block_rows, 0)
        scores = causal_scores(query_part, key_full, row_start)
        prob_full = jnp.exp(scores - log_total[block_index][..., None])
        prob_low = prob_full.astype(jnp.bfloat16)
        d_probs = jnp.einsum("qhd,khd->hqk", d_part, value_full, preferred_element_type=jnp.float32)
        row_delta = jnp.sum(prob_full * d_probs, axis=-1, keepdims=True)
        d_scores = (prob_full * (d_probs - row_delta)).astype(jnp.bfloat16)
        d_query_part = (
            jnp.einsum("hqk,khd->qhd", d_scores, key_full, preferred_element_type=jnp.float32)
            * score_scale
        )
        d_key_sum = (
            d_key_sum
            + jnp.einsum("hqk,qhd->khd", d_scores, query_part, preferred_element_type=jnp.float32)
            * score_scale
        )
        d_value_sum = d_value_sum + jnp.einsum(
            "hqk,qhd->khd", prob_low, d_part, preferred_element_type=jnp.float32
        )
        return ((d_key_sum, d_value_sum), d_query_part)

    zero_grad = jnp.zeros(key_full.shape, jnp.float32)
    (d_key_sum, d_value_sum), d_query = lax.scan(
        one_block,
        (zero_grad, zero_grad),
        jnp.arange(sequence_length // block_rows, dtype=jnp.int32),
    )
    return (d_query.reshape(query_rows_all.shape), d_key_sum, d_value_sum)


def routed_body(
    tokens,
    query_key_value_weight,
    w_out_t,
    w_router,
    w_in,
    w_down,
    attn_gain,
    ffn_gain,
    q_gain,
    k_gain,
    routes,
    cotangent,
):
    sequence_count = lax.axis_size("seq")
    shard_count = lax.axis_size("fsdp")
    experts = sequence_count * shard_count
    token_row_count = tokens.shape[1]
    model_width = tokens.shape[2]
    query_group_width = QUERY_HEADS // KEY_VALUE_HEADS
    capacity = 2 * token_row_count * TOPK // experts
    slot_shape = (sequence_count, shard_count, capacity, model_width)
    positions = lax.axis_index("seq") * token_row_count + jnp.arange(
        token_row_count, dtype=jnp.int32
    )
    full_qkv, full_out, full_router = (
        lax.all_gather(query_key_value_weight, ("seq", "fsdp"), axis=0, tiled=True),
        lax.all_gather(w_out_t, ("seq", "fsdp"), axis=0, tiled=True),
        lax.all_gather(w_router, ("seq", "fsdp"), axis=0, tiled=True),
    )
    resid_in = tokens[0].astype(jnp.float32)
    normed_one = rms_scale(resid_in, attn_gain).astype(jnp.bfloat16)
    projection_output = jnp.dot(normed_one, full_qkv, preferred_element_type=jnp.float32)
    q_raw = projection_output[:, : QUERY_HEADS * HEAD_DIMENSION].reshape(
        token_row_count, QUERY_HEADS, HEAD_DIMENSION
    )
    key_unnormed = projection_output[
        :, QUERY_HEADS * HEAD_DIMENSION : (QUERY_HEADS + KEY_VALUE_HEADS) * HEAD_DIMENSION
    ].reshape(token_row_count, KEY_VALUE_HEADS, HEAD_DIMENSION)
    value_per_head = (
        projection_output[:, (QUERY_HEADS + KEY_VALUE_HEADS) * HEAD_DIMENSION :]
        .reshape(token_row_count, KEY_VALUE_HEADS, HEAD_DIMENSION)
        .astype(jnp.bfloat16)
    )
    prepare = partial(head_prepare, positions=positions)
    query_rows_all = prepare(q_raw, q_gain).astype(jnp.bfloat16)
    key_per_head = prepare(key_unnormed, k_gain).astype(jnp.bfloat16)
    send_keys = jnp.repeat(key_per_head, query_group_width, axis=1)
    send_values = jnp.repeat(value_per_head, query_group_width, axis=1)
    head_queries, head_keys, head_values = (
        lax.all_to_all(query_rows_all, "seq", split_axis=1, concat_axis=0, tiled=True),
        lax.all_to_all(send_keys, "seq", split_axis=1, concat_axis=0, tiled=True),
        lax.all_to_all(send_values, "seq", split_axis=1, concat_axis=0, tiled=True),
    )
    mixed_heads, log_total = attend_forward(head_queries, head_keys, head_values)
    mixed_tok = lax.all_to_all(mixed_heads, "seq", split_axis=0, concat_axis=1, tiled=True)
    attention_result = mixed_tok.reshape(token_row_count, QUERY_HEADS * HEAD_DIMENSION)
    attn_out = jnp.einsum(
        "tj,dj->td", attention_result, full_out, preferred_element_type=jnp.float32
    )
    hidden = resid_in + attn_out
    normed_two = rms_scale(hidden, ffn_gain).astype(jnp.bfloat16)
    logits = jnp.dot(normed_two, full_router, preferred_element_type=jnp.float32)
    route_flat = routes[0].reshape(-1)
    onehot, slot_index = route_slots(route_flat, experts)
    onehot_float = onehot.reshape(token_row_count, TOPK, experts).astype(jnp.float32)
    chosen = jnp.sum(onehot_float * logits[:, None, :], axis=-1)
    row_max = jnp.max(chosen, axis=-1, keepdims=True)
    exp_part = jnp.exp(chosen - row_max)
    gate_probs = exp_part / jnp.sum(exp_part, axis=-1, keepdims=True)
    send_rows = pack_slots(jnp.repeat(normed_two, TOPK, axis=0), route_flat, slot_index, slot_shape)
    arrived = lax.all_to_all(
        lax.all_to_all(send_rows, "seq", split_axis=0, concat_axis=0, tiled=True),
        "fsdp",
        split_axis=1,
        concat_axis=1,
        tiled=True,
    )
    rows_in = arrived.reshape(-1, model_width)
    gate_weight = w_in[0]
    down_weight = w_down[0]
    gate_up = jnp.dot(rows_in, gate_weight, preferred_element_type=jnp.float32)
    gate_half = gate_up[:, :FF]
    up_half = gate_up[:, FF:]
    gate_sig = jax.nn.sigmoid(gate_half)
    silu_gate = gate_half * gate_sig
    inner_act = (silu_gate * up_half).astype(jnp.bfloat16)
    expert_out = jnp.dot(inner_act, down_weight, preferred_element_type=jnp.float32).astype(
        jnp.bfloat16
    )
    returned = lax.all_to_all(
        lax.all_to_all(
            expert_out.reshape(slot_shape), "seq", split_axis=0, concat_axis=0, tiled=True
        ),
        "fsdp",
        split_axis=1,
        concat_axis=1,
        tiled=True,
    )
    picked = (
        unpack_slots(returned, route_flat, slot_index)
        .astype(jnp.float32)
        .reshape(token_row_count, TOPK, model_width)
    )
    mixture = jnp.sum(gate_probs[..., None] * picked, axis=1)
    output = (hidden + mixture).astype(jnp.bfloat16)
    full_qkv, full_out, full_router = (
        lax.all_gather(query_key_value_weight, ("seq", "fsdp"), axis=0, tiled=True),
        lax.all_gather(w_out_t, ("seq", "fsdp"), axis=0, tiled=True),
        lax.all_gather(w_router, ("seq", "fsdp"), axis=0, tiled=True),
    )
    out_grad = cotangent[0].astype(jnp.float32)
    d_picked = (
        (gate_probs[..., None] * out_grad[:, None, :]).astype(jnp.bfloat16).reshape(-1, model_width)
    )
    d_gates = jnp.sum(picked * out_grad[:, None, :], axis=-1)
    d_send = pack_slots(d_picked, route_flat, slot_index, slot_shape)
    d_arrived = lax.all_to_all(
        lax.all_to_all(d_send, "seq", split_axis=0, concat_axis=0, tiled=True),
        "fsdp",
        split_axis=1,
        concat_axis=1,
        tiled=True,
    ).reshape(-1, model_width)
    d_inner = jnp.einsum("rd,fd->rf", d_arrived, down_weight, preferred_element_type=jnp.float32)
    d_gate_half = d_inner * up_half * gate_sig * (1.0 + gate_half * (1.0 - gate_sig))
    d_up_half = d_inner * silu_gate
    d_gate_up = jnp.concatenate([d_gate_half, d_up_half], axis=1).astype(jnp.bfloat16)
    d_w_down = jnp.einsum("rf,rd->fd", inner_act, d_arrived, preferred_element_type=jnp.float32)[
        None
    ]
    d_w_in = jnp.einsum("rd,rf->df", rows_in, d_gate_up, preferred_element_type=jnp.float32)[None]
    d_rows = jnp.einsum(
        "rf,df->rd", d_gate_up, gate_weight, preferred_element_type=jnp.float32
    ).astype(jnp.bfloat16)
    d_back = lax.all_to_all(
        lax.all_to_all(d_rows.reshape(slot_shape), "seq", split_axis=0, concat_axis=0, tiled=True),
        "fsdp",
        split_axis=1,
        concat_axis=1,
        tiled=True,
    )
    d_routed = jnp.sum(
        unpack_slots(d_back, route_flat, slot_index)
        .astype(jnp.float32)
        .reshape(token_row_count, TOPK, model_width),
        axis=1,
    )
    d_chosen = gate_probs * (d_gates - jnp.sum(gate_probs * d_gates, axis=-1, keepdims=True))
    d_logits = jnp.einsum("tk,tke->te", d_chosen, onehot_float).astype(jnp.bfloat16)
    d_normed_two = d_routed + jnp.einsum(
        "te,de->td", d_logits, full_router, preferred_element_type=jnp.float32
    )
    unused_two, pull_two = jax.vjp(rms_scale, hidden, ffn_gain)
    d_hidden_norm, d_ffn_gain = pull_two(d_normed_two)
    d_hidden = out_grad + d_hidden_norm
    d_attn = d_hidden.astype(jnp.bfloat16)
    d_attended = jnp.einsum(
        "td,dj->tj", d_attn, full_out, preferred_element_type=jnp.float32
    ).astype(jnp.bfloat16)
    d_heads = lax.all_to_all(
        d_attended.reshape(token_row_count, QUERY_HEADS, HEAD_DIMENSION),
        "seq",
        split_axis=1,
        concat_axis=0,
        tiled=True,
    )
    d_query, d_key_sum, d_value_sum = attend_backward(
        head_queries, head_keys, head_values, log_total, d_heads
    )
    seq_rows = head_queries.shape[0]
    local_cols = head_queries.shape[1] * HEAD_DIMENSION
    normed_all, d_attn_all = (
        lax.all_gather(normed_one, "seq", axis=0, tiled=True),
        lax.all_gather(d_attn, "seq", axis=0, tiled=True),
    )
    query_cols = lax.dynamic_slice_in_dim(
        full_qkv, lax.axis_index("seq") * local_cols, local_cols, 1
    )
    q_head_raw = jnp.dot(normed_all, query_cols, preferred_element_type=jnp.float32).reshape(
        head_queries.shape
    )
    seq_positions = jnp.arange(seq_rows, dtype=jnp.int32)
    unused_head, pull_head = jax.vjp(
        partial(head_prepare, positions=seq_positions), q_head_raw, q_gain
    )
    send_d_query, d_q_gain = pull_head(d_query)
    d_query_tok, grad_key_token_rows, grad_value_token_rows = (
        lax.all_to_all(
            send_d_query.astype(jnp.bfloat16), "seq", split_axis=0, concat_axis=1, tiled=True
        ).astype(send_d_query.dtype),
        lax.all_to_all(
            d_key_sum.astype(jnp.bfloat16), "seq", split_axis=0, concat_axis=1, tiled=True
        ).astype(d_key_sum.dtype),
        lax.all_to_all(
            d_value_sum.astype(jnp.bfloat16), "seq", split_axis=0, concat_axis=1, tiled=True
        ).astype(d_value_sum.dtype),
    )
    grad_key_per_head = jnp.sum(
        grad_key_token_rows.reshape(token_row_count, KEY_VALUE_HEADS, -1, HEAD_DIMENSION), axis=2
    )
    grad_value_per_head = jnp.sum(
        grad_value_token_rows.reshape(token_row_count, KEY_VALUE_HEADS, -1, HEAD_DIMENSION), axis=2
    )
    unused_k, pull_k = jax.vjp(prepare, key_unnormed, k_gain)
    grad_key_unnormed, d_k_gain = pull_k(grad_key_per_head)
    d_projected = jnp.concatenate(
        [
            d_query_tok.reshape(token_row_count, QUERY_HEADS * HEAD_DIMENSION),
            grad_key_unnormed.reshape(token_row_count, KEY_VALUE_HEADS * HEAD_DIMENSION),
            grad_value_per_head.reshape(token_row_count, KEY_VALUE_HEADS * HEAD_DIMENSION),
        ],
        axis=1,
    ).astype(jnp.bfloat16)
    d_normed_one = jnp.einsum(
        "tj,dj->td", d_projected, full_qkv, preferred_element_type=jnp.float32
    )
    unused_one, pull_one = jax.vjp(rms_scale, resid_in, attn_gain)
    d_resid_norm, d_attn_gain = pull_one(d_normed_one)
    d_tokens = (d_hidden + d_resid_norm).astype(jnp.bfloat16)[None]
    rows_dev = model_width // experts
    kv_count = 2 * KEY_VALUE_HEADS * HEAD_DIMENSION
    kv_grads = d_projected[:, QUERY_HEADS * HEAD_DIMENSION :]
    first_rows = normed_one
    summed = lax.psum_scatter(
        jnp.concatenate(
            [
                jnp.einsum("tc,tj->cj", first_rows, kv_grads, preferred_element_type=jnp.float32),
                jnp.einsum("tc,te->ce", normed_two, d_logits, preferred_element_type=jnp.float32),
            ],
            axis=1,
        ),
        ("seq", "fsdp"),
        scatter_dimension=0,
        tiled=True,
    )
    d_query_low = send_d_query.reshape(seq_rows, local_cols).astype(jnp.bfloat16)
    attended_heads = mixed_heads.reshape(seq_rows, local_cols)
    normed_order = (
        normed_all.reshape(seq_rows, sequence_count, shard_count, rows_dev)
        .transpose(0, 2, 1, 3)
        .reshape(seq_rows, model_width)
    )
    d_attn_order = (
        d_attn_all.reshape(seq_rows, sequence_count, shard_count, rows_dev)
        .transpose(0, 2, 1, 3)
        .reshape(seq_rows, model_width)
    )
    first_rows = normed_order
    head_sums = lax.psum_scatter(
        jnp.concatenate(
            [
                jnp.einsum(
                    "tc,tj->cj", first_rows, d_query_low, preferred_element_type=jnp.float32
                ),
                jnp.einsum(
                    "tc,tj->cj", d_attn_order, attended_heads, preferred_element_type=jnp.float32
                ),
            ],
            axis=1,
        ).astype(jnp.bfloat16),
        "fsdp",
        scatter_dimension=0,
        tiled=True,
    ).astype(jnp.float32)
    row_sums = (
        lax.all_to_all(
            head_sums.astype(jnp.bfloat16), "seq", split_axis=0, concat_axis=1, tiled=True
        )
        .astype(head_sums.dtype)
        .reshape(rows_dev, sequence_count, 2, local_cols)
    )
    d_w_query = row_sums[:, :, 0].reshape(rows_dev, QUERY_HEADS * HEAD_DIMENSION)
    d_w_out_t = row_sums[:, :, 1].reshape(rows_dev, QUERY_HEADS * HEAD_DIMENSION)
    d_w_qkv = jnp.concatenate([d_w_query, summed[:, :kv_count]], axis=1)
    d_w_router = summed[:, kv_count:]
    d_attn_gain, d_ffn_gain, d_q_gain, d_k_gain = lax.psum(
        (d_attn_gain, d_ffn_gain, d_q_gain, d_k_gain), ("seq", "fsdp")
    )
    return (
        output[None],
        d_tokens,
        d_w_qkv,
        d_w_out_t,
        d_w_router,
        d_w_in,
        d_w_down,
        d_attn_gain,
        d_ffn_gain,
        d_q_gain,
        d_k_gain,
    )


MESH = pl.DeviceIdType.MESH
VMEM_LIMIT = 60 * 2**20


class Place:
    def __init__(self):
        seq, shard = lax.axis_index("seq"), lax.axis_index("fsdp")
        self.z, self.x = seq // 2, seq % 2
        self.y, self.c = shard // 2, shard % 2
        self.z0, self.z1 = self.z % 2, self.z // 2
        self.low, self.high = self.z == 0, self.z == 3
        self.inner = (self.z0 + self.z1) == 1
        self.me = self.block(self.z, self.x, self.y, self.c)

    def device(self, z, x, y, c):
        return (z * 2 + x, y * 2 + c)

    def block(self, z, x, y, c):
        return (z * 2 + x) * 4 + y * 2 + c

    @property
    def by_x(self):
        return self.device(self.z, 1 - self.x, self.y, self.c)

    @property
    def by_y(self):
        return self.device(self.z, self.x, 1 - self.y, self.c)

    @property
    def by_core(self):
        return self.device(self.z, self.x, self.y, 1 - self.c)

    def by_z(self, step):
        return self.device(self.z + step, self.x, self.y, self.c)

    def near(self, k):
        return [self.z, 1 + self.z0, 2 - 2 * self.z0 + self.z1, 3 - 3 * self.z1][k]

    def onward(self, k):
        return [None, 2 * self.z1 - 1, 1 - 2 * self.z1, 2 * self.z1 - 1][k]

    def far(self, k):
        return self.near(3 - k)

    def toward(self, k):
        return [1 - 2 * self.z1, 1 - 2 * self.z0, 1 - 2 * self.z1][k]

    def greet(self, sides):
        barrier = pltpu.get_barrier_semaphore()
        for side in sides:
            if side != "z":
                target = {"x": self.by_x, "y": self.by_y, "core": self.by_core}[side]
                pl.semaphore_signal(barrier, inc=1, device_id=target, device_id_type=MESH)
        count = len([side for side in sides if side != "z"])
        if "z" in sides:

            @pl.when(jnp.logical_not(self.low))
            def _():
                pl.semaphore_signal(barrier, inc=1, device_id=self.by_z(-1), device_id_type=MESH)

            @pl.when(jnp.logical_not(self.high))
            def _():
                pl.semaphore_signal(barrier, inc=1, device_id=self.by_z(1), device_id_type=MESH)

            count = count + 1 + (self.z0 + self.z1) % 2
        pl.semaphore_wait(barrier, count)


def send(source, target, send_sem, recv_sem, device):
    pltpu.make_async_remote_copy(
        src_ref=source,
        dst_ref=target,
        send_sem=send_sem,
        recv_sem=recv_sem,
        device_id=device,
        device_id_type=MESH,
    ).start()


def await_bytes(ref, sem):
    pltpu.make_async_copy(ref, ref, sem).wait()


G_Z, G_X, G_Y, G_DX, G_DY, G_C0 = 0, 1, 2, 3, 4, 5
G_KINDS = 9


def gather_steps(place, own, out, ss, rs, zs, local_sem):
    p = place
    rows = out.shape[1]
    half = rows // 2
    x, y, c = p.x, p.y, p.c

    def cols(q):
        return [
            p.block(q, x, y, c),
            p.block(q, 1 - x, y, c),
            p.block(q, x, 1 - y, c),
            p.block(q, 1 - x, 1 - y, c),
        ]

    def to_core(q, j, src=None):
        b = cols(q)[j]
        send(out.at[b] if src is None else src, out.at[b], ss.at[q, G_C0 + j], rs.at[q, G_C0 + j], p.by_core)

    def plane_out(k):
        q = p.near(k)
        b = cols(q)[0]
        if k == 0:
            src = own
            for step, there in ((1, p.high), (-1, p.low)):

                @pl.when(jnp.logical_not(there))
                def _():
                    send(src, out.at[b], zs.at[q, 0 if step > 0 else 1], rs.at[q, G_Z], p.by_z(step))

            pltpu.make_async_copy(own, out.at[b], local_sem).start()
        else:
            src = out.at[b]
            await_bytes(src, rs.at[q, G_Z])

            @pl.when(p.inner)
            def _():
                send(src, src, zs.at[q, 0], rs.at[q, G_Z], p.by_z(p.onward(k)))

        send(src, out.at[b], ss.at[q, G_X], rs.at[q, G_X], p.by_x)
        send(src, out.at[b], ss.at[q, G_Y], rs.at[q, G_Y], p.by_y)
        to_core(q, 0, src)

    def plane_turn(k):
        q = p.near(k)
        bx, by = out.at[cols(q)[1]], out.at[cols(q)[2]]
        await_bytes(bx, rs.at[q, G_X])
        first = bx.at[pl.ds(0, half)]
        send(first, first, ss.at[q, G_DY], rs.at[q, G_DY], p.by_y)
        to_core(q, 1)
        await_bytes(by, rs.at[q, G_Y])
        second = by.at[pl.ds(half, half)]
        send(second, second, ss.at[q, G_DX], rs.at[q, G_DX], p.by_x)
        to_core(q, 2)

    def plane_end(k):
        q = p.near(k)
        bd = out.at[cols(q)[3]]
        await_bytes(bd.at[pl.ds(0, half)], rs.at[q, G_DY])
        await_bytes(bd.at[pl.ds(half, half)], rs.at[q, G_DX])
        to_core(q, 3)

    def plane_core(k):
        q = p.near(k)
        for j in range(4):
            await_bytes(own, rs.at[q, G_C0 + j])

    def finish():
        piece = own.at[pl.ds(0, half)]
        for q in range(4):
            for kind in (G_X, G_Y, G_C0, G_C0 + 1, G_C0 + 2, G_C0 + 3):
                await_bytes(own, ss.at[q, kind])
            for kind in (G_DX, G_DY):
                await_bytes(piece, ss.at[q, kind])
        for there, slot in ((p.high, 0), (p.low, 1)):

            @pl.when(jnp.logical_not(there))
            def _():
                await_bytes(own, zs.at[p.z, slot])

        for k in range(1, 4):

            @pl.when(p.inner)
            def _():
                await_bytes(own, zs.at[p.near(k), 0])

    return plane_out, plane_turn, plane_end, plane_core, finish


def gather_all_kernel(own, out, ss, rs, zs, local_sem):
    p = Place()
    p.greet(("x", "y", "core", "z"))
    plane_out, plane_turn, plane_end, plane_core, finish = gather_steps(p, own, out, ss, rs, zs, local_sem)
    plane_out(0)
    plane_out(1)
    plane_turn(0)
    plane_out(2)
    plane_end(0)
    plane_turn(1)
    plane_out(3)
    plane_end(1)
    plane_turn(2)
    plane_end(2)
    plane_turn(3)
    plane_end(3)
    for k in range(4):
        plane_core(k)
    pltpu.make_async_copy(own, out.at[p.me], local_sem).wait()
    finish()


def gather_all(own, blocks, collective_id):
    dma = pltpu.SemaphoreType.DMA
    return pl.pallas_call(
        gather_all_kernel,
        out_shape=jax.ShapeDtypeStruct((blocks, *own.shape), own.dtype),
        in_specs=[pl.BlockSpec(memory_space=pl.ANY)],
        out_specs=pl.BlockSpec(memory_space=pl.ANY),
        scratch_shapes=[dma((4, G_KINDS)), dma((4, G_KINDS)), dma((4, 2)), dma],
        compiler_params=pltpu.CompilerParams(
            collective_id=collective_id, has_side_effects=True, vmem_limit_bytes=VMEM_LIMIT
        ),
        name="gather_all",
    )(own)


def sum_all_parts(p, part, held, core_in, x_half, y_half, x_in, y_in, z_in, out, ls, cs, cr, ss, rs, zs, zr):
    rows, width = part.shape[1], part.shape[2]
    half = rows // 2
    x, y, c = p.x, p.y, p.c

    def columns(q):
        return [(q, x, y), (q, 1 - x, y), (q, x, 1 - y), (q, 1 - x, 1 - y)]

    def start():
        for k in range(4):
            q = p.far(k)
            for j, (zz, xx, yy) in reversed(list(enumerate(columns(q)))):
                send(
                    part.at[p.block(zz, xx, yy, 1 - c)],
                    core_in.at[q * 4 + j],
                    cs.at[q, j],
                    cr.at[q, j],
                    p.by_core,
                )
                pltpu.make_async_copy(
                    part.at[p.block(zz, xx, yy, c)], held.at[q * 4 + j], ls.at[q, j]
                ).start()

    chunk = 16

    def add(target, source, count):
        @pl.loop(0, count // chunk)
        def _(i):
            at = pl.ds(pl.multiple_of(i * chunk, chunk), chunk)
            target[at, :] = (
                target[at, :].astype(jnp.float32) + source[at, :].astype(jnp.float32)
            ).astype(target.dtype)

    def plane_core(k, js=(3, 1, 2, 0)):
        q = p.far(k)
        for j in js:
            slot = q * 4 + j
            await_bytes(held.at[slot], ls.at[q, j])
            await_bytes(core_in.at[slot], cr.at[q, j])
            add(held.at[slot], core_in.at[slot], rows)
            if j == 3:
                send(held.at[slot, pl.ds(0, half)], y_half.at[q], ss.at[q, 0], rs.at[q, 0], p.by_y)
                send(held.at[slot, pl.ds(half, half)], x_half.at[q], ss.at[q, 1], rs.at[q, 1], p.by_x)

    def plane_turn(k):
        q = p.far(k)
        await_bytes(y_half.at[q], rs.at[q, 0])
        add(held.at[q * 4 + 1, pl.ds(0, half)], y_half.at[q], half)
        send(held.at[q * 4 + 1], x_in.at[q], ss.at[q, 2], rs.at[q, 2], p.by_x)
        await_bytes(x_half.at[q], rs.at[q, 1])
        add(held.at[q * 4 + 2, pl.ds(half, half)], x_half.at[q], half)
        send(held.at[q * 4 + 2], y_in.at[q], ss.at[q, 3], rs.at[q, 3], p.by_y)

    def plane_end(k):
        q = p.far(k)
        mine = held.at[q * 4]
        await_bytes(x_in.at[q], rs.at[q, 2])
        add(mine, x_in.at[q], rows)
        await_bytes(y_in.at[q], rs.at[q, 3])
        add(mine, y_in.at[q], rows)
        if k < 3:
            step = p.toward(k)
            slot = (1 - step) // 2

            @pl.when(p.inner)
            def _():
                await_bytes(z_in.at[slot, q], zr.at[slot, q])
                add(mine, z_in.at[slot, q], rows)

            send(mine, z_in.at[slot, q], zs.at[k], zr.at[slot, q], p.by_z(step))
        else:
            for slot, there in ((0, p.low), (1, p.high)):

                @pl.when(jnp.logical_not(there))
                def _():
                    await_bytes(z_in.at[slot, q], zr.at[slot, q])
                    add(mine, z_in.at[slot, q], rows)

            out[...] = mine[...]

    def finish():
        whole, piece = x_in.at[0], x_half.at[0]
        for q in range(4):
            for j in range(4):
                await_bytes(whole, cs.at[q, j])
            for kind in (0, 1):
                await_bytes(piece, ss.at[q, kind])
            for kind in (2, 3):
                await_bytes(whole, ss.at[q, kind])
        for k in range(3):
            await_bytes(whole, zs.at[k])

    return start, plane_core, plane_turn, plane_end, finish


def sum_all_kernel(part, both, out, pair, both_held, both_in, pair_sems, *scratch):
    p = Place()
    p.greet(("x", "y", "core", "z"))
    start, plane_core, plane_turn, plane_end, finish = sum_all_parts(p, part, *scratch[:7], out, *scratch[7:])
    rows = both.shape[3]

    def pair_sum(first):
        for s in (first, first + 1):
            for y in range(2):
                add_rows(both_held.at[s, y], both_in.at[s, y], rows)

    start()
    send(both.at[:, :, 1 - p.c], both_in, pair_sems.at[0], pair_sems.at[1], p.by_core)
    pltpu.make_async_copy(both.at[:, :, p.c], both_held, pair_sems.at[2]).start()
    plane_core(0)
    plane_core(1)
    plane_turn(0)
    await_bytes(both_held, pair_sems.at[2])
    await_bytes(both_in, pair_sems.at[1])
    pair_sum(0)
    plane_core(2)
    plane_turn(1)
    plane_end(0)
    pair_sum(2)
    plane_core(3)
    plane_turn(2)
    plane_end(1)
    pair_sum(4)
    pair_sum(6)
    pltpu.make_async_copy(both_held, pair, pair_sems.at[2]).start()
    plane_turn(3)
    plane_end(2)
    plane_end(3)
    finish()
    await_bytes(both_in, pair_sems.at[0])
    pltpu.make_async_copy(both_held, pair, pair_sems.at[2]).wait()


def sum_all_scratch(rows, width):
    dma = pltpu.SemaphoreType.DMA
    bf16 = jnp.bfloat16
    return [
        pltpu.VMEM((16, rows, width), bf16),
        pltpu.VMEM((16, rows, width), bf16),
        pltpu.VMEM((4, rows // 2, width), bf16),
        pltpu.VMEM((4, rows // 2, width), bf16),
        pltpu.VMEM((4, rows, width), bf16),
        pltpu.VMEM((4, rows, width), bf16),
        pltpu.VMEM((2, 4, rows, width), bf16),
        dma((4, 4)),
        dma((4, 4)),
        dma((4, 4)),
        dma((4, 4)),
        dma((4, 4)),
        dma((3,)),
        dma((2, 4)),
    ]


def sum_all(part, both, collective_id):
    blocks, rows, width = part.shape
    both = both.reshape(blocks // 4, 2, 2, rows, -1)
    pair = (blocks // 4, 2, rows, both.shape[4])
    anywhere = pl.BlockSpec(memory_space=pl.ANY)
    return pl.pallas_call(
        sum_all_kernel,
        out_shape=[
            jax.ShapeDtypeStruct((rows, width), part.dtype),
            jax.ShapeDtypeStruct(pair, both.dtype),
        ],
        in_specs=[anywhere] * 2,
        out_specs=[pl.BlockSpec(memory_space=pltpu.VMEM), anywhere],
        scratch_shapes=[
            pltpu.VMEM(pair, both.dtype),
            pltpu.VMEM(pair, both.dtype),
            pltpu.SemaphoreType.DMA((3,)),
            *sum_all_scratch(rows, width),
        ],
        compiler_params=pltpu.CompilerParams(
            collective_id=collective_id, has_side_effects=True, vmem_limit_bytes=VMEM_LIMIT
        ),
        name="sum_all",
    )(part, both)


def gather_seq_kernel(own, out, ss, rs, zs, local_sem):
    p = Place()
    p.greet(("x", "z"))

    def at(q, x):
        return out.at[q * 2 + x]

    def plane_out(k):
        q = p.near(k)
        there = at(q, p.x)
        if k == 0:
            src = own
            for step, end in ((1, p.high), (-1, p.low)):

                @pl.when(jnp.logical_not(end))
                def _():
                    send(src, there, zs.at[q, 0 if step > 0 else 1], rs.at[q, 0], p.by_z(step))

            pltpu.make_async_copy(own, there, local_sem).start()
        else:
            src = there
            await_bytes(src, rs.at[q, 0])

            @pl.when(p.inner)
            def _():
                send(src, src, zs.at[q, 0], rs.at[q, 0], p.by_z(p.onward(k)))

        send(src, there, ss.at[q], rs.at[q, 1], p.by_x)

    for k in range(4):
        plane_out(k)
    for k in range(4):
        await_bytes(own, rs.at[p.near(k), 1])
    pltpu.make_async_copy(own, at(p.z, p.x), local_sem).wait()
    for q in range(4):
        await_bytes(own, ss.at[q])
    for there, slot in ((p.high, 0), (p.low, 1)):

        @pl.when(jnp.logical_not(there))
        def _():
            await_bytes(own, zs.at[p.z, slot])

    for k in range(1, 4):

        @pl.when(p.inner)
        def _():
            await_bytes(own, zs.at[p.near(k), 0])


def gather_seq(own, collective_id):
    dma = pltpu.SemaphoreType.DMA
    return pl.pallas_call(
        gather_seq_kernel,
        out_shape=jax.ShapeDtypeStruct((8, *own.shape), own.dtype),
        in_specs=[pl.BlockSpec(memory_space=pl.ANY)],
        out_specs=pl.BlockSpec(memory_space=pl.ANY),
        scratch_shapes=[dma((4,)), dma((4, 2)), dma((4, 2)), dma],
        compiler_params=pltpu.CompilerParams(
            collective_id=collective_id, has_side_effects=True, vmem_limit_bytes=VMEM_LIMIT
        ),
        name="gather_seq",
    )(own)


def add_rows(target, source, count, chunk=16):
    @pl.loop(0, count // chunk)
    def _(i):
        at = pl.ds(pl.multiple_of(i * chunk, chunk), chunk)
        target[at, :] = (
            target[at, :].astype(jnp.float32) + source[at, :].astype(jnp.float32)
        ).astype(target.dtype)


def sum_seq_kernel(part, out, held, x_in, z_in, ls, ss, rs, zs, zr):
    p = Place()
    p.greet(("x", "z"))
    rows = part.shape[1]
    for k in range(4):
        q = p.far(k)
        send(part.at[q * 2 + 1 - p.x], x_in.at[q], ss.at[q], rs.at[q], p.by_x)
        pltpu.make_async_copy(part.at[q * 2 + p.x], held.at[q], ls.at[q]).start()
    for k in range(4):
        q = p.far(k)
        mine = held.at[q]
        await_bytes(mine, ls.at[q])
        await_bytes(x_in.at[q], rs.at[q])
        add_rows(mine, x_in.at[q], rows)
        if k < 3:
            step = p.toward(k)
            slot = (1 - step) // 2

            @pl.when(p.inner)
            def _():
                await_bytes(z_in.at[slot, q], zr.at[slot, q])
                add_rows(mine, z_in.at[slot, q], rows)

            send(mine, z_in.at[slot, q], zs.at[k], zr.at[slot, q], p.by_z(step))
        else:
            for slot, there in ((0, p.low), (1, p.high)):

                @pl.when(jnp.logical_not(there))
                def _():
                    await_bytes(z_in.at[slot, q], zr.at[slot, q])
                    add_rows(mine, z_in.at[slot, q], rows)

            out[...] = mine[...]
    for q in range(4):
        await_bytes(x_in.at[0], ss.at[q])
    for k in range(3):
        await_bytes(x_in.at[0], zs.at[k])


def sum_seq(part, collective_id):
    _, rows, width = part.shape
    dma = pltpu.SemaphoreType.DMA
    bf16 = jnp.bfloat16
    return pl.pallas_call(
        sum_seq_kernel,
        out_shape=jax.ShapeDtypeStruct((rows, width), part.dtype),
        in_specs=[pl.BlockSpec(memory_space=pl.ANY)],
        out_specs=pl.BlockSpec(memory_space=pltpu.VMEM),
        scratch_shapes=[
            pltpu.VMEM((4, rows, width), bf16),
            pltpu.VMEM((4, rows, width), bf16),
            pltpu.VMEM((2, 4, rows, width), bf16),
            dma((4,)),
            dma((4,)),
            dma((4,)),
            dma((3,)),
            dma((2, 4)),
        ],
        compiler_params=pltpu.CompilerParams(
            collective_id=collective_id, has_side_effects=True, vmem_limit_bytes=VMEM_LIMIT
        ),
        name="sum_seq",
    )(part)


def seq_peer(p, d):
    return ((p.z * 2 + p.x + d) % 8, p.y * 2 + p.c)


def greet_seq(p, sides=("y", "core")):
    barrier = pltpu.get_barrier_semaphore()
    for d in range(1, 8):
        pl.semaphore_signal(barrier, inc=1, device_id=seq_peer(p, d), device_id_type=MESH)
    for side in sides:
        target = {"y": p.by_y, "core": p.by_core}[side]
        pl.semaphore_signal(barrier, inc=1, device_id=target, device_id_type=MESH)
    pl.semaphore_wait(barrier, 7 + len(sides))


def enter_kernel(own, pieces, rows_out, columns, ss, rs, zs, cs, cr, ys, yr, ks, kr, local_sems):
    p = Place()
    greet_seq(p)
    place, shard = p.z * 2 + p.x, p.y * 2 + p.c
    mine = place * 4 + shard

    def rows_at(q, x):
        return rows_out.at[q * 2 + x]

    def plane_out(k):
        q = p.near(k)
        there = rows_at(q, p.x)
        if k == 0:
            src = own
            for step, end in ((1, p.high), (-1, p.low)):

                @pl.when(jnp.logical_not(end))
                def _():
                    send(src, there, zs.at[q, 0 if step > 0 else 1], rs.at[q, 0], p.by_z(step))

            pltpu.make_async_copy(own, there, local_sems.at[0]).start()
        else:
            src = there
            await_bytes(src, rs.at[q, 0])

            @pl.when(p.inner)
            def _():
                send(src, src, zs.at[q, 0], rs.at[q, 0], p.by_z(p.onward(k)))

        send(src, there, ss.at[q], rs.at[q, 1], p.by_x)

    def pass_on(d):
        block = ((place + 8 - d) % 8) * 4 + shard
        src = pieces.at[place] if d == 0 else columns.at[block]
        if d > 0:
            await_bytes(src, cr.at[d])
        send(src, columns.at[block], ys.at[d], yr.at[d], p.by_y)
        send(src, columns.at[block], ks.at[0, d], kr.at[0, d], p.by_core)

    plane_out(0)
    for d in range(1, 8):
        send(pieces.at[(place + d) % 8], columns.at[mine], cs.at[d], cr.at[d], seq_peer(p, d))
    pltpu.make_async_copy(pieces.at[place], columns.at[mine], local_sems.at[1]).start()
    pass_on(0)
    plane_out(1)
    for d in (1, 2, 7):
        pass_on(d)
    plane_out(2)
    for d in (6, 3, 5):
        pass_on(d)
    plane_out(3)
    pass_on(4)
    other = p.y * 2 + 1 - p.c
    across = (1 - p.y) * 2 + p.c
    piece = pieces.at[0]
    for d in (0, 1, 2, 7, 6, 3, 5, 4):
        block = columns.at[((place + 8 - d) % 8) * 4 + across]
        await_bytes(block, yr.at[d])
        send(block, block, ks.at[1, d], kr.at[1, d], p.by_core)
    for k in range(4):
        await_bytes(own, rs.at[p.near(k), 1])
    for d in range(8):
        await_bytes(piece, kr.at[0, d])
        await_bytes(piece, kr.at[1, d])
    pltpu.make_async_copy(own, rows_at(p.z, p.x), local_sems.at[0]).wait()
    pltpu.make_async_copy(pieces.at[place], columns.at[mine], local_sems.at[1]).wait()
    for q in range(4):
        await_bytes(own, ss.at[q])
    for there, slot in ((p.high, 0), (p.low, 1)):

        @pl.when(jnp.logical_not(there))
        def _():
            await_bytes(own, zs.at[p.z, slot])

    for k in range(1, 4):

        @pl.when(p.inner)
        def _():
            await_bytes(own, zs.at[p.near(k), 0])

    for d in range(8):
        if d > 0:
            await_bytes(piece, cs.at[d])
        await_bytes(piece, ys.at[d])
        await_bytes(piece, ks.at[0, d])
        await_bytes(piece, ks.at[1, d])


def enter(own, pieces, collective_id):
    dma = pltpu.SemaphoreType.DMA
    count, piece_rows, piece_width = pieces.shape
    return pl.pallas_call(
        enter_kernel,
        out_shape=[
            jax.ShapeDtypeStruct((count, *own.shape), own.dtype),
            jax.ShapeDtypeStruct((count * 4, piece_rows, piece_width), pieces.dtype),
        ],
        in_specs=[pl.BlockSpec(memory_space=pl.ANY)] * 2,
        out_specs=[pl.BlockSpec(memory_space=pl.ANY)] * 2,
        scratch_shapes=[
            dma((4,)),
            dma((4, 2)),
            dma((4, 2)),
            dma((8,)),
            dma((8,)),
            dma((8,)),
            dma((8,)),
            dma((2, 8)),
            dma((2, 8)),
            dma((2,)),
        ],
        compiler_params=pltpu.CompilerParams(
            collective_id=collective_id, has_side_effects=True, vmem_limit_bytes=VMEM_LIMIT
        ),
        name="enter",
    )(own, pieces)


def leave_kernel(
    part, cols, tokens, d_hidden, gain, gains,
    d_tokens, cols_out, gains_out,
    held, x_in, z_in, c_held, c_core, c_y, g_send, g_in,
    ls, ss, rs, zs, zr, cl, cs, cr, ys, yr, ts, tr, gs, gr,
):
    p = Place()
    greet_seq(p)
    rows = part.shape[1]
    place = p.z * 2 + p.x
    for turn, side in ((0, 1 - p.y), (1, p.y)):
        send(cols.at[:, side, 1 - p.c], c_core.at[turn], cs.at[turn], cr.at[turn], p.by_core)
        pltpu.make_async_copy(cols.at[:, side, p.c], c_held.at[turn], cl.at[turn]).start()
    for k in range(4):
        q = p.far(k)
        send(part.at[q * 2 + 1 - p.x], x_in.at[q], ss.at[q], rs.at[q], p.by_x)
        pltpu.make_async_copy(part.at[q * 2 + p.x], held.at[q], ls.at[q]).start()
    piece_rows = c_held.shape[2]
    order = [(place + d) % 8 for d in range(1, 9)]
    for turn in range(2):
        await_bytes(c_held.at[turn], cl.at[turn])
        await_bytes(c_core.at[turn], cr.at[turn])
        for i, s in enumerate(order):
            add_rows(c_held.at[turn, s], c_core.at[turn, s], piece_rows)
            if turn == 0:
                send(c_held.at[0, s], c_y.at[s], ys.at[s], yr.at[s], p.by_y)

    def turn_in(i):
        s = order[i]
        await_bytes(c_y.at[s], yr.at[s])
        add_rows(c_held.at[1, s], c_y.at[s], piece_rows)
        if i < 7:
            send(c_held.at[1, s], cols_out.at[place], ts.at[i], tr.at[i], seq_peer(p, i + 1))
        else:
            pltpu.make_async_copy(c_held.at[1, s], cols_out.at[place], ts.at[7]).start()

    for k in range(4):
        q = p.far(k)
        mine = held.at[q]
        await_bytes(mine, ls.at[q])
        await_bytes(x_in.at[q], rs.at[q])
        add_rows(mine, x_in.at[q], rows)
        if k < 3:
            step = p.toward(k)
            slot = (1 - step) // 2

            @pl.when(p.inner)
            def _():
                await_bytes(z_in.at[slot, q], zr.at[slot, q])
                add_rows(mine, z_in.at[slot, q], rows)

            send(mine, z_in.at[slot, q], zs.at[k], zr.at[slot, q], p.by_z(step))
            for i in ((0, 1), (2, 3), (4, 5, 6, 7))[k]:
                turn_in(i)
        else:
            for slot, there in ((0, p.low), (1, p.high)):

                @pl.when(jnp.logical_not(there))
                def _():
                    await_bytes(z_in.at[slot, q], zr.at[slot, q])
                    add_rows(mine, z_in.at[slot, q], rows)

    mine = held.at[p.z]
    g_send[0] = jnp.zeros_like(g_send[0])
    chunk = 16

    @pl.loop(0, rows // chunk)
    def _(i):
        at = pl.ds(pl.multiple_of(i * chunk, chunk), chunk)
        d_out = mine[at, :].astype(jnp.float32)
        x = tokens[at, :].astype(jnp.float32)
        scale = lax.rsqrt(jnp.mean(x * x, axis=-1, keepdims=True) + EPS)
        u = d_out * gain[...]
        dot = jnp.mean(u * x, axis=-1, keepdims=True)
        d_x = scale * u - x * (scale * scale * scale * dot)
        d_tokens[at, :] = (d_hidden[at, :] + d_x).astype(d_tokens.dtype)
        terms = d_out * x * scale
        g_send[0] += terms[:8] + terms[8:]

    first = jnp.sum(g_send[0], axis=0, keepdims=True)
    row = lax.broadcasted_iota(jnp.int32, g_send[0].shape, 0)
    g_send[0] = jnp.where(row == 0, first, gains[...])
    for t, target in enumerate((p.by_core, p.by_y, p.by_x)):
        send(g_send.at[t], g_in.at[t], gs.at[t], gr.at[t], target)
        await_bytes(g_in.at[t], gr.at[t])
        g_send[t + 1] = g_send[t] + g_in[t]
    for d in (1, 2, 3):
        target = p.device((p.z + d) % 4, p.x, p.y, p.c)
        send(g_send.at[3], g_in.at[3 + p.z], gs.at[2 + d], gr.at[2 + d], target)
    g_in[3 + p.z] = g_send[3]
    for d in (1, 2, 3):
        await_bytes(g_in.at[0], gr.at[2 + d])
    gains_out[...] = g_in[3] + g_in[4] + g_in[5] + g_in[6]

    piece = c_y.at[0]
    for i in range(8):
        if i < 7:
            await_bytes(piece, tr.at[i])
        await_bytes(piece, ts.at[i])
        await_bytes(piece, ys.at[i])
    for turn in range(2):
        await_bytes(c_core.at[turn], cs.at[turn])
    for q in range(4):
        await_bytes(x_in.at[0], ss.at[q])
    for k in range(3):
        await_bytes(x_in.at[0], zs.at[k])
    for t in range(6):
        await_bytes(g_in.at[0], gs.at[t])


def leave(part, cols, tokens, d_hidden, gain, gains, collective_id):
    _, rows, width = part.shape
    piece_rows, piece_width = cols.shape[3:]
    dma = pltpu.SemaphoreType.DMA
    bf16, f32 = jnp.bfloat16, jnp.float32
    anywhere, vmem = pl.BlockSpec(memory_space=pl.ANY), pl.BlockSpec(memory_space=pltpu.VMEM)
    return pl.pallas_call(
        leave_kernel,
        out_shape=[
            jax.ShapeDtypeStruct((rows, width), bf16),
            jax.ShapeDtypeStruct((8, piece_rows, piece_width), bf16),
            jax.ShapeDtypeStruct(gains.shape, f32),
        ],
        in_specs=[anywhere] * 2 + [vmem] * 4,
        out_specs=[vmem, anywhere, vmem],
        scratch_shapes=[
            pltpu.VMEM((4, rows, width), bf16),
            pltpu.VMEM((4, rows, width), bf16),
            pltpu.VMEM((2, 4, rows, width), bf16),
            pltpu.VMEM((2, 8, piece_rows, piece_width), bf16),
            pltpu.VMEM((2, 8, piece_rows, piece_width), bf16),
            pltpu.VMEM((8, piece_rows, piece_width), bf16),
            pltpu.VMEM((4, *gains.shape), f32),
            pltpu.VMEM((7, *gains.shape), f32),
            dma((4,)),
            dma((4,)),
            dma((4,)),
            dma((3,)),
            dma((2, 4)),
            dma((2,)),
            dma((2,)),
            dma((2,)),
            dma((8,)),
            dma((8,)),
            dma((8,)),
            dma((7,)),
            dma((6,)),
            dma((6,)),
        ],
        compiler_params=pltpu.CompilerParams(
            collective_id=collective_id, has_side_effects=True, vmem_limit_bytes=VMEM_LIMIT
        ),
        name="leave",
    )(part, cols, tokens, d_hidden, gain, gains)


NT = (((1,), (1,)), ((), ()))
TILE = 256
WIDE = 512


def mxu(a, b, dims=(((1,), (0,)), ((), ()))):
    return lax.dot_general(a, b, dims, preferred_element_type=jnp.float32)


def experts_kernel(
    own, cot_all, w_in_hbm, w_down_hbm,
    rows_all, out_part, d_part, x_all, d_expert_all, inner_all, d_gate_up_all,
    w_in, w_down, row_buf, cot_buf, pick, pick_t, gates, d_gates, x, cot, d_expert,
    by_d_gate, by_d_up, inner, d_gate_up, held, out_stage, d_stage,
    ss, rs, zs, local_sem, load_sems, store_sems,
):
    p = Place()
    bf16, f32 = jnp.bfloat16, jnp.float32
    width = cot_all.shape[2]
    blocks = 8
    slots = gates.shape[0]
    capacity = slots // blocks
    tokens = row_buf.shape[2]
    group = 4
    experts = rows_all.shape[0]
    p.greet(("x", "y", "core", "z"))
    plane_out, plane_turn, plane_end, plane_core, finish = gather_steps(
        p, own, rows_all, ss, rs, zs, local_sem
    )

    def weights(start):
        for i, (src, dst) in enumerate(((w_in_hbm, w_in), (w_down_hbm, w_down))):
            copy = pltpu.make_async_copy(src, dst, load_sems.at[i])
            copy.start() if start else copy.wait()

    def cot_load(k):
        return pltpu.make_async_copy(
            cot_all.at[pl.ds(p.near(k) * blocks, blocks)], cot_buf.at[k % 2], load_sems.at[2 + k]
        )

    def row_load(k):
        return pltpu.make_async_copy(
            rows_all.at[pl.ds(p.near(k) * blocks, blocks)], row_buf.at[k % 2], load_sems.at[6 + k]
        )

    def arrived(k):
        plane_core(k)
        if k == 0:
            pltpu.make_async_copy(own, rows_all.at[p.me], local_sem).wait()
        row_load(k).start()

    at_slot = {}

    def store(k, i, src, dst):
        if (k, i) not in at_slot:
            at_slot[k, i] = pltpu.make_async_copy(src, dst, store_sems.at[i, k % 2])
        return at_slot[k, i]

    def stores(k):
        q = p.near(k)
        at = pl.ds(q * slots, slots)
        plane = pl.ds(q * blocks, blocks)
        return [
            (x, x_all.at[at]),
            (d_expert, d_expert_all.at[at]),
            (inner, inner_all.at[at]),
            (d_gate_up, d_gate_up_all.at[at]),
            (out_stage, out_part.at[plane]),
            (d_stage, d_part.at[plane]),
        ]

    def put(k, i):
        store(k, i, *stores(k)[i]).start()

    def free(k, i):
        if k > 0:
            store(k - 1, i, *stores(k - 1)[i]).wait()

    def pick_rows(k):
        lane = lax.broadcasted_iota(jnp.int32, (8, 128), 1)
        line = lax.broadcasted_iota(jnp.int32, (8, 128), 0)
        select = jnp.where((lane == line * experts + p.me) & (line < 3), 1.0, 0.0).astype(bf16)
        slot_id = lax.broadcasted_iota(jnp.int32, (capacity, tokens), 0).astype(f32) + 1.0
        rows, cots = row_buf.at[k % 2], cot_buf.at[k % 2]
        lines = mxu(select, rows[:, :, width:].reshape(blocks * tokens, 128), NT)
        for j in range(blocks):
            g, i = j // group, j % group
            mine = lines[:, j * tokens : (j + 1) * tokens]
            chosen = jnp.where(mine[2:3] == slot_id, 1.0, 0.0)
            gate = jnp.sum(chosen * (mine[0:1] + mine[1:2]), axis=1, keepdims=True)
            gates[j * capacity : (j + 1) * capacity, :] = jnp.broadcast_to(gate, (capacity, 128))
            lead = [jnp.zeros((capacity, tokens), bf16)] * i
            tail = [jnp.zeros((capacity, tokens), bf16)] * (group - 1 - i)
            pick[g, i * capacity : (i + 1) * capacity, :] = jnp.concatenate(
                lead + [chosen.astype(bf16)] + tail, axis=1
            )
            lead = [jnp.zeros((tokens, capacity), f32)] * i
            tail = [jnp.zeros((tokens, capacity), f32)] * (group - 1 - i)
            pick_t[g, i * tokens : (i + 1) * tokens, :] = jnp.concatenate(
                lead + [chosen.T] + tail, axis=1
            ).astype(bf16)
        for g in range(blocks // group):
            at = pl.ds(g * group * capacity, group * capacity)
            which = pl.ds(g * group, group)

            @pl.loop(0, width // WIDE)
            def _(n):
                cols = pl.ds(pl.multiple_of(n * WIDE, WIDE), WIDE)
                row_tile = rows[which, :, cols].reshape(group * tokens, WIDE)
                x[at, cols] = mxu(pick[g], row_tile).astype(bf16)
                cot_tile = cots[which, :, cols].reshape(group * tokens, WIDE)
                picked = mxu(pick[g], cot_tile)
                cot[at, cols] = picked.astype(bf16)
                scale = jnp.concatenate([gates[at, :]] * (WIDE // 128), axis=1)
                d_expert[at, cols] = (scale * picked).astype(bf16)

    def up(k):
        ff = inner.shape[1]

        @pl.loop(0, ff // TILE)
        def _(n):
            cols = pl.ds(pl.multiple_of(n * TILE, TILE), TILE)
            gate = mxu(x[...], w_in[:, cols])
            raised = mxu(x[...], w_in[:, pl.ds(pl.multiple_of(ff + n * TILE, TILE), TILE)])
            sig = jax.nn.sigmoid(gate)
            silu = gate * sig
            inner[:, cols] = (silu * raised).astype(bf16)
            by_d_up[:, cols] = silu
            by_d_gate[:, cols] = raised * sig * (1.0 + gate * (1.0 - sig))

    def d_up(k):
        ff = inner.shape[1]

        @pl.loop(0, ff // TILE)
        def _(n):
            cols = pl.ds(pl.multiple_of(n * TILE, TILE), TILE)
            d_inner = mxu(d_expert[...], w_down[cols, :], NT)
            d_gate_up[:, cols] = (d_inner * by_d_gate[:, cols]).astype(bf16)
            d_gate_up[:, pl.ds(pl.multiple_of(ff + n * TILE, TILE), TILE)] = (
                d_inner * by_d_up[:, cols]
            ).astype(bf16)

    def spread(stage):
        @pl.loop(0, width // WIDE)
        def _(n):
            cols = pl.ds(pl.multiple_of(n * WIDE, WIDE), WIDE)
            for g in range(blocks // group):
                part = held[g * group * capacity : (g + 1) * group * capacity, cols]
                result = mxu(pick_t[g], part).astype(bf16)
                stage[g * group : (g + 1) * group, :, cols] = result.reshape(group, tokens, WIDE)

    def down(k):
        d_gates[...] = jnp.zeros_like(d_gates)

        @pl.loop(0, width // TILE)
        def _(n):
            cols = pl.ds(pl.multiple_of(n * TILE, TILE), TILE)
            result = mxu(inner[...], w_down[:, cols]).astype(bf16).astype(f32)
            product = result * cot[:, cols].astype(f32)
            total = product[:, :128]
            for j in range(1, TILE // 128):
                total = total + product[:, j * 128 : (j + 1) * 128]
            d_gates[...] += total
            scale = jnp.concatenate([gates[...]] * (TILE // 128), axis=1)
            held[:, cols] = (scale * result).astype(bf16)

    def d_down(k):
        total = jnp.sum(d_gates[...], axis=1, keepdims=True)
        high = total.astype(bf16).astype(f32)
        lane = lax.broadcasted_iota(jnp.int32, (slots, 128), 1)
        info = jnp.where(lane == p.me, high, jnp.where(lane == experts + p.me, total - high, 0.0))
        info = info.astype(bf16)
        for g in range(blocks // group):
            result = mxu(pick_t[g], info[g * group * capacity : (g + 1) * group * capacity])
            d_stage[g * group : (g + 1) * group, :, width:] = result.astype(bf16).reshape(
                group, tokens, 128
            )

        @pl.loop(0, width // TILE)
        def _(n):
            cols = pl.ds(pl.multiple_of(n * TILE, TILE), TILE)
            held[:, cols] = mxu(d_gate_up[...], w_in[cols, :], NT).astype(bf16)

    plane_out(0)
    weights(True)
    cot_load(0).start()
    plane_turn(0)
    plane_out(1)
    plane_end(0)
    arrived(0)
    weights(False)
    after = {
        (0, 1): ((plane_turn, 1), (plane_out, 2)),
        (0, 3): ((plane_end, 1),),
        (0, 5): ((arrived, 1),),
        (1, 0): ((plane_turn, 2), (plane_out, 3)),
        (1, 3): ((plane_end, 2),),
        (1, 5): ((arrived, 2),),
        (2, 0): ((plane_turn, 3),),
        (2, 3): ((plane_end, 3),),
        (2, 5): ((arrived, 3),),
    }
    for k in range(4):

        def service(i):
            for step, plane in after.get((k, i), ()):
                step(plane)

        row_load(k).wait()
        cot_load(k).wait()
        if k < 3:
            cot_load(k + 1).start()
        free(k, 0)
        free(k, 1)
        pick_rows(k)
        put(k, 0)
        put(k, 1)
        service(0)
        free(k, 2)
        up(k)
        put(k, 2)
        service(1)
        free(k, 3)
        d_up(k)
        put(k, 3)
        service(2)
        free(k, 4)
        down(k)
        service(3)
        spread(out_stage)
        put(k, 4)
        service(4)
        free(k, 5)
        d_down(k)
        service(5)
        spread(d_stage)
        put(k, 5)
    for i in range(6):
        free(4, i)
    finish()


def experts_gathered(own, cot_all, w_in, w_down, capacity, collective_id):
    tokens, wide = own.shape
    experts, _, width = cot_all.shape
    ff = w_down.shape[0]
    slots = 8 * capacity
    dma = pltpu.SemaphoreType.DMA
    bf16, f32 = jnp.bfloat16, jnp.float32
    anywhere = pl.BlockSpec(memory_space=pl.ANY)

    def array(*shape):
        return jax.ShapeDtypeStruct(shape, bf16)

    return pl.pallas_call(
        experts_kernel,
        out_shape=[
            array(experts, tokens, wide),
            array(experts, tokens, width),
            array(experts, tokens, wide),
            array(experts * capacity, width),
            array(experts * capacity, width),
            array(experts * capacity, ff),
            array(experts * capacity, 2 * ff),
        ],
        in_specs=[anywhere] * 4,
        out_specs=[anywhere] * 7,
        scratch_shapes=[
            pltpu.VMEM(w_in.shape, bf16),
            pltpu.VMEM(w_down.shape, bf16),
            pltpu.VMEM((2, 8, tokens, wide), bf16),
            pltpu.VMEM((2, 8, tokens, width), bf16),
            pltpu.VMEM((2, 4 * capacity, 4 * tokens), bf16),
            pltpu.VMEM((2, 4 * tokens, 4 * capacity), bf16),
            pltpu.VMEM((slots, 128), f32),
            pltpu.VMEM((slots, 128), f32),
            pltpu.VMEM((slots, width), bf16),
            pltpu.VMEM((slots, width), bf16),
            pltpu.VMEM((slots, width), bf16),
            pltpu.VMEM((slots, ff), f32),
            pltpu.VMEM((slots, ff), f32),
            pltpu.VMEM((slots, ff), bf16),
            pltpu.VMEM((slots, 2 * ff), bf16),
            pltpu.VMEM((slots, width), bf16),
            pltpu.VMEM((8, tokens, width), bf16),
            pltpu.VMEM((8, tokens, wide), bf16),
            dma((4, G_KINDS)),
            dma((4, G_KINDS)),
            dma((4, 2)),
            dma,
            dma((10,)),
            dma((6, 2)),
        ],
        compiler_params=pltpu.CompilerParams(
            collective_id=collective_id, has_side_effects=True, vmem_limit_bytes=VMEM_LIMIT
        ),
        name="experts",
    )(own, cot_all, w_in, w_down)


TN = (((0,), (0,)), ((), ()))


def back_kernel(
    own, pair, rows_all, columns_hbm, normed_hbm, queries, keys, values, attended,
    q_raw, k_raw, cosine, sine, q_gain, k_gain,
    d_normed, d_columns, head_gains, mixture,
    d_attn, columns, normed, d_heads, d_query, d_key, d_value, d_proj, logits, q_sum, k_sum,
    held, x_in, y_in, z_in,
    gs, gr, gz, load_sems, local_sem, hs, ys, yr, xs, xr, zs, zr,
):
    p = Place()
    bf16, f32 = jnp.bfloat16, jnp.float32
    p.greet(("x", "y", "z"))
    rows, wide = own.shape
    length, head_cols = queries.shape
    heads = head_cols // HEAD_DIMENSION
    width = normed.shape[1]
    proj_cols = d_proj.shape[1]
    plane_rows = 2 * rows
    score_scale = 1.0 / math.sqrt(HEAD_DIMENSION)
    place, shard = p.z * 2 + p.x, p.y * 2 + p.c

    def rows_at(q, x):
        return d_attn.at[q * 2 + x]

    def gather_out(k):
        q = p.near(k)
        there = rows_at(q, p.x)
        if k == 0:
            src = own
            for step, end in ((1, p.high), (-1, p.low)):

                @pl.when(jnp.logical_not(end))
                def _():
                    send(src, there, gz.at[q, 0 if step > 0 else 1], gr.at[q, 0], p.by_z(step))

            pltpu.make_async_copy(own, there, local_sem).start()
        else:
            src = there
            await_bytes(src, gr.at[q, 0])

            @pl.when(p.inner)
            def _():
                send(src, src, gz.at[q, 0], gr.at[q, 0], p.by_z(p.onward(k)))

        send(src, there, gs.at[q], gr.at[q, 1], p.by_x)

    def gather_in(k):
        if k == 0:
            pltpu.make_async_copy(own, rows_at(p.z, p.x), local_sem).wait()
        await_bytes(own, gr.at[p.near(k), 1])

    def at_pair(q, x, y):
        return pair.at[q * 4 + x * 2 + y]

    def sum_start():
        for k in range(4):
            q = p.far(k)
            for j, x in ((1, 1 - p.x), (0, p.x)):
                send(at_pair(q, x, 1 - p.y), y_in.at[q * 2 + j], ys.at[q * 2 + j], yr.at[q * 2 + j], p.by_y)
                pltpu.make_async_copy(at_pair(q, x, p.y), held.at[q * 2 + j], hs.at[q * 2 + j]).start()

    def sum_turn(k):
        q = p.far(k)
        for j in (1, 0):
            slot = q * 2 + j
            await_bytes(held.at[slot], hs.at[slot])
            await_bytes(y_in.at[slot], yr.at[slot])
            add_rows(held.at[slot], y_in.at[slot], rows)
            if j == 1:
                send(held.at[slot], x_in.at[q], xs.at[q], xr.at[q], p.by_x)

    def sum_end(k):
        q = p.far(k)
        mine = held.at[q * 2]
        await_bytes(x_in.at[q], xr.at[q])
        add_rows(mine, x_in.at[q], rows)
        if k < 3:
            step = p.toward(k)
            slot = (1 - step) // 2

            @pl.when(p.inner)
            def _():
                await_bytes(z_in.at[slot, q], zr.at[slot, q])
                add_rows(mine, z_in.at[slot, q], rows)

            send(mine, z_in.at[slot, q], zs.at[k], zr.at[slot, q], p.by_z(step))
        else:
            for slot, there in ((0, p.low), (1, p.high)):

                @pl.when(jnp.logical_not(there))
                def _():
                    await_bytes(z_in.at[slot, q], zr.at[slot, q])
                    add_rows(mine, z_in.at[slot, q], rows)

            mixture[...] = mine[...]

    def attention(q):
        row_start = pl.multiple_of(q * plane_rows, plane_rows)
        at = pl.ds(row_start, plane_rows)

        @pl.loop(0, head_cols // TILE)
        def _(n):
            cols = pl.ds(pl.multiple_of(n * TILE, TILE), TILE)
            grad = d_attn[pl.ds(q * 2, 2), :, :width].reshape(plane_rows, width)
            weight_cols = pl.ds(pl.multiple_of(proj_cols + n * TILE, TILE), TILE)
            d_heads[at, cols] = mxu(grad, columns[:, weight_cols]).astype(bf16)

        def block(count):
            key, value = keys[:count], values[:count]
            row_pos = row_start + lax.broadcasted_iota(jnp.int32, (plane_rows, count), 0)
            allowed = lax.broadcasted_iota(jnp.int32, (plane_rows, count), 1) <= row_pos

            @pl.loop(0, heads)
            def _(h):
                cols = pl.ds(pl.multiple_of(h * HEAD_DIMENSION, HEAD_DIMENSION), HEAD_DIMENSION)
                query, d_out = queries[at, cols], d_heads[at, cols]
                scores = jnp.where(allowed, mxu(query, key, NT) * score_scale, -1e30)
                raised = jnp.exp(scores - jnp.max(scores, axis=-1, keepdims=True))
                prob = raised / jnp.sum(raised, axis=-1, keepdims=True)
                d_prob = mxu(d_out, value, NT)
                delta = jnp.sum(prob * d_prob, axis=-1, keepdims=True)
                d_scores = (prob * (d_prob - delta)).astype(bf16)
                d_query[at, cols] = mxu(d_scores, key) * score_scale
                d_key[:count] += mxu(d_scores, query, TN) * score_scale
                d_value[:count] += mxu(prob.astype(bf16), d_out, TN)

        half = length // 2

        @pl.when(q < 2)
        def _():
            block(half)

        @pl.when(q >= 2)
        def _():
            block(length)

    def unrotate(grad, at):
        swapped = jnp.concatenate(
            [grad[:, HEAD_DIMENSION // 2 :], grad[:, : HEAD_DIMENSION // 2]], axis=1
        )
        return grad * cosine[at, :] + swapped * sine[at, :]

    def raw_grads():
        q_sum[...] = jnp.zeros_like(q_sum)
        k_sum[...] = jnp.zeros_like(k_sum)

        def one(grad, raw, gain, total, at):
            turned = unrotate(grad, at)
            scale = lax.rsqrt(jnp.mean(raw * raw, axis=-1, keepdims=True) + EPS)
            total[...] += jnp.sum((turned * raw * scale).reshape(-1, 8, HEAD_DIMENSION), axis=0)
            u = turned * gain[...]
            dot = jnp.mean(u * raw, axis=-1, keepdims=True)
            return (scale * u - raw * (scale * scale * scale * dot)).astype(bf16)

        chunk = 128

        @pl.loop(0, length // chunk)
        def _(i):
            at = pl.ds(pl.multiple_of(i * chunk, chunk), chunk)
            for h in range(heads):
                cols = slice(h * HEAD_DIMENSION, (h + 1) * HEAD_DIMENSION)
                d_proj[at, cols] = one(d_query[at, cols], q_raw[at, cols], q_gain, q_sum, at)
            d_proj[at, head_cols : head_cols + HEAD_DIMENSION] = one(
                d_key[at, :], k_raw[at, :], k_gain, k_sum, at
            )
            d_proj[at, head_cols + HEAD_DIMENSION :] = d_value[at, :].astype(bf16)

        line = lax.broadcasted_iota(jnp.int32, (8, HEAD_DIMENSION), 0)
        head_gains[...] = jnp.where(
            line == 0,
            jnp.sum(q_sum[...], axis=0, keepdims=True),
            jnp.where(line == 1, jnp.sum(k_sum[...], axis=0, keepdims=True), 0.0),
        )

    def normed_grads():
        @pl.loop(0, width // TILE)
        def _(n):
            cols = pl.ds(pl.multiple_of(n * TILE, TILE), TILE)
            part = mxu(d_proj[...], columns[cols, :proj_cols], NT).astype(bf16)
            d_normed[:, :, cols] = part.reshape(length // rows, rows, TILE)

    def column_grads(source, value, first, count):
        @pl.loop(0, width // TILE)
        def _(n):
            cols = pl.ds(pl.multiple_of(n * TILE, TILE), TILE)
            part = source[..., cols].reshape(length, TILE)
            d_columns[cols, first : first + count] = mxu(part, value[...], TN).astype(bf16)

    loads = [
        pltpu.make_async_copy(columns_hbm, columns, load_sems.at[0]),
        pltpu.make_async_copy(normed_hbm, normed, load_sems.at[1]),
        pltpu.make_async_copy(rows_all.at[:, shard], d_attn, load_sems.at[2]),
    ]
    gather_out(0)
    loads[0].start()
    loads[1].start()
    sum_start()
    d_key[...] = jnp.zeros_like(d_key)
    d_value[...] = jnp.zeros_like(d_value)
    loads[0].wait()
    gather_in(0)
    gather_out(1)
    attention(p.near(0))
    gather_out(2)
    gather_in(1)
    attention(p.near(1))
    sum_turn(0)
    gather_out(3)
    gather_in(2)
    attention(p.near(2))
    sum_end(0)
    sum_turn(1)
    gather_in(3)
    attention(p.near(3))
    raw_grads()
    sum_end(1)
    normed_grads()
    loads[1].wait()
    column_grads(normed, d_proj, 0, proj_cols)
    sum_turn(2)
    column_grads(d_attn.at[:, :, pl.ds(0, width)], attended, proj_cols, head_cols)
    line = lax.broadcasted_iota(jnp.int32, (128, 128), 0)
    lane = lax.broadcasted_iota(jnp.int32, (128, 128), 1)
    router_cols = rows_all.shape[0] * rows_all.shape[1] // 8
    mine = (line == lane + place * router_cols) & (lane < router_cols)
    select = jnp.where(mine, 1.0, 0.0).astype(bf16)
    logits[...] = mxu(d_attn[:, :, width:].reshape(length, 128), select).astype(bf16)
    sum_end(2)
    for q in range(4):
        await_bytes(own, gs.at[q])
    for there, slot in ((p.high, 0), (p.low, 1)):

        @pl.when(jnp.logical_not(there))
        def _():
            await_bytes(own, gz.at[p.z, slot])

    for k in range(1, 4):

        @pl.when(p.inner)
        def _():
            await_bytes(own, gz.at[p.near(k), 0])

    loads[2].start()
    loads[2].wait()
    column_grads(d_attn.at[:, :, pl.ds(0, width)], logits, proj_cols + head_cols, 128)
    sum_turn(3)
    sum_end(3)
    piece = x_in.at[0]
    for i in range(8):
        await_bytes(piece, ys.at[i])
    for q in range(4):
        await_bytes(piece, xs.at[q])
    for k in range(3):
        await_bytes(piece, zs.at[k])


def back(
    own, pair, rows_all, columns, normed, queries, keys, values, attended,
    q_raw, k_raw, cosine, sine, q_gain, k_gain, collective_id,
):
    rows, wide = own.shape
    length, head_cols = queries.shape
    width = normed.shape[1]
    proj_cols = head_cols + 2 * HEAD_DIMENSION
    dma = pltpu.SemaphoreType.DMA
    bf16, f32 = jnp.bfloat16, jnp.float32
    anywhere, vmem = pl.BlockSpec(memory_space=pl.ANY), pl.BlockSpec(memory_space=pltpu.VMEM)
    return pl.pallas_call(
        back_kernel,
        out_shape=[
            jax.ShapeDtypeStruct((length // rows, rows, width), bf16),
            jax.ShapeDtypeStruct(columns.shape, bf16),
            jax.ShapeDtypeStruct((8, HEAD_DIMENSION), f32),
            jax.ShapeDtypeStruct((rows, width), bf16),
        ],
        in_specs=[anywhere] * 5 + [vmem] * 10,
        out_specs=[vmem] * 4,
        scratch_shapes=[
            pltpu.VMEM((8, rows, wide), bf16),
            pltpu.VMEM(columns.shape, bf16),
            pltpu.VMEM((length, width), bf16),
            pltpu.VMEM((length, head_cols), bf16),
            pltpu.VMEM((length, head_cols), f32),
            pltpu.VMEM((length, HEAD_DIMENSION), f32),
            pltpu.VMEM((length, HEAD_DIMENSION), f32),
            pltpu.VMEM((length, proj_cols), bf16),
            pltpu.VMEM((length, 128), bf16),
            pltpu.VMEM((8, HEAD_DIMENSION), f32),
            pltpu.VMEM((8, HEAD_DIMENSION), f32),
            pltpu.VMEM((8, rows, width), bf16),
            pltpu.VMEM((4, rows, width), bf16),
            pltpu.VMEM((8, rows, width), bf16),
            pltpu.VMEM((2, 4, rows, width), bf16),
            dma((4,)),
            dma((4, 2)),
            dma((4, 2)),
            dma((3,)),
            dma,
            dma((8,)),
            dma((8,)),
            dma((8,)),
            dma((4,)),
            dma((4,)),
            dma((3,)),
            dma((2, 4)),
        ],
        compiler_params=pltpu.CompilerParams(
            collective_id=collective_id, has_side_effects=True, vmem_limit_bytes=VMEM_LIMIT
        ),
        name="back",
    )(
        own, pair, rows_all, columns, normed, queries, keys, values, attended,
        q_raw, k_raw, cosine, sine, q_gain, k_gain,
    )


def head_columns(weight, group_index):
    rows = weight.shape[0]
    query_width = QUERY_HEADS * HEAD_DIMENSION
    key_width = KEY_VALUE_HEADS * HEAD_DIMENSION
    query = weight[:, :query_width].reshape(rows, len(group_index), -1).transpose(1, 0, 2)
    keys = weight[:, query_width : query_width + key_width].reshape(rows, KEY_VALUE_HEADS, -1)
    values = weight[:, query_width + key_width :].reshape(rows, KEY_VALUE_HEADS, -1)
    keys = jnp.stack([keys[:, group] for group in group_index])
    values = jnp.stack([values[:, group] for group in group_index])
    return jnp.concatenate([query, keys, values], axis=2)


def gathered_body(
    tokens,
    query_key_value_weight,
    w_out_t,
    w_router,
    w_in,
    w_down,
    attn_gain,
    ffn_gain,
    q_gain,
    k_gain,
    routes,
    cotangent,
):
    bf16, f32 = jnp.bfloat16, jnp.float32
    both = ("seq", "fsdp")
    seq_size = lax.axis_size("seq")
    shard_size = lax.axis_size("fsdp")
    experts = seq_size * shard_size
    rows = tokens.shape[1]
    width = tokens.shape[2]
    length = rows * seq_size
    weight_rows = query_key_value_weight.shape[0]
    heads = QUERY_HEADS // seq_size
    head_cols = heads * HEAD_DIMENSION
    kv_cols = HEAD_DIMENSION
    proj_cols = head_cols + 2 * kv_cols
    all_cols = proj_cols + head_cols
    spare_cols = 128
    group_index = [s * heads * KEY_VALUE_HEADS // QUERY_HEADS for s in range(seq_size)]
    capacity = 2 * rows * TOPK // experts

    pieces = jnp.concatenate(
        [
            head_columns(query_key_value_weight, group_index),
            w_out_t.reshape(weight_rows, seq_size, head_cols).transpose(1, 0, 2),
            jnp.broadcast_to(
                jnp.pad(w_router, ((0, 0), (0, spare_cols - experts))),
                (seq_size, weight_rows, spare_cols),
            ),
        ],
        axis=2,
    )
    resid_in = tokens[0].astype(f32)
    normed_one = rms_scale(resid_in, attn_gain).astype(bf16)
    normed_all, columns = enter(normed_one, pieces, 1)
    normed_all = normed_all.reshape(length, width)
    columns = columns.reshape(width, -1)
    proj_weight = columns[:, :proj_cols]
    out_weight = columns[:, proj_cols:all_cols]
    full_router = columns[:, all_cols : all_cols + experts]
    columns, cot_own = lax.optimization_barrier((columns, cotangent[0]))
    cot_all = lax.all_gather(cot_own, both)

    projected = jnp.dot(normed_all, proj_weight, preferred_element_type=f32)
    seq_positions = jnp.arange(length, dtype=jnp.int32)
    prepare = partial(head_prepare, positions=seq_positions)
    q_raw = projected[:, :head_cols].reshape(length, heads, HEAD_DIMENSION)
    k_raw = projected[:, head_cols : head_cols + kv_cols].reshape(length, 1, HEAD_DIMENSION)
    values = projected[:, head_cols + kv_cols :].astype(bf16).reshape(length, 1, HEAD_DIMENSION)
    queries = prepare(q_raw, q_gain).astype(bf16)
    keys = prepare(k_raw, k_gain).astype(bf16)
    repeat_keys = jnp.repeat(keys, heads, axis=1)
    repeat_values = jnp.repeat(values, heads, axis=1)
    mixed_heads, unused_total = attend_forward(queries, repeat_keys, repeat_values)
    attended = mixed_heads.reshape(length, head_cols)
    attn_part = jnp.einsum("tj,dj->td", attended, out_weight, preferred_element_type=f32)
    attn_out = sum_seq(attn_part.astype(bf16).reshape(seq_size, rows, width), 2)
    hidden = resid_in + attn_out.astype(f32)
    normed_two = rms_scale(hidden, ffn_gain).astype(bf16)

    logits = jnp.dot(normed_two, full_router, preferred_element_type=f32)
    onehot = routes[0][:, :, None] == jnp.arange(experts, dtype=jnp.int32)
    onehot_float = onehot.astype(f32)
    named = jnp.sum(onehot_float, axis=1)
    order = jnp.arange(rows, dtype=jnp.int32)
    upto = (order[None, :] <= order[:, None]).astype(bf16)
    slot_info = named * jnp.dot(upto, named.astype(bf16), preferred_element_type=f32)
    chosen = jnp.sum(onehot_float * logits[:, None, :], axis=-1)
    row_max = jnp.max(chosen, axis=-1, keepdims=True)
    exp_part = jnp.exp(chosen - row_max)
    gate_probs = exp_part / jnp.sum(exp_part, axis=-1, keepdims=True)
    gate_dense = jnp.sum(onehot_float * gate_probs[..., None], axis=1)

    gate_high = gate_dense.astype(bf16)
    gate_low = (gate_dense - gate_high.astype(f32)).astype(bf16)
    route_info = jnp.concatenate([gate_high, gate_low, slot_info.astype(bf16)], axis=1)
    route_info = jnp.pad(route_info, ((0, 0), (0, 128 - route_info.shape[1] % 128)))
    gate_weight = w_in[0]
    down_weight = w_down[0]
    rows_all, out_part, d_part, rows_in, d_expert, inner_act, d_gate_up = experts_gathered(
        jnp.concatenate([normed_two, route_info], axis=1),
        cot_all,
        gate_weight,
        down_weight,
        capacity,
        3,
    )
    d_back, out_pair = sum_all(d_part, out_part, 5)
    d_back = d_back.astype(f32)
    d_w_down = jnp.einsum("rf,rd->fd", inner_act, d_expert, preferred_element_type=f32)[None]
    d_w_in = jnp.einsum("rd,rf->df", rows_in, d_gate_up, preferred_element_type=f32)[None]

    d_gate_dense = d_back[:, width : width + experts] + d_back[:, width + experts : width + 2 * experts]
    d_gates = jnp.sum(onehot_float * d_gate_dense[:, None, :], axis=-1)
    d_chosen = gate_probs * (d_gates - jnp.sum(gate_probs * d_gates, axis=-1, keepdims=True))
    d_logits = jnp.sum(d_chosen[..., None] * onehot_float, axis=1).astype(bf16)
    d_normed_two = d_back[:, :width] + jnp.einsum(
        "te,de->td", d_logits, full_router, preferred_element_type=f32
    )
    out_grad = cotangent[0].astype(f32)
    unused_two, pull_two = jax.vjp(rms_scale, hidden, ffn_gain)
    d_hidden_norm, d_ffn_gain = pull_two(d_normed_two)
    d_hidden = out_grad + d_hidden_norm
    d_attn = d_hidden.astype(bf16)

    d_send = jnp.concatenate([d_attn, jnp.pad(d_logits, ((0, 0), (0, 128 - experts)))], axis=1)
    half_dim = HEAD_DIMENSION // 2
    frequency = ROPE_BASE ** (-2.0 * jnp.arange(half_dim, dtype=f32) / HEAD_DIMENSION)
    angles = seq_positions.astype(f32)[:, None] * frequency[None, :]
    cosine, sine = jnp.cos(angles), jnp.sin(angles)
    d_normed_part, d_columns, head_gains, mixture = back(
        d_send,
        out_pair.reshape(2 * seq_size, rows, width),
        rows_all.reshape(seq_size, shard_size, rows, -1),
        columns,
        normed_all,
        queries.reshape(length, head_cols),
        keys.reshape(length, kv_cols),
        values.reshape(length, kv_cols),
        attended,
        q_raw.reshape(length, head_cols),
        k_raw.reshape(length, kv_cols),
        jnp.concatenate([cosine, cosine], axis=1),
        jnp.concatenate([sine, -sine], axis=1),
        q_gain[None],
        k_gain[None],
        6,
    )
    output = (hidden + mixture.astype(f32)).astype(bf16)
    router_cols = experts // seq_size
    gains = jnp.pad(
        jnp.stack(
            [d_ffn_gain, jnp.pad(head_gains[:2].reshape(-1), (0, width - 2 * HEAD_DIMENSION))]
        ),
        ((1, 5), (0, 0)),
    )
    d_tokens, d_pieces, gains = leave(
        d_normed_part,
        d_columns.reshape(seq_size, 2, shard_size // 2, weight_rows, all_cols + spare_cols),
        tokens[0],
        d_hidden,
        attn_gain[None],
        gains,
        7,
    )
    d_tokens = d_tokens[None]
    d_pieces = d_pieces.astype(f32).transpose(1, 0, 2)
    per_group = seq_size // KEY_VALUE_HEADS
    d_kv = d_pieces[:, :, head_cols:proj_cols].reshape(
        weight_rows, KEY_VALUE_HEADS, per_group, 2, kv_cols
    )
    d_kv = jnp.sum(d_kv, axis=2).transpose(0, 2, 1, 3).reshape(weight_rows, -1)
    d_w_qkv = jnp.concatenate([d_pieces[:, :, :head_cols].reshape(weight_rows, -1), d_kv], axis=1)
    d_w_out_t = d_pieces[:, :, proj_cols:all_cols].reshape(weight_rows, -1)
    d_w_router = d_pieces[:, :, all_cols : all_cols + router_cols].reshape(weight_rows, experts)
    d_attn_gain, d_ffn_gain = gains[0], gains[1]
    d_q_gain = gains[2, :HEAD_DIMENSION]
    d_k_gain = gains[2, HEAD_DIMENSION : 2 * HEAD_DIMENSION]
    return (
        output[None],
        d_tokens,
        d_w_qkv,
        d_w_out_t,
        d_w_router,
        d_w_in,
        d_w_down,
        d_attn_gain,
        d_ffn_gain,
        d_q_gain,
        d_k_gain,
    )


def gathered_fits(mesh):
    return mesh.shape["seq"] == 8 and mesh.shape["fsdp"] == 4


def solution(mesh):
    return jax.shard_map(
        gathered_body if gathered_fits(mesh) else routed_body,
        mesh=mesh,
        in_specs=(
            P("fsdp", "seq", None),
            P(("seq", "fsdp"), None),
            P(("seq", "fsdp"), None),
            P(("seq", "fsdp"), None),
            P(("seq", "fsdp"), None, None),
            P(("seq", "fsdp"), None, None),
            P(),
            P(),
            P(),
            P(),
            P("fsdp", "seq", None),
            P("fsdp", "seq", None),
        ),
        out_specs=(
            P("fsdp", "seq", None),
            P("fsdp", "seq", None),
            P(("seq", "fsdp"), None),
            P(("seq", "fsdp"), None),
            P(("seq", "fsdp"), None),
            P(("seq", "fsdp"), None, None),
            P(("seq", "fsdp"), None, None),
            P(),
            P(),
            P(),
            P(),
        ),
        check_vma=False,
    )
```

```python
from functools import partial
import math

import jax
import jax.numpy as jnp
from jax import lax
from jax.experimental import pallas as pl
from jax.experimental.pallas import tpu as pltpu
from jax.sharding import PartitionSpec as P

QUERY_HEADS = 32
KEY_VALUE_HEADS = 4
HEAD_DIMENSION = 128
FF = 768
TOPK = 8


EPS = 1e-06
ROPE_BASE = 1000000.0


def rms_scale(values, gain):
    return values * lax.rsqrt(jnp.mean(values * values, axis=-1, keepdims=True) + EPS) * gain


def rotate(values, positions):
    half_dim = values.shape[-1] // 2
    frequency = ROPE_BASE ** (-2.0 * jnp.arange(half_dim, dtype=jnp.float32) / values.shape[-1])
    angles = positions.astype(jnp.float32)[:, None] * frequency[None, :]
    cosine = jnp.cos(angles)[:, None, :]
    sine_part = jnp.sin(angles)[:, None, :]
    first_half = values[..., :half_dim]
    second = values[..., half_dim:]
    return jnp.concatenate(
        [first_half * cosine - second * sine_part, second * cosine + first_half * sine_part],
        axis=-1,
    )


def head_prepare(raw_heads, gain, positions):
    return rotate(rms_scale(raw_heads, gain), positions)


def route_slots(route_flat, experts):
    onehot = (route_flat[:, None] == jnp.arange(experts, dtype=jnp.int32)[None, :]).astype(
        jnp.int32
    )
    earlier = jnp.cumsum(onehot, axis=0) - onehot
    return (onehot, jnp.sum(earlier * onehot, axis=1))


def pack_slots(row_values, expert_ids, slot_index, slot_shape):
    buffer = jnp.zeros(slot_shape, row_values.dtype)
    return buffer.at[expert_ids // slot_shape[1], expert_ids % slot_shape[1], slot_index].set(
        row_values
    )


def unpack_slots(buffer, expert_ids, slot_index):
    return buffer[expert_ids // buffer.shape[1], expert_ids % buffer.shape[1], slot_index]


def causal_scores(query_part, key_full, row_start):
    block_rows = query_part.shape[0]
    score_scale = 1.0 / math.sqrt(query_part.shape[2])
    scores = (
        jnp.einsum("qhd,khd->hqk", query_part, key_full, preferred_element_type=jnp.float32)
        * score_scale
    )
    key_pos = jnp.arange(key_full.shape[0], dtype=jnp.int32)
    row_pos = row_start + jnp.arange(block_rows, dtype=jnp.int32)
    allowed = key_pos[None, :] <= row_pos[:, None]
    return jnp.where(allowed[None], scores, -1e30)


def attend_forward(query_rows_all, key_full, value_full):
    sequence_length = query_rows_all.shape[0]
    block_rows = min(512, sequence_length)

    def one_block(block_index):
        row_start = block_index * block_rows
        query_part = lax.dynamic_slice_in_dim(query_rows_all, row_start, block_rows, 0)
        scores = causal_scores(query_part, key_full, row_start)
        row_max = jnp.max(scores, axis=-1, keepdims=True)
        weights = jnp.exp(scores - row_max)
        row_total = jnp.sum(weights, axis=-1, keepdims=True)
        prob_low = (weights / row_total).astype(jnp.bfloat16)
        mixed_out = jnp.einsum(
            "hqk,khd->qhd", prob_low, value_full, preferred_element_type=jnp.float32
        )
        return (mixed_out.astype(jnp.bfloat16), (row_max + jnp.log(row_total))[..., 0])

    mixed_out, log_total = lax.map(
        one_block, jnp.arange(sequence_length // block_rows, dtype=jnp.int32)
    )
    return (mixed_out.reshape(query_rows_all.shape), log_total)


def attend_backward(query_rows_all, key_full, value_full, log_total, d_mixed):
    sequence_length = query_rows_all.shape[0]
    block_rows = min(512, sequence_length)
    score_scale = 1.0 / math.sqrt(query_rows_all.shape[2])

    def one_block(running, block_index):
        d_key_sum, d_value_sum = running
        row_start = block_index * block_rows
        query_part = lax.dynamic_slice_in_dim(query_rows_all, row_start, block_rows, 0)
        d_part = lax.dynamic_slice_in_dim(d_mixed, row_start, block_rows, 0)
        scores = causal_scores(query_part, key_full, row_start)
        prob_full = jnp.exp(scores - log_total[block_index][..., None])
        prob_low = prob_full.astype(jnp.bfloat16)
        d_probs = jnp.einsum("qhd,khd->hqk", d_part, value_full, preferred_element_type=jnp.float32)
        row_delta = jnp.sum(prob_full * d_probs, axis=-1, keepdims=True)
        d_scores = (prob_full * (d_probs - row_delta)).astype(jnp.bfloat16)
        d_query_part = (
            jnp.einsum("hqk,khd->qhd", d_scores, key_full, preferred_element_type=jnp.float32)
            * score_scale
        )
        d_key_sum = (
            d_key_sum
            + jnp.einsum("hqk,qhd->khd", d_scores, query_part, preferred_element_type=jnp.float32)
            * score_scale
        )
        d_value_sum = d_value_sum + jnp.einsum(
            "hqk,qhd->khd", prob_low, d_part, preferred_element_type=jnp.float32
        )
        return ((d_key_sum, d_value_sum), d_query_part)

    zero_grad = jnp.zeros(key_full.shape, jnp.float32)
    (d_key_sum, d_value_sum), d_query = lax.scan(
        one_block,
        (zero_grad, zero_grad),
        jnp.arange(sequence_length // block_rows, dtype=jnp.int32),
    )
    return (d_query.reshape(query_rows_all.shape), d_key_sum, d_value_sum)


def routed_body(
    tokens,
    query_key_value_weight,
    w_out_t,
    w_router,
    w_in,
    w_down,
    attn_gain,
    ffn_gain,
    q_gain,
    k_gain,
    routes,
    cotangent,
):
    sequence_count = lax.axis_size("seq")
    shard_count = lax.axis_size("fsdp")
    experts = sequence_count * shard_count
    token_row_count = tokens.shape[1]
    model_width = tokens.shape[2]
    query_group_width = QUERY_HEADS // KEY_VALUE_HEADS
    capacity = 2 * token_row_count * TOPK // experts
    slot_shape = (sequence_count, shard_count, capacity, model_width)
    positions = lax.axis_index("seq") * token_row_count + jnp.arange(
        token_row_count, dtype=jnp.int32
    )
    full_qkv, full_out, full_router = (
        lax.all_gather(query_key_value_weight, ("seq", "fsdp"), axis=0, tiled=True),
        lax.all_gather(w_out_t, ("seq", "fsdp"), axis=0, tiled=True),
        lax.all_gather(w_router, ("seq", "fsdp"), axis=0, tiled=True),
    )
    resid_in = tokens[0].astype(jnp.float32)
    normed_one = rms_scale(resid_in, attn_gain).astype(jnp.bfloat16)
    projection_output = jnp.dot(normed_one, full_qkv, preferred_element_type=jnp.float32)
    q_raw = projection_output[:, : QUERY_HEADS * HEAD_DIMENSION].reshape(
        token_row_count, QUERY_HEADS, HEAD_DIMENSION
    )
    key_unnormed = projection_output[
        :, QUERY_HEADS * HEAD_DIMENSION : (QUERY_HEADS + KEY_VALUE_HEADS) * HEAD_DIMENSION
    ].reshape(token_row_count, KEY_VALUE_HEADS, HEAD_DIMENSION)
    value_per_head = (
        projection_output[:, (QUERY_HEADS + KEY_VALUE_HEADS) * HEAD_DIMENSION :]
        .reshape(token_row_count, KEY_VALUE_HEADS, HEAD_DIMENSION)
        .astype(jnp.bfloat16)
    )
    prepare = partial(head_prepare, positions=positions)
    query_rows_all = prepare(q_raw, q_gain).astype(jnp.bfloat16)
    key_per_head = prepare(key_unnormed, k_gain).astype(jnp.bfloat16)
    send_keys = jnp.repeat(key_per_head, query_group_width, axis=1)
    send_values = jnp.repeat(value_per_head, query_group_width, axis=1)
    head_queries, head_keys, head_values = (
        lax.all_to_all(query_rows_all, "seq", split_axis=1, concat_axis=0, tiled=True),
        lax.all_to_all(send_keys, "seq", split_axis=1, concat_axis=0, tiled=True),
        lax.all_to_all(send_values, "seq", split_axis=1, concat_axis=0, tiled=True),
    )
    mixed_heads, log_total = attend_forward(head_queries, head_keys, head_values)
    mixed_tok = lax.all_to_all(mixed_heads, "seq", split_axis=0, concat_axis=1, tiled=True)
    attention_result = mixed_tok.reshape(token_row_count, QUERY_HEADS * HEAD_DIMENSION)
    attn_out = jnp.einsum(
        "tj,dj->td", attention_result, full_out, preferred_element_type=jnp.float32
    )
    hidden = resid_in + attn_out
    normed_two = rms_scale(hidden, ffn_gain).astype(jnp.bfloat16)
    logits = jnp.dot(normed_two, full_router, preferred_element_type=jnp.float32)
    route_flat = routes[0].reshape(-1)
    onehot, slot_index = route_slots(route_flat, experts)
    onehot_float = onehot.reshape(token_row_count, TOPK, experts).astype(jnp.float32)
    chosen = jnp.sum(onehot_float * logits[:, None, :], axis=-1)
    row_max = jnp.max(chosen, axis=-1, keepdims=True)
    exp_part = jnp.exp(chosen - row_max)
    gate_probs = exp_part / jnp.sum(exp_part, axis=-1, keepdims=True)
    send_rows = pack_slots(jnp.repeat(normed_two, TOPK, axis=0), route_flat, slot_index, slot_shape)
    arrived = lax.all_to_all(
        lax.all_to_all(send_rows, "seq", split_axis=0, concat_axis=0, tiled=True),
        "fsdp",
        split_axis=1,
        concat_axis=1,
        tiled=True,
    )
    rows_in = arrived.reshape(-1, model_width)
    gate_weight = w_in[0]
    down_weight = w_down[0]
    gate_up = jnp.dot(rows_in, gate_weight, preferred_element_type=jnp.float32)
    gate_half = gate_up[:, :FF]
    up_half = gate_up[:, FF:]
    gate_sig = jax.nn.sigmoid(gate_half)
    silu_gate = gate_half * gate_sig
    inner_act = (silu_gate * up_half).astype(jnp.bfloat16)
    expert_out = jnp.dot(inner_act, down_weight, preferred_element_type=jnp.float32).astype(
        jnp.bfloat16
    )
    returned = lax.all_to_all(
        lax.all_to_all(
            expert_out.reshape(slot_shape), "seq", split_axis=0, concat_axis=0, tiled=True
        ),
        "fsdp",
        split_axis=1,
        concat_axis=1,
        tiled=True,
    )
    picked = (
        unpack_slots(returned, route_flat, slot_index)
        .astype(jnp.float32)
        .reshape(token_row_count, TOPK, model_width)
    )
    mixture = jnp.sum(gate_probs[..., None] * picked, axis=1)
    output = (hidden + mixture).astype(jnp.bfloat16)
    full_qkv, full_out, full_router = (
        lax.all_gather(query_key_value_weight, ("seq", "fsdp"), axis=0, tiled=True),
        lax.all_gather(w_out_t, ("seq", "fsdp"), axis=0, tiled=True),
        lax.all_gather(w_router, ("seq", "fsdp"), axis=0, tiled=True),
    )
    out_grad = cotangent[0].astype(jnp.float32)
    d_picked = (
        (gate_probs[..., None] * out_grad[:, None, :]).astype(jnp.bfloat16).reshape(-1, model_width)
    )
    d_gates = jnp.sum(picked * out_grad[:, None, :], axis=-1)
    d_send = pack_slots(d_picked, route_flat, slot_index, slot_shape)
    d_arrived = lax.all_to_all(
        lax.all_to_all(d_send, "seq", split_axis=0, concat_axis=0, tiled=True),
        "fsdp",
        split_axis=1,
        concat_axis=1,
        tiled=True,
    ).reshape(-1, model_width)
    d_inner = jnp.einsum("rd,fd->rf", d_arrived, down_weight, preferred_element_type=jnp.float32)
    d_gate_half = d_inner * up_half * gate_sig * (1.0 + gate_half * (1.0 - gate_sig))
    d_up_half = d_inner * silu_gate
    d_gate_up = jnp.concatenate([d_gate_half, d_up_half], axis=1).astype(jnp.bfloat16)
    d_w_down = jnp.einsum("rf,rd->fd", inner_act, d_arrived, preferred_element_type=jnp.float32)[
        None
    ]
    d_w_in = jnp.einsum("rd,rf->df", rows_in, d_gate_up, preferred_element_type=jnp.float32)[None]
    d_rows = jnp.einsum(
        "rf,df->rd", d_gate_up, gate_weight, preferred_element_type=jnp.float32
    ).astype(jnp.bfloat16)
    d_back = lax.all_to_all(
        lax.all_to_all(d_rows.reshape(slot_shape), "seq", split_axis=0, concat_axis=0, tiled=True),
        "fsdp",
        split_axis=1,
        concat_axis=1,
        tiled=True,
    )
    d_routed = jnp.sum(
        unpack_slots(d_back, route_flat, slot_index)
        .astype(jnp.float32)
        .reshape(token_row_count, TOPK, model_width),
        axis=1,
    )
    d_chosen = gate_probs * (d_gates - jnp.sum(gate_probs * d_gates, axis=-1, keepdims=True))
    d_logits = jnp.einsum("tk,tke->te", d_chosen, onehot_float).astype(jnp.bfloat16)
    d_normed_two = d_routed + jnp.einsum(
        "te,de->td", d_logits, full_router, preferred_element_type=jnp.float32
    )
    unused_two, pull_two = jax.vjp(rms_scale, hidden, ffn_gain)
    d_hidden_norm, d_ffn_gain = pull_two(d_normed_two)
    d_hidden = out_grad + d_hidden_norm
    d_attn = d_hidden.astype(jnp.bfloat16)
    d_attended = jnp.einsum(
        "td,dj->tj", d_attn, full_out, preferred_element_type=jnp.float32
    ).astype(jnp.bfloat16)
    d_heads = lax.all_to_all(
        d_attended.reshape(token_row_count, QUERY_HEADS, HEAD_DIMENSION),
        "seq",
        split_axis=1,
        concat_axis=0,
        tiled=True,
    )
    d_query, d_key_sum, d_value_sum = attend_backward(
        head_queries, head_keys, head_values, log_total, d_heads
    )
    seq_rows = head_queries.shape[0]
    local_cols = head_queries.shape[1] * HEAD_DIMENSION
    normed_all, d_attn_all = (
        lax.all_gather(normed_one, "seq", axis=0, tiled=True),
        lax.all_gather(d_attn, "seq", axis=0, tiled=True),
    )
    query_cols = lax.dynamic_slice_in_dim(
        full_qkv, lax.axis_index("seq") * local_cols, local_cols, 1
    )
    q_head_raw = jnp.dot(normed_all, query_cols, preferred_element_type=jnp.float32).reshape(
        head_queries.shape
    )
    seq_positions = jnp.arange(seq_rows, dtype=jnp.int32)
    unused_head, pull_head = jax.vjp(
        partial(head_prepare, positions=seq_positions), q_head_raw, q_gain
    )
    send_d_query, d_q_gain = pull_head(d_query)
    d_query_tok, grad_key_token_rows, grad_value_token_rows = (
        lax.all_to_all(
            send_d_query.astype(jnp.bfloat16), "seq", split_axis=0, concat_axis=1, tiled=True
        ).astype(send_d_query.dtype),
        lax.all_to_all(
            d_key_sum.astype(jnp.bfloat16), "seq", split_axis=0, concat_axis=1, tiled=True
        ).astype(d_key_sum.dtype),
        lax.all_to_all(
            d_value_sum.astype(jnp.bfloat16), "seq", split_axis=0, concat_axis=1, tiled=True
        ).astype(d_value_sum.dtype),
    )
    grad_key_per_head = jnp.sum(
        grad_key_token_rows.reshape(token_row_count, KEY_VALUE_HEADS, -1, HEAD_DIMENSION), axis=2
    )
    grad_value_per_head = jnp.sum(
        grad_value_token_rows.reshape(token_row_count, KEY_VALUE_HEADS, -1, HEAD_DIMENSION), axis=2
    )
    unused_k, pull_k = jax.vjp(prepare, key_unnormed, k_gain)
    grad_key_unnormed, d_k_gain = pull_k(grad_key_per_head)
    d_projected = jnp.concatenate(
        [
            d_query_tok.reshape(token_row_count, QUERY_HEADS * HEAD_DIMENSION),
            grad_key_unnormed.reshape(token_row_count, KEY_VALUE_HEADS * HEAD_DIMENSION),
            grad_value_per_head.reshape(token_row_count, KEY_VALUE_HEADS * HEAD_DIMENSION),
        ],
        axis=1,
    ).astype(jnp.bfloat16)
    d_normed_one = jnp.einsum(
        "tj,dj->td", d_projected, full_qkv, preferred_element_type=jnp.float32
    )
    unused_one, pull_one = jax.vjp(rms_scale, resid_in, attn_gain)
    d_resid_norm, d_attn_gain = pull_one(d_normed_one)
    d_tokens = (d_hidden + d_resid_norm).astype(jnp.bfloat16)[None]
    rows_dev = model_width // experts
    kv_count = 2 * KEY_VALUE_HEADS * HEAD_DIMENSION
    kv_grads = d_projected[:, QUERY_HEADS * HEAD_DIMENSION :]
    first_rows = normed_one
    summed = lax.psum_scatter(
        jnp.concatenate(
            [
                jnp.einsum("tc,tj->cj", first_rows, kv_grads, preferred_element_type=jnp.float32),
                jnp.einsum("tc,te->ce", normed_two, d_logits, preferred_element_type=jnp.float32),
            ],
            axis=1,
        ),
        ("seq", "fsdp"),
        scatter_dimension=0,
        tiled=True,
    )
    d_query_low = send_d_query.reshape(seq_rows, local_cols).astype(jnp.bfloat16)
    attended_heads = mixed_heads.reshape(seq_rows, local_cols)
    normed_order = (
        normed_all.reshape(seq_rows, sequence_count, shard_count, rows_dev)
        .transpose(0, 2, 1, 3)
        .reshape(seq_rows, model_width)
    )
    d_attn_order = (
        d_attn_all.reshape(seq_rows, sequence_count, shard_count, rows_dev)
        .transpose(0, 2, 1, 3)
        .reshape(seq_rows, model_width)
    )
    first_rows = normed_order
    head_sums = lax.psum_scatter(
        jnp.concatenate(
            [
                jnp.einsum(
                    "tc,tj->cj", first_rows, d_query_low, preferred_element_type=jnp.float32
                ),
                jnp.einsum(
                    "tc,tj->cj", d_attn_order, attended_heads, preferred_element_type=jnp.float32
                ),
            ],
            axis=1,
        ).astype(jnp.bfloat16),
        "fsdp",
        scatter_dimension=0,
        tiled=True,
    ).astype(jnp.float32)
    row_sums = (
        lax.all_to_all(
            head_sums.astype(jnp.bfloat16), "seq", split_axis=0, concat_axis=1, tiled=True
        )
        .astype(head_sums.dtype)
        .reshape(rows_dev, sequence_count, 2, local_cols)
    )
    d_w_query = row_sums[:, :, 0].reshape(rows_dev, QUERY_HEADS * HEAD_DIMENSION)
    d_w_out_t = row_sums[:, :, 1].reshape(rows_dev, QUERY_HEADS * HEAD_DIMENSION)
    d_w_qkv = jnp.concatenate([d_w_query, summed[:, :kv_count]], axis=1)
    d_w_router = summed[:, kv_count:]
    d_attn_gain, d_ffn_gain, d_q_gain, d_k_gain = lax.psum(
        (d_attn_gain, d_ffn_gain, d_q_gain, d_k_gain), ("seq", "fsdp")
    )
    return (
        output[None],
        d_tokens,
        d_w_qkv,
        d_w_out_t,
        d_w_router,
        d_w_in,
        d_w_down,
        d_attn_gain,
        d_ffn_gain,
        d_q_gain,
        d_k_gain,
    )


MESH = pl.DeviceIdType.MESH
VMEM_LIMIT = 60 * 2**20


class Place:
    def __init__(self):
        seq, shard = lax.axis_index("seq"), lax.axis_index("fsdp")
        self.z, self.x = seq // 2, seq % 2
        self.y, self.c = shard // 2, shard % 2
        self.z0, self.z1 = self.z % 2, self.z // 2
        self.low, self.high = self.z == 0, self.z == 3
        self.inner = (self.z0 + self.z1) == 1
        self.me = self.block(self.z, self.x, self.y, self.c)

    def device(self, z, x, y, c):
        return (z * 2 + x, y * 2 + c)

    def block(self, z, x, y, c):
        return (z * 2 + x) * 4 + y * 2 + c

    @property
    def by_x(self):
        return self.device(self.z, 1 - self.x, self.y, self.c)

    @property
    def by_y(self):
        return self.device(self.z, self.x, 1 - self.y, self.c)

    @property
    def by_core(self):
        return self.device(self.z, self.x, self.y, 1 - self.c)

    def by_z(self, step):
        return self.device(self.z + step, self.x, self.y, self.c)

    def near(self, k):
        return [self.z, 1 + self.z0, 2 - 2 * self.z0 + self.z1, 3 - 3 * self.z1][k]

    def onward(self, k):
        return [None, 2 * self.z1 - 1, 1 - 2 * self.z1, 2 * self.z1 - 1][k]

    def far(self, k):
        return self.near(3 - k)

    def toward(self, k):
        return [1 - 2 * self.z1, 1 - 2 * self.z0, 1 - 2 * self.z1][k]

    def greet(self, sides):
        barrier = pltpu.get_barrier_semaphore()
        for side in sides:
            if side != "z":
                target = {"x": self.by_x, "y": self.by_y, "core": self.by_core}[side]
                pl.semaphore_signal(barrier, inc=1, device_id=target, device_id_type=MESH)
        count = len([side for side in sides if side != "z"])
        if "z" in sides:

            @pl.when(jnp.logical_not(self.low))
            def _():
                pl.semaphore_signal(barrier, inc=1, device_id=self.by_z(-1), device_id_type=MESH)

            @pl.when(jnp.logical_not(self.high))
            def _():
                pl.semaphore_signal(barrier, inc=1, device_id=self.by_z(1), device_id_type=MESH)

            count = count + 1 + (self.z0 + self.z1) % 2
        pl.semaphore_wait(barrier, count)


def send(source, target, send_sem, recv_sem, device):
    pltpu.make_async_remote_copy(
        src_ref=source,
        dst_ref=target,
        send_sem=send_sem,
        recv_sem=recv_sem,
        device_id=device,
        device_id_type=MESH,
    ).start()


def await_bytes(ref, sem):
    pltpu.make_async_copy(ref, ref, sem).wait()


G_Z, G_X, G_Y, G_DX, G_DY, G_C0 = 0, 1, 2, 3, 4, 5
G_KINDS = 9


def gather_steps(place, own, out, ss, rs, zs, local_sem):
    p = place
    rows = out.shape[1]
    half = rows // 2
    x, y, c = p.x, p.y, p.c

    def cols(q):
        return [
            p.block(q, x, y, c),
            p.block(q, 1 - x, y, c),
            p.block(q, x, 1 - y, c),
            p.block(q, 1 - x, 1 - y, c),
        ]

    def to_core(q, j, src=None):
        b = cols(q)[j]
        send(out.at[b] if src is None else src, out.at[b], ss.at[q, G_C0 + j], rs.at[q, G_C0 + j], p.by_core)

    def plane_out(k):
        q = p.near(k)
        b = cols(q)[0]
        if k == 0:
            src = own
            for step, there in ((1, p.high), (-1, p.low)):

                @pl.when(jnp.logical_not(there))
                def _():
                    send(src, out.at[b], zs.at[q, 0 if step > 0 else 1], rs.at[q, G_Z], p.by_z(step))

            pltpu.make_async_copy(own, out.at[b], local_sem).start()
        else:
            src = out.at[b]
            await_bytes(src, rs.at[q, G_Z])

            @pl.when(p.inner)
            def _():
                send(src, src, zs.at[q, 0], rs.at[q, G_Z], p.by_z(p.onward(k)))

        send(src, out.at[b], ss.at[q, G_X], rs.at[q, G_X], p.by_x)
        send(src, out.at[b], ss.at[q, G_Y], rs.at[q, G_Y], p.by_y)
        to_core(q, 0, src)

    def plane_turn(k):
        q = p.near(k)
        bx, by = out.at[cols(q)[1]], out.at[cols(q)[2]]
        await_bytes(bx, rs.at[q, G_X])
        first = bx.at[pl.ds(0, half)]
        send(first, first, ss.at[q, G_DY], rs.at[q, G_DY], p.by_y)
        to_core(q, 1)
        await_bytes(by, rs.at[q, G_Y])
        second = by.at[pl.ds(half, half)]
        send(second, second, ss.at[q, G_DX], rs.at[q, G_DX], p.by_x)
        to_core(q, 2)

    def plane_end(k):
        q = p.near(k)
        bd = out.at[cols(q)[3]]
        await_bytes(bd.at[pl.ds(0, half)], rs.at[q, G_DY])
        await_bytes(bd.at[pl.ds(half, half)], rs.at[q, G_DX])
        to_core(q, 3)

    def plane_core(k):
        q = p.near(k)
        for j in range(4):
            await_bytes(own, rs.at[q, G_C0 + j])

    def finish():
        piece = own.at[pl.ds(0, half)]
        for q in range(4):
            for kind in (G_X, G_Y, G_C0, G_C0 + 1, G_C0 + 2, G_C0 + 3):
                await_bytes(own, ss.at[q, kind])
            for kind in (G_DX, G_DY):
                await_bytes(piece, ss.at[q, kind])
        for there, slot in ((p.high, 0), (p.low, 1)):

            @pl.when(jnp.logical_not(there))
            def _():
                await_bytes(own, zs.at[p.z, slot])

        for k in range(1, 4):

            @pl.when(p.inner)
            def _():
                await_bytes(own, zs.at[p.near(k), 0])

    return plane_out, plane_turn, plane_end, plane_core, finish


def sum_all_parts(p, part, held, core_in, x_half, y_half, x_in, y_in, z_in, out, ls, cs, cr, ss, rs, zs, zr):
    rows, width = part.shape[1], part.shape[2]
    half = rows // 2
    x, y, c = p.x, p.y, p.c

    def columns(q):
        return [(q, x, y), (q, 1 - x, y), (q, x, 1 - y), (q, 1 - x, 1 - y)]

    def start():
        for k in range(4):
            q = p.far(k)
            for j, (zz, xx, yy) in reversed(list(enumerate(columns(q)))):
                send(
                    part.at[p.block(zz, xx, yy, 1 - c)],
                    core_in.at[q * 4 + j],
                    cs.at[q, j],
                    cr.at[q, j],
                    p.by_core,
                )
                pltpu.make_async_copy(
                    part.at[p.block(zz, xx, yy, c)], held.at[q * 4 + j], ls.at[q, j]
                ).start()

    chunk = 16

    def add(target, source, count):
        @pl.loop(0, count // chunk)
        def _(i):
            at = pl.ds(pl.multiple_of(i * chunk, chunk), chunk)
            target[at, :] = (
                target[at, :].astype(jnp.float32) + source[at, :].astype(jnp.float32)
            ).astype(target.dtype)

    def plane_core(k, js=(3, 1, 2, 0)):
        q = p.far(k)
        for j in js:
            slot = q * 4 + j
            await_bytes(held.at[slot], ls.at[q, j])
            await_bytes(core_in.at[slot], cr.at[q, j])
            add(held.at[slot], core_in.at[slot], rows)
            if j == 3:
                send(held.at[slot, pl.ds(0, half)], y_half.at[q], ss.at[q, 0], rs.at[q, 0], p.by_y)
                send(held.at[slot, pl.ds(half, half)], x_half.at[q], ss.at[q, 1], rs.at[q, 1], p.by_x)

    def plane_turn(k):
        q = p.far(k)
        await_bytes(y_half.at[q], rs.at[q, 0])
        add(held.at[q * 4 + 1, pl.ds(0, half)], y_half.at[q], half)
        send(held.at[q * 4 + 1], x_in.at[q], ss.at[q, 2], rs.at[q, 2], p.by_x)
        await_bytes(x_half.at[q], rs.at[q, 1])
        add(held.at[q * 4 + 2, pl.ds(half, half)], x_half.at[q], half)
        send(held.at[q * 4 + 2], y_in.at[q], ss.at[q, 3], rs.at[q, 3], p.by_y)

    def plane_end(k):
        q = p.far(k)
        mine = held.at[q * 4]
        await_bytes(x_in.at[q], rs.at[q, 2])
        add(mine, x_in.at[q], rows)
        await_bytes(y_in.at[q], rs.at[q, 3])
        add(mine, y_in.at[q], rows)
        if k < 3:
            step = p.toward(k)
            slot = (1 - step) // 2

            @pl.when(p.inner)
            def _():
                await_bytes(z_in.at[slot, q], zr.at[slot, q])
                add(mine, z_in.at[slot, q], rows)

            send(mine, z_in.at[slot, q], zs.at[k], zr.at[slot, q], p.by_z(step))
        else:
            for slot, there in ((0, p.low), (1, p.high)):

                @pl.when(jnp.logical_not(there))
                def _():
                    await_bytes(z_in.at[slot, q], zr.at[slot, q])
                    add(mine, z_in.at[slot, q], rows)

            out[...] = mine[...]

    def finish():
        whole, piece = x_in.at[0], x_half.at[0]
        for q in range(4):
            for j in range(4):
                await_bytes(whole, cs.at[q, j])
            for kind in (0, 1):
                await_bytes(piece, ss.at[q, kind])
            for kind in (2, 3):
                await_bytes(whole, ss.at[q, kind])
        for k in range(3):
            await_bytes(whole, zs.at[k])

    return start, plane_core, plane_turn, plane_end, finish


def sum_all_kernel(part, both, out, pair, both_held, both_in, pair_sems, *scratch):
    p = Place()
    p.greet(("x", "y", "core", "z"))
    start, plane_core, plane_turn, plane_end, finish = sum_all_parts(p, part, *scratch[:7], out, *scratch[7:])
    rows = both.shape[3]

    def pair_sum(first):
        for s in (first, first + 1):
            for y in range(2):
                add_rows(both_held.at[s, y], both_in.at[s, y], rows)

    start()
    send(both.at[:, :, 1 - p.c], both_in, pair_sems.at[0], pair_sems.at[1], p.by_core)
    pltpu.make_async_copy(both.at[:, :, p.c], both_held, pair_sems.at[2]).start()
    plane_core(0)
    plane_core(1)
    plane_turn(0)
    await_bytes(both_held, pair_sems.at[2])
    await_bytes(both_in, pair_sems.at[1])
    pair_sum(0)
    plane_core(2)
    plane_turn(1)
    plane_end(0)
    pair_sum(2)
    plane_core(3)
    plane_turn(2)
    plane_end(1)
    pair_sum(4)
    pair_sum(6)
    pltpu.make_async_copy(both_held, pair, pair_sems.at[2]).start()
    plane_turn(3)
    plane_end(2)
    plane_end(3)
    finish()
    await_bytes(both_in, pair_sems.at[0])
    pltpu.make_async_copy(both_held, pair, pair_sems.at[2]).wait()


def sum_all_scratch(rows, width):
    dma = pltpu.SemaphoreType.DMA
    bf16 = jnp.bfloat16
    return [
        pltpu.VMEM((16, rows, width), bf16),
        pltpu.VMEM((16, rows, width), bf16),
        pltpu.VMEM((4, rows // 2, width), bf16),
        pltpu.VMEM((4, rows // 2, width), bf16),
        pltpu.VMEM((4, rows, width), bf16),
        pltpu.VMEM((4, rows, width), bf16),
        pltpu.VMEM((2, 4, rows, width), bf16),
        dma((4, 4)),
        dma((4, 4)),
        dma((4, 4)),
        dma((4, 4)),
        dma((4, 4)),
        dma((3,)),
        dma((2, 4)),
    ]


def sum_all(part, both, collective_id):
    blocks, rows, width = part.shape
    both = both.reshape(blocks // 4, 2, 2, rows, -1)
    pair = (blocks // 4, 2, rows, both.shape[4])
    anywhere = pl.BlockSpec(memory_space=pl.ANY)
    return pl.pallas_call(
        sum_all_kernel,
        out_shape=[
            jax.ShapeDtypeStruct((rows, width), part.dtype),
            jax.ShapeDtypeStruct(pair, both.dtype),
        ],
        in_specs=[anywhere] * 2,
        out_specs=[pl.BlockSpec(memory_space=pltpu.VMEM), anywhere],
        scratch_shapes=[
            pltpu.VMEM(pair, both.dtype),
            pltpu.VMEM(pair, both.dtype),
            pltpu.SemaphoreType.DMA((3,)),
            *sum_all_scratch(rows, width),
        ],
        compiler_params=pltpu.CompilerParams(
            collective_id=collective_id, has_side_effects=True, vmem_limit_bytes=VMEM_LIMIT
        ),
        name="sum_all",
    )(part, both)


def add_rows(target, source, count, chunk=16):
    @pl.loop(0, count // chunk)
    def _(i):
        at = pl.ds(pl.multiple_of(i * chunk, chunk), chunk)
        target[at, :] = (
            target[at, :].astype(jnp.float32) + source[at, :].astype(jnp.float32)
        ).astype(target.dtype)


def seq_peer(p, d):
    return ((p.z * 2 + p.x + d) % 8, p.y * 2 + p.c)


def greet_seq(p, sides=("y", "core")):
    barrier = pltpu.get_barrier_semaphore()
    for d in range(1, 8):
        pl.semaphore_signal(barrier, inc=1, device_id=seq_peer(p, d), device_id_type=MESH)
    for side in sides:
        target = {"y": p.by_y, "core": p.by_core}[side]
        pl.semaphore_signal(barrier, inc=1, device_id=target, device_id_type=MESH)
    pl.semaphore_wait(barrier, 7 + len(sides))


def leave_kernel(
    part, cols, rows_in, d_gate_up_hbm, inner, d_expert_hbm, tokens, d_hidden, gain,
    d_tokens, cols_out, d_w_in, d_w_down,
    held, x_in, z_in, c_held, c_core, c_y, d_gate_up, d_expert, left, product,
    ls, ss, rs, zs, zr, cl, cs, cr, ys, yr, ts, tr, load_sems, left_sems, product_sems,
):
    p = Place()
    greet_seq(p)
    wide_loads = [
        pltpu.make_async_copy(d_gate_up_hbm, d_gate_up, load_sems.at[0]),
        pltpu.make_async_copy(d_expert_hbm, d_expert, load_sems.at[1]),
    ]

    def left_load(source, i, slot):
        cols = pl.ds(pl.multiple_of(i * TILE, TILE), TILE)
        return pltpu.make_async_copy(source.at[:, cols], left.at[slot], left_sems.at[slot])

    def product_store(target, i, slot):
        at = pl.ds(pl.multiple_of(i * TILE, TILE), TILE)
        piece = product.at[slot, :, pl.ds(0, target.shape[1])]
        return pltpu.make_async_copy(piece, target.at[at], product_sems.at[slot])

    def tiles(source, right, target, first, last):
        count = source.shape[1] // TILE

        @pl.loop(first, last)
        def _(i):
            slot = i % 2
            left_load(source, i, slot).wait()

            @pl.when(i + 1 < count)
            def _():
                left_load(source, i + 1, 1 - slot).start()

            @pl.when(i >= 2)
            def _():
                product_store(target, i - 2, slot).wait()

            result = mxu(left[slot], right[...], TN)
            product[slot, :, : target.shape[1]] = result.astype(product.dtype)
            product_store(target, i, slot).start()

    def tiles_end(source, target):
        count = source.shape[1] // TILE
        for i in (count - 2, count - 1):
            product_store(target, i, i % 2).wait()

    rows, width = part.shape[1:]
    place = p.z * 2 + p.x
    for turn, side in ((0, 1 - p.y), (1, p.y)):
        send(cols.at[:, side, 1 - p.c], c_core.at[turn], cs.at[turn], cr.at[turn], p.by_core)
        pltpu.make_async_copy(cols.at[:, side, p.c], c_held.at[turn], cl.at[turn]).start()
    for k in range(4):
        q = p.far(k)
        send(part.at[q * 2 + 1 - p.x], x_in.at[q], ss.at[q], rs.at[q], p.by_x)
        pltpu.make_async_copy(part.at[q * 2 + p.x], held.at[q], ls.at[q]).start()
    piece_rows = c_held.shape[2]
    for load in wide_loads:
        load.start()
    left_load(rows_in, 0, 0).start()
    order = [(place + d) % 8 for d in range(1, 9)]
    for turn in range(2):
        await_bytes(c_held.at[turn], cl.at[turn])
        await_bytes(c_core.at[turn], cr.at[turn])
        for i, s in enumerate(order):
            add_rows(c_held.at[turn, s], c_core.at[turn, s], piece_rows)
            if turn == 0:
                send(c_held.at[0, s], c_y.at[s], ys.at[s], yr.at[s], p.by_y)

    def turn_in(i):
        s = order[i]
        await_bytes(c_y.at[s], yr.at[s])
        add_rows(c_held.at[1, s], c_y.at[s], piece_rows)
        if i < 7:
            send(c_held.at[1, s], cols_out.at[place], ts.at[i], tr.at[i], seq_peer(p, i + 1))
        else:
            pltpu.make_async_copy(c_held.at[1, s], cols_out.at[place], ts.at[7]).start()

    wide_loads[0].wait()
    per_plane = width // TILE // 4
    for k in range(4):
        q = p.far(k)
        mine = held.at[q]
        tiles(rows_in, d_gate_up, d_w_in, k * per_plane, (k + 1) * per_plane)
        await_bytes(mine, ls.at[q])
        await_bytes(x_in.at[q], rs.at[q])
        add_rows(mine, x_in.at[q], rows)
        if k < 3:
            step = p.toward(k)
            slot = (1 - step) // 2

            @pl.when(p.inner)
            def _():
                await_bytes(z_in.at[slot, q], zr.at[slot, q])
                add_rows(mine, z_in.at[slot, q], rows)

            send(mine, z_in.at[slot, q], zs.at[k], zr.at[slot, q], p.by_z(step))
            for i in ((0, 1), (2, 3), (4, 5, 6, 7))[k]:
                turn_in(i)
        else:
            for slot, there in ((0, p.low), (1, p.high)):

                @pl.when(jnp.logical_not(there))
                def _():
                    await_bytes(z_in.at[slot, q], zr.at[slot, q])
                    add_rows(mine, z_in.at[slot, q], rows)

    mine = held.at[p.z]
    chunk = 16

    @pl.loop(0, rows // chunk)
    def _(i):
        at = pl.ds(pl.multiple_of(i * chunk, chunk), chunk)
        d_out = mine[at, :].astype(jnp.float32)
        x = tokens[at, :].astype(jnp.float32)
        scale = lax.rsqrt(jnp.mean(x * x, axis=-1, keepdims=True) + EPS)
        u = d_out * gain[...]
        dot = jnp.mean(u * x, axis=-1, keepdims=True)
        d_x = scale * u - x * (scale * scale * scale * dot)
        d_tokens[at, :] = (d_hidden[at, :] + d_x).astype(d_tokens.dtype)

    tiles_end(rows_in, d_w_in)
    left_load(inner, 0, 0).start()
    wide_loads[1].wait()
    tiles(inner, d_expert, d_w_down, 0, inner.shape[1] // TILE)
    tiles_end(inner, d_w_down)
    piece = c_y.at[0]
    for i in range(8):
        if i < 7:
            await_bytes(piece, tr.at[i])
        await_bytes(piece, ts.at[i])
        await_bytes(piece, ys.at[i])
    for turn in range(2):
        await_bytes(c_core.at[turn], cs.at[turn])
    for q in range(4):
        await_bytes(x_in.at[0], ss.at[q])
    for k in range(3):
        await_bytes(x_in.at[0], zs.at[k])


def leave(part, cols, rows_in, d_gate_up, inner, d_expert, tokens, d_hidden, gain, collective_id):
    _, rows, width = part.shape
    piece_rows, piece_width = cols.shape[3:]
    dma = pltpu.SemaphoreType.DMA
    bf16 = jnp.bfloat16
    anywhere, vmem = pl.BlockSpec(memory_space=pl.ANY), pl.BlockSpec(memory_space=pltpu.VMEM)
    return pl.pallas_call(
        leave_kernel,
        out_shape=[
            jax.ShapeDtypeStruct((rows, width), bf16),
            jax.ShapeDtypeStruct((8, piece_rows, piece_width), bf16),
            jax.ShapeDtypeStruct((rows_in.shape[1], d_gate_up.shape[1]), bf16),
            jax.ShapeDtypeStruct((inner.shape[1], d_expert.shape[1]), bf16),
        ],
        in_specs=[anywhere] * 6 + [vmem] * 3,
        out_specs=[vmem] + [anywhere] * 3,
        scratch_shapes=[
            pltpu.VMEM((4, rows, width), bf16),
            pltpu.VMEM((4, rows, width), bf16),
            pltpu.VMEM((2, 4, rows, width), bf16),
            pltpu.VMEM((2, 8, piece_rows, piece_width), bf16),
            pltpu.VMEM((2, 8, piece_rows, piece_width), bf16),
            pltpu.VMEM((8, piece_rows, piece_width), bf16),
            pltpu.VMEM(d_gate_up.shape, bf16),
            pltpu.VMEM(d_expert.shape, bf16),
            pltpu.VMEM((2, rows_in.shape[0], TILE), bf16),
            pltpu.VMEM((2, TILE, d_expert.shape[1]), bf16),
            dma((4,)),
            dma((4,)),
            dma((4,)),
            dma((3,)),
            dma((2, 4)),
            dma((2,)),
            dma((2,)),
            dma((2,)),
            dma((8,)),
            dma((8,)),
            dma((8,)),
            dma((7,)),
            dma((2,)),
            dma((2,)),
            dma((2,)),
        ],
        compiler_params=pltpu.CompilerParams(
            collective_id=collective_id, has_side_effects=True, vmem_limit_bytes=VMEM_LIMIT
        ),
        name="leave",
    )(part, cols, rows_in, d_gate_up, inner, d_expert, tokens, d_hidden, gain)


NT = (((1,), (1,)), ((), ()))
TILE = 256
WIDE = 512


def mxu(a, b, dims=(((1,), (0,)), ((), ()))):
    return lax.dot_general(a, b, dims, preferred_element_type=jnp.float32)


def experts_kernel(
    own, cot_all, w_in_hbm, w_down_hbm,
    rows_all, out_part, d_part, x_all, d_expert_all, inner_all, d_gate_up_all,
    w_in, w_down, row_buf, cot_buf, pick, pick_t, gates, d_gates, x, cot, d_expert,
    by_d_gate, by_d_up, inner, d_gate_up, held, out_stage, d_stage,
    ss, rs, zs, local_sem, load_sems, store_sems,
):
    p = Place()
    bf16, f32 = jnp.bfloat16, jnp.float32
    width = cot_all.shape[2]
    blocks = 8
    slots = gates.shape[0]
    capacity = slots // blocks
    tokens = row_buf.shape[2]
    group = 4
    experts = rows_all.shape[0]
    p.greet(("x", "y", "core", "z"))
    plane_out, plane_turn, plane_end, plane_core, finish = gather_steps(
        p, own, rows_all, ss, rs, zs, local_sem
    )

    def weights(start):
        for i, (src, dst) in enumerate(((w_in_hbm, w_in), (w_down_hbm, w_down))):
            copy = pltpu.make_async_copy(src, dst, load_sems.at[i])
            copy.start() if start else copy.wait()

    def cot_load(k):
        return pltpu.make_async_copy(
            cot_all.at[pl.ds(p.near(k) * blocks, blocks)], cot_buf.at[k % 2], load_sems.at[2 + k]
        )

    def row_load(k):
        return pltpu.make_async_copy(
            rows_all.at[pl.ds(p.near(k) * blocks, blocks)], row_buf.at[k % 2], load_sems.at[6 + k]
        )

    def arrived(k):
        plane_core(k)
        if k == 0:
            pltpu.make_async_copy(own, rows_all.at[p.me], local_sem).wait()
        row_load(k).start()

    at_slot = {}

    def store(k, i, src, dst):
        if (k, i) not in at_slot:
            at_slot[k, i] = pltpu.make_async_copy(src, dst, store_sems.at[i, k % 2])
        return at_slot[k, i]

    def stores(k):
        q = p.near(k)
        at = pl.ds(q * slots, slots)
        plane = pl.ds(q * blocks, blocks)
        return [
            (x, x_all.at[at]),
            (d_expert, d_expert_all.at[at]),
            (inner, inner_all.at[at]),
            (d_gate_up, d_gate_up_all.at[at]),
            (out_stage, out_part.at[plane]),
            (d_stage, d_part.at[plane]),
        ]

    def put(k, i):
        store(k, i, *stores(k)[i]).start()

    def free(k, i):
        if k > 0:
            store(k - 1, i, *stores(k - 1)[i]).wait()

    def pick_rows(k):
        lane = lax.broadcasted_iota(jnp.int32, (8, 128), 1)
        line = lax.broadcasted_iota(jnp.int32, (8, 128), 0)
        select = jnp.where((lane == line * experts + p.me) & (line < 3), 1.0, 0.0).astype(bf16)
        slot_id = lax.broadcasted_iota(jnp.int32, (capacity, tokens), 0).astype(f32) + 1.0
        rows, cots = row_buf.at[k % 2], cot_buf.at[k % 2]
        lines = mxu(select, rows[:, :, width:].reshape(blocks * tokens, 128), NT)
        for j in range(blocks):
            g, i = j // group, j % group
            mine = lines[:, j * tokens : (j + 1) * tokens]
            chosen = jnp.where(mine[2:3] == slot_id, 1.0, 0.0)
            gate = jnp.sum(chosen * (mine[0:1] + mine[1:2]), axis=1, keepdims=True)
            gates[j * capacity : (j + 1) * capacity, :] = jnp.broadcast_to(gate, (capacity, 128))
            lead = [jnp.zeros((capacity, tokens), bf16)] * i
            tail = [jnp.zeros((capacity, tokens), bf16)] * (group - 1 - i)
            pick[g, i * capacity : (i + 1) * capacity, :] = jnp.concatenate(
                lead + [chosen.astype(bf16)] + tail, axis=1
            )
            lead = [jnp.zeros((tokens, capacity), f32)] * i
            tail = [jnp.zeros((tokens, capacity), f32)] * (group - 1 - i)
            pick_t[g, i * tokens : (i + 1) * tokens, :] = jnp.concatenate(
                lead + [chosen.T] + tail, axis=1
            ).astype(bf16)
        for g in range(blocks // group):
            at = pl.ds(g * group * capacity, group * capacity)
            which = pl.ds(g * group, group)

            @pl.loop(0, width // WIDE)
            def _(n):
                cols = pl.ds(pl.multiple_of(n * WIDE, WIDE), WIDE)
                row_tile = rows[which, :, cols].reshape(group * tokens, WIDE)
                x[at, cols] = mxu(pick[g], row_tile).astype(bf16)
                cot_tile = cots[which, :, cols].reshape(group * tokens, WIDE)
                picked = mxu(pick[g], cot_tile)
                cot[at, cols] = picked.astype(bf16)
                scale = jnp.concatenate([gates[at, :]] * (WIDE // 128), axis=1)
                d_expert[at, cols] = (scale * picked).astype(bf16)

    def up(k):
        ff = inner.shape[1]

        @pl.loop(0, ff // TILE)
        def _(n):
            cols = pl.ds(pl.multiple_of(n * TILE, TILE), TILE)
            gate = mxu(x[...], w_in[:, cols])
            raised = mxu(x[...], w_in[:, pl.ds(pl.multiple_of(ff + n * TILE, TILE), TILE)])
            sig = jax.nn.sigmoid(gate)
            silu = gate * sig
            inner[:, cols] = (silu * raised).astype(bf16)
            by_d_up[:, cols] = silu
            by_d_gate[:, cols] = raised * sig * (1.0 + gate * (1.0 - sig))

    def d_up(k):
        ff = inner.shape[1]

        @pl.loop(0, ff // TILE)
        def _(n):
            cols = pl.ds(pl.multiple_of(n * TILE, TILE), TILE)
            d_inner = mxu(d_expert[...], w_down[cols, :], NT)
            d_gate_up[:, cols] = (d_inner * by_d_gate[:, cols]).astype(bf16)
            d_gate_up[:, pl.ds(pl.multiple_of(ff + n * TILE, TILE), TILE)] = (
                d_inner * by_d_up[:, cols]
            ).astype(bf16)

    def spread(stage):
        @pl.loop(0, width // WIDE)
        def _(n):
            cols = pl.ds(pl.multiple_of(n * WIDE, WIDE), WIDE)
            for g in range(blocks // group):
                part = held[g * group * capacity : (g + 1) * group * capacity, cols]
                result = mxu(pick_t[g], part).astype(bf16)
                stage[g * group : (g + 1) * group, :, cols] = result.reshape(group, tokens, WIDE)

    def down(k):
        d_gates[...] = jnp.zeros_like(d_gates)

        @pl.loop(0, width // TILE)
        def _(n):
            cols = pl.ds(pl.multiple_of(n * TILE, TILE), TILE)
            result = mxu(inner[...], w_down[:, cols]).astype(bf16).astype(f32)
            product = result * cot[:, cols].astype(f32)
            total = product[:, :128]
            for j in range(1, TILE // 128):
                total = total + product[:, j * 128 : (j + 1) * 128]
            d_gates[...] += total
            scale = jnp.concatenate([gates[...]] * (TILE // 128), axis=1)
            held[:, cols] = (scale * result).astype(bf16)

    def d_down(k):
        total = jnp.sum(d_gates[...], axis=1, keepdims=True)
        high = total.astype(bf16).astype(f32)
        lane = lax.broadcasted_iota(jnp.int32, (slots, 128), 1)
        info = jnp.where(lane == p.me, high, jnp.where(lane == experts + p.me, total - high, 0.0))
        info = info.astype(bf16)
        for g in range(blocks // group):
            result = mxu(pick_t[g], info[g * group * capacity : (g + 1) * group * capacity])
            d_stage[g * group : (g + 1) * group, :, width:] = result.astype(bf16).reshape(
                group, tokens, 128
            )

        @pl.loop(0, width // TILE)
        def _(n):
            cols = pl.ds(pl.multiple_of(n * TILE, TILE), TILE)
            held[:, cols] = mxu(d_gate_up[...], w_in[cols, :], NT).astype(bf16)

    plane_out(0)
    weights(True)
    cot_load(0).start()
    plane_turn(0)
    plane_out(1)
    plane_end(0)
    arrived(0)
    weights(False)
    after = {
        (0, 1): ((plane_turn, 1), (plane_out, 2)),
        (0, 3): ((plane_end, 1),),
        (0, 5): ((arrived, 1),),
        (1, 0): ((plane_turn, 2), (plane_out, 3)),
        (1, 3): ((plane_end, 2),),
        (1, 5): ((arrived, 2),),
        (2, 0): ((plane_turn, 3),),
        (2, 3): ((plane_end, 3),),
        (2, 5): ((arrived, 3),),
    }
    for k in range(4):

        def service(i):
            for step, plane in after.get((k, i), ()):
                step(plane)

        row_load(k).wait()
        cot_load(k).wait()
        if k < 3:
            cot_load(k + 1).start()
        free(k, 0)
        free(k, 1)
        pick_rows(k)
        put(k, 0)
        put(k, 1)
        service(0)
        free(k, 2)
        up(k)
        put(k, 2)
        service(1)
        free(k, 3)
        d_up(k)
        put(k, 3)
        service(2)
        free(k, 4)
        down(k)
        service(3)
        spread(out_stage)
        put(k, 4)
        service(4)
        free(k, 5)
        d_down(k)
        service(5)
        spread(d_stage)
        put(k, 5)
    for i in range(6):
        free(4, i)
    finish()


def experts_gathered(own, cot_all, w_in, w_down, capacity, collective_id):
    tokens, wide = own.shape
    experts, _, width = cot_all.shape
    ff = w_down.shape[0]
    slots = 8 * capacity
    dma = pltpu.SemaphoreType.DMA
    bf16, f32 = jnp.bfloat16, jnp.float32
    anywhere = pl.BlockSpec(memory_space=pl.ANY)

    def array(*shape):
        return jax.ShapeDtypeStruct(shape, bf16)

    return pl.pallas_call(
        experts_kernel,
        out_shape=[
            array(experts, tokens, wide),
            array(experts, tokens, width),
            array(experts, tokens, wide),
            array(experts * capacity, width),
            array(experts * capacity, width),
            array(experts * capacity, ff),
            array(experts * capacity, 2 * ff),
        ],
        in_specs=[anywhere] * 4,
        out_specs=[anywhere] * 7,
        scratch_shapes=[
            pltpu.VMEM(w_in.shape, bf16),
            pltpu.VMEM(w_down.shape, bf16),
            pltpu.VMEM((2, 8, tokens, wide), bf16),
            pltpu.VMEM((2, 8, tokens, width), bf16),
            pltpu.VMEM((2, 4 * capacity, 4 * tokens), bf16),
            pltpu.VMEM((2, 4 * tokens, 4 * capacity), bf16),
            pltpu.VMEM((slots, 128), f32),
            pltpu.VMEM((slots, 128), f32),
            pltpu.VMEM((slots, width), bf16),
            pltpu.VMEM((slots, width), bf16),
            pltpu.VMEM((slots, width), bf16),
            pltpu.VMEM((slots, ff), f32),
            pltpu.VMEM((slots, ff), f32),
            pltpu.VMEM((slots, ff), bf16),
            pltpu.VMEM((slots, 2 * ff), bf16),
            pltpu.VMEM((slots, width), bf16),
            pltpu.VMEM((8, tokens, width), bf16),
            pltpu.VMEM((8, tokens, wide), bf16),
            dma((4, G_KINDS)),
            dma((4, G_KINDS)),
            dma((4, 2)),
            dma,
            dma((10,)),
            dma((6, 2)),
        ],
        compiler_params=pltpu.CompilerParams(
            collective_id=collective_id, has_side_effects=True, vmem_limit_bytes=VMEM_LIMIT
        ),
        name="experts",
    )(own, cot_all, w_in, w_down)


TN = (((0,), (0,)), ((), ()))


def back_kernel(
    own, pair, rows_all, columns_hbm, normed_hbm, queries, keys, values, attended,
    q_raw, k_raw, cosine, sine, q_gain, k_gain, attn_gain, gains,
    d_normed, d_columns, gains_out, mixture,
    d_attn, columns, normed, d_heads, d_query, d_key, d_value, d_proj, logits, q_sum, k_sum,
    held, x_in, y_in, z_in, g_send, g_in,
    gs, gr, gz, load_sems, local_sem, hs, ys, yr, xs, xr, zs, zr, ts, tr,
):
    p = Place()
    bf16, f32 = jnp.bfloat16, jnp.float32
    columns_z = [p.device((p.z + d) % 4, p.x, p.y, p.c) for d in (1, 2, 3)]
    barrier = pltpu.get_barrier_semaphore()
    for target in (p.by_core, p.by_x, p.by_y, *columns_z):
        pl.semaphore_signal(barrier, inc=1, device_id=target, device_id_type=MESH)
    pl.semaphore_wait(barrier, 6)
    rows, wide = own.shape
    length, head_cols = queries.shape
    heads = head_cols // HEAD_DIMENSION
    width = normed.shape[1]
    proj_cols = d_proj.shape[1]
    plane_rows = 2 * rows
    score_scale = 1.0 / math.sqrt(HEAD_DIMENSION)
    place, shard = p.z * 2 + p.x, p.y * 2 + p.c

    def rows_at(q, x):
        return d_attn.at[q * 2 + x]

    def gather_out(k):
        q = p.near(k)
        there = rows_at(q, p.x)
        if k == 0:
            src = own
            for step, end in ((1, p.high), (-1, p.low)):

                @pl.when(jnp.logical_not(end))
                def _():
                    send(src, there, gz.at[q, 0 if step > 0 else 1], gr.at[q, 0], p.by_z(step))

            pltpu.make_async_copy(own, there, local_sem).start()
        else:
            src = there
            await_bytes(src, gr.at[q, 0])

            @pl.when(p.inner)
            def _():
                send(src, src, gz.at[q, 0], gr.at[q, 0], p.by_z(p.onward(k)))

        send(src, there, gs.at[q], gr.at[q, 1], p.by_x)

    def gather_in(k):
        if k == 0:
            pltpu.make_async_copy(own, rows_at(p.z, p.x), local_sem).wait()
        await_bytes(own, gr.at[p.near(k), 1])

    def at_pair(q, x, y):
        return pair.at[q * 4 + x * 2 + y]

    def sum_start():
        for k in range(4):
            q = p.far(k)
            for j, x in ((1, 1 - p.x), (0, p.x)):
                send(at_pair(q, x, 1 - p.y), y_in.at[q * 2 + j], ys.at[q * 2 + j], yr.at[q * 2 + j], p.by_y)
                pltpu.make_async_copy(at_pair(q, x, p.y), held.at[q * 2 + j], hs.at[q * 2 + j]).start()

    def sum_turn(k):
        q = p.far(k)
        for j in (1, 0):
            slot = q * 2 + j
            await_bytes(held.at[slot], hs.at[slot])
            await_bytes(y_in.at[slot], yr.at[slot])
            add_rows(held.at[slot], y_in.at[slot], rows)
            if j == 1:
                send(held.at[slot], x_in.at[q], xs.at[q], xr.at[q], p.by_x)

    def sum_end(k):
        q = p.far(k)
        mine = held.at[q * 2]
        await_bytes(x_in.at[q], xr.at[q])
        add_rows(mine, x_in.at[q], rows)
        if k < 3:
            step = p.toward(k)
            slot = (1 - step) // 2

            @pl.when(p.inner)
            def _():
                await_bytes(z_in.at[slot, q], zr.at[slot, q])
                add_rows(mine, z_in.at[slot, q], rows)

            send(mine, z_in.at[slot, q], zs.at[k], zr.at[slot, q], p.by_z(step))
        else:
            for slot, there in ((0, p.low), (1, p.high)):

                @pl.when(jnp.logical_not(there))
                def _():
                    await_bytes(z_in.at[slot, q], zr.at[slot, q])
                    add_rows(mine, z_in.at[slot, q], rows)

            mixture[...] = mine[...]

    def attention(q):
        row_start = pl.multiple_of(q * plane_rows, plane_rows)
        at = pl.ds(row_start, plane_rows)

        @pl.loop(0, head_cols // TILE)
        def _(n):
            cols = pl.ds(pl.multiple_of(n * TILE, TILE), TILE)
            grad = d_attn[pl.ds(q * 2, 2), :, :width].reshape(plane_rows, width)
            weight_cols = pl.ds(pl.multiple_of(proj_cols + n * TILE, TILE), TILE)
            d_heads[at, cols] = mxu(grad, columns[:, weight_cols]).astype(bf16)

        def block(count):
            key, value = keys[:count], values[:count]
            row_pos = row_start + lax.broadcasted_iota(jnp.int32, (plane_rows, count), 0)
            allowed = lax.broadcasted_iota(jnp.int32, (plane_rows, count), 1) <= row_pos

            @pl.loop(0, heads)
            def _(h):
                cols = pl.ds(pl.multiple_of(h * HEAD_DIMENSION, HEAD_DIMENSION), HEAD_DIMENSION)
                query, d_out = queries[at, cols], d_heads[at, cols]
                scores = jnp.where(allowed, mxu(query, key, NT) * score_scale, -1e30)
                raised = jnp.exp(scores - jnp.max(scores, axis=-1, keepdims=True))
                prob = raised / jnp.sum(raised, axis=-1, keepdims=True)
                d_prob = mxu(d_out, value, NT)
                delta = jnp.sum(prob * d_prob, axis=-1, keepdims=True)
                d_scores = (prob * (d_prob - delta)).astype(bf16)
                d_query[at, cols] = mxu(d_scores, key) * score_scale
                d_key[:count] += mxu(d_scores, query, TN) * score_scale
                d_value[:count] += mxu(prob.astype(bf16), d_out, TN)

        half = length // 2

        @pl.when(q < 2)
        def _():
            block(half)

        @pl.when(q >= 2)
        def _():
            block(length)

    def unrotate(grad, at):
        swapped = jnp.concatenate(
            [grad[:, HEAD_DIMENSION // 2 :], grad[:, : HEAD_DIMENSION // 2]], axis=1
        )
        return grad * cosine[at, :] + swapped * sine[at, :]

    def raw_grads():
        q_sum[...] = jnp.zeros_like(q_sum)
        k_sum[...] = jnp.zeros_like(k_sum)

        def one(grad, raw, gain, total, at):
            turned = unrotate(grad, at)
            scale = lax.rsqrt(jnp.mean(raw * raw, axis=-1, keepdims=True) + EPS)
            total[...] += jnp.sum((turned * raw * scale).reshape(-1, 8, HEAD_DIMENSION), axis=0)
            u = turned * gain[...]
            dot = jnp.mean(u * raw, axis=-1, keepdims=True)
            return (scale * u - raw * (scale * scale * scale * dot)).astype(bf16)

        chunk = 128

        @pl.loop(0, length // chunk)
        def _(i):
            at = pl.ds(pl.multiple_of(i * chunk, chunk), chunk)
            for h in range(heads):
                cols = slice(h * HEAD_DIMENSION, (h + 1) * HEAD_DIMENSION)
                d_proj[at, cols] = one(d_query[at, cols], q_raw[at, cols], q_gain, q_sum, at)
            d_proj[at, head_cols : head_cols + HEAD_DIMENSION] = one(
                d_key[at, :], k_raw[at, :], k_gain, k_sum, at
            )
            d_proj[at, head_cols + HEAD_DIMENSION :] = d_value[at, :].astype(bf16)

        g_send[0] = gains[...]
        g_send[0, 2:3, :HEAD_DIMENSION] = jnp.sum(q_sum[...], axis=0, keepdims=True)
        g_send[0, 2:3, HEAD_DIMENSION : 2 * HEAD_DIMENSION] = jnp.sum(
            k_sum[...], axis=0, keepdims=True
        )

    def normed_grads():
        @pl.loop(0, width // TILE)
        def _(n):
            cols = pl.ds(pl.multiple_of(n * TILE, TILE), TILE)
            part = mxu(d_proj[...], columns[cols, :proj_cols], NT)
            d_normed[:, :, cols] = part.astype(bf16).reshape(length // rows, rows, TILE)
            total = jnp.sum(part * normed[:, cols].astype(f32), axis=0, keepdims=True)
            g_send[0, 0:1, cols] = total / attn_gain[:, cols]

    def gains_pass(t, target):
        send(g_send.at[t], g_in.at[t], ts.at[t], tr.at[t], target)

    def gains_take(t):
        await_bytes(g_in.at[t], tr.at[t])
        g_send[t + 1] = g_send[t] + g_in[t]

    def gains_z_pass():
        g_in[2 + p.z] = g_send[2]
        for d, target in enumerate(columns_z):
            send(g_send.at[2], g_in.at[2 + p.z], ts.at[2 + d], tr.at[2 + d], target)

    def gains_z_take():
        for d in range(3):
            await_bytes(g_in.at[0], tr.at[2 + d])
        g_send[3] = g_in[2] + g_in[3] + g_in[4] + g_in[5]

    def column_grads(source, value, first, count):
        @pl.loop(0, width // TILE)
        def _(n):
            cols = pl.ds(pl.multiple_of(n * TILE, TILE), TILE)
            part = source[..., cols].reshape(length, TILE)
            d_columns[cols, first : first + count] = mxu(part, value[...], TN).astype(bf16)

    loads = [
        pltpu.make_async_copy(columns_hbm, columns, load_sems.at[0]),
        pltpu.make_async_copy(normed_hbm, normed, load_sems.at[1]),
        pltpu.make_async_copy(rows_all.at[:, shard], d_attn, load_sems.at[2]),
    ]
    gather_out(0)
    loads[0].start()
    loads[1].start()
    sum_start()
    d_key[...] = jnp.zeros_like(d_key)
    d_value[...] = jnp.zeros_like(d_value)
    loads[0].wait()
    gather_in(0)
    gather_out(1)
    attention(p.near(0))
    gather_out(2)
    gather_in(1)
    attention(p.near(1))
    sum_turn(0)
    gather_out(3)
    gather_in(2)
    attention(p.near(2))
    sum_end(0)
    sum_turn(1)
    gather_in(3)
    attention(p.near(3))
    raw_grads()
    sum_end(1)
    loads[1].wait()
    normed_grads()
    gains_pass(0, p.by_core)
    column_grads(normed, d_proj, 0, proj_cols)
    gains_take(0)
    gains_pass(1, p.by_x)
    sum_turn(2)
    gains_take(1)
    gains_z_pass()
    column_grads(d_attn.at[:, :, pl.ds(0, width)], attended, proj_cols, head_cols)
    line = lax.broadcasted_iota(jnp.int32, (128, 128), 0)
    lane = lax.broadcasted_iota(jnp.int32, (128, 128), 1)
    router_cols = rows_all.shape[0] * rows_all.shape[1] // 8
    mine = (line == lane + place * router_cols) & (lane < router_cols)
    select = jnp.where(mine, 1.0, 0.0).astype(bf16)
    logits[...] = mxu(d_attn[:, :, width:].reshape(length, 128), select).astype(bf16)
    sum_end(2)
    gains_z_take()
    send(g_send.at[3], g_in.at[6], ts.at[5], tr.at[5], p.by_y)
    for q in range(4):
        await_bytes(own, gs.at[q])
    for there, slot in ((p.high, 0), (p.low, 1)):

        @pl.when(jnp.logical_not(there))
        def _():
            await_bytes(own, gz.at[p.z, slot])

    for k in range(1, 4):

        @pl.when(p.inner)
        def _():
            await_bytes(own, gz.at[p.near(k), 0])

    loads[2].start()
    loads[2].wait()
    column_grads(d_attn.at[:, :, pl.ds(0, width)], logits, proj_cols + head_cols, 128)
    sum_turn(3)
    sum_end(3)
    await_bytes(g_in.at[6], tr.at[5])
    gains_out[...] = g_send[3] + g_in[6]
    for t in range(6):
        await_bytes(g_in.at[0], ts.at[t])
    piece = x_in.at[0]
    for i in range(8):
        await_bytes(piece, ys.at[i])
    for q in range(4):
        await_bytes(piece, xs.at[q])
    for k in range(3):
        await_bytes(piece, zs.at[k])


def back(
    own, pair, rows_all, columns, normed, queries, keys, values, attended,
    q_raw, k_raw, cosine, sine, q_gain, k_gain, attn_gain, gains, collective_id,
):
    rows, wide = own.shape
    length, head_cols = queries.shape
    width = normed.shape[1]
    proj_cols = head_cols + 2 * HEAD_DIMENSION
    dma = pltpu.SemaphoreType.DMA
    bf16, f32 = jnp.bfloat16, jnp.float32
    anywhere, vmem = pl.BlockSpec(memory_space=pl.ANY), pl.BlockSpec(memory_space=pltpu.VMEM)
    return pl.pallas_call(
        back_kernel,
        out_shape=[
            jax.ShapeDtypeStruct((length // rows, rows, width), bf16),
            jax.ShapeDtypeStruct(columns.shape, bf16),
            jax.ShapeDtypeStruct(gains.shape, f32),
            jax.ShapeDtypeStruct((rows, width), bf16),
        ],
        in_specs=[anywhere] * 5 + [vmem] * 12,
        out_specs=[vmem] * 4,
        scratch_shapes=[
            pltpu.VMEM((8, rows, wide), bf16),
            pltpu.VMEM(columns.shape, bf16),
            pltpu.VMEM((length, width), bf16),
            pltpu.VMEM((length, head_cols), bf16),
            pltpu.VMEM((length, head_cols), f32),
            pltpu.VMEM((length, HEAD_DIMENSION), f32),
            pltpu.VMEM((length, HEAD_DIMENSION), f32),
            pltpu.VMEM((length, proj_cols), bf16),
            pltpu.VMEM((length, 128), bf16),
            pltpu.VMEM((8, HEAD_DIMENSION), f32),
            pltpu.VMEM((8, HEAD_DIMENSION), f32),
            pltpu.VMEM((8, rows, width), bf16),
            pltpu.VMEM((4, rows, width), bf16),
            pltpu.VMEM((8, rows, width), bf16),
            pltpu.VMEM((2, 4, rows, width), bf16),
            pltpu.VMEM((4, *gains.shape), f32),
            pltpu.VMEM((7, *gains.shape), f32),
            dma((4,)),
            dma((4, 2)),
            dma((4, 2)),
            dma((3,)),
            dma,
            dma((8,)),
            dma((8,)),
            dma((8,)),
            dma((4,)),
            dma((4,)),
            dma((3,)),
            dma((2, 4)),
            dma((6,)),
            dma((6,)),
        ],
        compiler_params=pltpu.CompilerParams(
            collective_id=collective_id, has_side_effects=True, vmem_limit_bytes=VMEM_LIMIT
        ),
        name="back",
    )(
        own, pair, rows_all, columns, normed, queries, keys, values, attended,
        q_raw, k_raw, cosine, sine, q_gain, k_gain, attn_gain, gains,
    )


C_Z, C_X, C_Y, C_C, C_KINDS = 0, 1, 2, 4, 8


def front_kernel(
    own, pieces, cot, cosine, sine, q_gain, k_gain,
    normed_out, columns_out, cot_all, queries, keys, values, attended, q_raw, k_raw, attn_out,
    normed, columns, part, x_in, z_in,
    ss, rs, zs, cs, cr, ys, yr, ks, kr, local_sems, gs, gr, gz, xs, xr, us, ur,
):
    p = Place()
    bf16 = jnp.bfloat16
    greet_seq(p)
    place, shard = p.z * 2 + p.x, p.y * 2 + p.c
    mine = place * 4 + shard
    rows, width = own.shape
    length, head_cols = queries.shape
    heads = head_cols // HEAD_DIMENSION
    proj_cols = head_cols + 2 * HEAD_DIMENSION
    plane_rows = 2 * rows
    score_scale = 1.0 / math.sqrt(HEAD_DIMENSION)

    def rows_at(q, x):
        return normed.at[q * 2 + x]

    def rows_move(k):
        q = p.near(k)
        there = rows_at(q, p.x)
        if k == 0:
            src = own
            for step, end in ((1, p.high), (-1, p.low)):

                @pl.when(jnp.logical_not(end))
                def _():
                    send(src, there, zs.at[q, 0 if step > 0 else 1], rs.at[q, 0], p.by_z(step))

            pltpu.make_async_copy(own, there, local_sems.at[0]).start()
        else:
            src = there
            await_bytes(src, rs.at[q, 0])

            @pl.when(p.inner)
            def _():
                send(src, src, zs.at[q, 0], rs.at[q, 0], p.by_z(p.onward(k)))

        send(src, there, ss.at[q], rs.at[q, 1], p.by_x)

    def pass_on(d):
        block = ((place + 8 - d) % 8) * 4 + shard
        src = pieces.at[place] if d == 0 else columns.at[block]
        if d > 0:
            await_bytes(src, cr.at[d])
        send(src, columns.at[block], ys.at[d], yr.at[d], p.by_y)
        send(src, columns.at[block], ks.at[0, d], kr.at[0, d], p.by_core)

    def pass_across(d):
        block = columns.at[((place + 8 - d) % 8) * 4 + (1 - p.y) * 2 + p.c]
        await_bytes(block, yr.at[d])
        send(block, block, ks.at[1, d], kr.at[1, d], p.by_core)

    def cot_at(q, x, y):
        return cot_all.at[p.block(q, x, y, p.c)]

    def cot_core(q, j, src):
        x, y = (p.x, 1 - p.x)[j % 2], (p.y, 1 - p.y)[j // 2]
        send(src, cot_at(q, x, y), gs.at[q, C_C + j], gr.at[q, C_C + j], p.by_core)

    def cot_move(k):
        q = p.near(k)
        there = cot_at(q, p.x, p.y)
        if k == 0:
            src = cot
            for step, end in ((1, p.high), (-1, p.low)):

                @pl.when(jnp.logical_not(end))
                def _():
                    send(src, there, gz.at[q, 0 if step > 0 else 1], gr.at[q, C_Z], p.by_z(step))

            pltpu.make_async_copy(cot, there, local_sems.at[2]).start()
        else:
            src = there
            await_bytes(src, gr.at[q, C_Z])

            @pl.when(p.inner)
            def _():
                send(src, src, gz.at[q, 0], gr.at[q, C_Z], p.by_z(p.onward(k)))

        send(src, there, gs.at[q, C_Y], gr.at[q, C_Y], p.by_y)
        send(src, there, gs.at[q, C_X], gr.at[q, C_X], p.by_x)
        cot_core(q, 0, src)

    def cot_turn(k):
        q = p.near(k)
        there = cot_at(q, 1 - p.x, p.y)
        await_bytes(there, gr.at[q, C_X])
        send(there, there, gs.at[q, C_Y + 1], gr.at[q, C_Y + 1], p.by_y)
        cot_core(q, 1, there)

    def cot_end(k):
        q = p.near(k)
        for j, x in ((0, p.x), (1, 1 - p.x)):
            there = cot_at(q, x, 1 - p.y)
            await_bytes(there, gr.at[q, C_Y + j])
            cot_core(q, 2 + j, there)

    def sum_end(k):
        q = p.far(k)
        held = part.at[q * 2 + p.x]
        await_bytes(x_in.at[q], xr.at[q])
        add_rows(held, x_in.at[q], rows)
        if k < 3:
            step = p.toward(k)
            slot = (1 - step) // 2

            @pl.when(p.inner)
            def _():
                await_bytes(z_in.at[slot, q], ur.at[slot, q])
                add_rows(held, z_in.at[slot, q], rows)

            send(held, z_in.at[slot, q], us.at[k], ur.at[slot, q], p.by_z(step))
        else:
            for slot, there in ((0, p.low), (1, p.high)):

                @pl.when(jnp.logical_not(there))
                def _():
                    await_bytes(z_in.at[slot, q], ur.at[slot, q])
                    add_rows(held, z_in.at[slot, q], rows)

            attn_out[...] = held[...]

    def project(n):
        cols = slice(n * TILE, (n + 1) * TILE)
        weight = columns[:, :, cols].reshape(width, TILE)
        result = mxu(normed[...].reshape(length, width), weight)
        if n * TILE < head_cols:
            q_raw[:, cols] = result
        else:
            k_raw[...] = result[:, :HEAD_DIMENSION]
            values[...] = result[:, HEAD_DIMENSION:].astype(bf16)

    def prepare():
        def one(raw, gain, at):
            scaled = raw * lax.rsqrt(jnp.mean(raw * raw, axis=-1, keepdims=True) + EPS) * gain[...]
            swapped = jnp.concatenate(
                [scaled[:, HEAD_DIMENSION // 2 :], scaled[:, : HEAD_DIMENSION // 2]], axis=1
            )
            return (scaled * cosine[at, :] - swapped * sine[at, :]).astype(bf16)

        chunk = 128

        @pl.loop(0, length // chunk)
        def _(i):
            at = pl.ds(pl.multiple_of(i * chunk, chunk), chunk)
            for h in range(heads):
                cols = slice(h * HEAD_DIMENSION, (h + 1) * HEAD_DIMENSION)
                queries[at, cols] = one(q_raw[at, cols], q_gain, at)
            keys[at, :] = one(k_raw[at, :], k_gain, at)

    def attention(k):
        q = p.far(k)
        row_start = pl.multiple_of(q * plane_rows, plane_rows)
        at = pl.ds(row_start, plane_rows)

        def block(count):
            row_pos = row_start + lax.broadcasted_iota(jnp.int32, (plane_rows, count), 0)
            allowed = lax.broadcasted_iota(jnp.int32, (plane_rows, count), 1) <= row_pos

            @pl.loop(0, heads)
            def _(h):
                cols = pl.ds(pl.multiple_of(h * HEAD_DIMENSION, HEAD_DIMENSION), HEAD_DIMENSION)
                scores = mxu(queries[at, cols], keys[:count], NT) * score_scale
                scores = jnp.where(allowed, scores, -1e30)
                raised = jnp.exp(scores - jnp.max(scores, axis=-1, keepdims=True))
                prob = raised / jnp.sum(raised, axis=-1, keepdims=True)
                attended[at, cols] = mxu(prob.astype(bf16), values[:count]).astype(bf16)

        @pl.when(q < 2)
        def _():
            block(length // 2)

        @pl.when(q >= 2)
        def _():
            block(length)

        per_tile = TILE // columns.shape[1]

        @pl.loop(0, width // TILE)
        def _(n):
            cols = pl.ds(pl.multiple_of(n * TILE, TILE), TILE)
            weight = columns[pl.ds(n * per_tile, per_tile), :, proj_cols : proj_cols + head_cols]
            result = mxu(attended[at, :], weight.reshape(TILE, head_cols), NT).astype(bf16)
            part[pl.ds(q * 2, 2), :, cols] = result.reshape(2, rows, TILE)

        send(part.at[q * 2 + 1 - p.x], x_in.at[q], xs.at[q], xr.at[q], p.by_x)

    rows_move(0)
    for d in range(1, 8):
        send(pieces.at[(place + d) % 8], columns.at[mine], cs.at[d], cr.at[d], seq_peer(p, d))
    pltpu.make_async_copy(pieces.at[place], columns.at[mine], local_sems.at[1]).start()
    pass_on(0)
    rows_move(1)
    for d in (1, 2, 7):
        pass_on(d)
    rows_move(2)
    cot_move(0)
    for d in (6, 3, 5):
        pass_on(d)
    rows_move(3)
    pass_on(4)
    for d in (0, 1, 2, 7, 6, 3, 5, 4):
        pass_across(d)
    cot_move(1)
    for k in range(4):
        await_bytes(own, rs.at[p.near(k), 1])
    pltpu.make_async_copy(own, rows_at(p.z, p.x), local_sems.at[0]).wait()
    pltpu.make_async_copy(pieces.at[place], columns.at[mine], local_sems.at[1]).wait()
    piece = pieces.at[0]
    for d in range(8):
        await_bytes(piece, kr.at[0, d])
        await_bytes(piece, kr.at[1, d])
    pltpu.make_async_copy(normed, normed_out, local_sems.at[0]).start()
    pltpu.make_async_copy(columns, columns_out, local_sems.at[1]).start()
    cot_turn(0)
    for n in range(proj_cols // TILE):
        project(n)
    cot_move(2)
    prepare()
    cot_turn(1)
    attention(0)
    cot_end(0)
    attention(1)
    cot_move(3)
    sum_end(0)
    attention(2)
    cot_turn(2)
    cot_end(1)
    sum_end(1)
    attention(3)
    cot_turn(3)
    sum_end(2)
    cot_end(2)
    sum_end(3)
    cot_end(3)
    for q in range(4):
        for j in range(4):
            await_bytes(cot, gr.at[q, C_C + j])
            await_bytes(cot, gs.at[q, C_C + j])
        for kind in (C_X, C_Y, C_Y + 1):
            await_bytes(cot, gs.at[q, kind])
        await_bytes(own, ss.at[q])
        await_bytes(own, xs.at[q])
    for there, slot in ((p.high, 0), (p.low, 1)):

        @pl.when(jnp.logical_not(there))
        def _():
            await_bytes(own, zs.at[p.z, slot])
            await_bytes(cot, gz.at[p.z, slot])

    for k in range(1, 4):

        @pl.when(p.inner)
        def _():
            await_bytes(own, zs.at[p.near(k), 0])
            await_bytes(cot, gz.at[p.near(k), 0])

    for k in range(3):
        await_bytes(own, us.at[k])
    for d in range(8):
        if d > 0:
            await_bytes(piece, cs.at[d])
        await_bytes(piece, ys.at[d])
        await_bytes(piece, ks.at[0, d])
        await_bytes(piece, ks.at[1, d])
    pltpu.make_async_copy(cot, cot_at(p.z, p.x, p.y), local_sems.at[2]).wait()
    pltpu.make_async_copy(normed, normed_out, local_sems.at[0]).wait()
    pltpu.make_async_copy(columns, columns_out, local_sems.at[1]).wait()


def front(own, pieces, cot, cosine, sine, q_gain, k_gain, head_cols, collective_id):
    dma = pltpu.SemaphoreType.DMA
    bf16, f32 = jnp.bfloat16, jnp.float32
    rows, width = own.shape
    count, piece_rows, piece_width = pieces.shape
    length = count * rows
    anywhere, vmem = pl.BlockSpec(memory_space=pl.ANY), pl.BlockSpec(memory_space=pltpu.VMEM)
    return pl.pallas_call(
        front_kernel,
        out_shape=[
            jax.ShapeDtypeStruct((count, rows, width), bf16),
            jax.ShapeDtypeStruct((count * 4, piece_rows, piece_width), bf16),
            jax.ShapeDtypeStruct((count * 4, rows, width), bf16),
            jax.ShapeDtypeStruct((length, head_cols), bf16),
            jax.ShapeDtypeStruct((length, HEAD_DIMENSION), bf16),
            jax.ShapeDtypeStruct((length, HEAD_DIMENSION), bf16),
            jax.ShapeDtypeStruct((length, head_cols), bf16),
            jax.ShapeDtypeStruct((length, head_cols), f32),
            jax.ShapeDtypeStruct((length, HEAD_DIMENSION), f32),
            jax.ShapeDtypeStruct((rows, width), bf16),
        ],
        in_specs=[anywhere] * 3 + [vmem] * 4,
        out_specs=[anywhere] * 3 + [vmem] * 7,
        scratch_shapes=[
            pltpu.VMEM((count, rows, width), bf16),
            pltpu.VMEM((count * 4, piece_rows, piece_width), bf16),
            pltpu.VMEM((count, rows, width), bf16),
            pltpu.VMEM((4, rows, width), bf16),
            pltpu.VMEM((2, 4, rows, width), bf16),
            dma((4,)),
            dma((4, 2)),
            dma((4, 2)),
            dma((8,)),
            dma((8,)),
            dma((8,)),
            dma((8,)),
            dma((2, 8)),
            dma((2, 8)),
            dma((3,)),
            dma((4, C_KINDS)),
            dma((4, C_KINDS)),
            dma((4, 2)),
            dma((4,)),
            dma((4,)),
            dma((3,)),
            dma((2, 4)),
        ],
        compiler_params=pltpu.CompilerParams(
            collective_id=collective_id, has_side_effects=True, vmem_limit_bytes=VMEM_LIMIT
        ),
        name="front",
    )(own, pieces, cot, cosine, sine, q_gain, k_gain)


def head_columns(weight, group_index):
    rows = weight.shape[0]
    query_width = QUERY_HEADS * HEAD_DIMENSION
    key_width = KEY_VALUE_HEADS * HEAD_DIMENSION
    query = weight[:, :query_width].reshape(rows, len(group_index), -1).transpose(1, 0, 2)
    keys = weight[:, query_width : query_width + key_width].reshape(rows, KEY_VALUE_HEADS, -1)
    values = weight[:, query_width + key_width :].reshape(rows, KEY_VALUE_HEADS, -1)
    keys = jnp.stack([keys[:, group] for group in group_index])
    values = jnp.stack([values[:, group] for group in group_index])
    return jnp.concatenate([query, keys, values], axis=2)


def gathered_body(
    tokens,
    query_key_value_weight,
    w_out_t,
    w_router,
    w_in,
    w_down,
    attn_gain,
    ffn_gain,
    q_gain,
    k_gain,
    routes,
    cotangent,
):
    bf16, f32 = jnp.bfloat16, jnp.float32
    both = ("seq", "fsdp")
    seq_size = lax.axis_size("seq")
    shard_size = lax.axis_size("fsdp")
    experts = seq_size * shard_size
    rows = tokens.shape[1]
    width = tokens.shape[2]
    length = rows * seq_size
    weight_rows = query_key_value_weight.shape[0]
    heads = QUERY_HEADS // seq_size
    head_cols = heads * HEAD_DIMENSION
    kv_cols = HEAD_DIMENSION
    proj_cols = head_cols + 2 * kv_cols
    all_cols = proj_cols + head_cols
    spare_cols = 128
    group_index = [s * heads * KEY_VALUE_HEADS // QUERY_HEADS for s in range(seq_size)]
    capacity = 2 * rows * TOPK // experts

    pieces = jnp.concatenate(
        [
            head_columns(query_key_value_weight, group_index),
            w_out_t.reshape(weight_rows, seq_size, head_cols).transpose(1, 0, 2),
            jnp.broadcast_to(
                jnp.pad(w_router, ((0, 0), (0, spare_cols - experts))),
                (seq_size, weight_rows, spare_cols),
            ),
        ],
        axis=2,
    )
    resid_in = tokens[0].astype(f32)
    normed_one = rms_scale(resid_in, attn_gain).astype(bf16)
    half_dim = HEAD_DIMENSION // 2
    frequency = ROPE_BASE ** (-2.0 * jnp.arange(half_dim, dtype=f32) / HEAD_DIMENSION)
    angles = jnp.arange(length, dtype=f32)[:, None] * frequency[None, :]
    cosine, sine = jnp.cos(angles), jnp.sin(angles)
    cosine = jnp.concatenate([cosine, cosine], axis=1)
    sine = jnp.concatenate([sine, -sine], axis=1)
    normed_all, columns, cot_all, queries, keys, values, attended, q_raw, k_raw, attn_out = front(
        normed_one, pieces, cotangent[0], cosine, sine, q_gain[None], k_gain[None], head_cols, 1
    )
    normed_all = normed_all.reshape(length, width)
    columns = columns.reshape(width, -1)
    full_router = columns[:, all_cols : all_cols + experts]
    hidden = resid_in + attn_out.astype(f32)
    normed_two = rms_scale(hidden, ffn_gain).astype(bf16)

    logits = jnp.dot(normed_two, full_router, preferred_element_type=f32)
    onehot = routes[0][:, :, None] == jnp.arange(experts, dtype=jnp.int32)
    onehot_float = onehot.astype(f32)
    named = jnp.sum(onehot_float, axis=1)
    order = jnp.arange(rows, dtype=jnp.int32)
    upto = (order[None, :] <= order[:, None]).astype(bf16)
    slot_info = named * jnp.dot(upto, named.astype(bf16), preferred_element_type=f32)
    chosen = jnp.sum(onehot_float * logits[:, None, :], axis=-1)
    row_max = jnp.max(chosen, axis=-1, keepdims=True)
    exp_part = jnp.exp(chosen - row_max)
    gate_probs = exp_part / jnp.sum(exp_part, axis=-1, keepdims=True)
    gate_dense = jnp.sum(onehot_float * gate_probs[..., None], axis=1)

    gate_high = gate_dense.astype(bf16)
    gate_low = (gate_dense - gate_high.astype(f32)).astype(bf16)
    route_info = jnp.concatenate([gate_high, gate_low, slot_info.astype(bf16)], axis=1)
    route_info = jnp.pad(route_info, ((0, 0), (0, 128 - route_info.shape[1] % 128)))
    gate_weight = w_in[0]
    down_weight = w_down[0]
    rows_all, out_part, d_part, rows_in, d_expert, inner_act, d_gate_up = experts_gathered(
        jnp.concatenate([normed_two, route_info], axis=1),
        cot_all,
        gate_weight,
        down_weight,
        capacity,
        3,
    )
    d_back, out_pair = sum_all(d_part, out_part, 5)
    d_back = d_back.astype(f32)

    d_gate_dense = d_back[:, width : width + experts] + d_back[:, width + experts : width + 2 * experts]
    d_gates = jnp.sum(onehot_float * d_gate_dense[:, None, :], axis=-1)
    d_chosen = gate_probs * (d_gates - jnp.sum(gate_probs * d_gates, axis=-1, keepdims=True))
    d_logits = jnp.sum(d_chosen[..., None] * onehot_float, axis=1).astype(bf16)
    d_normed_two = d_back[:, :width] + jnp.einsum(
        "te,de->td", d_logits, full_router, preferred_element_type=f32
    )
    out_grad = cotangent[0].astype(f32)
    unused_two, pull_two = jax.vjp(rms_scale, hidden, ffn_gain)
    d_hidden_norm, d_ffn_gain = pull_two(d_normed_two)
    d_hidden = out_grad + d_hidden_norm
    d_attn = d_hidden.astype(bf16)

    d_send = jnp.concatenate([d_attn, jnp.pad(d_logits, ((0, 0), (0, 128 - experts)))], axis=1)
    gains = jnp.pad(d_ffn_gain[None], ((1, 6), (0, 0)))
    d_normed_part, d_columns, gains, mixture = back(
        d_send,
        out_pair.reshape(2 * seq_size, rows, width),
        rows_all.reshape(seq_size, shard_size, rows, -1),
        columns,
        normed_all,
        queries,
        keys,
        values,
        attended,
        q_raw,
        k_raw,
        cosine,
        sine,
        q_gain[None],
        k_gain[None],
        attn_gain[None],
        gains,
        6,
    )
    output = (hidden + mixture.astype(f32)).astype(bf16)
    router_cols = experts // seq_size
    d_tokens, d_pieces, d_w_in, d_w_down = leave(
        d_normed_part,
        d_columns.reshape(seq_size, 2, shard_size // 2, weight_rows, all_cols + spare_cols),
        rows_in,
        d_gate_up,
        inner_act,
        d_expert,
        tokens[0],
        d_hidden,
        attn_gain[None],
        7,
    )
    d_w_in, d_w_down = d_w_in.astype(f32)[None], d_w_down.astype(f32)[None]
    d_tokens = d_tokens[None]
    d_pieces = d_pieces.astype(f32).transpose(1, 0, 2)
    per_group = seq_size // KEY_VALUE_HEADS
    d_kv = d_pieces[:, :, head_cols:proj_cols].reshape(
        weight_rows, KEY_VALUE_HEADS, per_group, 2, kv_cols
    )
    d_kv = jnp.sum(d_kv, axis=2).transpose(0, 2, 1, 3).reshape(weight_rows, -1)
    d_w_qkv = jnp.concatenate([d_pieces[:, :, :head_cols].reshape(weight_rows, -1), d_kv], axis=1)
    d_w_out_t = d_pieces[:, :, proj_cols:all_cols].reshape(weight_rows, -1)
    d_w_router = d_pieces[:, :, all_cols : all_cols + router_cols].reshape(weight_rows, experts)
    d_attn_gain, d_ffn_gain = gains[0], gains[1]
    d_q_gain = gains[2, :HEAD_DIMENSION]
    d_k_gain = gains[2, HEAD_DIMENSION : 2 * HEAD_DIMENSION]
    return (
        output[None],
        d_tokens,
        d_w_qkv,
        d_w_out_t,
        d_w_router,
        d_w_in,
        d_w_down,
        d_attn_gain,
        d_ffn_gain,
        d_q_gain,
        d_k_gain,
    )


def gathered_fits(mesh):
    return mesh.shape["seq"] == 8 and mesh.shape["fsdp"] == 4


def solution(mesh):
    return jax.shard_map(
        gathered_body if gathered_fits(mesh) else routed_body,
        mesh=mesh,
        in_specs=(
            P("fsdp", "seq", None),
            P(("seq", "fsdp"), None),
            P(("seq", "fsdp"), None),
            P(("seq", "fsdp"), None),
            P(("seq", "fsdp"), None, None),
            P(("seq", "fsdp"), None, None),
            P(),
            P(),
            P(),
            P(),
            P("fsdp", "seq", None),
            P("fsdp", "seq", None),
        ),
        out_specs=(
            P("fsdp", "seq", None),
            P("fsdp", "seq", None),
            P(("seq", "fsdp"), None),
            P(("seq", "fsdp"), None),
            P(("seq", "fsdp"), None),
            P(("seq", "fsdp"), None, None),
            P(("seq", "fsdp"), None, None),
            P(),
            P(),
            P(),
            P(),
        ),
        check_vma=False,
    )
```

```python
from functools import partial
import math

import jax
import jax.numpy as jnp
import numpy as np
from jax import lax
from jax.experimental import pallas as pl
from jax.experimental.pallas import tpu as pltpu
from jax.sharding import PartitionSpec as P

QUERY_HEADS = 32
KEY_VALUE_HEADS = 4
HEAD_DIMENSION = 128
FF = 768
TOPK = 8


EPS = 1e-06
ROPE_BASE = 1000000.0


def rms_scale(values, gain):
    return values * lax.rsqrt(jnp.mean(values * values, axis=-1, keepdims=True) + EPS) * gain


def rotate(values, positions):
    half_dim = values.shape[-1] // 2
    frequency = ROPE_BASE ** (-2.0 * jnp.arange(half_dim, dtype=jnp.float32) / values.shape[-1])
    angles = positions.astype(jnp.float32)[:, None] * frequency[None, :]
    cosine = jnp.cos(angles)[:, None, :]
    sine_part = jnp.sin(angles)[:, None, :]
    first_half = values[..., :half_dim]
    second = values[..., half_dim:]
    return jnp.concatenate(
        [first_half * cosine - second * sine_part, second * cosine + first_half * sine_part],
        axis=-1,
    )


def head_prepare(raw_heads, gain, positions):
    return rotate(rms_scale(raw_heads, gain), positions)


def route_slots(route_flat, experts):
    onehot = (route_flat[:, None] == jnp.arange(experts, dtype=jnp.int32)[None, :]).astype(
        jnp.int32
    )
    earlier = jnp.cumsum(onehot, axis=0) - onehot
    return (onehot, jnp.sum(earlier * onehot, axis=1))


def pack_slots(row_values, expert_ids, slot_index, slot_shape):
    buffer = jnp.zeros(slot_shape, row_values.dtype)
    return buffer.at[expert_ids // slot_shape[1], expert_ids % slot_shape[1], slot_index].set(
        row_values
    )


def unpack_slots(buffer, expert_ids, slot_index):
    return buffer[expert_ids // buffer.shape[1], expert_ids % buffer.shape[1], slot_index]


def causal_scores(query_part, key_full, row_start):
    block_rows = query_part.shape[0]
    score_scale = 1.0 / math.sqrt(query_part.shape[2])
    scores = (
        jnp.einsum("qhd,khd->hqk", query_part, key_full, preferred_element_type=jnp.float32)
        * score_scale
    )
    key_pos = jnp.arange(key_full.shape[0], dtype=jnp.int32)
    row_pos = row_start + jnp.arange(block_rows, dtype=jnp.int32)
    allowed = key_pos[None, :] <= row_pos[:, None]
    return jnp.where(allowed[None], scores, -1e30)


def attend_forward(query_rows_all, key_full, value_full):
    sequence_length = query_rows_all.shape[0]
    block_rows = min(512, sequence_length)

    def one_block(block_index):
        row_start = block_index * block_rows
        query_part = lax.dynamic_slice_in_dim(query_rows_all, row_start, block_rows, 0)
        scores = causal_scores(query_part, key_full, row_start)
        row_max = jnp.max(scores, axis=-1, keepdims=True)
        weights = jnp.exp(scores - row_max)
        row_total = jnp.sum(weights, axis=-1, keepdims=True)
        prob_low = (weights / row_total).astype(jnp.bfloat16)
        mixed_out = jnp.einsum(
            "hqk,khd->qhd", prob_low, value_full, preferred_element_type=jnp.float32
        )
        return (mixed_out.astype(jnp.bfloat16), (row_max + jnp.log(row_total))[..., 0])

    mixed_out, log_total = lax.map(
        one_block, jnp.arange(sequence_length // block_rows, dtype=jnp.int32)
    )
    return (mixed_out.reshape(query_rows_all.shape), log_total)


def attend_backward(query_rows_all, key_full, value_full, log_total, d_mixed):
    sequence_length = query_rows_all.shape[0]
    block_rows = min(512, sequence_length)
    score_scale = 1.0 / math.sqrt(query_rows_all.shape[2])

    def one_block(running, block_index):
        d_key_sum, d_value_sum = running
        row_start = block_index * block_rows
        query_part = lax.dynamic_slice_in_dim(query_rows_all, row_start, block_rows, 0)
        d_part = lax.dynamic_slice_in_dim(d_mixed, row_start, block_rows, 0)
        scores = causal_scores(query_part, key_full, row_start)
        prob_full = jnp.exp(scores - log_total[block_index][..., None])
        prob_low = prob_full.astype(jnp.bfloat16)
        d_probs = jnp.einsum("qhd,khd->hqk", d_part, value_full, preferred_element_type=jnp.float32)
        row_delta = jnp.sum(prob_full * d_probs, axis=-1, keepdims=True)
        d_scores = (prob_full * (d_probs - row_delta)).astype(jnp.bfloat16)
        d_query_part = (
            jnp.einsum("hqk,khd->qhd", d_scores, key_full, preferred_element_type=jnp.float32)
            * score_scale
        )
        d_key_sum = (
            d_key_sum
            + jnp.einsum("hqk,qhd->khd", d_scores, query_part, preferred_element_type=jnp.float32)
            * score_scale
        )
        d_value_sum = d_value_sum + jnp.einsum(
            "hqk,qhd->khd", prob_low, d_part, preferred_element_type=jnp.float32
        )
        return ((d_key_sum, d_value_sum), d_query_part)

    zero_grad = jnp.zeros(key_full.shape, jnp.float32)
    (d_key_sum, d_value_sum), d_query = lax.scan(
        one_block,
        (zero_grad, zero_grad),
        jnp.arange(sequence_length // block_rows, dtype=jnp.int32),
    )
    return (d_query.reshape(query_rows_all.shape), d_key_sum, d_value_sum)


def routed_body(
    tokens,
    query_key_value_weight,
    w_out_t,
    w_router,
    w_in,
    w_down,
    attn_gain,
    ffn_gain,
    q_gain,
    k_gain,
    routes,
    cotangent,
):
    sequence_count = lax.axis_size("seq")
    shard_count = lax.axis_size("fsdp")
    experts = sequence_count * shard_count
    token_row_count = tokens.shape[1]
    model_width = tokens.shape[2]
    query_group_width = QUERY_HEADS // KEY_VALUE_HEADS
    capacity = 2 * token_row_count * TOPK // experts
    slot_shape = (sequence_count, shard_count, capacity, model_width)
    positions = lax.axis_index("seq") * token_row_count + jnp.arange(
        token_row_count, dtype=jnp.int32
    )
    full_qkv, full_out, full_router = (
        lax.all_gather(query_key_value_weight, ("seq", "fsdp"), axis=0, tiled=True),
        lax.all_gather(w_out_t, ("seq", "fsdp"), axis=0, tiled=True),
        lax.all_gather(w_router, ("seq", "fsdp"), axis=0, tiled=True),
    )
    resid_in = tokens[0].astype(jnp.float32)
    normed_one = rms_scale(resid_in, attn_gain).astype(jnp.bfloat16)
    projection_output = jnp.dot(normed_one, full_qkv, preferred_element_type=jnp.float32)
    q_raw = projection_output[:, : QUERY_HEADS * HEAD_DIMENSION].reshape(
        token_row_count, QUERY_HEADS, HEAD_DIMENSION
    )
    key_unnormed = projection_output[
        :, QUERY_HEADS * HEAD_DIMENSION : (QUERY_HEADS + KEY_VALUE_HEADS) * HEAD_DIMENSION
    ].reshape(token_row_count, KEY_VALUE_HEADS, HEAD_DIMENSION)
    value_per_head = (
        projection_output[:, (QUERY_HEADS + KEY_VALUE_HEADS) * HEAD_DIMENSION :]
        .reshape(token_row_count, KEY_VALUE_HEADS, HEAD_DIMENSION)
        .astype(jnp.bfloat16)
    )
    prepare = partial(head_prepare, positions=positions)
    query_rows_all = prepare(q_raw, q_gain).astype(jnp.bfloat16)
    key_per_head = prepare(key_unnormed, k_gain).astype(jnp.bfloat16)
    send_keys = jnp.repeat(key_per_head, query_group_width, axis=1)
    send_values = jnp.repeat(value_per_head, query_group_width, axis=1)
    head_queries, head_keys, head_values = (
        lax.all_to_all(query_rows_all, "seq", split_axis=1, concat_axis=0, tiled=True),
        lax.all_to_all(send_keys, "seq", split_axis=1, concat_axis=0, tiled=True),
        lax.all_to_all(send_values, "seq", split_axis=1, concat_axis=0, tiled=True),
    )
    mixed_heads, log_total = attend_forward(head_queries, head_keys, head_values)
    mixed_tok = lax.all_to_all(mixed_heads, "seq", split_axis=0, concat_axis=1, tiled=True)
    attention_result = mixed_tok.reshape(token_row_count, QUERY_HEADS * HEAD_DIMENSION)
    attn_out = jnp.einsum(
        "tj,dj->td", attention_result, full_out, preferred_element_type=jnp.float32
    )
    hidden = resid_in + attn_out
    normed_two = rms_scale(hidden, ffn_gain).astype(jnp.bfloat16)
    logits = jnp.dot(normed_two, full_router, preferred_element_type=jnp.float32)
    route_flat = routes[0].reshape(-1)
    onehot, slot_index = route_slots(route_flat, experts)
    onehot_float = onehot.reshape(token_row_count, TOPK, experts).astype(jnp.float32)
    chosen = jnp.sum(onehot_float * logits[:, None, :], axis=-1)
    row_max = jnp.max(chosen, axis=-1, keepdims=True)
    exp_part = jnp.exp(chosen - row_max)
    gate_probs = exp_part / jnp.sum(exp_part, axis=-1, keepdims=True)
    send_rows = pack_slots(jnp.repeat(normed_two, TOPK, axis=0), route_flat, slot_index, slot_shape)
    arrived = lax.all_to_all(
        lax.all_to_all(send_rows, "seq", split_axis=0, concat_axis=0, tiled=True),
        "fsdp",
        split_axis=1,
        concat_axis=1,
        tiled=True,
    )
    rows_in = arrived.reshape(-1, model_width)
    gate_weight = w_in[0]
    down_weight = w_down[0]
    gate_up = jnp.dot(rows_in, gate_weight, preferred_element_type=jnp.float32)
    gate_half = gate_up[:, :FF]
    up_half = gate_up[:, FF:]
    gate_sig = jax.nn.sigmoid(gate_half)
    silu_gate = gate_half * gate_sig
    inner_act = (silu_gate * up_half).astype(jnp.bfloat16)
    expert_out = jnp.dot(inner_act, down_weight, preferred_element_type=jnp.float32).astype(
        jnp.bfloat16
    )
    returned = lax.all_to_all(
        lax.all_to_all(
            expert_out.reshape(slot_shape), "seq", split_axis=0, concat_axis=0, tiled=True
        ),
        "fsdp",
        split_axis=1,
        concat_axis=1,
        tiled=True,
    )
    picked = (
        unpack_slots(returned, route_flat, slot_index)
        .astype(jnp.float32)
        .reshape(token_row_count, TOPK, model_width)
    )
    mixture = jnp.sum(gate_probs[..., None] * picked, axis=1)
    output = (hidden + mixture).astype(jnp.bfloat16)
    full_qkv, full_out, full_router = (
        lax.all_gather(query_key_value_weight, ("seq", "fsdp"), axis=0, tiled=True),
        lax.all_gather(w_out_t, ("seq", "fsdp"), axis=0, tiled=True),
        lax.all_gather(w_router, ("seq", "fsdp"), axis=0, tiled=True),
    )
    out_grad = cotangent[0].astype(jnp.float32)
    d_picked = (
        (gate_probs[..., None] * out_grad[:, None, :]).astype(jnp.bfloat16).reshape(-1, model_width)
    )
    d_gates = jnp.sum(picked * out_grad[:, None, :], axis=-1)
    d_send = pack_slots(d_picked, route_flat, slot_index, slot_shape)
    d_arrived = lax.all_to_all(
        lax.all_to_all(d_send, "seq", split_axis=0, concat_axis=0, tiled=True),
        "fsdp",
        split_axis=1,
        concat_axis=1,
        tiled=True,
    ).reshape(-1, model_width)
    d_inner = jnp.einsum("rd,fd->rf", d_arrived, down_weight, preferred_element_type=jnp.float32)
    d_gate_half = d_inner * up_half * gate_sig * (1.0 + gate_half * (1.0 - gate_sig))
    d_up_half = d_inner * silu_gate
    d_gate_up = jnp.concatenate([d_gate_half, d_up_half], axis=1).astype(jnp.bfloat16)
    d_w_down = jnp.einsum("rf,rd->fd", inner_act, d_arrived, preferred_element_type=jnp.float32)[
        None
    ]
    d_w_in = jnp.einsum("rd,rf->df", rows_in, d_gate_up, preferred_element_type=jnp.float32)[None]
    d_rows = jnp.einsum(
        "rf,df->rd", d_gate_up, gate_weight, preferred_element_type=jnp.float32
    ).astype(jnp.bfloat16)
    d_back = lax.all_to_all(
        lax.all_to_all(d_rows.reshape(slot_shape), "seq", split_axis=0, concat_axis=0, tiled=True),
        "fsdp",
        split_axis=1,
        concat_axis=1,
        tiled=True,
    )
    d_routed = jnp.sum(
        unpack_slots(d_back, route_flat, slot_index)
        .astype(jnp.float32)
        .reshape(token_row_count, TOPK, model_width),
        axis=1,
    )
    d_chosen = gate_probs * (d_gates - jnp.sum(gate_probs * d_gates, axis=-1, keepdims=True))
    d_logits = jnp.einsum("tk,tke->te", d_chosen, onehot_float).astype(jnp.bfloat16)
    d_normed_two = d_routed + jnp.einsum(
        "te,de->td", d_logits, full_router, preferred_element_type=jnp.float32
    )
    unused_two, pull_two = jax.vjp(rms_scale, hidden, ffn_gain)
    d_hidden_norm, d_ffn_gain = pull_two(d_normed_two)
    d_hidden = out_grad + d_hidden_norm
    d_attn = d_hidden.astype(jnp.bfloat16)
    d_attended = jnp.einsum(
        "td,dj->tj", d_attn, full_out, preferred_element_type=jnp.float32
    ).astype(jnp.bfloat16)
    d_heads = lax.all_to_all(
        d_attended.reshape(token_row_count, QUERY_HEADS, HEAD_DIMENSION),
        "seq",
        split_axis=1,
        concat_axis=0,
        tiled=True,
    )
    d_query, d_key_sum, d_value_sum = attend_backward(
        head_queries, head_keys, head_values, log_total, d_heads
    )
    seq_rows = head_queries.shape[0]
    local_cols = head_queries.shape[1] * HEAD_DIMENSION
    normed_all, d_attn_all = (
        lax.all_gather(normed_one, "seq", axis=0, tiled=True),
        lax.all_gather(d_attn, "seq", axis=0, tiled=True),
    )
    query_cols = lax.dynamic_slice_in_dim(
        full_qkv, lax.axis_index("seq") * local_cols, local_cols, 1
    )
    q_head_raw = jnp.dot(normed_all, query_cols, preferred_element_type=jnp.float32).reshape(
        head_queries.shape
    )
    seq_positions = jnp.arange(seq_rows, dtype=jnp.int32)
    unused_head, pull_head = jax.vjp(
        partial(head_prepare, positions=seq_positions), q_head_raw, q_gain
    )
    send_d_query, d_q_gain = pull_head(d_query)
    d_query_tok, grad_key_token_rows, grad_value_token_rows = (
        lax.all_to_all(
            send_d_query.astype(jnp.bfloat16), "seq", split_axis=0, concat_axis=1, tiled=True
        ).astype(send_d_query.dtype),
        lax.all_to_all(
            d_key_sum.astype(jnp.bfloat16), "seq", split_axis=0, concat_axis=1, tiled=True
        ).astype(d_key_sum.dtype),
        lax.all_to_all(
            d_value_sum.astype(jnp.bfloat16), "seq", split_axis=0, concat_axis=1, tiled=True
        ).astype(d_value_sum.dtype),
    )
    grad_key_per_head = jnp.sum(
        grad_key_token_rows.reshape(token_row_count, KEY_VALUE_HEADS, -1, HEAD_DIMENSION), axis=2
    )
    grad_value_per_head = jnp.sum(
        grad_value_token_rows.reshape(token_row_count, KEY_VALUE_HEADS, -1, HEAD_DIMENSION), axis=2
    )
    unused_k, pull_k = jax.vjp(prepare, key_unnormed, k_gain)
    grad_key_unnormed, d_k_gain = pull_k(grad_key_per_head)
    d_projected = jnp.concatenate(
        [
            d_query_tok.reshape(token_row_count, QUERY_HEADS * HEAD_DIMENSION),
            grad_key_unnormed.reshape(token_row_count, KEY_VALUE_HEADS * HEAD_DIMENSION),
            grad_value_per_head.reshape(token_row_count, KEY_VALUE_HEADS * HEAD_DIMENSION),
        ],
        axis=1,
    ).astype(jnp.bfloat16)
    d_normed_one = jnp.einsum(
        "tj,dj->td", d_projected, full_qkv, preferred_element_type=jnp.float32
    )
    unused_one, pull_one = jax.vjp(rms_scale, resid_in, attn_gain)
    d_resid_norm, d_attn_gain = pull_one(d_normed_one)
    d_tokens = (d_hidden + d_resid_norm).astype(jnp.bfloat16)[None]
    rows_dev = model_width // experts
    kv_count = 2 * KEY_VALUE_HEADS * HEAD_DIMENSION
    kv_grads = d_projected[:, QUERY_HEADS * HEAD_DIMENSION :]
    first_rows = normed_one
    summed = lax.psum_scatter(
        jnp.concatenate(
            [
                jnp.einsum("tc,tj->cj", first_rows, kv_grads, preferred_element_type=jnp.float32),
                jnp.einsum("tc,te->ce", normed_two, d_logits, preferred_element_type=jnp.float32),
            ],
            axis=1,
        ),
        ("seq", "fsdp"),
        scatter_dimension=0,
        tiled=True,
    )
    d_query_low = send_d_query.reshape(seq_rows, local_cols).astype(jnp.bfloat16)
    attended_heads = mixed_heads.reshape(seq_rows, local_cols)
    normed_order = (
        normed_all.reshape(seq_rows, sequence_count, shard_count, rows_dev)
        .transpose(0, 2, 1, 3)
        .reshape(seq_rows, model_width)
    )
    d_attn_order = (
        d_attn_all.reshape(seq_rows, sequence_count, shard_count, rows_dev)
        .transpose(0, 2, 1, 3)
        .reshape(seq_rows, model_width)
    )
    first_rows = normed_order
    head_sums = lax.psum_scatter(
        jnp.concatenate(
            [
                jnp.einsum(
                    "tc,tj->cj", first_rows, d_query_low, preferred_element_type=jnp.float32
                ),
                jnp.einsum(
                    "tc,tj->cj", d_attn_order, attended_heads, preferred_element_type=jnp.float32
                ),
            ],
            axis=1,
        ).astype(jnp.bfloat16),
        "fsdp",
        scatter_dimension=0,
        tiled=True,
    ).astype(jnp.float32)
    row_sums = (
        lax.all_to_all(
            head_sums.astype(jnp.bfloat16), "seq", split_axis=0, concat_axis=1, tiled=True
        )
        .astype(head_sums.dtype)
        .reshape(rows_dev, sequence_count, 2, local_cols)
    )
    d_w_query = row_sums[:, :, 0].reshape(rows_dev, QUERY_HEADS * HEAD_DIMENSION)
    d_w_out_t = row_sums[:, :, 1].reshape(rows_dev, QUERY_HEADS * HEAD_DIMENSION)
    d_w_qkv = jnp.concatenate([d_w_query, summed[:, :kv_count]], axis=1)
    d_w_router = summed[:, kv_count:]
    d_attn_gain, d_ffn_gain, d_q_gain, d_k_gain = lax.psum(
        (d_attn_gain, d_ffn_gain, d_q_gain, d_k_gain), ("seq", "fsdp")
    )
    return (
        output[None],
        d_tokens,
        d_w_qkv,
        d_w_out_t,
        d_w_router,
        d_w_in,
        d_w_down,
        d_attn_gain,
        d_ffn_gain,
        d_q_gain,
        d_k_gain,
    )


MESH = pl.DeviceIdType.MESH
VMEM_LIMIT = 60 * 2**20


class Place:
    def __init__(self):
        seq, shard = lax.axis_index("seq"), lax.axis_index("fsdp")
        self.z, self.x = seq // 2, seq % 2
        self.y, self.c = shard // 2, shard % 2
        self.z0, self.z1 = self.z % 2, self.z // 2
        self.low, self.high = self.z == 0, self.z == 3
        self.inner = (self.z0 + self.z1) == 1
        self.me = self.block(self.z, self.x, self.y, self.c)

    def device(self, z, x, y, c):
        return (z * 2 + x, y * 2 + c)

    def block(self, z, x, y, c):
        return (z * 2 + x) * 4 + y * 2 + c

    @property
    def by_x(self):
        return self.device(self.z, 1 - self.x, self.y, self.c)

    @property
    def by_y(self):
        return self.device(self.z, self.x, 1 - self.y, self.c)

    @property
    def by_core(self):
        return self.device(self.z, self.x, self.y, 1 - self.c)

    def by_z(self, step):
        return self.device(self.z + step, self.x, self.y, self.c)

    def near(self, k):
        return [self.z, 1 + self.z0, 2 - 2 * self.z0 + self.z1, 3 - 3 * self.z1][k]

    def onward(self, k):
        return [None, 2 * self.z1 - 1, 1 - 2 * self.z1, 2 * self.z1 - 1][k]

    def far(self, k):
        return self.near(3 - k)

    def toward(self, k):
        return [1 - 2 * self.z1, 1 - 2 * self.z0, 1 - 2 * self.z1][k]

    def greet(self, sides):
        barrier = pltpu.get_barrier_semaphore()
        for side in sides:
            if side != "z":
                target = {"x": self.by_x, "y": self.by_y, "core": self.by_core}[side]
                pl.semaphore_signal(barrier, inc=1, device_id=target, device_id_type=MESH)
        count = len([side for side in sides if side != "z"])
        if "z" in sides:

            @pl.when(jnp.logical_not(self.low))
            def _():
                pl.semaphore_signal(barrier, inc=1, device_id=self.by_z(-1), device_id_type=MESH)

            @pl.when(jnp.logical_not(self.high))
            def _():
                pl.semaphore_signal(barrier, inc=1, device_id=self.by_z(1), device_id_type=MESH)

            count = count + 1 + (self.z0 + self.z1) % 2
        pl.semaphore_wait(barrier, count)


def send(source, target, send_sem, recv_sem, device):
    pltpu.make_async_remote_copy(
        src_ref=source,
        dst_ref=target,
        send_sem=send_sem,
        recv_sem=recv_sem,
        device_id=device,
        device_id_type=MESH,
    ).start()


def await_bytes(ref, sem):
    pltpu.make_async_copy(ref, ref, sem).wait()


G_Z, G_X, G_Y, G_DX, G_DY, G_C0 = 0, 1, 2, 3, 4, 5
G_KINDS = 9


def gather_steps(place, own, out, ss, rs, zs, local_sem):
    p = place
    rows = out.shape[1]
    half = rows // 2
    x, y, c = p.x, p.y, p.c

    def cols(q):
        return [
            p.block(q, x, y, c),
            p.block(q, 1 - x, y, c),
            p.block(q, x, 1 - y, c),
            p.block(q, 1 - x, 1 - y, c),
        ]

    def to_core(q, j, src=None):
        b = cols(q)[j]
        send(out.at[b] if src is None else src, out.at[b], ss.at[q, G_C0 + j], rs.at[q, G_C0 + j], p.by_core)

    def plane_out(k):
        q = p.near(k)
        b = cols(q)[0]
        if k == 0:
            src = own
            for step, there in ((1, p.high), (-1, p.low)):

                @pl.when(jnp.logical_not(there))
                def _():
                    send(src, out.at[b], zs.at[q, 0 if step > 0 else 1], rs.at[q, G_Z], p.by_z(step))

            pltpu.make_async_copy(own, out.at[b], local_sem).start()
        else:
            src = out.at[b]
            await_bytes(src, rs.at[q, G_Z])

            @pl.when(p.inner)
            def _():
                send(src, src, zs.at[q, 0], rs.at[q, G_Z], p.by_z(p.onward(k)))

        send(src, out.at[b], ss.at[q, G_X], rs.at[q, G_X], p.by_x)
        send(src, out.at[b], ss.at[q, G_Y], rs.at[q, G_Y], p.by_y)
        to_core(q, 0, src)

    def plane_turn(k):
        q = p.near(k)
        bx, by = out.at[cols(q)[1]], out.at[cols(q)[2]]
        await_bytes(bx, rs.at[q, G_X])
        first = bx.at[pl.ds(0, half)]
        send(first, first, ss.at[q, G_DY], rs.at[q, G_DY], p.by_y)
        to_core(q, 1)
        await_bytes(by, rs.at[q, G_Y])
        second = by.at[pl.ds(half, half)]
        send(second, second, ss.at[q, G_DX], rs.at[q, G_DX], p.by_x)
        to_core(q, 2)

    def plane_end(k):
        q = p.near(k)
        bd = out.at[cols(q)[3]]
        await_bytes(bd.at[pl.ds(0, half)], rs.at[q, G_DY])
        await_bytes(bd.at[pl.ds(half, half)], rs.at[q, G_DX])
        to_core(q, 3)

    def plane_core(k):
        q = p.near(k)
        for j in range(4):
            await_bytes(own, rs.at[q, G_C0 + j])

    def finish():
        piece = own.at[pl.ds(0, half)]
        for q in range(4):
            for kind in (G_X, G_Y, G_C0, G_C0 + 1, G_C0 + 2, G_C0 + 3):
                await_bytes(own, ss.at[q, kind])
            for kind in (G_DX, G_DY):
                await_bytes(piece, ss.at[q, kind])
        for there, slot in ((p.high, 0), (p.low, 1)):

            @pl.when(jnp.logical_not(there))
            def _():
                await_bytes(own, zs.at[p.z, slot])

        for k in range(1, 4):

            @pl.when(p.inner)
            def _():
                await_bytes(own, zs.at[p.near(k), 0])

    return plane_out, plane_turn, plane_end, plane_core, finish


def sum_all_parts(p, part, held, core_in, x_half, y_half, x_in, y_in, z_in, out, ls, cs, cr, ss, rs, zs, zr):
    rows, width = part.shape[1], part.shape[2]
    half = rows // 2
    x, y, c = p.x, p.y, p.c

    def columns(q):
        return [(q, x, y), (q, 1 - x, y), (q, x, 1 - y), (q, 1 - x, 1 - y)]

    def start():
        for k in range(4):
            q = p.far(k)
            for j, (zz, xx, yy) in reversed(list(enumerate(columns(q)))):
                send(
                    part.at[p.block(zz, xx, yy, 1 - c)],
                    core_in.at[q * 4 + j],
                    cs.at[q, j],
                    cr.at[q, j],
                    p.by_core,
                )
                pltpu.make_async_copy(
                    part.at[p.block(zz, xx, yy, c)], held.at[q * 4 + j], ls.at[q, j]
                ).start()

    add = add_rows

    def plane_core(k, js=(3, 1, 2, 0)):
        q = p.far(k)
        for j in js:
            slot = q * 4 + j
            await_bytes(held.at[slot], ls.at[q, j])
            await_bytes(core_in.at[slot], cr.at[q, j])
            add(held.at[slot], core_in.at[slot], rows)
            if j == 3:
                send(held.at[slot, pl.ds(0, half)], y_half.at[q], ss.at[q, 0], rs.at[q, 0], p.by_y)
                send(held.at[slot, pl.ds(half, half)], x_half.at[q], ss.at[q, 1], rs.at[q, 1], p.by_x)

    def plane_turn(k):
        q = p.far(k)
        await_bytes(y_half.at[q], rs.at[q, 0])
        add(held.at[q * 4 + 1, pl.ds(0, half)], y_half.at[q], half)
        send(held.at[q * 4 + 1], x_in.at[q], ss.at[q, 2], rs.at[q, 2], p.by_x)
        await_bytes(x_half.at[q], rs.at[q, 1])
        add(held.at[q * 4 + 2, pl.ds(half, half)], x_half.at[q], half)
        send(held.at[q * 4 + 2], y_in.at[q], ss.at[q, 3], rs.at[q, 3], p.by_y)

    def plane_end(k):
        q = p.far(k)
        mine = held.at[q * 4]
        await_bytes(x_in.at[q], rs.at[q, 2])
        add(mine, x_in.at[q], rows)
        await_bytes(y_in.at[q], rs.at[q, 3])
        add(mine, y_in.at[q], rows)
        if k < 3:
            step = p.toward(k)
            slot = (1 - step) // 2

            @pl.when(p.inner)
            def _():
                await_bytes(z_in.at[slot, q], zr.at[slot, q])
                add(mine, z_in.at[slot, q], rows)

            send(mine, z_in.at[slot, q], zs.at[k], zr.at[slot, q], p.by_z(step))
        else:
            for slot, there in ((0, p.low), (1, p.high)):

                @pl.when(jnp.logical_not(there))
                def _():
                    await_bytes(z_in.at[slot, q], zr.at[slot, q])
                    add(mine, z_in.at[slot, q], rows)

            out[...] = mine[...]

    def finish():
        whole, piece = x_in.at[0], x_half.at[0]
        for q in range(4):
            for j in range(4):
                await_bytes(whole, cs.at[q, j])
            for kind in (0, 1):
                await_bytes(piece, ss.at[q, kind])
            for kind in (2, 3):
                await_bytes(whole, ss.at[q, kind])
        for k in range(3):
            await_bytes(whole, zs.at[k])

    return start, plane_core, plane_turn, plane_end, finish


def sum_all_kernel(
    part, both, rows_in, d_gate_up, inner, d_expert,
    out, pair, d_w_in, d_w_down,
    both_held, both_in, left, product, pair_sems, load_sems, left_sems, product_sems, *scratch,
):
    p = Place()
    p.greet(("x", "y", "core", "z"))
    start, plane_core, plane_turn, plane_end, finish = sum_all_parts(p, part, *scratch[:7], out, *scratch[7:])
    rows = both.shape[3]

    def pair_sum(first):
        for s in (first, first + 1):
            for y in range(2):
                add_rows(both_held.at[s, y], both_in.at[s, y], rows)

    def right_load(source, i):
        width = source.shape[3]
        return pltpu.make_async_copy(source, both_in.at[:, :, :, pl.ds(0, width)], load_sems.at[i])

    def left_load(source, i, slot):
        cols = pl.ds(pl.multiple_of(i * TILE, TILE), TILE)
        return pltpu.make_async_copy(source.at[:, cols], left.at[slot], left_sems.at[slot])

    def product_store(target, i, slot):
        at = pl.ds(pl.multiple_of(i * TILE, TILE), TILE)
        piece = product.at[slot, :, pl.ds(0, target.shape[1])]
        return pltpu.make_async_copy(piece, target.at[at], product_sems.at[slot])

    def tiles(source, target, first, last):
        count, wide = source.shape[1] // TILE, target.shape[1]

        @pl.loop(first, last)
        def _(i):
            slot = i % 2
            left_load(source, i, slot).wait()

            @pl.when(i + 1 < count)
            def _():
                left_load(source, i + 1, 1 - slot).start()

            @pl.when(i >= 2)
            def _():
                product_store(target, i - 2, slot).wait()

            right = both_in[:, :, :, :wide].reshape(source.shape[0], wide)
            product[slot, :, :wide] = mxu(left[slot], right, TN).astype(product.dtype)
            product_store(target, i, slot).start()

    def tiles_end(source, target):
        count = source.shape[1] // TILE
        for i in (count - 2, count - 1):
            product_store(target, i, i % 2).wait()

    start()
    send(both.at[:, :, 1 - p.c], both_in, pair_sems.at[0], pair_sems.at[1], p.by_core)
    pltpu.make_async_copy(both.at[:, :, p.c], both_held, pair_sems.at[2]).start()
    plane_core(0)
    plane_core(1)
    plane_turn(0)
    await_bytes(both_held, pair_sems.at[2])
    await_bytes(both_in, pair_sems.at[1])
    for first in (0, 2, 4, 6):
        pair_sum(first)
    pltpu.make_async_copy(both_held, pair, pair_sems.at[2]).start()
    right_load(d_gate_up, 0).start()
    left_load(rows_in, 0, 0).start()
    plane_core(2)
    plane_turn(1)
    plane_end(0)
    plane_core(3)
    right_load(d_gate_up, 0).wait()
    tiles(rows_in, d_w_in, 0, 2)
    plane_turn(2)
    tiles(rows_in, d_w_in, 2, 4)
    plane_end(1)
    tiles(rows_in, d_w_in, 4, 6)
    plane_turn(3)
    tiles(rows_in, d_w_in, 6, 8)
    right_load(d_expert, 1).start()
    tiles_end(rows_in, d_w_in)
    left_load(inner, 0, 0).start()
    plane_end(2)
    right_load(d_expert, 1).wait()
    tiles(inner, d_w_down, 0, 3)
    plane_end(3)
    tiles_end(inner, d_w_down)
    finish()
    await_bytes(both_held, pair_sems.at[0])
    pltpu.make_async_copy(both_held, pair, pair_sems.at[2]).wait()


def sum_all_scratch(rows, width):
    dma = pltpu.SemaphoreType.DMA
    bf16 = jnp.bfloat16
    return [
        pltpu.VMEM((16, rows, width), bf16),
        pltpu.VMEM((16, rows, width), bf16),
        pltpu.VMEM((4, rows // 2, width), bf16),
        pltpu.VMEM((4, rows // 2, width), bf16),
        pltpu.VMEM((4, rows, width), bf16),
        pltpu.VMEM((4, rows, width), bf16),
        pltpu.VMEM((2, 4, rows, width), bf16),
        dma((4, 4)),
        dma((4, 4)),
        dma((4, 4)),
        dma((4, 4)),
        dma((4, 4)),
        dma((3,)),
        dma((2, 4)),
    ]


def sum_all(part, both, rows_in, d_gate_up, inner, d_expert, collective_id):
    blocks, rows, width = part.shape
    both = both.reshape(blocks // 4, 2, 2, rows, -1)
    pair = (blocks // 4, 2, rows, both.shape[4])
    anywhere = pl.BlockSpec(memory_space=pl.ANY)
    return pl.pallas_call(
        sum_all_kernel,
        out_shape=[
            jax.ShapeDtypeStruct((rows, width), part.dtype),
            jax.ShapeDtypeStruct(pair, both.dtype),
            jax.ShapeDtypeStruct((rows_in.shape[1], d_gate_up.shape[1]), both.dtype),
            jax.ShapeDtypeStruct((inner.shape[1], d_expert.shape[1]), both.dtype),
        ],
        in_specs=[anywhere] * 6,
        out_specs=[pl.BlockSpec(memory_space=pltpu.VMEM)] + [anywhere] * 3,
        scratch_shapes=[
            pltpu.VMEM(pair, both.dtype),
            pltpu.VMEM(pair, both.dtype),
            pltpu.VMEM((2, rows_in.shape[0], TILE), both.dtype),
            pltpu.VMEM((2, TILE, d_expert.shape[1]), both.dtype),
            pltpu.SemaphoreType.DMA((3,)),
            pltpu.SemaphoreType.DMA((2,)),
            pltpu.SemaphoreType.DMA((2,)),
            pltpu.SemaphoreType.DMA((2,)),
            *sum_all_scratch(rows, width),
        ],
        compiler_params=pltpu.CompilerParams(
            collective_id=collective_id, has_side_effects=True, vmem_limit_bytes=VMEM_LIMIT
        ),
        name="sum_all",
    )(
        part,
        both,
        rows_in,
        d_gate_up.reshape(*pair[:3], -1),
        inner,
        d_expert.reshape(*pair[:3], -1),
    )


def add_rows(target, source, count, chunk=32):
    @pl.loop(0, count // chunk)
    def _(i):
        at = pl.ds(pl.multiple_of(i * chunk, chunk), chunk)
        target[at, :] = target[at, :] + source[at, :]


def seq_peer(p, d):
    return ((p.z * 2 + p.x + d) % 8, p.y * 2 + p.c)


def greet_seq(p, sides=("y", "core")):
    barrier = pltpu.get_barrier_semaphore()
    for d in range(1, 8):
        pl.semaphore_signal(barrier, inc=1, device_id=seq_peer(p, d), device_id_type=MESH)
    for side in sides:
        target = {"y": p.by_y, "core": p.by_core}[side]
        pl.semaphore_signal(barrier, inc=1, device_id=target, device_id_type=MESH)
    pl.semaphore_wait(barrier, 7 + len(sides))


NT = (((1,), (1,)), ((), ()))
TILE = 256
WIDE = 512


def mxu(a, b, dims=(((1,), (0,)), ((), ()))):
    return lax.dot_general(a, b, dims, preferred_element_type=jnp.float32)


def experts_kernel(
    own, cot_all, w_in_hbm, w_down_hbm,
    rows_all, out_part, d_part, x_all, d_expert_all, inner_all, d_gate_up_all,
    w_in, w_down, row_buf, cot_buf, pick, pick_t, gates, d_gates, x, cot, d_expert,
    by_d_gate, by_d_up, inner, d_gate_up, held, out_stage, d_stage,
    ss, rs, zs, local_sem, load_sems, store_sems,
):
    p = Place()
    bf16, f32 = jnp.bfloat16, jnp.float32
    width = cot_all.shape[2]
    blocks = 8
    slots = gates.shape[0]
    capacity = slots // blocks
    tokens = row_buf.shape[2]
    group = 4
    experts = rows_all.shape[0]
    p.greet(("x", "y", "core", "z"))
    plane_out, plane_turn, plane_end, plane_core, finish = gather_steps(
        p, own, rows_all, ss, rs, zs, local_sem
    )

    def weights(start):
        for i, (src, dst) in enumerate(((w_in_hbm, w_in), (w_down_hbm, w_down))):
            copy = pltpu.make_async_copy(src, dst, load_sems.at[i])
            copy.start() if start else copy.wait()

    def cot_load(k):
        return pltpu.make_async_copy(
            cot_all.at[pl.ds(p.near(k) * blocks, blocks)], cot_buf.at[k % 2], load_sems.at[2 + k]
        )

    def row_load(k):
        return pltpu.make_async_copy(
            rows_all.at[pl.ds(p.near(k) * blocks, blocks)], row_buf.at[k % 2], load_sems.at[6 + k]
        )

    def arrived(k):
        plane_core(k)
        if k == 0:
            pltpu.make_async_copy(own, rows_all.at[p.me], local_sem).wait()
        row_load(k).start()

    at_slot = {}

    def store(k, i, src, dst):
        if (k, i) not in at_slot:
            at_slot[k, i] = pltpu.make_async_copy(src, dst, store_sems.at[i, k % 2])
        return at_slot[k, i]

    def stores(k):
        q = p.near(k)
        at = pl.ds(q * slots, slots)
        plane = pl.ds(q * blocks, blocks)
        return [
            (x, x_all.at[at]),
            (d_expert, d_expert_all.at[at]),
            (inner, inner_all.at[at]),
            (d_gate_up, d_gate_up_all.at[at]),
            (out_stage, out_part.at[plane]),
            (d_stage, d_part.at[plane]),
        ]

    def put(k, i):
        store(k, i, *stores(k)[i]).start()

    def free(k, i):
        if k > 0:
            store(k - 1, i, *stores(k - 1)[i]).wait()

    def pick_rows(k):
        lane = lax.broadcasted_iota(jnp.int32, (8, 128), 1)
        line = lax.broadcasted_iota(jnp.int32, (8, 128), 0)
        select = jnp.where((lane == line * experts + p.me) & (line < 3), 1.0, 0.0).astype(bf16)
        slot_id = lax.broadcasted_iota(jnp.int32, (capacity, tokens), 0).astype(f32) + 1.0
        rows, cots = row_buf.at[k % 2], cot_buf.at[k % 2]
        lines = mxu(select, rows[:, :, width:].reshape(blocks * tokens, 128), NT)
        for j in range(blocks):
            g, i = j // group, j % group
            mine = lines[:, j * tokens : (j + 1) * tokens]
            chosen = jnp.where(mine[2:3] == slot_id, 1.0, 0.0)
            gate = jnp.sum(chosen * (mine[0:1] + mine[1:2]), axis=1, keepdims=True)
            gates[j * capacity : (j + 1) * capacity, :] = jnp.broadcast_to(gate, (capacity, 128))
            lead = [jnp.zeros((capacity, tokens), bf16)] * i
            tail = [jnp.zeros((capacity, tokens), bf16)] * (group - 1 - i)
            pick[g, i * capacity : (i + 1) * capacity, :] = jnp.concatenate(
                lead + [chosen.astype(bf16)] + tail, axis=1
            )
            lead = [jnp.zeros((tokens, capacity), f32)] * i
            tail = [jnp.zeros((tokens, capacity), f32)] * (group - 1 - i)
            pick_t[g, i * tokens : (i + 1) * tokens, :] = jnp.concatenate(
                lead + [chosen.T] + tail, axis=1
            ).astype(bf16)
        for g in range(blocks // group):
            at = pl.ds(g * group * capacity, group * capacity)
            which = pl.ds(g * group, group)

            @pl.loop(0, width // WIDE)
            def _(n):
                cols = pl.ds(pl.multiple_of(n * WIDE, WIDE), WIDE)
                row_tile = rows[which, :, cols].reshape(group * tokens, WIDE)
                x[at, cols] = mxu(pick[g], row_tile).astype(bf16)
                cot_tile = cots[which, :, cols].reshape(group * tokens, WIDE)
                picked = mxu(pick[g], cot_tile)
                cot[at, cols] = picked.astype(bf16)
                scale = jnp.concatenate([gates[at, :]] * (WIDE // 128), axis=1)
                d_expert[at, cols] = (scale * picked).astype(bf16)

    def up(k):
        ff = inner.shape[1]

        @pl.loop(0, ff // TILE)
        def _(n):
            cols = pl.ds(pl.multiple_of(n * TILE, TILE), TILE)
            gate = mxu(x[...], w_in[:, cols])
            raised = mxu(x[...], w_in[:, pl.ds(pl.multiple_of(ff + n * TILE, TILE), TILE)])
            sig = jax.nn.sigmoid(gate)
            silu = gate * sig
            inner[:, cols] = (silu * raised).astype(bf16)
            by_d_up[:, cols] = silu
            by_d_gate[:, cols] = raised * sig * (1.0 + gate * (1.0 - sig))

    def d_up(k):
        ff = inner.shape[1]

        @pl.loop(0, ff // TILE)
        def _(n):
            cols = pl.ds(pl.multiple_of(n * TILE, TILE), TILE)
            d_inner = mxu(d_expert[...], w_down[cols, :], NT)
            d_gate_up[:, cols] = (d_inner * by_d_gate[:, cols]).astype(bf16)
            d_gate_up[:, pl.ds(pl.multiple_of(ff + n * TILE, TILE), TILE)] = (
                d_inner * by_d_up[:, cols]
            ).astype(bf16)

    def spread(stage):
        @pl.loop(0, width // WIDE)
        def _(n):
            cols = pl.ds(pl.multiple_of(n * WIDE, WIDE), WIDE)
            for g in range(blocks // group):
                part = held[g * group * capacity : (g + 1) * group * capacity, cols]
                result = mxu(pick_t[g], part).astype(bf16)
                stage[g * group : (g + 1) * group, :, cols] = result.reshape(group, tokens, WIDE)

    def down(k):
        d_gates[...] = jnp.zeros_like(d_gates)

        @pl.loop(0, width // TILE)
        def _(n):
            cols = pl.ds(pl.multiple_of(n * TILE, TILE), TILE)
            result = mxu(inner[...], w_down[:, cols]).astype(bf16).astype(f32)
            product = result * cot[:, cols].astype(f32)
            total = product[:, :128]
            for j in range(1, TILE // 128):
                total = total + product[:, j * 128 : (j + 1) * 128]
            d_gates[...] += total
            scale = jnp.concatenate([gates[...]] * (TILE // 128), axis=1)
            held[:, cols] = (scale * result).astype(bf16)

    def d_down(k):
        total = jnp.sum(d_gates[...], axis=1, keepdims=True)
        high = total.astype(bf16).astype(f32)
        lane = lax.broadcasted_iota(jnp.int32, (slots, 128), 1)
        info = jnp.where(lane == p.me, high, jnp.where(lane == experts + p.me, total - high, 0.0))
        info = info.astype(bf16)
        for g in range(blocks // group):
            result = mxu(pick_t[g], info[g * group * capacity : (g + 1) * group * capacity])
            d_stage[g * group : (g + 1) * group, :, width:] = result.astype(bf16).reshape(
                group, tokens, 128
            )

        @pl.loop(0, width // TILE)
        def _(n):
            cols = pl.ds(pl.multiple_of(n * TILE, TILE), TILE)
            held[:, cols] = mxu(d_gate_up[...], w_in[cols, :], NT).astype(bf16)

    plane_out(0)
    weights(True)
    cot_load(0).start()
    plane_turn(0)
    plane_out(1)
    plane_end(0)
    arrived(0)
    weights(False)
    after = {
        (0, 1): ((plane_turn, 1), (plane_out, 2)),
        (0, 3): ((plane_end, 1),),
        (0, 5): ((arrived, 1),),
        (1, 0): ((plane_turn, 2), (plane_out, 3)),
        (1, 3): ((plane_end, 2),),
        (1, 5): ((arrived, 2),),
        (2, 0): ((plane_turn, 3),),
        (2, 3): ((plane_end, 3),),
        (2, 5): ((arrived, 3),),
    }
    for k in range(4):

        def service(i):
            for step, plane in after.get((k, i), ()):
                step(plane)

        row_load(k).wait()
        cot_load(k).wait()
        if k < 3:
            cot_load(k + 1).start()
        free(k, 0)
        free(k, 1)
        pick_rows(k)
        put(k, 0)
        put(k, 1)
        service(0)
        free(k, 2)
        up(k)
        put(k, 2)
        service(1)
        free(k, 3)
        d_up(k)
        put(k, 3)
        service(2)
        free(k, 4)
        down(k)
        service(3)
        spread(out_stage)
        put(k, 4)
        service(4)
        free(k, 5)
        d_down(k)
        service(5)
        spread(d_stage)
        put(k, 5)
    for i in range(6):
        free(4, i)
    finish()


def experts_gathered(own, cot_all, w_in, w_down, capacity, collective_id):
    tokens, wide = own.shape
    experts, _, width = cot_all.shape
    ff = w_down.shape[0]
    slots = 8 * capacity
    dma = pltpu.SemaphoreType.DMA
    bf16, f32 = jnp.bfloat16, jnp.float32
    anywhere = pl.BlockSpec(memory_space=pl.ANY)

    def array(*shape):
        return jax.ShapeDtypeStruct(shape, bf16)

    return pl.pallas_call(
        experts_kernel,
        out_shape=[
            array(experts, tokens, wide),
            array(experts, tokens, width),
            array(experts, tokens, wide),
            array(experts * capacity, width),
            array(experts * capacity, width),
            array(experts * capacity, ff),
            array(experts * capacity, 2 * ff),
        ],
        in_specs=[anywhere] * 4,
        out_specs=[anywhere] * 7,
        scratch_shapes=[
            pltpu.VMEM(w_in.shape, bf16),
            pltpu.VMEM(w_down.shape, bf16),
            pltpu.VMEM((2, 8, tokens, wide), bf16),
            pltpu.VMEM((2, 8, tokens, width), bf16),
            pltpu.VMEM((2, 4 * capacity, 4 * tokens), bf16),
            pltpu.VMEM((2, 4 * tokens, 4 * capacity), bf16),
            pltpu.VMEM((slots, 128), f32),
            pltpu.VMEM((slots, 128), f32),
            pltpu.VMEM((slots, width), bf16),
            pltpu.VMEM((slots, width), bf16),
            pltpu.VMEM((slots, width), bf16),
            pltpu.VMEM((slots, ff), f32),
            pltpu.VMEM((slots, ff), f32),
            pltpu.VMEM((slots, ff), bf16),
            pltpu.VMEM((slots, 2 * ff), bf16),
            pltpu.VMEM((slots, width), bf16),
            pltpu.VMEM((8, tokens, width), bf16),
            pltpu.VMEM((8, tokens, wide), bf16),
            dma((4, G_KINDS)),
            dma((4, G_KINDS)),
            dma((4, 2)),
            dma,
            dma((10,)),
            dma((6, 2)),
        ],
        compiler_params=pltpu.CompilerParams(
            collective_id=collective_id, has_side_effects=True, vmem_limit_bytes=VMEM_LIMIT
        ),
        name="experts",
    )(own, cot_all, w_in, w_down)


TN = (((0,), (0,)), ((), ()))


def back_kernel(
    own, pair, rows_all, columns_hbm, normed_hbm, queries, keys, values, attended,
    q_raw, k_raw, cosine, sine, q_gain, k_gain, attn_gain, gains, tokens, d_hidden,
    d_tokens, cols_out, gains_out, mixture,
    d_attn, columns, normed, d_normed, d_heads, d_query, d_key, d_value, d_proj, logits, q_sum, k_sum,
    held, x_in, y_in, z_in, g_send, g_in, x_two, z_two, c_core, c_y,
    gs, gr, gz, load_sems, local_sem, hs, ys, yr, xs, xr, zs, zr, ts, tr,
    normed_sems, free, xs2, xr2, zs2, zr2, cs, cr, cys, cyr, as_, ar,
):
    p = Place()
    bf16, f32 = jnp.bfloat16, jnp.float32
    columns_z = [p.device((p.z + d) % 4, p.x, p.y, p.c) for d in (1, 2, 3)]
    greet_seq(p)
    rows, wide = own.shape
    length, head_cols = queries.shape
    heads = head_cols // HEAD_DIMENSION
    width = d_normed.shape[2]
    proj_cols = d_proj.shape[1]
    plane_rows = 2 * rows
    score_scale = 1.0 / math.sqrt(HEAD_DIMENSION)
    place, shard = p.z * 2 + p.x, p.y * 2 + p.c

    def rows_at(q, x):
        return d_attn.at[q * 2 + x]

    def gather_out(k):
        q = p.near(k)
        there = rows_at(q, p.x)
        if k == 0:
            src = own
            for step, end in ((1, p.high), (-1, p.low)):

                @pl.when(jnp.logical_not(end))
                def _():
                    send(src, there, gz.at[q, 0 if step > 0 else 1], gr.at[q, 0], p.by_z(step))

            pltpu.make_async_copy(own, there, local_sem).start()
        else:
            src = there
            await_bytes(src, gr.at[q, 0])

            @pl.when(p.inner)
            def _():
                send(src, src, gz.at[q, 0], gr.at[q, 0], p.by_z(p.onward(k)))

        send(src, there, gs.at[q], gr.at[q, 1], p.by_x)

    def gather_in(k):
        if k == 0:
            pltpu.make_async_copy(own, rows_at(p.z, p.x), local_sem).wait()
        await_bytes(own, gr.at[p.near(k), 1])

    def at_pair(q, x, y):
        return pair.at[q * 4 + x * 2 + y]

    def sum_send(k):
        q = p.far(k)
        for j, x in ((1, 1 - p.x), (0, p.x)):
            i = q * 2 + j
            send(at_pair(q, x, 1 - p.y), y_in.at[k % 2 * 2 + j], ys.at[i], yr.at[i], p.by_y)

    def sum_start():
        sum_send(0)
        sum_send(1)
        for k in range(4):
            q = p.far(k)
            for j, x in ((1, 1 - p.x), (0, p.x)):
                pltpu.make_async_copy(at_pair(q, x, p.y), held.at[q * 2 + j], hs.at[q * 2 + j]).start()

    def sum_turn(k):
        q = p.far(k)
        for j in (1, 0):
            slot = q * 2 + j
            landed = y_in.at[k % 2 * 2 + j]
            await_bytes(held.at[slot], hs.at[slot])
            await_bytes(landed, yr.at[slot])
            add_rows(held.at[slot], landed, rows)
            if j == 1:
                send(held.at[slot], x_in.at[q], xs.at[q], xr.at[q], p.by_x)
        if k < 2:
            pl.semaphore_signal(free, inc=1, device_id=p.by_y, device_id_type=MESH)
            pl.semaphore_wait(free, 1)
            sum_send(k + 2)

    def line_sum(k, mine, landed, sends, arrivals):
        q = p.far(k)
        if k < 3:
            step = p.toward(k)
            slot, hops = (1 - step) // 2, (q - p.z) * step

            @pl.when(p.inner)
            def _():
                await_bytes(landed.at[slot, hops], arrivals.at[slot, hops])
                add_rows(mine, landed.at[slot, hops], rows)

            send(mine, landed.at[slot, hops - 1], sends.at[k], arrivals.at[slot, hops - 1], p.by_z(step))
        else:
            for slot, there in ((0, p.low), (1, p.high)):

                @pl.when(jnp.logical_not(there))
                def _():
                    await_bytes(landed.at[slot, 0], arrivals.at[slot, 0])
                    add_rows(mine, landed.at[slot, 0], rows)

    def sum_end(k):
        q = p.far(k)
        mine = held.at[q * 2]
        await_bytes(x_in.at[q], xr.at[q])
        add_rows(mine, x_in.at[q], rows)
        line_sum(k, mine, z_in, zs, zr)
        if k == 3:
            mixture[...] = mine[...]

    def two_start(*steps):
        for k in steps:
            q = p.far(k)
            send(d_normed.at[q * 2 + 1 - p.x], x_two.at[q], xs2.at[q], xr2.at[q], p.by_x)

    def two_end(k):
        q = p.far(k)
        mine = d_normed.at[q * 2 + p.x]
        await_bytes(x_two.at[q], xr2.at[q])
        add_rows(mine, x_two.at[q], rows)
        line_sum(k, mine, z_two, zs2, zr2)

    piece_rows = c_y.shape[1]
    order = [(place + d) % 8 for d in range(1, 9)]

    def cols_start():
        for turn, side in ((0, 1 - p.y), (1, p.y)):
            send(columns.at[:, side, 1 - p.c], c_core.at[turn], cs.at[turn], cr.at[turn], p.by_core)

    def cols_core():
        for turn, side in ((0, 1 - p.y), (1, p.y)):
            await_bytes(c_core.at[turn], cr.at[turn])
            for s in order:
                add_rows(columns.at[s, side, p.c], c_core.at[turn, s], piece_rows)
                if turn == 0:
                    send(columns.at[s, side, p.c], c_y.at[s], cys.at[s], cyr.at[s], p.by_y)

    def cols_turn(*steps):
        for i in steps:
            s = order[i]
            mine = columns.at[s, p.y, p.c]
            await_bytes(c_y.at[s], cyr.at[s])
            add_rows(mine, c_y.at[s], piece_rows)
            if i < 7:
                send(mine, cols_out.at[place], as_.at[i], ar.at[i], seq_peer(p, i + 1))
            else:
                pltpu.make_async_copy(mine, cols_out.at[place], as_.at[7]).start()

    def norm_back():
        mine = d_normed.at[p.z * 2 + p.x]
        chunk = 16

        @pl.loop(0, rows // chunk)
        def _(i):
            at = pl.ds(pl.multiple_of(i * chunk, chunk), chunk)
            d_out = mine[at, :].astype(f32)
            x = tokens[at, :].astype(f32)
            scale = lax.rsqrt(jnp.mean(x * x, axis=-1, keepdims=True) + EPS)
            u = d_out * attn_gain[...]
            dot = jnp.mean(u * x, axis=-1, keepdims=True)
            d_x = scale * u - x * (scale * scale * scale * dot)
            d_tokens[at, :] = (d_hidden[at, :] + d_x).astype(d_tokens.dtype)

    def attention(q):
        row_start = pl.multiple_of(q * plane_rows, plane_rows)
        at = pl.ds(row_start, plane_rows)

        @pl.loop(0, head_cols // TILE)
        def _(n):
            cols = pl.ds(pl.multiple_of(n * TILE, TILE), TILE)
            grad = d_attn[pl.ds(q * 2, 2), :, :width].reshape(plane_rows, width)
            weight_cols = pl.ds(pl.multiple_of(proj_cols + n * TILE, TILE), TILE)
            weight = columns[..., weight_cols].reshape(width, TILE)
            d_heads[at, cols] = mxu(grad, weight).astype(bf16)

        def block(count):
            key, value = keys[:count], values[:count]
            row_pos = row_start + lax.broadcasted_iota(jnp.int32, (plane_rows, count), 0)
            allowed = lax.broadcasted_iota(jnp.int32, (plane_rows, count), 1) <= row_pos

            @pl.loop(0, heads)
            def _(h):
                cols = pl.ds(pl.multiple_of(h * HEAD_DIMENSION, HEAD_DIMENSION), HEAD_DIMENSION)
                query, d_out = queries[at, cols], d_heads[at, cols]
                scores = jnp.where(allowed, mxu(query, key, NT) * score_scale, -1e30)
                raised = jnp.exp(scores - jnp.max(scores, axis=-1, keepdims=True))
                prob = raised / jnp.sum(raised, axis=-1, keepdims=True)
                d_prob = mxu(d_out, value, NT)
                delta = jnp.sum(prob * d_prob, axis=-1, keepdims=True)
                d_scores = (prob * (d_prob - delta)).astype(bf16)
                d_query[at, cols] = mxu(d_scores, key) * score_scale
                d_key[:count] += mxu(d_scores, query, TN) * score_scale
                d_value[:count] += mxu(prob.astype(bf16), d_out, TN)

        half = length // 2

        @pl.when(q < 2)
        def _():
            block(half)

        @pl.when(q >= 2)
        def _():
            block(length)

    def unrotate(grad, at):
        swapped = jnp.concatenate(
            [grad[:, HEAD_DIMENSION // 2 :], grad[:, : HEAD_DIMENSION // 2]], axis=1
        )
        return grad * cosine[at, :] + swapped * sine[at, :]

    def raw_grads():
        q_sum[...] = jnp.zeros_like(q_sum)
        k_sum[...] = jnp.zeros_like(k_sum)

        def one(grad, raw, gain, total, at):
            turned = unrotate(grad, at)
            scale = lax.rsqrt(jnp.mean(raw * raw, axis=-1, keepdims=True) + EPS)
            total[...] += jnp.sum((turned * raw * scale).reshape(-1, 8, HEAD_DIMENSION), axis=0)
            u = turned * gain[...]
            dot = jnp.mean(u * raw, axis=-1, keepdims=True)
            return (scale * u - raw * (scale * scale * scale * dot)).astype(bf16)

        chunk = 128

        @pl.loop(0, length // chunk)
        def _(i):
            at = pl.ds(pl.multiple_of(i * chunk, chunk), chunk)
            for h in range(heads):
                cols = slice(h * HEAD_DIMENSION, (h + 1) * HEAD_DIMENSION)
                d_proj[at, cols] = one(d_query[at, cols], q_raw[at, cols], q_gain, q_sum, at)
            d_proj[at, head_cols : head_cols + HEAD_DIMENSION] = one(
                d_key[at, :], k_raw[at, :], k_gain, k_sum, at
            )
            d_proj[at, head_cols + HEAD_DIMENSION :] = d_value[at, :].astype(bf16)

        g_send[0] = gains[...]
        g_send[0, 2:3, :HEAD_DIMENSION] = jnp.sum(q_sum[...], axis=0, keepdims=True)
        g_send[0, 2:3, HEAD_DIMENSION : 2 * HEAD_DIMENSION] = jnp.sum(
            k_sum[...], axis=0, keepdims=True
        )

    def normed_load(n, slot):
        cols = pl.ds(pl.multiple_of(n * TILE, TILE), TILE)
        return pltpu.make_async_copy(normed_hbm.at[:, cols], normed.at[slot], normed_sems.at[slot])

    def normed_grads():
        @pl.loop(0, width // TILE)
        def _(n):
            cols = pl.ds(pl.multiple_of(n * TILE, TILE), TILE)
            slot = n % 2
            normed_load(n, slot).wait()

            @pl.when(n + 1 < width // TILE)
            def _():
                normed_load(n + 1, 1 - slot).start()

            weight = columns[n, :, :, :, :proj_cols].reshape(TILE, proj_cols)
            part = mxu(d_proj[...], weight, NT)
            d_normed[:, :, cols] = part.astype(bf16).reshape(length // rows, rows, TILE)
            total = jnp.sum(part * normed[slot].astype(f32), axis=0, keepdims=True)
            g_send[0, 0:1, cols] = total / attn_gain[:, cols]
            grad = mxu(normed[slot], d_proj[...], TN).astype(bf16)
            columns[n, :, :, :, :proj_cols] = grad.reshape(2, 2, -1, proj_cols)

    def gains_pass(t, target):
        send(g_send.at[t], g_in.at[t], ts.at[t], tr.at[t], target)

    def gains_take(t):
        await_bytes(g_in.at[t], tr.at[t])
        g_send[t + 1] = g_send[t] + g_in[t]

    def gains_z_pass():
        g_in[2 + p.z] = g_send[2]
        for d, target in enumerate(columns_z):
            send(g_send.at[2], g_in.at[2 + p.z], ts.at[2 + d], tr.at[2 + d], target)

    def gains_z_take():
        for d in range(3):
            await_bytes(g_in.at[0], tr.at[2 + d])
        g_send[3] = g_in[2] + g_in[3] + g_in[4] + g_in[5]

    def column_grads(value, first, count):
        @pl.loop(0, width // TILE)
        def _(n):
            cols = pl.ds(pl.multiple_of(n * TILE, TILE), TILE)
            part = d_attn[:, :, cols].reshape(length, TILE)
            grad = mxu(part, value[...], TN).astype(bf16)
            columns[n, :, :, :, first : first + count] = grad.reshape(2, 2, -1, count)

    loads = [
        pltpu.make_async_copy(columns_hbm, columns, load_sems.at[0]),
        pltpu.make_async_copy(rows_all.at[:, shard], d_attn, load_sems.at[1]),
    ]
    gather_out(0)
    loads[0].start()
    normed_load(0, 0).start()
    sum_start()
    d_key[...] = jnp.zeros_like(d_key)
    d_value[...] = jnp.zeros_like(d_value)
    loads[0].wait()
    gather_in(0)
    gather_out(1)
    attention(p.near(0))
    gather_out(2)
    gather_in(1)
    attention(p.near(1))
    sum_turn(0)
    gather_out(3)
    gather_in(2)
    attention(p.near(2))
    sum_end(0)
    sum_turn(1)
    gather_in(3)
    attention(p.near(3))
    raw_grads()
    sum_end(1)
    normed_grads()
    gains_pass(0, p.by_core)
    column_grads(attended, proj_cols, head_cols)
    gains_take(0)
    gains_pass(1, p.by_x)
    two_start(0, 1)
    line = lax.broadcasted_iota(jnp.int32, (128, 128), 0)
    lane = lax.broadcasted_iota(jnp.int32, (128, 128), 1)
    router_cols = rows_all.shape[0] * rows_all.shape[1] // 8
    mine = (line == lane + place * router_cols) & (lane < router_cols)
    select = jnp.where(mine, 1.0, 0.0).astype(bf16)
    logits[...] = mxu(d_attn[:, :, width:].reshape(length, 128), select).astype(bf16)
    for q in range(4):
        await_bytes(own, gs.at[q])
    for there, slot in ((p.high, 0), (p.low, 1)):

        @pl.when(jnp.logical_not(there))
        def _():
            await_bytes(own, gz.at[p.z, slot])

    for k in range(1, 4):

        @pl.when(p.inner)
        def _():
            await_bytes(own, gz.at[p.near(k), 0])

    loads[1].start()
    loads[1].wait()
    column_grads(logits, proj_cols + head_cols, 128)
    cols_start()
    gains_take(1)
    gains_z_pass()
    sum_turn(2)
    two_start(2, 3)
    cols_core()
    two_end(0)
    sum_turn(3)
    gains_z_take()
    send(g_send.at[3], g_in.at[6], ts.at[5], tr.at[5], p.by_y)
    two_end(1)
    cols_turn(0, 1)
    sum_end(2)
    cols_turn(2, 3, 4, 5)
    two_end(2)
    cols_turn(6, 7)
    two_end(3)
    norm_back()
    sum_end(3)
    await_bytes(g_in.at[6], tr.at[5])
    gains_out[...] = g_send[3] + g_in[6]
    for t in range(6):
        await_bytes(g_in.at[0], ts.at[t])
    piece = x_in.at[0]
    for i in range(8):
        await_bytes(piece, ys.at[i])
    for q in range(4):
        await_bytes(piece, xs.at[q])
    for k in range(3):
        await_bytes(piece, zs.at[k])
        await_bytes(piece, zs2.at[k])
    for q in range(4):
        await_bytes(piece, xs2.at[q])
    for turn in range(2):
        await_bytes(c_core.at[turn], cs.at[turn])
    for i in range(8):
        if i < 7:
            await_bytes(c_y.at[0], ar.at[i])
        await_bytes(c_y.at[0], as_.at[i])
        await_bytes(c_y.at[0], cys.at[i])


def back(
    own, pair, rows_all, columns, normed, queries, keys, values, attended,
    q_raw, k_raw, cosine, sine, q_gain, k_gain, attn_gain, gains, tokens, d_hidden,
    collective_id,
):
    rows, wide = own.shape
    length, head_cols = queries.shape
    width = normed.shape[1]
    piece_rows, piece_width = columns.shape[3:]
    proj_cols = head_cols + 2 * HEAD_DIMENSION
    dma = pltpu.SemaphoreType.DMA
    bf16, f32 = jnp.bfloat16, jnp.float32
    anywhere, vmem = pl.BlockSpec(memory_space=pl.ANY), pl.BlockSpec(memory_space=pltpu.VMEM)
    return pl.pallas_call(
        back_kernel,
        out_shape=[
            jax.ShapeDtypeStruct((rows, width), bf16),
            jax.ShapeDtypeStruct((8, piece_rows, piece_width), bf16),
            jax.ShapeDtypeStruct(gains.shape, f32),
            jax.ShapeDtypeStruct((rows, width), bf16),
        ],
        in_specs=[anywhere] * 5 + [vmem] * 14,
        out_specs=[vmem, anywhere, vmem, vmem],
        scratch_shapes=[
            pltpu.VMEM((8, rows, wide), bf16),
            pltpu.VMEM(columns.shape, bf16),
            pltpu.VMEM((2, length, TILE), bf16),
            pltpu.VMEM((length // rows, rows, width), bf16),
            pltpu.VMEM((length, head_cols), bf16),
            pltpu.VMEM((length, head_cols), f32),
            pltpu.VMEM((length, HEAD_DIMENSION), f32),
            pltpu.VMEM((length, HEAD_DIMENSION), f32),
            pltpu.VMEM((length, proj_cols), bf16),
            pltpu.VMEM((length, 128), bf16),
            pltpu.VMEM((8, HEAD_DIMENSION), f32),
            pltpu.VMEM((8, HEAD_DIMENSION), f32),
            pltpu.VMEM((8, rows, width), bf16),
            pltpu.VMEM((4, rows, width), bf16),
            pltpu.VMEM((4, rows, width), bf16),
            pltpu.VMEM((2, 3, rows, width), bf16),
            pltpu.VMEM((4, *gains.shape), f32),
            pltpu.VMEM((7, *gains.shape), f32),
            pltpu.VMEM((4, rows, width), bf16),
            pltpu.VMEM((2, 3, rows, width), bf16),
            pltpu.VMEM((2, 8, piece_rows, piece_width), bf16),
            pltpu.VMEM((8, piece_rows, piece_width), bf16),
            dma((4,)),
            dma((4, 2)),
            dma((4, 2)),
            dma((2,)),
            dma,
            dma((8,)),
            dma((8,)),
            dma((8,)),
            dma((4,)),
            dma((4,)),
            dma((3,)),
            dma((2, 3)),
            dma((6,)),
            dma((6,)),
            dma((2,)),
            pltpu.SemaphoreType.REGULAR,
            dma((4,)),
            dma((4,)),
            dma((3,)),
            dma((2, 3)),
            dma((2,)),
            dma((2,)),
            dma((8,)),
            dma((8,)),
            dma((8,)),
            dma((7,)),
        ],
        compiler_params=pltpu.CompilerParams(
            collective_id=collective_id, has_side_effects=True, vmem_limit_bytes=VMEM_LIMIT
        ),
        name="back",
    )(
        own, pair, rows_all, columns, normed, queries, keys, values, attended,
        q_raw, k_raw, cosine, sine, q_gain, k_gain, attn_gain, gains, tokens, d_hidden,
    )


C_Z, C_X, C_Y, C_C, C_KINDS = 0, 1, 2, 4, 8


def front_kernel(
    tokens, pieces, cot, cosine, sine, q_gain, k_gain, attn_gain,
    normed_out, columns_out, cot_all, queries, keys, values, attended, q_raw, k_raw, attn_out,
    own, normed, columns, part, x_in, z_in,
    ss, rs, zs, cs, cr, ys, yr, ks, kr, local_sems, gs, gr, gz, xs, xr, us, ur,
):
    p = Place()
    bf16 = jnp.bfloat16
    greet_seq(p)
    place, shard = p.z * 2 + p.x, p.y * 2 + p.c
    mine = place * 4 + shard
    rows, width = own.shape
    length, head_cols = queries.shape
    heads = head_cols // HEAD_DIMENSION
    proj_cols = head_cols + 2 * HEAD_DIMENSION
    plane_rows = 2 * rows
    score_scale = 1.0 / math.sqrt(HEAD_DIMENSION)

    x = tokens[...].astype(jnp.float32)
    scale = lax.rsqrt(jnp.mean(x * x, axis=-1, keepdims=True) + EPS)
    own[...] = (x * scale * attn_gain[...]).astype(bf16)

    def rows_at(q, x):
        return normed.at[q * 2 + x]

    def rows_move(k):
        q = p.near(k)
        there = rows_at(q, p.x)
        if k == 0:
            src = own
            for step, end in ((1, p.high), (-1, p.low)):

                @pl.when(jnp.logical_not(end))
                def _():
                    send(src, there, zs.at[q, 0 if step > 0 else 1], rs.at[q, 0], p.by_z(step))

            pltpu.make_async_copy(own, there, local_sems.at[0]).start()
        else:
            src = there
            await_bytes(src, rs.at[q, 0])

            @pl.when(p.inner)
            def _():
                send(src, src, zs.at[q, 0], rs.at[q, 0], p.by_z(p.onward(k)))

        send(src, there, ss.at[q], rs.at[q, 1], p.by_x)

    def pass_on(d):
        block = ((place + 8 - d) % 8) * 4 + shard
        src = pieces.at[place] if d == 0 else columns.at[block]
        if d > 0:
            await_bytes(src, cr.at[d])
        send(src, columns.at[block], ys.at[d], yr.at[d], p.by_y)
        send(src, columns.at[block], ks.at[0, d], kr.at[0, d], p.by_core)

    def pass_across(d):
        block = columns.at[((place + 8 - d) % 8) * 4 + (1 - p.y) * 2 + p.c]
        await_bytes(block, yr.at[d])
        send(block, block, ks.at[1, d], kr.at[1, d], p.by_core)

    def cot_at(q, x, y):
        return cot_all.at[p.block(q, x, y, p.c)]

    def cot_core(q, j, src):
        x, y = (p.x, 1 - p.x)[j % 2], (p.y, 1 - p.y)[j // 2]
        send(src, cot_at(q, x, y), gs.at[q, C_C + j], gr.at[q, C_C + j], p.by_core)

    def cot_move(k):
        q = p.near(k)
        there = cot_at(q, p.x, p.y)
        if k == 0:
            src = cot
            for step, end in ((1, p.high), (-1, p.low)):

                @pl.when(jnp.logical_not(end))
                def _():
                    send(src, there, gz.at[q, 0 if step > 0 else 1], gr.at[q, C_Z], p.by_z(step))

            pltpu.make_async_copy(cot, there, local_sems.at[2]).start()
        else:
            src = there
            await_bytes(src, gr.at[q, C_Z])

            @pl.when(p.inner)
            def _():
                send(src, src, gz.at[q, 0], gr.at[q, C_Z], p.by_z(p.onward(k)))

        send(src, there, gs.at[q, C_Y], gr.at[q, C_Y], p.by_y)
        send(src, there, gs.at[q, C_X], gr.at[q, C_X], p.by_x)
        cot_core(q, 0, src)

    def cot_turn(k):
        q = p.near(k)
        there = cot_at(q, 1 - p.x, p.y)
        await_bytes(there, gr.at[q, C_X])
        send(there, there, gs.at[q, C_Y + 1], gr.at[q, C_Y + 1], p.by_y)
        cot_core(q, 1, there)

    def cot_end(k):
        q = p.near(k)
        for j, x in ((0, p.x), (1, 1 - p.x)):
            there = cot_at(q, x, 1 - p.y)
            await_bytes(there, gr.at[q, C_Y + j])
            cot_core(q, 2 + j, there)

    def sum_end(k):
        q = p.far(k)
        held = part.at[q * 2 + p.x]
        await_bytes(x_in.at[q], xr.at[q])
        add_rows(held, x_in.at[q], rows)
        if k < 3:
            step = p.toward(k)
            slot = (1 - step) // 2

            @pl.when(p.inner)
            def _():
                await_bytes(z_in.at[slot, q], ur.at[slot, q])
                add_rows(held, z_in.at[slot, q], rows)

            send(held, z_in.at[slot, q], us.at[k], ur.at[slot, q], p.by_z(step))
        else:
            for slot, there in ((0, p.low), (1, p.high)):

                @pl.when(jnp.logical_not(there))
                def _():
                    await_bytes(z_in.at[slot, q], ur.at[slot, q])
                    add_rows(held, z_in.at[slot, q], rows)

            attn_out[...] = held[...]

    def project(n):
        cols = slice(n * TILE, (n + 1) * TILE)
        weight = columns[:, :, cols].reshape(width, TILE)
        result = mxu(normed[...].reshape(length, width), weight)
        if n * TILE < head_cols:
            q_raw[:, cols] = result
        else:
            k_raw[...] = result[:, :HEAD_DIMENSION]
            values[...] = result[:, HEAD_DIMENSION:].astype(bf16)

    def prepare():
        def one(raw, gain, at):
            scaled = raw * lax.rsqrt(jnp.mean(raw * raw, axis=-1, keepdims=True) + EPS) * gain[...]
            swapped = jnp.concatenate(
                [scaled[:, HEAD_DIMENSION // 2 :], scaled[:, : HEAD_DIMENSION // 2]], axis=1
            )
            return (scaled * cosine[at, :] - swapped * sine[at, :]).astype(bf16)

        chunk = 128

        @pl.loop(0, length // chunk)
        def _(i):
            at = pl.ds(pl.multiple_of(i * chunk, chunk), chunk)
            for h in range(heads):
                cols = slice(h * HEAD_DIMENSION, (h + 1) * HEAD_DIMENSION)
                queries[at, cols] = one(q_raw[at, cols], q_gain, at)
            keys[at, :] = one(k_raw[at, :], k_gain, at)

    def attention(k):
        q = p.far(k)
        row_start = pl.multiple_of(q * plane_rows, plane_rows)
        at = pl.ds(row_start, plane_rows)

        def block(count):
            row_pos = row_start + lax.broadcasted_iota(jnp.int32, (plane_rows, count), 0)
            allowed = lax.broadcasted_iota(jnp.int32, (plane_rows, count), 1) <= row_pos

            @pl.loop(0, heads)
            def _(h):
                cols = pl.ds(pl.multiple_of(h * HEAD_DIMENSION, HEAD_DIMENSION), HEAD_DIMENSION)
                scores = mxu(queries[at, cols], keys[:count], NT) * score_scale
                scores = jnp.where(allowed, scores, -1e30)
                raised = jnp.exp(scores - jnp.max(scores, axis=-1, keepdims=True))
                prob = raised / jnp.sum(raised, axis=-1, keepdims=True)
                attended[at, cols] = mxu(prob.astype(bf16), values[:count]).astype(bf16)

        @pl.when(q < 2)
        def _():
            block(length // 2)

        @pl.when(q >= 2)
        def _():
            block(length)

        per_tile = TILE // columns.shape[1]

        @pl.loop(0, width // TILE)
        def _(n):
            cols = pl.ds(pl.multiple_of(n * TILE, TILE), TILE)
            weight = columns[pl.ds(n * per_tile, per_tile), :, proj_cols : proj_cols + head_cols]
            result = mxu(attended[at, :], weight.reshape(TILE, head_cols), NT).astype(bf16)
            part[pl.ds(q * 2, 2), :, cols] = result.reshape(2, rows, TILE)

        send(part.at[q * 2 + 1 - p.x], x_in.at[q], xs.at[q], xr.at[q], p.by_x)

    rows_move(0)
    for d in range(1, 8):
        send(pieces.at[(place + d) % 8], columns.at[mine], cs.at[d], cr.at[d], seq_peer(p, d))
    pltpu.make_async_copy(pieces.at[place], columns.at[mine], local_sems.at[1]).start()
    pass_on(0)
    rows_move(1)
    for d in (1, 2, 7):
        pass_on(d)
    rows_move(2)
    cot_move(0)
    for d in (6, 3, 5):
        pass_on(d)
    rows_move(3)
    pass_on(4)
    for d in (0, 1, 2, 7, 6, 3, 5, 4):
        pass_across(d)
    cot_move(1)
    for k in range(4):
        await_bytes(own, rs.at[p.near(k), 1])
    pltpu.make_async_copy(own, rows_at(p.z, p.x), local_sems.at[0]).wait()
    pltpu.make_async_copy(pieces.at[place], columns.at[mine], local_sems.at[1]).wait()
    piece = pieces.at[0]
    for d in range(8):
        await_bytes(piece, kr.at[0, d])
        await_bytes(piece, kr.at[1, d])
    pltpu.make_async_copy(normed, normed_out, local_sems.at[0]).start()
    pltpu.make_async_copy(columns, columns_out, local_sems.at[1]).start()
    cot_turn(0)
    for n in range(proj_cols // TILE):
        project(n)
    cot_move(2)
    prepare()
    cot_turn(1)
    attention(0)
    cot_end(0)
    attention(1)
    cot_move(3)
    sum_end(0)
    attention(2)
    cot_turn(2)
    cot_end(1)
    sum_end(1)
    attention(3)
    cot_turn(3)
    sum_end(2)
    cot_end(2)
    sum_end(3)
    cot_end(3)
    for q in range(4):
        for j in range(4):
            await_bytes(cot, gr.at[q, C_C + j])
            await_bytes(cot, gs.at[q, C_C + j])
        for kind in (C_X, C_Y, C_Y + 1):
            await_bytes(cot, gs.at[q, kind])
        await_bytes(own, ss.at[q])
        await_bytes(own, xs.at[q])
    for there, slot in ((p.high, 0), (p.low, 1)):

        @pl.when(jnp.logical_not(there))
        def _():
            await_bytes(own, zs.at[p.z, slot])
            await_bytes(cot, gz.at[p.z, slot])

    for k in range(1, 4):

        @pl.when(p.inner)
        def _():
            await_bytes(own, zs.at[p.near(k), 0])
            await_bytes(cot, gz.at[p.near(k), 0])

    for k in range(3):
        await_bytes(own, us.at[k])
    for d in range(8):
        if d > 0:
            await_bytes(piece, cs.at[d])
        await_bytes(piece, ys.at[d])
        await_bytes(piece, ks.at[0, d])
        await_bytes(piece, ks.at[1, d])
    pltpu.make_async_copy(cot, cot_at(p.z, p.x, p.y), local_sems.at[2]).wait()
    pltpu.make_async_copy(normed, normed_out, local_sems.at[0]).wait()
    pltpu.make_async_copy(columns, columns_out, local_sems.at[1]).wait()


def front(tokens, pieces, cot, cosine, sine, q_gain, k_gain, attn_gain, head_cols, collective_id):
    dma = pltpu.SemaphoreType.DMA
    bf16, f32 = jnp.bfloat16, jnp.float32
    rows, width = tokens.shape
    count, piece_rows, piece_width = pieces.shape
    length = count * rows
    anywhere, vmem = pl.BlockSpec(memory_space=pl.ANY), pl.BlockSpec(memory_space=pltpu.VMEM)
    return pl.pallas_call(
        front_kernel,
        out_shape=[
            jax.ShapeDtypeStruct((count, rows, width), bf16),
            jax.ShapeDtypeStruct((count * 4, piece_rows, piece_width), bf16),
            jax.ShapeDtypeStruct((count * 4, rows, width), bf16),
            jax.ShapeDtypeStruct((length, head_cols), bf16),
            jax.ShapeDtypeStruct((length, HEAD_DIMENSION), bf16),
            jax.ShapeDtypeStruct((length, HEAD_DIMENSION), bf16),
            jax.ShapeDtypeStruct((length, head_cols), bf16),
            jax.ShapeDtypeStruct((length, head_cols), f32),
            jax.ShapeDtypeStruct((length, HEAD_DIMENSION), f32),
            jax.ShapeDtypeStruct((rows, width), bf16),
        ],
        in_specs=[vmem] + [anywhere] * 2 + [vmem] * 5,
        out_specs=[anywhere] * 3 + [vmem] * 7,
        scratch_shapes=[
            pltpu.VMEM((rows, width), bf16),
            pltpu.VMEM((count, rows, width), bf16),
            pltpu.VMEM((count * 4, piece_rows, piece_width), bf16),
            pltpu.VMEM((count, rows, width), bf16),
            pltpu.VMEM((4, rows, width), bf16),
            pltpu.VMEM((2, 4, rows, width), bf16),
            dma((4,)),
            dma((4, 2)),
            dma((4, 2)),
            dma((8,)),
            dma((8,)),
            dma((8,)),
            dma((8,)),
            dma((2, 8)),
            dma((2, 8)),
            dma((3,)),
            dma((4, C_KINDS)),
            dma((4, C_KINDS)),
            dma((4, 2)),
            dma((4,)),
            dma((4,)),
            dma((3,)),
            dma((2, 4)),
        ],
        compiler_params=pltpu.CompilerParams(
            collective_id=collective_id, has_side_effects=True, vmem_limit_bytes=VMEM_LIMIT
        ),
        name="front",
    )(tokens, pieces, cot, cosine, sine, q_gain, k_gain, attn_gain)


def head_columns(weight, group_index):
    rows = weight.shape[0]
    query_width = QUERY_HEADS * HEAD_DIMENSION
    key_width = KEY_VALUE_HEADS * HEAD_DIMENSION
    query = weight[:, :query_width].reshape(rows, len(group_index), -1).transpose(1, 0, 2)
    keys = weight[:, query_width : query_width + key_width].reshape(rows, KEY_VALUE_HEADS, -1)
    values = weight[:, query_width + key_width :].reshape(rows, KEY_VALUE_HEADS, -1)
    keys = jnp.stack([keys[:, group] for group in group_index])
    values = jnp.stack([values[:, group] for group in group_index])
    return jnp.concatenate([query, keys, values], axis=2)


def gathered_body(
    tokens,
    query_key_value_weight,
    w_out_t,
    w_router,
    w_in,
    w_down,
    attn_gain,
    ffn_gain,
    q_gain,
    k_gain,
    routes,
    cotangent,
):
    bf16, f32 = jnp.bfloat16, jnp.float32
    both = ("seq", "fsdp")
    seq_size = lax.axis_size("seq")
    shard_size = lax.axis_size("fsdp")
    experts = seq_size * shard_size
    rows = tokens.shape[1]
    width = tokens.shape[2]
    length = rows * seq_size
    weight_rows = query_key_value_weight.shape[0]
    heads = QUERY_HEADS // seq_size
    head_cols = heads * HEAD_DIMENSION
    kv_cols = HEAD_DIMENSION
    proj_cols = head_cols + 2 * kv_cols
    all_cols = proj_cols + head_cols
    spare_cols = 128
    group_index = [s * heads * KEY_VALUE_HEADS // QUERY_HEADS for s in range(seq_size)]
    capacity = 2 * rows * TOPK // experts

    pieces = jnp.concatenate(
        [
            head_columns(query_key_value_weight, group_index),
            w_out_t.reshape(weight_rows, seq_size, head_cols).transpose(1, 0, 2),
            jnp.broadcast_to(
                jnp.pad(w_router, ((0, 0), (0, spare_cols - experts))),
                (seq_size, weight_rows, spare_cols),
            ),
        ],
        axis=2,
    )
    resid_in = tokens[0].astype(f32)
    half_dim = HEAD_DIMENSION // 2
    exponents = -2.0 * np.arange(half_dim, dtype=np.float32) / HEAD_DIMENSION
    frequency = np.float32(ROPE_BASE) ** exponents.astype(np.float32)
    angles = np.arange(length, dtype=np.float32)[:, None] * frequency[None, :]
    cosine, sine = np.cos(angles), np.sin(angles)
    cosine = jnp.asarray(np.concatenate([cosine, cosine], axis=1), f32)
    sine = jnp.asarray(np.concatenate([sine, -sine], axis=1), f32)
    normed_all, columns, cot_all, queries, keys, values, attended, q_raw, k_raw, attn_out = front(
        tokens[0],
        pieces,
        cotangent[0],
        cosine,
        sine,
        q_gain[None],
        k_gain[None],
        attn_gain[None],
        head_cols,
        1,
    )
    normed_all = normed_all.reshape(length, width)
    columns = columns.reshape(width, -1)
    full_router = columns[:, all_cols : all_cols + experts]
    hidden = resid_in + attn_out.astype(f32)
    normed_two = rms_scale(hidden, ffn_gain).astype(bf16)

    logits = jnp.dot(normed_two, full_router, preferred_element_type=f32)
    onehot = routes[0][:, :, None] == jnp.arange(experts, dtype=jnp.int32)
    onehot_float = onehot.astype(f32)
    named = jnp.sum(onehot_float, axis=1)
    order = jnp.arange(rows, dtype=jnp.int32)
    upto = (order[None, :] <= order[:, None]).astype(bf16)
    slot_info = named * jnp.dot(upto, named.astype(bf16), preferred_element_type=f32)
    chosen = jnp.sum(onehot_float * logits[:, None, :], axis=-1)
    row_max = jnp.max(chosen, axis=-1, keepdims=True)
    exp_part = jnp.exp(chosen - row_max)
    gate_probs = exp_part / jnp.sum(exp_part, axis=-1, keepdims=True)
    gate_dense = jnp.sum(onehot_float * gate_probs[..., None], axis=1)

    gate_high = gate_dense.astype(bf16)
    gate_low = (gate_dense - gate_high.astype(f32)).astype(bf16)
    route_info = jnp.concatenate([gate_high, gate_low, slot_info.astype(bf16)], axis=1)
    route_info = jnp.pad(route_info, ((0, 0), (0, 128 - route_info.shape[1] % 128)))
    gate_weight = w_in[0]
    down_weight = w_down[0]
    rows_all, out_part, d_part, rows_in, d_expert, inner_act, d_gate_up = experts_gathered(
        jnp.concatenate([normed_two, route_info], axis=1),
        cot_all,
        gate_weight,
        down_weight,
        capacity,
        3,
    )
    d_back, out_pair, d_w_in, d_w_down = sum_all(
        d_part, out_part, rows_in, d_gate_up, inner_act, d_expert, 5
    )
    d_w_in, d_w_down = d_w_in.astype(f32)[None], d_w_down.astype(f32)[None]
    d_back = d_back.astype(f32)

    d_gate_dense = d_back[:, width : width + experts] + d_back[:, width + experts : width + 2 * experts]
    d_gates = jnp.sum(onehot_float * d_gate_dense[:, None, :], axis=-1)
    d_chosen = gate_probs * (d_gates - jnp.sum(gate_probs * d_gates, axis=-1, keepdims=True))
    d_logits = jnp.sum(d_chosen[..., None] * onehot_float, axis=1).astype(bf16)
    d_normed_two = d_back[:, :width] + jnp.einsum(
        "te,de->td", d_logits, full_router, preferred_element_type=f32
    )
    out_grad = cotangent[0].astype(f32)
    unused_two, pull_two = jax.vjp(rms_scale, hidden, ffn_gain)
    d_hidden_norm, d_ffn_gain = pull_two(d_normed_two)
    d_hidden = out_grad + d_hidden_norm
    d_attn = d_hidden.astype(bf16)

    d_send = jnp.concatenate([d_attn, jnp.pad(d_logits, ((0, 0), (0, 128 - experts)))], axis=1)
    gains = jnp.pad(d_ffn_gain[None], ((1, 6), (0, 0)))
    d_tokens, d_pieces, gains, mixture = back(
        d_send,
        out_pair.reshape(2 * seq_size, rows, width),
        rows_all.reshape(seq_size, shard_size, rows, -1),
        columns.reshape(seq_size, 2, shard_size // 2, weight_rows, all_cols + spare_cols),
        normed_all,
        queries,
        keys,
        values,
        attended,
        q_raw,
        k_raw,
        cosine,
        sine,
        q_gain[None],
        k_gain[None],
        attn_gain[None],
        gains,
        tokens[0],
        d_hidden,
        6,
    )
    output = (hidden + mixture.astype(f32)).astype(bf16)
    router_cols = experts // seq_size
    d_tokens = d_tokens[None]
    d_pieces = d_pieces.astype(f32).transpose(1, 0, 2)
    per_group = seq_size // KEY_VALUE_HEADS
    d_kv = d_pieces[:, :, head_cols:proj_cols].reshape(
        weight_rows, KEY_VALUE_HEADS, per_group, 2, kv_cols
    )
    d_kv = jnp.sum(d_kv, axis=2).transpose(0, 2, 1, 3).reshape(weight_rows, -1)
    d_w_qkv = jnp.concatenate([d_pieces[:, :, :head_cols].reshape(weight_rows, -1), d_kv], axis=1)
    d_w_out_t = d_pieces[:, :, proj_cols:all_cols].reshape(weight_rows, -1)
    d_w_router = d_pieces[:, :, all_cols : all_cols + router_cols].reshape(weight_rows, experts)
    d_attn_gain, d_ffn_gain = gains[0], gains[1]
    d_q_gain = gains[2, :HEAD_DIMENSION]
    d_k_gain = gains[2, HEAD_DIMENSION : 2 * HEAD_DIMENSION]
    return (
        output[None],
        d_tokens,
        d_w_qkv,
        d_w_out_t,
        d_w_router,
        d_w_in,
        d_w_down,
        d_attn_gain,
        d_ffn_gain,
        d_q_gain,
        d_k_gain,
    )


def gathered_fits(mesh):
    return mesh.shape["seq"] == 8 and mesh.shape["fsdp"] == 4


def solution(mesh):
    return jax.shard_map(
        gathered_body if gathered_fits(mesh) else routed_body,
        mesh=mesh,
        in_specs=(
            P("fsdp", "seq", None),
            P(("seq", "fsdp"), None),
            P(("seq", "fsdp"), None),
            P(("seq", "fsdp"), None),
            P(("seq", "fsdp"), None, None),
            P(("seq", "fsdp"), None, None),
            P(),
            P(),
            P(),
            P(),
            P("fsdp", "seq", None),
            P("fsdp", "seq", None),
        ),
        out_specs=(
            P("fsdp", "seq", None),
            P("fsdp", "seq", None),
            P(("seq", "fsdp"), None),
            P(("seq", "fsdp"), None),
            P(("seq", "fsdp"), None),
            P(("seq", "fsdp"), None, None),
            P(("seq", "fsdp"), None, None),
            P(),
            P(),
            P(),
            P(),
        ),
        check_vma=False,
    )
```

```python
from functools import partial
import math

import jax
import jax.numpy as jnp
import numpy as np
from jax import lax
from jax.experimental import pallas as pl
from jax.experimental.pallas import tpu as pltpu
from jax.sharding import PartitionSpec as P

QUERY_HEADS = 32
KEY_VALUE_HEADS = 4
HEAD_DIMENSION = 128
FF = 768
TOPK = 8


EPS = 1e-06
ROPE_BASE = 1000000.0


def rms_scale(values, gain):
    return values * lax.rsqrt(jnp.mean(values * values, axis=-1, keepdims=True) + EPS) * gain


def rotate(values, positions):
    half_dim = values.shape[-1] // 2
    frequency = ROPE_BASE ** (-2.0 * jnp.arange(half_dim, dtype=jnp.float32) / values.shape[-1])
    angles = positions.astype(jnp.float32)[:, None] * frequency[None, :]
    cosine = jnp.cos(angles)[:, None, :]
    sine_part = jnp.sin(angles)[:, None, :]
    first_half = values[..., :half_dim]
    second = values[..., half_dim:]
    return jnp.concatenate(
        [first_half * cosine - second * sine_part, second * cosine + first_half * sine_part],
        axis=-1,
    )


def head_prepare(raw_heads, gain, positions):
    return rotate(rms_scale(raw_heads, gain), positions)


def route_slots(route_flat, experts):
    onehot = (route_flat[:, None] == jnp.arange(experts, dtype=jnp.int32)[None, :]).astype(
        jnp.int32
    )
    earlier = jnp.cumsum(onehot, axis=0) - onehot
    return (onehot, jnp.sum(earlier * onehot, axis=1))


def pack_slots(row_values, expert_ids, slot_index, slot_shape):
    buffer = jnp.zeros(slot_shape, row_values.dtype)
    return buffer.at[expert_ids // slot_shape[1], expert_ids % slot_shape[1], slot_index].set(
        row_values
    )


def unpack_slots(buffer, expert_ids, slot_index):
    return buffer[expert_ids // buffer.shape[1], expert_ids % buffer.shape[1], slot_index]


def causal_scores(query_part, key_full, row_start):
    block_rows = query_part.shape[0]
    score_scale = 1.0 / math.sqrt(query_part.shape[2])
    scores = (
        jnp.einsum("qhd,khd->hqk", query_part, key_full, preferred_element_type=jnp.float32)
        * score_scale
    )
    key_pos = jnp.arange(key_full.shape[0], dtype=jnp.int32)
    row_pos = row_start + jnp.arange(block_rows, dtype=jnp.int32)
    allowed = key_pos[None, :] <= row_pos[:, None]
    return jnp.where(allowed[None], scores, -1e30)


def attend_forward(query_rows_all, key_full, value_full):
    sequence_length = query_rows_all.shape[0]
    block_rows = min(512, sequence_length)

    def one_block(block_index):
        row_start = block_index * block_rows
        query_part = lax.dynamic_slice_in_dim(query_rows_all, row_start, block_rows, 0)
        scores = causal_scores(query_part, key_full, row_start)
        row_max = jnp.max(scores, axis=-1, keepdims=True)
        weights = jnp.exp(scores - row_max)
        row_total = jnp.sum(weights, axis=-1, keepdims=True)
        prob_low = (weights / row_total).astype(jnp.bfloat16)
        mixed_out = jnp.einsum(
            "hqk,khd->qhd", prob_low, value_full, preferred_element_type=jnp.float32
        )
        return (mixed_out.astype(jnp.bfloat16), (row_max + jnp.log(row_total))[..., 0])

    mixed_out, log_total = lax.map(
        one_block, jnp.arange(sequence_length // block_rows, dtype=jnp.int32)
    )
    return (mixed_out.reshape(query_rows_all.shape), log_total)


def attend_backward(query_rows_all, key_full, value_full, log_total, d_mixed):
    sequence_length = query_rows_all.shape[0]
    block_rows = min(512, sequence_length)
    score_scale = 1.0 / math.sqrt(query_rows_all.shape[2])

    def one_block(running, block_index):
        d_key_sum, d_value_sum = running
        row_start = block_index * block_rows
        query_part = lax.dynamic_slice_in_dim(query_rows_all, row_start, block_rows, 0)
        d_part = lax.dynamic_slice_in_dim(d_mixed, row_start, block_rows, 0)
        scores = causal_scores(query_part, key_full, row_start)
        prob_full = jnp.exp(scores - log_total[block_index][..., None])
        prob_low = prob_full.astype(jnp.bfloat16)
        d_probs = jnp.einsum("qhd,khd->hqk", d_part, value_full, preferred_element_type=jnp.float32)
        row_delta = jnp.sum(prob_full * d_probs, axis=-1, keepdims=True)
        d_scores = (prob_full * (d_probs - row_delta)).astype(jnp.bfloat16)
        d_query_part = (
            jnp.einsum("hqk,khd->qhd", d_scores, key_full, preferred_element_type=jnp.float32)
            * score_scale
        )
        d_key_sum = (
            d_key_sum
            + jnp.einsum("hqk,qhd->khd", d_scores, query_part, preferred_element_type=jnp.float32)
            * score_scale
        )
        d_value_sum = d_value_sum + jnp.einsum(
            "hqk,qhd->khd", prob_low, d_part, preferred_element_type=jnp.float32
        )
        return ((d_key_sum, d_value_sum), d_query_part)

    zero_grad = jnp.zeros(key_full.shape, jnp.float32)
    (d_key_sum, d_value_sum), d_query = lax.scan(
        one_block,
        (zero_grad, zero_grad),
        jnp.arange(sequence_length // block_rows, dtype=jnp.int32),
    )
    return (d_query.reshape(query_rows_all.shape), d_key_sum, d_value_sum)


def routed_body(
    tokens,
    query_key_value_weight,
    w_out_t,
    w_router,
    w_in,
    w_down,
    attn_gain,
    ffn_gain,
    q_gain,
    k_gain,
    routes,
    cotangent,
):
    sequence_count = lax.axis_size("seq")
    shard_count = lax.axis_size("fsdp")
    experts = sequence_count * shard_count
    token_row_count = tokens.shape[1]
    model_width = tokens.shape[2]
    query_group_width = QUERY_HEADS // KEY_VALUE_HEADS
    capacity = 2 * token_row_count * TOPK // experts
    slot_shape = (sequence_count, shard_count, capacity, model_width)
    positions = lax.axis_index("seq") * token_row_count + jnp.arange(
        token_row_count, dtype=jnp.int32
    )
    full_qkv, full_out, full_router = (
        lax.all_gather(query_key_value_weight, ("seq", "fsdp"), axis=0, tiled=True),
        lax.all_gather(w_out_t, ("seq", "fsdp"), axis=0, tiled=True),
        lax.all_gather(w_router, ("seq", "fsdp"), axis=0, tiled=True),
    )
    resid_in = tokens[0].astype(jnp.float32)
    normed_one = rms_scale(resid_in, attn_gain).astype(jnp.bfloat16)
    projection_output = jnp.dot(normed_one, full_qkv, preferred_element_type=jnp.float32)
    q_raw = projection_output[:, : QUERY_HEADS * HEAD_DIMENSION].reshape(
        token_row_count, QUERY_HEADS, HEAD_DIMENSION
    )
    key_unnormed = projection_output[
        :, QUERY_HEADS * HEAD_DIMENSION : (QUERY_HEADS + KEY_VALUE_HEADS) * HEAD_DIMENSION
    ].reshape(token_row_count, KEY_VALUE_HEADS, HEAD_DIMENSION)
    value_per_head = (
        projection_output[:, (QUERY_HEADS + KEY_VALUE_HEADS) * HEAD_DIMENSION :]
        .reshape(token_row_count, KEY_VALUE_HEADS, HEAD_DIMENSION)
        .astype(jnp.bfloat16)
    )
    prepare = partial(head_prepare, positions=positions)
    query_rows_all = prepare(q_raw, q_gain).astype(jnp.bfloat16)
    key_per_head = prepare(key_unnormed, k_gain).astype(jnp.bfloat16)
    send_keys = jnp.repeat(key_per_head, query_group_width, axis=1)
    send_values = jnp.repeat(value_per_head, query_group_width, axis=1)
    head_queries, head_keys, head_values = (
        lax.all_to_all(query_rows_all, "seq", split_axis=1, concat_axis=0, tiled=True),
        lax.all_to_all(send_keys, "seq", split_axis=1, concat_axis=0, tiled=True),
        lax.all_to_all(send_values, "seq", split_axis=1, concat_axis=0, tiled=True),
    )
    mixed_heads, log_total = attend_forward(head_queries, head_keys, head_values)
    mixed_tok = lax.all_to_all(mixed_heads, "seq", split_axis=0, concat_axis=1, tiled=True)
    attention_result = mixed_tok.reshape(token_row_count, QUERY_HEADS * HEAD_DIMENSION)
    attn_out = jnp.einsum(
        "tj,dj->td", attention_result, full_out, preferred_element_type=jnp.float32
    )
    hidden = resid_in + attn_out
    normed_two = rms_scale(hidden, ffn_gain).astype(jnp.bfloat16)
    logits = jnp.dot(normed_two, full_router, preferred_element_type=jnp.float32)
    route_flat = routes[0].reshape(-1)
    onehot, slot_index = route_slots(route_flat, experts)
    onehot_float = onehot.reshape(token_row_count, TOPK, experts).astype(jnp.float32)
    chosen = jnp.sum(onehot_float * logits[:, None, :], axis=-1)
    row_max = jnp.max(chosen, axis=-1, keepdims=True)
    exp_part = jnp.exp(chosen - row_max)
    gate_probs = exp_part / jnp.sum(exp_part, axis=-1, keepdims=True)
    send_rows = pack_slots(jnp.repeat(normed_two, TOPK, axis=0), route_flat, slot_index, slot_shape)
    arrived = lax.all_to_all(
        lax.all_to_all(send_rows, "seq", split_axis=0, concat_axis=0, tiled=True),
        "fsdp",
        split_axis=1,
        concat_axis=1,
        tiled=True,
    )
    rows_in = arrived.reshape(-1, model_width)
    gate_weight = w_in[0]
    down_weight = w_down[0]
    gate_up = jnp.dot(rows_in, gate_weight, preferred_element_type=jnp.float32)
    gate_half = gate_up[:, :FF]
    up_half = gate_up[:, FF:]
    gate_sig = jax.nn.sigmoid(gate_half)
    silu_gate = gate_half * gate_sig
    inner_act = (silu_gate * up_half).astype(jnp.bfloat16)
    expert_out = jnp.dot(inner_act, down_weight, preferred_element_type=jnp.float32).astype(
        jnp.bfloat16
    )
    returned = lax.all_to_all(
        lax.all_to_all(
            expert_out.reshape(slot_shape), "seq", split_axis=0, concat_axis=0, tiled=True
        ),
        "fsdp",
        split_axis=1,
        concat_axis=1,
        tiled=True,
    )
    picked = (
        unpack_slots(returned, route_flat, slot_index)
        .astype(jnp.float32)
        .reshape(token_row_count, TOPK, model_width)
    )
    mixture = jnp.sum(gate_probs[..., None] * picked, axis=1)
    output = (hidden + mixture).astype(jnp.bfloat16)
    full_qkv, full_out, full_router = (
        lax.all_gather(query_key_value_weight, ("seq", "fsdp"), axis=0, tiled=True),
        lax.all_gather(w_out_t, ("seq", "fsdp"), axis=0, tiled=True),
        lax.all_gather(w_router, ("seq", "fsdp"), axis=0, tiled=True),
    )
    out_grad = cotangent[0].astype(jnp.float32)
    d_picked = (
        (gate_probs[..., None] * out_grad[:, None, :]).astype(jnp.bfloat16).reshape(-1, model_width)
    )
    d_gates = jnp.sum(picked * out_grad[:, None, :], axis=-1)
    d_send = pack_slots(d_picked, route_flat, slot_index, slot_shape)
    d_arrived = lax.all_to_all(
        lax.all_to_all(d_send, "seq", split_axis=0, concat_axis=0, tiled=True),
        "fsdp",
        split_axis=1,
        concat_axis=1,
        tiled=True,
    ).reshape(-1, model_width)
    d_inner = jnp.einsum("rd,fd->rf", d_arrived, down_weight, preferred_element_type=jnp.float32)
    d_gate_half = d_inner * up_half * gate_sig * (1.0 + gate_half * (1.0 - gate_sig))
    d_up_half = d_inner * silu_gate
    d_gate_up = jnp.concatenate([d_gate_half, d_up_half], axis=1).astype(jnp.bfloat16)
    d_w_down = jnp.einsum("rf,rd->fd", inner_act, d_arrived, preferred_element_type=jnp.float32)[
        None
    ]
    d_w_in = jnp.einsum("rd,rf->df", rows_in, d_gate_up, preferred_element_type=jnp.float32)[None]
    d_rows = jnp.einsum(
        "rf,df->rd", d_gate_up, gate_weight, preferred_element_type=jnp.float32
    ).astype(jnp.bfloat16)
    d_back = lax.all_to_all(
        lax.all_to_all(d_rows.reshape(slot_shape), "seq", split_axis=0, concat_axis=0, tiled=True),
        "fsdp",
        split_axis=1,
        concat_axis=1,
        tiled=True,
    )
    d_routed = jnp.sum(
        unpack_slots(d_back, route_flat, slot_index)
        .astype(jnp.float32)
        .reshape(token_row_count, TOPK, model_width),
        axis=1,
    )
    d_chosen = gate_probs * (d_gates - jnp.sum(gate_probs * d_gates, axis=-1, keepdims=True))
    d_logits = jnp.einsum("tk,tke->te", d_chosen, onehot_float).astype(jnp.bfloat16)
    d_normed_two = d_routed + jnp.einsum(
        "te,de->td", d_logits, full_router, preferred_element_type=jnp.float32
    )
    unused_two, pull_two = jax.vjp(rms_scale, hidden, ffn_gain)
    d_hidden_norm, d_ffn_gain = pull_two(d_normed_two)
    d_hidden = out_grad + d_hidden_norm
    d_attn = d_hidden.astype(jnp.bfloat16)
    d_attended = jnp.einsum(
        "td,dj->tj", d_attn, full_out, preferred_element_type=jnp.float32
    ).astype(jnp.bfloat16)
    d_heads = lax.all_to_all(
        d_attended.reshape(token_row_count, QUERY_HEADS, HEAD_DIMENSION),
        "seq",
        split_axis=1,
        concat_axis=0,
        tiled=True,
    )
    d_query, d_key_sum, d_value_sum = attend_backward(
        head_queries, head_keys, head_values, log_total, d_heads
    )
    seq_rows = head_queries.shape[0]
    local_cols = head_queries.shape[1] * HEAD_DIMENSION
    normed_all, d_attn_all = (
        lax.all_gather(normed_one, "seq", axis=0, tiled=True),
        lax.all_gather(d_attn, "seq", axis=0, tiled=True),
    )
    query_cols = lax.dynamic_slice_in_dim(
        full_qkv, lax.axis_index("seq") * local_cols, local_cols, 1
    )
    q_head_raw = jnp.dot(normed_all, query_cols, preferred_element_type=jnp.float32).reshape(
        head_queries.shape
    )
    seq_positions = jnp.arange(seq_rows, dtype=jnp.int32)
    unused_head, pull_head = jax.vjp(
        partial(head_prepare, positions=seq_positions), q_head_raw, q_gain
    )
    send_d_query, d_q_gain = pull_head(d_query)
    d_query_tok, grad_key_token_rows, grad_value_token_rows = (
        lax.all_to_all(
            send_d_query.astype(jnp.bfloat16), "seq", split_axis=0, concat_axis=1, tiled=True
        ).astype(send_d_query.dtype),
        lax.all_to_all(
            d_key_sum.astype(jnp.bfloat16), "seq", split_axis=0, concat_axis=1, tiled=True
        ).astype(d_key_sum.dtype),
        lax.all_to_all(
            d_value_sum.astype(jnp.bfloat16), "seq", split_axis=0, concat_axis=1, tiled=True
        ).astype(d_value_sum.dtype),
    )
    grad_key_per_head = jnp.sum(
        grad_key_token_rows.reshape(token_row_count, KEY_VALUE_HEADS, -1, HEAD_DIMENSION), axis=2
    )
    grad_value_per_head = jnp.sum(
        grad_value_token_rows.reshape(token_row_count, KEY_VALUE_HEADS, -1, HEAD_DIMENSION), axis=2
    )
    unused_k, pull_k = jax.vjp(prepare, key_unnormed, k_gain)
    grad_key_unnormed, d_k_gain = pull_k(grad_key_per_head)
    d_projected = jnp.concatenate(
        [
            d_query_tok.reshape(token_row_count, QUERY_HEADS * HEAD_DIMENSION),
            grad_key_unnormed.reshape(token_row_count, KEY_VALUE_HEADS * HEAD_DIMENSION),
            grad_value_per_head.reshape(token_row_count, KEY_VALUE_HEADS * HEAD_DIMENSION),
        ],
        axis=1,
    ).astype(jnp.bfloat16)
    d_normed_one = jnp.einsum(
        "tj,dj->td", d_projected, full_qkv, preferred_element_type=jnp.float32
    )
    unused_one, pull_one = jax.vjp(rms_scale, resid_in, attn_gain)
    d_resid_norm, d_attn_gain = pull_one(d_normed_one)
    d_tokens = (d_hidden + d_resid_norm).astype(jnp.bfloat16)[None]
    rows_dev = model_width // experts
    kv_count = 2 * KEY_VALUE_HEADS * HEAD_DIMENSION
    kv_grads = d_projected[:, QUERY_HEADS * HEAD_DIMENSION :]
    first_rows = normed_one
    summed = lax.psum_scatter(
        jnp.concatenate(
            [
                jnp.einsum("tc,tj->cj", first_rows, kv_grads, preferred_element_type=jnp.float32),
                jnp.einsum("tc,te->ce", normed_two, d_logits, preferred_element_type=jnp.float32),
            ],
            axis=1,
        ),
        ("seq", "fsdp"),
        scatter_dimension=0,
        tiled=True,
    )
    d_query_low = send_d_query.reshape(seq_rows, local_cols).astype(jnp.bfloat16)
    attended_heads = mixed_heads.reshape(seq_rows, local_cols)
    normed_order = (
        normed_all.reshape(seq_rows, sequence_count, shard_count, rows_dev)
        .transpose(0, 2, 1, 3)
        .reshape(seq_rows, model_width)
    )
    d_attn_order = (
        d_attn_all.reshape(seq_rows, sequence_count, shard_count, rows_dev)
        .transpose(0, 2, 1, 3)
        .reshape(seq_rows, model_width)
    )
    first_rows = normed_order
    head_sums = lax.psum_scatter(
        jnp.concatenate(
            [
                jnp.einsum(
                    "tc,tj->cj", first_rows, d_query_low, preferred_element_type=jnp.float32
                ),
                jnp.einsum(
                    "tc,tj->cj", d_attn_order, attended_heads, preferred_element_type=jnp.float32
                ),
            ],
            axis=1,
        ).astype(jnp.bfloat16),
        "fsdp",
        scatter_dimension=0,
        tiled=True,
    ).astype(jnp.float32)
    row_sums = (
        lax.all_to_all(
            head_sums.astype(jnp.bfloat16), "seq", split_axis=0, concat_axis=1, tiled=True
        )
        .astype(head_sums.dtype)
        .reshape(rows_dev, sequence_count, 2, local_cols)
    )
    d_w_query = row_sums[:, :, 0].reshape(rows_dev, QUERY_HEADS * HEAD_DIMENSION)
    d_w_out_t = row_sums[:, :, 1].reshape(rows_dev, QUERY_HEADS * HEAD_DIMENSION)
    d_w_qkv = jnp.concatenate([d_w_query, summed[:, :kv_count]], axis=1)
    d_w_router = summed[:, kv_count:]
    d_attn_gain, d_ffn_gain, d_q_gain, d_k_gain = lax.psum(
        (d_attn_gain, d_ffn_gain, d_q_gain, d_k_gain), ("seq", "fsdp")
    )
    return (
        output[None],
        d_tokens,
        d_w_qkv,
        d_w_out_t,
        d_w_router,
        d_w_in,
        d_w_down,
        d_attn_gain,
        d_ffn_gain,
        d_q_gain,
        d_k_gain,
    )


MESH = pl.DeviceIdType.MESH
VMEM_LIMIT = 60 * 2**20


class Place:
    def __init__(self):
        seq, shard = lax.axis_index("seq"), lax.axis_index("fsdp")
        self.z, self.x = seq // 2, seq % 2
        self.y, self.c = shard // 2, shard % 2
        self.z0, self.z1 = self.z % 2, self.z // 2
        self.low, self.high = self.z == 0, self.z == 3
        self.inner = (self.z0 + self.z1) == 1
        self.me = self.block(self.z, self.x, self.y, self.c)

    def device(self, z, x, y, c):
        return (z * 2 + x, y * 2 + c)

    def block(self, z, x, y, c):
        return (z * 2 + x) * 4 + y * 2 + c

    @property
    def by_x(self):
        return self.device(self.z, 1 - self.x, self.y, self.c)

    @property
    def by_y(self):
        return self.device(self.z, self.x, 1 - self.y, self.c)

    @property
    def by_core(self):
        return self.device(self.z, self.x, self.y, 1 - self.c)

    def by_z(self, step):
        return self.device(self.z + step, self.x, self.y, self.c)

    def near(self, k):
        return [self.z, 1 + self.z0, 2 - 2 * self.z0 + self.z1, 3 - 3 * self.z1][k]

    def onward(self, k):
        return [None, 2 * self.z1 - 1, 1 - 2 * self.z1, 2 * self.z1 - 1][k]

    def far(self, k):
        return self.near(3 - k)

    def toward(self, k):
        return [1 - 2 * self.z1, 1 - 2 * self.z0, 1 - 2 * self.z1][k]

    def greet(self, sides):
        barrier = pltpu.get_barrier_semaphore()
        for side in sides:
            if side != "z":
                target = {"x": self.by_x, "y": self.by_y, "core": self.by_core}[side]
                pl.semaphore_signal(barrier, inc=1, device_id=target, device_id_type=MESH)
        count = len([side for side in sides if side != "z"])
        if "z" in sides:

            @pl.when(jnp.logical_not(self.low))
            def _():
                pl.semaphore_signal(barrier, inc=1, device_id=self.by_z(-1), device_id_type=MESH)

            @pl.when(jnp.logical_not(self.high))
            def _():
                pl.semaphore_signal(barrier, inc=1, device_id=self.by_z(1), device_id_type=MESH)

            count = count + 1 + (self.z0 + self.z1) % 2
        pl.semaphore_wait(barrier, count)


def send(source, target, send_sem, recv_sem, device):
    pltpu.make_async_remote_copy(
        src_ref=source,
        dst_ref=target,
        send_sem=send_sem,
        recv_sem=recv_sem,
        device_id=device,
        device_id_type=MESH,
    ).start()


def await_bytes(ref, sem):
    pltpu.make_async_copy(ref, ref, sem).wait()


G_Z, G_X, G_Y, G_DX, G_DY, G_C0 = 0, 1, 2, 3, 4, 5
G_KINDS = 9


def gather_steps(place, own, out, ss, rs, zs, local_sem):
    p = place
    rows = out.shape[1]
    half = rows // 2
    x, y, c = p.x, p.y, p.c

    def cols(q):
        return [
            p.block(q, x, y, c),
            p.block(q, 1 - x, y, c),
            p.block(q, x, 1 - y, c),
            p.block(q, 1 - x, 1 - y, c),
        ]

    def to_core(q, j, src=None):
        b = cols(q)[j]
        send(out.at[b] if src is None else src, out.at[b], ss.at[q, G_C0 + j], rs.at[q, G_C0 + j], p.by_core)

    def plane_out(k):
        q = p.near(k)
        b = cols(q)[0]
        if k == 0:
            src = own
            for step, there in ((1, p.high), (-1, p.low)):

                @pl.when(jnp.logical_not(there))
                def _():
                    send(src, out.at[b], zs.at[q, 0 if step > 0 else 1], rs.at[q, G_Z], p.by_z(step))

            pltpu.make_async_copy(own, out.at[b], local_sem).start()
        else:
            src = out.at[b]

            @pl.when(jnp.logical_not(p.inner))
            def _():
                await_bytes(src, rs.at[q, G_Z])

        send(src, out.at[b], ss.at[q, G_X], rs.at[q, G_X], p.by_x)
        send(src, out.at[b], ss.at[q, G_Y], rs.at[q, G_Y], p.by_y)
        to_core(q, 0, src)

    def plane_hop(k):
        q = p.near(k)
        src = out.at[cols(q)[0]]

        @pl.when(p.inner)
        def _():
            await_bytes(src, rs.at[q, G_Z])
            send(src, src, zs.at[q, 0], rs.at[q, G_Z], p.by_z(p.onward(k)))

    def plane_turn(k):
        q = p.near(k)
        bx, by = out.at[cols(q)[1]], out.at[cols(q)[2]]
        await_bytes(bx, rs.at[q, G_X])
        first = bx.at[pl.ds(0, half)]
        send(first, first, ss.at[q, G_DY], rs.at[q, G_DY], p.by_y)
        to_core(q, 1)
        await_bytes(by, rs.at[q, G_Y])
        second = by.at[pl.ds(half, half)]
        send(second, second, ss.at[q, G_DX], rs.at[q, G_DX], p.by_x)
        to_core(q, 2)

    def plane_end(k):
        q = p.near(k)
        bd = out.at[cols(q)[3]]
        await_bytes(bd.at[pl.ds(0, half)], rs.at[q, G_DY])
        await_bytes(bd.at[pl.ds(half, half)], rs.at[q, G_DX])
        to_core(q, 3)

    def plane_core(k, js=(0, 1, 2, 3)):
        q = p.near(k)
        for j in js:
            await_bytes(own, rs.at[q, G_C0 + j])

    def finish():
        piece = own.at[pl.ds(0, half)]
        for q in range(4):
            for kind in (G_X, G_Y, G_C0, G_C0 + 1, G_C0 + 2, G_C0 + 3):
                await_bytes(own, ss.at[q, kind])
            for kind in (G_DX, G_DY):
                await_bytes(piece, ss.at[q, kind])
        for there, slot in ((p.high, 0), (p.low, 1)):

            @pl.when(jnp.logical_not(there))
            def _():
                await_bytes(own, zs.at[p.z, slot])

        for k in range(1, 4):

            @pl.when(p.inner)
            def _():
                await_bytes(own, zs.at[p.near(k), 0])

    return plane_out, plane_hop, plane_turn, plane_end, plane_core, finish


def sum_all_parts(p, part, held, core_in, x_half, y_half, x_in, y_in, z_in, out, ls, cs, cr, ss, rs, zs, zr):
    rows, width = part.shape[1], part.shape[2]
    half = rows // 2
    x, y, c = p.x, p.y, p.c

    def columns(q):
        return [(q, x, y), (q, 1 - x, y), (q, x, 1 - y), (q, 1 - x, 1 - y)]

    def start():
        for k in range(4):
            q = p.far(k)
            for j, (zz, xx, yy) in reversed(list(enumerate(columns(q)))):
                send(
                    part.at[p.block(zz, xx, yy, 1 - c)],
                    core_in.at[q * 4 + j],
                    cs.at[q, j],
                    cr.at[q, j],
                    p.by_core,
                )
                pltpu.make_async_copy(
                    part.at[p.block(zz, xx, yy, c)], held.at[q * 4 + j], ls.at[q, j]
                ).start()

    add = add_rows

    def plane_core(k, js=(3, 1, 2, 0)):
        q = p.far(k)
        for j in js:
            slot = q * 4 + j
            await_bytes(held.at[slot], ls.at[q, j])
            await_bytes(core_in.at[slot], cr.at[q, j])
            add(held.at[slot], core_in.at[slot], rows)
            if j == 3:
                send(held.at[slot, pl.ds(0, half)], y_half.at[q], ss.at[q, 0], rs.at[q, 0], p.by_y)
                send(held.at[slot, pl.ds(half, half)], x_half.at[q], ss.at[q, 1], rs.at[q, 1], p.by_x)

    def plane_turn(k):
        q = p.far(k)
        await_bytes(y_half.at[q], rs.at[q, 0])
        add(held.at[q * 4 + 1, pl.ds(0, half)], y_half.at[q], half)
        send(held.at[q * 4 + 1], x_in.at[q], ss.at[q, 2], rs.at[q, 2], p.by_x)
        await_bytes(x_half.at[q], rs.at[q, 1])
        add(held.at[q * 4 + 2, pl.ds(half, half)], x_half.at[q], half)
        send(held.at[q * 4 + 2], y_in.at[q], ss.at[q, 3], rs.at[q, 3], p.by_y)

    def plane_end(k):
        q = p.far(k)
        mine = held.at[q * 4]
        await_bytes(x_in.at[q], rs.at[q, 2])
        add(mine, x_in.at[q], rows)
        await_bytes(y_in.at[q], rs.at[q, 3])
        add(mine, y_in.at[q], rows)
        if k < 3:
            step = p.toward(k)
            slot = (1 - step) // 2

            @pl.when(p.inner)
            def _():
                await_bytes(z_in.at[slot, q], zr.at[slot, q])
                add(mine, z_in.at[slot, q], rows)

            send(mine, z_in.at[slot, q], zs.at[k], zr.at[slot, q], p.by_z(step))
        else:
            for slot, there in ((0, p.low), (1, p.high)):

                @pl.when(jnp.logical_not(there))
                def _():
                    await_bytes(z_in.at[slot, q], zr.at[slot, q])
                    add(mine, z_in.at[slot, q], rows)

            out[...] = mine[...]

    def finish():
        whole, piece = x_in.at[0], x_half.at[0]
        for q in range(4):
            for j in range(4):
                await_bytes(whole, cs.at[q, j])
            for kind in (0, 1):
                await_bytes(piece, ss.at[q, kind])
            for kind in (2, 3):
                await_bytes(whole, ss.at[q, kind])
        for k in range(3):
            await_bytes(whole, zs.at[k])

    return start, plane_core, plane_turn, plane_end, finish


def sum_all_kernel(
    part, both, rows_in, d_gate_up, inner, d_expert, columns, hidden, cot, gates, ffn_gain,
    out, d_hidden, gains, pair, d_w_in, d_w_down,
    d_rows, router, router_sem, both_held, both_in, left, product, pair_sems, load_sems, left_sems, product_sems, *scratch,
):
    p = Place()
    p.greet(("x", "y", "core", "z"))
    start, plane_core, plane_turn, plane_end, finish = sum_all_parts(p, part, *scratch[:7], d_rows, *scratch[7:])
    rows = both.shape[3]

    def pair_sum(first):
        for s in (first, first + 1):
            for y in range(2):
                add_rows(both_held.at[s, y], both_in.at[s, y], rows)

    def right_load(source, i):
        width = source.shape[3]
        return pltpu.make_async_copy(source, both_in.at[:, :, :, pl.ds(0, width)], load_sems.at[i])

    def left_load(source, i, slot):
        cols = pl.ds(pl.multiple_of(i * TILE, TILE), TILE)
        return pltpu.make_async_copy(source.at[:, cols], left.at[slot], left_sems.at[slot])

    def product_store(target, i, slot):
        at = pl.ds(pl.multiple_of(i * TILE, TILE), TILE)
        piece = product.at[slot, :, pl.ds(0, target.shape[1])]
        return pltpu.make_async_copy(piece, target.at[at], product_sems.at[slot])

    def tiles(source, target, first, last):
        count, wide = source.shape[1] // TILE, target.shape[1]

        @pl.loop(first, last)
        def _(i):
            slot = i % 2
            left_load(source, i, slot).wait()

            @pl.when(i + 1 < count)
            def _():
                left_load(source, i + 1, 1 - slot).start()

            @pl.when(i >= 2)
            def _():
                product_store(target, i - 2, slot).wait()

            right = both_in[:, :, :, :wide].reshape(source.shape[0], wide)
            product[slot, :, :wide] = mxu(left[slot], right, TN).astype(product.dtype)
            product_store(target, i, slot).start()

    def tiles_end(source, target):
        count = source.shape[1] // TILE
        for i in (count - 2, count - 1):
            product_store(target, i, i % 2).wait()

    first = columns.shape[2] - 128
    router_load = pltpu.make_async_copy(columns.at[:, :, pl.ds(first, 128)], router, router_sem)
    router_load.start()
    start()
    send(both.at[:, :, 1 - p.c], both_in, pair_sems.at[0], pair_sems.at[1], p.by_core)
    pltpu.make_async_copy(both.at[:, :, p.c], both_held, pair_sems.at[2]).start()
    plane_core(0)
    plane_core(1)
    plane_turn(0)
    await_bytes(both_held, pair_sems.at[2])
    await_bytes(both_in, pair_sems.at[1])
    pair_sum(0)
    plane_core(2)
    pair_sum(2)
    plane_turn(1)
    pair_sum(4)
    pair_sum(6)
    pltpu.make_async_copy(both_held, pair, pair_sems.at[2]).start()
    right_load(d_gate_up, 0).start()
    left_load(rows_in, 0, 0).start()
    plane_end(0)
    plane_core(3)
    right_load(d_gate_up, 0).wait()
    tiles(rows_in, d_w_in, 0, 2)
    plane_turn(2)
    tiles(rows_in, d_w_in, 2, 4)
    plane_end(1)
    tiles(rows_in, d_w_in, 4, 6)
    plane_turn(3)
    tiles(rows_in, d_w_in, 6, 8)
    right_load(d_expert, 1).start()
    tiles_end(rows_in, d_w_in)
    left_load(inner, 0, 0).start()
    plane_end(2)
    right_load(d_expert, 1).wait()
    tiles(inner, d_w_down, 0, 3)
    plane_end(3)
    router_load.wait()
    width = hidden.shape[1]
    experts = part.shape[0]
    tail = d_rows[:, width:].astype(jnp.float32)
    lane = lax.broadcasted_iota(jnp.int32, tail.shape, 1)
    d_gates = jnp.where(lane < experts, tail + pltpu.roll(tail, 128 - experts, 1), 0.0)
    gate = gates[...]
    d_chosen = gate * (d_gates - jnp.sum(gate * d_gates, axis=-1, keepdims=True))
    out[:, width:] = d_chosen.astype(out.dtype)
    gains[...] = jnp.zeros_like(gains)
    chunk = 32

    @pl.loop(0, rows // chunk)
    def _(i):
        at = pl.ds(pl.multiple_of(i * chunk, chunk), chunk)
        routed = mxu(out[at, width:], router[...].reshape(width, 128), NT)
        d_out = d_rows[at, :width].astype(jnp.float32) + routed
        x = hidden[at, :]
        scale = lax.rsqrt(jnp.mean(x * x, axis=-1, keepdims=True) + EPS)
        u = d_out * ffn_gain[...]
        dot = jnp.mean(u * x, axis=-1, keepdims=True)
        grad = cot[at, :].astype(jnp.float32) + scale * u - x * (scale * scale * scale * dot)
        d_hidden[at, :] = grad
        out[at, :width] = grad.astype(out.dtype)
        gains[1:2, :] += jnp.sum(d_out * x * scale, axis=0, keepdims=True)

    tiles_end(inner, d_w_down)
    finish()
    await_bytes(both_held, pair_sems.at[0])
    pltpu.make_async_copy(both_held, pair, pair_sems.at[2]).wait()


def sum_all_scratch(rows, width):
    dma = pltpu.SemaphoreType.DMA
    bf16 = jnp.bfloat16
    return [
        pltpu.VMEM((16, rows, width), bf16),
        pltpu.VMEM((16, rows, width), bf16),
        pltpu.VMEM((4, rows // 2, width), bf16),
        pltpu.VMEM((4, rows // 2, width), bf16),
        pltpu.VMEM((4, rows, width), bf16),
        pltpu.VMEM((4, rows, width), bf16),
        pltpu.VMEM((2, 4, rows, width), bf16),
        dma((4, 4)),
        dma((4, 4)),
        dma((4, 4)),
        dma((4, 4)),
        dma((4, 4)),
        dma((3,)),
        dma((2, 4)),
    ]


def sum_all(
    part, both, rows_in, d_gate_up, inner, d_expert, columns, hidden, cot, gates, ffn_gain, collective_id
):
    blocks, rows, width = part.shape
    both = both.reshape(blocks // 4, 2, 2, rows, -1)
    pair = (blocks // 4, 2, rows, both.shape[4])
    anywhere, vmem = pl.BlockSpec(memory_space=pl.ANY), pl.BlockSpec(memory_space=pltpu.VMEM)
    return pl.pallas_call(
        sum_all_kernel,
        out_shape=[
            jax.ShapeDtypeStruct((rows, width), part.dtype),
            jax.ShapeDtypeStruct(hidden.shape, jnp.float32),
            jax.ShapeDtypeStruct((8, hidden.shape[1]), jnp.float32),
            jax.ShapeDtypeStruct(pair, both.dtype),
            jax.ShapeDtypeStruct((rows_in.shape[1], d_gate_up.shape[1]), both.dtype),
            jax.ShapeDtypeStruct((inner.shape[1], d_expert.shape[1]), both.dtype),
        ],
        in_specs=[anywhere] * 7 + [vmem] * 4,
        out_specs=[vmem] * 3 + [anywhere] * 3,
        scratch_shapes=[
            pltpu.VMEM((rows, width), part.dtype),
            pltpu.VMEM((*columns.shape[:2], 128), part.dtype),
            pltpu.SemaphoreType.DMA,
            pltpu.VMEM(pair, both.dtype),
            pltpu.VMEM(pair, both.dtype),
            pltpu.VMEM((2, rows_in.shape[0], TILE), both.dtype),
            pltpu.VMEM((2, TILE, d_expert.shape[1]), both.dtype),
            pltpu.SemaphoreType.DMA((3,)),
            pltpu.SemaphoreType.DMA((2,)),
            pltpu.SemaphoreType.DMA((2,)),
            pltpu.SemaphoreType.DMA((2,)),
            *sum_all_scratch(rows, width),
        ],
        compiler_params=pltpu.CompilerParams(
            collective_id=collective_id, has_side_effects=True, vmem_limit_bytes=VMEM_LIMIT
        ),
        name="sum_all",
    )(
        part,
        both,
        rows_in,
        d_gate_up.reshape(*pair[:3], -1),
        inner,
        d_expert.reshape(*pair[:3], -1),
        columns,
        hidden,
        cot,
        gates,
        ffn_gain,
    )


def add_rows(target, source, count, chunk=32):
    @pl.loop(0, count // chunk)
    def _(i):
        at = pl.ds(pl.multiple_of(i * chunk, chunk), chunk)
        target[at, :] = target[at, :] + source[at, :]


def seq_peer(p, d):
    return ((p.z * 2 + p.x + d) % 8, p.y * 2 + p.c)


def greet_seq(p, sides=("y", "core")):
    barrier = pltpu.get_barrier_semaphore()
    for d in range(1, 8):
        pl.semaphore_signal(barrier, inc=1, device_id=seq_peer(p, d), device_id_type=MESH)
    for side in sides:
        target = {"y": p.by_y, "core": p.by_core}[side]
        pl.semaphore_signal(barrier, inc=1, device_id=target, device_id_type=MESH)
    pl.semaphore_wait(barrier, 7 + len(sides))


NT = (((1,), (1,)), ((), ()))
TILE = 256
WIDE = 512


def mxu(a, b, dims=(((1,), (0,)), ((), ()))):
    return lax.dot_general(a, b, dims, preferred_element_type=jnp.float32)


def experts_kernel(
    own, cot_all, w_in_hbm, w_down_hbm,
    rows_all, out_part, d_part, x_all, d_expert_all, inner_all, d_gate_up_all,
    w_in, w_down, row_buf, cot_buf, pick, pick_t, gates, d_gates, x, cot, d_expert,
    by_d_gate, by_d_up, inner, d_gate_up, held, out_stage, d_stage,
    ss, rs, zs, local_sem, load_sems, store_sems,
):
    p = Place()
    bf16, f32 = jnp.bfloat16, jnp.float32
    width = cot_all.shape[2]
    blocks = 8
    slots = gates.shape[0]
    capacity = slots // blocks
    tokens = row_buf.shape[2]
    group = 4
    experts = rows_all.shape[0]
    p.greet(("x", "y", "core", "z"))
    plane_out, plane_hop, plane_turn, plane_end, plane_core, finish = gather_steps(
        p, own, rows_all, ss, rs, zs, local_sem
    )

    def weights(start):
        for i, (src, dst) in enumerate(((w_in_hbm, w_in), (w_down_hbm, w_down))):
            copy = pltpu.make_async_copy(src, dst, load_sems.at[i])
            copy.start() if start else copy.wait()

    def cot_load(k):
        return pltpu.make_async_copy(
            cot_all.at[pl.ds(p.near(k) * blocks, blocks)], cot_buf.at[k % 2], load_sems.at[2 + k]
        )

    def row_load(k):
        return pltpu.make_async_copy(
            rows_all.at[pl.ds(p.near(k) * blocks, blocks)], row_buf.at[k % 2], load_sems.at[6 + k]
        )

    def arrived(k):
        plane_core(k)
        row_load(k).start()

    sides = (p.x, 1 - p.x)

    def side_load(i):
        at = pl.ds(sides[i] * group, group)
        source = rows_all.at[pl.ds(p.z * blocks + sides[i] * group, group)]
        return pltpu.make_async_copy(source, row_buf.at[0, at], load_sems.at[(6, 10)[i]])

    def side_arrived(i):
        plane_core(0, ((0, 2), (1, 3))[i])
        if i == 0:
            pltpu.make_async_copy(own, rows_all.at[p.me], local_sem).wait()
        side_load(i).start()

    at_slot = {}

    def store(k, i, src, dst):
        if (k, i) not in at_slot:
            at_slot[k, i] = pltpu.make_async_copy(src, dst, store_sems.at[i, k % 2])
        return at_slot[k, i]

    def stores(k):
        q = p.near(k)
        at = pl.ds(q * slots, slots)
        plane = pl.ds(q * blocks, blocks)
        return [
            (x, x_all.at[at]),
            (d_expert, d_expert_all.at[at]),
            (inner, inner_all.at[at]),
            (d_gate_up, d_gate_up_all.at[at]),
            (out_stage, out_part.at[plane]),
            (d_stage, d_part.at[plane]),
        ]

    def put(k, i):
        store(k, i, *stores(k)[i]).start()

    def free(k, i):
        if k > 0:
            store(k - 1, i, *stores(k - 1)[i]).wait()

    def pick_rows(k, g):
        lane = lax.broadcasted_iota(jnp.int32, (8, 128), 1)
        line = lax.broadcasted_iota(jnp.int32, (8, 128), 0)
        select = jnp.where((lane == line * experts + p.me) & (line < 3), 1.0, 0.0).astype(bf16)
        slot_id = lax.broadcasted_iota(jnp.int32, (capacity, tokens), 0).astype(f32) + 1.0
        rows, cots = row_buf.at[k % 2], cot_buf.at[k % 2]
        which = pl.ds(g * group, group)
        lines = mxu(select, rows[which, :, width:].reshape(group * tokens, 128), NT)
        for i in range(group):
            mine = lines[:, i * tokens : (i + 1) * tokens]
            chosen = jnp.where(mine[2:3] == slot_id, 1.0, 0.0)
            gate = jnp.sum(chosen * (mine[0:1] + mine[1:2]), axis=1, keepdims=True)
            at = pl.ds(pl.multiple_of((g * group + i) * capacity, capacity), capacity)
            gates[at, :] = jnp.broadcast_to(gate, (capacity, 128))
            lead = [jnp.zeros((capacity, tokens), bf16)] * i
            tail = [jnp.zeros((capacity, tokens), bf16)] * (group - 1 - i)
            pick[g, i * capacity : (i + 1) * capacity, :] = jnp.concatenate(
                lead + [chosen.astype(bf16)] + tail, axis=1
            )
            lead = [jnp.zeros((tokens, capacity), f32)] * i
            tail = [jnp.zeros((tokens, capacity), f32)] * (group - 1 - i)
            pick_t[g, i * tokens : (i + 1) * tokens, :] = jnp.concatenate(
                lead + [chosen.T] + tail, axis=1
            ).astype(bf16)
        at = slots_at(g)

        @pl.loop(0, width // WIDE)
        def _(n):
            cols = pl.ds(pl.multiple_of(n * WIDE, WIDE), WIDE)
            row_tile = rows[which, :, cols].reshape(group * tokens, WIDE)
            x[at, cols] = mxu(pick[g], row_tile).astype(bf16)
            cot_tile = cots[which, :, cols].reshape(group * tokens, WIDE)
            picked = mxu(pick[g], cot_tile)
            cot[at, cols] = picked.astype(bf16)
            scale = jnp.concatenate([gates[at, :]] * (WIDE // 128), axis=1)
            d_expert[at, cols] = (scale * picked).astype(bf16)

    def slots_at(g):
        if g is None:
            return pl.ds(0, slots)
        return pl.ds(pl.multiple_of(g * group * capacity, group * capacity), group * capacity)

    def up(g=None):
        ff = inner.shape[1]
        at = slots_at(g)

        @pl.loop(0, ff // TILE)
        def _(n):
            cols = pl.ds(pl.multiple_of(n * TILE, TILE), TILE)
            gate = mxu(x[at, :], w_in[:, cols])
            raised = mxu(x[at, :], w_in[:, pl.ds(pl.multiple_of(ff + n * TILE, TILE), TILE)])
            sig = jax.nn.sigmoid(gate)
            silu = gate * sig
            inner[at, cols] = (silu * raised).astype(bf16)
            by_d_up[at, cols] = silu
            by_d_gate[at, cols] = raised * sig * (1.0 + gate * (1.0 - sig))

    def d_up(g=None):
        ff = inner.shape[1]
        at = slots_at(g)

        @pl.loop(0, ff // TILE)
        def _(n):
            cols = pl.ds(pl.multiple_of(n * TILE, TILE), TILE)
            d_inner = mxu(d_expert[at, :], w_down[cols, :], NT)
            d_gate_up[at, cols] = (d_inner * by_d_gate[at, cols]).astype(bf16)
            d_gate_up[at, pl.ds(pl.multiple_of(ff + n * TILE, TILE), TILE)] = (
                d_inner * by_d_up[at, cols]
            ).astype(bf16)

    def spread(stage, sides_done=(0, 1)):
        @pl.loop(0, width // WIDE)
        def _(n):
            cols = pl.ds(pl.multiple_of(n * WIDE, WIDE), WIDE)
            for g in sides_done:
                result = mxu(pick_t[g], held[slots_at(g), cols]).astype(bf16)
                stage[pl.ds(g * group, group), :, cols] = result.reshape(group, tokens, WIDE)

    def down(g=None):
        at = slots_at(g)
        d_gates[at, :] = jnp.zeros_like(d_gates[at, :])

        @pl.loop(0, width // TILE)
        def _(n):
            cols = pl.ds(pl.multiple_of(n * TILE, TILE), TILE)
            result = mxu(inner[at, :], w_down[:, cols]).astype(bf16).astype(f32)
            product = result * cot[at, cols].astype(f32)
            total = product[:, :128]
            for j in range(1, TILE // 128):
                total = total + product[:, j * 128 : (j + 1) * 128]
            d_gates[at, :] += total
            scale = jnp.concatenate([gates[at, :]] * (TILE // 128), axis=1)
            held[at, cols] = (scale * result).astype(bf16)

    def d_down(g=None, sides_done=(0, 1)):
        for side in sides_done:
            at = slots_at(side)
            total = jnp.sum(d_gates[at, :], axis=1, keepdims=True)
            high = total.astype(bf16).astype(f32)
            lane = lax.broadcasted_iota(jnp.int32, (group * capacity, 128), 1)
            info = jnp.where(
                lane == p.me, high, jnp.where(lane == experts + p.me, total - high, 0.0)
            )
            result = mxu(pick_t[side], info.astype(bf16)).astype(bf16)
            d_stage[pl.ds(side * group, group), :, width:] = result.reshape(group, tokens, 128)
        at = slots_at(g)

        @pl.loop(0, width // TILE)
        def _(n):
            cols = pl.ds(pl.multiple_of(n * TILE, TILE), TILE)
            held[at, cols] = mxu(d_gate_up[at, :], w_in[cols, :], NT).astype(bf16)

    plane_out(0)
    weights(True)
    cot_load(0).start()
    plane_turn(0)
    side_arrived(0)
    plane_hop(1)
    plane_out(1)
    plane_hop(2)
    weights(False)
    cot_load(0).wait()
    cot_load(1).start()
    side_load(0).wait()
    side = sides[0]
    pick_rows(0, side)
    up(side)
    plane_end(0)
    d_up(side)
    down(side)
    plane_hop(3)
    side_arrived(1)
    spread(out_stage, (side,))
    d_down(side, (side,))
    plane_turn(1)
    plane_out(2)
    spread(d_stage, (side,))
    side_load(1).wait()
    side = sides[1]
    pick_rows(0, side)
    put(0, 0)
    put(0, 1)
    up(side)
    put(0, 2)
    plane_end(1)
    d_up(side)
    put(0, 3)
    down(side)
    spread(out_stage, (side,))
    put(0, 4)
    arrived(1)
    d_down(side, (side,))
    spread(d_stage, (side,))
    put(0, 5)
    after = {
        (1, 0): ((plane_turn, 2), (plane_out, 3)),
        (1, 3): ((plane_end, 2),),
        (1, 5): ((arrived, 2),),
        (2, 0): ((plane_turn, 3),),
        (2, 3): ((plane_end, 3),),
        (2, 5): ((arrived, 3),),
    }
    for k in range(1, 4):

        def service(i):
            for step, plane in after.get((k, i), ()):
                step(plane)

        row_load(k).wait()
        cot_load(k).wait()
        if k < 3:
            cot_load(k + 1).start()
        free(k, 0)
        free(k, 1)
        for g in range(2):
            pick_rows(k, g)
        put(k, 0)
        put(k, 1)
        service(0)
        free(k, 2)
        up()
        put(k, 2)
        service(1)
        free(k, 3)
        d_up()
        put(k, 3)
        service(2)
        free(k, 4)
        down()
        service(3)
        spread(out_stage)
        put(k, 4)
        service(4)
        free(k, 5)
        d_down()
        service(5)
        spread(d_stage)
        put(k, 5)
    for i in range(6):
        free(4, i)
    finish()


def experts_gathered(own, cot_all, w_in, w_down, capacity, collective_id):
    tokens, wide = own.shape
    experts, _, width = cot_all.shape
    ff = w_down.shape[0]
    slots = 8 * capacity
    dma = pltpu.SemaphoreType.DMA
    bf16, f32 = jnp.bfloat16, jnp.float32
    anywhere = pl.BlockSpec(memory_space=pl.ANY)

    def array(*shape):
        return jax.ShapeDtypeStruct(shape, bf16)

    return pl.pallas_call(
        experts_kernel,
        out_shape=[
            array(experts, tokens, wide),
            array(experts, tokens, width),
            array(experts, tokens, wide),
            array(experts * capacity, width),
            array(experts * capacity, width),
            array(experts * capacity, ff),
            array(experts * capacity, 2 * ff),
        ],
        in_specs=[anywhere] * 4,
        out_specs=[anywhere] * 7,
        scratch_shapes=[
            pltpu.VMEM(w_in.shape, bf16),
            pltpu.VMEM(w_down.shape, bf16),
            pltpu.VMEM((2, 8, tokens, wide), bf16),
            pltpu.VMEM((2, 8, tokens, width), bf16),
            pltpu.VMEM((2, 4 * capacity, 4 * tokens), bf16),
            pltpu.VMEM((2, 4 * tokens, 4 * capacity), bf16),
            pltpu.VMEM((slots, 128), f32),
            pltpu.VMEM((slots, 128), f32),
            pltpu.VMEM((slots, width), bf16),
            pltpu.VMEM((slots, width), bf16),
            pltpu.VMEM((slots, width), bf16),
            pltpu.VMEM((slots, ff), f32),
            pltpu.VMEM((slots, ff), f32),
            pltpu.VMEM((slots, ff), bf16),
            pltpu.VMEM((slots, 2 * ff), bf16),
            pltpu.VMEM((slots, width), bf16),
            pltpu.VMEM((8, tokens, width), bf16),
            pltpu.VMEM((8, tokens, wide), bf16),
            dma((4, G_KINDS)),
            dma((4, G_KINDS)),
            dma((4, 2)),
            dma,
            dma((11,)),
            dma((6, 2)),
        ],
        compiler_params=pltpu.CompilerParams(
            collective_id=collective_id, has_side_effects=True, vmem_limit_bytes=VMEM_LIMIT
        ),
        name="experts",
    )(own, cot_all, w_in, w_down)


TN = (((0,), (0,)), ((), ()))


def back_kernel(
    own, pair, rows_all, columns_hbm, normed_hbm, queries, keys, values, attended,
    q_raw, k_raw, cosine, sine, q_gain, k_gain, attn_gain, gains, tokens, d_hidden,
    d_tokens, d_qkv, d_out_t, d_router, gains_out, mixture,
    cols_out, d_attn, columns, normed, d_normed, d_heads, d_query, d_key, d_value, d_proj, logits, q_sum, k_sum,
    held, x_in, y_in, z_in, g_send, g_in, x_two, z_two, c_core, c_y,
    gs, gr, gz, load_sems, local_sem, hs, ys, yr, xs, xr, zs, zr, ts, tr,
    normed_sems, free, xs2, xr2, zs2, zr2, cs, cr, cys, cyr, as_, ar,
):
    p = Place()
    bf16, f32 = jnp.bfloat16, jnp.float32
    columns_z = [p.device((p.z + d) % 4, p.x, p.y, p.c) for d in (1, 2, 3)]
    greet_seq(p)
    rows, wide = own.shape
    length, head_cols = queries.shape
    heads = head_cols // HEAD_DIMENSION
    width = d_normed.shape[2]
    proj_cols = d_proj.shape[1]
    plane_rows = 2 * rows
    score_scale = 1.0 / math.sqrt(HEAD_DIMENSION)
    place, shard = p.z * 2 + p.x, p.y * 2 + p.c

    def rows_at(q, x):
        return d_attn.at[q * 2 + x]

    def gather_out(k):
        q = p.near(k)
        there = rows_at(q, p.x)
        if k == 0:
            src = own
            for step, end in ((1, p.high), (-1, p.low)):

                @pl.when(jnp.logical_not(end))
                def _():
                    send(src, there, gz.at[q, 0 if step > 0 else 1], gr.at[q, 0], p.by_z(step))

            pltpu.make_async_copy(own, there, local_sem).start()
        else:
            src = there

            @pl.when(jnp.logical_not(p.inner))
            def _():
                await_bytes(src, gr.at[q, 0])

        send(src, there, gs.at[q], gr.at[q, 1], p.by_x)

    def gather_hop(k):
        q = p.near(k)
        there = rows_at(q, p.x)

        @pl.when(p.inner)
        def _():
            await_bytes(there, gr.at[q, 0])
            send(there, there, gz.at[q, 0], gr.at[q, 0], p.by_z(p.onward(k)))

    def gather_in(k):
        if k == 0:
            pltpu.make_async_copy(own, rows_at(p.z, p.x), local_sem).wait()
        await_bytes(own, gr.at[p.near(k), 1])

    def at_pair(q, x, y):
        return pair.at[q * 4 + x * 2 + y]

    def sum_send(k):
        q = p.far(k)
        for j, x in ((1, 1 - p.x), (0, p.x)):
            i = q * 2 + j
            send(at_pair(q, x, 1 - p.y), y_in.at[k % 2 * 2 + j], ys.at[i], yr.at[i], p.by_y)

    def sum_start():
        sum_send(0)
        sum_send(1)
        for k in range(4):
            q = p.far(k)
            for j, x in ((1, 1 - p.x), (0, p.x)):
                pltpu.make_async_copy(at_pair(q, x, p.y), held.at[q * 2 + j], hs.at[q * 2 + j]).start()

    def sum_turn(k):
        q = p.far(k)
        for j in (1, 0):
            slot = q * 2 + j
            landed = y_in.at[k % 2 * 2 + j]
            await_bytes(held.at[slot], hs.at[slot])
            await_bytes(landed, yr.at[slot])
            add_rows(held.at[slot], landed, rows)
            if j == 1:
                send(held.at[slot], x_in.at[q], xs.at[q], xr.at[q], p.by_x)
        if k < 2:
            pl.semaphore_signal(free, inc=1, device_id=p.by_y, device_id_type=MESH)
            pl.semaphore_wait(free, 1)
            sum_send(k + 2)

    def line_sum(k, mine, landed, sends, arrivals):
        q = p.far(k)
        if k < 3:
            step = p.toward(k)
            slot, hops = (1 - step) // 2, (q - p.z) * step

            @pl.when(p.inner)
            def _():
                await_bytes(landed.at[slot, hops], arrivals.at[slot, hops])
                add_rows(mine, landed.at[slot, hops], rows)

            send(mine, landed.at[slot, hops - 1], sends.at[k], arrivals.at[slot, hops - 1], p.by_z(step))
        else:
            for slot, there in ((0, p.low), (1, p.high)):

                @pl.when(jnp.logical_not(there))
                def _():
                    await_bytes(landed.at[slot, 0], arrivals.at[slot, 0])
                    add_rows(mine, landed.at[slot, 0], rows)

    def sum_end(k):
        q = p.far(k)
        mine = held.at[q * 2]
        await_bytes(x_in.at[q], xr.at[q])
        add_rows(mine, x_in.at[q], rows)
        line_sum(k, mine, z_in, zs, zr)
        if k == 3:
            mixture[...] = mine[...]

    def two_start(*steps):
        for k in steps:
            q = p.far(k)
            send(d_normed.at[q * 2 + 1 - p.x], x_two.at[q], xs2.at[q], xr2.at[q], p.by_x)

    def two_end(k):
        q = p.far(k)
        mine = d_normed.at[q * 2 + p.x]
        await_bytes(x_two.at[q], xr2.at[q])
        add_rows(mine, x_two.at[q], rows)
        line_sum(k, mine, z_two, zs2, zr2)

    piece_rows = c_y.shape[1]
    order = [(place + d) % 8 for d in range(1, 9)]
    piece_width = c_y.shape[2]
    cols_at = cols_out.at[place]

    def cols_start():
        for turn, side in ((0, 1 - p.y), (1, p.y)):
            send(columns.at[:, side, 1 - p.c], c_core.at[turn], cs.at[turn], cr.at[turn], p.by_core)

    def cols_core():
        for turn, side in ((0, 1 - p.y), (1, p.y)):
            await_bytes(c_core.at[turn], cr.at[turn])
            for s in order:
                add_rows(columns.at[s, side, p.c], c_core.at[turn, s], piece_rows)
                if turn == 0:
                    send(columns.at[s, side, p.c], c_y.at[s], cys.at[s], cyr.at[s], p.by_y)

    def cols_turn(*steps):
        for i in steps:
            s = order[i]
            mine = columns.at[s, p.y, p.c]
            await_bytes(c_y.at[s], cyr.at[s])
            add_rows(mine, c_y.at[s], piece_rows)
            if i < 7:
                send(mine, cols_at, as_.at[i], ar.at[i], seq_peer(p, i + 1))
            else:
                pltpu.make_async_copy(mine, cols_at, as_.at[7]).start()

    def norm_back():
        mine = d_normed.at[p.z * 2 + p.x]
        chunk = 16

        @pl.loop(0, rows // chunk)
        def _(i):
            at = pl.ds(pl.multiple_of(i * chunk, chunk), chunk)
            d_out = mine[at, :].astype(f32)
            x = tokens[at, :].astype(f32)
            scale = lax.rsqrt(jnp.mean(x * x, axis=-1, keepdims=True) + EPS)
            u = d_out * attn_gain[...]
            dot = jnp.mean(u * x, axis=-1, keepdims=True)
            d_x = scale * u - x * (scale * scale * scale * dot)
            d_tokens[at, :] = (d_hidden[at, :] + d_x).astype(d_tokens.dtype)

    def attention(q):
        row_start = pl.multiple_of(q * plane_rows, plane_rows)
        at = pl.ds(row_start, plane_rows)

        @pl.loop(0, head_cols // TILE)
        def _(n):
            cols = pl.ds(pl.multiple_of(n * TILE, TILE), TILE)
            grad = d_attn[pl.ds(q * 2, 2), :, :width].reshape(plane_rows, width)
            weight_cols = pl.ds(pl.multiple_of(proj_cols + n * TILE, TILE), TILE)
            weight = columns[..., weight_cols].reshape(width, TILE)
            d_heads[at, cols] = mxu(grad, weight).astype(bf16)

        def block(count):
            key, value = keys[:count], values[:count]
            row_pos = row_start + lax.broadcasted_iota(jnp.int32, (plane_rows, count), 0)
            allowed = lax.broadcasted_iota(jnp.int32, (plane_rows, count), 1) <= row_pos

            @pl.loop(0, heads)
            def _(h):
                cols = pl.ds(pl.multiple_of(h * HEAD_DIMENSION, HEAD_DIMENSION), HEAD_DIMENSION)
                query, d_out = queries[at, cols], d_heads[at, cols]
                scores = jnp.where(allowed, mxu(query, key, NT) * score_scale, -1e30)
                raised = jnp.exp(scores - jnp.max(scores, axis=-1, keepdims=True))
                prob = raised / jnp.sum(raised, axis=-1, keepdims=True)
                d_prob = mxu(d_out, value, NT)
                delta = jnp.sum(prob * d_prob, axis=-1, keepdims=True)
                d_scores = (prob * (d_prob - delta)).astype(bf16)
                d_query[at, cols] = mxu(d_scores, key) * score_scale
                d_key[:count] += mxu(d_scores, query, TN) * score_scale
                d_value[:count] += mxu(prob.astype(bf16), d_out, TN)

        half = length // 2

        @pl.when(q < 2)
        def _():
            block(half)

        @pl.when(q >= 2)
        def _():
            block(length)

    def unrotate(grad, at):
        swapped = jnp.concatenate(
            [grad[:, HEAD_DIMENSION // 2 :], grad[:, : HEAD_DIMENSION // 2]], axis=1
        )
        return grad * cosine[at, :] + swapped * sine[at, :]

    def raw_grads():
        q_sum[...] = jnp.zeros_like(q_sum)
        k_sum[...] = jnp.zeros_like(k_sum)

        def one(grad, raw, gain, total, at):
            turned = unrotate(grad, at)
            scale = lax.rsqrt(jnp.mean(raw * raw, axis=-1, keepdims=True) + EPS)
            total[...] += jnp.sum((turned * raw * scale).reshape(-1, 8, HEAD_DIMENSION), axis=0)
            u = turned * gain[...]
            dot = jnp.mean(u * raw, axis=-1, keepdims=True)
            return (scale * u - raw * (scale * scale * scale * dot)).astype(bf16)

        chunk = 128

        @pl.loop(0, length // chunk)
        def _(i):
            at = pl.ds(pl.multiple_of(i * chunk, chunk), chunk)
            for h in range(heads):
                cols = slice(h * HEAD_DIMENSION, (h + 1) * HEAD_DIMENSION)
                d_proj[at, cols] = one(d_query[at, cols], q_raw[at, cols], q_gain, q_sum, at)
            d_proj[at, head_cols : head_cols + HEAD_DIMENSION] = one(
                d_key[at, :], k_raw[at, :], k_gain, k_sum, at
            )
            d_proj[at, head_cols + HEAD_DIMENSION :] = d_value[at, :].astype(bf16)

        g_send[0] = gains[...]
        g_send[0, 2:3, :HEAD_DIMENSION] = jnp.sum(q_sum[...], axis=0, keepdims=True)
        g_send[0, 2:3, HEAD_DIMENSION : 2 * HEAD_DIMENSION] = jnp.sum(
            k_sum[...], axis=0, keepdims=True
        )

    def normed_load(n, slot):
        cols = pl.ds(pl.multiple_of(n * TILE, TILE), TILE)
        return pltpu.make_async_copy(normed_hbm.at[:, cols], normed.at[slot], normed_sems.at[slot])

    def normed_grads():
        @pl.loop(0, width // TILE)
        def _(n):
            cols = pl.ds(pl.multiple_of(n * TILE, TILE), TILE)
            slot = n % 2
            normed_load(n, slot).wait()

            @pl.when(n + 1 < width // TILE)
            def _():
                normed_load(n + 1, 1 - slot).start()

            weight = columns[n, :, :, :, :proj_cols].reshape(TILE, proj_cols)
            part = mxu(d_proj[...], weight, NT)
            d_normed[:, :, cols] = part.astype(bf16).reshape(length // rows, rows, TILE)
            total = jnp.sum(part * normed[slot].astype(f32), axis=0, keepdims=True)
            g_send[0, 0:1, cols] = total / attn_gain[:, cols]
            grad = mxu(normed[slot], d_proj[...], TN).astype(bf16)
            columns[n, :, :, :, :proj_cols] = grad.reshape(2, 2, -1, proj_cols)

    def gains_pass(t, target):
        send(g_send.at[t], g_in.at[t], ts.at[t], tr.at[t], target)

    def gains_take(t):
        await_bytes(g_in.at[t], tr.at[t])
        g_send[t + 1] = g_send[t] + g_in[t]

    def gains_z_pass():
        g_in[2 + p.z] = g_send[2]
        for d, target in enumerate(columns_z):
            send(g_send.at[2], g_in.at[2 + p.z], ts.at[2 + d], tr.at[2 + d], target)

    def gains_z_take():
        for d in range(3):
            await_bytes(g_in.at[0], tr.at[2 + d])
        g_send[3] = g_in[2] + g_in[3] + g_in[4] + g_in[5]

    def column_grads(value, first, count):
        @pl.loop(0, width // TILE)
        def _(n):
            cols = pl.ds(pl.multiple_of(n * TILE, TILE), TILE)
            part = d_attn[:, :, cols].reshape(length, TILE)
            grad = mxu(part, value[...], TN).astype(bf16)
            columns[n, :, :, :, first : first + count] = grad.reshape(2, 2, -1, count)

    loads = [
        pltpu.make_async_copy(columns_hbm, columns, load_sems.at[0]),
        pltpu.make_async_copy(rows_all.at[:, shard], d_attn, load_sems.at[1]),
    ]
    gather_out(0)
    loads[0].start()
    normed_load(0, 0).start()
    sum_start()
    d_key[...] = jnp.zeros_like(d_key)
    d_value[...] = jnp.zeros_like(d_value)
    loads[0].wait()
    gather_in(0)
    gather_hop(1)
    gather_out(1)
    gather_hop(2)
    attention(p.near(0))
    gather_out(2)
    gather_hop(3)
    gather_in(1)
    attention(p.near(1))
    sum_turn(0)
    gather_out(3)
    gather_in(2)
    attention(p.near(2))
    sum_end(0)
    sum_turn(1)
    gather_in(3)
    attention(p.near(3))
    raw_grads()
    sum_end(1)
    normed_grads()
    gains_pass(0, p.by_core)
    column_grads(attended, proj_cols, head_cols)
    gains_take(0)
    gains_pass(1, p.by_x)
    two_start(0, 1)
    line = lax.broadcasted_iota(jnp.int32, (128, 128), 0)
    lane = lax.broadcasted_iota(jnp.int32, (128, 128), 1)
    router_cols = rows_all.shape[0] * rows_all.shape[1] // 8
    mine = (line == lane + place * router_cols) & (lane < router_cols)
    select = jnp.where(mine, 1.0, 0.0).astype(bf16)
    logits[...] = mxu(d_attn[:, :, width:].reshape(length, 128), select).astype(bf16)
    for q in range(4):
        await_bytes(own, gs.at[q])
    for there, slot in ((p.high, 0), (p.low, 1)):

        @pl.when(jnp.logical_not(there))
        def _():
            await_bytes(own, gz.at[p.z, slot])

    for k in range(1, 4):

        @pl.when(p.inner)
        def _():
            await_bytes(own, gz.at[p.near(k), 0])

    loads[1].start()
    loads[1].wait()
    column_grads(logits, proj_cols + head_cols, 128)
    cols_start()
    gains_take(1)
    gains_z_pass()
    sum_turn(2)
    two_start(2, 3)
    cols_core()
    two_end(0)
    sum_turn(3)
    gains_z_take()
    send(g_send.at[3], g_in.at[6], ts.at[5], tr.at[5], p.by_y)
    two_end(1)
    cols_turn(0, 1)
    sum_end(2)
    cols_turn(2, 3, 4, 5)
    two_end(2)
    cols_turn(6, 7)
    two_end(3)
    norm_back()
    sum_end(3)
    await_bytes(g_in.at[6], tr.at[5])
    gains_out[...] = g_send[3] + g_in[6]
    for t in range(6):
        await_bytes(g_in.at[0], ts.at[t])
    piece = x_in.at[0]
    for i in range(8):
        await_bytes(piece, ys.at[i])
    for q in range(4):
        await_bytes(piece, xs.at[q])
    for k in range(3):
        await_bytes(piece, zs.at[k])
        await_bytes(piece, zs2.at[k])
    for q in range(4):
        await_bytes(piece, xs2.at[q])
    for i in range(8):
        if i < 7:
            await_bytes(c_y.at[0], ar.at[i])
        await_bytes(c_y.at[0], as_.at[i])
        await_bytes(c_y.at[0], cys.at[i])
    for turn in range(2):
        await_bytes(c_core.at[turn], cs.at[turn])
    key_cols = KEY_VALUE_HEADS * HEAD_DIMENSION
    per_group = 8 // KEY_VALUE_HEADS
    router_total = jnp.zeros((piece_rows, 128), f32)
    for s in range(8):
        d_qkv[:, s * head_cols : (s + 1) * head_cols] = cols_out[s, :, :head_cols].astype(f32)
        d_out_t[:, s * head_cols : (s + 1) * head_cols] = cols_out[
            s, :, proj_cols : proj_cols + head_cols
        ].astype(f32)
        part = cols_out[s, :, proj_cols + head_cols :].astype(f32)
        router_total = router_total + (pltpu.roll(part, s * router_cols, 1) if s else part)
    d_router[...] = router_total
    for g in range(KEY_VALUE_HEADS):
        for j in range(2):
            lanes = slice(head_cols + j * HEAD_DIMENSION, head_cols + (j + 1) * HEAD_DIMENSION)
            total = cols_out[g * per_group, :, lanes].astype(f32)
            for s in range(1, per_group):
                total = total + cols_out[g * per_group + s, :, lanes].astype(f32)
            first = 8 * head_cols + j * key_cols + g * HEAD_DIMENSION
            d_qkv[:, first : first + HEAD_DIMENSION] = total


def back(
    own, pair, rows_all, columns, normed, queries, keys, values, attended,
    q_raw, k_raw, cosine, sine, q_gain, k_gain, attn_gain, gains, tokens, d_hidden,
    collective_id,
):
    rows, wide = own.shape
    length, head_cols = queries.shape
    width = normed.shape[1]
    piece_rows, piece_width = columns.shape[3:]
    proj_cols = head_cols + 2 * HEAD_DIMENSION
    dma = pltpu.SemaphoreType.DMA
    bf16, f32 = jnp.bfloat16, jnp.float32
    anywhere, vmem = pl.BlockSpec(memory_space=pl.ANY), pl.BlockSpec(memory_space=pltpu.VMEM)
    return pl.pallas_call(
        back_kernel,
        out_shape=[
            jax.ShapeDtypeStruct((rows, width), bf16),
            jax.ShapeDtypeStruct((piece_rows, 8 * head_cols + 2 * KEY_VALUE_HEADS * HEAD_DIMENSION), f32),
            jax.ShapeDtypeStruct((piece_rows, 8 * head_cols), f32),
            jax.ShapeDtypeStruct((piece_rows, 128), f32),
            jax.ShapeDtypeStruct(gains.shape, f32),
            jax.ShapeDtypeStruct((rows, width), bf16),
        ],
        in_specs=[anywhere] * 5 + [vmem] * 14,
        out_specs=[vmem] * 6,
        scratch_shapes=[
            pltpu.VMEM((8, piece_rows, piece_width), bf16),
            pltpu.VMEM((8, rows, wide), bf16),
            pltpu.VMEM(columns.shape, bf16),
            pltpu.VMEM((2, length, TILE), bf16),
            pltpu.VMEM((length // rows, rows, width), bf16),
            pltpu.VMEM((length, head_cols), bf16),
            pltpu.VMEM((length, head_cols), f32),
            pltpu.VMEM((length, HEAD_DIMENSION), f32),
            pltpu.VMEM((length, HEAD_DIMENSION), f32),
            pltpu.VMEM((length, proj_cols), bf16),
            pltpu.VMEM((length, 128), bf16),
            pltpu.VMEM((8, HEAD_DIMENSION), f32),
            pltpu.VMEM((8, HEAD_DIMENSION), f32),
            pltpu.VMEM((8, rows, width), bf16),
            pltpu.VMEM((4, rows, width), bf16),
            pltpu.VMEM((4, rows, width), bf16),
            pltpu.VMEM((2, 3, rows, width), bf16),
            pltpu.VMEM((4, *gains.shape), f32),
            pltpu.VMEM((7, *gains.shape), f32),
            pltpu.VMEM((4, rows, width), bf16),
            pltpu.VMEM((2, 3, rows, width), bf16),
            pltpu.VMEM((2, 8, piece_rows, piece_width), bf16),
            pltpu.VMEM((8, piece_rows, piece_width), bf16),
            dma((4,)),
            dma((4, 2)),
            dma((4, 2)),
            dma((2,)),
            dma,
            dma((8,)),
            dma((8,)),
            dma((8,)),
            dma((4,)),
            dma((4,)),
            dma((3,)),
            dma((2, 3)),
            dma((6,)),
            dma((6,)),
            dma((2,)),
            pltpu.SemaphoreType.REGULAR,
            dma((4,)),
            dma((4,)),
            dma((3,)),
            dma((2, 3)),
            dma((2,)),
            dma((2,)),
            dma((8,)),
            dma((8,)),
            dma((8,)),
            dma((7,)),
        ],
        compiler_params=pltpu.CompilerParams(
            collective_id=collective_id, has_side_effects=True, vmem_limit_bytes=VMEM_LIMIT
        ),
        name="back",
    )(
        own, pair, rows_all, columns, normed, queries, keys, values, attended,
        q_raw, k_raw, cosine, sine, q_gain, k_gain, attn_gain, gains, tokens, d_hidden,
    )


C_Z, C_X, C_Y, C_C, C_KINDS = 0, 1, 2, 4, 8


def front_kernel(
    tokens, pieces, cot, cosine, sine, q_gain, k_gain, attn_gain, ffn_gain, routes,
    normed_out, columns_out, cot_all, queries, keys, values, attended, q_raw, k_raw, hidden, gates, routed,
    own, normed, columns, part, x_in, z_in,
    ss, rs, zs, cs, cr, ys, yr, ks, kr, local_sems, gs, gr, gz, xs, xr, us, ur,
):
    p = Place()
    bf16 = jnp.bfloat16
    greet_seq(p)
    place, shard = p.z * 2 + p.x, p.y * 2 + p.c
    mine = place * 4 + shard
    rows, width = own.shape
    length, head_cols = queries.shape
    heads = head_cols // HEAD_DIMENSION
    proj_cols = head_cols + 2 * HEAD_DIMENSION
    plane_rows = 2 * rows
    score_scale = 1.0 / math.sqrt(HEAD_DIMENSION)

    x = tokens[...].astype(jnp.float32)
    scale = lax.rsqrt(jnp.mean(x * x, axis=-1, keepdims=True) + EPS)
    own[...] = (x * scale * attn_gain[...]).astype(bf16)

    def rows_at(q, x):
        return normed.at[q * 2 + x]

    def rows_move(k):
        q = p.near(k)
        there = rows_at(q, p.x)
        if k == 0:
            src = own
            for step, end in ((1, p.high), (-1, p.low)):

                @pl.when(jnp.logical_not(end))
                def _():
                    send(src, there, zs.at[q, 0 if step > 0 else 1], rs.at[q, 0], p.by_z(step))

            pltpu.make_async_copy(own, there, local_sems.at[0]).start()
        else:
            src = there

            @pl.when(jnp.logical_not(p.inner))
            def _():
                await_bytes(src, rs.at[q, 0])

        send(src, there, ss.at[q], rs.at[q, 1], p.by_x)

    def rows_hop(k):
        q = p.near(k)
        there = rows_at(q, p.x)

        @pl.when(p.inner)
        def _():
            await_bytes(there, rs.at[q, 0])
            send(there, there, zs.at[q, 0], rs.at[q, 0], p.by_z(p.onward(k)))

    def pass_on(d):
        block = ((place + 8 - d) % 8) * 4 + shard
        src = pieces.at[place] if d == 0 else columns.at[block]
        if d > 0:
            await_bytes(src, cr.at[d])
        send(src, columns.at[block], ys.at[d], yr.at[d], p.by_y)
        send(src, columns.at[block], ks.at[0, d], kr.at[0, d], p.by_core)

    def pass_across(d):
        block = columns.at[((place + 8 - d) % 8) * 4 + (1 - p.y) * 2 + p.c]
        await_bytes(block, yr.at[d])
        send(block, block, ks.at[1, d], kr.at[1, d], p.by_core)

    def cot_at(q, x, y):
        return cot_all.at[p.block(q, x, y, p.c)]

    def cot_core(q, j, src):
        x, y = (p.x, 1 - p.x)[j % 2], (p.y, 1 - p.y)[j // 2]
        send(src, cot_at(q, x, y), gs.at[q, C_C + j], gr.at[q, C_C + j], p.by_core)

    def cot_move(k):
        q = p.near(k)
        there = cot_at(q, p.x, p.y)
        if k == 0:
            src = cot
            for step, end in ((1, p.high), (-1, p.low)):

                @pl.when(jnp.logical_not(end))
                def _():
                    send(src, there, gz.at[q, 0 if step > 0 else 1], gr.at[q, C_Z], p.by_z(step))

            pltpu.make_async_copy(cot, there, local_sems.at[2]).start()
        else:
            src = there

            @pl.when(jnp.logical_not(p.inner))
            def _():
                await_bytes(src, gr.at[q, C_Z])

        send(src, there, gs.at[q, C_Y], gr.at[q, C_Y], p.by_y)
        send(src, there, gs.at[q, C_X], gr.at[q, C_X], p.by_x)
        cot_core(q, 0, src)

    def cot_hop(k):
        q = p.near(k)
        there = cot_at(q, p.x, p.y)

        @pl.when(p.inner)
        def _():
            await_bytes(there, gr.at[q, C_Z])
            send(there, there, gz.at[q, 0], gr.at[q, C_Z], p.by_z(p.onward(k)))

    def cot_turn(k):
        q = p.near(k)
        there = cot_at(q, 1 - p.x, p.y)
        await_bytes(there, gr.at[q, C_X])
        send(there, there, gs.at[q, C_Y + 1], gr.at[q, C_Y + 1], p.by_y)
        cot_core(q, 1, there)

    def cot_end(k):
        q = p.near(k)
        for j, x in ((0, p.x), (1, 1 - p.x)):
            there = cot_at(q, x, 1 - p.y)
            await_bytes(there, gr.at[q, C_Y + j])
            cot_core(q, 2 + j, there)

    def sum_end(k):
        q = p.far(k)
        held = part.at[q * 2 + p.x]
        await_bytes(x_in.at[q], xr.at[q])
        add_rows(held, x_in.at[q], rows)
        if k < 3:
            step = p.toward(k)
            slot = (1 - step) // 2

            @pl.when(p.inner)
            def _():
                await_bytes(z_in.at[slot, q], ur.at[slot, q])
                add_rows(held, z_in.at[slot, q], rows)

            send(held, z_in.at[slot, q], us.at[k], ur.at[slot, q], p.by_z(step))
        else:
            for slot, there in ((0, p.low), (1, p.high)):

                @pl.when(jnp.logical_not(there))
                def _():
                    await_bytes(z_in.at[slot, q], ur.at[slot, q])
                    add_rows(held, z_in.at[slot, q], rows)

    def route():
        total = tokens[...].astype(jnp.float32) + part[p.z * 2 + p.x].astype(jnp.float32)
        hidden[...] = total
        scale = lax.rsqrt(jnp.mean(total * total, axis=-1, keepdims=True) + EPS)
        routed[:, :width] = (total * scale * ffn_gain[...]).astype(bf16)
        router = columns[:, :, proj_cols + head_cols :].reshape(width, 128)
        logits = mxu(routed[:, :width], router)
        lane = lax.broadcasted_iota(jnp.int32, (rows, 128), 1)
        line = lax.broadcasted_iota(jnp.int32, (rows, 128), 0)
        turned = routes[...].astype(jnp.float32).T
        lanes = lane.astype(jnp.float32)
        named = lanes == turned[:, 0:1]
        for k in range(1, TOPK):
            named = named | (lanes == turned[:, k : k + 1])
        chosen = jnp.where(named, logits, -1e30)
        raised = jnp.where(named, jnp.exp(chosen - jnp.max(chosen, axis=-1, keepdims=True)), 0.0)
        gate = raised / jnp.sum(raised, axis=-1, keepdims=True)
        gates[...] = gate
        counted = jnp.where(named, 1.0, 0.0)
        slot = counted * mxu(jnp.where(lane <= line, 1.0, 0.0).astype(bf16), counted.astype(bf16))
        high = gate.astype(bf16).astype(jnp.float32)
        experts = columns.shape[0]
        info = high + pltpu.roll(gate - high, experts, 1) + pltpu.roll(slot, 2 * experts, 1)
        routed[:, width:] = info.astype(bf16)

    def project(n):
        cols = slice(n * TILE, (n + 1) * TILE)
        weight = columns[:, :, cols].reshape(width, TILE)
        result = mxu(normed[...].reshape(length, width), weight)
        if n * TILE < head_cols:
            q_raw[:, cols] = result
        else:
            k_raw[...] = result[:, :HEAD_DIMENSION]
            values[...] = result[:, HEAD_DIMENSION:].astype(bf16)

    def prepare():
        def one(raw, gain, at):
            scaled = raw * lax.rsqrt(jnp.mean(raw * raw, axis=-1, keepdims=True) + EPS) * gain[...]
            swapped = jnp.concatenate(
                [scaled[:, HEAD_DIMENSION // 2 :], scaled[:, : HEAD_DIMENSION // 2]], axis=1
            )
            return (scaled * cosine[at, :] - swapped * sine[at, :]).astype(bf16)

        chunk = 128

        @pl.loop(0, length // chunk)
        def _(i):
            at = pl.ds(pl.multiple_of(i * chunk, chunk), chunk)
            for h in range(heads):
                cols = slice(h * HEAD_DIMENSION, (h + 1) * HEAD_DIMENSION)
                queries[at, cols] = one(q_raw[at, cols], q_gain, at)
            keys[at, :] = one(k_raw[at, :], k_gain, at)

    def attention(k):
        q = p.far(k)
        row_start = pl.multiple_of(q * plane_rows, plane_rows)
        at = pl.ds(row_start, plane_rows)

        def block(count):
            row_pos = row_start + lax.broadcasted_iota(jnp.int32, (plane_rows, count), 0)
            allowed = lax.broadcasted_iota(jnp.int32, (plane_rows, count), 1) <= row_pos

            @pl.loop(0, heads)
            def _(h):
                cols = pl.ds(pl.multiple_of(h * HEAD_DIMENSION, HEAD_DIMENSION), HEAD_DIMENSION)
                scores = mxu(queries[at, cols], keys[:count], NT) * score_scale
                scores = jnp.where(allowed, scores, -1e30)
                raised = jnp.exp(scores - jnp.max(scores, axis=-1, keepdims=True))
                prob = raised / jnp.sum(raised, axis=-1, keepdims=True)
                attended[at, cols] = mxu(prob.astype(bf16), values[:count]).astype(bf16)

        @pl.when(q < 2)
        def _():
            block(length // 2)

        @pl.when(q >= 2)
        def _():
            block(length)

        per_tile = TILE // columns.shape[1]

        @pl.loop(0, width // TILE)
        def _(n):
            cols = pl.ds(pl.multiple_of(n * TILE, TILE), TILE)
            weight = columns[pl.ds(n * per_tile, per_tile), :, proj_cols : proj_cols + head_cols]
            result = mxu(attended[at, :], weight.reshape(TILE, head_cols), NT).astype(bf16)
            part[pl.ds(q * 2, 2), :, cols] = result.reshape(2, rows, TILE)

        send(part.at[q * 2 + 1 - p.x], x_in.at[q], xs.at[q], xr.at[q], p.by_x)

    rows_move(0)
    for d in range(1, 8):
        send(pieces.at[(place + d) % 8], columns.at[mine], cs.at[d], cr.at[d], seq_peer(p, d))
    pltpu.make_async_copy(pieces.at[place], columns.at[mine], local_sems.at[1]).start()
    pass_on(0)
    rows_hop(1)
    rows_move(1)
    for d in (1, 2, 7):
        pass_on(d)
    rows_hop(2)
    rows_move(2)
    cot_move(0)
    for d in (6, 3, 5):
        pass_on(d)
    rows_hop(3)
    rows_move(3)
    pass_on(4)
    for d in (0, 1, 2, 7, 6, 3, 5, 4):
        pass_across(d)
    cot_hop(1)
    cot_move(1)
    for k in range(4):
        await_bytes(own, rs.at[p.near(k), 1])
    pltpu.make_async_copy(own, rows_at(p.z, p.x), local_sems.at[0]).wait()
    pltpu.make_async_copy(pieces.at[place], columns.at[mine], local_sems.at[1]).wait()
    piece = pieces.at[0]
    for d in range(8):
        await_bytes(piece, kr.at[0, d])
        await_bytes(piece, kr.at[1, d])
    pltpu.make_async_copy(normed, normed_out, local_sems.at[0]).start()
    pltpu.make_async_copy(columns, columns_out, local_sems.at[1]).start()
    cot_turn(0)
    for n in range(proj_cols // TILE):
        project(n)
    cot_hop(2)
    cot_move(2)
    prepare()
    cot_turn(1)
    attention(0)
    cot_end(0)
    attention(1)
    cot_hop(3)
    cot_move(3)
    sum_end(0)
    attention(2)
    cot_turn(2)
    cot_end(1)
    sum_end(1)
    attention(3)
    cot_turn(3)
    sum_end(2)
    cot_end(2)
    sum_end(3)
    cot_end(3)
    route()
    for q in range(4):
        for j in range(4):
            await_bytes(cot, gr.at[q, C_C + j])
            await_bytes(cot, gs.at[q, C_C + j])
        for kind in (C_X, C_Y, C_Y + 1):
            await_bytes(cot, gs.at[q, kind])
        await_bytes(own, ss.at[q])
        await_bytes(own, xs.at[q])
    for there, slot in ((p.high, 0), (p.low, 1)):

        @pl.when(jnp.logical_not(there))
        def _():
            await_bytes(own, zs.at[p.z, slot])
            await_bytes(cot, gz.at[p.z, slot])

    for k in range(1, 4):

        @pl.when(p.inner)
        def _():
            await_bytes(own, zs.at[p.near(k), 0])
            await_bytes(cot, gz.at[p.near(k), 0])

    for k in range(3):
        await_bytes(own, us.at[k])
    for d in range(8):
        if d > 0:
            await_bytes(piece, cs.at[d])
        await_bytes(piece, ys.at[d])
        await_bytes(piece, ks.at[0, d])
        await_bytes(piece, ks.at[1, d])
    pltpu.make_async_copy(cot, cot_at(p.z, p.x, p.y), local_sems.at[2]).wait()
    pltpu.make_async_copy(normed, normed_out, local_sems.at[0]).wait()
    pltpu.make_async_copy(columns, columns_out, local_sems.at[1]).wait()


def front(
    tokens, pieces, cot, cosine, sine, q_gain, k_gain, attn_gain, ffn_gain, routes, head_cols, collective_id
):
    dma = pltpu.SemaphoreType.DMA
    bf16, f32 = jnp.bfloat16, jnp.float32
    rows, width = tokens.shape
    count, piece_rows, piece_width = pieces.shape
    length = count * rows
    anywhere, vmem = pl.BlockSpec(memory_space=pl.ANY), pl.BlockSpec(memory_space=pltpu.VMEM)
    return pl.pallas_call(
        front_kernel,
        out_shape=[
            jax.ShapeDtypeStruct((count, rows, width), bf16),
            jax.ShapeDtypeStruct((count * 4, piece_rows, piece_width), bf16),
            jax.ShapeDtypeStruct((count * 4, rows, width), bf16),
            jax.ShapeDtypeStruct((length, head_cols), bf16),
            jax.ShapeDtypeStruct((length, HEAD_DIMENSION), bf16),
            jax.ShapeDtypeStruct((length, HEAD_DIMENSION), bf16),
            jax.ShapeDtypeStruct((length, head_cols), bf16),
            jax.ShapeDtypeStruct((length, head_cols), f32),
            jax.ShapeDtypeStruct((length, HEAD_DIMENSION), f32),
            jax.ShapeDtypeStruct((rows, width), f32),
            jax.ShapeDtypeStruct((rows, 128), f32),
            jax.ShapeDtypeStruct((rows, width + 128), bf16),
        ],
        in_specs=[vmem] + [anywhere] * 2 + [vmem] * 7,
        out_specs=[anywhere] * 3 + [vmem] * 9,
        scratch_shapes=[
            pltpu.VMEM((rows, width), bf16),
            pltpu.VMEM((count, rows, width), bf16),
            pltpu.VMEM((count * 4, piece_rows, piece_width), bf16),
            pltpu.VMEM((count, rows, width), bf16),
            pltpu.VMEM((4, rows, width), bf16),
            pltpu.VMEM((2, 4, rows, width), bf16),
            dma((4,)),
            dma((4, 2)),
            dma((4, 2)),
            dma((8,)),
            dma((8,)),
            dma((8,)),
            dma((8,)),
            dma((2, 8)),
            dma((2, 8)),
            dma((3,)),
            dma((4, C_KINDS)),
            dma((4, C_KINDS)),
            dma((4, 2)),
            dma((4,)),
            dma((4,)),
            dma((3,)),
            dma((2, 4)),
        ],
        compiler_params=pltpu.CompilerParams(
            collective_id=collective_id, has_side_effects=True, vmem_limit_bytes=VMEM_LIMIT
        ),
        name="front",
    )(tokens, pieces, cot, cosine, sine, q_gain, k_gain, attn_gain, ffn_gain, routes)


def head_columns(weight, group_index):
    rows = weight.shape[0]
    query_width = QUERY_HEADS * HEAD_DIMENSION
    key_width = KEY_VALUE_HEADS * HEAD_DIMENSION
    query = weight[:, :query_width].reshape(rows, len(group_index), -1).transpose(1, 0, 2)
    keys = weight[:, query_width : query_width + key_width].reshape(rows, KEY_VALUE_HEADS, -1)
    values = weight[:, query_width + key_width :].reshape(rows, KEY_VALUE_HEADS, -1)
    keys = jnp.stack([keys[:, group] for group in group_index])
    values = jnp.stack([values[:, group] for group in group_index])
    return jnp.concatenate([query, keys, values], axis=2)


def gathered_body(
    tokens,
    query_key_value_weight,
    w_out_t,
    w_router,
    w_in,
    w_down,
    attn_gain,
    ffn_gain,
    q_gain,
    k_gain,
    routes,
    cotangent,
):
    bf16, f32 = jnp.bfloat16, jnp.float32
    both = ("seq", "fsdp")
    seq_size = lax.axis_size("seq")
    shard_size = lax.axis_size("fsdp")
    experts = seq_size * shard_size
    rows = tokens.shape[1]
    width = tokens.shape[2]
    length = rows * seq_size
    weight_rows = query_key_value_weight.shape[0]
    heads = QUERY_HEADS // seq_size
    head_cols = heads * HEAD_DIMENSION
    kv_cols = HEAD_DIMENSION
    proj_cols = head_cols + 2 * kv_cols
    all_cols = proj_cols + head_cols
    spare_cols = 128
    group_index = [s * heads * KEY_VALUE_HEADS // QUERY_HEADS for s in range(seq_size)]
    capacity = 2 * rows * TOPK // experts

    pieces = jnp.concatenate(
        [
            head_columns(query_key_value_weight, group_index),
            w_out_t.reshape(weight_rows, seq_size, head_cols).transpose(1, 0, 2),
            jnp.broadcast_to(
                jnp.pad(w_router, ((0, 0), (0, spare_cols - experts))),
                (seq_size, weight_rows, spare_cols),
            ),
        ],
        axis=2,
    )
    half_dim = HEAD_DIMENSION // 2
    exponents = -2.0 * np.arange(half_dim, dtype=np.float32) / HEAD_DIMENSION
    frequency = np.float32(ROPE_BASE) ** exponents.astype(np.float32)
    angles = np.arange(length, dtype=np.float32)[:, None] * frequency[None, :]
    cosine, sine = np.cos(angles), np.sin(angles)
    cosine = jnp.asarray(np.concatenate([cosine, cosine], axis=1), f32)
    sine = jnp.asarray(np.concatenate([sine, -sine], axis=1), f32)
    (
        normed_all,
        columns,
        cot_all,
        queries,
        keys,
        values,
        attended,
        q_raw,
        k_raw,
        hidden,
        gates,
        routed,
    ) = front(
        tokens[0],
        pieces,
        cotangent[0],
        cosine,
        sine,
        q_gain[None],
        k_gain[None],
        attn_gain[None],
        ffn_gain[None],
        routes[0].T,
        head_cols,
        1,
    )
    normed_all = normed_all.reshape(length, width)

    gate_weight = w_in[0]
    down_weight = w_down[0]
    rows_all, out_part, d_part, rows_in, d_expert, inner_act, d_gate_up = experts_gathered(
        routed,
        cot_all,
        gate_weight,
        down_weight,
        capacity,
        3,
    )
    d_send, d_hidden, gains, out_pair, d_w_in, d_w_down = sum_all(
        d_part,
        out_part,
        rows_in,
        d_gate_up,
        inner_act,
        d_expert,
        columns,
        hidden,
        cotangent[0],
        gates,
        ffn_gain[None],
        5,
    )
    d_w_in, d_w_down = d_w_in.astype(f32)[None], d_w_down.astype(f32)[None]

    d_tokens, d_w_qkv, d_w_out_t, d_w_router, gains, mixture = back(
        d_send,
        out_pair.reshape(2 * seq_size, rows, width),
        rows_all.reshape(seq_size, shard_size, rows, -1),
        columns.reshape(seq_size, 2, shard_size // 2, weight_rows, all_cols + spare_cols),
        normed_all,
        queries,
        keys,
        values,
        attended,
        q_raw,
        k_raw,
        cosine,
        sine,
        q_gain[None],
        k_gain[None],
        attn_gain[None],
        gains,
        tokens[0],
        d_hidden,
        6,
    )
    output = (hidden + mixture.astype(f32)).astype(bf16)
    d_tokens = d_tokens[None]
    d_w_router = d_w_router[:, :experts]
    d_attn_gain, d_ffn_gain = gains[0], gains[1]
    d_q_gain = gains[2, :HEAD_DIMENSION]
    d_k_gain = gains[2, HEAD_DIMENSION : 2 * HEAD_DIMENSION]
    return (
        output[None],
        d_tokens,
        d_w_qkv,
        d_w_out_t,
        d_w_router,
        d_w_in,
        d_w_down,
        d_attn_gain,
        d_ffn_gain,
        d_q_gain,
        d_k_gain,
    )


def gathered_fits(mesh):
    return mesh.shape["seq"] == 8 and mesh.shape["fsdp"] == 4


def solution(mesh):
    return jax.shard_map(
        gathered_body if gathered_fits(mesh) else routed_body,
        mesh=mesh,
        in_specs=(
            P("fsdp", "seq", None),
            P(("seq", "fsdp"), None),
            P(("seq", "fsdp"), None),
            P(("seq", "fsdp"), None),
            P(("seq", "fsdp"), None, None),
            P(("seq", "fsdp"), None, None),
            P(),
            P(),
            P(),
            P(),
            P("fsdp", "seq", None),
            P("fsdp", "seq", None),
        ),
        out_specs=(
            P("fsdp", "seq", None),
            P("fsdp", "seq", None),
            P(("seq", "fsdp"), None),
            P(("seq", "fsdp"), None),
            P(("seq", "fsdp"), None),
            P(("seq", "fsdp"), None, None),
            P(("seq", "fsdp"), None, None),
            P(),
            P(),
            P(),
            P(),
        ),
        check_vma=False,
    )
```

```python
from functools import partial
import math

import jax
import jax.numpy as jnp
import numpy as np
from jax import lax
from jax.experimental import pallas as pl
from jax.experimental.pallas import tpu as pltpu
from jax.sharding import PartitionSpec as P

QUERY_HEADS = 32
KEY_VALUE_HEADS = 4
HEAD_DIMENSION = 128
FF = 768
TOPK = 8


EPS = 1e-06
ROPE_BASE = 1000000.0


def rms_scale(values, gain):
    return values * lax.rsqrt(jnp.mean(values * values, axis=-1, keepdims=True) + EPS) * gain


def rotate(values, positions):
    half_dim = values.shape[-1] // 2
    frequency = ROPE_BASE ** (-2.0 * jnp.arange(half_dim, dtype=jnp.float32) / values.shape[-1])
    angles = positions.astype(jnp.float32)[:, None] * frequency[None, :]
    cosine = jnp.cos(angles)[:, None, :]
    sine_part = jnp.sin(angles)[:, None, :]
    first_half = values[..., :half_dim]
    second = values[..., half_dim:]
    return jnp.concatenate(
        [first_half * cosine - second * sine_part, second * cosine + first_half * sine_part],
        axis=-1,
    )


def head_prepare(raw_heads, gain, positions):
    return rotate(rms_scale(raw_heads, gain), positions)


def route_slots(route_flat, experts):
    onehot = (route_flat[:, None] == jnp.arange(experts, dtype=jnp.int32)[None, :]).astype(
        jnp.int32
    )
    earlier = jnp.cumsum(onehot, axis=0) - onehot
    return (onehot, jnp.sum(earlier * onehot, axis=1))


def pack_slots(row_values, expert_ids, slot_index, slot_shape):
    buffer = jnp.zeros(slot_shape, row_values.dtype)
    return buffer.at[expert_ids // slot_shape[1], expert_ids % slot_shape[1], slot_index].set(
        row_values
    )


def unpack_slots(buffer, expert_ids, slot_index):
    return buffer[expert_ids // buffer.shape[1], expert_ids % buffer.shape[1], slot_index]


def causal_scores(query_part, key_full, row_start):
    block_rows = query_part.shape[0]
    score_scale = 1.0 / math.sqrt(query_part.shape[2])
    scores = (
        jnp.einsum("qhd,khd->hqk", query_part, key_full, preferred_element_type=jnp.float32)
        * score_scale
    )
    key_pos = jnp.arange(key_full.shape[0], dtype=jnp.int32)
    row_pos = row_start + jnp.arange(block_rows, dtype=jnp.int32)
    allowed = key_pos[None, :] <= row_pos[:, None]
    return jnp.where(allowed[None], scores, -1e30)


def attend_forward(query_rows_all, key_full, value_full):
    sequence_length = query_rows_all.shape[0]
    block_rows = min(512, sequence_length)

    def one_block(block_index):
        row_start = block_index * block_rows
        query_part = lax.dynamic_slice_in_dim(query_rows_all, row_start, block_rows, 0)
        scores = causal_scores(query_part, key_full, row_start)
        row_max = jnp.max(scores, axis=-1, keepdims=True)
        weights = jnp.exp(scores - row_max)
        row_total = jnp.sum(weights, axis=-1, keepdims=True)
        prob_low = (weights / row_total).astype(jnp.bfloat16)
        mixed_out = jnp.einsum(
            "hqk,khd->qhd", prob_low, value_full, preferred_element_type=jnp.float32
        )
        return (mixed_out.astype(jnp.bfloat16), (row_max + jnp.log(row_total))[..., 0])

    mixed_out, log_total = lax.map(
        one_block, jnp.arange(sequence_length // block_rows, dtype=jnp.int32)
    )
    return (mixed_out.reshape(query_rows_all.shape), log_total)


def attend_backward(query_rows_all, key_full, value_full, log_total, d_mixed):
    sequence_length = query_rows_all.shape[0]
    block_rows = min(512, sequence_length)
    score_scale = 1.0 / math.sqrt(query_rows_all.shape[2])

    def one_block(running, block_index):
        d_key_sum, d_value_sum = running
        row_start = block_index * block_rows
        query_part = lax.dynamic_slice_in_dim(query_rows_all, row_start, block_rows, 0)
        d_part = lax.dynamic_slice_in_dim(d_mixed, row_start, block_rows, 0)
        scores = causal_scores(query_part, key_full, row_start)
        prob_full = jnp.exp(scores - log_total[block_index][..., None])
        prob_low = prob_full.astype(jnp.bfloat16)
        d_probs = jnp.einsum("qhd,khd->hqk", d_part, value_full, preferred_element_type=jnp.float32)
        row_delta = jnp.sum(prob_full * d_probs, axis=-1, keepdims=True)
        d_scores = (prob_full * (d_probs - row_delta)).astype(jnp.bfloat16)
        d_query_part = (
            jnp.einsum("hqk,khd->qhd", d_scores, key_full, preferred_element_type=jnp.float32)
            * score_scale
        )
        d_key_sum = (
            d_key_sum
            + jnp.einsum("hqk,qhd->khd", d_scores, query_part, preferred_element_type=jnp.float32)
            * score_scale
        )
        d_value_sum = d_value_sum + jnp.einsum(
            "hqk,qhd->khd", prob_low, d_part, preferred_element_type=jnp.float32
        )
        return ((d_key_sum, d_value_sum), d_query_part)

    zero_grad = jnp.zeros(key_full.shape, jnp.float32)
    (d_key_sum, d_value_sum), d_query = lax.scan(
        one_block,
        (zero_grad, zero_grad),
        jnp.arange(sequence_length // block_rows, dtype=jnp.int32),
    )
    return (d_query.reshape(query_rows_all.shape), d_key_sum, d_value_sum)


def routed_body(
    tokens,
    query_key_value_weight,
    w_out_t,
    w_router,
    w_in,
    w_down,
    attn_gain,
    ffn_gain,
    q_gain,
    k_gain,
    routes,
    cotangent,
):
    sequence_count = lax.axis_size("seq")
    shard_count = lax.axis_size("fsdp")
    experts = sequence_count * shard_count
    token_row_count = tokens.shape[1]
    model_width = tokens.shape[2]
    query_group_width = QUERY_HEADS // KEY_VALUE_HEADS
    capacity = 2 * token_row_count * TOPK // experts
    slot_shape = (sequence_count, shard_count, capacity, model_width)
    positions = lax.axis_index("seq") * token_row_count + jnp.arange(
        token_row_count, dtype=jnp.int32
    )
    full_qkv, full_out, full_router = (
        lax.all_gather(query_key_value_weight, ("seq", "fsdp"), axis=0, tiled=True),
        lax.all_gather(w_out_t, ("seq", "fsdp"), axis=0, tiled=True),
        lax.all_gather(w_router, ("seq", "fsdp"), axis=0, tiled=True),
    )
    resid_in = tokens[0].astype(jnp.float32)
    normed_one = rms_scale(resid_in, attn_gain).astype(jnp.bfloat16)
    projection_output = jnp.dot(normed_one, full_qkv, preferred_element_type=jnp.float32)
    q_raw = projection_output[:, : QUERY_HEADS * HEAD_DIMENSION].reshape(
        token_row_count, QUERY_HEADS, HEAD_DIMENSION
    )
    key_unnormed = projection_output[
        :, QUERY_HEADS * HEAD_DIMENSION : (QUERY_HEADS + KEY_VALUE_HEADS) * HEAD_DIMENSION
    ].reshape(token_row_count, KEY_VALUE_HEADS, HEAD_DIMENSION)
    value_per_head = (
        projection_output[:, (QUERY_HEADS + KEY_VALUE_HEADS) * HEAD_DIMENSION :]
        .reshape(token_row_count, KEY_VALUE_HEADS, HEAD_DIMENSION)
        .astype(jnp.bfloat16)
    )
    prepare = partial(head_prepare, positions=positions)
    query_rows_all = prepare(q_raw, q_gain).astype(jnp.bfloat16)
    key_per_head = prepare(key_unnormed, k_gain).astype(jnp.bfloat16)
    send_keys = jnp.repeat(key_per_head, query_group_width, axis=1)
    send_values = jnp.repeat(value_per_head, query_group_width, axis=1)
    head_queries, head_keys, head_values = (
        lax.all_to_all(query_rows_all, "seq", split_axis=1, concat_axis=0, tiled=True),
        lax.all_to_all(send_keys, "seq", split_axis=1, concat_axis=0, tiled=True),
        lax.all_to_all(send_values, "seq", split_axis=1, concat_axis=0, tiled=True),
    )
    mixed_heads, log_total = attend_forward(head_queries, head_keys, head_values)
    mixed_tok = lax.all_to_all(mixed_heads, "seq", split_axis=0, concat_axis=1, tiled=True)
    attention_result = mixed_tok.reshape(token_row_count, QUERY_HEADS * HEAD_DIMENSION)
    attn_out = jnp.einsum(
        "tj,dj->td", attention_result, full_out, preferred_element_type=jnp.float32
    )
    hidden = resid_in + attn_out
    normed_two = rms_scale(hidden, ffn_gain).astype(jnp.bfloat16)
    logits = jnp.dot(normed_two, full_router, preferred_element_type=jnp.float32)
    route_flat = routes[0].reshape(-1)
    onehot, slot_index = route_slots(route_flat, experts)
    onehot_float = onehot.reshape(token_row_count, TOPK, experts).astype(jnp.float32)
    chosen = jnp.sum(onehot_float * logits[:, None, :], axis=-1)
    row_max = jnp.max(chosen, axis=-1, keepdims=True)
    exp_part = jnp.exp(chosen - row_max)
    gate_probs = exp_part / jnp.sum(exp_part, axis=-1, keepdims=True)
    send_rows = pack_slots(jnp.repeat(normed_two, TOPK, axis=0), route_flat, slot_index, slot_shape)
    arrived = lax.all_to_all(
        lax.all_to_all(send_rows, "seq", split_axis=0, concat_axis=0, tiled=True),
        "fsdp",
        split_axis=1,
        concat_axis=1,
        tiled=True,
    )
    rows_in = arrived.reshape(-1, model_width)
    gate_weight = w_in[0]
    down_weight = w_down[0]
    gate_up = jnp.dot(rows_in, gate_weight, preferred_element_type=jnp.float32)
    gate_half = gate_up[:, :FF]
    up_half = gate_up[:, FF:]
    gate_sig = jax.nn.sigmoid(gate_half)
    silu_gate = gate_half * gate_sig
    inner_act = (silu_gate * up_half).astype(jnp.bfloat16)
    expert_out = jnp.dot(inner_act, down_weight, preferred_element_type=jnp.float32).astype(
        jnp.bfloat16
    )
    returned = lax.all_to_all(
        lax.all_to_all(
            expert_out.reshape(slot_shape), "seq", split_axis=0, concat_axis=0, tiled=True
        ),
        "fsdp",
        split_axis=1,
        concat_axis=1,
        tiled=True,
    )
    picked = (
        unpack_slots(returned, route_flat, slot_index)
        .astype(jnp.float32)
        .reshape(token_row_count, TOPK, model_width)
    )
    mixture = jnp.sum(gate_probs[..., None] * picked, axis=1)
    output = (hidden + mixture).astype(jnp.bfloat16)
    full_qkv, full_out, full_router = (
        lax.all_gather(query_key_value_weight, ("seq", "fsdp"), axis=0, tiled=True),
        lax.all_gather(w_out_t, ("seq", "fsdp"), axis=0, tiled=True),
        lax.all_gather(w_router, ("seq", "fsdp"), axis=0, tiled=True),
    )
    out_grad = cotangent[0].astype(jnp.float32)
    d_picked = (
        (gate_probs[..., None] * out_grad[:, None, :]).astype(jnp.bfloat16).reshape(-1, model_width)
    )
    d_gates = jnp.sum(picked * out_grad[:, None, :], axis=-1)
    d_send = pack_slots(d_picked, route_flat, slot_index, slot_shape)
    d_arrived = lax.all_to_all(
        lax.all_to_all(d_send, "seq", split_axis=0, concat_axis=0, tiled=True),
        "fsdp",
        split_axis=1,
        concat_axis=1,
        tiled=True,
    ).reshape(-1, model_width)
    d_inner = jnp.einsum("rd,fd->rf", d_arrived, down_weight, preferred_element_type=jnp.float32)
    d_gate_half = d_inner * up_half * gate_sig * (1.0 + gate_half * (1.0 - gate_sig))
    d_up_half = d_inner * silu_gate
    d_gate_up = jnp.concatenate([d_gate_half, d_up_half], axis=1).astype(jnp.bfloat16)
    d_w_down = jnp.einsum("rf,rd->fd", inner_act, d_arrived, preferred_element_type=jnp.float32)[
        None
    ]
    d_w_in = jnp.einsum("rd,rf->df", rows_in, d_gate_up, preferred_element_type=jnp.float32)[None]
    d_rows = jnp.einsum(
        "rf,df->rd", d_gate_up, gate_weight, preferred_element_type=jnp.float32
    ).astype(jnp.bfloat16)
    d_back = lax.all_to_all(
        lax.all_to_all(d_rows.reshape(slot_shape), "seq", split_axis=0, concat_axis=0, tiled=True),
        "fsdp",
        split_axis=1,
        concat_axis=1,
        tiled=True,
    )
    d_routed = jnp.sum(
        unpack_slots(d_back, route_flat, slot_index)
        .astype(jnp.float32)
        .reshape(token_row_count, TOPK, model_width),
        axis=1,
    )
    d_chosen = gate_probs * (d_gates - jnp.sum(gate_probs * d_gates, axis=-1, keepdims=True))
    d_logits = jnp.einsum("tk,tke->te", d_chosen, onehot_float).astype(jnp.bfloat16)
    d_normed_two = d_routed + jnp.einsum(
        "te,de->td", d_logits, full_router, preferred_element_type=jnp.float32
    )
    unused_two, pull_two = jax.vjp(rms_scale, hidden, ffn_gain)
    d_hidden_norm, d_ffn_gain = pull_two(d_normed_two)
    d_hidden = out_grad + d_hidden_norm
    d_attn = d_hidden.astype(jnp.bfloat16)
    d_attended = jnp.einsum(
        "td,dj->tj", d_attn, full_out, preferred_element_type=jnp.float32
    ).astype(jnp.bfloat16)
    d_heads = lax.all_to_all(
        d_attended.reshape(token_row_count, QUERY_HEADS, HEAD_DIMENSION),
        "seq",
        split_axis=1,
        concat_axis=0,
        tiled=True,
    )
    d_query, d_key_sum, d_value_sum = attend_backward(
        head_queries, head_keys, head_values, log_total, d_heads
    )
    seq_rows = head_queries.shape[0]
    local_cols = head_queries.shape[1] * HEAD_DIMENSION
    normed_all, d_attn_all = (
        lax.all_gather(normed_one, "seq", axis=0, tiled=True),
        lax.all_gather(d_attn, "seq", axis=0, tiled=True),
    )
    query_cols = lax.dynamic_slice_in_dim(
        full_qkv, lax.axis_index("seq") * local_cols, local_cols, 1
    )
    q_head_raw = jnp.dot(normed_all, query_cols, preferred_element_type=jnp.float32).reshape(
        head_queries.shape
    )
    seq_positions = jnp.arange(seq_rows, dtype=jnp.int32)
    unused_head, pull_head = jax.vjp(
        partial(head_prepare, positions=seq_positions), q_head_raw, q_gain
    )
    send_d_query, d_q_gain = pull_head(d_query)
    d_query_tok, grad_key_token_rows, grad_value_token_rows = (
        lax.all_to_all(
            send_d_query.astype(jnp.bfloat16), "seq", split_axis=0, concat_axis=1, tiled=True
        ).astype(send_d_query.dtype),
        lax.all_to_all(
            d_key_sum.astype(jnp.bfloat16), "seq", split_axis=0, concat_axis=1, tiled=True
        ).astype(d_key_sum.dtype),
        lax.all_to_all(
            d_value_sum.astype(jnp.bfloat16), "seq", split_axis=0, concat_axis=1, tiled=True
        ).astype(d_value_sum.dtype),
    )
    grad_key_per_head = jnp.sum(
        grad_key_token_rows.reshape(token_row_count, KEY_VALUE_HEADS, -1, HEAD_DIMENSION), axis=2
    )
    grad_value_per_head = jnp.sum(
        grad_value_token_rows.reshape(token_row_count, KEY_VALUE_HEADS, -1, HEAD_DIMENSION), axis=2
    )
    unused_k, pull_k = jax.vjp(prepare, key_unnormed, k_gain)
    grad_key_unnormed, d_k_gain = pull_k(grad_key_per_head)
    d_projected = jnp.concatenate(
        [
            d_query_tok.reshape(token_row_count, QUERY_HEADS * HEAD_DIMENSION),
            grad_key_unnormed.reshape(token_row_count, KEY_VALUE_HEADS * HEAD_DIMENSION),
            grad_value_per_head.reshape(token_row_count, KEY_VALUE_HEADS * HEAD_DIMENSION),
        ],
        axis=1,
    ).astype(jnp.bfloat16)
    d_normed_one = jnp.einsum(
        "tj,dj->td", d_projected, full_qkv, preferred_element_type=jnp.float32
    )
    unused_one, pull_one = jax.vjp(rms_scale, resid_in, attn_gain)
    d_resid_norm, d_attn_gain = pull_one(d_normed_one)
    d_tokens = (d_hidden + d_resid_norm).astype(jnp.bfloat16)[None]
    rows_dev = model_width // experts
    kv_count = 2 * KEY_VALUE_HEADS * HEAD_DIMENSION
    kv_grads = d_projected[:, QUERY_HEADS * HEAD_DIMENSION :]
    first_rows = normed_one
    summed = lax.psum_scatter(
        jnp.concatenate(
            [
                jnp.einsum("tc,tj->cj", first_rows, kv_grads, preferred_element_type=jnp.float32),
                jnp.einsum("tc,te->ce", normed_two, d_logits, preferred_element_type=jnp.float32),
            ],
            axis=1,
        ),
        ("seq", "fsdp"),
        scatter_dimension=0,
        tiled=True,
    )
    d_query_low = send_d_query.reshape(seq_rows, local_cols).astype(jnp.bfloat16)
    attended_heads = mixed_heads.reshape(seq_rows, local_cols)
    normed_order = (
        normed_all.reshape(seq_rows, sequence_count, shard_count, rows_dev)
        .transpose(0, 2, 1, 3)
        .reshape(seq_rows, model_width)
    )
    d_attn_order = (
        d_attn_all.reshape(seq_rows, sequence_count, shard_count, rows_dev)
        .transpose(0, 2, 1, 3)
        .reshape(seq_rows, model_width)
    )
    first_rows = normed_order
    head_sums = lax.psum_scatter(
        jnp.concatenate(
            [
                jnp.einsum(
                    "tc,tj->cj", first_rows, d_query_low, preferred_element_type=jnp.float32
                ),
                jnp.einsum(
                    "tc,tj->cj", d_attn_order, attended_heads, preferred_element_type=jnp.float32
                ),
            ],
            axis=1,
        ).astype(jnp.bfloat16),
        "fsdp",
        scatter_dimension=0,
        tiled=True,
    ).astype(jnp.float32)
    row_sums = (
        lax.all_to_all(
            head_sums.astype(jnp.bfloat16), "seq", split_axis=0, concat_axis=1, tiled=True
        )
        .astype(head_sums.dtype)
        .reshape(rows_dev, sequence_count, 2, local_cols)
    )
    d_w_query = row_sums[:, :, 0].reshape(rows_dev, QUERY_HEADS * HEAD_DIMENSION)
    d_w_out_t = row_sums[:, :, 1].reshape(rows_dev, QUERY_HEADS * HEAD_DIMENSION)
    d_w_qkv = jnp.concatenate([d_w_query, summed[:, :kv_count]], axis=1)
    d_w_router = summed[:, kv_count:]
    d_attn_gain, d_ffn_gain, d_q_gain, d_k_gain = lax.psum(
        (d_attn_gain, d_ffn_gain, d_q_gain, d_k_gain), ("seq", "fsdp")
    )
    return (
        output[None],
        d_tokens,
        d_w_qkv,
        d_w_out_t,
        d_w_router,
        d_w_in,
        d_w_down,
        d_attn_gain,
        d_ffn_gain,
        d_q_gain,
        d_k_gain,
    )


MESH = pl.DeviceIdType.MESH
VMEM_LIMIT = 60 * 2**20


class Place:
    def __init__(self):
        seq, shard = lax.axis_index("seq"), lax.axis_index("fsdp")
        self.z, self.x = seq // 2, seq % 2
        self.y, self.c = shard // 2, shard % 2
        self.z0, self.z1 = self.z % 2, self.z // 2
        self.low, self.high = self.z == 0, self.z == 3
        self.inner = (self.z0 + self.z1) == 1
        self.me = self.block(self.z, self.x, self.y, self.c)

    def device(self, z, x, y, c):
        return (z * 2 + x, y * 2 + c)

    def block(self, z, x, y, c):
        return (z * 2 + x) * 4 + y * 2 + c

    @property
    def by_x(self):
        return self.device(self.z, 1 - self.x, self.y, self.c)

    @property
    def by_y(self):
        return self.device(self.z, self.x, 1 - self.y, self.c)

    @property
    def by_core(self):
        return self.device(self.z, self.x, self.y, 1 - self.c)

    def by_z(self, step):
        return self.device(self.z + step, self.x, self.y, self.c)

    def near(self, k):
        return [self.z, 1 + self.z0, 2 - 2 * self.z0 + self.z1, 3 - 3 * self.z1][k]

    def onward(self, k):
        return [None, 2 * self.z1 - 1, 1 - 2 * self.z1, 2 * self.z1 - 1][k]

    def far(self, k):
        return self.near(3 - k)

    def toward(self, k):
        return [1 - 2 * self.z1, 1 - 2 * self.z0, 1 - 2 * self.z1][k]

    def greet(self, sides):
        barrier = pltpu.get_barrier_semaphore()
        for side in sides:
            if side != "z":
                target = {"x": self.by_x, "y": self.by_y, "core": self.by_core}[side]
                pl.semaphore_signal(barrier, inc=1, device_id=target, device_id_type=MESH)
        count = len([side for side in sides if side != "z"])
        if "z" in sides:

            @pl.when(jnp.logical_not(self.low))
            def _():
                pl.semaphore_signal(barrier, inc=1, device_id=self.by_z(-1), device_id_type=MESH)

            @pl.when(jnp.logical_not(self.high))
            def _():
                pl.semaphore_signal(barrier, inc=1, device_id=self.by_z(1), device_id_type=MESH)

            count = count + 1 + (self.z0 + self.z1) % 2
        pl.semaphore_wait(barrier, count)


def send(source, target, send_sem, recv_sem, device):
    pltpu.make_async_remote_copy(
        src_ref=source,
        dst_ref=target,
        send_sem=send_sem,
        recv_sem=recv_sem,
        device_id=device,
        device_id_type=MESH,
    ).start()


def await_bytes(ref, sem):
    pltpu.make_async_copy(ref, ref, sem).wait()


G_Z, G_X, G_Y, G_DX, G_DY, G_C0 = 0, 1, 2, 3, 4, 5
G_KINDS = 9


def gather_steps(place, own, out, ss, rs, zs, local_sem):
    p = place
    rows = out.shape[1]
    half = rows // 2
    x, y, c = p.x, p.y, p.c

    def cols(q):
        return [
            p.block(q, x, y, c),
            p.block(q, 1 - x, y, c),
            p.block(q, x, 1 - y, c),
            p.block(q, 1 - x, 1 - y, c),
        ]

    def to_core(q, j, src=None):
        b = cols(q)[j]
        send(out.at[b] if src is None else src, out.at[b], ss.at[q, G_C0 + j], rs.at[q, G_C0 + j], p.by_core)

    def plane_out(k):
        q = p.near(k)
        b = cols(q)[0]
        if k == 0:
            src = own
            for step, there in ((1, p.high), (-1, p.low)):

                @pl.when(jnp.logical_not(there))
                def _():
                    send(src, out.at[b], zs.at[q, 0 if step > 0 else 1], rs.at[q, G_Z], p.by_z(step))

            pltpu.make_async_copy(own, out.at[b], local_sem).start()
        else:
            src = out.at[b]

            @pl.when(jnp.logical_not(p.inner))
            def _():
                await_bytes(src, rs.at[q, G_Z])

        send(src, out.at[b], ss.at[q, G_X], rs.at[q, G_X], p.by_x)
        send(src, out.at[b], ss.at[q, G_Y], rs.at[q, G_Y], p.by_y)
        to_core(q, 0, src)

    def plane_hop(k):
        q = p.near(k)
        src = out.at[cols(q)[0]]

        @pl.when(p.inner)
        def _():
            await_bytes(src, rs.at[q, G_Z])
            send(src, src, zs.at[q, 0], rs.at[q, G_Z], p.by_z(p.onward(k)))

    def plane_turn(k):
        q = p.near(k)
        bx, by = out.at[cols(q)[1]], out.at[cols(q)[2]]
        await_bytes(bx, rs.at[q, G_X])
        first = bx.at[pl.ds(0, half)]
        send(first, first, ss.at[q, G_DY], rs.at[q, G_DY], p.by_y)
        to_core(q, 1)
        await_bytes(by, rs.at[q, G_Y])
        second = by.at[pl.ds(half, half)]
        send(second, second, ss.at[q, G_DX], rs.at[q, G_DX], p.by_x)
        to_core(q, 2)

    def plane_end(k):
        q = p.near(k)
        bd = out.at[cols(q)[3]]
        await_bytes(bd.at[pl.ds(0, half)], rs.at[q, G_DY])
        await_bytes(bd.at[pl.ds(half, half)], rs.at[q, G_DX])
        to_core(q, 3)

    def plane_core(k, js=(0, 1, 2, 3)):
        q = p.near(k)
        for j in js:
            await_bytes(own, rs.at[q, G_C0 + j])

    def finish():
        piece = own.at[pl.ds(0, half)]
        for q in range(4):
            for kind in (G_X, G_Y, G_C0, G_C0 + 1, G_C0 + 2, G_C0 + 3):
                await_bytes(own, ss.at[q, kind])
            for kind in (G_DX, G_DY):
                await_bytes(piece, ss.at[q, kind])
        for there, slot in ((p.high, 0), (p.low, 1)):

            @pl.when(jnp.logical_not(there))
            def _():
                await_bytes(own, zs.at[p.z, slot])

        for k in range(1, 4):

            @pl.when(p.inner)
            def _():
                await_bytes(own, zs.at[p.near(k), 0])

    return plane_out, plane_hop, plane_turn, plane_end, plane_core, finish


def sum_all_parts(p, part, held, core_in, x_half, y_half, x_in, y_in, z_in, out, ls, cs, cr, ss, rs, zs, zr):
    rows, width = part.shape[1], part.shape[2]
    half = rows // 2
    x, y, c = p.x, p.y, p.c

    def columns(q):
        return [(q, x, y), (q, 1 - x, y), (q, x, 1 - y), (q, 1 - x, 1 - y)]

    def start():
        for k in range(4):
            q = p.far(k)
            for j, (zz, xx, yy) in reversed(list(enumerate(columns(q)))):
                send(
                    part.at[p.block(zz, xx, yy, 1 - c)],
                    core_in.at[q * 4 + j],
                    cs.at[q, j],
                    cr.at[q, j],
                    p.by_core,
                )
                pltpu.make_async_copy(
                    part.at[p.block(zz, xx, yy, c)], held.at[q * 4 + j], ls.at[q, j]
                ).start()

    add = add_rows

    def plane_core(k, js=(3, 1, 2, 0)):
        q = p.far(k)
        for j in js:
            slot = q * 4 + j
            await_bytes(held.at[slot], ls.at[q, j])
            await_bytes(core_in.at[slot], cr.at[q, j])
            add(held.at[slot], core_in.at[slot], rows)
            if j == 3:
                send(held.at[slot, pl.ds(0, half)], y_half.at[q], ss.at[q, 0], rs.at[q, 0], p.by_y)
                send(held.at[slot, pl.ds(half, half)], x_half.at[q], ss.at[q, 1], rs.at[q, 1], p.by_x)

    def plane_turn(k):
        q = p.far(k)
        await_bytes(y_half.at[q], rs.at[q, 0])
        add(held.at[q * 4 + 1, pl.ds(0, half)], y_half.at[q], half)
        send(held.at[q * 4 + 1], x_in.at[q], ss.at[q, 2], rs.at[q, 2], p.by_x)
        await_bytes(x_half.at[q], rs.at[q, 1])
        add(held.at[q * 4 + 2, pl.ds(half, half)], x_half.at[q], half)
        send(held.at[q * 4 + 2], y_in.at[q], ss.at[q, 3], rs.at[q, 3], p.by_y)

    def plane_end(k):
        q = p.far(k)
        mine = held.at[q * 4]
        await_bytes(x_in.at[q], rs.at[q, 2])
        add(mine, x_in.at[q], rows)
        await_bytes(y_in.at[q], rs.at[q, 3])
        add(mine, y_in.at[q], rows)
        if k < 3:
            step = p.toward(k)
            slot = (1 - step) // 2

            @pl.when(p.inner)
            def _():
                await_bytes(z_in.at[slot, q], zr.at[slot, q])
                add(mine, z_in.at[slot, q], rows)

            send(mine, z_in.at[slot, q], zs.at[k], zr.at[slot, q], p.by_z(step))
        else:
            for slot, there in ((0, p.low), (1, p.high)):

                @pl.when(jnp.logical_not(there))
                def _():
                    await_bytes(z_in.at[slot, q], zr.at[slot, q])
                    add(mine, z_in.at[slot, q], rows)

            out[...] = mine[...]

    def finish():
        whole, piece = x_in.at[0], x_half.at[0]
        for q in range(4):
            for j in range(4):
                await_bytes(whole, cs.at[q, j])
            for kind in (0, 1):
                await_bytes(piece, ss.at[q, kind])
            for kind in (2, 3):
                await_bytes(whole, ss.at[q, kind])
        for k in range(3):
            await_bytes(whole, zs.at[k])

    return start, plane_core, plane_turn, plane_end, finish


def sum_all_kernel(
    part, both, rows_in, d_gate_up, inner, d_expert, columns, hidden, cot, gates, ffn_gain,
    out, d_logits, d_hidden, gains, pair, d_w_in, d_w_down,
    d_rows, router, router_sem, both_held, both_in, left, product, pair_sems, load_sems, left_sems, product_sems, *scratch,
):
    p = Place()
    p.greet(("x", "y", "core", "z"))
    start, plane_core, plane_turn, plane_end, finish = sum_all_parts(p, part, *scratch[:7], d_rows, *scratch[7:])
    rows = both.shape[3]

    def pair_sum(first):
        for s in (first, first + 1):
            for y in range(2):
                add_rows(both_held.at[s, y], both_in.at[s, y], rows)

    def right_load(source, i):
        width = source.shape[3]
        return pltpu.make_async_copy(source, both_in.at[:, :, :, pl.ds(0, width)], load_sems.at[i])

    def left_load(source, i, slot):
        cols = pl.ds(pl.multiple_of(i * TILE, TILE), TILE)
        return pltpu.make_async_copy(source.at[:, cols], left.at[slot], left_sems.at[slot])

    def product_store(target, i, slot):
        at = pl.ds(pl.multiple_of(i * TILE, TILE), TILE)
        piece = product.at[slot, :, pl.ds(0, target.shape[1])]
        return pltpu.make_async_copy(piece, target.at[at], product_sems.at[slot])

    def tiles(source, target, first, last):
        count, wide = source.shape[1] // TILE, target.shape[1]

        @pl.loop(first, last)
        def _(i):
            slot = i % 2
            left_load(source, i, slot).wait()

            @pl.when(i + 1 < count)
            def _():
                left_load(source, i + 1, 1 - slot).start()

            @pl.when(i >= 2)
            def _():
                product_store(target, i - 2, slot).wait()

            right = both_in[:, :, :, :wide].reshape(source.shape[0], wide)
            product[slot, :, :wide] = mxu(left[slot], right, TN).astype(product.dtype)
            product_store(target, i, slot).start()

    def tiles_end(source, target):
        count = source.shape[1] // TILE
        for i in (count - 2, count - 1):
            product_store(target, i, i % 2).wait()

    first = columns.shape[2] - 128
    router_load = pltpu.make_async_copy(columns.at[:, :, pl.ds(first, 128)], router, router_sem)
    router_load.start()
    start()
    send(both.at[:, :, 1 - p.c], both_in, pair_sems.at[0], pair_sems.at[1], p.by_core)
    pltpu.make_async_copy(both.at[:, :, p.c], both_held, pair_sems.at[2]).start()
    plane_core(0)
    plane_core(1)
    plane_turn(0)
    await_bytes(both_held, pair_sems.at[2])
    await_bytes(both_in, pair_sems.at[1])
    pair_sum(0)
    plane_core(2)
    pair_sum(2)
    plane_turn(1)
    pair_sum(4)
    pair_sum(6)
    pltpu.make_async_copy(both_held, pair, pair_sems.at[2]).start()
    right_load(d_gate_up, 0).start()
    left_load(rows_in, 0, 0).start()
    plane_end(0)
    plane_core(3)
    right_load(d_gate_up, 0).wait()
    tiles(rows_in, d_w_in, 0, 2)
    plane_turn(2)
    tiles(rows_in, d_w_in, 2, 4)
    plane_end(1)
    tiles(rows_in, d_w_in, 4, 6)
    plane_turn(3)
    tiles(rows_in, d_w_in, 6, 8)
    right_load(d_expert, 1).start()
    tiles_end(rows_in, d_w_in)
    left_load(inner, 0, 0).start()
    plane_end(2)
    right_load(d_expert, 1).wait()
    tiles(inner, d_w_down, 0, 3)
    plane_end(3)
    router_load.wait()
    width = hidden.shape[1]
    experts = part.shape[0]
    tail = d_rows[:, width:].astype(jnp.float32)
    lane = lax.broadcasted_iota(jnp.int32, tail.shape, 1)
    d_gates = jnp.where(lane < experts, tail + pltpu.roll(tail, 128 - experts, 1), 0.0)
    gate = gates[...]
    d_chosen = gate * (d_gates - jnp.sum(gate * d_gates, axis=-1, keepdims=True))
    d_logits[...] = d_chosen.astype(d_logits.dtype)
    gains[...] = jnp.zeros_like(gains)
    chunk = 32

    @pl.loop(0, rows // chunk)
    def _(i):
        at = pl.ds(pl.multiple_of(i * chunk, chunk), chunk)
        routed = mxu(d_logits[at, :], router[...].reshape(width, 128), NT)
        d_out = d_rows[at, :width].astype(jnp.float32) + routed
        x = hidden[at, :]
        scale = lax.rsqrt(jnp.mean(x * x, axis=-1, keepdims=True) + EPS)
        u = d_out * ffn_gain[...]
        dot = jnp.mean(u * x, axis=-1, keepdims=True)
        grad = cot[at, :].astype(jnp.float32) + scale * u - x * (scale * scale * scale * dot)
        d_hidden[at, :] = grad
        out[at, :] = grad.astype(out.dtype)
        gains[1:2, :] += jnp.sum(d_out * x * scale, axis=0, keepdims=True)

    tiles_end(inner, d_w_down)
    finish()
    await_bytes(both_held, pair_sems.at[0])
    pltpu.make_async_copy(both_held, pair, pair_sems.at[2]).wait()


def sum_all_scratch(rows, width):
    dma = pltpu.SemaphoreType.DMA
    bf16 = jnp.bfloat16
    return [
        pltpu.VMEM((16, rows, width), bf16),
        pltpu.VMEM((16, rows, width), bf16),
        pltpu.VMEM((4, rows // 2, width), bf16),
        pltpu.VMEM((4, rows // 2, width), bf16),
        pltpu.VMEM((4, rows, width), bf16),
        pltpu.VMEM((4, rows, width), bf16),
        pltpu.VMEM((2, 4, rows, width), bf16),
        dma((4, 4)),
        dma((4, 4)),
        dma((4, 4)),
        dma((4, 4)),
        dma((4, 4)),
        dma((3,)),
        dma((2, 4)),
    ]


def sum_all(
    part, both, rows_in, d_gate_up, inner, d_expert, columns, hidden, cot, gates, ffn_gain, collective_id
):
    blocks, rows, width = part.shape
    both = both.reshape(blocks // 4, 2, 2, rows, -1)
    pair = (blocks // 4, 2, rows, both.shape[4])
    anywhere, vmem = pl.BlockSpec(memory_space=pl.ANY), pl.BlockSpec(memory_space=pltpu.VMEM)
    return pl.pallas_call(
        sum_all_kernel,
        out_shape=[
            jax.ShapeDtypeStruct(hidden.shape, part.dtype),
            jax.ShapeDtypeStruct((rows, 128), part.dtype),
            jax.ShapeDtypeStruct(hidden.shape, jnp.float32),
            jax.ShapeDtypeStruct((8, hidden.shape[1]), jnp.float32),
            jax.ShapeDtypeStruct(pair, both.dtype),
            jax.ShapeDtypeStruct((rows_in.shape[1], d_gate_up.shape[1]), both.dtype),
            jax.ShapeDtypeStruct((inner.shape[1], d_expert.shape[1]), both.dtype),
        ],
        in_specs=[anywhere] * 7 + [vmem] * 4,
        out_specs=[vmem] * 4 + [anywhere] * 3,
        scratch_shapes=[
            pltpu.VMEM((rows, width), part.dtype),
            pltpu.VMEM((*columns.shape[:2], 128), part.dtype),
            pltpu.SemaphoreType.DMA,
            pltpu.VMEM(pair, both.dtype),
            pltpu.VMEM(pair, both.dtype),
            pltpu.VMEM((2, rows_in.shape[0], TILE), both.dtype),
            pltpu.VMEM((2, TILE, d_expert.shape[1]), both.dtype),
            pltpu.SemaphoreType.DMA((3,)),
            pltpu.SemaphoreType.DMA((2,)),
            pltpu.SemaphoreType.DMA((2,)),
            pltpu.SemaphoreType.DMA((2,)),
            *sum_all_scratch(rows, width),
        ],
        compiler_params=pltpu.CompilerParams(
            collective_id=collective_id, has_side_effects=True, vmem_limit_bytes=VMEM_LIMIT
        ),
        name="sum_all",
    )(
        part,
        both,
        rows_in,
        d_gate_up.reshape(*pair[:3], -1),
        inner,
        d_expert.reshape(*pair[:3], -1),
        columns,
        hidden,
        cot,
        gates,
        ffn_gain,
    )


def add_rows(target, source, count, chunk=32):
    @pl.loop(0, count // chunk)
    def _(i):
        at = pl.ds(pl.multiple_of(i * chunk, chunk), chunk)
        target[at, :] = target[at, :] + source[at, :]


def seq_peer(p, d):
    return ((p.z * 2 + p.x + d) % 8, p.y * 2 + p.c)


def greet_seq(p, sides=("y", "core")):
    barrier = pltpu.get_barrier_semaphore()
    for d in range(1, 8):
        pl.semaphore_signal(barrier, inc=1, device_id=seq_peer(p, d), device_id_type=MESH)
    for side in sides:
        target = {"y": p.by_y, "core": p.by_core}[side]
        pl.semaphore_signal(barrier, inc=1, device_id=target, device_id_type=MESH)
    pl.semaphore_wait(barrier, 7 + len(sides))


NT = (((1,), (1,)), ((), ()))
TILE = 256
WIDE = 512


def mxu(a, b, dims=(((1,), (0,)), ((), ()))):
    return lax.dot_general(a, b, dims, preferred_element_type=jnp.float32)


def experts_kernel(
    own, cot_all, w_in_hbm, w_down_hbm,
    rows_all, out_part, d_part, x_all, d_expert_all, inner_all, d_gate_up_all,
    w_in, w_down, row_buf, cot_buf, pick, pick_t, gates, d_gates, x, cot, d_expert,
    by_d_gate, by_d_up, inner, d_gate_up, held, out_stage, d_stage,
    ss, rs, zs, local_sem, load_sems, store_sems,
):
    p = Place()
    bf16, f32 = jnp.bfloat16, jnp.float32
    width = cot_all.shape[2]
    blocks = 8
    slots = gates.shape[0]
    capacity = slots // blocks
    tokens = row_buf.shape[2]
    group = 4
    experts = rows_all.shape[0]
    p.greet(("x", "y", "core", "z"))
    plane_out, plane_hop, plane_turn, plane_end, plane_core, finish = gather_steps(
        p, own, rows_all, ss, rs, zs, local_sem
    )

    def weights(start):
        for i, (src, dst) in enumerate(((w_in_hbm, w_in), (w_down_hbm, w_down))):
            copy = pltpu.make_async_copy(src, dst, load_sems.at[i])
            copy.start() if start else copy.wait()

    def cot_load(k):
        return pltpu.make_async_copy(
            cot_all.at[pl.ds(p.near(k) * blocks, blocks)], cot_buf.at[k % 2], load_sems.at[2 + k]
        )

    def row_load(k):
        return pltpu.make_async_copy(
            rows_all.at[pl.ds(p.near(k) * blocks, blocks)], row_buf.at[k % 2], load_sems.at[6 + k]
        )

    def arrived(k):
        plane_core(k)
        row_load(k).start()

    sides = (p.x, 1 - p.x)

    def side_load(i):
        at = pl.ds(sides[i] * group, group)
        source = rows_all.at[pl.ds(p.z * blocks + sides[i] * group, group)]
        return pltpu.make_async_copy(source, row_buf.at[0, at], load_sems.at[(6, 10)[i]])

    def side_arrived(i):
        plane_core(0, ((0, 2), (1, 3))[i])
        if i == 0:
            pltpu.make_async_copy(own, rows_all.at[p.me], local_sem).wait()
        side_load(i).start()

    at_slot = {}

    def store(k, i, src, dst):
        if (k, i) not in at_slot:
            at_slot[k, i] = pltpu.make_async_copy(src, dst, store_sems.at[i, k % 2])
        return at_slot[k, i]

    def stores(k):
        q = p.near(k)
        at = pl.ds(q * slots, slots)
        plane = pl.ds(q * blocks, blocks)
        return [
            (x, x_all.at[at]),
            (d_expert, d_expert_all.at[at]),
            (inner, inner_all.at[at]),
            (d_gate_up, d_gate_up_all.at[at]),
            (out_stage, out_part.at[plane]),
            (d_stage, d_part.at[plane]),
        ]

    def put(k, i):
        store(k, i, *stores(k)[i]).start()

    def free(k, i):
        if k > 0:
            store(k - 1, i, *stores(k - 1)[i]).wait()

    def pick_rows(k, g):
        lane = lax.broadcasted_iota(jnp.int32, (8, 128), 1)
        line = lax.broadcasted_iota(jnp.int32, (8, 128), 0)
        select = jnp.where((lane == line * experts + p.me) & (line < 3), 1.0, 0.0).astype(bf16)
        slot_id = lax.broadcasted_iota(jnp.int32, (capacity, tokens), 0).astype(f32) + 1.0
        rows, cots = row_buf.at[k % 2], cot_buf.at[k % 2]
        which = pl.ds(g * group, group)
        lines = mxu(select, rows[which, :, width:].reshape(group * tokens, 128), NT)
        for i in range(group):
            mine = lines[:, i * tokens : (i + 1) * tokens]
            chosen = jnp.where(mine[2:3] == slot_id, 1.0, 0.0)
            gate = jnp.sum(chosen * (mine[0:1] + mine[1:2]), axis=1, keepdims=True)
            at = pl.ds(pl.multiple_of((g * group + i) * capacity, capacity), capacity)
            gates[at, :] = jnp.broadcast_to(gate, (capacity, 128))
            lead = [jnp.zeros((capacity, tokens), bf16)] * i
            tail = [jnp.zeros((capacity, tokens), bf16)] * (group - 1 - i)
            pick[g, i * capacity : (i + 1) * capacity, :] = jnp.concatenate(
                lead + [chosen.astype(bf16)] + tail, axis=1
            )
            lead = [jnp.zeros((tokens, capacity), f32)] * i
            tail = [jnp.zeros((tokens, capacity), f32)] * (group - 1 - i)
            pick_t[g, i * tokens : (i + 1) * tokens, :] = jnp.concatenate(
                lead + [chosen.T] + tail, axis=1
            ).astype(bf16)
        at = slots_at(g)

        @pl.loop(0, width // WIDE)
        def _(n):
            cols = pl.ds(pl.multiple_of(n * WIDE, WIDE), WIDE)
            row_tile = rows[which, :, cols].reshape(group * tokens, WIDE)
            x[at, cols] = mxu(pick[g], row_tile).astype(bf16)
            cot_tile = cots[which, :, cols].reshape(group * tokens, WIDE)
            picked = mxu(pick[g], cot_tile)
            cot[at, cols] = picked.astype(bf16)
            scale = jnp.concatenate([gates[at, :]] * (WIDE // 128), axis=1)
            d_expert[at, cols] = (scale * picked).astype(bf16)

    def slots_at(g):
        if g is None:
            return pl.ds(0, slots)
        return pl.ds(pl.multiple_of(g * group * capacity, group * capacity), group * capacity)

    def up(g=None):
        ff = inner.shape[1]
        at = slots_at(g)

        @pl.loop(0, ff // TILE)
        def _(n):
            cols = pl.ds(pl.multiple_of(n * TILE, TILE), TILE)
            gate = mxu(x[at, :], w_in[:, cols])
            raised = mxu(x[at, :], w_in[:, pl.ds(pl.multiple_of(ff + n * TILE, TILE), TILE)])
            sig = jax.nn.sigmoid(gate)
            silu = gate * sig
            inner[at, cols] = (silu * raised).astype(bf16)
            by_d_up[at, cols] = silu
            by_d_gate[at, cols] = raised * sig * (1.0 + gate * (1.0 - sig))

    def d_up(g=None):
        ff = inner.shape[1]
        at = slots_at(g)

        @pl.loop(0, ff // TILE)
        def _(n):
            cols = pl.ds(pl.multiple_of(n * TILE, TILE), TILE)
            d_inner = mxu(d_expert[at, :], w_down[cols, :], NT)
            d_gate_up[at, cols] = (d_inner * by_d_gate[at, cols]).astype(bf16)
            d_gate_up[at, pl.ds(pl.multiple_of(ff + n * TILE, TILE), TILE)] = (
                d_inner * by_d_up[at, cols]
            ).astype(bf16)

    def spread(stage, sides_done=(0, 1)):
        @pl.loop(0, width // WIDE)
        def _(n):
            cols = pl.ds(pl.multiple_of(n * WIDE, WIDE), WIDE)
            for g in sides_done:
                result = mxu(pick_t[g], held[slots_at(g), cols]).astype(bf16)
                stage[pl.ds(g * group, group), :, cols] = result.reshape(group, tokens, WIDE)

    def down(g=None):
        at = slots_at(g)
        d_gates[at, :] = jnp.zeros_like(d_gates[at, :])

        @pl.loop(0, width // TILE)
        def _(n):
            cols = pl.ds(pl.multiple_of(n * TILE, TILE), TILE)
            result = mxu(inner[at, :], w_down[:, cols]).astype(bf16).astype(f32)
            product = result * cot[at, cols].astype(f32)
            total = product[:, :128]
            for j in range(1, TILE // 128):
                total = total + product[:, j * 128 : (j + 1) * 128]
            d_gates[at, :] += total
            scale = jnp.concatenate([gates[at, :]] * (TILE // 128), axis=1)
            held[at, cols] = (scale * result).astype(bf16)

    def d_down(g=None, sides_done=(0, 1)):
        for side in sides_done:
            at = slots_at(side)
            total = jnp.sum(d_gates[at, :], axis=1, keepdims=True)
            high = total.astype(bf16).astype(f32)
            lane = lax.broadcasted_iota(jnp.int32, (group * capacity, 128), 1)
            info = jnp.where(
                lane == p.me, high, jnp.where(lane == experts + p.me, total - high, 0.0)
            )
            result = mxu(pick_t[side], info.astype(bf16)).astype(bf16)
            d_stage[pl.ds(side * group, group), :, width:] = result.reshape(group, tokens, 128)
        at = slots_at(g)

        @pl.loop(0, width // TILE)
        def _(n):
            cols = pl.ds(pl.multiple_of(n * TILE, TILE), TILE)
            held[at, cols] = mxu(d_gate_up[at, :], w_in[cols, :], NT).astype(bf16)

    plane_out(0)
    weights(True)
    cot_load(0).start()
    plane_turn(0)
    side_arrived(0)
    plane_hop(1)
    plane_out(1)
    plane_hop(2)
    weights(False)
    cot_load(0).wait()
    cot_load(1).start()
    side_load(0).wait()
    side = sides[0]
    pick_rows(0, side)
    up(side)
    plane_end(0)
    d_up(side)
    down(side)
    plane_hop(3)
    side_arrived(1)
    spread(out_stage, (side,))
    d_down(side, (side,))
    plane_turn(1)
    plane_out(2)
    spread(d_stage, (side,))
    side_load(1).wait()
    side = sides[1]
    pick_rows(0, side)
    put(0, 0)
    put(0, 1)
    up(side)
    put(0, 2)
    plane_end(1)
    d_up(side)
    put(0, 3)
    down(side)
    spread(out_stage, (side,))
    put(0, 4)
    arrived(1)
    d_down(side, (side,))
    spread(d_stage, (side,))
    put(0, 5)
    after = {
        (1, 0): ((plane_turn, 2), (plane_out, 3)),
        (1, 3): ((plane_end, 2),),
        (1, 5): ((arrived, 2),),
        (2, 0): ((plane_turn, 3),),
        (2, 3): ((plane_end, 3),),
        (2, 5): ((arrived, 3),),
    }
    for k in range(1, 4):

        def service(i):
            for step, plane in after.get((k, i), ()):
                step(plane)

        row_load(k).wait()
        cot_load(k).wait()
        if k < 3:
            cot_load(k + 1).start()
        free(k, 0)
        free(k, 1)
        for g in range(2):
            pick_rows(k, g)
        put(k, 0)
        put(k, 1)
        service(0)
        free(k, 2)
        up()
        put(k, 2)
        service(1)
        free(k, 3)
        d_up()
        put(k, 3)
        service(2)
        free(k, 4)
        down()
        service(3)
        spread(out_stage)
        put(k, 4)
        service(4)
        free(k, 5)
        d_down()
        service(5)
        spread(d_stage)
        put(k, 5)
    for i in range(6):
        free(4, i)
    finish()


def experts_gathered(own, cot_all, w_in, w_down, capacity, collective_id):
    tokens, wide = own.shape
    experts, _, width = cot_all.shape
    ff = w_down.shape[0]
    slots = 8 * capacity
    dma = pltpu.SemaphoreType.DMA
    bf16, f32 = jnp.bfloat16, jnp.float32
    anywhere = pl.BlockSpec(memory_space=pl.ANY)

    def array(*shape):
        return jax.ShapeDtypeStruct(shape, bf16)

    return pl.pallas_call(
        experts_kernel,
        out_shape=[
            array(experts, tokens, wide),
            array(experts, tokens, width),
            array(experts, tokens, wide),
            array(experts * capacity, width),
            array(experts * capacity, width),
            array(experts * capacity, ff),
            array(experts * capacity, 2 * ff),
        ],
        in_specs=[anywhere] * 4,
        out_specs=[anywhere] * 7,
        scratch_shapes=[
            pltpu.VMEM(w_in.shape, bf16),
            pltpu.VMEM(w_down.shape, bf16),
            pltpu.VMEM((2, 8, tokens, wide), bf16),
            pltpu.VMEM((2, 8, tokens, width), bf16),
            pltpu.VMEM((2, 4 * capacity, 4 * tokens), bf16),
            pltpu.VMEM((2, 4 * tokens, 4 * capacity), bf16),
            pltpu.VMEM((slots, 128), f32),
            pltpu.VMEM((slots, 128), f32),
            pltpu.VMEM((slots, width), bf16),
            pltpu.VMEM((slots, width), bf16),
            pltpu.VMEM((slots, width), bf16),
            pltpu.VMEM((slots, ff), f32),
            pltpu.VMEM((slots, ff), f32),
            pltpu.VMEM((slots, ff), bf16),
            pltpu.VMEM((slots, 2 * ff), bf16),
            pltpu.VMEM((slots, width), bf16),
            pltpu.VMEM((8, tokens, width), bf16),
            pltpu.VMEM((8, tokens, wide), bf16),
            dma((4, G_KINDS)),
            dma((4, G_KINDS)),
            dma((4, 2)),
            dma,
            dma((11,)),
            dma((6, 2)),
        ],
        compiler_params=pltpu.CompilerParams(
            collective_id=collective_id, has_side_effects=True, vmem_limit_bytes=VMEM_LIMIT
        ),
        name="experts",
    )(own, cot_all, w_in, w_down)


TN = (((0,), (0,)), ((), ()))


def back_kernel(
    own, pair, columns_hbm, normed_hbm, queries_hbm, keys_hbm, values_hbm, attended_hbm,
    q_raw_hbm, k_raw_hbm, cosine_hbm, sine_hbm, tokens_hbm, d_hidden_hbm, routed_hbm, d_logits_hbm,
    q_gain, k_gain, attn_gain, gains,
    d_tokens, d_qkv, d_out_t, d_router, gains_out, mixture,
    queries, keys, values, attended, q_raw, k_raw, cosine, sine, tokens, d_hidden, routed, d_logits, input_sems,
    cols_out, d_attn, columns, normed, d_normed, d_heads, d_query, d_key, d_value, d_proj, q_sum, k_sum,
    held, x_in, y_in, z_in, g_send, g_in, x_two, z_two, c_core, c_y,
    gs, gr, gz, load_sems, local_sem, hs, ys, yr, xs, xr, zs, zr, ts, tr,
    normed_sems, free, xs2, xr2, zs2, zr2, cs, cr, cys, cyr, as_, ar,
):
    p = Place()
    bf16, f32 = jnp.bfloat16, jnp.float32
    columns_z = [p.device((p.z + d) % 4, p.x, p.y, p.c) for d in (1, 2, 3)]
    greet_seq(p)
    rows, wide = own.shape
    length, head_cols = queries.shape
    heads = head_cols // HEAD_DIMENSION
    width = d_normed.shape[2]
    proj_cols = d_proj.shape[1]
    plane_rows = 2 * rows
    score_scale = 1.0 / math.sqrt(HEAD_DIMENSION)
    place = p.z * 2 + p.x

    def rows_at(q, x):
        return d_attn.at[q * 2 + x]

    def gather_out(k):
        q = p.near(k)
        there = rows_at(q, p.x)
        if k == 0:
            src = own
            for step, end in ((1, p.high), (-1, p.low)):

                @pl.when(jnp.logical_not(end))
                def _():
                    send(src, there, gz.at[q, 0 if step > 0 else 1], gr.at[q, 0], p.by_z(step))

            pltpu.make_async_copy(own, there, local_sem).start()
        else:
            src = there

            @pl.when(jnp.logical_not(p.inner))
            def _():
                await_bytes(src, gr.at[q, 0])

        send(src, there, gs.at[q], gr.at[q, 1], p.by_x)

    def gather_hop(k):
        q = p.near(k)
        there = rows_at(q, p.x)

        @pl.when(p.inner)
        def _():
            await_bytes(there, gr.at[q, 0])
            send(there, there, gz.at[q, 0], gr.at[q, 0], p.by_z(p.onward(k)))

    def gather_in(k):
        if k == 0:
            pltpu.make_async_copy(own, rows_at(p.z, p.x), local_sem).wait()
        await_bytes(own, gr.at[p.near(k), 1])

    def at_pair(q, x, y):
        return pair.at[q * 4 + x * 2 + y]

    def sum_send(k):
        q = p.far(k)
        for j, x in ((1, 1 - p.x), (0, p.x)):
            i = q * 2 + j
            send(at_pair(q, x, 1 - p.y), y_in.at[k % 2 * 2 + j], ys.at[i], yr.at[i], p.by_y)

    def sum_start():
        sum_send(0)
        sum_send(1)
        for k in range(4):
            q = p.far(k)
            for j, x in ((1, 1 - p.x), (0, p.x)):
                pltpu.make_async_copy(at_pair(q, x, p.y), held.at[q * 2 + j], hs.at[q * 2 + j]).start()

    def sum_turn(k):
        q = p.far(k)
        for j in (1, 0):
            slot = q * 2 + j
            landed = y_in.at[k % 2 * 2 + j]
            await_bytes(held.at[slot], hs.at[slot])
            await_bytes(landed, yr.at[slot])
            add_rows(held.at[slot], landed, rows)
            if j == 1:
                send(held.at[slot], x_in.at[q], xs.at[q], xr.at[q], p.by_x)
        if k < 2:
            pl.semaphore_signal(free, inc=1, device_id=p.by_y, device_id_type=MESH)
            pl.semaphore_wait(free, 1)
            sum_send(k + 2)

    def line_sum(k, mine, landed, sends, arrivals):
        q = p.far(k)
        if k < 3:
            step = p.toward(k)
            slot, hops = (1 - step) // 2, (q - p.z) * step

            @pl.when(p.inner)
            def _():
                await_bytes(landed.at[slot, hops], arrivals.at[slot, hops])
                add_rows(mine, landed.at[slot, hops], rows)

            send(mine, landed.at[slot, hops - 1], sends.at[k], arrivals.at[slot, hops - 1], p.by_z(step))
        else:
            for slot, there in ((0, p.low), (1, p.high)):

                @pl.when(jnp.logical_not(there))
                def _():
                    await_bytes(landed.at[slot, 0], arrivals.at[slot, 0])
                    add_rows(mine, landed.at[slot, 0], rows)

    def sum_end(k):
        q = p.far(k)
        mine = held.at[q * 2]
        await_bytes(x_in.at[q], xr.at[q])
        add_rows(mine, x_in.at[q], rows)
        line_sum(k, mine, z_in, zs, zr)
        if k == 3:
            mixture[...] = mine[...]

    def two_start(*steps):
        for k in steps:
            q = p.far(k)
            send(d_normed.at[q * 2 + 1 - p.x], x_two.at[q], xs2.at[q], xr2.at[q], p.by_x)

    def two_end(k):
        q = p.far(k)
        mine = d_normed.at[q * 2 + p.x]
        await_bytes(x_two.at[q], xr2.at[q])
        add_rows(mine, x_two.at[q], rows)
        line_sum(k, mine, z_two, zs2, zr2)

    piece_rows = c_y.shape[1]
    order = [(place + d) % 8 for d in range(1, 9)]
    piece_width = c_y.shape[2]
    cols_at = cols_out.at[place]

    def cols_start():
        for turn, side in ((0, 1 - p.y), (1, p.y)):
            send(columns.at[:, side, 1 - p.c], c_core.at[turn], cs.at[turn], cr.at[turn], p.by_core)

    def cols_core():
        for turn, side in ((0, 1 - p.y), (1, p.y)):
            await_bytes(c_core.at[turn], cr.at[turn])
            for s in order:
                add_rows(columns.at[s, side, p.c], c_core.at[turn, s], piece_rows)
                if turn == 0:
                    send(columns.at[s, side, p.c], c_y.at[s], cys.at[s], cyr.at[s], p.by_y)

    def cols_turn(*steps):
        for i in steps:
            s = order[i]
            mine = columns.at[s, p.y, p.c]
            await_bytes(c_y.at[s], cyr.at[s])
            add_rows(mine, c_y.at[s], piece_rows)
            if i < 7:
                send(mine, cols_at, as_.at[i], ar.at[i], seq_peer(p, i + 1))
            else:
                pltpu.make_async_copy(mine, cols_at, as_.at[7]).start()

    def norm_back():
        mine = d_normed.at[p.z * 2 + p.x]
        chunk = 16

        @pl.loop(0, rows // chunk)
        def _(i):
            at = pl.ds(pl.multiple_of(i * chunk, chunk), chunk)
            d_out = mine[at, :].astype(f32)
            x = tokens[at, :].astype(f32)
            scale = lax.rsqrt(jnp.mean(x * x, axis=-1, keepdims=True) + EPS)
            u = d_out * attn_gain[...]
            dot = jnp.mean(u * x, axis=-1, keepdims=True)
            d_x = scale * u - x * (scale * scale * scale * dot)
            d_tokens[at, :] = (d_hidden[at, :] + d_x).astype(d_tokens.dtype)

    def attention(q):
        row_start = pl.multiple_of(q * plane_rows, plane_rows)
        at = pl.ds(row_start, plane_rows)

        @pl.loop(0, head_cols // TILE)
        def _(n):
            cols = pl.ds(pl.multiple_of(n * TILE, TILE), TILE)
            grad = d_attn[pl.ds(q * 2, 2)].reshape(plane_rows, width)
            weight_cols = pl.ds(pl.multiple_of(proj_cols + n * TILE, TILE), TILE)
            weight = columns[..., weight_cols].reshape(width, TILE)
            d_heads[at, cols] = mxu(grad, weight).astype(bf16)

        def block(count):
            key, value = keys[:count], values[:count]
            row_pos = row_start + lax.broadcasted_iota(jnp.int32, (plane_rows, count), 0)
            allowed = lax.broadcasted_iota(jnp.int32, (plane_rows, count), 1) <= row_pos

            @pl.loop(0, heads)
            def _(h):
                cols = pl.ds(pl.multiple_of(h * HEAD_DIMENSION, HEAD_DIMENSION), HEAD_DIMENSION)
                query, d_out = queries[at, cols], d_heads[at, cols]
                scores = jnp.where(allowed, mxu(query, key, NT) * score_scale, -1e30)
                raised = jnp.exp(scores - jnp.max(scores, axis=-1, keepdims=True))
                prob = raised / jnp.sum(raised, axis=-1, keepdims=True)
                d_prob = mxu(d_out, value, NT)
                delta = jnp.sum(prob * d_prob, axis=-1, keepdims=True)
                d_scores = (prob * (d_prob - delta)).astype(bf16)
                d_query[at, cols] = mxu(d_scores, key) * score_scale
                d_key[:count] += mxu(d_scores, query, TN) * score_scale
                d_value[:count] += mxu(prob.astype(bf16), d_out, TN)

        half = length // 2

        @pl.when(q < 2)
        def _():
            block(half)

        @pl.when(q >= 2)
        def _():
            block(length)

    def unrotate(grad, at):
        swapped = jnp.concatenate(
            [grad[:, HEAD_DIMENSION // 2 :], grad[:, : HEAD_DIMENSION // 2]], axis=1
        )
        return grad * cosine[at, :] + swapped * sine[at, :]

    def raw_grads():
        q_sum[...] = jnp.zeros_like(q_sum)
        k_sum[...] = jnp.zeros_like(k_sum)

        def one(grad, raw, gain, total, at):
            turned = unrotate(grad, at)
            scale = lax.rsqrt(jnp.mean(raw * raw, axis=-1, keepdims=True) + EPS)
            total[...] += jnp.sum((turned * raw * scale).reshape(-1, 8, HEAD_DIMENSION), axis=0)
            u = turned * gain[...]
            dot = jnp.mean(u * raw, axis=-1, keepdims=True)
            return (scale * u - raw * (scale * scale * scale * dot)).astype(bf16)

        chunk = 128

        @pl.loop(0, length // chunk)
        def _(i):
            at = pl.ds(pl.multiple_of(i * chunk, chunk), chunk)
            for h in range(heads):
                cols = slice(h * HEAD_DIMENSION, (h + 1) * HEAD_DIMENSION)
                d_proj[at, cols] = one(d_query[at, cols], q_raw[at, cols], q_gain, q_sum, at)
            d_proj[at, head_cols : head_cols + HEAD_DIMENSION] = one(
                d_key[at, :], k_raw[at, :], k_gain, k_sum, at
            )
            d_proj[at, head_cols + HEAD_DIMENSION :] = d_value[at, :].astype(bf16)

        g_send[0] = gains[...]
        g_send[0, 2:3, :HEAD_DIMENSION] = jnp.sum(q_sum[...], axis=0, keepdims=True)
        g_send[0, 2:3, HEAD_DIMENSION : 2 * HEAD_DIMENSION] = jnp.sum(
            k_sum[...], axis=0, keepdims=True
        )

    def normed_load(n, slot):
        cols = pl.ds(pl.multiple_of(n * TILE, TILE), TILE)
        return pltpu.make_async_copy(normed_hbm.at[:, cols], normed.at[slot], normed_sems.at[slot])

    def normed_grads():
        @pl.loop(0, width // TILE)
        def _(n):
            cols = pl.ds(pl.multiple_of(n * TILE, TILE), TILE)
            slot = n % 2
            normed_load(n, slot).wait()

            @pl.when(n + 1 < width // TILE)
            def _():
                normed_load(n + 1, 1 - slot).start()

            weight = columns[n, :, :, :, :proj_cols].reshape(TILE, proj_cols)
            part = mxu(d_proj[...], weight, NT)
            d_normed[:, :, cols] = part.astype(bf16).reshape(length // rows, rows, TILE)
            total = jnp.sum(part * normed[slot].astype(f32), axis=0, keepdims=True)
            g_send[0, 0:1, cols] = total / attn_gain[:, cols]
            grad = mxu(normed[slot], d_proj[...], TN).astype(bf16)
            columns[n, :, :, :, :proj_cols] = grad.reshape(2, 2, -1, proj_cols)

    def gains_pass(t, target):
        send(g_send.at[t], g_in.at[t], ts.at[t], tr.at[t], target)

    def gains_take(t):
        await_bytes(g_in.at[t], tr.at[t])
        g_send[t + 1] = g_send[t] + g_in[t]

    def gains_z_pass():
        g_in[2 + p.z] = g_send[2]
        for d, target in enumerate(columns_z):
            send(g_send.at[2], g_in.at[2 + p.z], ts.at[2 + d], tr.at[2 + d], target)

    def gains_z_take():
        for d in range(3):
            await_bytes(g_in.at[0], tr.at[2 + d])
        g_send[3] = g_in[2] + g_in[3] + g_in[4] + g_in[5]

    def router_grads():
        @pl.loop(0, width // TILE)
        def _(n):
            cols = pl.ds(pl.multiple_of(n * TILE, TILE), TILE)
            grad = mxu(routed[:, cols], d_logits[...], TN).astype(bf16)
            columns[n, :, :, :, proj_cols + head_cols :] = grad.reshape(2, 2, -1, 128)

    def column_grads(value, first, count):
        @pl.loop(0, width // TILE)
        def _(n):
            cols = pl.ds(pl.multiple_of(n * TILE, TILE), TILE)
            part = d_attn[:, :, cols].reshape(length, TILE)
            grad = mxu(part, value[...], TN).astype(bf16)
            columns[n, :, :, :, first : first + count] = grad.reshape(2, 2, -1, count)

    loads = [
        pltpu.make_async_copy(columns_hbm, columns, load_sems.at[0]),
    ]
    gather_out(0)
    inputs = [
        pltpu.make_async_copy(source, target, input_sems.at[i])
        for i, (source, target) in enumerate(
            (
                (queries_hbm, queries),
                (keys_hbm, keys),
                (values_hbm, values),
                (attended_hbm, attended),
                (q_raw_hbm, q_raw),
                (k_raw_hbm, k_raw),
                (cosine_hbm, cosine),
                (sine_hbm, sine),
                (tokens_hbm, tokens),
                (d_hidden_hbm, d_hidden),
                (routed_hbm, routed),
                (d_logits_hbm, d_logits),
            )
        )
    ]
    loads[0].start()
    for copy in inputs:
        copy.start()
    normed_load(0, 0).start()
    sum_start()
    d_key[...] = jnp.zeros_like(d_key)
    d_value[...] = jnp.zeros_like(d_value)
    loads[0].wait()
    for copy in inputs:
        copy.wait()
    gather_in(0)
    gather_hop(1)
    gather_out(1)
    gather_hop(2)
    attention(p.near(0))
    gather_out(2)
    gather_hop(3)
    gather_in(1)
    attention(p.near(1))
    sum_turn(0)
    gather_out(3)
    gather_in(2)
    attention(p.near(2))
    sum_end(0)
    sum_turn(1)
    gather_in(3)
    attention(p.near(3))
    raw_grads()
    sum_end(1)
    normed_grads()
    gains_pass(0, p.by_core)
    column_grads(attended, proj_cols, head_cols)
    gains_take(0)
    gains_pass(1, p.by_x)
    two_start(0, 1)
    router_grads()
    cols_start()
    gains_take(1)
    gains_z_pass()
    sum_turn(2)
    two_start(2, 3)
    cols_core()
    two_end(0)
    sum_turn(3)
    gains_z_take()
    send(g_send.at[3], g_in.at[6], ts.at[5], tr.at[5], p.by_y)
    two_end(1)
    cols_turn(0, 1)
    sum_end(2)
    cols_turn(2, 3, 4, 5)
    two_end(2)
    cols_turn(6, 7)
    two_end(3)
    norm_back()
    sum_end(3)
    await_bytes(g_in.at[6], tr.at[5])
    gains_out[...] = g_send[3] + g_in[6]
    for t in range(6):
        await_bytes(g_in.at[0], ts.at[t])
    for q in range(4):
        await_bytes(own, gs.at[q])
    for there, slot in ((p.high, 0), (p.low, 1)):

        @pl.when(jnp.logical_not(there))
        def _():
            await_bytes(own, gz.at[p.z, slot])

    for k in range(1, 4):

        @pl.when(p.inner)
        def _():
            await_bytes(own, gz.at[p.near(k), 0])

    piece = x_in.at[0]
    for i in range(8):
        await_bytes(piece, ys.at[i])
    for q in range(4):
        await_bytes(piece, xs.at[q])
    for k in range(3):
        await_bytes(piece, zs.at[k])
        await_bytes(piece, zs2.at[k])
    for q in range(4):
        await_bytes(piece, xs2.at[q])
    for i in range(8):
        if i < 7:
            await_bytes(c_y.at[0], ar.at[i])
        await_bytes(c_y.at[0], as_.at[i])
        await_bytes(c_y.at[0], cys.at[i])
    for turn in range(2):
        await_bytes(c_core.at[turn], cs.at[turn])
    key_cols = KEY_VALUE_HEADS * HEAD_DIMENSION
    per_group = 8 // KEY_VALUE_HEADS
    router_total = jnp.zeros((piece_rows, 128), f32)
    for s in range(8):
        d_qkv[:, s * head_cols : (s + 1) * head_cols] = cols_out[s, :, :head_cols].astype(f32)
        d_out_t[:, s * head_cols : (s + 1) * head_cols] = cols_out[
            s, :, proj_cols : proj_cols + head_cols
        ].astype(f32)
        part = cols_out[s, :, proj_cols + head_cols :].astype(f32)
        router_total = router_total + part
    d_router[...] = router_total
    for g in range(KEY_VALUE_HEADS):
        for j in range(2):
            lanes = slice(head_cols + j * HEAD_DIMENSION, head_cols + (j + 1) * HEAD_DIMENSION)
            total = cols_out[g * per_group, :, lanes].astype(f32)
            for s in range(1, per_group):
                total = total + cols_out[g * per_group + s, :, lanes].astype(f32)
            first = 8 * head_cols + j * key_cols + g * HEAD_DIMENSION
            d_qkv[:, first : first + HEAD_DIMENSION] = total


def back(
    own, pair, columns, normed, queries, keys, values, attended,
    q_raw, k_raw, cosine, sine, q_gain, k_gain, attn_gain, gains, tokens, d_hidden,
    routed, d_logits, collective_id,
):
    inputs = (
        queries, keys, values, attended, q_raw, k_raw, cosine, sine, tokens, d_hidden, routed, d_logits,
    )
    rows, wide = own.shape
    length, head_cols = queries.shape
    width = normed.shape[1]
    piece_rows, piece_width = columns.shape[3:]
    proj_cols = head_cols + 2 * HEAD_DIMENSION
    dma = pltpu.SemaphoreType.DMA
    bf16, f32 = jnp.bfloat16, jnp.float32
    anywhere, vmem = pl.BlockSpec(memory_space=pl.ANY), pl.BlockSpec(memory_space=pltpu.VMEM)
    return pl.pallas_call(
        back_kernel,
        out_shape=[
            jax.ShapeDtypeStruct((rows, width), bf16),
            jax.ShapeDtypeStruct((piece_rows, 8 * head_cols + 2 * KEY_VALUE_HEADS * HEAD_DIMENSION), f32),
            jax.ShapeDtypeStruct((piece_rows, 8 * head_cols), f32),
            jax.ShapeDtypeStruct((piece_rows, 128), f32),
            jax.ShapeDtypeStruct(gains.shape, f32),
            jax.ShapeDtypeStruct((rows, width), bf16),
        ],
        in_specs=[anywhere] * 16 + [vmem] * 4,
        out_specs=[vmem] * 6,
        scratch_shapes=[
            *[pltpu.VMEM(array.shape, array.dtype) for array in inputs],
            dma((len(inputs),)),
            pltpu.VMEM((8, piece_rows, piece_width), bf16),
            pltpu.VMEM((8, rows, wide), bf16),
            pltpu.VMEM(columns.shape, bf16),
            pltpu.VMEM((2, length, TILE), bf16),
            pltpu.VMEM((length // rows, rows, width), bf16),
            pltpu.VMEM((length, head_cols), bf16),
            pltpu.VMEM((length, head_cols), f32),
            pltpu.VMEM((length, HEAD_DIMENSION), f32),
            pltpu.VMEM((length, HEAD_DIMENSION), f32),
            pltpu.VMEM((length, proj_cols), bf16),
            pltpu.VMEM((8, HEAD_DIMENSION), f32),
            pltpu.VMEM((8, HEAD_DIMENSION), f32),
            pltpu.VMEM((8, rows, width), bf16),
            pltpu.VMEM((4, rows, width), bf16),
            pltpu.VMEM((4, rows, width), bf16),
            pltpu.VMEM((2, 3, rows, width), bf16),
            pltpu.VMEM((4, *gains.shape), f32),
            pltpu.VMEM((7, *gains.shape), f32),
            pltpu.VMEM((4, rows, width), bf16),
            pltpu.VMEM((2, 3, rows, width), bf16),
            pltpu.VMEM((2, 8, piece_rows, piece_width), bf16),
            pltpu.VMEM((8, piece_rows, piece_width), bf16),
            dma((4,)),
            dma((4, 2)),
            dma((4, 2)),
            dma((2,)),
            dma,
            dma((8,)),
            dma((8,)),
            dma((8,)),
            dma((4,)),
            dma((4,)),
            dma((3,)),
            dma((2, 3)),
            dma((6,)),
            dma((6,)),
            dma((2,)),
            pltpu.SemaphoreType.REGULAR,
            dma((4,)),
            dma((4,)),
            dma((3,)),
            dma((2, 3)),
            dma((2,)),
            dma((2,)),
            dma((8,)),
            dma((8,)),
            dma((8,)),
            dma((7,)),
        ],
        compiler_params=pltpu.CompilerParams(
            collective_id=collective_id, has_side_effects=True, vmem_limit_bytes=VMEM_LIMIT
        ),
        name="back",
    )(
        own, pair, columns, normed, *inputs, q_gain, k_gain, attn_gain, gains,
    )


C_Z, C_X, C_Y, C_C, C_KINDS = 0, 1, 2, 4, 8


def front_kernel(
    tokens, pieces, cot, cosine_hbm, sine_hbm, q_gain, k_gain, attn_gain, ffn_gain, routes,
    normed_out, columns_out, cot_all, queries_out, keys_out, values_out, attended_out, q_raw_out, k_raw_out,
    hidden, gates, routed,
    queries, keys, values, attended, q_raw, k_raw, cosine, sine, result_sems, table_sems,
    own, normed, columns, part, x_in, z_in,
    ss, rs, zs, cs, cr, ys, yr, ks, kr, local_sems, gs, gr, gz, xs, xr, us, ur,
):
    p = Place()
    bf16 = jnp.bfloat16
    greet_seq(p)
    place, shard = p.z * 2 + p.x, p.y * 2 + p.c
    mine = place * 4 + shard
    rows, width = own.shape
    length, head_cols = queries.shape
    heads = head_cols // HEAD_DIMENSION
    proj_cols = head_cols + 2 * HEAD_DIMENSION
    plane_rows = 2 * rows
    score_scale = 1.0 / math.sqrt(HEAD_DIMENSION)

    x = tokens[...].astype(jnp.float32)
    scale = lax.rsqrt(jnp.mean(x * x, axis=-1, keepdims=True) + EPS)
    own[...] = (x * scale * attn_gain[...]).astype(bf16)

    def rows_at(q, x):
        return normed.at[q * 2 + x]

    def rows_move(k):
        q = p.near(k)
        there = rows_at(q, p.x)
        if k == 0:
            src = own
            for step, end in ((1, p.high), (-1, p.low)):

                @pl.when(jnp.logical_not(end))
                def _():
                    send(src, there, zs.at[q, 0 if step > 0 else 1], rs.at[q, 0], p.by_z(step))

            pltpu.make_async_copy(own, there, local_sems.at[0]).start()
        else:
            src = there

            @pl.when(jnp.logical_not(p.inner))
            def _():
                await_bytes(src, rs.at[q, 0])

        send(src, there, ss.at[q], rs.at[q, 1], p.by_x)

    def rows_hop(k):
        q = p.near(k)
        there = rows_at(q, p.x)

        @pl.when(p.inner)
        def _():
            await_bytes(there, rs.at[q, 0])
            send(there, there, zs.at[q, 0], rs.at[q, 0], p.by_z(p.onward(k)))

    def pass_on(d):
        block = ((place + 8 - d) % 8) * 4 + shard
        src = pieces.at[place] if d == 0 else columns.at[block]
        if d > 0:
            await_bytes(src, cr.at[d])
        send(src, columns.at[block], ys.at[d], yr.at[d], p.by_y)
        send(src, columns.at[block], ks.at[0, d], kr.at[0, d], p.by_core)

    def pass_across(d):
        block = columns.at[((place + 8 - d) % 8) * 4 + (1 - p.y) * 2 + p.c]
        await_bytes(block, yr.at[d])
        send(block, block, ks.at[1, d], kr.at[1, d], p.by_core)

    def cot_at(q, x, y):
        return cot_all.at[p.block(q, x, y, p.c)]

    def cot_core(q, j, src):
        x, y = (p.x, 1 - p.x)[j % 2], (p.y, 1 - p.y)[j // 2]
        send(src, cot_at(q, x, y), gs.at[q, C_C + j], gr.at[q, C_C + j], p.by_core)

    def cot_move(k):
        q = p.near(k)
        there = cot_at(q, p.x, p.y)
        if k == 0:
            src = cot
            for step, end in ((1, p.high), (-1, p.low)):

                @pl.when(jnp.logical_not(end))
                def _():
                    send(src, there, gz.at[q, 0 if step > 0 else 1], gr.at[q, C_Z], p.by_z(step))

            pltpu.make_async_copy(cot, there, local_sems.at[2]).start()
        else:
            src = there

            @pl.when(jnp.logical_not(p.inner))
            def _():
                await_bytes(src, gr.at[q, C_Z])

        send(src, there, gs.at[q, C_Y], gr.at[q, C_Y], p.by_y)
        send(src, there, gs.at[q, C_X], gr.at[q, C_X], p.by_x)
        cot_core(q, 0, src)

    def cot_hop(k):
        q = p.near(k)
        there = cot_at(q, p.x, p.y)

        @pl.when(p.inner)
        def _():
            await_bytes(there, gr.at[q, C_Z])
            send(there, there, gz.at[q, 0], gr.at[q, C_Z], p.by_z(p.onward(k)))

    def cot_turn(k):
        q = p.near(k)
        there = cot_at(q, 1 - p.x, p.y)
        await_bytes(there, gr.at[q, C_X])
        send(there, there, gs.at[q, C_Y + 1], gr.at[q, C_Y + 1], p.by_y)
        cot_core(q, 1, there)

    def cot_end(k):
        q = p.near(k)
        for j, x in ((0, p.x), (1, 1 - p.x)):
            there = cot_at(q, x, 1 - p.y)
            await_bytes(there, gr.at[q, C_Y + j])
            cot_core(q, 2 + j, there)

    def sum_end(k):
        q = p.far(k)
        held = part.at[q * 2 + p.x]
        await_bytes(x_in.at[q], xr.at[q])
        add_rows(held, x_in.at[q], rows)
        if k < 3:
            step = p.toward(k)
            slot = (1 - step) // 2

            @pl.when(p.inner)
            def _():
                await_bytes(z_in.at[slot, q], ur.at[slot, q])
                add_rows(held, z_in.at[slot, q], rows)

            send(held, z_in.at[slot, q], us.at[k], ur.at[slot, q], p.by_z(step))
        else:
            for slot, there in ((0, p.low), (1, p.high)):

                @pl.when(jnp.logical_not(there))
                def _():
                    await_bytes(z_in.at[slot, q], ur.at[slot, q])
                    add_rows(held, z_in.at[slot, q], rows)

    def route():
        total = tokens[...].astype(jnp.float32) + part[p.z * 2 + p.x].astype(jnp.float32)
        hidden[...] = total
        scale = lax.rsqrt(jnp.mean(total * total, axis=-1, keepdims=True) + EPS)
        routed[:, :width] = (total * scale * ffn_gain[...]).astype(bf16)
        router = columns[:, :, proj_cols + head_cols :].reshape(width, 128)
        logits = mxu(routed[:, :width], router)
        lane = lax.broadcasted_iota(jnp.int32, (rows, 128), 1)
        line = lax.broadcasted_iota(jnp.int32, (rows, 128), 0)
        turned = routes[...].astype(jnp.float32).T
        lanes = lane.astype(jnp.float32)
        named = lanes == turned[:, 0:1]
        for k in range(1, TOPK):
            named = named | (lanes == turned[:, k : k + 1])
        chosen = jnp.where(named, logits, -1e30)
        raised = jnp.where(named, jnp.exp(chosen - jnp.max(chosen, axis=-1, keepdims=True)), 0.0)
        gate = raised / jnp.sum(raised, axis=-1, keepdims=True)
        gates[...] = gate
        counted = jnp.where(named, 1.0, 0.0)
        slot = counted * mxu(jnp.where(lane <= line, 1.0, 0.0).astype(bf16), counted.astype(bf16))
        high = gate.astype(bf16).astype(jnp.float32)
        experts = columns.shape[0]
        info = high + pltpu.roll(gate - high, experts, 1) + pltpu.roll(slot, 2 * experts, 1)
        routed[:, width:] = info.astype(bf16)

    def project(n):
        cols = slice(n * TILE, (n + 1) * TILE)
        weight = columns[:, :, cols].reshape(width, TILE)
        result = mxu(normed[...].reshape(length, width), weight)
        if n * TILE < head_cols:
            q_raw[:, cols] = result
        else:
            k_raw[...] = result[:, :HEAD_DIMENSION]
            values[...] = result[:, HEAD_DIMENSION:].astype(bf16)

    def prepare():
        def one(raw, gain, at):
            scaled = raw * lax.rsqrt(jnp.mean(raw * raw, axis=-1, keepdims=True) + EPS) * gain[...]
            swapped = jnp.concatenate(
                [scaled[:, HEAD_DIMENSION // 2 :], scaled[:, : HEAD_DIMENSION // 2]], axis=1
            )
            return (scaled * cosine[at, :] - swapped * sine[at, :]).astype(bf16)

        chunk = 128

        @pl.loop(0, length // chunk)
        def _(i):
            at = pl.ds(pl.multiple_of(i * chunk, chunk), chunk)
            for h in range(heads):
                cols = slice(h * HEAD_DIMENSION, (h + 1) * HEAD_DIMENSION)
                queries[at, cols] = one(q_raw[at, cols], q_gain, at)
            keys[at, :] = one(k_raw[at, :], k_gain, at)

    def attention(k):
        q = p.far(k)
        row_start = pl.multiple_of(q * plane_rows, plane_rows)
        at = pl.ds(row_start, plane_rows)

        def block(count):
            row_pos = row_start + lax.broadcasted_iota(jnp.int32, (plane_rows, count), 0)
            allowed = lax.broadcasted_iota(jnp.int32, (plane_rows, count), 1) <= row_pos

            @pl.loop(0, heads)
            def _(h):
                cols = pl.ds(pl.multiple_of(h * HEAD_DIMENSION, HEAD_DIMENSION), HEAD_DIMENSION)
                scores = mxu(queries[at, cols], keys[:count], NT) * score_scale
                scores = jnp.where(allowed, scores, -1e30)
                raised = jnp.exp(scores - jnp.max(scores, axis=-1, keepdims=True))
                prob = raised / jnp.sum(raised, axis=-1, keepdims=True)
                attended[at, cols] = mxu(prob.astype(bf16), values[:count]).astype(bf16)

        @pl.when(q < 2)
        def _():
            block(length // 2)

        @pl.when(q >= 2)
        def _():
            block(length)

        per_tile = TILE // columns.shape[1]

        @pl.loop(0, width // TILE)
        def _(n):
            cols = pl.ds(pl.multiple_of(n * TILE, TILE), TILE)
            weight = columns[pl.ds(n * per_tile, per_tile), :, proj_cols : proj_cols + head_cols]
            result = mxu(attended[at, :], weight.reshape(TILE, head_cols), NT).astype(bf16)
            part[pl.ds(q * 2, 2), :, cols] = result.reshape(2, rows, TILE)

        send(part.at[q * 2 + 1 - p.x], x_in.at[q], xs.at[q], xr.at[q], p.by_x)

    tables = [
        pltpu.make_async_copy(cosine_hbm, cosine, table_sems.at[0]),
        pltpu.make_async_copy(sine_hbm, sine, table_sems.at[1]),
    ]
    results = [
        pltpu.make_async_copy(source, target, result_sems.at[i])
        for i, (source, target) in enumerate(
            (
                (queries, queries_out),
                (keys, keys_out),
                (values, values_out),
                (q_raw, q_raw_out),
                (k_raw, k_raw_out),
                (attended, attended_out),
            )
        )
    ]
    rows_move(0)
    for copy in tables:
        copy.start()
    for d in range(1, 8):
        send(pieces.at[(place + d) % 8], columns.at[mine], cs.at[d], cr.at[d], seq_peer(p, d))
    pltpu.make_async_copy(pieces.at[place], columns.at[mine], local_sems.at[1]).start()
    pass_on(0)
    rows_hop(1)
    rows_move(1)
    for d in (1, 2, 7):
        pass_on(d)
    rows_hop(2)
    rows_move(2)
    cot_move(0)
    for d in (6, 3, 5):
        pass_on(d)
    rows_hop(3)
    rows_move(3)
    pass_on(4)
    for d in (0, 1, 2, 7, 6, 3, 5, 4):
        pass_across(d)
    cot_hop(1)
    cot_move(1)
    for k in range(4):
        await_bytes(own, rs.at[p.near(k), 1])
    pltpu.make_async_copy(own, rows_at(p.z, p.x), local_sems.at[0]).wait()
    pltpu.make_async_copy(pieces.at[place], columns.at[mine], local_sems.at[1]).wait()
    piece = pieces.at[0]
    for d in range(8):
        await_bytes(piece, kr.at[0, d])
        await_bytes(piece, kr.at[1, d])
    pltpu.make_async_copy(normed, normed_out, local_sems.at[0]).start()
    pltpu.make_async_copy(columns, columns_out, local_sems.at[1]).start()
    cot_turn(0)
    for n in range(proj_cols // TILE):
        project(n)
    cot_hop(2)
    cot_move(2)
    for copy in tables:
        copy.wait()
    prepare()
    for copy in results[:5]:
        copy.start()
    cot_turn(1)
    attention(0)
    cot_end(0)
    attention(1)
    cot_hop(3)
    cot_move(3)
    sum_end(0)
    attention(2)
    cot_turn(2)
    cot_end(1)
    sum_end(1)
    attention(3)
    results[5].start()
    cot_turn(3)
    sum_end(2)
    cot_end(2)
    sum_end(3)
    cot_end(3)
    route()
    for copy in results:
        copy.wait()
    for q in range(4):
        for j in range(4):
            await_bytes(cot, gr.at[q, C_C + j])
            await_bytes(cot, gs.at[q, C_C + j])
        for kind in (C_X, C_Y, C_Y + 1):
            await_bytes(cot, gs.at[q, kind])
        await_bytes(own, ss.at[q])
        await_bytes(own, xs.at[q])
    for there, slot in ((p.high, 0), (p.low, 1)):

        @pl.when(jnp.logical_not(there))
        def _():
            await_bytes(own, zs.at[p.z, slot])
            await_bytes(cot, gz.at[p.z, slot])

    for k in range(1, 4):

        @pl.when(p.inner)
        def _():
            await_bytes(own, zs.at[p.near(k), 0])
            await_bytes(cot, gz.at[p.near(k), 0])

    for k in range(3):
        await_bytes(own, us.at[k])
    for d in range(8):
        if d > 0:
            await_bytes(piece, cs.at[d])
        await_bytes(piece, ys.at[d])
        await_bytes(piece, ks.at[0, d])
        await_bytes(piece, ks.at[1, d])
    pltpu.make_async_copy(cot, cot_at(p.z, p.x, p.y), local_sems.at[2]).wait()
    pltpu.make_async_copy(normed, normed_out, local_sems.at[0]).wait()
    pltpu.make_async_copy(columns, columns_out, local_sems.at[1]).wait()


def front(
    tokens, pieces, cot, cosine, sine, q_gain, k_gain, attn_gain, ffn_gain, routes, head_cols, collective_id
):
    dma = pltpu.SemaphoreType.DMA
    bf16, f32 = jnp.bfloat16, jnp.float32
    rows, width = tokens.shape
    count, piece_rows, piece_width = pieces.shape
    length = count * rows
    anywhere, vmem = pl.BlockSpec(memory_space=pl.ANY), pl.BlockSpec(memory_space=pltpu.VMEM)
    return pl.pallas_call(
        front_kernel,
        out_shape=[
            jax.ShapeDtypeStruct((count, rows, width), bf16),
            jax.ShapeDtypeStruct((count * 4, piece_rows, piece_width), bf16),
            jax.ShapeDtypeStruct((count * 4, rows, width), bf16),
            jax.ShapeDtypeStruct((length, head_cols), bf16),
            jax.ShapeDtypeStruct((length, HEAD_DIMENSION), bf16),
            jax.ShapeDtypeStruct((length, HEAD_DIMENSION), bf16),
            jax.ShapeDtypeStruct((length, head_cols), bf16),
            jax.ShapeDtypeStruct((length, head_cols), f32),
            jax.ShapeDtypeStruct((length, HEAD_DIMENSION), f32),
            jax.ShapeDtypeStruct((rows, width), f32),
            jax.ShapeDtypeStruct((rows, 128), f32),
            jax.ShapeDtypeStruct((rows, width + 128), bf16),
        ],
        in_specs=[vmem] + [anywhere] * 4 + [vmem] * 5,
        out_specs=[anywhere] * 9 + [vmem] * 3,
        scratch_shapes=[
            pltpu.VMEM((length, head_cols), bf16),
            pltpu.VMEM((length, HEAD_DIMENSION), bf16),
            pltpu.VMEM((length, HEAD_DIMENSION), bf16),
            pltpu.VMEM((length, head_cols), bf16),
            pltpu.VMEM((length, head_cols), f32),
            pltpu.VMEM((length, HEAD_DIMENSION), f32),
            pltpu.VMEM(cosine.shape, f32),
            pltpu.VMEM(sine.shape, f32),
            dma((6,)),
            dma((2,)),
            pltpu.VMEM((rows, width), bf16),
            pltpu.VMEM((count, rows, width), bf16),
            pltpu.VMEM((count * 4, piece_rows, piece_width), bf16),
            pltpu.VMEM((count, rows, width), bf16),
            pltpu.VMEM((4, rows, width), bf16),
            pltpu.VMEM((2, 4, rows, width), bf16),
            dma((4,)),
            dma((4, 2)),
            dma((4, 2)),
            dma((8,)),
            dma((8,)),
            dma((8,)),
            dma((8,)),
            dma((2, 8)),
            dma((2, 8)),
            dma((3,)),
            dma((4, C_KINDS)),
            dma((4, C_KINDS)),
            dma((4, 2)),
            dma((4,)),
            dma((4,)),
            dma((3,)),
            dma((2, 4)),
        ],
        compiler_params=pltpu.CompilerParams(
            collective_id=collective_id, has_side_effects=True, vmem_limit_bytes=VMEM_LIMIT
        ),
        name="front",
    )(tokens, pieces, cot, cosine, sine, q_gain, k_gain, attn_gain, ffn_gain, routes)


def head_columns(weight, group_index):
    rows = weight.shape[0]
    query_width = QUERY_HEADS * HEAD_DIMENSION
    key_width = KEY_VALUE_HEADS * HEAD_DIMENSION
    query = weight[:, :query_width].reshape(rows, len(group_index), -1).transpose(1, 0, 2)
    keys = weight[:, query_width : query_width + key_width].reshape(rows, KEY_VALUE_HEADS, -1)
    values = weight[:, query_width + key_width :].reshape(rows, KEY_VALUE_HEADS, -1)
    keys = jnp.stack([keys[:, group] for group in group_index])
    values = jnp.stack([values[:, group] for group in group_index])
    return jnp.concatenate([query, keys, values], axis=2)


def gathered_body(
    tokens,
    query_key_value_weight,
    w_out_t,
    w_router,
    w_in,
    w_down,
    attn_gain,
    ffn_gain,
    q_gain,
    k_gain,
    routes,
    cotangent,
):
    bf16, f32 = jnp.bfloat16, jnp.float32
    both = ("seq", "fsdp")
    seq_size = lax.axis_size("seq")
    shard_size = lax.axis_size("fsdp")
    experts = seq_size * shard_size
    rows = tokens.shape[1]
    width = tokens.shape[2]
    length = rows * seq_size
    weight_rows = query_key_value_weight.shape[0]
    heads = QUERY_HEADS // seq_size
    head_cols = heads * HEAD_DIMENSION
    kv_cols = HEAD_DIMENSION
    proj_cols = head_cols + 2 * kv_cols
    all_cols = proj_cols + head_cols
    spare_cols = 128
    group_index = [s * heads * KEY_VALUE_HEADS // QUERY_HEADS for s in range(seq_size)]
    capacity = 2 * rows * TOPK // experts

    pieces = jnp.concatenate(
        [
            head_columns(query_key_value_weight, group_index),
            w_out_t.reshape(weight_rows, seq_size, head_cols).transpose(1, 0, 2),
            jnp.broadcast_to(
                jnp.pad(w_router, ((0, 0), (0, spare_cols - experts))),
                (seq_size, weight_rows, spare_cols),
            ),
        ],
        axis=2,
    )
    half_dim = HEAD_DIMENSION // 2
    exponents = -2.0 * np.arange(half_dim, dtype=np.float32) / HEAD_DIMENSION
    frequency = np.float32(ROPE_BASE) ** exponents.astype(np.float32)
    angles = np.arange(length, dtype=np.float32)[:, None] * frequency[None, :]
    cosine, sine = np.cos(angles), np.sin(angles)
    cosine = jnp.asarray(np.concatenate([cosine, cosine], axis=1), f32)
    sine = jnp.asarray(np.concatenate([sine, -sine], axis=1), f32)
    (
        normed_all,
        columns,
        cot_all,
        queries,
        keys,
        values,
        attended,
        q_raw,
        k_raw,
        hidden,
        gates,
        routed,
    ) = front(
        tokens[0],
        pieces,
        cotangent[0],
        cosine,
        sine,
        q_gain[None],
        k_gain[None],
        attn_gain[None],
        ffn_gain[None],
        routes[0].T,
        head_cols,
        1,
    )
    normed_all = normed_all.reshape(length, width)

    gate_weight = w_in[0]
    down_weight = w_down[0]
    unused_rows, out_part, d_part, rows_in, d_expert, inner_act, d_gate_up = experts_gathered(
        routed,
        cot_all,
        gate_weight,
        down_weight,
        capacity,
        3,
    )
    d_attn, d_logits, d_hidden, gains, out_pair, d_w_in, d_w_down = sum_all(
        d_part,
        out_part,
        rows_in,
        d_gate_up,
        inner_act,
        d_expert,
        columns,
        hidden,
        cotangent[0],
        gates,
        ffn_gain[None],
        5,
    )
    d_w_in, d_w_down = d_w_in.astype(f32)[None], d_w_down.astype(f32)[None]

    d_tokens, d_w_qkv, d_w_out_t, d_w_router, gains, mixture = back(
        d_attn,
        out_pair.reshape(2 * seq_size, rows, width),
        columns.reshape(seq_size, 2, shard_size // 2, weight_rows, all_cols + spare_cols),
        normed_all,
        queries,
        keys,
        values,
        attended,
        q_raw,
        k_raw,
        cosine,
        sine,
        q_gain[None],
        k_gain[None],
        attn_gain[None],
        gains,
        tokens[0],
        d_hidden,
        routed,
        d_logits,
        6,
    )
    output = (hidden + mixture.astype(f32)).astype(bf16)
    d_tokens = d_tokens[None]
    d_w_router = d_w_router[:, :experts]
    d_attn_gain, d_ffn_gain = gains[0], gains[1]
    d_q_gain = gains[2, :HEAD_DIMENSION]
    d_k_gain = gains[2, HEAD_DIMENSION : 2 * HEAD_DIMENSION]
    return (
        output[None],
        d_tokens,
        d_w_qkv,
        d_w_out_t,
        d_w_router,
        d_w_in,
        d_w_down,
        d_attn_gain,
        d_ffn_gain,
        d_q_gain,
        d_k_gain,
    )


def gathered_fits(mesh):
    return mesh.shape["seq"] == 8 and mesh.shape["fsdp"] == 4


def solution(mesh):
    return jax.shard_map(
        gathered_body if gathered_fits(mesh) else routed_body,
        mesh=mesh,
        in_specs=(
            P("fsdp", "seq", None),
            P(("seq", "fsdp"), None),
            P(("seq", "fsdp"), None),
            P(("seq", "fsdp"), None),
            P(("seq", "fsdp"), None, None),
            P(("seq", "fsdp"), None, None),
            P(),
            P(),
            P(),
            P(),
            P("fsdp", "seq", None),
            P("fsdp", "seq", None),
        ),
        out_specs=(
            P("fsdp", "seq", None),
            P("fsdp", "seq", None),
            P(("seq", "fsdp"), None),
            P(("seq", "fsdp"), None),
            P(("seq", "fsdp"), None),
            P(("seq", "fsdp"), None, None),
            P(("seq", "fsdp"), None, None),
            P(),
            P(),
            P(),
            P(),
        ),
        check_vma=False,
    )
```

```python
from functools import partial
import math

import jax
import jax.numpy as jnp
import numpy as np
from jax import lax
from jax.experimental import pallas as pl
from jax.experimental.pallas import tpu as pltpu
from jax.sharding import PartitionSpec as P

QUERY_HEADS = 32
KEY_VALUE_HEADS = 4
HEAD_DIMENSION = 128
FF = 768
TOPK = 8


EPS = 1e-06
ROPE_BASE = 1000000.0


def rms_scale(values, gain):
    return values * lax.rsqrt(jnp.mean(values * values, axis=-1, keepdims=True) + EPS) * gain


def rotate(values, positions):
    half_dim = values.shape[-1] // 2
    frequency = ROPE_BASE ** (-2.0 * jnp.arange(half_dim, dtype=jnp.float32) / values.shape[-1])
    angles = positions.astype(jnp.float32)[:, None] * frequency[None, :]
    cosine = jnp.cos(angles)[:, None, :]
    sine_part = jnp.sin(angles)[:, None, :]
    first_half = values[..., :half_dim]
    second = values[..., half_dim:]
    return jnp.concatenate(
        [first_half * cosine - second * sine_part, second * cosine + first_half * sine_part],
        axis=-1,
    )


def head_prepare(raw_heads, gain, positions):
    return rotate(rms_scale(raw_heads, gain), positions)


def route_slots(route_flat, experts):
    onehot = (route_flat[:, None] == jnp.arange(experts, dtype=jnp.int32)[None, :]).astype(
        jnp.int32
    )
    earlier = jnp.cumsum(onehot, axis=0) - onehot
    return (onehot, jnp.sum(earlier * onehot, axis=1))


def pack_slots(row_values, expert_ids, slot_index, slot_shape):
    buffer = jnp.zeros(slot_shape, row_values.dtype)
    return buffer.at[expert_ids // slot_shape[1], expert_ids % slot_shape[1], slot_index].set(
        row_values
    )


def unpack_slots(buffer, expert_ids, slot_index):
    return buffer[expert_ids // buffer.shape[1], expert_ids % buffer.shape[1], slot_index]


def causal_scores(query_part, key_full, row_start):
    block_rows = query_part.shape[0]
    score_scale = 1.0 / math.sqrt(query_part.shape[2])
    scores = (
        jnp.einsum("qhd,khd->hqk", query_part, key_full, preferred_element_type=jnp.float32)
        * score_scale
    )
    key_pos = jnp.arange(key_full.shape[0], dtype=jnp.int32)
    row_pos = row_start + jnp.arange(block_rows, dtype=jnp.int32)
    allowed = key_pos[None, :] <= row_pos[:, None]
    return jnp.where(allowed[None], scores, -1e30)


def attend_forward(query_rows_all, key_full, value_full):
    sequence_length = query_rows_all.shape[0]
    block_rows = min(512, sequence_length)

    def one_block(block_index):
        row_start = block_index * block_rows
        query_part = lax.dynamic_slice_in_dim(query_rows_all, row_start, block_rows, 0)
        scores = causal_scores(query_part, key_full, row_start)
        row_max = jnp.max(scores, axis=-1, keepdims=True)
        weights = jnp.exp(scores - row_max)
        row_total = jnp.sum(weights, axis=-1, keepdims=True)
        prob_low = (weights / row_total).astype(jnp.bfloat16)
        mixed_out = jnp.einsum(
            "hqk,khd->qhd", prob_low, value_full, preferred_element_type=jnp.float32
        )
        return (mixed_out.astype(jnp.bfloat16), (row_max + jnp.log(row_total))[..., 0])

    mixed_out, log_total = lax.map(
        one_block, jnp.arange(sequence_length // block_rows, dtype=jnp.int32)
    )
    return (mixed_out.reshape(query_rows_all.shape), log_total)


def attend_backward(query_rows_all, key_full, value_full, log_total, d_mixed):
    sequence_length = query_rows_all.shape[0]
    block_rows = min(512, sequence_length)
    score_scale = 1.0 / math.sqrt(query_rows_all.shape[2])

    def one_block(running, block_index):
        d_key_sum, d_value_sum = running
        row_start = block_index * block_rows
        query_part = lax.dynamic_slice_in_dim(query_rows_all, row_start, block_rows, 0)
        d_part = lax.dynamic_slice_in_dim(d_mixed, row_start, block_rows, 0)
        scores = causal_scores(query_part, key_full, row_start)
        prob_full = jnp.exp(scores - log_total[block_index][..., None])
        prob_low = prob_full.astype(jnp.bfloat16)
        d_probs = jnp.einsum("qhd,khd->hqk", d_part, value_full, preferred_element_type=jnp.float32)
        row_delta = jnp.sum(prob_full * d_probs, axis=-1, keepdims=True)
        d_scores = (prob_full * (d_probs - row_delta)).astype(jnp.bfloat16)
        d_query_part = (
            jnp.einsum("hqk,khd->qhd", d_scores, key_full, preferred_element_type=jnp.float32)
            * score_scale
        )
        d_key_sum = (
            d_key_sum
            + jnp.einsum("hqk,qhd->khd", d_scores, query_part, preferred_element_type=jnp.float32)
            * score_scale
        )
        d_value_sum = d_value_sum + jnp.einsum(
            "hqk,qhd->khd", prob_low, d_part, preferred_element_type=jnp.float32
        )
        return ((d_key_sum, d_value_sum), d_query_part)

    zero_grad = jnp.zeros(key_full.shape, jnp.float32)
    (d_key_sum, d_value_sum), d_query = lax.scan(
        one_block,
        (zero_grad, zero_grad),
        jnp.arange(sequence_length // block_rows, dtype=jnp.int32),
    )
    return (d_query.reshape(query_rows_all.shape), d_key_sum, d_value_sum)


def routed_body(
    tokens,
    query_key_value_weight,
    w_out_t,
    w_router,
    w_in,
    w_down,
    attn_gain,
    ffn_gain,
    q_gain,
    k_gain,
    routes,
    cotangent,
):
    sequence_count = lax.axis_size("seq")
    shard_count = lax.axis_size("fsdp")
    experts = sequence_count * shard_count
    token_row_count = tokens.shape[1]
    model_width = tokens.shape[2]
    query_group_width = QUERY_HEADS // KEY_VALUE_HEADS
    capacity = 2 * token_row_count * TOPK // experts
    slot_shape = (sequence_count, shard_count, capacity, model_width)
    positions = lax.axis_index("seq") * token_row_count + jnp.arange(
        token_row_count, dtype=jnp.int32
    )
    full_qkv, full_out, full_router = (
        lax.all_gather(query_key_value_weight, ("seq", "fsdp"), axis=0, tiled=True),
        lax.all_gather(w_out_t, ("seq", "fsdp"), axis=0, tiled=True),
        lax.all_gather(w_router, ("seq", "fsdp"), axis=0, tiled=True),
    )
    resid_in = tokens[0].astype(jnp.float32)
    normed_one = rms_scale(resid_in, attn_gain).astype(jnp.bfloat16)
    projection_output = jnp.dot(normed_one, full_qkv, preferred_element_type=jnp.float32)
    q_raw = projection_output[:, : QUERY_HEADS * HEAD_DIMENSION].reshape(
        token_row_count, QUERY_HEADS, HEAD_DIMENSION
    )
    key_unnormed = projection_output[
        :, QUERY_HEADS * HEAD_DIMENSION : (QUERY_HEADS + KEY_VALUE_HEADS) * HEAD_DIMENSION
    ].reshape(token_row_count, KEY_VALUE_HEADS, HEAD_DIMENSION)
    value_per_head = (
        projection_output[:, (QUERY_HEADS + KEY_VALUE_HEADS) * HEAD_DIMENSION :]
        .reshape(token_row_count, KEY_VALUE_HEADS, HEAD_DIMENSION)
        .astype(jnp.bfloat16)
    )
    prepare = partial(head_prepare, positions=positions)
    query_rows_all = prepare(q_raw, q_gain).astype(jnp.bfloat16)
    key_per_head = prepare(key_unnormed, k_gain).astype(jnp.bfloat16)
    send_keys = jnp.repeat(key_per_head, query_group_width, axis=1)
    send_values = jnp.repeat(value_per_head, query_group_width, axis=1)
    head_queries, head_keys, head_values = (
        lax.all_to_all(query_rows_all, "seq", split_axis=1, concat_axis=0, tiled=True),
        lax.all_to_all(send_keys, "seq", split_axis=1, concat_axis=0, tiled=True),
        lax.all_to_all(send_values, "seq", split_axis=1, concat_axis=0, tiled=True),
    )
    mixed_heads, log_total = attend_forward(head_queries, head_keys, head_values)
    mixed_tok = lax.all_to_all(mixed_heads, "seq", split_axis=0, concat_axis=1, tiled=True)
    attention_result = mixed_tok.reshape(token_row_count, QUERY_HEADS * HEAD_DIMENSION)
    attn_out = jnp.einsum(
        "tj,dj->td", attention_result, full_out, preferred_element_type=jnp.float32
    )
    hidden = resid_in + attn_out
    normed_two = rms_scale(hidden, ffn_gain).astype(jnp.bfloat16)
    logits = jnp.dot(normed_two, full_router, preferred_element_type=jnp.float32)
    route_flat = routes[0].reshape(-1)
    onehot, slot_index = route_slots(route_flat, experts)
    onehot_float = onehot.reshape(token_row_count, TOPK, experts).astype(jnp.float32)
    chosen = jnp.sum(onehot_float * logits[:, None, :], axis=-1)
    row_max = jnp.max(chosen, axis=-1, keepdims=True)
    exp_part = jnp.exp(chosen - row_max)
    gate_probs = exp_part / jnp.sum(exp_part, axis=-1, keepdims=True)
    send_rows = pack_slots(jnp.repeat(normed_two, TOPK, axis=0), route_flat, slot_index, slot_shape)
    arrived = lax.all_to_all(
        lax.all_to_all(send_rows, "seq", split_axis=0, concat_axis=0, tiled=True),
        "fsdp",
        split_axis=1,
        concat_axis=1,
        tiled=True,
    )
    rows_in = arrived.reshape(-1, model_width)
    gate_weight = w_in[0]
    down_weight = w_down[0]
    gate_up = jnp.dot(rows_in, gate_weight, preferred_element_type=jnp.float32)
    gate_half = gate_up[:, :FF]
    up_half = gate_up[:, FF:]
    gate_sig = jax.nn.sigmoid(gate_half)
    silu_gate = gate_half * gate_sig
    inner_act = (silu_gate * up_half).astype(jnp.bfloat16)
    expert_out = jnp.dot(inner_act, down_weight, preferred_element_type=jnp.float32).astype(
        jnp.bfloat16
    )
    returned = lax.all_to_all(
        lax.all_to_all(
            expert_out.reshape(slot_shape), "seq", split_axis=0, concat_axis=0, tiled=True
        ),
        "fsdp",
        split_axis=1,
        concat_axis=1,
        tiled=True,
    )
    picked = (
        unpack_slots(returned, route_flat, slot_index)
        .astype(jnp.float32)
        .reshape(token_row_count, TOPK, model_width)
    )
    mixture = jnp.sum(gate_probs[..., None] * picked, axis=1)
    output = (hidden + mixture).astype(jnp.bfloat16)
    full_qkv, full_out, full_router = (
        lax.all_gather(query_key_value_weight, ("seq", "fsdp"), axis=0, tiled=True),
        lax.all_gather(w_out_t, ("seq", "fsdp"), axis=0, tiled=True),
        lax.all_gather(w_router, ("seq", "fsdp"), axis=0, tiled=True),
    )
    out_grad = cotangent[0].astype(jnp.float32)
    d_picked = (
        (gate_probs[..., None] * out_grad[:, None, :]).astype(jnp.bfloat16).reshape(-1, model_width)
    )
    d_gates = jnp.sum(picked * out_grad[:, None, :], axis=-1)
    d_send = pack_slots(d_picked, route_flat, slot_index, slot_shape)
    d_arrived = lax.all_to_all(
        lax.all_to_all(d_send, "seq", split_axis=0, concat_axis=0, tiled=True),
        "fsdp",
        split_axis=1,
        concat_axis=1,
        tiled=True,
    ).reshape(-1, model_width)
    d_inner = jnp.einsum("rd,fd->rf", d_arrived, down_weight, preferred_element_type=jnp.float32)
    d_gate_half = d_inner * up_half * gate_sig * (1.0 + gate_half * (1.0 - gate_sig))
    d_up_half = d_inner * silu_gate
    d_gate_up = jnp.concatenate([d_gate_half, d_up_half], axis=1).astype(jnp.bfloat16)
    d_w_down = jnp.einsum("rf,rd->fd", inner_act, d_arrived, preferred_element_type=jnp.float32)[
        None
    ]
    d_w_in = jnp.einsum("rd,rf->df", rows_in, d_gate_up, preferred_element_type=jnp.float32)[None]
    d_rows = jnp.einsum(
        "rf,df->rd", d_gate_up, gate_weight, preferred_element_type=jnp.float32
    ).astype(jnp.bfloat16)
    d_back = lax.all_to_all(
        lax.all_to_all(d_rows.reshape(slot_shape), "seq", split_axis=0, concat_axis=0, tiled=True),
        "fsdp",
        split_axis=1,
        concat_axis=1,
        tiled=True,
    )
    d_routed = jnp.sum(
        unpack_slots(d_back, route_flat, slot_index)
        .astype(jnp.float32)
        .reshape(token_row_count, TOPK, model_width),
        axis=1,
    )
    d_chosen = gate_probs * (d_gates - jnp.sum(gate_probs * d_gates, axis=-1, keepdims=True))
    d_logits = jnp.einsum("tk,tke->te", d_chosen, onehot_float).astype(jnp.bfloat16)
    d_normed_two = d_routed + jnp.einsum(
        "te,de->td", d_logits, full_router, preferred_element_type=jnp.float32
    )
    unused_two, pull_two = jax.vjp(rms_scale, hidden, ffn_gain)
    d_hidden_norm, d_ffn_gain = pull_two(d_normed_two)
    d_hidden = out_grad + d_hidden_norm
    d_attn = d_hidden.astype(jnp.bfloat16)
    d_attended = jnp.einsum(
        "td,dj->tj", d_attn, full_out, preferred_element_type=jnp.float32
    ).astype(jnp.bfloat16)
    d_heads = lax.all_to_all(
        d_attended.reshape(token_row_count, QUERY_HEADS, HEAD_DIMENSION),
        "seq",
        split_axis=1,
        concat_axis=0,
        tiled=True,
    )
    d_query, d_key_sum, d_value_sum = attend_backward(
        head_queries, head_keys, head_values, log_total, d_heads
    )
    seq_rows = head_queries.shape[0]
    local_cols = head_queries.shape[1] * HEAD_DIMENSION
    normed_all, d_attn_all = (
        lax.all_gather(normed_one, "seq", axis=0, tiled=True),
        lax.all_gather(d_attn, "seq", axis=0, tiled=True),
    )
    query_cols = lax.dynamic_slice_in_dim(
        full_qkv, lax.axis_index("seq") * local_cols, local_cols, 1
    )
    q_head_raw = jnp.dot(normed_all, query_cols, preferred_element_type=jnp.float32).reshape(
        head_queries.shape
    )
    seq_positions = jnp.arange(seq_rows, dtype=jnp.int32)
    unused_head, pull_head = jax.vjp(
        partial(head_prepare, positions=seq_positions), q_head_raw, q_gain
    )
    send_d_query, d_q_gain = pull_head(d_query)
    d_query_tok, grad_key_token_rows, grad_value_token_rows = (
        lax.all_to_all(
            send_d_query.astype(jnp.bfloat16), "seq", split_axis=0, concat_axis=1, tiled=True
        ).astype(send_d_query.dtype),
        lax.all_to_all(
            d_key_sum.astype(jnp.bfloat16), "seq", split_axis=0, concat_axis=1, tiled=True
        ).astype(d_key_sum.dtype),
        lax.all_to_all(
            d_value_sum.astype(jnp.bfloat16), "seq", split_axis=0, concat_axis=1, tiled=True
        ).astype(d_value_sum.dtype),
    )
    grad_key_per_head = jnp.sum(
        grad_key_token_rows.reshape(token_row_count, KEY_VALUE_HEADS, -1, HEAD_DIMENSION), axis=2
    )
    grad_value_per_head = jnp.sum(
        grad_value_token_rows.reshape(token_row_count, KEY_VALUE_HEADS, -1, HEAD_DIMENSION), axis=2
    )
    unused_k, pull_k = jax.vjp(prepare, key_unnormed, k_gain)
    grad_key_unnormed, d_k_gain = pull_k(grad_key_per_head)
    d_projected = jnp.concatenate(
        [
            d_query_tok.reshape(token_row_count, QUERY_HEADS * HEAD_DIMENSION),
            grad_key_unnormed.reshape(token_row_count, KEY_VALUE_HEADS * HEAD_DIMENSION),
            grad_value_per_head.reshape(token_row_count, KEY_VALUE_HEADS * HEAD_DIMENSION),
        ],
        axis=1,
    ).astype(jnp.bfloat16)
    d_normed_one = jnp.einsum(
        "tj,dj->td", d_projected, full_qkv, preferred_element_type=jnp.float32
    )
    unused_one, pull_one = jax.vjp(rms_scale, resid_in, attn_gain)
    d_resid_norm, d_attn_gain = pull_one(d_normed_one)
    d_tokens = (d_hidden + d_resid_norm).astype(jnp.bfloat16)[None]
    rows_dev = model_width // experts
    kv_count = 2 * KEY_VALUE_HEADS * HEAD_DIMENSION
    kv_grads = d_projected[:, QUERY_HEADS * HEAD_DIMENSION :]
    first_rows = normed_one
    summed = lax.psum_scatter(
        jnp.concatenate(
            [
                jnp.einsum("tc,tj->cj", first_rows, kv_grads, preferred_element_type=jnp.float32),
                jnp.einsum("tc,te->ce", normed_two, d_logits, preferred_element_type=jnp.float32),
            ],
            axis=1,
        ),
        ("seq", "fsdp"),
        scatter_dimension=0,
        tiled=True,
    )
    d_query_low = send_d_query.reshape(seq_rows, local_cols).astype(jnp.bfloat16)
    attended_heads = mixed_heads.reshape(seq_rows, local_cols)
    normed_order = (
        normed_all.reshape(seq_rows, sequence_count, shard_count, rows_dev)
        .transpose(0, 2, 1, 3)
        .reshape(seq_rows, model_width)
    )
    d_attn_order = (
        d_attn_all.reshape(seq_rows, sequence_count, shard_count, rows_dev)
        .transpose(0, 2, 1, 3)
        .reshape(seq_rows, model_width)
    )
    first_rows = normed_order
    head_sums = lax.psum_scatter(
        jnp.concatenate(
            [
                jnp.einsum(
                    "tc,tj->cj", first_rows, d_query_low, preferred_element_type=jnp.float32
                ),
                jnp.einsum(
                    "tc,tj->cj", d_attn_order, attended_heads, preferred_element_type=jnp.float32
                ),
            ],
            axis=1,
        ).astype(jnp.bfloat16),
        "fsdp",
        scatter_dimension=0,
        tiled=True,
    ).astype(jnp.float32)
    row_sums = (
        lax.all_to_all(
            head_sums.astype(jnp.bfloat16), "seq", split_axis=0, concat_axis=1, tiled=True
        )
        .astype(head_sums.dtype)
        .reshape(rows_dev, sequence_count, 2, local_cols)
    )
    d_w_query = row_sums[:, :, 0].reshape(rows_dev, QUERY_HEADS * HEAD_DIMENSION)
    d_w_out_t = row_sums[:, :, 1].reshape(rows_dev, QUERY_HEADS * HEAD_DIMENSION)
    d_w_qkv = jnp.concatenate([d_w_query, summed[:, :kv_count]], axis=1)
    d_w_router = summed[:, kv_count:]
    d_attn_gain, d_ffn_gain, d_q_gain, d_k_gain = lax.psum(
        (d_attn_gain, d_ffn_gain, d_q_gain, d_k_gain), ("seq", "fsdp")
    )
    return (
        output[None],
        d_tokens,
        d_w_qkv,
        d_w_out_t,
        d_w_router,
        d_w_in,
        d_w_down,
        d_attn_gain,
        d_ffn_gain,
        d_q_gain,
        d_k_gain,
    )


MESH = pl.DeviceIdType.MESH
VMEM_LIMIT = 60 * 2**20


class Place:
    def __init__(self):
        seq, shard = lax.axis_index("seq"), lax.axis_index("fsdp")
        self.z, self.x = seq // 2, seq % 2
        self.y, self.c = shard // 2, shard % 2
        self.z0, self.z1 = self.z % 2, self.z // 2
        self.low, self.high = self.z == 0, self.z == 3
        self.inner = (self.z0 + self.z1) == 1
        self.me = self.block(self.z, self.x, self.y, self.c)

    def device(self, z, x, y, c):
        return (z * 2 + x, y * 2 + c)

    def block(self, z, x, y, c):
        return (z * 2 + x) * 4 + y * 2 + c

    @property
    def by_x(self):
        return self.device(self.z, 1 - self.x, self.y, self.c)

    @property
    def by_y(self):
        return self.device(self.z, self.x, 1 - self.y, self.c)

    @property
    def by_core(self):
        return self.device(self.z, self.x, self.y, 1 - self.c)

    def by_z(self, step):
        return self.device(self.z + step, self.x, self.y, self.c)

    def near(self, k):
        return [self.z, 1 + self.z0, 2 - 2 * self.z0 + self.z1, 3 - 3 * self.z1][k]

    def onward(self, k):
        return [None, 2 * self.z1 - 1, 1 - 2 * self.z1, 2 * self.z1 - 1][k]

    def far(self, k):
        return self.near(3 - k)

    def toward(self, k):
        return [1 - 2 * self.z1, 1 - 2 * self.z0, 1 - 2 * self.z1][k]

    def greet(self, sides):
        barrier = pltpu.get_barrier_semaphore()
        for side in sides:
            if side != "z":
                target = {"x": self.by_x, "y": self.by_y, "core": self.by_core}[side]
                pl.semaphore_signal(barrier, inc=1, device_id=target, device_id_type=MESH)
        count = len([side for side in sides if side != "z"])
        if "z" in sides:

            @pl.when(jnp.logical_not(self.low))
            def _():
                pl.semaphore_signal(barrier, inc=1, device_id=self.by_z(-1), device_id_type=MESH)

            @pl.when(jnp.logical_not(self.high))
            def _():
                pl.semaphore_signal(barrier, inc=1, device_id=self.by_z(1), device_id_type=MESH)

            count = count + 1 + (self.z0 + self.z1) % 2
        pl.semaphore_wait(barrier, count)


def send(source, target, send_sem, recv_sem, device):
    pltpu.make_async_remote_copy(
        src_ref=source,
        dst_ref=target,
        send_sem=send_sem,
        recv_sem=recv_sem,
        device_id=device,
        device_id_type=MESH,
    ).start()


def await_bytes(ref, sem):
    pltpu.make_async_copy(ref, ref, sem).wait()


G_Z, G_X, G_Y, G_DX, G_DY, G_C0 = 0, 1, 2, 3, 4, 5
G_KINDS = 9


def gather_steps(place, own, out, ss, rs, zs, local_sem):
    p = place
    rows = out.shape[1]
    half = rows // 2
    x, y, c = p.x, p.y, p.c

    def cols(q):
        return [
            p.block(q, x, y, c),
            p.block(q, 1 - x, y, c),
            p.block(q, x, 1 - y, c),
            p.block(q, 1 - x, 1 - y, c),
        ]

    def to_core(q, j, src=None):
        b = cols(q)[j]
        send(out.at[b] if src is None else src, out.at[b], ss.at[q, G_C0 + j], rs.at[q, G_C0 + j], p.by_core)

    def plane_out(k):
        q = p.near(k)
        b = cols(q)[0]
        if k == 0:
            src = own
            for step, there in ((1, p.high), (-1, p.low)):

                @pl.when(jnp.logical_not(there))
                def _():
                    send(src, out.at[b], zs.at[q, 0 if step > 0 else 1], rs.at[q, G_Z], p.by_z(step))

            pltpu.make_async_copy(own, out.at[b], local_sem).start()
        else:
            src = out.at[b]

            @pl.when(jnp.logical_not(p.inner))
            def _():
                await_bytes(src, rs.at[q, G_Z])

        send(src, out.at[b], ss.at[q, G_X], rs.at[q, G_X], p.by_x)
        send(src, out.at[b], ss.at[q, G_Y], rs.at[q, G_Y], p.by_y)
        to_core(q, 0, src)

    def plane_hop(k):
        q = p.near(k)
        src = out.at[cols(q)[0]]

        @pl.when(p.inner)
        def _():
            await_bytes(src, rs.at[q, G_Z])
            send(src, src, zs.at[q, 0], rs.at[q, G_Z], p.by_z(p.onward(k)))

    def plane_turn(k):
        q = p.near(k)
        bx, by = out.at[cols(q)[1]], out.at[cols(q)[2]]
        await_bytes(bx, rs.at[q, G_X])
        first = bx.at[pl.ds(0, half)]
        send(first, first, ss.at[q, G_DY], rs.at[q, G_DY], p.by_y)
        to_core(q, 1)
        await_bytes(by, rs.at[q, G_Y])
        second = by.at[pl.ds(half, half)]
        send(second, second, ss.at[q, G_DX], rs.at[q, G_DX], p.by_x)
        to_core(q, 2)

    def plane_end(k):
        q = p.near(k)
        bd = out.at[cols(q)[3]]
        await_bytes(bd.at[pl.ds(0, half)], rs.at[q, G_DY])
        await_bytes(bd.at[pl.ds(half, half)], rs.at[q, G_DX])
        to_core(q, 3)

    def plane_core(k, js=(0, 1, 2, 3)):
        q = p.near(k)
        for j in js:
            await_bytes(own, rs.at[q, G_C0 + j])

    def finish():
        piece = own.at[pl.ds(0, half)]
        for q in range(4):
            for kind in (G_X, G_Y, G_C0, G_C0 + 1, G_C0 + 2, G_C0 + 3):
                await_bytes(own, ss.at[q, kind])
            for kind in (G_DX, G_DY):
                await_bytes(piece, ss.at[q, kind])
        for there, slot in ((p.high, 0), (p.low, 1)):

            @pl.when(jnp.logical_not(there))
            def _():
                await_bytes(own, zs.at[p.z, slot])

        for k in range(1, 4):

            @pl.when(p.inner)
            def _():
                await_bytes(own, zs.at[p.near(k), 0])

    return plane_out, plane_hop, plane_turn, plane_end, plane_core, finish


def sum_all_parts(p, part, held, core_in, x_half, y_half, x_in, y_in, z_in, out, ls, cs, cr, ss, rs, zs, zr):
    rows, width = part.shape[1], part.shape[2]
    half = rows // 2
    x, y, c = p.x, p.y, p.c

    def columns(q):
        return [(q, x, y), (q, 1 - x, y), (q, x, 1 - y), (q, 1 - x, 1 - y)]

    def start():
        for k in range(4):
            q = p.far(k)
            for j, (zz, xx, yy) in reversed(list(enumerate(columns(q)))):
                send(
                    part.at[p.block(zz, xx, yy, 1 - c)],
                    core_in.at[q * 4 + j],
                    cs.at[q, j],
                    cr.at[q, j],
                    p.by_core,
                )
                pltpu.make_async_copy(
                    part.at[p.block(zz, xx, yy, c)], held.at[q * 4 + j], ls.at[q, j]
                ).start()

    add = add_rows

    def plane_core(k, js=(3, 1, 2, 0)):
        q = p.far(k)
        for j in js:
            slot = q * 4 + j
            await_bytes(held.at[slot], ls.at[q, j])
            await_bytes(core_in.at[slot], cr.at[q, j])
            add(held.at[slot], core_in.at[slot], rows)
            if j == 3:
                send(held.at[slot, pl.ds(0, half)], y_half.at[q], ss.at[q, 0], rs.at[q, 0], p.by_y)
                send(held.at[slot, pl.ds(half, half)], x_half.at[q], ss.at[q, 1], rs.at[q, 1], p.by_x)

    def plane_turn(k):
        q = p.far(k)
        await_bytes(y_half.at[q], rs.at[q, 0])
        add(held.at[q * 4 + 1, pl.ds(0, half)], y_half.at[q], half)
        send(held.at[q * 4 + 1], x_in.at[q], ss.at[q, 2], rs.at[q, 2], p.by_x)
        await_bytes(x_half.at[q], rs.at[q, 1])
        add(held.at[q * 4 + 2, pl.ds(half, half)], x_half.at[q], half)
        send(held.at[q * 4 + 2], y_in.at[q], ss.at[q, 3], rs.at[q, 3], p.by_y)

    def plane_end(k):
        q = p.far(k)
        mine = held.at[q * 4]
        await_bytes(x_in.at[q], rs.at[q, 2])
        add(mine, x_in.at[q], rows)
        await_bytes(y_in.at[q], rs.at[q, 3])
        add(mine, y_in.at[q], rows)
        if k < 3:
            step = p.toward(k)
            slot = (1 - step) // 2

            @pl.when(p.inner)
            def _():
                await_bytes(z_in.at[slot, q], zr.at[slot, q])
                add(mine, z_in.at[slot, q], rows)

            send(mine, z_in.at[slot, q], zs.at[k], zr.at[slot, q], p.by_z(step))
        else:
            for slot, there in ((0, p.low), (1, p.high)):

                @pl.when(jnp.logical_not(there))
                def _():
                    await_bytes(z_in.at[slot, q], zr.at[slot, q])
                    add(mine, z_in.at[slot, q], rows)

            out[...] = mine[...]

    def finish():
        whole, piece = x_in.at[0], x_half.at[0]
        for q in range(4):
            for j in range(4):
                await_bytes(whole, cs.at[q, j])
            for kind in (0, 1):
                await_bytes(piece, ss.at[q, kind])
            for kind in (2, 3):
                await_bytes(whole, ss.at[q, kind])
        for k in range(3):
            await_bytes(whole, zs.at[k])

    return start, plane_core, plane_turn, plane_end, finish


def sum_all_kernel(
    part, both, rows_in, d_gate_up, inner, d_expert, columns, hidden, cot, gates, ffn_gain,
    out, d_logits, d_hidden, gains, pair, d_w_in, d_w_down,
    d_rows, router, router_sem, both_held, both_in, left, product, pair_sems, load_sems, left_sems, product_sems, *scratch,
):
    p = Place()
    p.greet(("x", "y", "core", "z"))
    start, plane_core, plane_turn, plane_end, finish = sum_all_parts(p, part, *scratch[:7], d_rows, *scratch[7:])
    rows = both.shape[3]

    def pair_sum(first):
        for s in (first, first + 1):
            for y in range(2):
                add_rows(both_held.at[s, y], both_in.at[s, y], rows)

    def right_load(source, i):
        width = source.shape[3]
        return pltpu.make_async_copy(source, both_in.at[:, :, :, pl.ds(0, width)], load_sems.at[i])

    def left_load(source, i, slot):
        cols = pl.ds(pl.multiple_of(i * TILE, TILE), TILE)
        return pltpu.make_async_copy(source.at[:, cols], left.at[slot], left_sems.at[slot])

    def product_store(target, i, slot):
        at = pl.ds(pl.multiple_of(i * TILE, TILE), TILE)
        piece = product.at[slot, :, pl.ds(0, target.shape[1])]
        return pltpu.make_async_copy(piece, target.at[at], product_sems.at[slot])

    def tiles(source, target, first, last):
        count, wide = source.shape[1] // TILE, target.shape[1]

        @pl.loop(first, last)
        def _(i):
            slot = i % 2
            left_load(source, i, slot).wait()

            @pl.when(i + 1 < count)
            def _():
                left_load(source, i + 1, 1 - slot).start()

            @pl.when(i >= 2)
            def _():
                product_store(target, i - 2, slot).wait()

            right = both_in[:, :, :, :wide].reshape(source.shape[0], wide)
            product[slot, :, :wide] = mxu(left[slot], right, TN).astype(product.dtype)
            product_store(target, i, slot).start()

    def tiles_end(source, target):
        count = source.shape[1] // TILE
        for i in (count - 2, count - 1):
            product_store(target, i, i % 2).wait()

    first = columns.shape[2] - 128
    router_load = pltpu.make_async_copy(columns.at[:, :, pl.ds(first, 128)], router, router_sem)
    router_load.start()
    start()
    send(both.at[:, :, 1 - p.c], both_in, pair_sems.at[0], pair_sems.at[1], p.by_core)
    pltpu.make_async_copy(both.at[:, :, p.c], both_held, pair_sems.at[2]).start()
    plane_core(0)
    plane_core(1)
    plane_turn(0)
    await_bytes(both_held, pair_sems.at[2])
    await_bytes(both_in, pair_sems.at[1])
    pair_sum(0)
    plane_core(2)
    pair_sum(2)
    plane_turn(1)
    pair_sum(4)
    pair_sum(6)
    pltpu.make_async_copy(both_held, pair, pair_sems.at[2]).start()
    right_load(d_gate_up, 0).start()
    left_load(rows_in, 0, 0).start()
    plane_end(0)
    plane_core(3)
    right_load(d_gate_up, 0).wait()
    tiles(rows_in, d_w_in, 0, 2)
    plane_turn(2)
    tiles(rows_in, d_w_in, 2, 4)
    plane_end(1)
    tiles(rows_in, d_w_in, 4, 6)
    plane_turn(3)
    tiles(rows_in, d_w_in, 6, 8)
    right_load(d_expert, 1).start()
    tiles_end(rows_in, d_w_in)
    left_load(inner, 0, 0).start()
    plane_end(2)
    right_load(d_expert, 1).wait()
    tiles(inner, d_w_down, 0, 3)
    plane_end(3)
    router_load.wait()
    width = hidden.shape[1]
    experts = part.shape[0]
    tail = d_rows[:, width:].astype(jnp.float32)
    lane = lax.broadcasted_iota(jnp.int32, tail.shape, 1)
    d_gates = jnp.where(lane < experts, tail + pltpu.roll(tail, 128 - experts, 1), 0.0)
    gate = gates[...]
    d_chosen = gate * (d_gates - jnp.sum(gate * d_gates, axis=-1, keepdims=True))
    d_logits[...] = d_chosen.astype(d_logits.dtype)
    gains[...] = jnp.zeros_like(gains)
    chunk = 32

    @pl.loop(0, rows // chunk)
    def _(i):
        at = pl.ds(pl.multiple_of(i * chunk, chunk), chunk)
        routed = mxu(d_logits[at, :], router[...].reshape(width, 128), NT)
        d_out = d_rows[at, :width].astype(jnp.float32) + routed
        x = hidden[at, :]
        scale = lax.rsqrt(jnp.mean(x * x, axis=-1, keepdims=True) + EPS)
        u = d_out * ffn_gain[...]
        dot = jnp.mean(u * x, axis=-1, keepdims=True)
        grad = cot[at, :].astype(jnp.float32) + scale * u - x * (scale * scale * scale * dot)
        d_hidden[at, :] = grad
        out[at, :] = grad.astype(out.dtype)
        gains[1:2, :] += jnp.sum(d_out * x * scale, axis=0, keepdims=True)

    tiles_end(inner, d_w_down)
    finish()
    await_bytes(both_held, pair_sems.at[0])
    pltpu.make_async_copy(both_held, pair, pair_sems.at[2]).wait()


def sum_all_scratch(rows, width):
    dma = pltpu.SemaphoreType.DMA
    bf16 = jnp.bfloat16
    return [
        pltpu.VMEM((16, rows, width), bf16),
        pltpu.VMEM((16, rows, width), bf16),
        pltpu.VMEM((4, rows // 2, width), bf16),
        pltpu.VMEM((4, rows // 2, width), bf16),
        pltpu.VMEM((4, rows, width), bf16),
        pltpu.VMEM((4, rows, width), bf16),
        pltpu.VMEM((2, 4, rows, width), bf16),
        dma((4, 4)),
        dma((4, 4)),
        dma((4, 4)),
        dma((4, 4)),
        dma((4, 4)),
        dma((3,)),
        dma((2, 4)),
    ]


def sum_all(
    part, both, rows_in, d_gate_up, inner, d_expert, columns, hidden, cot, gates, ffn_gain, collective_id
):
    blocks, rows, width = part.shape
    both = both.reshape(blocks // 4, 2, 2, rows, -1)
    pair = (blocks // 4, 2, rows, both.shape[4])
    anywhere, vmem = pl.BlockSpec(memory_space=pl.ANY), pl.BlockSpec(memory_space=pltpu.VMEM)
    return pl.pallas_call(
        sum_all_kernel,
        out_shape=[
            jax.ShapeDtypeStruct(hidden.shape, part.dtype),
            jax.ShapeDtypeStruct((rows, 128), part.dtype),
            jax.ShapeDtypeStruct(hidden.shape, jnp.float32),
            jax.ShapeDtypeStruct((8, hidden.shape[1]), jnp.float32),
            jax.ShapeDtypeStruct(pair, both.dtype),
            jax.ShapeDtypeStruct((rows_in.shape[1], d_gate_up.shape[1]), both.dtype),
            jax.ShapeDtypeStruct((inner.shape[1], d_expert.shape[1]), both.dtype),
        ],
        in_specs=[anywhere] * 7 + [vmem] * 4,
        out_specs=[vmem] * 4 + [anywhere] * 3,
        scratch_shapes=[
            pltpu.VMEM((rows, width), part.dtype),
            pltpu.VMEM((*columns.shape[:2], 128), part.dtype),
            pltpu.SemaphoreType.DMA,
            pltpu.VMEM(pair, both.dtype),
            pltpu.VMEM(pair, both.dtype),
            pltpu.VMEM((2, rows_in.shape[0], TILE), both.dtype),
            pltpu.VMEM((2, TILE, d_expert.shape[1]), both.dtype),
            pltpu.SemaphoreType.DMA((3,)),
            pltpu.SemaphoreType.DMA((2,)),
            pltpu.SemaphoreType.DMA((2,)),
            pltpu.SemaphoreType.DMA((2,)),
            *sum_all_scratch(rows, width),
        ],
        compiler_params=pltpu.CompilerParams(
            collective_id=collective_id, has_side_effects=True, vmem_limit_bytes=VMEM_LIMIT
        ),
        name="sum_all",
    )(
        part,
        both,
        rows_in,
        d_gate_up.reshape(*pair[:3], -1),
        inner,
        d_expert.reshape(*pair[:3], -1),
        columns,
        hidden,
        cot,
        gates,
        ffn_gain,
    )


def add_rows(target, source, count, chunk=32):
    @pl.loop(0, count // chunk)
    def _(i):
        at = pl.ds(pl.multiple_of(i * chunk, chunk), chunk)
        target[at, :] = target[at, :] + source[at, :]


def seq_peer(p, d):
    return ((p.z * 2 + p.x + d) % 8, p.y * 2 + p.c)


def greet_seq(p, sides=("y", "core")):
    barrier = pltpu.get_barrier_semaphore()
    for d in range(1, 8):
        pl.semaphore_signal(barrier, inc=1, device_id=seq_peer(p, d), device_id_type=MESH)
    for side in sides:
        target = {"y": p.by_y, "core": p.by_core}[side]
        pl.semaphore_signal(barrier, inc=1, device_id=target, device_id_type=MESH)
    pl.semaphore_wait(barrier, 7 + len(sides))


NT = (((1,), (1,)), ((), ()))
TILE = 256
WIDE = 1024
TALL = 512


def mxu(a, b, dims=(((1,), (0,)), ((), ()))):
    return lax.dot_general(a, b, dims, preferred_element_type=jnp.float32)


def experts_kernel(
    own, cot_all, w_in_hbm, w_down_hbm,
    rows_all, out_part, d_part, x_all, d_expert_all, inner_all, d_gate_up_all,
    w_in, w_down, row_buf, cot_buf, pick, pick_t, gates, d_gates, x, cot, d_expert,
    by_d_gate, by_d_up, inner, d_gate_up, held, out_stage, d_stage,
    ss, rs, zs, local_sem, load_sems, store_sems,
):
    p = Place()
    bf16, f32 = jnp.bfloat16, jnp.float32
    width = cot_all.shape[2]
    blocks = 8
    slots = gates.shape[0]
    capacity = slots // blocks
    tokens = row_buf.shape[2]
    group = 4
    experts = rows_all.shape[0]
    p.greet(("x", "y", "core", "z"))
    plane_out, plane_hop, plane_turn, plane_end, plane_core, finish = gather_steps(
        p, own, rows_all, ss, rs, zs, local_sem
    )

    def weights(start):
        for i, (src, dst) in enumerate(((w_in_hbm, w_in), (w_down_hbm, w_down))):
            copy = pltpu.make_async_copy(src, dst, load_sems.at[i])
            copy.start() if start else copy.wait()

    def cot_load(k):
        return pltpu.make_async_copy(
            cot_all.at[pl.ds(p.near(k) * blocks, blocks)], cot_buf.at[k % 2], load_sems.at[2 + k]
        )

    def row_load(k):
        return pltpu.make_async_copy(
            rows_all.at[pl.ds(p.near(k) * blocks, blocks)], row_buf.at[k % 2], load_sems.at[6 + k]
        )

    def arrived(k):
        plane_core(k)
        row_load(k).start()

    sides = (p.x, 1 - p.x)

    def side_load(i):
        at = pl.ds(sides[i] * group, group)
        source = rows_all.at[pl.ds(p.z * blocks + sides[i] * group, group)]
        return pltpu.make_async_copy(source, row_buf.at[0, at], load_sems.at[(6, 10)[i]])

    def side_arrived(i):
        plane_core(0, ((0, 2), (1, 3))[i])
        if i == 0:
            pltpu.make_async_copy(own, rows_all.at[p.me], local_sem).wait()
        side_load(i).start()

    at_slot = {}

    def store(k, i, src, dst):
        if (k, i) not in at_slot:
            at_slot[k, i] = pltpu.make_async_copy(src, dst, store_sems.at[i, k % 2])
        return at_slot[k, i]

    def stores(k):
        q = p.near(k)
        at = pl.ds(q * slots, slots)
        plane = pl.ds(q * blocks, blocks)
        return [
            (x, x_all.at[at]),
            (d_expert, d_expert_all.at[at]),
            (inner, inner_all.at[at]),
            (d_gate_up, d_gate_up_all.at[at]),
            (out_stage, out_part.at[plane]),
            (d_stage, d_part.at[plane]),
        ]

    def put(k, i):
        store(k, i, *stores(k)[i]).start()

    def free(k, i):
        if k > 0:
            store(k - 1, i, *stores(k - 1)[i]).wait()

    def pick_rows(k, g):
        lane = lax.broadcasted_iota(jnp.int32, (8, 128), 1)
        line = lax.broadcasted_iota(jnp.int32, (8, 128), 0)
        select = jnp.where((lane == line * experts + p.me) & (line < 3), 1.0, 0.0).astype(bf16)
        slot_id = lax.broadcasted_iota(jnp.int32, (capacity, tokens), 0).astype(f32) + 1.0
        rows, cots = row_buf.at[k % 2], cot_buf.at[k % 2]
        which = pl.ds(g * group, group)
        lines = mxu(select, rows[which, :, width:].reshape(group * tokens, 128), NT)
        for i in range(group):
            mine = lines[:, i * tokens : (i + 1) * tokens]
            chosen = jnp.where(mine[2:3] == slot_id, 1.0, 0.0)
            gate = jnp.sum(chosen * (mine[0:1] + mine[1:2]), axis=1, keepdims=True)
            at = pl.ds(pl.multiple_of((g * group + i) * capacity, capacity), capacity)
            gates[at, :] = jnp.broadcast_to(gate, (capacity, 128))
            lead = [jnp.zeros((capacity, tokens), bf16)] * i
            tail = [jnp.zeros((capacity, tokens), bf16)] * (group - 1 - i)
            pick[g, i * capacity : (i + 1) * capacity, :] = jnp.concatenate(
                lead + [chosen.astype(bf16)] + tail, axis=1
            )
            lead = [jnp.zeros((tokens, capacity), f32)] * i
            tail = [jnp.zeros((tokens, capacity), f32)] * (group - 1 - i)
            pick_t[g, i * tokens : (i + 1) * tokens, :] = jnp.concatenate(
                lead + [chosen.T] + tail, axis=1
            ).astype(bf16)
        at = slots_at(g)

        @pl.loop(0, width // WIDE)
        def _(n):
            cols = pl.ds(pl.multiple_of(n * WIDE, WIDE), WIDE)
            row_tile = rows[which, :, cols].reshape(group * tokens, WIDE)
            x[at, cols] = mxu(pick[g], row_tile).astype(bf16)
            cot_tile = cots[which, :, cols].reshape(group * tokens, WIDE)
            picked = mxu(pick[g], cot_tile)
            cot[at, cols] = picked.astype(bf16)
            scale = jnp.concatenate([gates[at, :]] * (WIDE // 128), axis=1)
            d_expert[at, cols] = (scale * picked).astype(bf16)

    def slots_at(g):
        if g is None:
            return pl.ds(0, slots)
        return pl.ds(pl.multiple_of(g * group * capacity, group * capacity), group * capacity)

    def up(g=None):
        ff = inner.shape[1]
        at = slots_at(g)

        @pl.loop(0, ff // TILE)
        def _(n):
            cols = pl.ds(pl.multiple_of(n * TILE, TILE), TILE)
            gate = mxu(x[at, :], w_in[:, cols])
            raised = mxu(x[at, :], w_in[:, pl.ds(pl.multiple_of(ff + n * TILE, TILE), TILE)])
            sig = jax.nn.sigmoid(gate)
            silu = gate * sig
            inner[at, cols] = (silu * raised).astype(bf16)
            by_d_up[at, cols] = silu
            by_d_gate[at, cols] = raised * sig * (1.0 + gate * (1.0 - sig))

    def d_up(g=None):
        ff = inner.shape[1]
        at = slots_at(g)

        @pl.loop(0, ff // TILE)
        def _(n):
            cols = pl.ds(pl.multiple_of(n * TILE, TILE), TILE)
            d_inner = mxu(d_expert[at, :], w_down[cols, :], NT)
            d_gate_up[at, cols] = (d_inner * by_d_gate[at, cols]).astype(bf16)
            d_gate_up[at, pl.ds(pl.multiple_of(ff + n * TILE, TILE), TILE)] = (
                d_inner * by_d_up[at, cols]
            ).astype(bf16)

    def spread(stage, sides_done=(0, 1)):
        @pl.loop(0, width // WIDE)
        def _(n):
            cols = pl.ds(pl.multiple_of(n * WIDE, WIDE), WIDE)
            for g in sides_done:
                result = mxu(pick_t[g], held[slots_at(g), cols]).astype(bf16)
                stage[pl.ds(g * group, group), :, cols] = result.reshape(group, tokens, WIDE)

    def down(g=None):
        at = slots_at(g)
        d_gates[at, :] = jnp.zeros_like(d_gates[at, :])

        @pl.loop(0, width // TALL)
        def _(n):
            cols = pl.ds(pl.multiple_of(n * TALL, TALL), TALL)
            result = mxu(inner[at, :], w_down[:, cols]).astype(bf16).astype(f32)
            product = result * cot[at, cols].astype(f32)
            total = product[:, :128]
            for j in range(1, TALL // 128):
                total = total + product[:, j * 128 : (j + 1) * 128]
            d_gates[at, :] += total
            scale = jnp.concatenate([gates[at, :]] * (TALL // 128), axis=1)
            held[at, cols] = (scale * result).astype(bf16)

    def d_down(g=None, sides_done=(0, 1)):
        for side in sides_done:
            at = slots_at(side)
            total = jnp.sum(d_gates[at, :], axis=1, keepdims=True)
            high = total.astype(bf16).astype(f32)
            lane = lax.broadcasted_iota(jnp.int32, (group * capacity, 128), 1)
            info = jnp.where(
                lane == p.me, high, jnp.where(lane == experts + p.me, total - high, 0.0)
            )
            result = mxu(pick_t[side], info.astype(bf16)).astype(bf16)
            d_stage[pl.ds(side * group, group), :, width:] = result.reshape(group, tokens, 128)
        at = slots_at(g)

        @pl.loop(0, width // TALL)
        def _(n):
            cols = pl.ds(pl.multiple_of(n * TALL, TALL), TALL)
            held[at, cols] = mxu(d_gate_up[at, :], w_in[cols, :], NT).astype(bf16)

    plane_out(0)
    weights(True)
    cot_load(0).start()
    plane_turn(0)
    side_arrived(0)
    plane_hop(1)
    plane_out(1)
    plane_hop(2)
    weights(False)
    cot_load(0).wait()
    cot_load(1).start()
    side_load(0).wait()
    side = sides[0]
    pick_rows(0, side)
    up(side)
    plane_end(0)
    d_up(side)
    down(side)
    plane_hop(3)
    side_arrived(1)
    spread(out_stage, (side,))
    d_down(side, (side,))
    plane_turn(1)
    plane_out(2)
    spread(d_stage, (side,))
    side_load(1).wait()
    side = sides[1]
    pick_rows(0, side)
    put(0, 0)
    put(0, 1)
    up(side)
    put(0, 2)
    plane_end(1)
    d_up(side)
    put(0, 3)
    down(side)
    spread(out_stage, (side,))
    put(0, 4)
    arrived(1)
    d_down(side, (side,))
    spread(d_stage, (side,))
    put(0, 5)
    after = {
        (1, 0): ((plane_turn, 2), (plane_out, 3)),
        (1, 3): ((plane_end, 2),),
        (1, 5): ((arrived, 2),),
        (2, 0): ((plane_turn, 3),),
        (2, 3): ((plane_end, 3),),
        (2, 5): ((arrived, 3),),
    }
    for k in range(1, 4):

        def service(i):
            for step, plane in after.get((k, i), ()):
                step(plane)

        row_load(k).wait()
        cot_load(k).wait()
        if k < 3:
            cot_load(k + 1).start()
        free(k, 0)
        free(k, 1)
        for g in range(2):
            pick_rows(k, g)
        put(k, 0)
        put(k, 1)
        service(0)
        free(k, 2)
        up()
        put(k, 2)
        service(1)
        free(k, 3)
        d_up()
        put(k, 3)
        service(2)
        free(k, 4)
        down()
        service(3)
        spread(out_stage)
        put(k, 4)
        service(4)
        free(k, 5)
        d_down()
        service(5)
        spread(d_stage)
        put(k, 5)
    for i in range(6):
        free(4, i)
    finish()


def experts_gathered(own, cot_all, w_in, w_down, capacity, collective_id):
    tokens, wide = own.shape
    experts, _, width = cot_all.shape
    ff = w_down.shape[0]
    slots = 8 * capacity
    dma = pltpu.SemaphoreType.DMA
    bf16, f32 = jnp.bfloat16, jnp.float32
    anywhere = pl.BlockSpec(memory_space=pl.ANY)

    def array(*shape):
        return jax.ShapeDtypeStruct(shape, bf16)

    return pl.pallas_call(
        experts_kernel,
        out_shape=[
            array(experts, tokens, wide),
            array(experts, tokens, width),
            array(experts, tokens, wide),
            array(experts * capacity, width),
            array(experts * capacity, width),
            array(experts * capacity, ff),
            array(experts * capacity, 2 * ff),
        ],
        in_specs=[anywhere] * 4,
        out_specs=[anywhere] * 7,
        scratch_shapes=[
            pltpu.VMEM(w_in.shape, bf16),
            pltpu.VMEM(w_down.shape, bf16),
            pltpu.VMEM((2, 8, tokens, wide), bf16),
            pltpu.VMEM((2, 8, tokens, width), bf16),
            pltpu.VMEM((2, 4 * capacity, 4 * tokens), bf16),
            pltpu.VMEM((2, 4 * tokens, 4 * capacity), bf16),
            pltpu.VMEM((slots, 128), f32),
            pltpu.VMEM((slots, 128), f32),
            pltpu.VMEM((slots, width), bf16),
            pltpu.VMEM((slots, width), bf16),
            pltpu.VMEM((slots, width), bf16),
            pltpu.VMEM((slots, ff), f32),
            pltpu.VMEM((slots, ff), f32),
            pltpu.VMEM((slots, ff), bf16),
            pltpu.VMEM((slots, 2 * ff), bf16),
            pltpu.VMEM((slots, width), bf16),
            pltpu.VMEM((8, tokens, width), bf16),
            pltpu.VMEM((8, tokens, wide), bf16),
            dma((4, G_KINDS)),
            dma((4, G_KINDS)),
            dma((4, 2)),
            dma,
            dma((11,)),
            dma((6, 2)),
        ],
        compiler_params=pltpu.CompilerParams(
            collective_id=collective_id, has_side_effects=True, vmem_limit_bytes=VMEM_LIMIT
        ),
        name="experts",
    )(own, cot_all, w_in, w_down)


TN = (((0,), (0,)), ((), ()))


def back_kernel(
    own, pair, columns_hbm, normed_hbm, queries_hbm, keys_hbm, values_hbm, attended_hbm,
    q_raw_hbm, k_raw_hbm, cosine_hbm, sine_hbm, tokens_hbm, d_hidden_hbm, routed_hbm, d_logits_hbm,
    q_gain, k_gain, attn_gain, gains,
    d_tokens, d_qkv, d_out_t, d_router, gains_out, mixture,
    queries, keys, values, attended, q_raw, k_raw, cosine, sine, tokens, d_hidden, routed, d_logits, input_sems,
    cols_out, d_attn, columns, normed, d_normed, d_heads, d_query, d_key, d_value, d_proj, q_sum, k_sum,
    held, x_in, y_in, z_in, g_send, g_in, x_two, z_two, c_core, c_y,
    gs, gr, gz, load_sems, local_sem, hs, ys, yr, xs, xr, zs, zr, ts, tr,
    normed_sems, free, xs2, xr2, zs2, zr2, cs, cr, cys, cyr, as_, ar,
):
    p = Place()
    bf16, f32 = jnp.bfloat16, jnp.float32
    columns_z = [p.device((p.z + d) % 4, p.x, p.y, p.c) for d in (1, 2, 3)]
    greet_seq(p)
    rows, wide = own.shape
    length, head_cols = queries.shape
    heads = head_cols // HEAD_DIMENSION
    width = d_normed.shape[2]
    proj_cols = d_proj.shape[1]
    plane_rows = 2 * rows
    score_scale = 1.0 / math.sqrt(HEAD_DIMENSION)
    place = p.z * 2 + p.x

    def rows_at(q, x):
        return d_attn.at[q * 2 + x]

    def gather_out(k):
        q = p.near(k)
        there = rows_at(q, p.x)
        if k == 0:
            src = own
            for step, end in ((1, p.high), (-1, p.low)):

                @pl.when(jnp.logical_not(end))
                def _():
                    send(src, there, gz.at[q, 0 if step > 0 else 1], gr.at[q, 0], p.by_z(step))

            pltpu.make_async_copy(own, there, local_sem).start()
        else:
            src = there

            @pl.when(jnp.logical_not(p.inner))
            def _():
                await_bytes(src, gr.at[q, 0])

        send(src, there, gs.at[q], gr.at[q, 1], p.by_x)

    def gather_hop(k):
        q = p.near(k)
        there = rows_at(q, p.x)

        @pl.when(p.inner)
        def _():
            await_bytes(there, gr.at[q, 0])
            send(there, there, gz.at[q, 0], gr.at[q, 0], p.by_z(p.onward(k)))

    def gather_in(k):
        if k == 0:
            pltpu.make_async_copy(own, rows_at(p.z, p.x), local_sem).wait()
        await_bytes(own, gr.at[p.near(k), 1])

    def at_pair(q, x, y):
        return pair.at[q * 4 + x * 2 + y]

    def sum_send(k):
        q = p.far(k)
        for j, x in ((1, 1 - p.x), (0, p.x)):
            i = q * 2 + j
            send(at_pair(q, x, 1 - p.y), y_in.at[k % 2 * 2 + j], ys.at[i], yr.at[i], p.by_y)

    def sum_start():
        sum_send(0)
        sum_send(1)
        for k in range(4):
            q = p.far(k)
            for j, x in ((1, 1 - p.x), (0, p.x)):
                pltpu.make_async_copy(at_pair(q, x, p.y), held.at[q * 2 + j], hs.at[q * 2 + j]).start()

    def sum_turn(k):
        q = p.far(k)
        for j in (1, 0):
            slot = q * 2 + j
            landed = y_in.at[k % 2 * 2 + j]
            await_bytes(held.at[slot], hs.at[slot])
            await_bytes(landed, yr.at[slot])
            add_rows(held.at[slot], landed, rows)
            if j == 1:
                send(held.at[slot], x_in.at[q], xs.at[q], xr.at[q], p.by_x)
        if k < 2:
            pl.semaphore_signal(free, inc=1, device_id=p.by_y, device_id_type=MESH)
            pl.semaphore_wait(free, 1)
            sum_send(k + 2)

    def line_sum(k, mine, landed, sends, arrivals):
        q = p.far(k)
        if k < 3:
            step = p.toward(k)
            slot, hops = (1 - step) // 2, (q - p.z) * step

            @pl.when(p.inner)
            def _():
                await_bytes(landed.at[slot, hops], arrivals.at[slot, hops])
                add_rows(mine, landed.at[slot, hops], rows)

            send(mine, landed.at[slot, hops - 1], sends.at[k], arrivals.at[slot, hops - 1], p.by_z(step))
        else:
            for slot, there in ((0, p.low), (1, p.high)):

                @pl.when(jnp.logical_not(there))
                def _():
                    await_bytes(landed.at[slot, 0], arrivals.at[slot, 0])
                    add_rows(mine, landed.at[slot, 0], rows)

    def sum_end(k):
        q = p.far(k)
        mine = held.at[q * 2]
        await_bytes(x_in.at[q], xr.at[q])
        add_rows(mine, x_in.at[q], rows)
        line_sum(k, mine, z_in, zs, zr)
        if k == 3:
            mixture[...] = mine[...]

    def two_start(*steps):
        for k in steps:
            q = p.far(k)
            send(d_normed.at[q * 2 + 1 - p.x], x_two.at[q], xs2.at[q], xr2.at[q], p.by_x)

    def two_end(k):
        q = p.far(k)
        mine = d_normed.at[q * 2 + p.x]
        await_bytes(x_two.at[q], xr2.at[q])
        add_rows(mine, x_two.at[q], rows)
        line_sum(k, mine, z_two, zs2, zr2)

    piece_rows = c_y.shape[1]
    order = [(place + d) % 8 for d in range(1, 9)]
    piece_width = c_y.shape[2]
    cols_at = cols_out.at[place]

    def cols_start():
        for turn, side in ((0, 1 - p.y), (1, p.y)):
            send(columns.at[:, side, 1 - p.c], c_core.at[turn], cs.at[turn], cr.at[turn], p.by_core)

    def cols_core():
        for turn, side in ((0, 1 - p.y), (1, p.y)):
            await_bytes(c_core.at[turn], cr.at[turn])
            for s in order:
                add_rows(columns.at[s, side, p.c], c_core.at[turn, s], piece_rows)
                if turn == 0:
                    send(columns.at[s, side, p.c], c_y.at[s], cys.at[s], cyr.at[s], p.by_y)

    def cols_turn(*steps):
        for i in steps:
            s = order[i]
            mine = columns.at[s, p.y, p.c]
            await_bytes(c_y.at[s], cyr.at[s])
            add_rows(mine, c_y.at[s], piece_rows)
            if i < 7:
                send(mine, cols_at, as_.at[i], ar.at[i], seq_peer(p, i + 1))
            else:
                pltpu.make_async_copy(mine, cols_at, as_.at[7]).start()

    def norm_back():
        mine = d_normed.at[p.z * 2 + p.x]
        chunk = 16

        @pl.loop(0, rows // chunk)
        def _(i):
            at = pl.ds(pl.multiple_of(i * chunk, chunk), chunk)
            d_out = mine[at, :].astype(f32)
            x = tokens[at, :].astype(f32)
            scale = lax.rsqrt(jnp.mean(x * x, axis=-1, keepdims=True) + EPS)
            u = d_out * attn_gain[...]
            dot = jnp.mean(u * x, axis=-1, keepdims=True)
            d_x = scale * u - x * (scale * scale * scale * dot)
            d_tokens[at, :] = (d_hidden[at, :] + d_x).astype(d_tokens.dtype)

    def attention(q):
        row_start = pl.multiple_of(q * plane_rows, plane_rows)
        at = pl.ds(row_start, plane_rows)

        @pl.loop(0, head_cols // TILE)
        def _(n):
            cols = pl.ds(pl.multiple_of(n * TILE, TILE), TILE)
            grad = d_attn[pl.ds(q * 2, 2)].reshape(plane_rows, width)
            weight_cols = pl.ds(pl.multiple_of(proj_cols + n * TILE, TILE), TILE)
            weight = columns[..., weight_cols].reshape(width, TILE)
            d_heads[at, cols] = mxu(grad, weight).astype(bf16)

        def block(count):
            key, value = keys[:count], values[:count]
            row_pos = row_start + lax.broadcasted_iota(jnp.int32, (plane_rows, count), 0)
            allowed = lax.broadcasted_iota(jnp.int32, (plane_rows, count), 1) <= row_pos

            @pl.loop(0, heads)
            def _(h):
                cols = pl.ds(pl.multiple_of(h * HEAD_DIMENSION, HEAD_DIMENSION), HEAD_DIMENSION)
                query, d_out = queries[at, cols], d_heads[at, cols]
                scores = jnp.where(allowed, mxu(query, key, NT) * score_scale, -1e30)
                raised = jnp.exp(scores - jnp.max(scores, axis=-1, keepdims=True))
                prob = raised / jnp.sum(raised, axis=-1, keepdims=True)
                d_prob = mxu(d_out, value, NT)
                delta = jnp.sum(prob * d_prob, axis=-1, keepdims=True)
                d_scores = (prob * (d_prob - delta)).astype(bf16)
                d_query[at, cols] = mxu(d_scores, key) * score_scale
                d_key[:count] += mxu(d_scores, query, TN) * score_scale
                d_value[:count] += mxu(prob.astype(bf16), d_out, TN)

        half = length // 2

        @pl.when(q < 2)
        def _():
            block(half)

        @pl.when(q >= 2)
        def _():
            block(length)

    def unrotate(grad, at):
        swapped = jnp.concatenate(
            [grad[:, HEAD_DIMENSION // 2 :], grad[:, : HEAD_DIMENSION // 2]], axis=1
        )
        return grad * cosine[at, :] + swapped * sine[at, :]

    def raw_grads():
        q_sum[...] = jnp.zeros_like(q_sum)
        k_sum[...] = jnp.zeros_like(k_sum)

        def one(grad, raw, gain, total, at):
            turned = unrotate(grad, at)
            scale = lax.rsqrt(jnp.mean(raw * raw, axis=-1, keepdims=True) + EPS)
            total[...] += jnp.sum((turned * raw * scale).reshape(-1, 8, HEAD_DIMENSION), axis=0)
            u = turned * gain[...]
            dot = jnp.mean(u * raw, axis=-1, keepdims=True)
            return (scale * u - raw * (scale * scale * scale * dot)).astype(bf16)

        chunk = 128

        @pl.loop(0, length // chunk)
        def _(i):
            at = pl.ds(pl.multiple_of(i * chunk, chunk), chunk)
            for h in range(heads):
                cols = slice(h * HEAD_DIMENSION, (h + 1) * HEAD_DIMENSION)
                d_proj[at, cols] = one(d_query[at, cols], q_raw[at, cols], q_gain, q_sum, at)
            d_proj[at, head_cols : head_cols + HEAD_DIMENSION] = one(
                d_key[at, :], k_raw[at, :], k_gain, k_sum, at
            )
            d_proj[at, head_cols + HEAD_DIMENSION :] = d_value[at, :].astype(bf16)

        g_send[0] = gains[...]
        g_send[0, 2:3, :HEAD_DIMENSION] = jnp.sum(q_sum[...], axis=0, keepdims=True)
        g_send[0, 2:3, HEAD_DIMENSION : 2 * HEAD_DIMENSION] = jnp.sum(
            k_sum[...], axis=0, keepdims=True
        )

    def normed_load(n, slot):
        cols = pl.ds(pl.multiple_of(n * TILE, TILE), TILE)
        return pltpu.make_async_copy(normed_hbm.at[:, cols], normed.at[slot], normed_sems.at[slot])

    def normed_grads():
        @pl.loop(0, width // TILE)
        def _(n):
            cols = pl.ds(pl.multiple_of(n * TILE, TILE), TILE)
            slot = n % 2
            normed_load(n, slot).wait()

            @pl.when(n + 1 < width // TILE)
            def _():
                normed_load(n + 1, 1 - slot).start()

            weight = columns[n, :, :, :, :proj_cols].reshape(TILE, proj_cols)
            part = mxu(d_proj[...], weight, NT)
            d_normed[:, :, cols] = part.astype(bf16).reshape(length // rows, rows, TILE)
            total = jnp.sum(part * normed[slot].astype(f32), axis=0, keepdims=True)
            g_send[0, 0:1, cols] = total / attn_gain[:, cols]
            grad = mxu(normed[slot], d_proj[...], TN).astype(bf16)
            columns[n, :, :, :, :proj_cols] = grad.reshape(2, 2, -1, proj_cols)

    def gains_pass(t, target):
        send(g_send.at[t], g_in.at[t], ts.at[t], tr.at[t], target)

    def gains_take(t):
        await_bytes(g_in.at[t], tr.at[t])
        g_send[t + 1] = g_send[t] + g_in[t]

    def gains_z_pass():
        g_in[2 + p.z] = g_send[2]
        for d, target in enumerate(columns_z):
            send(g_send.at[2], g_in.at[2 + p.z], ts.at[2 + d], tr.at[2 + d], target)

    def gains_z_take():
        for d in range(3):
            await_bytes(g_in.at[0], tr.at[2 + d])
        g_send[3] = g_in[2] + g_in[3] + g_in[4] + g_in[5]

    def router_grads():
        @pl.loop(0, width // TILE)
        def _(n):
            cols = pl.ds(pl.multiple_of(n * TILE, TILE), TILE)
            grad = mxu(routed[:, cols], d_logits[...], TN).astype(bf16)
            columns[n, :, :, :, proj_cols + head_cols :] = grad.reshape(2, 2, -1, 128)

    def column_grads(value, first, count):
        @pl.loop(0, width // TILE)
        def _(n):
            cols = pl.ds(pl.multiple_of(n * TILE, TILE), TILE)
            part = d_attn[:, :, cols].reshape(length, TILE)
            grad = mxu(part, value[...], TN).astype(bf16)
            columns[n, :, :, :, first : first + count] = grad.reshape(2, 2, -1, count)

    loads = [
        pltpu.make_async_copy(columns_hbm, columns, load_sems.at[0]),
    ]
    gather_out(0)
    inputs = [
        pltpu.make_async_copy(source, target, input_sems.at[i])
        for i, (source, target) in enumerate(
            (
                (queries_hbm, queries),
                (keys_hbm, keys),
                (values_hbm, values),
                (attended_hbm, attended),
                (q_raw_hbm, q_raw),
                (k_raw_hbm, k_raw),
                (cosine_hbm, cosine),
                (sine_hbm, sine),
                (tokens_hbm, tokens),
                (d_hidden_hbm, d_hidden),
                (routed_hbm, routed),
                (d_logits_hbm, d_logits),
            )
        )
    ]
    loads[0].start()
    for copy in inputs:
        copy.start()
    normed_load(0, 0).start()
    sum_start()
    d_key[...] = jnp.zeros_like(d_key)
    d_value[...] = jnp.zeros_like(d_value)
    loads[0].wait()
    for copy in inputs:
        copy.wait()
    gather_in(0)
    gather_hop(1)
    gather_out(1)
    gather_hop(2)
    attention(p.near(0))
    gather_out(2)
    gather_hop(3)
    gather_in(1)
    attention(p.near(1))
    sum_turn(0)
    gather_out(3)
    gather_in(2)
    attention(p.near(2))
    sum_end(0)
    sum_turn(1)
    gather_in(3)
    attention(p.near(3))
    raw_grads()
    sum_end(1)
    normed_grads()
    gains_pass(0, p.by_core)
    column_grads(attended, proj_cols, head_cols)
    gains_take(0)
    gains_pass(1, p.by_x)
    two_start(0, 1)
    router_grads()
    cols_start()
    gains_take(1)
    gains_z_pass()
    sum_turn(2)
    two_start(2, 3)
    cols_core()
    two_end(0)
    sum_turn(3)
    gains_z_take()
    send(g_send.at[3], g_in.at[6], ts.at[5], tr.at[5], p.by_y)
    two_end(1)
    cols_turn(0, 1)
    sum_end(2)
    cols_turn(2, 3, 4, 5)
    two_end(2)
    cols_turn(6, 7)
    two_end(3)
    norm_back()
    sum_end(3)
    await_bytes(g_in.at[6], tr.at[5])
    gains_out[...] = g_send[3] + g_in[6]
    for t in range(6):
        await_bytes(g_in.at[0], ts.at[t])
    for q in range(4):
        await_bytes(own, gs.at[q])
    for there, slot in ((p.high, 0), (p.low, 1)):

        @pl.when(jnp.logical_not(there))
        def _():
            await_bytes(own, gz.at[p.z, slot])

    for k in range(1, 4):

        @pl.when(p.inner)
        def _():
            await_bytes(own, gz.at[p.near(k), 0])

    piece = x_in.at[0]
    for i in range(8):
        await_bytes(piece, ys.at[i])
    for q in range(4):
        await_bytes(piece, xs.at[q])
    for k in range(3):
        await_bytes(piece, zs.at[k])
        await_bytes(piece, zs2.at[k])
    for q in range(4):
        await_bytes(piece, xs2.at[q])
    for i in range(8):
        if i < 7:
            await_bytes(c_y.at[0], ar.at[i])
        await_bytes(c_y.at[0], as_.at[i])
        await_bytes(c_y.at[0], cys.at[i])
    for turn in range(2):
        await_bytes(c_core.at[turn], cs.at[turn])
    key_cols = KEY_VALUE_HEADS * HEAD_DIMENSION
    per_group = 8 // KEY_VALUE_HEADS
    router_total = jnp.zeros((piece_rows, 128), f32)
    for s in range(8):
        d_qkv[:, s * head_cols : (s + 1) * head_cols] = cols_out[s, :, :head_cols].astype(f32)
        d_out_t[:, s * head_cols : (s + 1) * head_cols] = cols_out[
            s, :, proj_cols : proj_cols + head_cols
        ].astype(f32)
        part = cols_out[s, :, proj_cols + head_cols :].astype(f32)
        router_total = router_total + part
    d_router[...] = router_total
    for g in range(KEY_VALUE_HEADS):
        for j in range(2):
            lanes = slice(head_cols + j * HEAD_DIMENSION, head_cols + (j + 1) * HEAD_DIMENSION)
            total = cols_out[g * per_group, :, lanes].astype(f32)
            for s in range(1, per_group):
                total = total + cols_out[g * per_group + s, :, lanes].astype(f32)
            first = 8 * head_cols + j * key_cols + g * HEAD_DIMENSION
            d_qkv[:, first : first + HEAD_DIMENSION] = total


def back(
    own, pair, columns, normed, queries, keys, values, attended,
    q_raw, k_raw, cosine, sine, q_gain, k_gain, attn_gain, gains, tokens, d_hidden,
    routed, d_logits, collective_id,
):
    inputs = (
        queries, keys, values, attended, q_raw, k_raw, cosine, sine, tokens, d_hidden, routed, d_logits,
    )
    rows, wide = own.shape
    length, head_cols = queries.shape
    width = normed.shape[1]
    piece_rows, piece_width = columns.shape[3:]
    proj_cols = head_cols + 2 * HEAD_DIMENSION
    dma = pltpu.SemaphoreType.DMA
    bf16, f32 = jnp.bfloat16, jnp.float32
    anywhere, vmem = pl.BlockSpec(memory_space=pl.ANY), pl.BlockSpec(memory_space=pltpu.VMEM)
    return pl.pallas_call(
        back_kernel,
        out_shape=[
            jax.ShapeDtypeStruct((rows, width), bf16),
            jax.ShapeDtypeStruct((piece_rows, 8 * head_cols + 2 * KEY_VALUE_HEADS * HEAD_DIMENSION), f32),
            jax.ShapeDtypeStruct((piece_rows, 8 * head_cols), f32),
            jax.ShapeDtypeStruct((piece_rows, 128), f32),
            jax.ShapeDtypeStruct(gains.shape, f32),
            jax.ShapeDtypeStruct((rows, width), bf16),
        ],
        in_specs=[anywhere] * 16 + [vmem] * 4,
        out_specs=[vmem] * 6,
        scratch_shapes=[
            *[pltpu.VMEM(array.shape, array.dtype) for array in inputs],
            dma((len(inputs),)),
            pltpu.VMEM((8, piece_rows, piece_width), bf16),
            pltpu.VMEM((8, rows, wide), bf16),
            pltpu.VMEM(columns.shape, bf16),
            pltpu.VMEM((2, length, TILE), bf16),
            pltpu.VMEM((length // rows, rows, width), bf16),
            pltpu.VMEM((length, head_cols), bf16),
            pltpu.VMEM((length, head_cols), f32),
            pltpu.VMEM((length, HEAD_DIMENSION), f32),
            pltpu.VMEM((length, HEAD_DIMENSION), f32),
            pltpu.VMEM((length, proj_cols), bf16),
            pltpu.VMEM((8, HEAD_DIMENSION), f32),
            pltpu.VMEM((8, HEAD_DIMENSION), f32),
            pltpu.VMEM((8, rows, width), bf16),
            pltpu.VMEM((4, rows, width), bf16),
            pltpu.VMEM((4, rows, width), bf16),
            pltpu.VMEM((2, 3, rows, width), bf16),
            pltpu.VMEM((4, *gains.shape), f32),
            pltpu.VMEM((7, *gains.shape), f32),
            pltpu.VMEM((4, rows, width), bf16),
            pltpu.VMEM((2, 3, rows, width), bf16),
            pltpu.VMEM((2, 8, piece_rows, piece_width), bf16),
            pltpu.VMEM((8, piece_rows, piece_width), bf16),
            dma((4,)),
            dma((4, 2)),
            dma((4, 2)),
            dma((2,)),
            dma,
            dma((8,)),
            dma((8,)),
            dma((8,)),
            dma((4,)),
            dma((4,)),
            dma((3,)),
            dma((2, 3)),
            dma((6,)),
            dma((6,)),
            dma((2,)),
            pltpu.SemaphoreType.REGULAR,
            dma((4,)),
            dma((4,)),
            dma((3,)),
            dma((2, 3)),
            dma((2,)),
            dma((2,)),
            dma((8,)),
            dma((8,)),
            dma((8,)),
            dma((7,)),
        ],
        compiler_params=pltpu.CompilerParams(
            collective_id=collective_id, has_side_effects=True, vmem_limit_bytes=VMEM_LIMIT
        ),
        name="back",
    )(
        own, pair, columns, normed, *inputs, q_gain, k_gain, attn_gain, gains,
    )


C_Z, C_X, C_Y, C_C, C_KINDS = 0, 1, 2, 4, 8


def front_kernel(
    tokens, pieces, cot, cosine_hbm, sine_hbm, q_gain, k_gain, attn_gain, ffn_gain, routes,
    normed_out, columns_out, cot_all, queries_out, keys_out, values_out, attended_out, q_raw_out, k_raw_out,
    hidden, gates, routed,
    queries, keys, values, attended, q_raw, k_raw, cosine, sine, result_sems, table_sems,
    own, normed, columns, part, x_in, z_in,
    ss, rs, zs, cs, cr, ys, yr, ks, kr, local_sems, gs, gr, gz, xs, xr, us, ur,
):
    p = Place()
    bf16 = jnp.bfloat16
    greet_seq(p)
    place, shard = p.z * 2 + p.x, p.y * 2 + p.c
    mine = place * 4 + shard
    rows, width = own.shape
    length, head_cols = queries.shape
    heads = head_cols // HEAD_DIMENSION
    proj_cols = head_cols + 2 * HEAD_DIMENSION
    plane_rows = 2 * rows
    score_scale = 1.0 / math.sqrt(HEAD_DIMENSION)

    x = tokens[...].astype(jnp.float32)
    scale = lax.rsqrt(jnp.mean(x * x, axis=-1, keepdims=True) + EPS)
    own[...] = (x * scale * attn_gain[...]).astype(bf16)

    def rows_at(q, x):
        return normed.at[q * 2 + x]

    def rows_move(k):
        q = p.near(k)
        there = rows_at(q, p.x)
        if k == 0:
            src = own
            for step, end in ((1, p.high), (-1, p.low)):

                @pl.when(jnp.logical_not(end))
                def _():
                    send(src, there, zs.at[q, 0 if step > 0 else 1], rs.at[q, 0], p.by_z(step))

            pltpu.make_async_copy(own, there, local_sems.at[0]).start()
        else:
            src = there

            @pl.when(jnp.logical_not(p.inner))
            def _():
                await_bytes(src, rs.at[q, 0])

        send(src, there, ss.at[q], rs.at[q, 1], p.by_x)

    def rows_hop(k):
        q = p.near(k)
        there = rows_at(q, p.x)

        @pl.when(p.inner)
        def _():
            await_bytes(there, rs.at[q, 0])
            send(there, there, zs.at[q, 0], rs.at[q, 0], p.by_z(p.onward(k)))

    def pass_on(d):
        block = ((place + 8 - d) % 8) * 4 + shard
        src = pieces.at[place] if d == 0 else columns.at[block]
        if d > 0:
            await_bytes(src, cr.at[d])
        send(src, columns.at[block], ys.at[d], yr.at[d], p.by_y)
        send(src, columns.at[block], ks.at[0, d], kr.at[0, d], p.by_core)

    def pass_across(d):
        block = columns.at[((place + 8 - d) % 8) * 4 + (1 - p.y) * 2 + p.c]
        await_bytes(block, yr.at[d])
        send(block, block, ks.at[1, d], kr.at[1, d], p.by_core)

    def cot_at(q, x, y):
        return cot_all.at[p.block(q, x, y, p.c)]

    def cot_core(q, j, src):
        x, y = (p.x, 1 - p.x)[j % 2], (p.y, 1 - p.y)[j // 2]
        send(src, cot_at(q, x, y), gs.at[q, C_C + j], gr.at[q, C_C + j], p.by_core)

    def cot_move(k):
        q = p.near(k)
        there = cot_at(q, p.x, p.y)
        if k == 0:
            src = cot
            for step, end in ((1, p.high), (-1, p.low)):

                @pl.when(jnp.logical_not(end))
                def _():
                    send(src, there, gz.at[q, 0 if step > 0 else 1], gr.at[q, C_Z], p.by_z(step))

            pltpu.make_async_copy(cot, there, local_sems.at[2]).start()
        else:
            src = there

            @pl.when(jnp.logical_not(p.inner))
            def _():
                await_bytes(src, gr.at[q, C_Z])

        send(src, there, gs.at[q, C_Y], gr.at[q, C_Y], p.by_y)
        send(src, there, gs.at[q, C_X], gr.at[q, C_X], p.by_x)
        cot_core(q, 0, src)

    def cot_hop(k):
        q = p.near(k)
        there = cot_at(q, p.x, p.y)

        @pl.when(p.inner)
        def _():
            await_bytes(there, gr.at[q, C_Z])
            send(there, there, gz.at[q, 0], gr.at[q, C_Z], p.by_z(p.onward(k)))

    def cot_turn(k):
        q = p.near(k)
        there = cot_at(q, 1 - p.x, p.y)
        await_bytes(there, gr.at[q, C_X])
        send(there, there, gs.at[q, C_Y + 1], gr.at[q, C_Y + 1], p.by_y)
        cot_core(q, 1, there)

    def cot_end(k):
        q = p.near(k)
        for j, x in ((0, p.x), (1, 1 - p.x)):
            there = cot_at(q, x, 1 - p.y)
            await_bytes(there, gr.at[q, C_Y + j])
            cot_core(q, 2 + j, there)

    def sum_end(k):
        q = p.far(k)
        held = part.at[q * 2 + p.x]
        await_bytes(x_in.at[q], xr.at[q])
        add_rows(held, x_in.at[q], rows)
        if k < 3:
            step = p.toward(k)
            slot = (1 - step) // 2

            @pl.when(p.inner)
            def _():
                await_bytes(z_in.at[slot, q], ur.at[slot, q])
                add_rows(held, z_in.at[slot, q], rows)

            send(held, z_in.at[slot, q], us.at[k], ur.at[slot, q], p.by_z(step))
        else:
            for slot, there in ((0, p.low), (1, p.high)):

                @pl.when(jnp.logical_not(there))
                def _():
                    await_bytes(z_in.at[slot, q], ur.at[slot, q])
                    add_rows(held, z_in.at[slot, q], rows)

    def route():
        total = tokens[...].astype(jnp.float32) + part[p.z * 2 + p.x].astype(jnp.float32)
        hidden[...] = total
        scale = lax.rsqrt(jnp.mean(total * total, axis=-1, keepdims=True) + EPS)
        routed[:, :width] = (total * scale * ffn_gain[...]).astype(bf16)
        router = columns[:, :, proj_cols + head_cols :].reshape(width, 128)
        logits = mxu(routed[:, :width], router)
        lane = lax.broadcasted_iota(jnp.int32, (rows, 128), 1)
        line = lax.broadcasted_iota(jnp.int32, (rows, 128), 0)
        turned = routes[...].astype(jnp.float32).T
        lanes = lane.astype(jnp.float32)
        named = lanes == turned[:, 0:1]
        for k in range(1, TOPK):
            named = named | (lanes == turned[:, k : k + 1])
        chosen = jnp.where(named, logits, -1e30)
        raised = jnp.where(named, jnp.exp(chosen - jnp.max(chosen, axis=-1, keepdims=True)), 0.0)
        gate = raised / jnp.sum(raised, axis=-1, keepdims=True)
        gates[...] = gate
        counted = jnp.where(named, 1.0, 0.0)
        slot = counted * mxu(jnp.where(lane <= line, 1.0, 0.0).astype(bf16), counted.astype(bf16))
        high = gate.astype(bf16).astype(jnp.float32)
        experts = columns.shape[0]
        info = high + pltpu.roll(gate - high, experts, 1) + pltpu.roll(slot, 2 * experts, 1)
        routed[:, width:] = info.astype(bf16)

    def project(n):
        cols = slice(n * TILE, (n + 1) * TILE)
        weight = columns[:, :, cols].reshape(width, TILE)
        result = mxu(normed[...].reshape(length, width), weight)
        if n * TILE < head_cols:
            q_raw[:, cols] = result
        else:
            k_raw[...] = result[:, :HEAD_DIMENSION]
            values[...] = result[:, HEAD_DIMENSION:].astype(bf16)

    def prepare():
        def one(raw, gain, at):
            scaled = raw * lax.rsqrt(jnp.mean(raw * raw, axis=-1, keepdims=True) + EPS) * gain[...]
            swapped = jnp.concatenate(
                [scaled[:, HEAD_DIMENSION // 2 :], scaled[:, : HEAD_DIMENSION // 2]], axis=1
            )
            return (scaled * cosine[at, :] - swapped * sine[at, :]).astype(bf16)

        chunk = 128

        @pl.loop(0, length // chunk)
        def _(i):
            at = pl.ds(pl.multiple_of(i * chunk, chunk), chunk)
            for h in range(heads):
                cols = slice(h * HEAD_DIMENSION, (h + 1) * HEAD_DIMENSION)
                queries[at, cols] = one(q_raw[at, cols], q_gain, at)
            keys[at, :] = one(k_raw[at, :], k_gain, at)

    def attention(k):
        q = p.far(k)
        row_start = pl.multiple_of(q * plane_rows, plane_rows)
        at = pl.ds(row_start, plane_rows)

        def block(count):
            row_pos = row_start + lax.broadcasted_iota(jnp.int32, (plane_rows, count), 0)
            allowed = lax.broadcasted_iota(jnp.int32, (plane_rows, count), 1) <= row_pos

            @pl.loop(0, heads)
            def _(h):
                cols = pl.ds(pl.multiple_of(h * HEAD_DIMENSION, HEAD_DIMENSION), HEAD_DIMENSION)
                scores = mxu(queries[at, cols], keys[:count], NT) * score_scale
                scores = jnp.where(allowed, scores, -1e30)
                raised = jnp.exp(scores - jnp.max(scores, axis=-1, keepdims=True))
                prob = raised / jnp.sum(raised, axis=-1, keepdims=True)
                attended[at, cols] = mxu(prob.astype(bf16), values[:count]).astype(bf16)

        @pl.when(q < 2)
        def _():
            block(length // 2)

        @pl.when(q >= 2)
        def _():
            block(length)

        per_tile = TILE // columns.shape[1]

        @pl.loop(0, width // TILE)
        def _(n):
            cols = pl.ds(pl.multiple_of(n * TILE, TILE), TILE)
            weight = columns[pl.ds(n * per_tile, per_tile), :, proj_cols : proj_cols + head_cols]
            result = mxu(attended[at, :], weight.reshape(TILE, head_cols), NT).astype(bf16)
            part[pl.ds(q * 2, 2), :, cols] = result.reshape(2, rows, TILE)

        send(part.at[q * 2 + 1 - p.x], x_in.at[q], xs.at[q], xr.at[q], p.by_x)

    tables = [
        pltpu.make_async_copy(cosine_hbm, cosine, table_sems.at[0]),
        pltpu.make_async_copy(sine_hbm, sine, table_sems.at[1]),
    ]
    results = [
        pltpu.make_async_copy(source, target, result_sems.at[i])
        for i, (source, target) in enumerate(
            (
                (queries, queries_out),
                (keys, keys_out),
                (values, values_out),
                (q_raw, q_raw_out),
                (k_raw, k_raw_out),
                (attended, attended_out),
            )
        )
    ]
    rows_move(0)
    for copy in tables:
        copy.start()
    for d in range(1, 8):
        send(pieces.at[(place + d) % 8], columns.at[mine], cs.at[d], cr.at[d], seq_peer(p, d))
    pltpu.make_async_copy(pieces.at[place], columns.at[mine], local_sems.at[1]).start()
    pass_on(0)
    rows_hop(1)
    rows_move(1)
    for d in (1, 2, 7):
        pass_on(d)
    rows_hop(2)
    rows_move(2)
    cot_move(0)
    for d in (6, 3, 5):
        pass_on(d)
    rows_hop(3)
    rows_move(3)
    pass_on(4)
    for d in (0, 1, 2, 7, 6, 3, 5, 4):
        pass_across(d)
    cot_hop(1)
    cot_move(1)
    for k in range(4):
        await_bytes(own, rs.at[p.near(k), 1])
    pltpu.make_async_copy(own, rows_at(p.z, p.x), local_sems.at[0]).wait()
    pltpu.make_async_copy(pieces.at[place], columns.at[mine], local_sems.at[1]).wait()
    piece = pieces.at[0]
    for d in range(8):
        await_bytes(piece, kr.at[0, d])
        await_bytes(piece, kr.at[1, d])
    pltpu.make_async_copy(normed, normed_out, local_sems.at[0]).start()
    pltpu.make_async_copy(columns, columns_out, local_sems.at[1]).start()
    cot_turn(0)
    for n in range(proj_cols // TILE):
        project(n)
    cot_hop(2)
    cot_move(2)
    for copy in tables:
        copy.wait()
    prepare()
    for copy in results[:5]:
        copy.start()
    cot_turn(1)
    attention(0)
    cot_end(0)
    attention(1)
    cot_hop(3)
    cot_move(3)
    sum_end(0)
    attention(2)
    cot_turn(2)
    cot_end(1)
    sum_end(1)
    attention(3)
    results[5].start()
    cot_turn(3)
    sum_end(2)
    cot_end(2)
    sum_end(3)
    cot_end(3)
    route()
    for copy in results:
        copy.wait()
    for q in range(4):
        for j in range(4):
            await_bytes(cot, gr.at[q, C_C + j])
            await_bytes(cot, gs.at[q, C_C + j])
        for kind in (C_X, C_Y, C_Y + 1):
            await_bytes(cot, gs.at[q, kind])
        await_bytes(own, ss.at[q])
        await_bytes(own, xs.at[q])
    for there, slot in ((p.high, 0), (p.low, 1)):

        @pl.when(jnp.logical_not(there))
        def _():
            await_bytes(own, zs.at[p.z, slot])
            await_bytes(cot, gz.at[p.z, slot])

    for k in range(1, 4):

        @pl.when(p.inner)
        def _():
            await_bytes(own, zs.at[p.near(k), 0])
            await_bytes(cot, gz.at[p.near(k), 0])

    for k in range(3):
        await_bytes(own, us.at[k])
    for d in range(8):
        if d > 0:
            await_bytes(piece, cs.at[d])
        await_bytes(piece, ys.at[d])
        await_bytes(piece, ks.at[0, d])
        await_bytes(piece, ks.at[1, d])
    pltpu.make_async_copy(cot, cot_at(p.z, p.x, p.y), local_sems.at[2]).wait()
    pltpu.make_async_copy(normed, normed_out, local_sems.at[0]).wait()
    pltpu.make_async_copy(columns, columns_out, local_sems.at[1]).wait()


def front(
    tokens, pieces, cot, cosine, sine, q_gain, k_gain, attn_gain, ffn_gain, routes, head_cols, collective_id
):
    dma = pltpu.SemaphoreType.DMA
    bf16, f32 = jnp.bfloat16, jnp.float32
    rows, width = tokens.shape
    count, piece_rows, piece_width = pieces.shape
    length = count * rows
    anywhere, vmem = pl.BlockSpec(memory_space=pl.ANY), pl.BlockSpec(memory_space=pltpu.VMEM)
    return pl.pallas_call(
        front_kernel,
        out_shape=[
            jax.ShapeDtypeStruct((count, rows, width), bf16),
            jax.ShapeDtypeStruct((count * 4, piece_rows, piece_width), bf16),
            jax.ShapeDtypeStruct((count * 4, rows, width), bf16),
            jax.ShapeDtypeStruct((length, head_cols), bf16),
            jax.ShapeDtypeStruct((length, HEAD_DIMENSION), bf16),
            jax.ShapeDtypeStruct((length, HEAD_DIMENSION), bf16),
            jax.ShapeDtypeStruct((length, head_cols), bf16),
            jax.ShapeDtypeStruct((length, head_cols), f32),
            jax.ShapeDtypeStruct((length, HEAD_DIMENSION), f32),
            jax.ShapeDtypeStruct((rows, width), f32),
            jax.ShapeDtypeStruct((rows, 128), f32),
            jax.ShapeDtypeStruct((rows, width + 128), bf16),
        ],
        in_specs=[vmem] + [anywhere] * 4 + [vmem] * 5,
        out_specs=[anywhere] * 9 + [vmem] * 3,
        scratch_shapes=[
            pltpu.VMEM((length, head_cols), bf16),
            pltpu.VMEM((length, HEAD_DIMENSION), bf16),
            pltpu.VMEM((length, HEAD_DIMENSION), bf16),
            pltpu.VMEM((length, head_cols), bf16),
            pltpu.VMEM((length, head_cols), f32),
            pltpu.VMEM((length, HEAD_DIMENSION), f32),
            pltpu.VMEM(cosine.shape, f32),
            pltpu.VMEM(sine.shape, f32),
            dma((6,)),
            dma((2,)),
            pltpu.VMEM((rows, width), bf16),
            pltpu.VMEM((count, rows, width), bf16),
            pltpu.VMEM((count * 4, piece_rows, piece_width), bf16),
            pltpu.VMEM((count, rows, width), bf16),
            pltpu.VMEM((4, rows, width), bf16),
            pltpu.VMEM((2, 4, rows, width), bf16),
            dma((4,)),
            dma((4, 2)),
            dma((4, 2)),
            dma((8,)),
            dma((8,)),
            dma((8,)),
            dma((8,)),
            dma((2, 8)),
            dma((2, 8)),
            dma((3,)),
            dma((4, C_KINDS)),
            dma((4, C_KINDS)),
            dma((4, 2)),
            dma((4,)),
            dma((4,)),
            dma((3,)),
            dma((2, 4)),
        ],
        compiler_params=pltpu.CompilerParams(
            collective_id=collective_id, has_side_effects=True, vmem_limit_bytes=VMEM_LIMIT
        ),
        name="front",
    )(tokens, pieces, cot, cosine, sine, q_gain, k_gain, attn_gain, ffn_gain, routes)


def head_columns(weight, group_index):
    rows = weight.shape[0]
    query_width = QUERY_HEADS * HEAD_DIMENSION
    key_width = KEY_VALUE_HEADS * HEAD_DIMENSION
    query = weight[:, :query_width].reshape(rows, len(group_index), -1).transpose(1, 0, 2)
    keys = weight[:, query_width : query_width + key_width].reshape(rows, KEY_VALUE_HEADS, -1)
    values = weight[:, query_width + key_width :].reshape(rows, KEY_VALUE_HEADS, -1)
    keys = jnp.stack([keys[:, group] for group in group_index])
    values = jnp.stack([values[:, group] for group in group_index])
    return jnp.concatenate([query, keys, values], axis=2)


def gathered_body(
    tokens,
    query_key_value_weight,
    w_out_t,
    w_router,
    w_in,
    w_down,
    attn_gain,
    ffn_gain,
    q_gain,
    k_gain,
    routes,
    cotangent,
):
    bf16, f32 = jnp.bfloat16, jnp.float32
    both = ("seq", "fsdp")
    seq_size = lax.axis_size("seq")
    shard_size = lax.axis_size("fsdp")
    experts = seq_size * shard_size
    rows = tokens.shape[1]
    width = tokens.shape[2]
    length = rows * seq_size
    weight_rows = query_key_value_weight.shape[0]
    heads = QUERY_HEADS // seq_size
    head_cols = heads * HEAD_DIMENSION
    kv_cols = HEAD_DIMENSION
    proj_cols = head_cols + 2 * kv_cols
    all_cols = proj_cols + head_cols
    spare_cols = 128
    group_index = [s * heads * KEY_VALUE_HEADS // QUERY_HEADS for s in range(seq_size)]
    capacity = 2 * rows * TOPK // experts

    pieces = jnp.concatenate(
        [
            head_columns(query_key_value_weight, group_index),
            w_out_t.reshape(weight_rows, seq_size, head_cols).transpose(1, 0, 2),
            jnp.broadcast_to(
                jnp.pad(w_router, ((0, 0), (0, spare_cols - experts))),
                (seq_size, weight_rows, spare_cols),
            ),
        ],
        axis=2,
    )
    half_dim = HEAD_DIMENSION // 2
    exponents = -2.0 * np.arange(half_dim, dtype=np.float32) / HEAD_DIMENSION
    frequency = np.float32(ROPE_BASE) ** exponents.astype(np.float32)
    angles = np.arange(length, dtype=np.float32)[:, None] * frequency[None, :]
    cosine, sine = np.cos(angles), np.sin(angles)
    cosine = jnp.asarray(np.concatenate([cosine, cosine], axis=1), f32)
    sine = jnp.asarray(np.concatenate([sine, -sine], axis=1), f32)
    (
        normed_all,
        columns,
        cot_all,
        queries,
        keys,
        values,
        attended,
        q_raw,
        k_raw,
        hidden,
        gates,
        routed,
    ) = front(
        tokens[0],
        pieces,
        cotangent[0],
        cosine,
        sine,
        q_gain[None],
        k_gain[None],
        attn_gain[None],
        ffn_gain[None],
        routes[0].T,
        head_cols,
        1,
    )
    normed_all = normed_all.reshape(length, width)

    gate_weight = w_in[0]
    down_weight = w_down[0]
    unused_rows, out_part, d_part, rows_in, d_expert, inner_act, d_gate_up = experts_gathered(
        routed,
        cot_all,
        gate_weight,
        down_weight,
        capacity,
        3,
    )
    d_attn, d_logits, d_hidden, gains, out_pair, d_w_in, d_w_down = sum_all(
        d_part,
        out_part,
        rows_in,
        d_gate_up,
        inner_act,
        d_expert,
        columns,
        hidden,
        cotangent[0],
        gates,
        ffn_gain[None],
        5,
    )
    d_w_in, d_w_down = d_w_in.astype(f32)[None], d_w_down.astype(f32)[None]

    d_tokens, d_w_qkv, d_w_out_t, d_w_router, gains, mixture = back(
        d_attn,
        out_pair.reshape(2 * seq_size, rows, width),
        columns.reshape(seq_size, 2, shard_size // 2, weight_rows, all_cols + spare_cols),
        normed_all,
        queries,
        keys,
        values,
        attended,
        q_raw,
        k_raw,
        cosine,
        sine,
        q_gain[None],
        k_gain[None],
        attn_gain[None],
        gains,
        tokens[0],
        d_hidden,
        routed,
        d_logits,
        6,
    )
    output = (hidden + mixture.astype(f32)).astype(bf16)
    d_tokens = d_tokens[None]
    d_w_router = d_w_router[:, :experts]
    d_attn_gain, d_ffn_gain = gains[0], gains[1]
    d_q_gain = gains[2, :HEAD_DIMENSION]
    d_k_gain = gains[2, HEAD_DIMENSION : 2 * HEAD_DIMENSION]
    return (
        output[None],
        d_tokens,
        d_w_qkv,
        d_w_out_t,
        d_w_router,
        d_w_in,
        d_w_down,
        d_attn_gain,
        d_ffn_gain,
        d_q_gain,
        d_k_gain,
    )


def gathered_fits(mesh):
    return mesh.shape["seq"] == 8 and mesh.shape["fsdp"] == 4


def solution(mesh):
    return jax.shard_map(
        gathered_body if gathered_fits(mesh) else routed_body,
        mesh=mesh,
        in_specs=(
            P("fsdp", "seq", None),
            P(("seq", "fsdp"), None),
            P(("seq", "fsdp"), None),
            P(("seq", "fsdp"), None),
            P(("seq", "fsdp"), None, None),
            P(("seq", "fsdp"), None, None),
            P(),
            P(),
            P(),
            P(),
            P("fsdp", "seq", None),
            P("fsdp", "seq", None),
        ),
        out_specs=(
            P("fsdp", "seq", None),
            P("fsdp", "seq", None),
            P(("seq", "fsdp"), None),
            P(("seq", "fsdp"), None),
            P(("seq", "fsdp"), None),
            P(("seq", "fsdp"), None, None),
            P(("seq", "fsdp"), None, None),
            P(),
            P(),
            P(),
            P(),
        ),
        check_vma=False,
    )
```

```python
from functools import partial
import math

import jax
import jax.numpy as jnp
import numpy as np
from jax import lax
from jax.experimental import pallas as pl
from jax.experimental.pallas import tpu as pltpu
from jax.sharding import PartitionSpec as P

QUERY_HEADS = 32
KEY_VALUE_HEADS = 4
HEAD_DIMENSION = 128
FF = 768
TOPK = 8


EPS = 1e-06
ROPE_BASE = 1000000.0


def rms_scale(values, gain):
    return values * lax.rsqrt(jnp.mean(values * values, axis=-1, keepdims=True) + EPS) * gain


def rotate(values, positions):
    half_dim = values.shape[-1] // 2
    frequency = ROPE_BASE ** (-2.0 * jnp.arange(half_dim, dtype=jnp.float32) / values.shape[-1])
    angles = positions.astype(jnp.float32)[:, None] * frequency[None, :]
    cosine = jnp.cos(angles)[:, None, :]
    sine_part = jnp.sin(angles)[:, None, :]
    first_half = values[..., :half_dim]
    second = values[..., half_dim:]
    return jnp.concatenate(
        [first_half * cosine - second * sine_part, second * cosine + first_half * sine_part],
        axis=-1,
    )


def head_prepare(raw_heads, gain, positions):
    return rotate(rms_scale(raw_heads, gain), positions)


def route_slots(route_flat, experts):
    onehot = (route_flat[:, None] == jnp.arange(experts, dtype=jnp.int32)[None, :]).astype(
        jnp.int32
    )
    earlier = jnp.cumsum(onehot, axis=0) - onehot
    return (onehot, jnp.sum(earlier * onehot, axis=1))


def pack_slots(row_values, expert_ids, slot_index, slot_shape):
    buffer = jnp.zeros(slot_shape, row_values.dtype)
    return buffer.at[expert_ids // slot_shape[1], expert_ids % slot_shape[1], slot_index].set(
        row_values
    )


def unpack_slots(buffer, expert_ids, slot_index):
    return buffer[expert_ids // buffer.shape[1], expert_ids % buffer.shape[1], slot_index]


def causal_scores(query_part, key_full, row_start):
    block_rows = query_part.shape[0]
    score_scale = 1.0 / math.sqrt(query_part.shape[2])
    scores = (
        jnp.einsum("qhd,khd->hqk", query_part, key_full, preferred_element_type=jnp.float32)
        * score_scale
    )
    key_pos = jnp.arange(key_full.shape[0], dtype=jnp.int32)
    row_pos = row_start + jnp.arange(block_rows, dtype=jnp.int32)
    allowed = key_pos[None, :] <= row_pos[:, None]
    return jnp.where(allowed[None], scores, -1e30)


def attend_forward(query_rows_all, key_full, value_full):
    sequence_length = query_rows_all.shape[0]
    block_rows = min(512, sequence_length)

    def one_block(block_index):
        row_start = block_index * block_rows
        query_part = lax.dynamic_slice_in_dim(query_rows_all, row_start, block_rows, 0)
        scores = causal_scores(query_part, key_full, row_start)
        row_max = jnp.max(scores, axis=-1, keepdims=True)
        weights = jnp.exp(scores - row_max)
        row_total = jnp.sum(weights, axis=-1, keepdims=True)
        prob_low = (weights / row_total).astype(jnp.bfloat16)
        mixed_out = jnp.einsum(
            "hqk,khd->qhd", prob_low, value_full, preferred_element_type=jnp.float32
        )
        return (mixed_out.astype(jnp.bfloat16), (row_max + jnp.log(row_total))[..., 0])

    mixed_out, log_total = lax.map(
        one_block, jnp.arange(sequence_length // block_rows, dtype=jnp.int32)
    )
    return (mixed_out.reshape(query_rows_all.shape), log_total)


def attend_backward(query_rows_all, key_full, value_full, log_total, d_mixed):
    sequence_length = query_rows_all.shape[0]
    block_rows = min(512, sequence_length)
    score_scale = 1.0 / math.sqrt(query_rows_all.shape[2])

    def one_block(running, block_index):
        d_key_sum, d_value_sum = running
        row_start = block_index * block_rows
        query_part = lax.dynamic_slice_in_dim(query_rows_all, row_start, block_rows, 0)
        d_part = lax.dynamic_slice_in_dim(d_mixed, row_start, block_rows, 0)
        scores = causal_scores(query_part, key_full, row_start)
        prob_full = jnp.exp(scores - log_total[block_index][..., None])
        prob_low = prob_full.astype(jnp.bfloat16)
        d_probs = jnp.einsum("qhd,khd->hqk", d_part, value_full, preferred_element_type=jnp.float32)
        row_delta = jnp.sum(prob_full * d_probs, axis=-1, keepdims=True)
        d_scores = (prob_full * (d_probs - row_delta)).astype(jnp.bfloat16)
        d_query_part = (
            jnp.einsum("hqk,khd->qhd", d_scores, key_full, preferred_element_type=jnp.float32)
            * score_scale
        )
        d_key_sum = (
            d_key_sum
            + jnp.einsum("hqk,qhd->khd", d_scores, query_part, preferred_element_type=jnp.float32)
            * score_scale
        )
        d_value_sum = d_value_sum + jnp.einsum(
            "hqk,qhd->khd", prob_low, d_part, preferred_element_type=jnp.float32
        )
        return ((d_key_sum, d_value_sum), d_query_part)

    zero_grad = jnp.zeros(key_full.shape, jnp.float32)
    (d_key_sum, d_value_sum), d_query = lax.scan(
        one_block,
        (zero_grad, zero_grad),
        jnp.arange(sequence_length // block_rows, dtype=jnp.int32),
    )
    return (d_query.reshape(query_rows_all.shape), d_key_sum, d_value_sum)


def routed_body(
    tokens,
    query_key_value_weight,
    w_out_t,
    w_router,
    w_in,
    w_down,
    attn_gain,
    ffn_gain,
    q_gain,
    k_gain,
    routes,
    cotangent,
):
    sequence_count = lax.axis_size("seq")
    shard_count = lax.axis_size("fsdp")
    experts = sequence_count * shard_count
    token_row_count = tokens.shape[1]
    model_width = tokens.shape[2]
    query_group_width = QUERY_HEADS // KEY_VALUE_HEADS
    capacity = 2 * token_row_count * TOPK // experts
    slot_shape = (sequence_count, shard_count, capacity, model_width)
    positions = lax.axis_index("seq") * token_row_count + jnp.arange(
        token_row_count, dtype=jnp.int32
    )
    full_qkv, full_out, full_router = (
        lax.all_gather(query_key_value_weight, ("seq", "fsdp"), axis=0, tiled=True),
        lax.all_gather(w_out_t, ("seq", "fsdp"), axis=0, tiled=True),
        lax.all_gather(w_router, ("seq", "fsdp"), axis=0, tiled=True),
    )
    resid_in = tokens[0].astype(jnp.float32)
    normed_one = rms_scale(resid_in, attn_gain).astype(jnp.bfloat16)
    projection_output = jnp.dot(normed_one, full_qkv, preferred_element_type=jnp.float32)
    q_raw = projection_output[:, : QUERY_HEADS * HEAD_DIMENSION].reshape(
        token_row_count, QUERY_HEADS, HEAD_DIMENSION
    )
    key_unnormed = projection_output[
        :, QUERY_HEADS * HEAD_DIMENSION : (QUERY_HEADS + KEY_VALUE_HEADS) * HEAD_DIMENSION
    ].reshape(token_row_count, KEY_VALUE_HEADS, HEAD_DIMENSION)
    value_per_head = (
        projection_output[:, (QUERY_HEADS + KEY_VALUE_HEADS) * HEAD_DIMENSION :]
        .reshape(token_row_count, KEY_VALUE_HEADS, HEAD_DIMENSION)
        .astype(jnp.bfloat16)
    )
    prepare = partial(head_prepare, positions=positions)
    query_rows_all = prepare(q_raw, q_gain).astype(jnp.bfloat16)
    key_per_head = prepare(key_unnormed, k_gain).astype(jnp.bfloat16)
    send_keys = jnp.repeat(key_per_head, query_group_width, axis=1)
    send_values = jnp.repeat(value_per_head, query_group_width, axis=1)
    head_queries, head_keys, head_values = (
        lax.all_to_all(query_rows_all, "seq", split_axis=1, concat_axis=0, tiled=True),
        lax.all_to_all(send_keys, "seq", split_axis=1, concat_axis=0, tiled=True),
        lax.all_to_all(send_values, "seq", split_axis=1, concat_axis=0, tiled=True),
    )
    mixed_heads, log_total = attend_forward(head_queries, head_keys, head_values)
    mixed_tok = lax.all_to_all(mixed_heads, "seq", split_axis=0, concat_axis=1, tiled=True)
    attention_result = mixed_tok.reshape(token_row_count, QUERY_HEADS * HEAD_DIMENSION)
    attn_out = jnp.einsum(
        "tj,dj->td", attention_result, full_out, preferred_element_type=jnp.float32
    )
    hidden = resid_in + attn_out
    normed_two = rms_scale(hidden, ffn_gain).astype(jnp.bfloat16)
    logits = jnp.dot(normed_two, full_router, preferred_element_type=jnp.float32)
    route_flat = routes[0].reshape(-1)
    onehot, slot_index = route_slots(route_flat, experts)
    onehot_float = onehot.reshape(token_row_count, TOPK, experts).astype(jnp.float32)
    chosen = jnp.sum(onehot_float * logits[:, None, :], axis=-1)
    row_max = jnp.max(chosen, axis=-1, keepdims=True)
    exp_part = jnp.exp(chosen - row_max)
    gate_probs = exp_part / jnp.sum(exp_part, axis=-1, keepdims=True)
    send_rows = pack_slots(jnp.repeat(normed_two, TOPK, axis=0), route_flat, slot_index, slot_shape)
    arrived = lax.all_to_all(
        lax.all_to_all(send_rows, "seq", split_axis=0, concat_axis=0, tiled=True),
        "fsdp",
        split_axis=1,
        concat_axis=1,
        tiled=True,
    )
    rows_in = arrived.reshape(-1, model_width)
    gate_weight = w_in[0]
    down_weight = w_down[0]
    gate_up = jnp.dot(rows_in, gate_weight, preferred_element_type=jnp.float32)
    gate_half = gate_up[:, :FF]
    up_half = gate_up[:, FF:]
    gate_sig = jax.nn.sigmoid(gate_half)
    silu_gate = gate_half * gate_sig
    inner_act = (silu_gate * up_half).astype(jnp.bfloat16)
    expert_out = jnp.dot(inner_act, down_weight, preferred_element_type=jnp.float32).astype(
        jnp.bfloat16
    )
    returned = lax.all_to_all(
        lax.all_to_all(
            expert_out.reshape(slot_shape), "seq", split_axis=0, concat_axis=0, tiled=True
        ),
        "fsdp",
        split_axis=1,
        concat_axis=1,
        tiled=True,
    )
    picked = (
        unpack_slots(returned, route_flat, slot_index)
        .astype(jnp.float32)
        .reshape(token_row_count, TOPK, model_width)
    )
    mixture = jnp.sum(gate_probs[..., None] * picked, axis=1)
    output = (hidden + mixture).astype(jnp.bfloat16)
    full_qkv, full_out, full_router = (
        lax.all_gather(query_key_value_weight, ("seq", "fsdp"), axis=0, tiled=True),
        lax.all_gather(w_out_t, ("seq", "fsdp"), axis=0, tiled=True),
        lax.all_gather(w_router, ("seq", "fsdp"), axis=0, tiled=True),
    )
    out_grad = cotangent[0].astype(jnp.float32)
    d_picked = (
        (gate_probs[..., None] * out_grad[:, None, :]).astype(jnp.bfloat16).reshape(-1, model_width)
    )
    d_gates = jnp.sum(picked * out_grad[:, None, :], axis=-1)
    d_send = pack_slots(d_picked, route_flat, slot_index, slot_shape)
    d_arrived = lax.all_to_all(
        lax.all_to_all(d_send, "seq", split_axis=0, concat_axis=0, tiled=True),
        "fsdp",
        split_axis=1,
        concat_axis=1,
        tiled=True,
    ).reshape(-1, model_width)
    d_inner = jnp.einsum("rd,fd->rf", d_arrived, down_weight, preferred_element_type=jnp.float32)
    d_gate_half = d_inner * up_half * gate_sig * (1.0 + gate_half * (1.0 - gate_sig))
    d_up_half = d_inner * silu_gate
    d_gate_up = jnp.concatenate([d_gate_half, d_up_half], axis=1).astype(jnp.bfloat16)
    d_w_down = jnp.einsum("rf,rd->fd", inner_act, d_arrived, preferred_element_type=jnp.float32)[
        None
    ]
    d_w_in = jnp.einsum("rd,rf->df", rows_in, d_gate_up, preferred_element_type=jnp.float32)[None]
    d_rows = jnp.einsum(
        "rf,df->rd", d_gate_up, gate_weight, preferred_element_type=jnp.float32
    ).astype(jnp.bfloat16)
    d_back = lax.all_to_all(
        lax.all_to_all(d_rows.reshape(slot_shape), "seq", split_axis=0, concat_axis=0, tiled=True),
        "fsdp",
        split_axis=1,
        concat_axis=1,
        tiled=True,
    )
    d_routed = jnp.sum(
        unpack_slots(d_back, route_flat, slot_index)
        .astype(jnp.float32)
        .reshape(token_row_count, TOPK, model_width),
        axis=1,
    )
    d_chosen = gate_probs * (d_gates - jnp.sum(gate_probs * d_gates, axis=-1, keepdims=True))
    d_logits = jnp.einsum("tk,tke->te", d_chosen, onehot_float).astype(jnp.bfloat16)
    d_normed_two = d_routed + jnp.einsum(
        "te,de->td", d_logits, full_router, preferred_element_type=jnp.float32
    )
    unused_two, pull_two = jax.vjp(rms_scale, hidden, ffn_gain)
    d_hidden_norm, d_ffn_gain = pull_two(d_normed_two)
    d_hidden = out_grad + d_hidden_norm
    d_attn = d_hidden.astype(jnp.bfloat16)
    d_attended = jnp.einsum(
        "td,dj->tj", d_attn, full_out, preferred_element_type=jnp.float32
    ).astype(jnp.bfloat16)
    d_heads = lax.all_to_all(
        d_attended.reshape(token_row_count, QUERY_HEADS, HEAD_DIMENSION),
        "seq",
        split_axis=1,
        concat_axis=0,
        tiled=True,
    )
    d_query, d_key_sum, d_value_sum = attend_backward(
        head_queries, head_keys, head_values, log_total, d_heads
    )
    seq_rows = head_queries.shape[0]
    local_cols = head_queries.shape[1] * HEAD_DIMENSION
    normed_all, d_attn_all = (
        lax.all_gather(normed_one, "seq", axis=0, tiled=True),
        lax.all_gather(d_attn, "seq", axis=0, tiled=True),
    )
    query_cols = lax.dynamic_slice_in_dim(
        full_qkv, lax.axis_index("seq") * local_cols, local_cols, 1
    )
    q_head_raw = jnp.dot(normed_all, query_cols, preferred_element_type=jnp.float32).reshape(
        head_queries.shape
    )
    seq_positions = jnp.arange(seq_rows, dtype=jnp.int32)
    unused_head, pull_head = jax.vjp(
        partial(head_prepare, positions=seq_positions), q_head_raw, q_gain
    )
    send_d_query, d_q_gain = pull_head(d_query)
    d_query_tok, grad_key_token_rows, grad_value_token_rows = (
        lax.all_to_all(
            send_d_query.astype(jnp.bfloat16), "seq", split_axis=0, concat_axis=1, tiled=True
        ).astype(send_d_query.dtype),
        lax.all_to_all(
            d_key_sum.astype(jnp.bfloat16), "seq", split_axis=0, concat_axis=1, tiled=True
        ).astype(d_key_sum.dtype),
        lax.all_to_all(
            d_value_sum.astype(jnp.bfloat16), "seq", split_axis=0, concat_axis=1, tiled=True
        ).astype(d_value_sum.dtype),
    )
    grad_key_per_head = jnp.sum(
        grad_key_token_rows.reshape(token_row_count, KEY_VALUE_HEADS, -1, HEAD_DIMENSION), axis=2
    )
    grad_value_per_head = jnp.sum(
        grad_value_token_rows.reshape(token_row_count, KEY_VALUE_HEADS, -1, HEAD_DIMENSION), axis=2
    )
    unused_k, pull_k = jax.vjp(prepare, key_unnormed, k_gain)
    grad_key_unnormed, d_k_gain = pull_k(grad_key_per_head)
    d_projected = jnp.concatenate(
        [
            d_query_tok.reshape(token_row_count, QUERY_HEADS * HEAD_DIMENSION),
            grad_key_unnormed.reshape(token_row_count, KEY_VALUE_HEADS * HEAD_DIMENSION),
            grad_value_per_head.reshape(token_row_count, KEY_VALUE_HEADS * HEAD_DIMENSION),
        ],
        axis=1,
    ).astype(jnp.bfloat16)
    d_normed_one = jnp.einsum(
        "tj,dj->td", d_projected, full_qkv, preferred_element_type=jnp.float32
    )
    unused_one, pull_one = jax.vjp(rms_scale, resid_in, attn_gain)
    d_resid_norm, d_attn_gain = pull_one(d_normed_one)
    d_tokens = (d_hidden + d_resid_norm).astype(jnp.bfloat16)[None]
    rows_dev = model_width // experts
    kv_count = 2 * KEY_VALUE_HEADS * HEAD_DIMENSION
    kv_grads = d_projected[:, QUERY_HEADS * HEAD_DIMENSION :]
    first_rows = normed_one
    summed = lax.psum_scatter(
        jnp.concatenate(
            [
                jnp.einsum("tc,tj->cj", first_rows, kv_grads, preferred_element_type=jnp.float32),
                jnp.einsum("tc,te->ce", normed_two, d_logits, preferred_element_type=jnp.float32),
            ],
            axis=1,
        ),
        ("seq", "fsdp"),
        scatter_dimension=0,
        tiled=True,
    )
    d_query_low = send_d_query.reshape(seq_rows, local_cols).astype(jnp.bfloat16)
    attended_heads = mixed_heads.reshape(seq_rows, local_cols)
    normed_order = (
        normed_all.reshape(seq_rows, sequence_count, shard_count, rows_dev)
        .transpose(0, 2, 1, 3)
        .reshape(seq_rows, model_width)
    )
    d_attn_order = (
        d_attn_all.reshape(seq_rows, sequence_count, shard_count, rows_dev)
        .transpose(0, 2, 1, 3)
        .reshape(seq_rows, model_width)
    )
    first_rows = normed_order
    head_sums = lax.psum_scatter(
        jnp.concatenate(
            [
                jnp.einsum(
                    "tc,tj->cj", first_rows, d_query_low, preferred_element_type=jnp.float32
                ),
                jnp.einsum(
                    "tc,tj->cj", d_attn_order, attended_heads, preferred_element_type=jnp.float32
                ),
            ],
            axis=1,
        ).astype(jnp.bfloat16),
        "fsdp",
        scatter_dimension=0,
        tiled=True,
    ).astype(jnp.float32)
    row_sums = (
        lax.all_to_all(
            head_sums.astype(jnp.bfloat16), "seq", split_axis=0, concat_axis=1, tiled=True
        )
        .astype(head_sums.dtype)
        .reshape(rows_dev, sequence_count, 2, local_cols)
    )
    d_w_query = row_sums[:, :, 0].reshape(rows_dev, QUERY_HEADS * HEAD_DIMENSION)
    d_w_out_t = row_sums[:, :, 1].reshape(rows_dev, QUERY_HEADS * HEAD_DIMENSION)
    d_w_qkv = jnp.concatenate([d_w_query, summed[:, :kv_count]], axis=1)
    d_w_router = summed[:, kv_count:]
    d_attn_gain, d_ffn_gain, d_q_gain, d_k_gain = lax.psum(
        (d_attn_gain, d_ffn_gain, d_q_gain, d_k_gain), ("seq", "fsdp")
    )
    return (
        output[None],
        d_tokens,
        d_w_qkv,
        d_w_out_t,
        d_w_router,
        d_w_in,
        d_w_down,
        d_attn_gain,
        d_ffn_gain,
        d_q_gain,
        d_k_gain,
    )


MESH = pl.DeviceIdType.MESH
VMEM_LIMIT = 60 * 2**20


class Place:
    def __init__(self):
        seq, shard = lax.axis_index("seq"), lax.axis_index("fsdp")
        self.z, self.x = seq // 2, seq % 2
        self.y, self.c = shard // 2, shard % 2
        self.z0, self.z1 = self.z % 2, self.z // 2
        self.low, self.high = self.z == 0, self.z == 3
        self.inner = (self.z0 + self.z1) == 1
        self.me = self.block(self.z, self.x, self.y, self.c)

    def device(self, z, x, y, c):
        return (z * 2 + x, y * 2 + c)

    def block(self, z, x, y, c):
        return (z * 2 + x) * 4 + y * 2 + c

    @property
    def by_x(self):
        return self.device(self.z, 1 - self.x, self.y, self.c)

    @property
    def by_y(self):
        return self.device(self.z, self.x, 1 - self.y, self.c)

    @property
    def by_core(self):
        return self.device(self.z, self.x, self.y, 1 - self.c)

    def by_z(self, step):
        return self.device(self.z + step, self.x, self.y, self.c)

    def near(self, k):
        return [self.z, 1 + self.z0, 2 - 2 * self.z0 + self.z1, 3 - 3 * self.z1][k]

    def onward(self, k):
        return [None, 2 * self.z1 - 1, 1 - 2 * self.z1, 2 * self.z1 - 1][k]

    def far(self, k):
        return self.near(3 - k)

    def toward(self, k):
        return [1 - 2 * self.z1, 1 - 2 * self.z0, 1 - 2 * self.z1][k]

    def greet(self, sides):
        barrier = pltpu.get_barrier_semaphore()
        for side in sides:
            if side != "z":
                target = {"x": self.by_x, "y": self.by_y, "core": self.by_core}[side]
                pl.semaphore_signal(barrier, inc=1, device_id=target, device_id_type=MESH)
        count = len([side for side in sides if side != "z"])
        if "z" in sides:

            @pl.when(jnp.logical_not(self.low))
            def _():
                pl.semaphore_signal(barrier, inc=1, device_id=self.by_z(-1), device_id_type=MESH)

            @pl.when(jnp.logical_not(self.high))
            def _():
                pl.semaphore_signal(barrier, inc=1, device_id=self.by_z(1), device_id_type=MESH)

            count = count + 1 + (self.z0 + self.z1) % 2
        pl.semaphore_wait(barrier, count)


def send(source, target, send_sem, recv_sem, device):
    pltpu.make_async_remote_copy(
        src_ref=source,
        dst_ref=target,
        send_sem=send_sem,
        recv_sem=recv_sem,
        device_id=device,
        device_id_type=MESH,
    ).start()


def await_bytes(ref, sem):
    pltpu.make_async_copy(ref, ref, sem).wait()


G_Z, G_X, G_Y, G_DX, G_DY, G_C0 = 0, 1, 2, 3, 4, 5
G_KINDS = 9


def gather_steps(place, own, out, ss, rs, zs, local_sem):
    p = place
    rows = out.shape[1]
    half = rows // 2
    x, y, c = p.x, p.y, p.c

    def cols(q):
        return [
            p.block(q, x, y, c),
            p.block(q, 1 - x, y, c),
            p.block(q, x, 1 - y, c),
            p.block(q, 1 - x, 1 - y, c),
        ]

    def to_core(q, j, src=None):
        b = cols(q)[j]
        send(out.at[b] if src is None else src, out.at[b], ss.at[q, G_C0 + j], rs.at[q, G_C0 + j], p.by_core)

    def plane_out(k):
        q = p.near(k)
        b = cols(q)[0]
        if k == 0:
            src = own
            for step, there in ((1, p.high), (-1, p.low)):

                @pl.when(jnp.logical_not(there))
                def _():
                    send(src, out.at[b], zs.at[q, 0 if step > 0 else 1], rs.at[q, G_Z], p.by_z(step))

            pltpu.make_async_copy(own, out.at[b], local_sem).start()
        else:
            src = out.at[b]

            @pl.when(jnp.logical_not(p.inner))
            def _():
                await_bytes(src, rs.at[q, G_Z])

        send(src, out.at[b], ss.at[q, G_X], rs.at[q, G_X], p.by_x)
        send(src, out.at[b], ss.at[q, G_Y], rs.at[q, G_Y], p.by_y)
        to_core(q, 0, src)

    def plane_hop(k):
        q = p.near(k)
        src = out.at[cols(q)[0]]

        @pl.when(p.inner)
        def _():
            await_bytes(src, rs.at[q, G_Z])
            send(src, src, zs.at[q, 0], rs.at[q, G_Z], p.by_z(p.onward(k)))

    def plane_turn(k):
        q = p.near(k)
        bx, by = out.at[cols(q)[1]], out.at[cols(q)[2]]
        await_bytes(bx, rs.at[q, G_X])
        first = bx.at[pl.ds(0, half)]
        send(first, first, ss.at[q, G_DY], rs.at[q, G_DY], p.by_y)
        to_core(q, 1)
        await_bytes(by, rs.at[q, G_Y])
        second = by.at[pl.ds(half, half)]
        send(second, second, ss.at[q, G_DX], rs.at[q, G_DX], p.by_x)
        to_core(q, 2)

    def plane_end(k):
        q = p.near(k)
        bd = out.at[cols(q)[3]]
        await_bytes(bd.at[pl.ds(0, half)], rs.at[q, G_DY])
        await_bytes(bd.at[pl.ds(half, half)], rs.at[q, G_DX])
        to_core(q, 3)

    def plane_core(k, js=(0, 1, 2, 3)):
        q = p.near(k)
        for j in js:
            await_bytes(own, rs.at[q, G_C0 + j])

    def finish():
        piece = own.at[pl.ds(0, half)]
        for q in range(4):
            for kind in (G_X, G_Y, G_C0, G_C0 + 1, G_C0 + 2, G_C0 + 3):
                await_bytes(own, ss.at[q, kind])
            for kind in (G_DX, G_DY):
                await_bytes(piece, ss.at[q, kind])
        for there, slot in ((p.high, 0), (p.low, 1)):

            @pl.when(jnp.logical_not(there))
            def _():
                await_bytes(own, zs.at[p.z, slot])

        for k in range(1, 4):

            @pl.when(p.inner)
            def _():
                await_bytes(own, zs.at[p.near(k), 0])

    return plane_out, plane_hop, plane_turn, plane_end, plane_core, finish


def sum_all_parts(p, part, held, core_in, x_half, y_half, x_in, y_in, z_in, out, ls, cs, cr, ss, rs, zs, zr):
    rows, width = part.shape[1], part.shape[2]
    half = rows // 2
    x, y, c = p.x, p.y, p.c

    def columns(q):
        return [(q, x, y), (q, 1 - x, y), (q, x, 1 - y), (q, 1 - x, 1 - y)]

    def start():
        for k in range(4):
            q = p.far(k)
            for j, (zz, xx, yy) in reversed(list(enumerate(columns(q)))):
                send(
                    part.at[p.block(zz, xx, yy, 1 - c)],
                    core_in.at[q * 4 + j],
                    cs.at[q, j],
                    cr.at[q, j],
                    p.by_core,
                )
                pltpu.make_async_copy(
                    part.at[p.block(zz, xx, yy, c)], held.at[q * 4 + j], ls.at[q, j]
                ).start()

    add = add_rows

    def plane_core(k, js=(3, 1, 2, 0)):
        q = p.far(k)
        for j in js:
            slot = q * 4 + j
            await_bytes(held.at[slot], ls.at[q, j])
            await_bytes(core_in.at[slot], cr.at[q, j])
            add(held.at[slot], core_in.at[slot], rows)
            if j == 3:
                send(held.at[slot, pl.ds(0, half)], y_half.at[q], ss.at[q, 0], rs.at[q, 0], p.by_y)
                send(held.at[slot, pl.ds(half, half)], x_half.at[q], ss.at[q, 1], rs.at[q, 1], p.by_x)

    def plane_turn(k):
        q = p.far(k)
        await_bytes(y_half.at[q], rs.at[q, 0])
        add(held.at[q * 4 + 1, pl.ds(0, half)], y_half.at[q], half)
        send(held.at[q * 4 + 1], x_in.at[q], ss.at[q, 2], rs.at[q, 2], p.by_x)
        await_bytes(x_half.at[q], rs.at[q, 1])
        add(held.at[q * 4 + 2, pl.ds(half, half)], x_half.at[q], half)
        send(held.at[q * 4 + 2], y_in.at[q], ss.at[q, 3], rs.at[q, 3], p.by_y)

    def plane_end(k):
        q = p.far(k)
        mine = held.at[q * 4]
        await_bytes(x_in.at[q], rs.at[q, 2])
        add(mine, x_in.at[q], rows)
        await_bytes(y_in.at[q], rs.at[q, 3])
        add(mine, y_in.at[q], rows)
        if k < 3:
            step = p.toward(k)
            slot = (1 - step) // 2

            @pl.when(p.inner)
            def _():
                await_bytes(z_in.at[slot, q], zr.at[slot, q])
                add(mine, z_in.at[slot, q], rows)

            send(mine, z_in.at[slot, q], zs.at[k], zr.at[slot, q], p.by_z(step))
        else:
            for slot, there in ((0, p.low), (1, p.high)):

                @pl.when(jnp.logical_not(there))
                def _():
                    await_bytes(z_in.at[slot, q], zr.at[slot, q])
                    add(mine, z_in.at[slot, q], rows)

            out[...] = mine[...]

    def finish():
        whole, piece = x_in.at[0], x_half.at[0]
        for q in range(4):
            for j in range(4):
                await_bytes(whole, cs.at[q, j])
            for kind in (0, 1):
                await_bytes(piece, ss.at[q, kind])
            for kind in (2, 3):
                await_bytes(whole, ss.at[q, kind])
        for k in range(3):
            await_bytes(whole, zs.at[k])

    return start, plane_core, plane_turn, plane_end, finish


def sum_all_kernel(
    part, both, rows_in, d_gate_up, inner, d_expert, columns, hidden, cot, gates, ffn_gain,
    out, d_logits, d_hidden, gains, pair, d_w_in, d_w_down,
    d_rows, router, router_sem, both_held, both_in, left, product, pair_sems, load_sems, left_sems, product_sems, *scratch,
):
    p = Place()
    p.greet(("x", "y", "core", "z"))
    start, plane_core, plane_turn, plane_end, finish = sum_all_parts(p, part, *scratch[:7], d_rows, *scratch[7:])
    rows = both.shape[3]

    def pair_sum(first):
        for s in (first, first + 1):
            for y in range(2):
                add_rows(both_held.at[s, y], both_in.at[s, y], rows)

    def right_load(source, i):
        width = source.shape[3]
        return pltpu.make_async_copy(source, both_in.at[:, :, :, pl.ds(0, width)], load_sems.at[i])

    def left_load(source, i, slot):
        cols = pl.ds(pl.multiple_of(i * TILE, TILE), TILE)
        return pltpu.make_async_copy(source.at[:, cols], left.at[slot], left_sems.at[slot])

    def product_store(target, i, slot):
        at = pl.ds(pl.multiple_of(i * TILE, TILE), TILE)
        piece = product.at[slot, :, pl.ds(0, target.shape[1])]
        return pltpu.make_async_copy(piece, target.at[at], product_sems.at[slot])

    def tiles(source, target, first, last):
        count, wide = source.shape[1] // TILE, target.shape[1]

        @pl.loop(first, last)
        def _(i):
            slot = i % 2
            left_load(source, i, slot).wait()

            @pl.when(i + 1 < count)
            def _():
                left_load(source, i + 1, 1 - slot).start()

            @pl.when(i >= 2)
            def _():
                product_store(target, i - 2, slot).wait()

            right = both_in[:, :, :, :wide].reshape(source.shape[0], wide)
            product[slot, :, :wide] = mxu(left[slot], right, TN).astype(product.dtype)
            product_store(target, i, slot).start()

    def tiles_end(source, target):
        count = source.shape[1] // TILE
        for i in (count - 2, count - 1):
            product_store(target, i, i % 2).wait()

    first = columns.shape[2] - 128
    router_load = pltpu.make_async_copy(columns.at[:, :, pl.ds(first, 128)], router, router_sem)
    router_load.start()
    start()
    send(both.at[:, :, 1 - p.c], both_in, pair_sems.at[0], pair_sems.at[1], p.by_core)
    pltpu.make_async_copy(both.at[:, :, p.c], both_held, pair_sems.at[2]).start()
    plane_core(0)
    plane_core(1)
    plane_turn(0)
    await_bytes(both_held, pair_sems.at[2])
    await_bytes(both_in, pair_sems.at[1])
    pair_sum(0)
    plane_core(2)
    pair_sum(2)
    plane_turn(1)
    pair_sum(4)
    pair_sum(6)
    pltpu.make_async_copy(both_held, pair, pair_sems.at[2]).start()
    right_load(d_gate_up, 0).start()
    left_load(rows_in, 0, 0).start()
    plane_end(0)
    plane_core(3)
    right_load(d_gate_up, 0).wait()
    tiles(rows_in, d_w_in, 0, 2)
    plane_turn(2)
    tiles(rows_in, d_w_in, 2, 4)
    plane_end(1)
    tiles(rows_in, d_w_in, 4, 6)
    plane_turn(3)
    tiles(rows_in, d_w_in, 6, 8)
    right_load(d_expert, 1).start()
    tiles_end(rows_in, d_w_in)
    left_load(inner, 0, 0).start()
    plane_end(2)
    right_load(d_expert, 1).wait()
    tiles(inner, d_w_down, 0, 3)
    plane_end(3)
    router_load.wait()
    width = hidden.shape[1]
    experts = part.shape[0]
    tail = d_rows[:, width:].astype(jnp.float32)
    lane = lax.broadcasted_iota(jnp.int32, tail.shape, 1)
    d_gates = jnp.where(lane < experts, tail + pltpu.roll(tail, 128 - experts, 1), 0.0)
    gate = gates[...]
    d_chosen = gate * (d_gates - jnp.sum(gate * d_gates, axis=-1, keepdims=True))
    d_logits[...] = d_chosen.astype(d_logits.dtype)
    gains[...] = jnp.zeros_like(gains)
    chunk = 32

    @pl.loop(0, rows // chunk)
    def _(i):
        at = pl.ds(pl.multiple_of(i * chunk, chunk), chunk)
        routed = mxu(d_logits[at, :], router[...].reshape(width, 128), NT)
        d_out = d_rows[at, :width].astype(jnp.float32) + routed
        x = hidden[at, :]
        scale = lax.rsqrt(jnp.mean(x * x, axis=-1, keepdims=True) + EPS)
        u = d_out * ffn_gain[...]
        dot = jnp.mean(u * x, axis=-1, keepdims=True)
        grad = cot[at, :].astype(jnp.float32) + scale * u - x * (scale * scale * scale * dot)
        d_hidden[at, :] = grad
        out[at, :] = grad.astype(out.dtype)
        gains[1:2, :] += jnp.sum(d_out * x * scale, axis=0, keepdims=True)

    tiles_end(inner, d_w_down)
    finish()
    await_bytes(both_held, pair_sems.at[0])
    pltpu.make_async_copy(both_held, pair, pair_sems.at[2]).wait()


def sum_all_scratch(rows, width):
    dma = pltpu.SemaphoreType.DMA
    bf16 = jnp.bfloat16
    return [
        pltpu.VMEM((16, rows, width), bf16),
        pltpu.VMEM((16, rows, width), bf16),
        pltpu.VMEM((4, rows // 2, width), bf16),
        pltpu.VMEM((4, rows // 2, width), bf16),
        pltpu.VMEM((4, rows, width), bf16),
        pltpu.VMEM((4, rows, width), bf16),
        pltpu.VMEM((2, 4, rows, width), bf16),
        dma((4, 4)),
        dma((4, 4)),
        dma((4, 4)),
        dma((4, 4)),
        dma((4, 4)),
        dma((3,)),
        dma((2, 4)),
    ]


def sum_all(
    part, both, rows_in, d_gate_up, inner, d_expert, columns, hidden, cot, gates, ffn_gain, collective_id
):
    blocks, rows, width = part.shape
    both = both.reshape(blocks // 4, 2, 2, rows, -1)
    pair = (blocks // 4, 2, rows, both.shape[4])
    anywhere, vmem = pl.BlockSpec(memory_space=pl.ANY), pl.BlockSpec(memory_space=pltpu.VMEM)
    return pl.pallas_call(
        sum_all_kernel,
        out_shape=[
            jax.ShapeDtypeStruct(hidden.shape, part.dtype),
            jax.ShapeDtypeStruct((rows, 128), part.dtype),
            jax.ShapeDtypeStruct(hidden.shape, jnp.float32),
            jax.ShapeDtypeStruct((8, hidden.shape[1]), jnp.float32),
            jax.ShapeDtypeStruct(pair, both.dtype),
            jax.ShapeDtypeStruct((rows_in.shape[1], d_gate_up.shape[1]), both.dtype),
            jax.ShapeDtypeStruct((inner.shape[1], d_expert.shape[1]), both.dtype),
        ],
        in_specs=[anywhere] * 7 + [vmem] * 4,
        out_specs=[vmem] * 4 + [anywhere] * 3,
        scratch_shapes=[
            pltpu.VMEM((rows, width), part.dtype),
            pltpu.VMEM((*columns.shape[:2], 128), part.dtype),
            pltpu.SemaphoreType.DMA,
            pltpu.VMEM(pair, both.dtype),
            pltpu.VMEM(pair, both.dtype),
            pltpu.VMEM((2, rows_in.shape[0], TILE), both.dtype),
            pltpu.VMEM((2, TILE, d_expert.shape[1]), both.dtype),
            pltpu.SemaphoreType.DMA((3,)),
            pltpu.SemaphoreType.DMA((2,)),
            pltpu.SemaphoreType.DMA((2,)),
            pltpu.SemaphoreType.DMA((2,)),
            *sum_all_scratch(rows, width),
        ],
        compiler_params=pltpu.CompilerParams(
            collective_id=collective_id, has_side_effects=True, vmem_limit_bytes=VMEM_LIMIT
        ),
        name="sum_all",
    )(
        part,
        both,
        rows_in,
        d_gate_up.reshape(*pair[:3], -1),
        inner,
        d_expert.reshape(*pair[:3], -1),
        columns,
        hidden,
        cot,
        gates,
        ffn_gain,
    )


def add_rows(target, source, count, chunk=32):
    @pl.loop(0, count // chunk)
    def _(i):
        at = pl.ds(pl.multiple_of(i * chunk, chunk), chunk)
        target[at, :] = target[at, :] + source[at, :]


def seq_peer(p, d):
    return ((p.z * 2 + p.x + d) % 8, p.y * 2 + p.c)


def greet_seq(p, sides=("y", "core")):
    barrier = pltpu.get_barrier_semaphore()
    for d in range(1, 8):
        pl.semaphore_signal(barrier, inc=1, device_id=seq_peer(p, d), device_id_type=MESH)
    for side in sides:
        target = {"y": p.by_y, "core": p.by_core}[side]
        pl.semaphore_signal(barrier, inc=1, device_id=target, device_id_type=MESH)
    pl.semaphore_wait(barrier, 7 + len(sides))


NT = (((1,), (1,)), ((), ()))
TILE = 256
WIDE = 1024
TALL = 1024


def mxu(a, b, dims=(((1,), (0,)), ((), ()))):
    return lax.dot_general(a, b, dims, preferred_element_type=jnp.float32)


def experts_kernel(
    own, cot_all, w_in_hbm, w_down_hbm,
    rows_all, out_part, d_part, x_all, d_expert_all, inner_all, d_gate_up_all,
    w_in, w_down, row_buf, cot_buf, pick, pick_t, gates, d_gates, x, cot, d_expert,
    by_d_gate, by_d_up, inner, d_gate_up, held, out_stage, d_stage,
    ss, rs, zs, local_sem, load_sems, store_sems,
):
    p = Place()
    bf16, f32 = jnp.bfloat16, jnp.float32
    width = cot_all.shape[2]
    blocks = 8
    slots = gates.shape[0]
    capacity = slots // blocks
    tokens = row_buf.shape[2]
    group = 4
    experts = rows_all.shape[0]
    p.greet(("x", "y", "core", "z"))
    plane_out, plane_hop, plane_turn, plane_end, plane_core, finish = gather_steps(
        p, own, rows_all, ss, rs, zs, local_sem
    )

    def weights(start):
        for i, (src, dst) in enumerate(((w_in_hbm, w_in), (w_down_hbm, w_down))):
            copy = pltpu.make_async_copy(src, dst, load_sems.at[i])
            copy.start() if start else copy.wait()

    def cot_load(k):
        return pltpu.make_async_copy(
            cot_all.at[pl.ds(p.near(k) * blocks, blocks)], cot_buf.at[k % 2], load_sems.at[2 + k]
        )

    def row_load(k):
        return pltpu.make_async_copy(
            rows_all.at[pl.ds(p.near(k) * blocks, blocks)], row_buf.at[k % 2], load_sems.at[6 + k]
        )

    def arrived(k):
        plane_core(k)
        row_load(k).start()

    sides = (p.x, 1 - p.x)

    def side_load(i):
        at = pl.ds(sides[i] * group, group)
        source = rows_all.at[pl.ds(p.z * blocks + sides[i] * group, group)]
        return pltpu.make_async_copy(source, row_buf.at[0, at], load_sems.at[(6, 10)[i]])

    def side_arrived(i):
        plane_core(0, ((0, 2), (1, 3))[i])
        if i == 0:
            pltpu.make_async_copy(own, rows_all.at[p.me], local_sem).wait()
        side_load(i).start()

    at_slot = {}

    def store(k, i, src, dst):
        if (k, i) not in at_slot:
            at_slot[k, i] = pltpu.make_async_copy(src, dst, store_sems.at[i, k % 2])
        return at_slot[k, i]

    def stores(k):
        q = p.near(k)
        at = pl.ds(q * slots, slots)
        plane = pl.ds(q * blocks, blocks)
        return [
            (x, x_all.at[at]),
            (d_expert, d_expert_all.at[at]),
            (inner, inner_all.at[at]),
            (d_gate_up, d_gate_up_all.at[at]),
            (out_stage, out_part.at[plane]),
            (d_stage, d_part.at[plane]),
        ]

    def put(k, i):
        store(k, i, *stores(k)[i]).start()

    def free(k, i):
        if k > 0:
            store(k - 1, i, *stores(k - 1)[i]).wait()

    def pick_rows(k, g):
        lane = lax.broadcasted_iota(jnp.int32, (8, 128), 1)
        line = lax.broadcasted_iota(jnp.int32, (8, 128), 0)
        select = jnp.where((lane == line * experts + p.me) & (line < 3), 1.0, 0.0).astype(bf16)
        slot_id = lax.broadcasted_iota(jnp.int32, (capacity, tokens), 0).astype(f32) + 1.0
        rows, cots = row_buf.at[k % 2], cot_buf.at[k % 2]
        which = pl.ds(g * group, group)
        lines = mxu(select, rows[which, :, width:].reshape(group * tokens, 128), NT)
        for i in range(group):
            mine = lines[:, i * tokens : (i + 1) * tokens]
            chosen = jnp.where(mine[2:3] == slot_id, 1.0, 0.0)
            gate = jnp.sum(chosen * (mine[0:1] + mine[1:2]), axis=1, keepdims=True)
            at = pl.ds(pl.multiple_of((g * group + i) * capacity, capacity), capacity)
            gates[at, :] = jnp.broadcast_to(gate, (capacity, 128))
            lead = [jnp.zeros((capacity, tokens), bf16)] * i
            tail = [jnp.zeros((capacity, tokens), bf16)] * (group - 1 - i)
            pick[g, i * capacity : (i + 1) * capacity, :] = jnp.concatenate(
                lead + [chosen.astype(bf16)] + tail, axis=1
            )
            lead = [jnp.zeros((tokens, capacity), f32)] * i
            tail = [jnp.zeros((tokens, capacity), f32)] * (group - 1 - i)
            pick_t[g, i * tokens : (i + 1) * tokens, :] = jnp.concatenate(
                lead + [chosen.T] + tail, axis=1
            ).astype(bf16)
        at = slots_at(g)

        @pl.loop(0, width // WIDE)
        def _(n):
            cols = pl.ds(pl.multiple_of(n * WIDE, WIDE), WIDE)
            row_tile = rows[which, :, cols].reshape(group * tokens, WIDE)
            x[at, cols] = mxu(pick[g], row_tile).astype(bf16)
            cot_tile = cots[which, :, cols].reshape(group * tokens, WIDE)
            picked = mxu(pick[g], cot_tile)
            cot[at, cols] = picked.astype(bf16)
            scale = jnp.concatenate([gates[at, :]] * (WIDE // 128), axis=1)
            d_expert[at, cols] = (scale * picked).astype(bf16)

    def slots_at(g):
        if g is None:
            return pl.ds(0, slots)
        return pl.ds(pl.multiple_of(g * group * capacity, group * capacity), group * capacity)

    def up(g=None):
        ff = inner.shape[1]
        at = slots_at(g)

        @pl.loop(0, ff // TILE)
        def _(n):
            cols = pl.ds(pl.multiple_of(n * TILE, TILE), TILE)
            gate = mxu(x[at, :], w_in[:, cols])
            raised = mxu(x[at, :], w_in[:, pl.ds(pl.multiple_of(ff + n * TILE, TILE), TILE)])
            sig = jax.nn.sigmoid(gate)
            silu = gate * sig
            inner[at, cols] = (silu * raised).astype(bf16)
            by_d_up[at, cols] = silu
            by_d_gate[at, cols] = raised * sig * (1.0 + gate * (1.0 - sig))

    def d_up(g=None):
        ff = inner.shape[1]
        at = slots_at(g)

        @pl.loop(0, ff // TILE)
        def _(n):
            cols = pl.ds(pl.multiple_of(n * TILE, TILE), TILE)
            d_inner = mxu(d_expert[at, :], w_down[cols, :], NT)
            d_gate_up[at, cols] = (d_inner * by_d_gate[at, cols]).astype(bf16)
            d_gate_up[at, pl.ds(pl.multiple_of(ff + n * TILE, TILE), TILE)] = (
                d_inner * by_d_up[at, cols]
            ).astype(bf16)

    def spread(stage, sides_done=(0, 1)):
        @pl.loop(0, width // WIDE)
        def _(n):
            cols = pl.ds(pl.multiple_of(n * WIDE, WIDE), WIDE)
            for g in sides_done:
                result = mxu(pick_t[g], held[slots_at(g), cols]).astype(bf16)
                stage[pl.ds(g * group, group), :, cols] = result.reshape(group, tokens, WIDE)

    def down(g=None):
        at = slots_at(g)
        d_gates[at, :] = jnp.zeros_like(d_gates[at, :])

        @pl.loop(0, width // TALL)
        def _(n):
            cols = pl.ds(pl.multiple_of(n * TALL, TALL), TALL)
            result = mxu(inner[at, :], w_down[:, cols]).astype(bf16).astype(f32)
            product = result * cot[at, cols].astype(f32)
            total = product[:, :128]
            for j in range(1, TALL // 128):
                total = total + product[:, j * 128 : (j + 1) * 128]
            d_gates[at, :] += total
            scale = jnp.concatenate([gates[at, :]] * (TALL // 128), axis=1)
            held[at, cols] = (scale * result).astype(bf16)

    def d_down(g=None, sides_done=(0, 1)):
        for side in sides_done:
            at = slots_at(side)
            total = jnp.sum(d_gates[at, :], axis=1, keepdims=True)
            high = total.astype(bf16).astype(f32)
            lane = lax.broadcasted_iota(jnp.int32, (group * capacity, 128), 1)
            info = jnp.where(
                lane == p.me, high, jnp.where(lane == experts + p.me, total - high, 0.0)
            )
            result = mxu(pick_t[side], info.astype(bf16)).astype(bf16)
            d_stage[pl.ds(side * group, group), :, width:] = result.reshape(group, tokens, 128)
        at = slots_at(g)

        @pl.loop(0, width // TALL)
        def _(n):
            cols = pl.ds(pl.multiple_of(n * TALL, TALL), TALL)
            held[at, cols] = mxu(d_gate_up[at, :], w_in[cols, :], NT).astype(bf16)

    plane_out(0)
    weights(True)
    cot_load(0).start()
    plane_turn(0)
    side_arrived(0)
    plane_hop(1)
    plane_out(1)
    plane_hop(2)
    weights(False)
    cot_load(0).wait()
    cot_load(1).start()
    side_load(0).wait()
    side = sides[0]
    pick_rows(0, side)
    up(side)
    plane_end(0)
    d_up(side)
    down(side)
    plane_hop(3)
    side_arrived(1)
    spread(out_stage, (side,))
    d_down(side, (side,))
    plane_turn(1)
    plane_out(2)
    spread(d_stage, (side,))
    side_load(1).wait()
    side = sides[1]
    pick_rows(0, side)
    put(0, 0)
    put(0, 1)
    up(side)
    put(0, 2)
    plane_end(1)
    d_up(side)
    put(0, 3)
    down(side)
    spread(out_stage, (side,))
    put(0, 4)
    arrived(1)
    d_down(side, (side,))
    spread(d_stage, (side,))
    put(0, 5)
    after = {
        (1, 0): ((plane_turn, 2), (plane_out, 3)),
        (1, 3): ((plane_end, 2),),
        (1, 5): ((arrived, 2),),
        (2, 0): ((plane_turn, 3),),
        (2, 3): ((plane_end, 3),),
        (2, 5): ((arrived, 3),),
    }
    for k in range(1, 4):

        def service(i):
            for step, plane in after.get((k, i), ()):
                step(plane)

        row_load(k).wait()
        cot_load(k).wait()
        if k < 3:
            cot_load(k + 1).start()
        free(k, 0)
        free(k, 1)
        for g in range(2):
            pick_rows(k, g)
        put(k, 0)
        put(k, 1)
        service(0)
        free(k, 2)
        up()
        put(k, 2)
        service(1)
        free(k, 3)
        d_up()
        put(k, 3)
        service(2)
        free(k, 4)
        down()
        service(3)
        spread(out_stage)
        put(k, 4)
        service(4)
        free(k, 5)
        d_down()
        service(5)
        spread(d_stage)
        put(k, 5)
    for i in range(6):
        free(4, i)
    finish()


def experts_gathered(own, cot_all, w_in, w_down, capacity, collective_id):
    tokens, wide = own.shape
    experts, _, width = cot_all.shape
    ff = w_down.shape[0]
    slots = 8 * capacity
    dma = pltpu.SemaphoreType.DMA
    bf16, f32 = jnp.bfloat16, jnp.float32
    anywhere = pl.BlockSpec(memory_space=pl.ANY)

    def array(*shape):
        return jax.ShapeDtypeStruct(shape, bf16)

    return pl.pallas_call(
        experts_kernel,
        out_shape=[
            array(experts, tokens, wide),
            array(experts, tokens, width),
            array(experts, tokens, wide),
            array(experts * capacity, width),
            array(experts * capacity, width),
            array(experts * capacity, ff),
            array(experts * capacity, 2 * ff),
        ],
        in_specs=[anywhere] * 4,
        out_specs=[anywhere] * 7,
        scratch_shapes=[
            pltpu.VMEM(w_in.shape, bf16),
            pltpu.VMEM(w_down.shape, bf16),
            pltpu.VMEM((2, 8, tokens, wide), bf16),
            pltpu.VMEM((2, 8, tokens, width), bf16),
            pltpu.VMEM((2, 4 * capacity, 4 * tokens), bf16),
            pltpu.VMEM((2, 4 * tokens, 4 * capacity), bf16),
            pltpu.VMEM((slots, 128), f32),
            pltpu.VMEM((slots, 128), f32),
            pltpu.VMEM((slots, width), bf16),
            pltpu.VMEM((slots, width), bf16),
            pltpu.VMEM((slots, width), bf16),
            pltpu.VMEM((slots, ff), f32),
            pltpu.VMEM((slots, ff), f32),
            pltpu.VMEM((slots, ff), bf16),
            pltpu.VMEM((slots, 2 * ff), bf16),
            pltpu.VMEM((slots, width), bf16),
            pltpu.VMEM((8, tokens, width), bf16),
            pltpu.VMEM((8, tokens, wide), bf16),
            dma((4, G_KINDS)),
            dma((4, G_KINDS)),
            dma((4, 2)),
            dma,
            dma((11,)),
            dma((6, 2)),
        ],
        compiler_params=pltpu.CompilerParams(
            collective_id=collective_id, has_side_effects=True, vmem_limit_bytes=VMEM_LIMIT
        ),
        name="experts",
    )(own, cot_all, w_in, w_down)


TN = (((0,), (0,)), ((), ()))


def back_kernel(
    own, pair, columns_hbm, normed_hbm, queries_hbm, keys_hbm, values_hbm, attended_hbm,
    q_raw_hbm, k_raw_hbm, cosine_hbm, sine_hbm, tokens_hbm, d_hidden_hbm, routed_hbm, d_logits_hbm,
    q_gain, k_gain, attn_gain, gains,
    d_tokens, d_qkv, d_out_t, d_router, gains_out, mixture,
    queries, keys, values, attended, q_raw, k_raw, cosine, sine, tokens, d_hidden, routed, d_logits, input_sems,
    cols_out, d_attn, columns, normed, d_normed, d_heads, d_query, d_key, d_value, d_proj, q_sum, k_sum,
    held, x_in, y_in, z_in, g_send, g_in, x_two, z_two, c_core, c_y,
    gs, gr, gz, load_sems, local_sem, hs, ys, yr, xs, xr, zs, zr, ts, tr,
    normed_sems, free, xs2, xr2, zs2, zr2, cs, cr, cys, cyr, as_, ar,
):
    p = Place()
    bf16, f32 = jnp.bfloat16, jnp.float32
    columns_z = [p.device((p.z + d) % 4, p.x, p.y, p.c) for d in (1, 2, 3)]
    greet_seq(p)
    rows, wide = own.shape
    length, head_cols = queries.shape
    heads = head_cols // HEAD_DIMENSION
    width = d_normed.shape[2]
    proj_cols = d_proj.shape[1]
    plane_rows = 2 * rows
    score_scale = 1.0 / math.sqrt(HEAD_DIMENSION)
    place = p.z * 2 + p.x

    def rows_at(q, x):
        return d_attn.at[q * 2 + x]

    def gather_out(k):
        q = p.near(k)
        there = rows_at(q, p.x)
        if k == 0:
            src = own
            for step, end in ((1, p.high), (-1, p.low)):

                @pl.when(jnp.logical_not(end))
                def _():
                    send(src, there, gz.at[q, 0 if step > 0 else 1], gr.at[q, 0], p.by_z(step))

            pltpu.make_async_copy(own, there, local_sem).start()
        else:
            src = there

            @pl.when(jnp.logical_not(p.inner))
            def _():
                await_bytes(src, gr.at[q, 0])

        send(src, there, gs.at[q], gr.at[q, 1], p.by_x)

    def gather_hop(k):
        q = p.near(k)
        there = rows_at(q, p.x)

        @pl.when(p.inner)
        def _():
            await_bytes(there, gr.at[q, 0])
            send(there, there, gz.at[q, 0], gr.at[q, 0], p.by_z(p.onward(k)))

    def gather_in(k):
        if k == 0:
            pltpu.make_async_copy(own, rows_at(p.z, p.x), local_sem).wait()
        await_bytes(own, gr.at[p.near(k), 1])

    def at_pair(q, x, y):
        return pair.at[q * 4 + x * 2 + y]

    def sum_send(k):
        q = p.far(k)
        for j, x in ((1, 1 - p.x), (0, p.x)):
            i = q * 2 + j
            send(at_pair(q, x, 1 - p.y), y_in.at[k % 2 * 2 + j], ys.at[i], yr.at[i], p.by_y)

    def sum_start():
        sum_send(0)
        sum_send(1)
        for k in range(4):
            q = p.far(k)
            for j, x in ((1, 1 - p.x), (0, p.x)):
                pltpu.make_async_copy(at_pair(q, x, p.y), held.at[q * 2 + j], hs.at[q * 2 + j]).start()

    def sum_turn(k):
        q = p.far(k)
        for j in (1, 0):
            slot = q * 2 + j
            landed = y_in.at[k % 2 * 2 + j]
            await_bytes(held.at[slot], hs.at[slot])
            await_bytes(landed, yr.at[slot])
            add_rows(held.at[slot], landed, rows)
            if j == 1:
                send(held.at[slot], x_in.at[q], xs.at[q], xr.at[q], p.by_x)
        if k < 2:
            pl.semaphore_signal(free, inc=1, device_id=p.by_y, device_id_type=MESH)
            pl.semaphore_wait(free, 1)
            sum_send(k + 2)

    def line_sum(k, mine, landed, sends, arrivals):
        q = p.far(k)
        if k < 3:
            step = p.toward(k)
            slot, hops = (1 - step) // 2, (q - p.z) * step

            @pl.when(p.inner)
            def _():
                await_bytes(landed.at[slot, hops], arrivals.at[slot, hops])
                add_rows(mine, landed.at[slot, hops], rows)

            send(mine, landed.at[slot, hops - 1], sends.at[k], arrivals.at[slot, hops - 1], p.by_z(step))
        else:
            for slot, there in ((0, p.low), (1, p.high)):

                @pl.when(jnp.logical_not(there))
                def _():
                    await_bytes(landed.at[slot, 0], arrivals.at[slot, 0])
                    add_rows(mine, landed.at[slot, 0], rows)

    def sum_end(k):
        q = p.far(k)
        mine = held.at[q * 2]
        await_bytes(x_in.at[q], xr.at[q])
        add_rows(mine, x_in.at[q], rows)
        line_sum(k, mine, z_in, zs, zr)
        if k == 3:
            mixture[...] = mine[...]

    def two_start(*steps):
        for k in steps:
            q = p.far(k)
            send(d_normed.at[q * 2 + 1 - p.x], x_two.at[q], xs2.at[q], xr2.at[q], p.by_x)

    def two_end(k):
        q = p.far(k)
        mine = d_normed.at[q * 2 + p.x]
        await_bytes(x_two.at[q], xr2.at[q])
        add_rows(mine, x_two.at[q], rows)
        line_sum(k, mine, z_two, zs2, zr2)

    piece_rows = c_y.shape[1]
    order = [(place + d) % 8 for d in range(1, 9)]
    piece_width = c_y.shape[2]
    cols_at = cols_out.at[place]

    def cols_start():
        for turn, side in ((0, 1 - p.y), (1, p.y)):
            send(columns.at[:, side, 1 - p.c], c_core.at[turn], cs.at[turn], cr.at[turn], p.by_core)

    def cols_core():
        for turn, side in ((0, 1 - p.y), (1, p.y)):
            await_bytes(c_core.at[turn], cr.at[turn])
            for s in order:
                add_rows(columns.at[s, side, p.c], c_core.at[turn, s], piece_rows)
                if turn == 0:
                    send(columns.at[s, side, p.c], c_y.at[s], cys.at[s], cyr.at[s], p.by_y)

    def cols_turn(*steps):
        for i in steps:
            s = order[i]
            mine = columns.at[s, p.y, p.c]
            await_bytes(c_y.at[s], cyr.at[s])
            add_rows(mine, c_y.at[s], piece_rows)
            if i < 7:
                send(mine, cols_at, as_.at[i], ar.at[i], seq_peer(p, i + 1))
            else:
                pltpu.make_async_copy(mine, cols_at, as_.at[7]).start()

    def norm_back():
        mine = d_normed.at[p.z * 2 + p.x]
        chunk = 16

        @pl.loop(0, rows // chunk)
        def _(i):
            at = pl.ds(pl.multiple_of(i * chunk, chunk), chunk)
            d_out = mine[at, :].astype(f32)
            x = tokens[at, :].astype(f32)
            scale = lax.rsqrt(jnp.mean(x * x, axis=-1, keepdims=True) + EPS)
            u = d_out * attn_gain[...]
            dot = jnp.mean(u * x, axis=-1, keepdims=True)
            d_x = scale * u - x * (scale * scale * scale * dot)
            d_tokens[at, :] = (d_hidden[at, :] + d_x).astype(d_tokens.dtype)

    def attention(q):
        row_start = pl.multiple_of(q * plane_rows, plane_rows)
        at = pl.ds(row_start, plane_rows)

        @pl.loop(0, head_cols // TILE)
        def _(n):
            cols = pl.ds(pl.multiple_of(n * TILE, TILE), TILE)
            grad = d_attn[pl.ds(q * 2, 2)].reshape(plane_rows, width)
            weight_cols = pl.ds(pl.multiple_of(proj_cols + n * TILE, TILE), TILE)
            weight = columns[..., weight_cols].reshape(width, TILE)
            d_heads[at, cols] = mxu(grad, weight).astype(bf16)

        def block(count):
            key, value = keys[:count], values[:count]
            row_pos = row_start + lax.broadcasted_iota(jnp.int32, (plane_rows, count), 0)
            allowed = lax.broadcasted_iota(jnp.int32, (plane_rows, count), 1) <= row_pos

            @pl.loop(0, heads)
            def _(h):
                cols = pl.ds(pl.multiple_of(h * HEAD_DIMENSION, HEAD_DIMENSION), HEAD_DIMENSION)
                query, d_out = queries[at, cols], d_heads[at, cols]
                scores = jnp.where(allowed, mxu(query, key, NT) * score_scale, -1e30)
                raised = jnp.exp(scores - jnp.max(scores, axis=-1, keepdims=True))
                prob = raised / jnp.sum(raised, axis=-1, keepdims=True)
                d_prob = mxu(d_out, value, NT)
                delta = jnp.sum(prob * d_prob, axis=-1, keepdims=True)
                d_scores = (prob * (d_prob - delta)).astype(bf16)
                d_query[at, cols] = mxu(d_scores, key) * score_scale
                d_key[:count] += mxu(d_scores, query, TN) * score_scale
                d_value[:count] += mxu(prob.astype(bf16), d_out, TN)

        half = length // 2

        @pl.when(q < 2)
        def _():
            block(half)

        @pl.when(q >= 2)
        def _():
            block(length)

    def unrotate(grad, at):
        swapped = jnp.concatenate(
            [grad[:, HEAD_DIMENSION // 2 :], grad[:, : HEAD_DIMENSION // 2]], axis=1
        )
        return grad * cosine[at, :] + swapped * sine[at, :]

    def raw_grads():
        q_sum[...] = jnp.zeros_like(q_sum)
        k_sum[...] = jnp.zeros_like(k_sum)

        def one(grad, raw, gain, total, at):
            turned = unrotate(grad, at)
            scale = lax.rsqrt(jnp.mean(raw * raw, axis=-1, keepdims=True) + EPS)
            total[...] += jnp.sum((turned * raw * scale).reshape(-1, 8, HEAD_DIMENSION), axis=0)
            u = turned * gain[...]
            dot = jnp.mean(u * raw, axis=-1, keepdims=True)
            return (scale * u - raw * (scale * scale * scale * dot)).astype(bf16)

        chunk = 128

        @pl.loop(0, length // chunk)
        def _(i):
            at = pl.ds(pl.multiple_of(i * chunk, chunk), chunk)
            for h in range(heads):
                cols = slice(h * HEAD_DIMENSION, (h + 1) * HEAD_DIMENSION)
                d_proj[at, cols] = one(d_query[at, cols], q_raw[at, cols], q_gain, q_sum, at)
            d_proj[at, head_cols : head_cols + HEAD_DIMENSION] = one(
                d_key[at, :], k_raw[at, :], k_gain, k_sum, at
            )
            d_proj[at, head_cols + HEAD_DIMENSION :] = d_value[at, :].astype(bf16)

        g_send[0] = gains[...]
        g_send[0, 2:3, :HEAD_DIMENSION] = jnp.sum(q_sum[...], axis=0, keepdims=True)
        g_send[0, 2:3, HEAD_DIMENSION : 2 * HEAD_DIMENSION] = jnp.sum(
            k_sum[...], axis=0, keepdims=True
        )

    def normed_load(n, slot):
        cols = pl.ds(pl.multiple_of(n * TILE, TILE), TILE)
        return pltpu.make_async_copy(normed_hbm.at[:, cols], normed.at[slot], normed_sems.at[slot])

    def normed_grads():
        @pl.loop(0, width // TILE)
        def _(n):
            cols = pl.ds(pl.multiple_of(n * TILE, TILE), TILE)
            slot = n % 2
            normed_load(n, slot).wait()

            @pl.when(n + 1 < width // TILE)
            def _():
                normed_load(n + 1, 1 - slot).start()

            weight = columns[n, :, :, :, :proj_cols].reshape(TILE, proj_cols)
            part = mxu(d_proj[...], weight, NT)
            d_normed[:, :, cols] = part.astype(bf16).reshape(length // rows, rows, TILE)
            total = jnp.sum(part * normed[slot].astype(f32), axis=0, keepdims=True)
            g_send[0, 0:1, cols] = total / attn_gain[:, cols]
            grad = mxu(normed[slot], d_proj[...], TN).astype(bf16)
            columns[n, :, :, :, :proj_cols] = grad.reshape(2, 2, -1, proj_cols)

    def gains_pass(t, target):
        send(g_send.at[t], g_in.at[t], ts.at[t], tr.at[t], target)

    def gains_take(t):
        await_bytes(g_in.at[t], tr.at[t])
        g_send[t + 1] = g_send[t] + g_in[t]

    def gains_z_pass():
        g_in[2 + p.z] = g_send[2]
        for d, target in enumerate(columns_z):
            send(g_send.at[2], g_in.at[2 + p.z], ts.at[2 + d], tr.at[2 + d], target)

    def gains_z_take():
        for d in range(3):
            await_bytes(g_in.at[0], tr.at[2 + d])
        g_send[3] = g_in[2] + g_in[3] + g_in[4] + g_in[5]

    def router_grads():
        @pl.loop(0, width // TILE)
        def _(n):
            cols = pl.ds(pl.multiple_of(n * TILE, TILE), TILE)
            grad = mxu(routed[:, cols], d_logits[...], TN).astype(bf16)
            columns[n, :, :, :, proj_cols + head_cols :] = grad.reshape(2, 2, -1, 128)

    def column_grads(value, first, count):
        @pl.loop(0, width // TILE)
        def _(n):
            cols = pl.ds(pl.multiple_of(n * TILE, TILE), TILE)
            part = d_attn[:, :, cols].reshape(length, TILE)
            grad = mxu(part, value[...], TN).astype(bf16)
            columns[n, :, :, :, first : first + count] = grad.reshape(2, 2, -1, count)

    loads = [
        pltpu.make_async_copy(columns_hbm, columns, load_sems.at[0]),
    ]
    gather_out(0)
    inputs = [
        pltpu.make_async_copy(source, target, input_sems.at[i])
        for i, (source, target) in enumerate(
            (
                (queries_hbm, queries),
                (keys_hbm, keys),
                (values_hbm, values),
                (attended_hbm, attended),
                (q_raw_hbm, q_raw),
                (k_raw_hbm, k_raw),
                (cosine_hbm, cosine),
                (sine_hbm, sine),
                (tokens_hbm, tokens),
                (d_hidden_hbm, d_hidden),
                (routed_hbm, routed),
                (d_logits_hbm, d_logits),
            )
        )
    ]
    loads[0].start()
    for copy in inputs:
        copy.start()
    normed_load(0, 0).start()
    sum_start()
    d_key[...] = jnp.zeros_like(d_key)
    d_value[...] = jnp.zeros_like(d_value)
    loads[0].wait()
    for copy in inputs:
        copy.wait()
    gather_in(0)
    gather_hop(1)
    gather_out(1)
    gather_hop(2)
    attention(p.near(0))
    gather_out(2)
    gather_hop(3)
    gather_in(1)
    attention(p.near(1))
    sum_turn(0)
    gather_out(3)
    gather_in(2)
    attention(p.near(2))
    sum_end(0)
    sum_turn(1)
    gather_in(3)
    attention(p.near(3))
    raw_grads()
    sum_end(1)
    normed_grads()
    gains_pass(0, p.by_core)
    column_grads(attended, proj_cols, head_cols)
    gains_take(0)
    gains_pass(1, p.by_x)
    two_start(0, 1)
    router_grads()
    cols_start()
    gains_take(1)
    gains_z_pass()
    sum_turn(2)
    two_start(2, 3)
    cols_core()
    two_end(0)
    sum_turn(3)
    gains_z_take()
    send(g_send.at[3], g_in.at[6], ts.at[5], tr.at[5], p.by_y)
    two_end(1)
    cols_turn(0, 1)
    sum_end(2)
    cols_turn(2, 3, 4, 5)
    two_end(2)
    cols_turn(6, 7)
    two_end(3)
    norm_back()
    sum_end(3)
    await_bytes(g_in.at[6], tr.at[5])
    gains_out[...] = g_send[3] + g_in[6]
    for t in range(6):
        await_bytes(g_in.at[0], ts.at[t])
    for q in range(4):
        await_bytes(own, gs.at[q])
    for there, slot in ((p.high, 0), (p.low, 1)):

        @pl.when(jnp.logical_not(there))
        def _():
            await_bytes(own, gz.at[p.z, slot])

    for k in range(1, 4):

        @pl.when(p.inner)
        def _():
            await_bytes(own, gz.at[p.near(k), 0])

    piece = x_in.at[0]
    for i in range(8):
        await_bytes(piece, ys.at[i])
    for q in range(4):
        await_bytes(piece, xs.at[q])
    for k in range(3):
        await_bytes(piece, zs.at[k])
        await_bytes(piece, zs2.at[k])
    for q in range(4):
        await_bytes(piece, xs2.at[q])
    for i in range(8):
        if i < 7:
            await_bytes(c_y.at[0], ar.at[i])
        await_bytes(c_y.at[0], as_.at[i])
        await_bytes(c_y.at[0], cys.at[i])
    for turn in range(2):
        await_bytes(c_core.at[turn], cs.at[turn])
    key_cols = KEY_VALUE_HEADS * HEAD_DIMENSION
    per_group = 8 // KEY_VALUE_HEADS
    router_total = jnp.zeros((piece_rows, 128), f32)
    for s in range(8):
        d_qkv[:, s * head_cols : (s + 1) * head_cols] = cols_out[s, :, :head_cols].astype(f32)
        d_out_t[:, s * head_cols : (s + 1) * head_cols] = cols_out[
            s, :, proj_cols : proj_cols + head_cols
        ].astype(f32)
        part = cols_out[s, :, proj_cols + head_cols :].astype(f32)
        router_total = router_total + part
    d_router[...] = router_total
    for g in range(KEY_VALUE_HEADS):
        for j in range(2):
            lanes = slice(head_cols + j * HEAD_DIMENSION, head_cols + (j + 1) * HEAD_DIMENSION)
            total = cols_out[g * per_group, :, lanes].astype(f32)
            for s in range(1, per_group):
                total = total + cols_out[g * per_group + s, :, lanes].astype(f32)
            first = 8 * head_cols + j * key_cols + g * HEAD_DIMENSION
            d_qkv[:, first : first + HEAD_DIMENSION] = total


def back(
    own, pair, columns, normed, queries, keys, values, attended,
    q_raw, k_raw, cosine, sine, q_gain, k_gain, attn_gain, gains, tokens, d_hidden,
    routed, d_logits, collective_id,
):
    inputs = (
        queries, keys, values, attended, q_raw, k_raw, cosine, sine, tokens, d_hidden, routed, d_logits,
    )
    rows, wide = own.shape
    length, head_cols = queries.shape
    width = normed.shape[1]
    piece_rows, piece_width = columns.shape[3:]
    proj_cols = head_cols + 2 * HEAD_DIMENSION
    dma = pltpu.SemaphoreType.DMA
    bf16, f32 = jnp.bfloat16, jnp.float32
    anywhere, vmem = pl.BlockSpec(memory_space=pl.ANY), pl.BlockSpec(memory_space=pltpu.VMEM)
    return pl.pallas_call(
        back_kernel,
        out_shape=[
            jax.ShapeDtypeStruct((rows, width), bf16),
            jax.ShapeDtypeStruct((piece_rows, 8 * head_cols + 2 * KEY_VALUE_HEADS * HEAD_DIMENSION), f32),
            jax.ShapeDtypeStruct((piece_rows, 8 * head_cols), f32),
            jax.ShapeDtypeStruct((piece_rows, 128), f32),
            jax.ShapeDtypeStruct(gains.shape, f32),
            jax.ShapeDtypeStruct((rows, width), bf16),
        ],
        in_specs=[anywhere] * 16 + [vmem] * 4,
        out_specs=[vmem] * 6,
        scratch_shapes=[
            *[pltpu.VMEM(array.shape, array.dtype) for array in inputs],
            dma((len(inputs),)),
            pltpu.VMEM((8, piece_rows, piece_width), bf16),
            pltpu.VMEM((8, rows, wide), bf16),
            pltpu.VMEM(columns.shape, bf16),
            pltpu.VMEM((2, length, TILE), bf16),
            pltpu.VMEM((length // rows, rows, width), bf16),
            pltpu.VMEM((length, head_cols), bf16),
            pltpu.VMEM((length, head_cols), f32),
            pltpu.VMEM((length, HEAD_DIMENSION), f32),
            pltpu.VMEM((length, HEAD_DIMENSION), f32),
            pltpu.VMEM((length, proj_cols), bf16),
            pltpu.VMEM((8, HEAD_DIMENSION), f32),
            pltpu.VMEM((8, HEAD_DIMENSION), f32),
            pltpu.VMEM((8, rows, width), bf16),
            pltpu.VMEM((4, rows, width), bf16),
            pltpu.VMEM((4, rows, width), bf16),
            pltpu.VMEM((2, 3, rows, width), bf16),
            pltpu.VMEM((4, *gains.shape), f32),
            pltpu.VMEM((7, *gains.shape), f32),
            pltpu.VMEM((4, rows, width), bf16),
            pltpu.VMEM((2, 3, rows, width), bf16),
            pltpu.VMEM((2, 8, piece_rows, piece_width), bf16),
            pltpu.VMEM((8, piece_rows, piece_width), bf16),
            dma((4,)),
            dma((4, 2)),
            dma((4, 2)),
            dma((2,)),
            dma,
            dma((8,)),
            dma((8,)),
            dma((8,)),
            dma((4,)),
            dma((4,)),
            dma((3,)),
            dma((2, 3)),
            dma((6,)),
            dma((6,)),
            dma((2,)),
            pltpu.SemaphoreType.REGULAR,
            dma((4,)),
            dma((4,)),
            dma((3,)),
            dma((2, 3)),
            dma((2,)),
            dma((2,)),
            dma((8,)),
            dma((8,)),
            dma((8,)),
            dma((7,)),
        ],
        compiler_params=pltpu.CompilerParams(
            collective_id=collective_id, has_side_effects=True, vmem_limit_bytes=VMEM_LIMIT
        ),
        name="back",
    )(
        own, pair, columns, normed, *inputs, q_gain, k_gain, attn_gain, gains,
    )


C_Z, C_X, C_Y, C_C, C_KINDS = 0, 1, 2, 4, 8


def front_kernel(
    tokens, pieces, cot, cosine_hbm, sine_hbm, q_gain, k_gain, attn_gain, ffn_gain, routes,
    normed_out, columns_out, cot_all, queries_out, keys_out, values_out, attended_out, q_raw_out, k_raw_out,
    hidden, gates, routed,
    queries, keys, values, attended, q_raw, k_raw, cosine, sine, result_sems, table_sems,
    own, normed, columns, part, x_in, z_in,
    ss, rs, zs, cs, cr, ys, yr, ks, kr, local_sems, gs, gr, gz, xs, xr, us, ur,
):
    p = Place()
    bf16 = jnp.bfloat16
    greet_seq(p)
    place, shard = p.z * 2 + p.x, p.y * 2 + p.c
    mine = place * 4 + shard
    rows, width = own.shape
    length, head_cols = queries.shape
    heads = head_cols // HEAD_DIMENSION
    proj_cols = head_cols + 2 * HEAD_DIMENSION
    plane_rows = 2 * rows
    score_scale = 1.0 / math.sqrt(HEAD_DIMENSION)

    x = tokens[...].astype(jnp.float32)
    scale = lax.rsqrt(jnp.mean(x * x, axis=-1, keepdims=True) + EPS)
    own[...] = (x * scale * attn_gain[...]).astype(bf16)

    def rows_at(q, x):
        return normed.at[q * 2 + x]

    def rows_move(k):
        q = p.near(k)
        there = rows_at(q, p.x)
        if k == 0:
            src = own
            for step, end in ((1, p.high), (-1, p.low)):

                @pl.when(jnp.logical_not(end))
                def _():
                    send(src, there, zs.at[q, 0 if step > 0 else 1], rs.at[q, 0], p.by_z(step))

            pltpu.make_async_copy(own, there, local_sems.at[0]).start()
        else:
            src = there

            @pl.when(jnp.logical_not(p.inner))
            def _():
                await_bytes(src, rs.at[q, 0])

        send(src, there, ss.at[q], rs.at[q, 1], p.by_x)

    def rows_hop(k):
        q = p.near(k)
        there = rows_at(q, p.x)

        @pl.when(p.inner)
        def _():
            await_bytes(there, rs.at[q, 0])
            send(there, there, zs.at[q, 0], rs.at[q, 0], p.by_z(p.onward(k)))

    def pass_on(d):
        block = ((place + 8 - d) % 8) * 4 + shard
        src = pieces.at[place] if d == 0 else columns.at[block]
        if d > 0:
            await_bytes(src, cr.at[d])
        send(src, columns.at[block], ys.at[d], yr.at[d], p.by_y)
        send(src, columns.at[block], ks.at[0, d], kr.at[0, d], p.by_core)

    def pass_across(d):
        block = columns.at[((place + 8 - d) % 8) * 4 + (1 - p.y) * 2 + p.c]
        await_bytes(block, yr.at[d])
        send(block, block, ks.at[1, d], kr.at[1, d], p.by_core)

    def cot_at(q, x, y):
        return cot_all.at[p.block(q, x, y, p.c)]

    def cot_core(q, j, src):
        x, y = (p.x, 1 - p.x)[j % 2], (p.y, 1 - p.y)[j // 2]
        send(src, cot_at(q, x, y), gs.at[q, C_C + j], gr.at[q, C_C + j], p.by_core)

    def cot_move(k):
        q = p.near(k)
        there = cot_at(q, p.x, p.y)
        if k == 0:
            src = cot
            for step, end in ((1, p.high), (-1, p.low)):

                @pl.when(jnp.logical_not(end))
                def _():
                    send(src, there, gz.at[q, 0 if step > 0 else 1], gr.at[q, C_Z], p.by_z(step))

            pltpu.make_async_copy(cot, there, local_sems.at[2]).start()
        else:
            src = there

            @pl.when(jnp.logical_not(p.inner))
            def _():
                await_bytes(src, gr.at[q, C_Z])

        send(src, there, gs.at[q, C_Y], gr.at[q, C_Y], p.by_y)
        send(src, there, gs.at[q, C_X], gr.at[q, C_X], p.by_x)
        cot_core(q, 0, src)

    def cot_hop(k):
        q = p.near(k)
        there = cot_at(q, p.x, p.y)

        @pl.when(p.inner)
        def _():
            await_bytes(there, gr.at[q, C_Z])
            send(there, there, gz.at[q, 0], gr.at[q, C_Z], p.by_z(p.onward(k)))

    def cot_turn(k):
        q = p.near(k)
        there = cot_at(q, 1 - p.x, p.y)
        await_bytes(there, gr.at[q, C_X])
        send(there, there, gs.at[q, C_Y + 1], gr.at[q, C_Y + 1], p.by_y)
        cot_core(q, 1, there)

    def cot_end(k):
        q = p.near(k)
        for j, x in ((0, p.x), (1, 1 - p.x)):
            there = cot_at(q, x, 1 - p.y)
            await_bytes(there, gr.at[q, C_Y + j])
            cot_core(q, 2 + j, there)

    def sum_end(k):
        q = p.far(k)
        held = part.at[q * 2 + p.x]
        await_bytes(x_in.at[q], xr.at[q])
        add_rows(held, x_in.at[q], rows)
        if k < 3:
            step = p.toward(k)
            slot = (1 - step) // 2

            @pl.when(p.inner)
            def _():
                await_bytes(z_in.at[slot, q], ur.at[slot, q])
                add_rows(held, z_in.at[slot, q], rows)

            send(held, z_in.at[slot, q], us.at[k], ur.at[slot, q], p.by_z(step))
        else:
            for slot, there in ((0, p.low), (1, p.high)):

                @pl.when(jnp.logical_not(there))
                def _():
                    await_bytes(z_in.at[slot, q], ur.at[slot, q])
                    add_rows(held, z_in.at[slot, q], rows)

    def route():
        total = tokens[...].astype(jnp.float32) + part[p.z * 2 + p.x].astype(jnp.float32)
        hidden[...] = total
        scale = lax.rsqrt(jnp.mean(total * total, axis=-1, keepdims=True) + EPS)
        routed[:, :width] = (total * scale * ffn_gain[...]).astype(bf16)
        router = columns[:, :, proj_cols + head_cols :].reshape(width, 128)
        logits = mxu(routed[:, :width], router)
        lane = lax.broadcasted_iota(jnp.int32, (rows, 128), 1)
        line = lax.broadcasted_iota(jnp.int32, (rows, 128), 0)
        turned = routes[...].astype(jnp.float32).T
        lanes = lane.astype(jnp.float32)
        named = lanes == turned[:, 0:1]
        for k in range(1, TOPK):
            named = named | (lanes == turned[:, k : k + 1])
        chosen = jnp.where(named, logits, -1e30)
        raised = jnp.where(named, jnp.exp(chosen - jnp.max(chosen, axis=-1, keepdims=True)), 0.0)
        gate = raised / jnp.sum(raised, axis=-1, keepdims=True)
        gates[...] = gate
        counted = jnp.where(named, 1.0, 0.0)
        slot = counted * mxu(jnp.where(lane <= line, 1.0, 0.0).astype(bf16), counted.astype(bf16))
        high = gate.astype(bf16).astype(jnp.float32)
        experts = columns.shape[0]
        info = high + pltpu.roll(gate - high, experts, 1) + pltpu.roll(slot, 2 * experts, 1)
        routed[:, width:] = info.astype(bf16)

    def project(n):
        cols = slice(n * TILE, (n + 1) * TILE)
        weight = columns[:, :, cols].reshape(width, TILE)
        result = mxu(normed[...].reshape(length, width), weight)
        if n * TILE < head_cols:
            q_raw[:, cols] = result
        else:
            k_raw[...] = result[:, :HEAD_DIMENSION]
            values[...] = result[:, HEAD_DIMENSION:].astype(bf16)

    def prepare():
        def one(raw, gain, at):
            scaled = raw * lax.rsqrt(jnp.mean(raw * raw, axis=-1, keepdims=True) + EPS) * gain[...]
            swapped = jnp.concatenate(
                [scaled[:, HEAD_DIMENSION // 2 :], scaled[:, : HEAD_DIMENSION // 2]], axis=1
            )
            return (scaled * cosine[at, :] - swapped * sine[at, :]).astype(bf16)

        chunk = 128

        @pl.loop(0, length // chunk)
        def _(i):
            at = pl.ds(pl.multiple_of(i * chunk, chunk), chunk)
            for h in range(heads):
                cols = slice(h * HEAD_DIMENSION, (h + 1) * HEAD_DIMENSION)
                queries[at, cols] = one(q_raw[at, cols], q_gain, at)
            keys[at, :] = one(k_raw[at, :], k_gain, at)

    def attention(k):
        q = p.far(k)
        row_start = pl.multiple_of(q * plane_rows, plane_rows)
        at = pl.ds(row_start, plane_rows)

        def block(count):
            row_pos = row_start + lax.broadcasted_iota(jnp.int32, (plane_rows, count), 0)
            allowed = lax.broadcasted_iota(jnp.int32, (plane_rows, count), 1) <= row_pos

            @pl.loop(0, heads)
            def _(h):
                cols = pl.ds(pl.multiple_of(h * HEAD_DIMENSION, HEAD_DIMENSION), HEAD_DIMENSION)
                scores = mxu(queries[at, cols], keys[:count], NT) * score_scale
                scores = jnp.where(allowed, scores, -1e30)
                raised = jnp.exp(scores - jnp.max(scores, axis=-1, keepdims=True))
                prob = raised / jnp.sum(raised, axis=-1, keepdims=True)
                attended[at, cols] = mxu(prob.astype(bf16), values[:count]).astype(bf16)

        @pl.when(q < 2)
        def _():
            block(length // 2)

        @pl.when(q >= 2)
        def _():
            block(length)

        per_tile = TILE // columns.shape[1]

        @pl.loop(0, width // TILE)
        def _(n):
            cols = pl.ds(pl.multiple_of(n * TILE, TILE), TILE)
            weight = columns[pl.ds(n * per_tile, per_tile), :, proj_cols : proj_cols + head_cols]
            result = mxu(attended[at, :], weight.reshape(TILE, head_cols), NT).astype(bf16)
            part[pl.ds(q * 2, 2), :, cols] = result.reshape(2, rows, TILE)

        send(part.at[q * 2 + 1 - p.x], x_in.at[q], xs.at[q], xr.at[q], p.by_x)

    tables = [
        pltpu.make_async_copy(cosine_hbm, cosine, table_sems.at[0]),
        pltpu.make_async_copy(sine_hbm, sine, table_sems.at[1]),
    ]
    results = [
        pltpu.make_async_copy(source, target, result_sems.at[i])
        for i, (source, target) in enumerate(
            (
                (queries, queries_out),
                (keys, keys_out),
                (values, values_out),
                (q_raw, q_raw_out),
                (k_raw, k_raw_out),
                (attended, attended_out),
            )
        )
    ]
    rows_move(0)
    for copy in tables:
        copy.start()
    for d in range(1, 8):
        send(pieces.at[(place + d) % 8], columns.at[mine], cs.at[d], cr.at[d], seq_peer(p, d))
    pltpu.make_async_copy(pieces.at[place], columns.at[mine], local_sems.at[1]).start()
    pass_on(0)
    rows_hop(1)
    rows_move(1)
    for d in (1, 2, 7):
        pass_on(d)
    rows_hop(2)
    rows_move(2)
    cot_move(0)
    for d in (6, 3, 5):
        pass_on(d)
    rows_hop(3)
    rows_move(3)
    pass_on(4)
    for d in (0, 1, 2, 7, 6, 3, 5, 4):
        pass_across(d)
    cot_hop(1)
    cot_move(1)
    for k in range(4):
        await_bytes(own, rs.at[p.near(k), 1])
    pltpu.make_async_copy(own, rows_at(p.z, p.x), local_sems.at[0]).wait()
    pltpu.make_async_copy(pieces.at[place], columns.at[mine], local_sems.at[1]).wait()
    piece = pieces.at[0]
    for d in range(8):
        await_bytes(piece, kr.at[0, d])
        await_bytes(piece, kr.at[1, d])
    pltpu.make_async_copy(normed, normed_out, local_sems.at[0]).start()
    pltpu.make_async_copy(columns, columns_out, local_sems.at[1]).start()
    cot_turn(0)
    for n in range(proj_cols // TILE):
        project(n)
    cot_hop(2)
    cot_move(2)
    for copy in tables:
        copy.wait()
    prepare()
    for copy in results[:5]:
        copy.start()
    cot_turn(1)
    attention(0)
    cot_end(0)
    attention(1)
    cot_hop(3)
    cot_move(3)
    sum_end(0)
    attention(2)
    cot_turn(2)
    cot_end(1)
    sum_end(1)
    attention(3)
    results[5].start()
    cot_turn(3)
    sum_end(2)
    cot_end(2)
    sum_end(3)
    cot_end(3)
    route()
    for copy in results:
        copy.wait()
    for q in range(4):
        for j in range(4):
            await_bytes(cot, gr.at[q, C_C + j])
            await_bytes(cot, gs.at[q, C_C + j])
        for kind in (C_X, C_Y, C_Y + 1):
            await_bytes(cot, gs.at[q, kind])
        await_bytes(own, ss.at[q])
        await_bytes(own, xs.at[q])
    for there, slot in ((p.high, 0), (p.low, 1)):

        @pl.when(jnp.logical_not(there))
        def _():
            await_bytes(own, zs.at[p.z, slot])
            await_bytes(cot, gz.at[p.z, slot])

    for k in range(1, 4):

        @pl.when(p.inner)
        def _():
            await_bytes(own, zs.at[p.near(k), 0])
            await_bytes(cot, gz.at[p.near(k), 0])

    for k in range(3):
        await_bytes(own, us.at[k])
    for d in range(8):
        if d > 0:
            await_bytes(piece, cs.at[d])
        await_bytes(piece, ys.at[d])
        await_bytes(piece, ks.at[0, d])
        await_bytes(piece, ks.at[1, d])
    pltpu.make_async_copy(cot, cot_at(p.z, p.x, p.y), local_sems.at[2]).wait()
    pltpu.make_async_copy(normed, normed_out, local_sems.at[0]).wait()
    pltpu.make_async_copy(columns, columns_out, local_sems.at[1]).wait()


def front(
    tokens, pieces, cot, cosine, sine, q_gain, k_gain, attn_gain, ffn_gain, routes, head_cols, collective_id
):
    dma = pltpu.SemaphoreType.DMA
    bf16, f32 = jnp.bfloat16, jnp.float32
    rows, width = tokens.shape
    count, piece_rows, piece_width = pieces.shape
    length = count * rows
    anywhere, vmem = pl.BlockSpec(memory_space=pl.ANY), pl.BlockSpec(memory_space=pltpu.VMEM)
    return pl.pallas_call(
        front_kernel,
        out_shape=[
            jax.ShapeDtypeStruct((count, rows, width), bf16),
            jax.ShapeDtypeStruct((count * 4, piece_rows, piece_width), bf16),
            jax.ShapeDtypeStruct((count * 4, rows, width), bf16),
            jax.ShapeDtypeStruct((length, head_cols), bf16),
            jax.ShapeDtypeStruct((length, HEAD_DIMENSION), bf16),
            jax.ShapeDtypeStruct((length, HEAD_DIMENSION), bf16),
            jax.ShapeDtypeStruct((length, head_cols), bf16),
            jax.ShapeDtypeStruct((length, head_cols), f32),
            jax.ShapeDtypeStruct((length, HEAD_DIMENSION), f32),
            jax.ShapeDtypeStruct((rows, width), f32),
            jax.ShapeDtypeStruct((rows, 128), f32),
            jax.ShapeDtypeStruct((rows, width + 128), bf16),
        ],
        in_specs=[vmem] + [anywhere] * 4 + [vmem] * 5,
        out_specs=[anywhere] * 9 + [vmem] * 3,
        scratch_shapes=[
            pltpu.VMEM((length, head_cols), bf16),
            pltpu.VMEM((length, HEAD_DIMENSION), bf16),
            pltpu.VMEM((length, HEAD_DIMENSION), bf16),
            pltpu.VMEM((length, head_cols), bf16),
            pltpu.VMEM((length, head_cols), f32),
            pltpu.VMEM((length, HEAD_DIMENSION), f32),
            pltpu.VMEM(cosine.shape, f32),
            pltpu.VMEM(sine.shape, f32),
            dma((6,)),
            dma((2,)),
            pltpu.VMEM((rows, width), bf16),
            pltpu.VMEM((count, rows, width), bf16),
            pltpu.VMEM((count * 4, piece_rows, piece_width), bf16),
            pltpu.VMEM((count, rows, width), bf16),
            pltpu.VMEM((4, rows, width), bf16),
            pltpu.VMEM((2, 4, rows, width), bf16),
            dma((4,)),
            dma((4, 2)),
            dma((4, 2)),
            dma((8,)),
            dma((8,)),
            dma((8,)),
            dma((8,)),
            dma((2, 8)),
            dma((2, 8)),
            dma((3,)),
            dma((4, C_KINDS)),
            dma((4, C_KINDS)),
            dma((4, 2)),
            dma((4,)),
            dma((4,)),
            dma((3,)),
            dma((2, 4)),
        ],
        compiler_params=pltpu.CompilerParams(
            collective_id=collective_id, has_side_effects=True, vmem_limit_bytes=VMEM_LIMIT
        ),
        name="front",
    )(tokens, pieces, cot, cosine, sine, q_gain, k_gain, attn_gain, ffn_gain, routes)


def head_columns(weight, group_index):
    rows = weight.shape[0]
    query_width = QUERY_HEADS * HEAD_DIMENSION
    key_width = KEY_VALUE_HEADS * HEAD_DIMENSION
    query = weight[:, :query_width].reshape(rows, len(group_index), -1).transpose(1, 0, 2)
    keys = weight[:, query_width : query_width + key_width].reshape(rows, KEY_VALUE_HEADS, -1)
    values = weight[:, query_width + key_width :].reshape(rows, KEY_VALUE_HEADS, -1)
    keys = jnp.stack([keys[:, group] for group in group_index])
    values = jnp.stack([values[:, group] for group in group_index])
    return jnp.concatenate([query, keys, values], axis=2)


def gathered_body(
    tokens,
    query_key_value_weight,
    w_out_t,
    w_router,
    w_in,
    w_down,
    attn_gain,
    ffn_gain,
    q_gain,
    k_gain,
    routes,
    cotangent,
):
    bf16, f32 = jnp.bfloat16, jnp.float32
    both = ("seq", "fsdp")
    seq_size = lax.axis_size("seq")
    shard_size = lax.axis_size("fsdp")
    experts = seq_size * shard_size
    rows = tokens.shape[1]
    width = tokens.shape[2]
    length = rows * seq_size
    weight_rows = query_key_value_weight.shape[0]
    heads = QUERY_HEADS // seq_size
    head_cols = heads * HEAD_DIMENSION
    kv_cols = HEAD_DIMENSION
    proj_cols = head_cols + 2 * kv_cols
    all_cols = proj_cols + head_cols
    spare_cols = 128
    group_index = [s * heads * KEY_VALUE_HEADS // QUERY_HEADS for s in range(seq_size)]
    capacity = 2 * rows * TOPK // experts

    pieces = jnp.concatenate(
        [
            head_columns(query_key_value_weight, group_index),
            w_out_t.reshape(weight_rows, seq_size, head_cols).transpose(1, 0, 2),
            jnp.broadcast_to(
                jnp.pad(w_router, ((0, 0), (0, spare_cols - experts))),
                (seq_size, weight_rows, spare_cols),
            ),
        ],
        axis=2,
    )
    half_dim = HEAD_DIMENSION // 2
    exponents = -2.0 * np.arange(half_dim, dtype=np.float32) / HEAD_DIMENSION
    frequency = np.float32(ROPE_BASE) ** exponents.astype(np.float32)
    angles = np.arange(length, dtype=np.float32)[:, None] * frequency[None, :]
    cosine, sine = np.cos(angles), np.sin(angles)
    cosine = jnp.asarray(np.concatenate([cosine, cosine], axis=1), f32)
    sine = jnp.asarray(np.concatenate([sine, -sine], axis=1), f32)
    (
        normed_all,
        columns,
        cot_all,
        queries,
        keys,
        values,
        attended,
        q_raw,
        k_raw,
        hidden,
        gates,
        routed,
    ) = front(
        tokens[0],
        pieces,
        cotangent[0],
        cosine,
        sine,
        q_gain[None],
        k_gain[None],
        attn_gain[None],
        ffn_gain[None],
        routes[0].T,
        head_cols,
        1,
    )
    normed_all = normed_all.reshape(length, width)

    gate_weight = w_in[0]
    down_weight = w_down[0]
    unused_rows, out_part, d_part, rows_in, d_expert, inner_act, d_gate_up = experts_gathered(
        routed,
        cot_all,
        gate_weight,
        down_weight,
        capacity,
        3,
    )
    d_attn, d_logits, d_hidden, gains, out_pair, d_w_in, d_w_down = sum_all(
        d_part,
        out_part,
        rows_in,
        d_gate_up,
        inner_act,
        d_expert,
        columns,
        hidden,
        cotangent[0],
        gates,
        ffn_gain[None],
        5,
    )
    d_w_in, d_w_down = d_w_in.astype(f32)[None], d_w_down.astype(f32)[None]

    d_tokens, d_w_qkv, d_w_out_t, d_w_router, gains, mixture = back(
        d_attn,
        out_pair.reshape(2 * seq_size, rows, width),
        columns.reshape(seq_size, 2, shard_size // 2, weight_rows, all_cols + spare_cols),
        normed_all,
        queries,
        keys,
        values,
        attended,
        q_raw,
        k_raw,
        cosine,
        sine,
        q_gain[None],
        k_gain[None],
        attn_gain[None],
        gains,
        tokens[0],
        d_hidden,
        routed,
        d_logits,
        6,
    )
    output = (hidden + mixture.astype(f32)).astype(bf16)
    d_tokens = d_tokens[None]
    d_w_router = d_w_router[:, :experts]
    d_attn_gain, d_ffn_gain = gains[0], gains[1]
    d_q_gain = gains[2, :HEAD_DIMENSION]
    d_k_gain = gains[2, HEAD_DIMENSION : 2 * HEAD_DIMENSION]
    return (
        output[None],
        d_tokens,
        d_w_qkv,
        d_w_out_t,
        d_w_router,
        d_w_in,
        d_w_down,
        d_attn_gain,
        d_ffn_gain,
        d_q_gain,
        d_k_gain,
    )


def gathered_fits(mesh):
    return mesh.shape["seq"] == 8 and mesh.shape["fsdp"] == 4


def solution(mesh):
    return jax.shard_map(
        gathered_body if gathered_fits(mesh) else routed_body,
        mesh=mesh,
        in_specs=(
            P("fsdp", "seq", None),
            P(("seq", "fsdp"), None),
            P(("seq", "fsdp"), None),
            P(("seq", "fsdp"), None),
            P(("seq", "fsdp"), None, None),
            P(("seq", "fsdp"), None, None),
            P(),
            P(),
            P(),
            P(),
            P("fsdp", "seq", None),
            P("fsdp", "seq", None),
        ),
        out_specs=(
            P("fsdp", "seq", None),
            P("fsdp", "seq", None),
            P(("seq", "fsdp"), None),
            P(("seq", "fsdp"), None),
            P(("seq", "fsdp"), None),
            P(("seq", "fsdp"), None, None),
            P(("seq", "fsdp"), None, None),
            P(),
            P(),
            P(),
            P(),
        ),
        check_vma=False,
    )
```
